32 devices in a mesh: ha: 2 (over core), wa: 2 (over x), batch: 8 (over z, y).
Axes of the slice: x: 2, y: 2, z: 4, core: 2. Of those that a mesh axis runs over, the one named last changes fastest.
Arguments:
- inputs: bfloat16 [2, 128, 8, 8, 512], P(None, 'batch', 'ha', 'wa'), may hold values from -22 to 22
- starts: int32 [2, 128], P(None, 'batch'), may hold values from 0 to 1, as said below
- first_spatial: bfloat16 [4608, 1152], P('batch'), may hold values from -0.09375 to 0.09375
- first_mid_gain: bfloat16 [1152], P('batch'), may hold values from 0.5 to 1.5
- first_mid_bias: bfloat16 [1152], P('batch'), may hold values from -3 to 3
- first_temporal: bfloat16 [3456, 512], P('batch'), may hold values from -0.109375 to 0.109375
- first_out_gain: bfloat16 [512], P('batch'), may hold values from 0.5 to 1.5
- first_out_bias: bfloat16 [512], P('batch'), may hold values from -3 to 3
- second_spatial: bfloat16 [4608, 1152], P('batch'), may hold values from -0.09375 to 0.09375
- second_mid_gain: bfloat16 [1152], P('batch'), may hold values from 0.5 to 1.5
- second_mid_bias: bfloat16 [1152], P('batch'), may hold values from -3 to 3
- second_temporal: bfloat16 [3456, 512], P('batch'), may hold values from -0.109375 to 0.109375
- second_out_gain: bfloat16 [512], P('batch'), may hold values from 0.5 to 1.5
- second_out_bias: bfloat16 [512], P('batch'), may hold values from -3 to 3
- cotangent: bfloat16 [2, 128, 8, 8, 512], P(None, 'batch', 'ha', 'wa'), may hold values from -22 to 22
Outputs:
- block_out: float32 [2, 128, 8, 8, 512], P(None, 'batch', 'ha', 'wa')
- grad_input: float32 [2, 128, 8, 8, 512], P(None, 'batch', 'ha', 'wa')
- grad_first_spatial: float32 [4608, 1152], P('batch')
- grad_first_mid_gain: float32 [1152], P('batch')
- grad_first_mid_bias: float32 [1152], P('batch')
- grad_first_temporal: float32 [3456, 512], P('batch')
- grad_first_out_gain: float32 [512], P('batch')
- grad_first_out_bias: float32 [512], P('batch')
- grad_second_spatial: float32 [4608, 1152], P('batch')
- grad_second_mid_gain: float32 [1152], P('batch')
- grad_second_mid_bias: float32 [1152], P('batch')
- grad_second_temporal: float32 [3456, 512], P('batch')
- grad_second_out_gain: float32 [512], P('batch')
- grad_second_out_bias: float32 [512], P('batch')
The draws below stay inside these ranges and needn't reach their ends.
Inputs may be any that keep to these rules, and one draw needn't show every extreme that they name: `starts`: 1 marks the first frame of a clip within its micro-batch; no temporal tap joins frames of different clips or micro-batches.
All inputs are finite; a program needn't handle non-finite values.
Results may differ from the reference program's by a relative error of at most 0.017.
Values may be sent and summed in bfloat16 or wider, within the bound.
A program may use at most 256 MiB of HBM per device.

```python
import math
import jax
import jax.numpy as jnp
from jax import lax

C = 512
M = 1152
HGT = 7
NMB = 2
FMB_DEV = 16
FRAMES_MB = 128
HP = 8


def cell_scale(key):
    spread = jnp.exp(jax.random.uniform(key, (NMB, FRAMES_MB, HP, HP, 1), jnp.float32, math.log(0.3), math.log(3.0)))
    position = jnp.arange(FRAMES_MB, dtype=jnp.float32) / max(FRAMES_MB - 1, 1)
    rising = 0.6 * jnp.exp(math.log(3.0) * position)
    return spread * rising[None, :, None, None, None]


def draw_inputs(key, part):
    key = jax.random.fold_in(key, 11)
    sample_key, scale_key = jax.random.split(key, 2)
    full_shape = (NMB, FRAMES_MB, HP, HP, C)
    samples = jnp.clip(jax.random.normal(sample_key, full_shape, jnp.float32), -4.0, 4.0)
    return (samples * cell_scale(scale_key)).astype(jnp.bfloat16)


def draw_cotangent(key, part):
    key = jax.random.fold_in(key, 23)
    sample_key, scale_key = jax.random.split(key, 2)
    full_shape = (NMB, FRAMES_MB, HP, HP, C)
    samples = jnp.clip(jax.random.normal(sample_key, full_shape, jnp.float32), -4.0, 4.0)
    return (samples * cell_scale(scale_key)).astype(jnp.bfloat16)


def draw_starts(key, part):
    key = jax.random.fold_in(key, 37)
    mark_key, long_key, first_key, last_key = jax.random.split(key, 4)
    marks = (jax.random.randint(mark_key, (NMB, FRAMES_MB), 0, 16) == 0).astype(jnp.int32)
    chosen = jax.random.randint(long_key, (), 0, NMB)
    opening_at = jax.random.randint(first_key, (), 0, FMB_DEV)
    closing_at = jax.random.randint(last_key, (), FRAMES_MB - FMB_DEV, FRAMES_MB)
    position = jnp.arange(FRAMES_MB)[None, :]
    which = jnp.arange(NMB)[:, None] == chosen
    inside = which & (position > opening_at) & (position <= closing_at)
    opening = which & (position == opening_at)
    return jnp.where(inside, 0, jnp.where(opening, 1, marks)).astype(jnp.int32)


def block_scale(key, shape, cuts, low, high):
    def one(axis_at, parts):
        draws = jax.random.uniform(jax.random.fold_in(jax.random.fold_in(key, 6), axis_at), (parts,), jnp.float32, low / len(cuts), high / len(cuts))
        return jnp.repeat(jnp.exp(draws), shape[axis_at] // parts).reshape((-1,) + (1,) * (len(shape) - axis_at - 1))

    level = one(*cuts[0])
    for cut in cuts[1:]:
        level = level * one(*cut)
    return level


def centred(rng, shape, scale, most, pieces=(), held_as=jnp.bfloat16):
    gain = block_scale(rng, shape, pieces, -0.22, 0.18) if pieces else 1.0
    result = jax.random.normal(rng, shape, jnp.float32) * scale * gain
    return jnp.minimum(jnp.maximum(result, -most), most).astype(held_as)


def setup_inputs(seed: int = 0) -> dict:
    arg_keys = jax.random.split(jax.random.key(seed), 16)
    inputs = draw_inputs(jax.random.fold_in(arg_keys[15], 71), 0)
    starts = draw_starts(jax.random.fold_in(arg_keys[15], 71), 0)
    first_spatial = centred(arg_keys[2], (9 * C, M), (9 * C) ** -0.5, 0.09375, ((0, 8),))
    first_mid_gain = jnp.clip(1.0 + 0.1 * jax.random.normal(arg_keys[3], (M,), jnp.float32), 0.5, 1.5).astype(jnp.bfloat16)
    first_mid_bias = centred(arg_keys[4], (M,), 0.3, 3.0, ((0, 8),))
    first_temporal = centred(arg_keys[5], (3 * M, C), (3 * M) ** -0.5, 0.109375, ((0, 8),))
    first_out_gain = jnp.clip(1.0 + 0.1 * jax.random.normal(arg_keys[6], (C,), jnp.float32), 0.5, 1.5).astype(jnp.bfloat16)
    first_out_bias = centred(arg_keys[7], (C,), 0.3, 3.0, ((0, 8),))
    second_spatial = centred(arg_keys[8], (9 * C, M), (9 * C) ** -0.5, 0.09375, ((0, 8),))
    second_mid_gain = jnp.clip(1.0 + 0.1 * jax.random.normal(arg_keys[9], (M,), jnp.float32), 0.5, 1.5).astype(jnp.bfloat16)
    second_mid_bias = centred(arg_keys[10], (M,), 0.3, 3.0, ((0, 8),))
    second_temporal = centred(arg_keys[11], (3 * M, C), (3 * M) ** -0.5, 0.109375, ((0, 8),))
    second_out_gain = jnp.clip(1.0 + 0.1 * jax.random.normal(arg_keys[12], (C,), jnp.float32), 0.5, 1.5).astype(jnp.bfloat16)
    second_out_bias = centred(arg_keys[13], (C,), 0.3, 3.0, ((0, 8),))
    cotangent = draw_cotangent(jax.random.fold_in(arg_keys[15], 71), 0)
    return {"inputs": inputs, "starts": starts, "first_spatial": first_spatial, "first_mid_gain": first_mid_gain, "first_mid_bias": first_mid_bias, "first_temporal": first_temporal, "first_out_gain": first_out_gain, "first_out_bias": first_out_bias, "second_spatial": second_spatial, "second_mid_gain": second_mid_gain, "second_mid_bias": second_mid_bias, "second_temporal": second_temporal, "second_out_gain": second_out_gain, "second_out_bias": second_out_bias, "cotangent": cotangent}


epsilon = 1e-05

@jax.custom_vjp
def low(v):
    return lax.optimization_barrier(v.astype(jnp.bfloat16)).astype(jnp.float32)

@jax.custom_vjp
def low_back(v):
    return v

def low_keep(v):
    return (low(v), None)

def low_pass(kept, grad):
    return (grad,)

def back_keep(v):
    return (v, None)

def back_low(kept, grad):
    return (low(grad),)
low.defvjp(low_keep, low_pass)
low_back.defvjp(back_keep, back_low)

def frame_valid():
    inside = jnp.arange(HP) < HGT
    return (inside[:, None] & inside[None, :]).astype(jnp.float32)[None, :, :, None]

def spatial_conv(field_in, kernel):
    width_in = field_in.shape[-1]
    padded = jnp.pad(field_in, ((0, 0), (1, 1), (1, 1), (0, 0)))
    running = jnp.zeros(field_in.shape[:3] + (kernel.shape[1],), jnp.float32)
    for offset in range(9):
        row_off = offset // 3
        col_off = offset % 3
        window = padded[:, row_off:row_off + HP, col_off:col_off + HP, :]
        running = running + jnp.einsum('fhwc,cm->fhwm', window, kernel[offset * width_in:(offset + 1) * width_in], precision=lax.Precision.HIGHEST)
    return running

def temporal_conv(field_in, clip_gate, kernel):
    width_in = field_in.shape[-1]
    gate_cols = clip_gate[:, None, None, None]
    empty_frame = jnp.zeros_like(field_in[:1])
    before = jnp.concatenate([empty_frame, field_in[:-1]], axis=0) * gate_cols
    after_tap = jnp.concatenate([field_in[1:] * gate_cols[1:], empty_frame], axis=0)
    running = jnp.einsum('fhwc,cm->fhwm', before, kernel[:width_in], precision=lax.Precision.HIGHEST)
    running = running + jnp.einsum('fhwc,cm->fhwm', field_in, kernel[width_in:2 * width_in], precision=lax.Precision.HIGHEST)
    running = running + jnp.einsum('fhwc,cm->fhwm', after_tap, kernel[2 * width_in:], precision=lax.Precision.HIGHEST)
    return running

def batch_norm(pre_norm, norm_gain, norm_bias, valid):
    cell_count = pre_norm.shape[0] * HGT * HGT
    mean_val = lax.optimization_barrier(jnp.sum(pre_norm * valid, axis=(0, 1, 2))) / cell_count
    square_mean = lax.optimization_barrier(jnp.sum(pre_norm * pre_norm * valid, axis=(0, 1, 2))) / cell_count
    inv_std = lax.rsqrt(square_mean - mean_val * mean_val + epsilon)
    return (pre_norm - mean_val) * inv_std * norm_gain + norm_bias

def block(field_in, clip_gate, params):
    valid = frame_valid()
    x_in = field_in * valid
    current = x_in
    normed_out = x_in
    for section_index in range(2):
        kernel_sp, mid_gain, mid_bias, kernel_tm, out_gain, out_bias = params[6 * section_index:6 * section_index + 6]
        spatial_out = low_back(spatial_conv(current, kernel_sp))
        hidden = low(jax.nn.silu(batch_norm(spatial_out, mid_gain, mid_bias, valid)) * valid)
        temporal_out = low_back(temporal_conv(hidden, clip_gate, kernel_tm))
        normed_out = batch_norm(temporal_out, out_gain, out_bias, valid)
        if section_index == 0:
            current = low(jax.nn.silu(normed_out) * valid)
    return jax.nn.silu(normed_out + x_in) * valid

def reference(inputs, starts, first_spatial, first_mid_gain, first_mid_bias, first_temporal, first_out_gain, first_out_bias, second_spatial, second_mid_gain, second_mid_bias, second_temporal, second_out_gain, second_out_bias, cotangent):
    params = tuple((weight.astype(jnp.float32) for weight in (first_spatial, first_mid_gain, first_mid_bias, first_temporal, first_out_gain, first_out_bias, second_spatial, second_mid_gain, second_mid_bias, second_temporal, second_out_gain, second_out_bias)))
    field_all = inputs.astype(jnp.float32)
    gates = (1 - starts).astype(jnp.float32)
    checked = jax.checkpoint(block)

    def whole(field_x, weights):
        return jnp.stack([checked(field_x[micro_step], gates[micro_step], weights) for micro_step in range(NMB)])
    block_out, pullback = jax.vjp(whole, field_all, params)
    grad_input, grads = pullback(cotangent.astype(jnp.float32))
    return (block_out, grad_input, grads[0], grads[1], grads[2], grads[3], grads[4], grads[5], grads[6], grads[7], grads[8], grads[9], grads[10], grads[11])
```

```python
import functools
from types import SimpleNamespace

import jax
import jax.numpy as jnp
from jax import lax
from jax.experimental import pallas as pl
from jax.experimental.pallas import tpu as pltpu
from jax.sharding import PartitionSpec as P

HGT = 7
epsilon = 1e-05
MESH = pl.DeviceIdType.MESH
F32 = jnp.float32
BF16 = jnp.bfloat16

BASE = 10
CELL = 8
ROWS = HGT * 8 * CELL
PADDED = (BASE + HGT * 8 + BASE) * CELL
MAIN = BASE * CELL
CHUNK = 2 * CELL
CHUNKS = ROWS // CHUNK
VMEM_LIMIT = 64 * 1024 * 1024 - 1024 * 1024


def when(cond, work):
    if cond is True:
        work()
    elif cond is not False:
        pl.when(cond)(work)


def nn(a, b):
    return jnp.dot(a, b, preferred_element_type=F32)


def nt(a, b):
    return lax.dot_general(a, b, (((1,), (1,)), ((), ())), preferred_element_type=F32)


def tn(a, b):
    return lax.dot_general(a, b, (((0,), (0,)), ((), ())), preferred_element_type=F32)


def rows_of(start, size, step=16):
    if not isinstance(start, int):
        start = pl.multiple_of(start, step)
    return pl.ds(start, size)


def per_batch(first, second, width):
    return jnp.concatenate(
        [jnp.broadcast_to(first, (CELL // 2, width)), jnp.broadcast_to(second, (CELL // 2, width))], axis=0
    )


def block_kernel(dims, names, *all_refs):
    r = SimpleNamespace(**dict(zip(names, all_refs, strict=True)))
    nb, chan, mid, cell_count = dims
    spat = 9 * chan // nb
    temp = 3 * mid // nb
    unit = spat // 6
    quarter = chan // 4
    sub_s, sub_t = spat // 3, temp // 3
    wide = 640
    skip = mid - wide
    half = chan // 2
    h = lax.axis_index("ha")
    w = lax.axis_index("wa")
    b = lax.axis_index("batch")
    par = lax.rem(b, 2)
    bh = lax.div(b, 2)
    pos = par * (nb - 1 - bh) + (1 - par) * bh
    way = 1 - 2 * h

    def at(p):
        p = lax.rem(p + 4 * nb, nb)
        upper = lax.div(p, nb // 2)
        return (1 - upper) * (2 * p) + upper * (2 * (nb - 1 - p) + 1)

    def at_group(j):
        jw = lax.div(j, 2)
        odd = lax.rem(j, 2)
        return (odd * (1 - jw) + (1 - odd) * jw, jw)

    mine = (1 - w) * h + w * (3 - h)
    sibling = (1 - h, w, b)
    beside = (h, 1 - w, b)
    onward = (h, w, at(pos + way))
    behind = (h, w, at(pos - way))
    later = lax.rem(mine + 1, 4)
    earlier = lax.rem(mine + 3, 4)
    later_dev = (*at_group(later), lax.rem(b + lax.div(mine + 1, 4), nb))
    earlier_dev = (*at_group(earlier), lax.rem(b + nb - lax.div(4 - mine, 4), nb))
    tile_group = [(lax.rem(mine + d, 4), (*at_group(lax.rem(mine + d, 4)), b)) for d in (1, 2, 3)]
    pos_b = w * 2 + par
    plane = []
    for d in (1, 2, 3):
        q = lax.rem(pos_b + d, 4)
        plane.append((q, (h, lax.div(q, 2), b - par + lax.rem(q, 2))))
    depth = nb // 2
    line = []
    for d in range(1, depth):
        q = lax.rem(bh + d, depth)
        line.append((q, (h, w, 2 * q + par)))

    def named(dev):
        return dict(ha=dev[0], wa=dev[1], batch=dev[2])

    def rc(src, dst, send, recv, dev):
        return pltpu.make_async_remote_copy(
            src_ref=src, dst_ref=dst, send_sem=send, recv_sem=recv, device_id=named(dev), device_id_type=MESH
        )

    def lc(src, dst, sem):
        return pltpu.make_async_copy(src, dst, sem)

    partners = [sibling, beside, onward, behind, later_dev, earlier_dev]
    partners += [dev for _, dev in tile_group + plane + line]
    barrier = pltpu.get_barrier_semaphore()
    for dev in partners:
        pl.semaphore_signal(barrier, inc=1, device_id=named(dev), device_id_type=MESH)
    pl.semaphore_wait(barrier, len(partners))

    shards = (r.first_spatial, r.first_temporal, r.second_spatial, r.second_temporal)
    whole = (r.w1s, r.w1t, r.w2s, r.w2t)
    shared = 2 * w + h
    shared_beside = 2 * (1 - w) + h
    own_units = (shared, 4 + h)

    def piece(i, ref, owner, u):
        if i % 2 == 0:
            return ref.at[rows_of(owner * spat + u * unit, unit), :]
        return ref.at[rows_of(owner * temp, temp), rows_of(u * quarter, quarter, 128)]

    def streams(i):
        return (0, 1) if i % 2 == 0 else (0,)

    def own_copy(i):
        rows = spat if i % 2 == 0 else temp
        return lc(shards[i], whole[i].at[rows_of(b * rows, rows), :], r.own_sem.at[i])

    def ring(i, st, s, owner, from_shard=False):
        dst = piece(i, whole[i], owner, own_units[st])
        src = piece(i, shards[i], 0, own_units[st]) if from_shard else dst
        return rc(src, dst, r.ring_send.at[i, st, s], r.ring_recv.at[i, st, s], onward)

    def cross(i, kind, s, owner, u):
        part = piece(i, whole[i], owner, u)
        return rc(part, part, r.sib_send.at[i, kind, s], r.sib_recv.at[i, kind, s], sibling)

    def over(i, s, owner, u):
        part = piece(i, whole[i], owner, u)
        return rc(part, part, r.over_send.at[i, s], r.over_recv.at[i, s], beside)

    def gather_start(i):
        for st in streams(i):
            ring(i, st, 1, b, True).start()
        own_copy(i).start()

    def gather_relay(i, s):
        owner = at(pos - way * s)
        over(i, s, owner, shared_beside).wait_recv()
        cross(i, 2, s, owner, shared_beside).start()

    def gather_pump(i, s):
        owner = at(pos - way * s)
        for st in streams(i):
            ring(i, st, s, owner).wait_recv()
            if isinstance(s, int):
                if s < nb - 1:
                    ring(i, st, s + 1, owner).start()
            else:
                pl.when(s < nb - 1)(lambda st=st: ring(i, st, s + 1, owner).start())
            cross(i, st, s, owner, own_units[st]).start()
            if st == 0:
                over(i, s, owner, shared).start()
        if isinstance(s, int):
            if s > 1:
                gather_relay(i, s - 1)
        else:
            pl.when(s > 1)(lambda: gather_relay(i, s - 1))

    def gather_finish(i):
        gather_relay(i, nb - 1)

        def body(s, _):
            owner = at(pos - way * s)
            theirs = at(pos + way * s)
            for st in streams(i):
                ring(i, st, s, owner).wait_send()
                cross(i, st, s, owner, own_units[st]).wait_send()
                cross(i, st, s, theirs, (2 * w + 1 - h, 5 - h)[st]).wait_recv()
            over(i, s, owner, shared).wait_send()
            cross(i, 2, s, owner, shared_beside).wait_send()
            cross(i, 2, s, theirs, 2 * (1 - w) + 1 - h).wait_recv()
            return 0

        lax.fori_loop(1, nb, body, 0)
        own_copy(i).wait()

    def total(k, width, value, works=()):
        slot = k % 2
        cols = pl.ds(0, width)
        works = list(works) + [None] * 3
        pair, four, far = r.sum_a, r.sum_b, r.sum_c
        pair[slot, h, :, cols] = value
        send_a = rc(
            pair.at[slot, h, :, cols], pair.at[slot, h, :, cols], r.sa_send.at[k], r.sa_recv.at[k], sibling
        )
        send_a.start()
        if works[0]:
            works[0]()
        rc(
            pair.at[slot, 1 - h, :, cols], pair.at[slot, 1 - h, :, cols], r.sa_send.at[k], r.sa_recv.at[k], sibling
        ).wait_recv()
        four[slot, pos_b, :, cols] = pair[slot, 0, :, cols] + pair[slot, 1, :, cols]
        sends = [send_a]
        for n, (q, dev) in enumerate(plane):
            part = four.at[slot, pos_b, :, cols]
            sends.append(rc(part, part, r.sb_send.at[k, n], r.sb_recv.at[k, pos_b], dev))
            sends[-1].start()
        if works[1]:
            works[1]()
        for n, (q, dev) in enumerate(plane):
            part = four.at[slot, q, :, cols]
            rc(part, part, r.sb_send.at[k, n], r.sb_recv.at[k, q], dev).wait_recv()
        far[slot, bh, :, cols] = (four[slot, 0, :, cols] + four[slot, 1, :, cols]) + (
            four[slot, 2, :, cols] + four[slot, 3, :, cols]
        )
        for n, (q, dev) in enumerate(line):
            part = far.at[slot, bh, :, cols]
            sends.append(rc(part, part, r.sc_send.at[k, n], r.sc_recv.at[k, bh], dev))
            sends[-1].start()
        if works[2]:
            works[2]()
        for n, (q, dev) in enumerate(line):
            part = far.at[slot, q, :, cols]
            rc(part, part, r.sc_send.at[k, n], r.sc_recv.at[k, q], dev).wait_recv()
        result = far[slot, 0, :, cols]
        for q in range(1, depth):
            result = result + far[slot, q, :, cols]
        for send in sends:
            send.wait_send()
        return result

    def chunk(ref, i, base=0, width=None):
        cols = slice(None) if width is None else pl.ds(0, width)
        value = ref[rows_of(base + i * CHUNK, CHUNK), cols]
        return value.astype(F32).reshape(2, CELL, value.shape[-1])

    def put(ref, i, value, base=0, width=None):
        cols = slice(None) if width is None else pl.ds(0, width)
        ref[rows_of(base + i * CHUNK, CHUNK), cols] = value.reshape(CHUNK, value.shape[-1]).astype(ref.dtype)

    def keep(i):
        inside = jnp.where(lax.rem(i, 4) == 3, 0.0, 1.0).astype(F32)
        first = lax.broadcasted_iota(jnp.int32, (2, 1, 1), 0) == 0
        return jnp.where(first, 1.0, inside)

    def packed(one, two, width):
        rows = [
            jnp.sum(v[k : k + CELL // 2], axis=0, keepdims=True) for v in (one, two) for k in (0, CELL // 2)
        ]
        return jnp.concatenate(rows + [jnp.zeros((4, width), F32)], axis=0)

    def moments(ref, width):
        def body(i, carry):
            v = chunk(ref, i)
            m = v * keep(i)
            return (carry[0] + m[0] + m[1], carry[1] + m[0] * v[0] + m[1] * v[1])

        zero = jnp.zeros((CELL, width), F32)
        return lax.fori_loop(0, CHUNKS, body, (zero, zero))

    def prepare(n, sums, width):
        tile = r.tile_mid if width == mid else r.tile_out
        n2 = n // 2
        gain = r.param[2 * n : 2 * n + 1, 0:width]
        bias = r.param[2 * n + 1 : 2 * n + 2, 0:width]
        mean = sums[0:2] / cell_count
        inv = lax.rsqrt(sums[2:4] / cell_count - mean * mean + epsilon)
        scale = inv * gain
        shift = bias - mean * scale
        for k, v in enumerate((scale, shift, inv, mean * inv)):
            tile[n2, k] = per_batch(v[0:1], v[1:2], width)

    def tiles(n, width):
        tile = r.tile_mid if width == mid else r.tile_out
        return [tile[n // 2, k][None] for k in range(4)]

    def fill(ref_a, ref_b, value_of, width):
        ref_a[0:MAIN, :] = jnp.zeros((MAIN, width), BF16)
        ref_a[MAIN + ROWS : PADDED, :] = jnp.zeros((PADDED - MAIN - ROWS, width), BF16)
        ref_b[0 : MAIN - CHUNK, :] = jnp.zeros((MAIN - CHUNK, width), BF16)
        ref_b[MAIN - CHUNK + ROWS : PADDED, :] = jnp.zeros((PADDED - MAIN + CHUNK - ROWS, width), BF16)

        def body(i, before):
            v = value_of(i)
            put(ref_a, i, v, MAIN)
            pair = jnp.concatenate([before[None], v[0:1]], axis=0)
            put(ref_b, i, pair, MAIN - CHUNK)
            return v[1]

        lax.fori_loop(0, CHUNKS, body, jnp.zeros((CELL, width), F32))

    def activated(src, n, width):
        def value(i):
            scale, shift, _, _ = tiles(n, width)
            y = chunk(src, i) * scale + shift
            return y * jax.nn.sigmoid(y) * keep(i)

        return value

    def taps(ref_a, ref_b, k, size=ROWS):
        r0 = MAIN - 8 * CELL + 8 * CELL * k
        return (
            ref_b[rows_of(r0 - CHUNK, size), :],
            ref_a[rows_of(r0, size), :],
            ref_b[rows_of(r0, size), :],
        )

    def conv(ref_a, ref_b, weight, out, pump=None):
        for n, (c0, cw) in enumerate(((0, 512), (512, mid - 512))):

            def body(a, _, c0=c0, cw=cw, n=n):
                x = taps(ref_a, ref_b, a)
                acc = nn(x[0], weight[rows_of(a * 3 * chan, chan), c0 : c0 + cw])
                acc += nn(x[1], weight[rows_of(a * 3 * chan + chan, chan), c0 : c0 + cw])
                acc += nn(x[2], weight[rows_of(a * 3 * chan + 2 * chan, chan), c0 : c0 + cw])

                @pl.when(a == 0)
                def _():
                    out[:, c0 : c0 + cw] = acc

                @pl.when(a > 0)
                def _():
                    out[:, c0 : c0 + cw] += acc

                if pump is not None:
                    pump(n * 3 + a)
                return 0

            lax.fori_loop(0, 3, body, 0)

    def conv_back(ref_a, ref_b, weight, out, pump=None):
        def body(k, _):
            e = taps(ref_a, ref_b, k)
            acc = None
            for j in range(3):
                tap = 8 - 3 * k - j
                term = nt(e[j], weight[rows_of(tap * chan, chan), :])
                acc = term if acc is None else acc + term

            @pl.when(k == 0)
            def _():
                out[:, 0:chan] = acc

            @pl.when(k > 0)
            def _():
                out[:, 0:chan] += acc

            if pump is not None:
                pump(k)
            return 0

        lax.fori_loop(0, 3, body, 0)

    def send_frames(k):
        down, up = r.down, r.up
        count = ROWS // 4
        for c in range(chan // 128):
            lanes = pl.ds(128 * c, 128)
            r.halo_out[0, :, lanes] = down[c, pl.ds(CELL + 3, count, stride=4), :].astype(BF16)
            r.halo_out[1, :, lanes] = up[c, pl.ds(0, count, stride=4), :].astype(BF16)
        copies = []
        for n, dev in ((0, later_dev), (1, earlier_dev)):
            copies.append(
                rc(r.halo_out.at[n], r.halo_in.at[k, n], r.halo_send.at[k, n], r.halo_recv.at[k, n], dev)
            )
            copies[-1].start()
        return copies

    def take_frames(k, copies):
        down, up = r.down, r.up
        count = ROWS // 4
        for copy in copies:
            copy.wait()
        at_start = jnp.logical_and(mine == 0, b == 0)
        at_end = jnp.logical_and(mine == 3, b == nb - 1)
        for c in range(chan // 128):
            lanes = pl.ds(128 * c, 128)
            before = r.halo_in[k, 0, :, lanes].astype(F32)
            after = r.halo_in[k, 1, :, lanes].astype(F32)
            down[c, pl.ds(CELL - 1, count, stride=4), :] = jnp.where(at_start, 0.0, before)
            up[c, pl.ds(4, count, stride=4), :] = jnp.where(at_end, 0.0, after)

    def by_lanes(ref, rows):
        return jnp.concatenate([ref[c, rows, :] for c in range(chan // 128)], axis=1)

    def put_lanes(ref, rows, value):
        for c in range(chan // 128):
            ref[c, rows, :] = value[:, 128 * c : 128 * c + 128]

    def shifted(i):
        before = by_lanes(r.down, rows_of(i * CHUNK, CHUNK + CELL))[CELL - 1 : CELL - 1 + CHUNK]
        after = by_lanes(r.up, rows_of(i * CHUNK, CHUNK + CELL))[1 : 1 + CHUNK]
        gate = r.gate[...][None]
        return (before.reshape(2, CELL, chan) * gate, after.reshape(2, CELL, chan))

    def temporal(k, v, weight, out, works=()):
        works = list(works) + [None] * 2
        put_lanes(r.down, pl.ds(CELL, ROWS), nn(v[...], weight[0:mid, :]))
        y2 = nn(v[...], weight[2 * mid : 3 * mid, :])
        y2 = (y2.reshape(ROWS // CELL, CELL, chan) * r.gate[...][None]).reshape(ROWS, chan)
        put_lanes(r.up, pl.ds(0, ROWS), y2)
        copies = send_frames(k)
        out[...] = nn(v[...], weight[mid : 2 * mid, :])
        if works[0]:
            works[0]()
        take_frames(k, copies)

        def body(i, carry):
            before, after = shifted(i)
            value = chunk(out, i) + before + after
            put(out, i, value)
            m = value * keep(i)
            return (carry[0] + m[0] + m[1], carry[1] + m[0] * value[0] + m[1] * value[1])

        zero = jnp.zeros((CELL, chan), F32)
        return lax.fori_loop(0, CHUNKS, body, (zero, zero))

    def temporal_back(k, weight, works=()):
        works = list(works) + [None] * 2
        copies = send_frames(k)
        e3 = r.e3
        for c0, cw in ((0, 512), (512, mid - 512)):
            r.grad_mid[:, c0 : c0 + cw] = nt(e3[1], weight[mid + c0 : mid + c0 + cw, :])
        if works[0]:
            works[0]()
        take_frames(k, copies)

        def body(i, _):
            before, after = shifted(i)
            e3[0, rows_of(i * CHUNK, CHUNK), :] = after.reshape(CHUNK, chan).astype(BF16)
            e3[2, rows_of(i * CHUNK, CHUNK), :] = before.reshape(CHUNK, chan).astype(BF16)
            return 0

        lax.fori_loop(0, CHUNKS, body, 0)
        share = share_e3(k)
        for c0, cw in ((0, 512), (512, mid - 512)):
            r.grad_mid[:, c0 : c0 + cw] += nt(e3[0], weight[c0 : c0 + cw, :]) + nt(
                e3[2], weight[2 * mid + c0 : 2 * mid + c0 + cw, :]
            )
        return share

    def share(k, src, dst):
        copy = rc(src, dst, r.share_send.at[k], r.share_recv.at[k], sibling)
        copy.start()
        return copy

    def share_e3(k):
        return share(
            k - 2, r.e3.at[:, :, rows_of((1 - h) * half, half, 128)], r.sib_e3
        )

    grads = (r.g1s, r.g1t, r.g2s, r.g2t)
    slots = (r.slot1s, r.slot1t, r.slot2s, r.slot2t)
    outs = (r.out1s, r.out1t, r.out2s, r.out2t)

    def stage_out(i, n, slot, value, start):
        rows, cols = value.shape
        return lc(
            r.stage.at[slot, 0:rows, 0:cols], grads[i].at[rows_of(start, rows), :], r.stage_sem.at[slot]
        )

    def spatial_grad(i, xa, xb, sa, sb, pump=None):
        cols = rows_of(h * skip, wide, 128)

        def body(a, _):
            x = taps(xa, xb, a)
            y = taps(sa, sb, a)
            for j in range(3):
                t = 3 * a + j
                slot = lax.rem(t, 2)
                acc = tn(x[j], r.ea[MAIN : MAIN + ROWS, cols]) + tn(y[j], r.sib_e[...])

                def done(t=t, slot=slot):
                    lc(
                        r.stage.at[slot, 0:chan, 0:wide],
                        grads[i].at[rows_of((t - 2) * chan, chan), :],
                        r.stage_sem.at[slot],
                    ).wait()

                if j == 2:
                    done()
                else:
                    pl.when(a > 0)(done)
                r.stage[slot, 0:chan, 0:wide] = acc.astype(BF16)
                lc(
                    r.stage.at[slot, 0:chan, 0:wide],
                    grads[i].at[rows_of(t * chan, chan), :],
                    r.stage_sem.at[slot],
                ).start()
            if pump is not None:
                pump(a)
            return 0

        lax.fori_loop(0, 3, body, 0)
        for t in (7, 8):
            lc(
                r.stage.at[t % 2, 0:chan, 0:wide],
                grads[i].at[pl.ds(t * chan, chan), :],
                r.stage_sem.at[t % 2],
            ).wait()

    def temporal_grad(i, k, v, sv):
        acc = tn(v[...], r.e3[k, :, rows_of(h * half, half, 128)]) + tn(sv[...], r.sib_e3[k])
        r.stage_t[...] = acc.astype(BF16)
        copy = lc(r.stage_t, grads[i].at[pl.ds(k * mid, mid), :], r.stage_sem.at[2])
        copy.start()
        copy.wait()

    def sub(i):
        return sub_s if i % 2 == 0 else sub_t

    def width_of(i):
        return wide if i % 2 == 0 else half

    def block_rows(i, owner, k):
        size = sub(i)
        return rows_of(owner * 3 * size + k * size, size)

    def hop(i, s, k, src):
        dst = slots[i].at[s, pl.ds(k * sub(i), sub(i)), :]
        return rc(src, dst, r.hop_send.at[i, s, k], r.hop_recv.at[i, s, k], onward)

    def stage_of(ref, i, k):
        return ref.at[k, 0 : sub(i), 0 : width_of(i)]

    def reduce_start(i):
        for k in range(3):
            hop(i, 0, k, grads[i].at[block_rows(i, at(pos - way), k), :]).start()

    def reduce_sum(i, s, k):
        owner = at(pos - way * (1 + s))
        load = lc(grads[i].at[block_rows(i, owner, k), :], stage_of(r.ours, i, k), r.ours_sem.at[k])
        load.start()
        hop(i, s - 1, k, stage_of(r.summed, i, k)).wait_recv()
        arrived = lc(
            slots[i].at[s - 1, pl.ds(k * sub(i), sub(i)), :], stage_of(r.theirs, i, k), r.theirs_sem.at[k]
        )
        arrived.start()
        hop(i, s - 1, k, stage_of(r.summed, i, k)).wait_send()
        load.wait()
        arrived.wait()
        parts = (slice(0, sub(i)), slice(0, width_of(i)))
        r.summed[(k, *parts)] = (
            r.ours[(k, *parts)].astype(F32) + r.theirs[(k, *parts)].astype(F32)
        ).astype(BF16)

    def reduce_pump(i, s):
        for k in range(3):
            reduce_sum(i, s, k)
            hop(i, s, k, stage_of(r.summed, i, k)).start()

    def beside_at(i, k):
        return 2 * PADDED + ROWS + (3 * i + k) * sub_s

    def final_over(i, k):
        return rc(
            stage_of(r.summed, i, k),
            r.w2s.at[pl.ds(beside_at(i, k), sub(i)), 0 : width_of(i)],
            r.fin_send.at[i, k],
            r.fin_recv.at[i, k],
            beside,
        )

    def final_out(i, k):
        part = outs[i].at[h, pl.ds(k * sub(i), sub(i)), :]
        src = stage_of(r.ours, i, k)
        return lc(src, part, r.out_sem.at[k]), rc(src, part, r.cast_send.at[i, k], r.cast_recv.at[i, k], sibling)

    def reduce_finish(i):
        for k in range(3):
            reduce_sum(i, nb - 1, k)
            final_over(i, k).start()
        for k in range(3):
            final_over(i, k).wait()
            parts = (slice(0, sub(i)), slice(0, width_of(i)))
            r.ours[(k, *parts)] = (
                r.summed[(k, *parts)].astype(F32) + r.w2s[pl.ds(beside_at(i, k), sub(i)), 0 : width_of(i)].astype(F32)
            ).astype(BF16)
            for copy in final_out(i, k):
                copy.start()
        for k in range(3):
            for copy in final_out(i, k):
                copy.wait()

    def tile_of(ref, jh, jw):
        return ref.at[rows_of(jh * 4, 4, 4), rows_of(jw * 32, 32), :]

    def scatter(src, dst, n):
        copies = []
        for d, (j, dev) in enumerate(tile_group):
            copies.append(
                rc(src.at[j], tile_of(dst, h, w), r.tile_send.at[n, d], r.tile_recv.at[n, mine], dev)
            )
        return copies

    def scattered(src, dst, n):
        for d, (j, dev) in enumerate(tile_group):
            jh, jw = at_group(j)
            rc(src.at[j], tile_of(dst, jh, jw), r.tile_send.at[n, d], r.tile_recv.at[n, j], dev).wait()

    for n, (src, dst) in enumerate(((r.x_tiles, r.x_grid), (r.cot_tiles, r.cot_grid))):
        for copy in scatter(src, dst, n):
            copy.start()
        lc(src.at[mine], tile_of(dst, h, w), r.tile_own.at[n]).start()
    gather_start(0)

    xg, cg = r.x_grid, r.cot_grid
    params = total(0, mid, r.param_in[...])
    r.param[...] = params
    for n, (src, dst) in enumerate(((r.x_tiles, xg), (r.cot_tiles, cg))):
        scattered(src, dst, n)
        lc(src.at[mine], tile_of(dst, h, w), r.tile_own.at[n]).wait()

    def grid_chunk(ref, i):
        v = ref[lax.div(i, 4), rows_of(lax.rem(i, 4) * CHUNK, CHUNK), :]
        return v.astype(F32).reshape(2, CELL, chan)

    fill(r.xa, r.xb, lambda i: grid_chunk(xg, i), chan)

    def loop_pump(i):
        def body(s, _):
            gather_pump(i, s)
            return 0

        lax.fori_loop(1, nb, body, 0)

    loop_pump(0)
    gather_start(1)
    gather_finish(0)
    gather_start(2)

    conv(r.xa, r.xb, r.w1s, r.mid1)
    loop_pump(1)
    gather_finish(1)
    sums = total(1, mid, packed(*moments(r.mid1, mid), mid), [lambda: gather_pump(2, 1)])
    prepare(0, sums, mid)

    def hidden(src, n, dst):
        value = activated(src, n, mid)

        def body(i, _):
            put(dst, i, value(i))
            return 0

        lax.fori_loop(0, CHUNKS, body, 0)

    hidden(r.mid1, 0, r.v1)
    stats = temporal(0, r.v1, r.w1t, r.time1, [lambda: gather_pump(2, 2)])
    sums = total(2, chan, packed(*stats, chan), [lambda: gather_pump(2, 3), lambda: gather_pump(2, 4)])
    prepare(1, sums, chan)
    fill(r.aa, r.ab, activated(r.time1, 1, chan), chan)
    gather_pump(2, 5)
    gather_pump(2, 6)
    gather_start(3)
    gather_pump(2, 7)
    gather_finish(2)

    conv(r.aa, r.ab, r.w2s, r.mid2)
    sums = total(
        3, mid, packed(*moments(r.mid2, mid), mid), [lambda: gather_pump(3, 1), lambda: gather_pump(3, 2)]
    )
    prepare(2, sums, mid)
    hidden(r.mid2, 2, r.v2)

    def body(s, _):
        gather_pump(3, s)
        return 0

    lax.fori_loop(3, nb, body, 0)
    gather_finish(3)
    stats = temporal(1, r.v2, r.w2t, r.time2)
    share_aa = share(2, r.aa, r.sib_aa)
    share_ab = share(3, r.ab, r.sib_ab)
    share_v2 = share(4, r.v2, r.sib_v2)
    sums = total(4, chan, packed(*stats, chan))
    prepare(3, sums, chan)

    out_grid = r.out_grid

    def grid_put(ref, i, v):
        ref[lax.div(i, 4), rows_of(lax.rem(i, 4) * CHUNK, CHUNK), :] = v.reshape(CHUNK, chan)

    def slope(y, s):
        return s * (1.0 + y * (1.0 - s))

    def pre_body(i, carry):
        scale, shift, inv, offset = tiles(3, chan)
        v = chunk(r.time2, i)
        y = v * scale + shift + chunk(r.xa, i, MAIN)
        s = jax.nn.sigmoid(y)
        m = keep(i)
        grid_put(out_grid, i, y * s * m)
        d = grid_chunk(cg, i) * m * slope(y, s)
        put(r.grad_pre, i, d)
        t = d * (v * inv - offset)
        return (carry[0] + d[0] + d[1], carry[1] + t[0] + t[1])

    zero_out = jnp.zeros((CELL, chan), F32)
    zero_mid = jnp.zeros((CELL, mid), F32)
    out_grid[HGT] = jnp.zeros((8 * CELL, chan), F32)
    gg = lax.fori_loop(0, CHUNKS, pre_body, (zero_out, zero_out))

    def send_tiles(src, dst, n):
        for d, (j, dev) in enumerate(tile_group):
            jh, jw = at_group(j)
            rc(tile_of(src, jh, jw), dst.at[mine], r.tile_send.at[n, d], r.tile_recv.at[n, mine], dev).start()
        lc(tile_of(src, h, w), dst.at[mine], r.tile_own.at[n]).start()

    def sent_tiles(src, dst, n):
        for d, (j, dev) in enumerate(tile_group):
            jh, jw = at_group(j)
            rc(tile_of(src, jh, jw), dst.at[j], r.tile_send.at[n, d], r.tile_recv.at[n, j], dev).wait()
        lc(tile_of(src, h, w), dst.at[mine], r.tile_own.at[n]).wait()

    send_tiles(out_grid, r.block_out, 2)

    def norm_back(n, sums, width):
        r.norm_grads[2 * n : 2 * n + 1, 0:width] = sums[2:3] + sums[3:4]
        r.norm_grads[2 * n + 1 : 2 * n + 2, 0:width] = sums[0:1] + sums[1:2]
        back = r.back
        back[0, :, 0:width] = per_batch(sums[0:1], sums[1:2], width) / cell_count
        back[1, :, 0:width] = per_batch(sums[2:3], sums[3:4], width) / cell_count

    def through_norm(n, src, grad, i, width):
        scale, _, inv, offset = tiles(n, width)
        xhat = chunk(src, i) * inv - offset
        bias_part = r.back[0, :, 0:width][None]
        gain_part = r.back[1, :, 0:width][None]
        return scale * (chunk(grad, i, 0, width) - bias_part - xhat * gain_part) * keep(i)

    def through_act(n, src, grad, width):
        def body(i, carry):
            scale, shift, inv, offset = tiles(n, width)
            v = chunk(src, i)
            y = v * scale + shift
            s = jax.nn.sigmoid(y)
            d = chunk(grad, i, 0, width) * keep(i) * slope(y, s)
            put(grad, i, d, 0, width)
            t = d * (v * inv - offset)
            return (carry[0] + d[0] + d[1], carry[1] + t[0] + t[1])

        zero = jnp.zeros((CELL, width), F32)
        return lax.fori_loop(0, CHUNKS, body, (zero, zero))

    def to_frames(n, src, grad):
        def body(i, _):
            e = through_norm(n, src, grad, i, chan).astype(BF16)
            ef = e.astype(F32)
            r.e3[1, rows_of(i * CHUNK, CHUNK), :] = e.reshape(CHUNK, chan)
            put_lanes(r.down, rows_of(i * CHUNK + CELL, CHUNK, CELL), ef.reshape(CHUNK, chan))
            put_lanes(r.up, rows_of(i * CHUNK, CHUNK), (ef * r.gate[...][None]).reshape(CHUNK, chan))
            return 0

        lax.fori_loop(0, CHUNKS, body, 0)

    sums = total(5, chan, packed(*gg, chan))
    norm_back(3, sums, chan)
    to_frames(3, r.time2, r.grad_pre)
    shared_e3 = temporal_back(2, r.w2t)
    gg = through_act(2, r.mid2, r.grad_mid, mid)
    shared_e3.wait()
    share_v2.wait()
    sums = total(
        6,
        mid,
        packed(*gg, mid),
        [functools.partial(temporal_grad, 3, k, r.v2, r.sib_v2) for k in range(3)],
    )
    reduce_start(3)
    norm_back(2, sums, mid)

    def share_e(k):
        return share(k, r.ea.at[pl.ds(MAIN, ROWS), rows_of((1 - h) * skip, wide, 128)], r.sib_e)

    fill(r.ea, r.eb, lambda i: through_norm(2, r.mid2, r.grad_mid, i, mid), mid)
    shared_e = share_e(5)
    conv_back(r.ea, r.eb, r.w2s, r.grad_mid)
    gg = through_act(1, r.time1, r.grad_mid, chan)
    for copy in (shared_e, share_aa, share_ab):
        copy.wait()

    def second_spatial():
        spatial_grad(2, r.aa, r.ab, r.sib_aa, r.sib_ab)

    sums = total(7, chan, packed(*gg, chan), [second_spatial])
    for s in range(1, nb - 1):
        pass

    def reduce_loop(i, lo, hi):
        def body(s, _):
            reduce_pump(i, s)
            return 0

        lax.fori_loop(lo, hi, body, 0)

    spare = r.w2s
    sib_xa, sib_xb = spare.at[0:PADDED, 0:chan], spare.at[PADDED : 2 * PADDED, 0:chan]
    sib_v1 = spare.at[2 * PADDED : 2 * PADDED + ROWS, :]
    share_xa = share(6, r.xa, sib_xa)
    share_xb = share(7, r.xb, sib_xb)
    share_v1 = share(8, r.v1, sib_v1)
    norm_back(1, sums, chan)
    to_frames(1, r.time1, r.grad_mid)
    reduce_loop(3, 1, nb - 1)
    reduce_finish(3)
    reduce_start(2)
    shared_e3 = temporal_back(3, r.w1t)
    gg = through_act(0, r.mid1, r.grad_mid, mid)
    shared_e3.wait()
    share_v1.wait()
    sums = total(
        8,
        mid,
        packed(*gg, mid),
        [functools.partial(temporal_grad, 1, k, r.v1, sib_v1) for k in range(3)],
    )
    norm_back(0, sums, mid)
    fill(r.ea, r.eb, lambda i: through_norm(0, r.mid1, r.grad_mid, i, mid), mid)
    shared_e = share_e(9)
    for copy in (shared_e, share_xa, share_xb):
        copy.wait()
    spatial_grad(0, r.xa, r.xb, sib_xa, sib_xb)
    reduce_loop(2, 1, nb - 1)
    reduce_finish(2)
    reduce_start(1)
    reduce_start(0)
    sent_tiles(out_grid, r.block_out, 2)
    conv_back(r.ea, r.eb, r.w1s, r.grad_mid)

    def last_body(i, _):
        grid_put(out_grid, i, (chunk(r.grad_mid, i, 0, chan) + chunk(r.grad_pre, i)) * keep(i))
        return 0

    lax.fori_loop(0, CHUNKS, last_body, 0)
    send_tiles(out_grid, r.grad_input, 3)
    reduce_loop(1, 1, nb - 1)
    reduce_finish(1)
    reduce_loop(0, 1, nb - 1)
    reduce_finish(0)
    sent_tiles(out_grid, r.grad_input, 3)


def per_device_fast(nb, *args):
    (
        inputs,
        starts,
        first_spatial,
        first_mid_gain,
        first_mid_bias,
        first_temporal,
        first_out_gain,
        first_out_bias,
        second_spatial,
        second_mid_gain,
        second_mid_bias,
        second_temporal,
        second_out_gain,
        second_out_bias,
        cotangent,
    ) = args
    micro, frames, side, _, chan = inputs.shape
    mid = first_spatial.shape[1]
    spat, temp = first_spatial.shape[0], first_temporal.shape[0]
    few = frames // 4
    h, w, b = (lax.axis_index(name) for name in ("ha", "wa", "batch"))
    mine = (1 - w) * h + w * (3 - h)
    offsets = jnp.arange(side)
    valid = (h * side + offsets < HGT)[:, None] & (w * side + offsets < HGT)[None, :]

    def tiles(array):
        array = array * valid.astype(BF16)[None, None, :, :, None]
        array = array.reshape(micro, 4, few, side, side, chan).transpose(1, 3, 4, 0, 2, 5)
        return array.reshape(4, side, side * micro * few, chan)

    def untiled(array):
        array = array.reshape(4, side, side, micro, few, chan).transpose(3, 0, 4, 1, 2, 5)
        return array.reshape(micro, frames, side, side, chan)

    gate = (1 - lax.dynamic_slice_in_dim(starts, mine * few, few, axis=1)).astype(F32)
    gate = jnp.broadcast_to(gate.reshape(micro * few, 1), (micro * few, chan))
    here = jnp.where((h == 0) & (w == 0), 1.0, 0.0)

    def placed(shard):
        row = jnp.zeros((mid,), F32)
        return lax.dynamic_update_slice(row, shard.astype(F32) * here, (b * shard.shape[0],))

    param = jnp.stack(
        [
            placed(v)
            for v in (
                first_mid_gain,
                first_mid_bias,
                first_out_gain,
                first_out_bias,
                second_mid_gain,
                second_mid_bias,
                second_out_gain,
                second_out_bias,
            )
        ]
    )
    wide = 640
    half = chan // 2
    few_rows = ROWS // 4
    big = max(spat, temp) // 3

    inputs_of = dict(
        x_tiles=(tiles(inputs), pl.ANY),
        cot_tiles=(tiles(cotangent), pl.ANY),
        gate=(gate, pltpu.VMEM),
        param_in=(param, pltpu.VMEM),
        first_spatial=(first_spatial, pl.ANY),
        first_temporal=(first_temporal, pl.ANY),
        second_spatial=(second_spatial, pl.ANY),
        second_temporal=(second_temporal, pl.ANY),
    )
    outputs_of = dict(
        block_out=((4, side, side * CELL, chan), F32, pl.ANY),
        grad_input=((4, side, side * CELL, chan), F32, pl.ANY),
        norm_grads=((8, mid), F32, pltpu.VMEM),
        out1s=((2, spat, wide), BF16, pl.ANY),
        out1t=((2, temp, half), BF16, pl.ANY),
        out2s=((2, spat, wide), BF16, pl.ANY),
        out2t=((2, temp, half), BF16, pl.ANY),
        g1s=((9 * chan, wide), BF16, pl.ANY),
        g1t=((3 * mid, half), BF16, pl.ANY),
        g2s=((9 * chan, wide), BF16, pl.ANY),
        g2t=((3 * mid, half), BF16, pl.ANY),
        slot1s=((nb - 1, spat, wide), BF16, pl.ANY),
        slot1t=((nb - 1, temp, half), BF16, pl.ANY),
        slot2s=((nb - 1, spat, wide), BF16, pl.ANY),
        slot2t=((nb - 1, temp, half), BF16, pl.ANY),
    )
    dma = pltpu.SemaphoreType.DMA
    scratch_of = dict(
        w1s=pltpu.VMEM((9 * chan, mid), BF16),
        w1t=pltpu.VMEM((3 * mid, chan), BF16),
        w2s=pltpu.VMEM((9 * chan, mid), BF16),
        w2t=pltpu.VMEM((3 * mid, chan), BF16),
        x_grid=pltpu.VMEM((8, 8 * CELL, chan), BF16),
        cot_grid=pltpu.VMEM((8, 8 * CELL, chan), BF16),
        out_grid=pltpu.VMEM((8, 8 * CELL, chan), F32),
        xa=pltpu.VMEM((PADDED, chan), BF16),
        xb=pltpu.VMEM((PADDED, chan), BF16),
        aa=pltpu.VMEM((PADDED, chan), BF16),
        ab=pltpu.VMEM((PADDED, chan), BF16),
        sib_aa=pltpu.VMEM((PADDED, chan), BF16),
        sib_ab=pltpu.VMEM((PADDED, chan), BF16),
        ea=pltpu.VMEM((PADDED, mid), BF16),
        eb=pltpu.VMEM((PADDED, mid), BF16),
        sib_e=pltpu.VMEM((ROWS, wide), BF16),
        mid1=pltpu.VMEM((ROWS, mid), F32),
        mid2=pltpu.VMEM((ROWS, mid), F32),
        grad_mid=pltpu.VMEM((ROWS, mid), F32),
        v1=pltpu.VMEM((ROWS, mid), BF16),
        v2=pltpu.VMEM((ROWS, mid), BF16),
        sib_v2=pltpu.VMEM((ROWS, mid), BF16),
        time1=pltpu.VMEM((ROWS, chan), F32),
        time2=pltpu.VMEM((ROWS, chan), F32),
        grad_pre=pltpu.VMEM((ROWS, chan), F32),
        down=pltpu.VMEM((chan // 128, ROWS + CHUNK, 128), F32),
        up=pltpu.VMEM((chan // 128, ROWS + CHUNK, 128), F32),
        e3=pltpu.VMEM((3, ROWS, chan), BF16),
        sib_e3=pltpu.VMEM((3, ROWS, half), BF16),
        halo_out=pltpu.VMEM((2, few_rows, chan), BF16),
        halo_in=pltpu.VMEM((4, 2, few_rows, chan), BF16),
        param=pltpu.VMEM((8, mid), F32),
        tile_mid=pltpu.VMEM((2, 4, CELL, mid), F32),
        tile_out=pltpu.VMEM((2, 4, CELL, chan), F32),
        back=pltpu.VMEM((2, CELL, mid), F32),
        sum_a=pltpu.VMEM((2, 2, 8, mid), F32),
        sum_b=pltpu.VMEM((2, 4, 8, mid), F32),
        sum_c=pltpu.VMEM((2, nb // 2, 8, mid), F32),
        stage=pltpu.VMEM((2, chan, wide), BF16),
        stage_t=pltpu.VMEM((mid, half), BF16),
        ours=pltpu.VMEM((3, big, wide), BF16),
        theirs=pltpu.VMEM((3, big, wide), BF16),
        summed=pltpu.VMEM((3, big, wide), BF16),
        own_sem=dma((4,)),
        ring_send=dma((4, 2, nb)),
        ring_recv=dma((4, 2, nb)),
        sib_send=dma((4, 3, nb)),
        sib_recv=dma((4, 3, nb)),
        over_send=dma((4, nb)),
        over_recv=dma((4, nb)),
        sa_send=dma((9,)),
        sa_recv=dma((9,)),
        sb_send=dma((9, 3)),
        sb_recv=dma((9, 4)),
        sc_send=dma((9, nb // 2)),
        sc_recv=dma((9, nb // 2)),
        halo_send=dma((4, 2)),
        halo_recv=dma((4, 2)),
        share_send=dma((10,)),
        share_recv=dma((10,)),
        stage_sem=dma((3,)),
        hop_send=dma((4, nb, 3)),
        hop_recv=dma((4, nb, 3)),
        ours_sem=dma((3,)),
        theirs_sem=dma((3,)),
        fin_send=dma((4, 3)),
        fin_recv=dma((4, 3)),
        cast_send=dma((4, 3)),
        cast_recv=dma((4, 3)),
        out_sem=dma((3,)),
        tile_send=dma((4, 3)),
        tile_recv=dma((4, 4)),
        tile_own=dma((4,)),
    )
    names = (*inputs_of, *outputs_of, *scratch_of)
    cell_count = float(frames * nb * HGT * HGT)
    results = pl.pallas_call(
        functools.partial(block_kernel, (nb, chan, mid, cell_count), names),
        out_shape=[jax.ShapeDtypeStruct(shape, dtype) for shape, dtype, _ in outputs_of.values()],
        in_specs=[pl.BlockSpec(memory_space=space) for _, space in inputs_of.values()],
        out_specs=[pl.BlockSpec(memory_space=space) for _, _, space in outputs_of.values()],
        scratch_shapes=list(scratch_of.values()),
        compiler_params=pltpu.CompilerParams(
            collective_id=0, has_side_effects=True, vmem_limit_bytes=VMEM_LIMIT
        ),
    )(*(array for array, _ in inputs_of.values()))
    got = SimpleNamespace(**dict(zip(outputs_of, results)))

    def spatial(pair):
        return jnp.concatenate([pair[0], pair[1][:, 2 * wide - mid :]], axis=1).astype(F32)

    def temporal(pair):
        return jnp.concatenate([pair[0], pair[1]], axis=1).astype(F32)

    def norm(row, like):
        size = like.shape[0]
        return lax.dynamic_slice_in_dim(got.norm_grads[row], b * size, size)

    return (
        untiled(got.block_out),
        untiled(got.grad_input),
        spatial(got.out1s),
        norm(0, first_mid_gain),
        norm(1, first_mid_bias),
        temporal(got.out1t),
        norm(2, first_out_gain),
        norm(3, first_out_bias),
        spatial(got.out2s),
        norm(4, second_mid_gain),
        norm(5, second_mid_bias),
        temporal(got.out2t),
        norm(6, second_out_gain),
        norm(7, second_out_bias),
    )


def extended(shard, sides, width):
    for axis, dim in sides:
        count, length = (lax.axis_size(axis), shard.shape[dim])
        up = [(i, (i + 1) % count) for i in range(count - 1)]
        down = [(j, i) for i, j in up]
        last = lax.slice_in_dim(shard, length - width, length, axis=dim)
        leading = lax.slice_in_dim(shard, 0, width, axis=dim)
        before = lax.ppermute(last, axis, up)
        after = lax.ppermute(leading, axis, down)
        shard = jnp.concatenate([before, shard, after], axis=dim)
    return shard


def passed_along(shard, axis, by):
    count = lax.axis_size(axis)
    pairs = [(i, i + by) for i in range(count) if 0 <= i + by < count]
    return lax.ppermute(shard, axis, pairs)


def for_sending(shard):

    def short(part):
        return part.astype(jnp.bfloat16) if part.dtype == jnp.float32 else part

    return jax.tree.map(short, shard)


def silu_slope(values):
    sigma = jax.nn.sigmoid(values)
    return sigma * (1.0 + values * (1.0 - sigma))


def spatial_forward(field_in, kernel):
    frames, tile_side = (field_in.shape[0], field_in.shape[1])
    padded = extended(field_in, (("ha", 1), ("wa", 2)), 1)
    pieces = [
        padded[:, offset // 3 : offset // 3 + tile_side, offset % 3 : offset % 3 + tile_side, :]
        for offset in range(9)
    ]
    patches = jnp.concatenate(pieces, axis=-1).reshape(frames * tile_side * tile_side, -1)
    return (patches, jnp.dot(patches, kernel, preferred_element_type=jnp.float32))


def spatial_backward(grad_out, patches, kernel):
    frames, tile_side, channels = (grad_out.shape[0], grad_out.shape[1], grad_out.shape[3])
    row_count = frames * tile_side * tile_side
    padded = extended(grad_out, (("ha", 1), ("wa", 2)), 1)
    pieces = [
        padded[
            :,
            2 - offset // 3 : 2 - offset // 3 + tile_side,
            2 - offset % 3 : 2 - offset % 3 + tile_side,
            :,
        ]
        for offset in range(9)
    ]
    stacked = jnp.concatenate(pieces, axis=-1).reshape(row_count, 9, channels)
    grad_in = jnp.einsum(
        "rkm,kcm->rc", stacked, kernel.reshape(9, -1, channels), preferred_element_type=jnp.float32
    )
    grad_kernel = jnp.einsum(
        "rk,rm->km",
        patches,
        grad_out.reshape(row_count, channels),
        preferred_element_type=jnp.float32,
    )
    return (grad_in, grad_kernel)


def temporal_forward(field_in, clip_gate, kernel):
    frames, tile_side = (field_in.shape[0], field_in.shape[1])
    gated_in = field_in * clip_gate
    earlier = passed_along(field_in[-1:], "batch", 1)
    later_frame = passed_along(gated_in[:1], "batch", -1)
    before = jnp.concatenate([earlier, field_in[:-1]], axis=0) * clip_gate
    after_tap = jnp.concatenate([gated_in[1:], later_frame], axis=0)
    joined = jnp.concatenate([before, field_in, after_tap], axis=-1).reshape(
        frames * tile_side * tile_side, -1
    )
    return (joined, jnp.dot(joined, kernel, preferred_element_type=jnp.float32))


def temporal_backward(grad_out, joined, clip_gate, kernel):
    frames, tile_side, channels = (grad_out.shape[0], grad_out.shape[1], grad_out.shape[3])
    row_count = frames * tile_side * tile_side
    gated_grad = grad_out * clip_gate
    later_frame = passed_along(gated_grad[:1], "batch", -1)
    earlier = passed_along(grad_out[-1:], "batch", 1)
    from_later = jnp.concatenate([gated_grad[1:], later_frame], axis=0)
    from_earlier = jnp.concatenate([earlier, grad_out[:-1]], axis=0) * clip_gate
    stacked = jnp.concatenate([from_later, grad_out, from_earlier], axis=-1).reshape(
        row_count, 3, channels
    )
    grad_in = jnp.einsum(
        "rkc,kmc->rm", stacked, kernel.reshape(3, -1, channels), preferred_element_type=jnp.float32
    )
    grad_kernel = jnp.einsum(
        "rk,rc->kc",
        joined,
        grad_out.reshape(row_count, channels),
        preferred_element_type=jnp.float32,
    )
    return (grad_in, grad_kernel)


def norm_forward(pre_norm, norm_gain, norm_bias, valid_rows, cell_count):
    first_sum = jnp.sum(pre_norm * valid_rows, axis=0)
    square_sum = jnp.sum(pre_norm * pre_norm * valid_rows, axis=0)
    first_sum, square_sum = lax.psum((first_sum, square_sum), ("ha", "wa", "batch"))
    mean_val = first_sum / cell_count
    inv_std = lax.rsqrt(square_sum / cell_count - mean_val * mean_val + epsilon)
    normed = (pre_norm - mean_val) * inv_std
    return (normed, inv_std, normed * norm_gain.astype(jnp.float32) + norm_bias.astype(jnp.float32))


def norm_backward(grad_norm, normed, inv_std, norm_gain, valid_rows, cell_count):
    bias_grad = jnp.sum(grad_norm, axis=0)
    gain_grad = jnp.sum(grad_norm * normed, axis=0)
    bias_grad, gain_grad = lax.psum((bias_grad, gain_grad), ("ha", "wa", "batch"))
    grad_in = (
        valid_rows
        * norm_gain.astype(jnp.float32)
        * inv_std
        * (grad_norm - bias_grad / cell_count - normed * gain_grad / cell_count)
    )
    return (grad_in, gain_grad, bias_grad)


def forward_pair(field_in, weights, clip_gate, valid_rows, cell_count):
    frames, tile_side = (field_in.shape[0], field_in.shape[1])
    patches, spatial_out = spatial_forward(field_in, weights[0])
    mid_hat, mid_scale, mid_norm = norm_forward(
        spatial_out, weights[1], weights[2], valid_rows, cell_count
    )
    hidden = (
        (jax.nn.silu(mid_norm) * valid_rows)
        .astype(jnp.bfloat16)
        .reshape(frames, tile_side, tile_side, -1)
    )
    joined, temporal_out = temporal_forward(hidden, clip_gate, weights[3])
    out_hat, out_scale, out_norm = norm_forward(
        temporal_out, weights[4], weights[5], valid_rows, cell_count
    )
    return ((patches, mid_hat, mid_scale, mid_norm, joined, out_hat, out_scale), out_norm)


def backward_pair(grad_norm, kept, weights, clip_gate, valid_rows, cell_count, tile_side):
    patches, mid_hat, mid_scale, mid_norm, joined, out_hat, out_scale = kept
    frames = clip_gate.shape[0]
    grad_time, out_gain_grad, out_bias_grad = norm_backward(
        grad_norm, out_hat, out_scale, weights[4], valid_rows, cell_count
    )
    grad_time = grad_time.astype(jnp.bfloat16).reshape(frames, tile_side, tile_side, -1)
    grad_hidden, temporal_grad = temporal_backward(grad_time, joined, clip_gate, weights[3])
    grad_mid = grad_hidden * valid_rows * silu_slope(mid_norm)
    grad_spatial, mid_gain_grad, mid_bias_grad = norm_backward(
        grad_mid, mid_hat, mid_scale, weights[1], valid_rows, cell_count
    )
    grad_spatial = grad_spatial.astype(jnp.bfloat16).reshape(frames, tile_side, tile_side, -1)
    grad_in, spatial_grad = spatial_backward(grad_spatial, patches, weights[0])
    return (
        grad_in,
        (spatial_grad, mid_gain_grad, mid_bias_grad, temporal_grad, out_gain_grad, out_bias_grad),
    )


def per_device(
    inputs,
    starts,
    first_spatial,
    first_mid_gain,
    first_mid_bias,
    first_temporal,
    first_out_gain,
    first_out_bias,
    second_spatial,
    second_mid_gain,
    second_mid_bias,
    second_temporal,
    second_out_gain,
    second_out_bias,
    cotangent,
):
    shards = (
        first_spatial,
        first_mid_gain,
        first_mid_bias,
        first_temporal,
        first_out_gain,
        first_out_bias,
        second_spatial,
        second_mid_gain,
        second_mid_bias,
        second_temporal,
        second_out_gain,
        second_out_bias,
    )
    micro_total, frames, tile_side, channels = (
        inputs.shape[0],
        inputs.shape[1],
        inputs.shape[2],
        inputs.shape[4],
    )
    row_count = frames * tile_side * tile_side
    cell_count = frames * lax.axis_size("batch") * HGT * HGT
    offsets = jnp.arange(tile_side)
    inside_h = lax.axis_index("ha") * tile_side + offsets < HGT
    inside_w = lax.axis_index("wa") * tile_side + offsets < HGT
    valid_grid = inside_h[:, None] & inside_w[None, :]
    valid_tile = valid_grid.astype(jnp.bfloat16)[None, :, :, None]
    valid_rows = jnp.broadcast_to(
        valid_grid.astype(jnp.float32)[None], (frames, tile_side, tile_side)
    ).reshape(row_count, 1)
    results = []
    input_grads = []
    kernel_total = None
    norm_total = None
    for micro_step in range(micro_total):
        gathered = (
            lax.all_gather(shards[0], "batch", axis=0, tiled=True),
            lax.all_gather(shards[1], "batch", axis=0, tiled=True),
            lax.all_gather(shards[2], "batch", axis=0, tiled=True),
            lax.all_gather(shards[3], "batch", axis=0, tiled=True),
            lax.all_gather(shards[4], "batch", axis=0, tiled=True),
            lax.all_gather(shards[5], "batch", axis=0, tiled=True),
            lax.all_gather(shards[6], "batch", axis=0, tiled=True),
            lax.all_gather(shards[7], "batch", axis=0, tiled=True),
            lax.all_gather(shards[8], "batch", axis=0, tiled=True),
            lax.all_gather(shards[9], "batch", axis=0, tiled=True),
            lax.all_gather(shards[10], "batch", axis=0, tiled=True),
            lax.all_gather(shards[11], "batch", axis=0, tiled=True),
        )
        clip_gate = (1 - starts[micro_step]).astype(jnp.bfloat16).reshape(frames, 1, 1, 1)
        x_in = inputs[micro_step] * valid_tile
        first_kept, first_norm = forward_pair(
            x_in, gathered[0:6], clip_gate, valid_rows, cell_count
        )
        first_act = (
            (jax.nn.silu(first_norm) * valid_rows)
            .astype(jnp.bfloat16)
            .reshape(frames, tile_side, tile_side, channels)
        )
        second_kept, second_norm = forward_pair(
            first_act, gathered[6:12], clip_gate, valid_rows, cell_count
        )
        pre_out = second_norm + x_in.reshape(row_count, channels).astype(jnp.float32)
        results.append(
            (jax.nn.silu(pre_out) * valid_rows).reshape(frames, tile_side, tile_side, channels)
        )
        grad_pre = (
            cotangent[micro_step].reshape(row_count, channels).astype(jnp.float32)
            * valid_rows
            * silu_slope(pre_out)
        )
        grad_act, second_grads = backward_pair(
            grad_pre, second_kept, gathered[6:12], clip_gate, valid_rows, cell_count, tile_side
        )
        grad_first = grad_act * valid_rows * silu_slope(first_norm)
        grad_conv, first_grads = backward_pair(
            grad_first, first_kept, gathered[0:6], clip_gate, valid_rows, cell_count, tile_side
        )
        input_grads.append(
            ((grad_conv + grad_pre) * valid_rows).reshape(frames, tile_side, tile_side, channels)
        )
        step_grads = first_grads + second_grads
        kernel_now = (step_grads[0], step_grads[3], step_grads[6], step_grads[9])
        norm_now = (
            step_grads[1],
            step_grads[2],
            step_grads[4],
            step_grads[5],
            step_grads[7],
            step_grads[8],
            step_grads[10],
            step_grads[11],
        )
        if micro_step == 0:
            kernel_total = kernel_now
            norm_total = norm_now
        else:
            kernel_total = jax.tree.map(jnp.add, kernel_total, kernel_now)
            norm_total = jax.tree.map(jnp.add, norm_total, norm_now)
    kernel_total = lax.psum_scatter(kernel_total, "batch", scatter_dimension=0, tiled=True)
    kernel_total = jax.tree.map(
        lambda part: part.astype(jnp.float32), lax.psum(for_sending(kernel_total), ("ha", "wa"))
    )
    shard_index = lax.axis_index("batch")
    batch_count = lax.axis_size("batch")
    norm_shards = tuple(
        (
            lax.dynamic_slice_in_dim(
                full_sum,
                shard_index * (full_sum.shape[0] // batch_count),
                full_sum.shape[0] // batch_count,
            )
            for full_sum in norm_total
        )
    )
    return (
        jnp.stack(results),
        jnp.stack(input_grads),
        kernel_total[0],
        norm_shards[0],
        norm_shards[1],
        kernel_total[1],
        norm_shards[2],
        norm_shards[3],
        kernel_total[2],
        norm_shards[4],
        norm_shards[5],
        kernel_total[3],
        norm_shards[6],
        norm_shards[7],
    )


def solution(mesh):
    in_specs = (
        P(None, "batch", "ha", "wa", None),
        P(None, "batch"),
        P("batch", None),
        P("batch"),
        P("batch"),
        P("batch", None),
        P("batch"),
        P("batch"),
        P("batch", None),
        P("batch"),
        P("batch"),
        P("batch", None),
        P("batch"),
        P("batch"),
        P(None, "batch", "ha", "wa", None),
    )
    out_specs = (
        P(None, "batch", "ha", "wa", None),
        P(None, "batch", "ha", "wa", None),
        P("batch", None),
        P("batch"),
        P("batch"),
        P("batch", None),
        P("batch"),
        P("batch"),
        P("batch", None),
        P("batch"),
        P("batch"),
        P("batch", None),
        P("batch"),
        P("batch"),
    )
    batch = mesh.shape["batch"]

    def program(*args):
        spat, temp = args[2].shape[0], args[5].shape[0]
        fits = args[0].shape == (2, 16, 4, 4, 512) and args[2].shape[1] == 1152
        if fits and batch % 2 == 0 and spat % 96 == 0 and temp % 48 == 0 and batch <= 16:
            return per_device_fast(batch, *args)
        return per_device(*args)

    return jax.shard_map(
        program, mesh=mesh, in_specs=in_specs, out_specs=out_specs, check_vma=False
    )
```

```python
import functools
from types import SimpleNamespace

import jax
import jax.numpy as jnp
from jax import lax
from jax.experimental import pallas as pl
from jax.experimental.pallas import tpu as pltpu
from jax.sharding import PartitionSpec as P

HGT = 7
epsilon = 1e-05
MESH = pl.DeviceIdType.MESH
F32 = jnp.float32
BF16 = jnp.bfloat16

BASE = 10
CELL = 8
ROWS = HGT * 8 * CELL
PADDED = (BASE + HGT * 8 + BASE) * CELL
MAIN = BASE * CELL
CHUNK = 2 * CELL
CHUNKS = ROWS // CHUNK
VMEM_LIMIT = 64 * 1024 * 1024 - 1024 * 1024


def when(cond, work):
    if cond is True:
        work()
    elif cond is not False:
        pl.when(cond)(work)


def nn(a, b):
    return jnp.dot(a, b, preferred_element_type=F32)


def nt(a, b):
    return lax.dot_general(a, b, (((1,), (1,)), ((), ())), preferred_element_type=F32)


def tn(a, b):
    return lax.dot_general(a, b, (((0,), (0,)), ((), ())), preferred_element_type=F32)


def rows_of(start, size, step=16):
    if not isinstance(start, int):
        start = pl.multiple_of(start, step)
    return pl.ds(start, size)


def per_batch(first, second, width):
    return jnp.concatenate(
        [jnp.broadcast_to(first, (CELL // 2, width)), jnp.broadcast_to(second, (CELL // 2, width))], axis=0
    )


def block_kernel(dims, names, *all_refs):
    r = SimpleNamespace(**dict(zip(names, all_refs, strict=True)))
    nb, chan, mid, cell_count = dims
    spat = 9 * chan // nb
    temp = 3 * mid // nb
    unit = spat // 6
    quarter = chan // 4
    half = chan // 2
    h = lax.axis_index("ha")
    w = lax.axis_index("wa")
    b = lax.axis_index("batch")
    par = lax.rem(b, 2)
    bh = lax.div(b, 2)
    pos = par * (nb - 1 - bh) + (1 - par) * bh
    way = 1 - 2 * h

    def at(p):
        p = lax.rem(p + 4 * nb, nb)
        upper = lax.div(p, nb // 2)
        return (1 - upper) * (2 * p) + upper * (2 * (nb - 1 - p) + 1)

    def at_group(j):
        jw = lax.div(j, 2)
        odd = lax.rem(j, 2)
        return (odd * (1 - jw) + (1 - odd) * jw, jw)

    mine = (1 - w) * h + w * (3 - h)
    sibling = (1 - h, w, b)
    beside = (h, 1 - w, b)
    onward = (h, w, at(pos + way))
    behind = (h, w, at(pos - way))
    later = lax.rem(mine + 1, 4)
    earlier = lax.rem(mine + 3, 4)
    later_dev = (*at_group(later), lax.rem(b + lax.div(mine + 1, 4), nb))
    earlier_dev = (*at_group(earlier), lax.rem(b + nb - lax.div(4 - mine, 4), nb))
    tile_group = [(lax.rem(mine + d, 4), (*at_group(lax.rem(mine + d, 4)), b)) for d in (1, 2, 3)]
    pos_b = w * 2 + par
    plane = []
    for d in (1, 2, 3):
        q = lax.rem(pos_b + d, 4)
        plane.append((q, (h, lax.div(q, 2), b - par + lax.rem(q, 2))))
    depth = nb // 2
    line = []
    for d in range(1, depth):
        q = lax.rem(bh + d, depth)
        line.append((q, (h, w, 2 * q + par)))

    def named(dev):
        return dict(ha=dev[0], wa=dev[1], batch=dev[2])

    def rc(src, dst, send, recv, dev):
        return pltpu.make_async_remote_copy(
            src_ref=src, dst_ref=dst, send_sem=send, recv_sem=recv, device_id=named(dev), device_id_type=MESH
        )

    def lc(src, dst, sem):
        return pltpu.make_async_copy(src, dst, sem)

    partners = [sibling, beside, onward, behind, later_dev, earlier_dev]
    partners += [dev for _, dev in tile_group + plane + line]
    barrier = pltpu.get_barrier_semaphore()
    for dev in partners:
        pl.semaphore_signal(barrier, inc=1, device_id=named(dev), device_id_type=MESH)
    pl.semaphore_wait(barrier, len(partners))

    shards = (r.first_spatial, r.first_temporal, r.second_spatial, r.second_temporal)
    whole = (r.w1s, r.w1t, r.w2s, r.w2t)
    shared = 2 * w + h
    shared_beside = 2 * (1 - w) + h
    own_units = (shared, 4 + h)

    def piece(i, ref, owner, u):
        if i % 2 == 0:
            return ref.at[rows_of(owner * spat + u * unit, unit), :]
        return ref.at[rows_of(owner * temp, temp), rows_of(u * quarter, quarter, 128)]

    def streams(i):
        return (0, 1) if i % 2 == 0 else (0,)

    def own_copy(i):
        rows = spat if i % 2 == 0 else temp
        return lc(shards[i], whole[i].at[rows_of(b * rows, rows), :], r.own_sem.at[i])

    def ring(i, st, s, owner, from_shard=False):
        dst = piece(i, whole[i], owner, own_units[st])
        src = piece(i, shards[i], 0, own_units[st]) if from_shard else dst
        return rc(src, dst, r.ring_send.at[i, st, s], r.ring_recv.at[i, st, s], onward)

    def cross(i, kind, s, owner, u):
        part = piece(i, whole[i], owner, u)
        return rc(part, part, r.sib_send.at[i, kind, s], r.sib_recv.at[i, kind, s], sibling)

    def over(i, s, owner, u):
        part = piece(i, whole[i], owner, u)
        return rc(part, part, r.over_send.at[i, s], r.over_recv.at[i, s], beside)

    def gather_start(i):
        for st in streams(i):
            ring(i, st, 1, b, True).start()
        own_copy(i).start()

    def gather_relay(i, s):
        owner = at(pos - way * s)
        over(i, s, owner, shared_beside).wait_recv()
        cross(i, 2, s, owner, shared_beside).start()

    def gather_pump(i, s):
        owner = at(pos - way * s)
        for st in streams(i):
            ring(i, st, s, owner).wait_recv()
            if isinstance(s, int):
                if s < nb - 1:
                    ring(i, st, s + 1, owner).start()
            else:
                pl.when(s < nb - 1)(lambda st=st: ring(i, st, s + 1, owner).start())
            cross(i, st, s, owner, own_units[st]).start()
            if st == 0:
                over(i, s, owner, shared).start()
        if isinstance(s, int):
            if s > 1:
                gather_relay(i, s - 1)
        else:
            pl.when(s > 1)(lambda: gather_relay(i, s - 1))

    def gather_finish(i):
        gather_relay(i, nb - 1)

        def body(s, _):
            owner = at(pos - way * s)
            theirs = at(pos + way * s)
            for st in streams(i):
                ring(i, st, s, owner).wait_send()
                cross(i, st, s, owner, own_units[st]).wait_send()
                cross(i, st, s, theirs, (2 * w + 1 - h, 5 - h)[st]).wait_recv()
            over(i, s, owner, shared).wait_send()
            cross(i, 2, s, owner, shared_beside).wait_send()
            cross(i, 2, s, theirs, 2 * (1 - w) + 1 - h).wait_recv()
            return 0

        lax.fori_loop(1, nb, body, 0)
        own_copy(i).wait()

    def total(k, width, value, works=()):
        slot = k % 2
        cols = pl.ds(0, width)
        works = list(works) + [None] * 3
        pair, four, far = r.sum_a, r.sum_b, r.sum_c
        pair[slot, h, :, cols] = value
        send_a = rc(
            pair.at[slot, h, :, cols], pair.at[slot, h, :, cols], r.sa_send.at[k], r.sa_recv.at[k], sibling
        )
        send_a.start()
        if works[0]:
            works[0]()
        rc(
            pair.at[slot, 1 - h, :, cols], pair.at[slot, 1 - h, :, cols], r.sa_send.at[k], r.sa_recv.at[k], sibling
        ).wait_recv()
        four[slot, pos_b, :, cols] = pair[slot, 0, :, cols] + pair[slot, 1, :, cols]
        sends = [send_a]
        for n, (q, dev) in enumerate(plane):
            part = four.at[slot, pos_b, :, cols]
            sends.append(rc(part, part, r.sb_send.at[k, n], r.sb_recv.at[k, pos_b], dev))
            sends[-1].start()
        if works[1]:
            works[1]()
        for n, (q, dev) in enumerate(plane):
            part = four.at[slot, q, :, cols]
            rc(part, part, r.sb_send.at[k, n], r.sb_recv.at[k, q], dev).wait_recv()
        far[slot, bh, :, cols] = (four[slot, 0, :, cols] + four[slot, 1, :, cols]) + (
            four[slot, 2, :, cols] + four[slot, 3, :, cols]
        )
        for n, (q, dev) in enumerate(line):
            part = far.at[slot, bh, :, cols]
            sends.append(rc(part, part, r.sc_send.at[k, n], r.sc_recv.at[k, bh], dev))
            sends[-1].start()
        if works[2]:
            works[2]()
        for n, (q, dev) in enumerate(line):
            part = far.at[slot, q, :, cols]
            rc(part, part, r.sc_send.at[k, n], r.sc_recv.at[k, q], dev).wait_recv()
        result = far[slot, 0, :, cols]
        for q in range(1, depth):
            result = result + far[slot, q, :, cols]
        for send in sends:
            send.wait_send()
        return result

    def chunk(ref, i, base=0, width=None):
        cols = slice(None) if width is None else pl.ds(0, width)
        value = ref[rows_of(base + i * CHUNK, CHUNK), cols]
        return value.astype(F32).reshape(2, CELL, value.shape[-1])

    def put(ref, i, value, base=0, width=None):
        cols = slice(None) if width is None else pl.ds(0, width)
        ref[rows_of(base + i * CHUNK, CHUNK), cols] = value.reshape(CHUNK, value.shape[-1]).astype(ref.dtype)

    def keep(i):
        inside = jnp.where(lax.rem(i, 4) == 3, 0.0, 1.0).astype(F32)
        first = lax.broadcasted_iota(jnp.int32, (2, 1, 1), 0) == 0
        return jnp.where(first, 1.0, inside)

    def packed(one, two, width):
        rows = [
            jnp.sum(v[k : k + CELL // 2], axis=0, keepdims=True) for v in (one, two) for k in (0, CELL // 2)
        ]
        return jnp.concatenate(rows + [jnp.zeros((4, width), F32)], axis=0)

    def moments(ref, width):
        def body(i, carry):
            v = chunk(ref, i)
            m = v * keep(i)
            return (carry[0] + m[0] + m[1], carry[1] + m[0] * v[0] + m[1] * v[1])

        zero = jnp.zeros((CELL, width), F32)
        return lax.fori_loop(0, CHUNKS, body, (zero, zero))

    def prepare(n, sums, width):
        tile = r.tile_mid if width == mid else r.tile_out
        n2 = n // 2
        gain = r.param[2 * n : 2 * n + 1, 0:width]
        bias = r.param[2 * n + 1 : 2 * n + 2, 0:width]
        mean = sums[0:2] / cell_count
        inv = lax.rsqrt(sums[2:4] / cell_count - mean * mean + epsilon)
        scale = inv * gain
        shift = bias - mean * scale
        for k, v in enumerate((scale, shift, inv, mean * inv)):
            tile[n2, k] = per_batch(v[0:1], v[1:2], width)

    def tiles(n, width):
        tile = r.tile_mid if width == mid else r.tile_out
        return [tile[n // 2, k][None] for k in range(4)]

    def fill(ref_a, ref_b, value_of, width):
        ref_a[0:MAIN, :] = jnp.zeros((MAIN, width), BF16)
        ref_a[MAIN + ROWS : PADDED, :] = jnp.zeros((PADDED - MAIN - ROWS, width), BF16)
        ref_b[0 : MAIN - CHUNK, :] = jnp.zeros((MAIN - CHUNK, width), BF16)
        ref_b[MAIN - CHUNK + ROWS : PADDED, :] = jnp.zeros((PADDED - MAIN + CHUNK - ROWS, width), BF16)

        def body(i, before):
            v = value_of(i)
            put(ref_a, i, v, MAIN)
            pair = jnp.concatenate([before[None], v[0:1]], axis=0)
            put(ref_b, i, pair, MAIN - CHUNK)
            return v[1]

        lax.fori_loop(0, CHUNKS, body, jnp.zeros((CELL, width), F32))

    def activated(src, n, width):
        def value(i):
            scale, shift, _, _ = tiles(n, width)
            y = chunk(src, i) * scale + shift
            return y * jax.nn.sigmoid(y) * keep(i)

        return value

    def taps(ref_a, ref_b, k, size=ROWS):
        r0 = MAIN - 8 * CELL + 8 * CELL * k
        return (
            ref_b[rows_of(r0 - CHUNK, size), :],
            ref_a[rows_of(r0, size), :],
            ref_b[rows_of(r0, size), :],
        )

    def conv(ref_a, ref_b, weight, out, pump=None):
        for n, (c0, cw) in enumerate(((0, 512), (512, mid - 512))):

            def body(a, _, c0=c0, cw=cw, n=n):
                x = taps(ref_a, ref_b, a)
                acc = nn(x[0], weight[rows_of(a * 3 * chan, chan), c0 : c0 + cw])
                acc += nn(x[1], weight[rows_of(a * 3 * chan + chan, chan), c0 : c0 + cw])
                acc += nn(x[2], weight[rows_of(a * 3 * chan + 2 * chan, chan), c0 : c0 + cw])

                @pl.when(a == 0)
                def _():
                    out[:, c0 : c0 + cw] = acc

                @pl.when(a > 0)
                def _():
                    out[:, c0 : c0 + cw] += acc

                if pump is not None:
                    pump(n * 3 + a)
                return 0

            lax.fori_loop(0, 3, body, 0)

    def conv_back(ref_a, ref_b, weight, out, pump=None):
        def body(k, _):
            e = taps(ref_a, ref_b, k)
            acc = None
            for j in range(3):
                tap = 8 - 3 * k - j
                term = nt(e[j], weight[rows_of(tap * chan, chan), :])
                acc = term if acc is None else acc + term

            @pl.when(k == 0)
            def _():
                out[:, 0:chan] = acc

            @pl.when(k > 0)
            def _():
                out[:, 0:chan] += acc

            if pump is not None:
                pump(k)
            return 0

        lax.fori_loop(0, 3, body, 0)

    def send_frames(k):
        down, up = r.down, r.up
        count = ROWS // 4
        for c in range(chan // 128):
            lanes = pl.ds(128 * c, 128)
            r.halo_out[0, :, lanes] = down[c, pl.ds(CELL + 3, count, stride=4), :].astype(BF16)
            r.halo_out[1, :, lanes] = up[c, pl.ds(0, count, stride=4), :].astype(BF16)
        copies = []
        for n, dev in ((0, later_dev), (1, earlier_dev)):
            copies.append(
                rc(r.halo_out.at[n], r.halo_in.at[k, n], r.halo_send.at[k, n], r.halo_recv.at[k, n], dev)
            )
            copies[-1].start()
        return copies

    def take_frames(k, copies):
        down, up = r.down, r.up
        count = ROWS // 4
        for copy in copies:
            copy.wait()
        at_start = jnp.logical_and(mine == 0, b == 0)
        at_end = jnp.logical_and(mine == 3, b == nb - 1)
        for c in range(chan // 128):
            lanes = pl.ds(128 * c, 128)
            before = r.halo_in[k, 0, :, lanes].astype(F32)
            after = r.halo_in[k, 1, :, lanes].astype(F32)
            down[c, pl.ds(CELL - 1, count, stride=4), :] = jnp.where(at_start, 0.0, before)
            up[c, pl.ds(4, count, stride=4), :] = jnp.where(at_end, 0.0, after)

    def by_lanes(ref, rows):
        return jnp.concatenate([ref[c, rows, :] for c in range(chan // 128)], axis=1)

    def put_lanes(ref, rows, value):
        for c in range(chan // 128):
            ref[c, rows, :] = value[:, 128 * c : 128 * c + 128]

    def shifted(i):
        before = by_lanes(r.down, rows_of(i * CHUNK, CHUNK + CELL))[CELL - 1 : CELL - 1 + CHUNK]
        after = by_lanes(r.up, rows_of(i * CHUNK, CHUNK + CELL))[1 : 1 + CHUNK]
        gate = r.gate[...][None]
        return (before.reshape(2, CELL, chan) * gate, after.reshape(2, CELL, chan))

    def temporal(k, v, weight, out, works=()):
        works = list(works) + [None] * 2
        put_lanes(r.down, pl.ds(CELL, ROWS), nn(v[...], weight[0:mid, :]))
        y2 = nn(v[...], weight[2 * mid : 3 * mid, :])
        y2 = (y2.reshape(ROWS // CELL, CELL, chan) * r.gate[...][None]).reshape(ROWS, chan)
        put_lanes(r.up, pl.ds(0, ROWS), y2)
        copies = send_frames(k)
        out[...] = nn(v[...], weight[mid : 2 * mid, :])
        if works[0]:
            works[0]()
        take_frames(k, copies)

        def body(i, carry):
            before, after = shifted(i)
            value = chunk(out, i) + before + after
            put(out, i, value)
            m = value * keep(i)
            return (carry[0] + m[0] + m[1], carry[1] + m[0] * value[0] + m[1] * value[1])

        zero = jnp.zeros((CELL, chan), F32)
        return lax.fori_loop(0, CHUNKS, body, (zero, zero))

    def temporal_back(k, weight, works=()):
        works = list(works) + [None] * 2
        copies = send_frames(k)
        e3 = r.e3
        for c0, cw in ((0, 512), (512, mid - 512)):
            r.grad_mid[:, c0 : c0 + cw] = nt(e3[1], weight[mid + c0 : mid + c0 + cw, :])
        if works[0]:
            works[0]()
        take_frames(k, copies)

        def body(i, _):
            before, after = shifted(i)
            e3[0, rows_of(i * CHUNK, CHUNK), :] = after.reshape(CHUNK, chan).astype(BF16)
            e3[2, rows_of(i * CHUNK, CHUNK), :] = before.reshape(CHUNK, chan).astype(BF16)
            return 0

        lax.fori_loop(0, CHUNKS, body, 0)
        share = share_e3(k)
        for c0, cw in ((0, 512), (512, mid - 512)):
            r.grad_mid[:, c0 : c0 + cw] += nt(e3[0], weight[c0 : c0 + cw, :]) + nt(
                e3[2], weight[2 * mid + c0 : 2 * mid + c0 + cw, :]
            )
        return share

    def share(k, src, dst):
        copy = rc(src, dst, r.share_send.at[k], r.share_recv.at[k], sibling)
        copy.start()
        return copy

    outs = (r.out1s, r.out1t, r.out2s, r.out2t)

    def share_e(k):
        own = r.e_all.at[0:ROWS, :]
        copies = [
            rc(own, r.e_all.at[ROWS : 2 * ROWS, :], r.e_send.at[k, 0], r.e_recv.at[k, 0], sibling),
            rc(own, r.e_all.at[2 * ROWS : 3 * ROWS, :], r.e_send.at[k, 1], r.e_recv.at[k, 1], beside),
        ]
        for copy in copies:
            copy.start()
        return copies

    def share_e_on(k, copies):
        copies[1].wait_recv()
        far = rc(
            r.e_all.at[2 * ROWS : 3 * ROWS, :], r.e_all.at[3 * ROWS : 4 * ROWS, :], r.e_send.at[k, 2], r.e_recv.at[k, 2], sibling
        )
        far.start()
        copies[1].wait_send()
        copies[0].wait()
        far.wait()

    def share_x(k, xa, xb, xq):
        copies = []
        for n, dev in enumerate((sibling, beside, (1 - h, 1 - w, b))):
            lanes = rows_of((2 * dev[1] + dev[0]) * quarter, quarter, 128)
            for c, ref in enumerate((xa, xb)):
                copies.append(
                    rc(ref.at[:, lanes], xq.at[n, c], r.xq_send.at[k, n, c], r.xq_recv.at[k, n, c], dev)
                )
                copies[-1].start()
        return copies

    def share_e3(k):
        return share(
            k - 2, r.e3.at[:, :, rows_of((1 - h) * half, half, 128)], r.sib_e3
        )

    def grad_tap(owner):
        return owner + jnp.where(owner > 2 * shared, 1, 0)

    spare = r.w2s

    def gq(i, row, size):
        return rows_of((mid if i == 0 else 0) + row, size)

    def inbox(i, row, size):
        return rows_of(2 * mid + (mid if i == 0 else 0) + row, size)

    def spatial_grad(i, xa, xb, xq):
        lanes = rows_of(shared * quarter, quarter, 128)

        def body(a, _):
            r0 = MAIN - 8 * CELL + 8 * CELL * a
            for j, (c, start) in enumerate(((1, r0 - CHUNK), (0, r0), (1, r0))):
                rows = rows_of(start, ROWS)
                own = (xb if c else xa)[rows, lanes]
                near = jnp.concatenate([own, xq[0, c, rows, :]], axis=0)
                far = jnp.concatenate([xq[1, c, rows, :], xq[2, c, rows, :]], axis=0)
                r.xt[j * quarter : (j + 1) * quarter, :] = near.T
                r.xt[(3 + j) * quarter : (4 + j) * quarter, :] = far.T
            for c0, cw in ((0, 512), (512, mid - 512)):
                acc = nn(r.xt[0 : 3 * quarter, :], r.e_all[0 : 2 * ROWS, c0 : c0 + cw])
                acc += nn(r.xt[3 * quarter : 6 * quarter, :], r.e_all[2 * ROWS : 4 * ROWS, c0 : c0 + cw])
                spare[gq(i, a * 3 * quarter, 3 * quarter), c0 : c0 + cw] = acc.astype(BF16)
            return 0

        lax.fori_loop(0, 3, body, 0)

    def transpose_v(v, sv):
        for c in range(mid // 128):
            lanes = pl.ds(128 * c, 128)
            r.xt[128 * c : 128 * c + 128, :] = jnp.concatenate([v[:, lanes], sv[:, lanes]], axis=0).T

    def temporal_grad(i, k):
        e = jnp.concatenate([r.e3[k, :, rows_of(h * half, half, 128)], r.sib_e3[k]], axis=0)
        whole[i][k * mid : (k + 1) * mid, 0:half] = nn(r.xt[...], e).astype(BF16)

    def s_block(i, owner):
        return spare.at[gq(i, grad_tap(owner) * quarter, quarter), :]

    def s_extra(i, side):
        return spare.at[gq(i, (2 * shared + 1) * quarter + side * 64, 64), :]

    def t_block(i, owner):
        return whole[i].at[rows_of(owner * temp, temp), 0:half]

    def t_inbox(i, n):
        return whole[i].at[rows_of(n * temp, temp), half:chan]

    def block_of(i, owner):
        return s_block(i, owner) if i % 2 == 0 else t_block(i, owner)

    def y_box(i, n):
        return spare.at[inbox(i, n * quarter, quarter), :] if i % 2 == 0 else t_inbox(i, n)

    def z_box(i, n):
        return spare.at[inbox(i, 576 + n * quarter, quarter), :] if i % 2 == 0 else t_inbox(i, 4 + n)

    def extra_y_box(i):
        return spare.at[inbox(i, 4 * quarter, 64), :]

    def extra_z_box(i, n):
        return spare.at[inbox(i, 576 + 3 * quarter + n * 64, 64), :]

    across = (h, w, b + 1 - 2 * par)

    def add_into(dst, parts, step):
        rows, cols = dst.shape

        def body(n, _):
            at_rows = rows_of(n * step, step)
            value = dst[at_rows, :].astype(F32)
            for part in parts:
                value = value + part[at_rows, :].astype(F32)
            dst[at_rows, :] = value.astype(BF16)
            return 0

        lax.fori_loop(0, rows // step, body, 0)

    def y_copy(i, d):
        place = lax.rem(bh + d, depth)
        src = block_of(i, 2 * place + 1 - par)
        return rc(src, y_box(i, place), r.y_send.at[i, d], r.y_recv.at[i, place], across)

    def z_copy(i, d):
        place = lax.rem(bh + d, depth)
        return rc(
            block_of(i, 2 * place + par), z_box(i, 3 - d), r.z_send.at[i, d], r.z_recv.at[i, 3 - d], (h, w, 2 * place + par)
        )

    def extra_y(i):
        return rc(s_extra(i, 1 - par), extra_y_box(i), r.y_send.at[i, 4], r.y_recv.at[i, 4], across)

    def extra_z(i):
        n = lax.rem(bh - shared + 3 + depth, depth)
        n = jnp.minimum(n, 2)
        return rc(
            s_extra(i, par), extra_z_box(i, n), r.z_send.at[i, 4], r.z_recv.at[i, 4 + n], (h, w, 2 * shared + par)
        )

    def step_of(i):
        return 16 if i % 2 == 0 else 48

    def reduce_start(i):
        for d in (1, 2, 3, 0):
            y_copy(i, d).start()
        if i % 2 == 0:
            extra_y(i).start()

    def reduce_middle(i):
        for d in (1, 2, 3, 0):
            place = lax.rem(bh + d, depth)
            y_copy(i, d).wait_send()
            box = y_box(i, place)
            rc(box, box, r.y_send.at[i, d], r.y_recv.at[i, place], across).wait_recv()
            add_into(block_of(i, 2 * place + par), [box], step_of(i))
            if d:
                z_copy(i, d).start()
        if i % 2 == 0:
            extra_y(i).wait()
            add_into(s_extra(i, par), [extra_y_box(i)], 16)
            pl.when(bh != shared)(lambda: extra_z(i).start())

    def final_copies(i):
        if i % 2:
            src = t_block(i, b)
            part = outs[i].at[h]
            return [lc(src, part, r.out_sem.at[i, 0])], [(src, part, sibling, r.cast_send.at[i, 0], r.cast_recv.at[i, 0])]
        src = s_block(i, b)
        part = outs[i].at[rows_of(quarter * shared - 64 * b + 512 * jnp.where(b > 2 * shared, 1, 0), quarter, 64), :]
        local = [lc(src, part, r.out_sem.at[i, 0])]
        sends = [
            (src, part, dev, r.cast_send.at[i, d], r.cast_recv.at[i, mine]) for d, (j, dev) in enumerate(tile_group)
        ]
        return local, sends

    def extra_copies(i):
        src = s_extra(i, par)
        part = outs[i].at[rows_of(512 * (1 - par), 64, 64), :]
        local = [lc(src, part, r.out_sem.at[i, 1])]
        sends = [
            (src, part, dev, r.cast_send.at[i, 3 + d], r.cast_recv.at[i, 4 + mine])
            for d, (j, dev) in enumerate(tile_group)
        ]
        return local, sends

    def beside_copy(i):
        return rc(t_block(i, b), t_inbox(i, 7), r.z_send.at[i, 4], r.z_recv.at[i, 4], beside)

    def reduce_last(i):
        for d in (1, 2, 3):
            z_copy(i, d).wait()
        add_into(block_of(i, b), [z_box(i, n) for n in range(3)], step_of(i))
        if i % 2:
            beside_copy(i).start()
            return
        local, sends = final_copies(i)
        for copy in local:
            copy.start()
        for send in sends:
            rc(send[0], send[1], send[3], send[4], send[2]).start()

        @pl.when(bh != shared)
        def _():
            extra_z(i).wait_send()

        @pl.when(bh == shared)
        def _():
            for n in range(3):
                box = extra_z_box(i, n)
                rc(box, box, r.z_send.at[i, 4], r.z_recv.at[i, 4 + n], across).wait_recv()
            add_into(s_extra(i, par), [extra_z_box(i, n) for n in range(3)], 16)
            local, sends = extra_copies(i)
            for copy in local:
                copy.start()
            for send in sends:
                rc(send[0], send[1], send[3], send[4], send[2]).start()

    def reduce_out(i):
        beside_copy(i).wait()
        add_into(t_block(i, b), [t_inbox(i, 7)], 48)
        local, sends = final_copies(i)
        for copy in local:
            copy.start()
        for send in sends:
            rc(send[0], send[1], send[3], send[4], send[2]).start()

    def reduce_wait(i):
        local, sends = final_copies(i)
        for copy in local:
            copy.wait()
        if i % 2:
            src, part, dev, one, two = sends[0]
            rc(src, outs[i].at[1 - h], one, two, dev).wait()
            return
        for d, (j, dev) in enumerate(tile_group):
            src, part, _, one, _ = sends[d]
            rc(src, part, one, r.cast_recv.at[i, j], dev).wait()
        local, sends = extra_copies(i)

        @pl.when(bh == shared)
        def _():
            for copy in local:
                copy.wait()
            for send in sends:
                rc(send[0], send[1], send[3], send[4], send[2]).wait_send()

        for d, (j, dev) in enumerate(tile_group):
            jh, jw = at_group(j)

            @pl.when(bh == 2 * jw + jh)
            def _(d=d, j=j, dev=dev):
                src, part, _, one, _ = sends[d]
                rc(src, part, one, r.cast_recv.at[i, 4 + j], dev).wait_recv()

    def tile_of(ref, jh, jw):
        return ref.at[rows_of(jh * 4, 4, 4), rows_of(jw * 32, 32), :]

    def scatter(src, dst, n):
        copies = []
        for d, (j, dev) in enumerate(tile_group):
            copies.append(
                rc(src.at[j], tile_of(dst, h, w), r.tile_send.at[n, d], r.tile_recv.at[n, mine], dev)
            )
        return copies

    def scattered(src, dst, n):
        for d, (j, dev) in enumerate(tile_group):
            jh, jw = at_group(j)
            rc(src.at[j], tile_of(dst, jh, jw), r.tile_send.at[n, d], r.tile_recv.at[n, j], dev).wait()

    for n, (src, dst) in enumerate(((r.x_tiles, r.x_grid), (r.cot_tiles, r.cot_grid))):
        for copy in scatter(src, dst, n):
            copy.start()
        lc(src.at[mine], tile_of(dst, h, w), r.tile_own.at[n]).start()
    gather_start(0)

    xg, cg = r.x_grid, r.cot_grid
    params = total(0, mid, r.param_in[...])
    r.param[...] = params
    for n, (src, dst) in enumerate(((r.x_tiles, xg), (r.cot_tiles, cg))):
        scattered(src, dst, n)
        lc(src.at[mine], tile_of(dst, h, w), r.tile_own.at[n]).wait()

    def grid_chunk(ref, i):
        v = ref[lax.div(i, 4), rows_of(lax.rem(i, 4) * CHUNK, CHUNK), :]
        return v.astype(F32).reshape(2, CELL, chan)

    fill(r.xa, r.xb, lambda i: grid_chunk(xg, i), chan)

    def loop_pump(i):
        def body(s, _):
            gather_pump(i, s)
            return 0

        lax.fori_loop(1, nb, body, 0)

    loop_pump(0)
    gather_start(1)
    gather_finish(0)
    gather_start(2)

    conv(r.xa, r.xb, r.w1s, r.mid1)
    loop_pump(1)
    gather_finish(1)
    sums = total(1, mid, packed(*moments(r.mid1, mid), mid), [lambda: gather_pump(2, 1)])
    prepare(0, sums, mid)

    def hidden(src, n, dst):
        value = activated(src, n, mid)

        def body(i, _):
            put(dst, i, value(i))
            return 0

        lax.fori_loop(0, CHUNKS, body, 0)

    hidden(r.mid1, 0, r.v1)
    stats = temporal(0, r.v1, r.w1t, r.time1, [lambda: gather_pump(2, 2)])
    sums = total(2, chan, packed(*stats, chan), [lambda: gather_pump(2, 3), lambda: gather_pump(2, 4)])
    prepare(1, sums, chan)
    fill(r.aa, r.ab, activated(r.time1, 1, chan), chan)
    gather_pump(2, 5)
    gather_pump(2, 6)
    gather_start(3)
    gather_pump(2, 7)
    gather_finish(2)

    conv(r.aa, r.ab, r.w2s, r.mid2)
    sums = total(
        3, mid, packed(*moments(r.mid2, mid), mid), [lambda: gather_pump(3, 1), lambda: gather_pump(3, 2)]
    )
    prepare(2, sums, mid)
    hidden(r.mid2, 2, r.v2)

    def body(s, _):
        gather_pump(3, s)
        return 0

    lax.fori_loop(3, nb, body, 0)
    gather_finish(3)
    stats = temporal(1, r.v2, r.w2t, r.time2)
    shared_xq = share_x(0, r.aa, r.ab, r.xq2) + share_x(1, r.xa, r.xb, r.xq1)
    share_v2 = share(4, r.v2, r.sib_v)
    sums = total(4, chan, packed(*stats, chan))
    prepare(3, sums, chan)

    out_grid = r.out_grid

    def grid_put(ref, i, v):
        ref[lax.div(i, 4), rows_of(lax.rem(i, 4) * CHUNK, CHUNK), :] = v.reshape(CHUNK, chan)

    def slope(y, s):
        return s * (1.0 + y * (1.0 - s))

    def pre_body(i, carry):
        scale, shift, inv, offset = tiles(3, chan)
        v = chunk(r.time2, i)
        y = v * scale + shift + chunk(r.xa, i, MAIN)
        s = jax.nn.sigmoid(y)
        m = keep(i)
        grid_put(out_grid, i, y * s * m)
        d = grid_chunk(cg, i) * m * slope(y, s)
        put(r.grad_pre, i, d)
        t = d * (v * inv - offset)
        return (carry[0] + d[0] + d[1], carry[1] + t[0] + t[1])

    zero_out = jnp.zeros((CELL, chan), F32)
    zero_mid = jnp.zeros((CELL, mid), F32)
    out_grid[HGT] = jnp.zeros((8 * CELL, chan), F32)
    gg = lax.fori_loop(0, CHUNKS, pre_body, (zero_out, zero_out))

    def send_tiles(src, dst, n):
        for d, (j, dev) in enumerate(tile_group):
            jh, jw = at_group(j)
            rc(tile_of(src, jh, jw), dst.at[mine], r.tile_send.at[n, d], r.tile_recv.at[n, mine], dev).start()
        lc(tile_of(src, h, w), dst.at[mine], r.tile_own.at[n]).start()

    def sent_tiles(src, dst, n):
        for d, (j, dev) in enumerate(tile_group):
            jh, jw = at_group(j)
            rc(tile_of(src, jh, jw), dst.at[j], r.tile_send.at[n, d], r.tile_recv.at[n, j], dev).wait()
        lc(tile_of(src, h, w), dst.at[mine], r.tile_own.at[n]).wait()

    send_tiles(out_grid, r.block_out, 2)

    def norm_back(n, sums, width):
        r.norm_grads[2 * n : 2 * n + 1, 0:width] = sums[2:3] + sums[3:4]
        r.norm_grads[2 * n + 1 : 2 * n + 2, 0:width] = sums[0:1] + sums[1:2]
        back = r.back
        back[0, :, 0:width] = per_batch(sums[0:1], sums[1:2], width) / cell_count
        back[1, :, 0:width] = per_batch(sums[2:3], sums[3:4], width) / cell_count

    def through_norm(n, src, grad, i, width):
        scale, _, inv, offset = tiles(n, width)
        xhat = chunk(src, i) * inv - offset
        bias_part = r.back[0, :, 0:width][None]
        gain_part = r.back[1, :, 0:width][None]
        return scale * (chunk(grad, i, 0, width) - bias_part - xhat * gain_part) * keep(i)

    def through_act(n, src, grad, width):
        def body(i, carry):
            scale, shift, inv, offset = tiles(n, width)
            v = chunk(src, i)
            y = v * scale + shift
            s = jax.nn.sigmoid(y)
            d = chunk(grad, i, 0, width) * keep(i) * slope(y, s)
            put(grad, i, d, 0, width)
            t = d * (v * inv - offset)
            return (carry[0] + d[0] + d[1], carry[1] + t[0] + t[1])

        zero = jnp.zeros((CELL, width), F32)
        return lax.fori_loop(0, CHUNKS, body, (zero, zero))

    def to_frames(n, src, grad):
        def body(i, _):
            e = through_norm(n, src, grad, i, chan).astype(BF16)
            ef = e.astype(F32)
            r.e3[1, rows_of(i * CHUNK, CHUNK), :] = e.reshape(CHUNK, chan)
            put_lanes(r.down, rows_of(i * CHUNK + CELL, CHUNK, CELL), ef.reshape(CHUNK, chan))
            put_lanes(r.up, rows_of(i * CHUNK, CHUNK), (ef * r.gate[...][None]).reshape(CHUNK, chan))
            return 0

        lax.fori_loop(0, CHUNKS, body, 0)

    sums = total(5, chan, packed(*gg, chan))
    norm_back(3, sums, chan)
    to_frames(3, r.time2, r.grad_pre)
    shared_e3 = temporal_back(2, r.w2t)
    gg = through_act(2, r.mid2, r.grad_mid, mid)
    shared_e3.wait()
    share_v2.wait()
    def temporal_grads(i, v):
        def first():
            transpose_v(v, r.sib_v)
            temporal_grad(i, 0)

        return [first, lambda: temporal_grad(i, 1), lambda: temporal_grad(i, 2)]

    sums = total(6, mid, packed(*gg, mid), temporal_grads(3, r.v2))
    reduce_start(3)
    norm_back(2, sums, mid)

    def fill_e(n, src):
        def value(i):
            v = through_norm(n, src, r.grad_mid, i, mid)
            put(r.e_all, i, v)
            return v

        fill(r.ea, r.eb, value, mid)

    fill_e(2, r.mid2)
    shared_e = share_e(0)
    conv_back(r.ea, r.eb, r.w2s, r.grad_mid)
    gg = through_act(1, r.time1, r.grad_mid, chan)
    for copy in shared_xq:
        copy.wait()
    share_e_on(0, shared_e)

    def second_spatial():
        spatial_grad(2, r.aa, r.ab, r.xq2)

    sums = total(7, chan, packed(*gg, chan), [second_spatial])
    reduce_middle(3)
    reduce_start(2)
    share_v1 = share(5, r.v1, r.sib_v)
    norm_back(1, sums, chan)
    to_frames(1, r.time1, r.grad_mid)
    shared_e3 = temporal_back(3, r.w1t)
    reduce_last(3)
    gg = through_act(0, r.mid1, r.grad_mid, mid)
    shared_e3.wait()
    share_v1.wait()
    sums = total(8, mid, packed(*gg, mid), temporal_grads(1, r.v1))
    reduce_start(1)
    norm_back(0, sums, mid)
    fill_e(0, r.mid1)
    shared_e = share_e(1)
    reduce_out(3)
    reduce_middle(2)
    sent_tiles(out_grid, r.block_out, 2)
    conv_back(r.ea, r.eb, r.w1s, r.grad_mid)
    share_e_on(1, shared_e)
    spatial_grad(0, r.xa, r.xb, r.xq1)
    reduce_start(0)

    def last_body(i, _):
        grid_put(out_grid, i, (chunk(r.grad_mid, i, 0, chan) + chunk(r.grad_pre, i)) * keep(i))
        return 0

    lax.fori_loop(0, CHUNKS, last_body, 0)
    send_tiles(out_grid, r.grad_input, 3)
    reduce_last(2)
    reduce_middle(1)
    reduce_middle(0)
    reduce_last(1)
    reduce_out(1)
    reduce_last(0)
    sent_tiles(out_grid, r.grad_input, 3)
    for i in (3, 2, 1, 0):
        reduce_wait(i)


def per_device_fast(nb, *args):
    (
        inputs,
        starts,
        first_spatial,
        first_mid_gain,
        first_mid_bias,
        first_temporal,
        first_out_gain,
        first_out_bias,
        second_spatial,
        second_mid_gain,
        second_mid_bias,
        second_temporal,
        second_out_gain,
        second_out_bias,
        cotangent,
    ) = args
    micro, frames, side, _, chan = inputs.shape
    mid = first_spatial.shape[1]
    spat, temp = first_spatial.shape[0], first_temporal.shape[0]
    few = frames // 4
    h, w, b = (lax.axis_index(name) for name in ("ha", "wa", "batch"))
    mine = (1 - w) * h + w * (3 - h)
    offsets = jnp.arange(side)
    valid = (h * side + offsets < HGT)[:, None] & (w * side + offsets < HGT)[None, :]

    def tiles(array):
        array = array * valid.astype(BF16)[None, None, :, :, None]
        array = array.reshape(micro, 4, few, side, side, chan).transpose(1, 3, 4, 0, 2, 5)
        return array.reshape(4, side, side * micro * few, chan)

    def untiled(array):
        array = array.reshape(4, side, side, micro, few, chan).transpose(3, 0, 4, 1, 2, 5)
        return array.reshape(micro, frames, side, side, chan)

    gate = (1 - lax.dynamic_slice_in_dim(starts, mine * few, few, axis=1)).astype(F32)
    gate = jnp.broadcast_to(gate.reshape(micro * few, 1), (micro * few, chan))
    here = jnp.where((h == 0) & (w == 0), 1.0, 0.0)

    def placed(shard):
        row = jnp.zeros((mid,), F32)
        return lax.dynamic_update_slice(row, shard.astype(F32) * here, (b * shard.shape[0],))

    param = jnp.stack(
        [
            placed(v)
            for v in (
                first_mid_gain,
                first_mid_bias,
                first_out_gain,
                first_out_bias,
                second_mid_gain,
                second_mid_bias,
                second_out_gain,
                second_out_bias,
            )
        ]
    )
    half = chan // 2
    few_rows = ROWS // 4

    inputs_of = dict(
        x_tiles=(tiles(inputs), pl.ANY),
        cot_tiles=(tiles(cotangent), pl.ANY),
        gate=(gate, pltpu.VMEM),
        param_in=(param, pltpu.VMEM),
        first_spatial=(first_spatial, pl.ANY),
        first_temporal=(first_temporal, pl.ANY),
        second_spatial=(second_spatial, pl.ANY),
        second_temporal=(second_temporal, pl.ANY),
    )
    outputs_of = dict(
        block_out=((4, side, side * CELL, chan), F32, pl.ANY),
        grad_input=((4, side, side * CELL, chan), F32, pl.ANY),
        norm_grads=((8, mid), F32, pltpu.VMEM),
        out1s=((spat, mid), BF16, pl.ANY),
        out1t=((2, temp, half), BF16, pl.ANY),
        out2s=((spat, mid), BF16, pl.ANY),
        out2t=((2, temp, half), BF16, pl.ANY),
    )
    dma = pltpu.SemaphoreType.DMA
    scratch_of = dict(
        w1s=pltpu.VMEM((9 * chan, mid), BF16),
        w1t=pltpu.VMEM((3 * mid, chan), BF16),
        w2s=pltpu.VMEM((9 * chan, mid), BF16),
        w2t=pltpu.VMEM((3 * mid, chan), BF16),
        x_grid=pltpu.VMEM((8, 8 * CELL, chan), BF16),
        cot_grid=pltpu.VMEM((8, 8 * CELL, chan), BF16),
        out_grid=pltpu.VMEM((8, 8 * CELL, chan), F32),
        xa=pltpu.VMEM((PADDED, chan), BF16),
        xb=pltpu.VMEM((PADDED, chan), BF16),
        aa=pltpu.VMEM((PADDED, chan), BF16),
        ab=pltpu.VMEM((PADDED, chan), BF16),
        ea=pltpu.VMEM((PADDED, mid), BF16),
        eb=pltpu.VMEM((PADDED, mid), BF16),
        mid1=pltpu.VMEM((ROWS, mid), F32),
        mid2=pltpu.VMEM((ROWS, mid), F32),
        grad_mid=pltpu.VMEM((ROWS, mid), F32),
        v1=pltpu.VMEM((ROWS, mid), BF16),
        v2=pltpu.VMEM((ROWS, mid), BF16),
        time1=pltpu.VMEM((ROWS, chan), F32),
        time2=pltpu.VMEM((ROWS, chan), F32),
        grad_pre=pltpu.VMEM((ROWS, chan), F32),
        down=pltpu.VMEM((chan // 128, ROWS + CHUNK, 128), F32),
        up=pltpu.VMEM((chan // 128, ROWS + CHUNK, 128), F32),
        e3=pltpu.VMEM((3, ROWS, chan), BF16),
        sib_e3=pltpu.VMEM((3, ROWS, half), BF16),
        halo_out=pltpu.VMEM((2, few_rows, chan), BF16),
        halo_in=pltpu.VMEM((4, 2, few_rows, chan), BF16),
        param=pltpu.VMEM((8, mid), F32),
        tile_mid=pltpu.VMEM((2, 4, CELL, mid), F32),
        tile_out=pltpu.VMEM((2, 4, CELL, chan), F32),
        back=pltpu.VMEM((2, CELL, mid), F32),
        sum_a=pltpu.VMEM((2, 2, 8, mid), F32),
        sum_b=pltpu.VMEM((2, 4, 8, mid), F32),
        sum_c=pltpu.VMEM((2, nb // 2, 8, mid), F32),
        own_sem=dma((4,)),
        ring_send=dma((4, 2, nb)),
        ring_recv=dma((4, 2, nb)),
        sib_send=dma((4, 3, nb)),
        sib_recv=dma((4, 3, nb)),
        over_send=dma((4, nb)),
        over_recv=dma((4, nb)),
        sa_send=dma((9,)),
        sa_recv=dma((9,)),
        sb_send=dma((9, 3)),
        sb_recv=dma((9, 4)),
        sc_send=dma((9, nb // 2)),
        sc_recv=dma((9, nb // 2)),
        halo_send=dma((4, 2)),
        halo_recv=dma((4, 2)),
        share_send=dma((6,)),
        share_recv=dma((6,)),
        e_all=pltpu.VMEM((4 * ROWS, mid), BF16),
        xq1=pltpu.VMEM((3, 2, PADDED, chan // 4), BF16),
        xq2=pltpu.VMEM((3, 2, PADDED, chan // 4), BF16),
        xt=pltpu.VMEM((mid, 2 * ROWS), BF16),
        sib_v=pltpu.VMEM((ROWS, mid), BF16),
        e_send=dma((2, 3)),
        e_recv=dma((2, 3)),
        xq_send=dma((2, 3, 2)),
        xq_recv=dma((2, 3, 2)),
        y_send=dma((4, 5)),
        y_recv=dma((4, 5)),
        z_send=dma((4, 5)),
        z_recv=dma((4, 7)),
        cast_send=dma((4, 6)),
        cast_recv=dma((4, 8)),
        out_sem=dma((4, 2)),
        tile_send=dma((4, 3)),
        tile_recv=dma((4, 4)),
        tile_own=dma((4,)),
    )
    names = (*inputs_of, *outputs_of, *scratch_of)
    cell_count = float(frames * nb * HGT * HGT)
    results = pl.pallas_call(
        functools.partial(block_kernel, (nb, chan, mid, cell_count), names),
        out_shape=[jax.ShapeDtypeStruct(shape, dtype) for shape, dtype, _ in outputs_of.values()],
        in_specs=[pl.BlockSpec(memory_space=space) for _, space in inputs_of.values()],
        out_specs=[pl.BlockSpec(memory_space=space) for _, _, space in outputs_of.values()],
        scratch_shapes=list(scratch_of.values()),
        compiler_params=pltpu.CompilerParams(
            collective_id=0, has_side_effects=True, vmem_limit_bytes=VMEM_LIMIT
        ),
    )(*(array for array, _ in inputs_of.values()))
    got = SimpleNamespace(**dict(zip(outputs_of, results)))

    def temporal(pair):
        return jnp.concatenate([pair[0], pair[1]], axis=1).astype(F32)

    def norm(row, like):
        size = like.shape[0]
        return lax.dynamic_slice_in_dim(got.norm_grads[row], b * size, size)

    return (
        untiled(got.block_out),
        untiled(got.grad_input),
        got.out1s.astype(F32),
        norm(0, first_mid_gain),
        norm(1, first_mid_bias),
        temporal(got.out1t),
        norm(2, first_out_gain),
        norm(3, first_out_bias),
        got.out2s.astype(F32),
        norm(4, second_mid_gain),
        norm(5, second_mid_bias),
        temporal(got.out2t),
        norm(6, second_out_gain),
        norm(7, second_out_bias),
    )


def extended(shard, sides, width):
    for axis, dim in sides:
        count, length = (lax.axis_size(axis), shard.shape[dim])
        up = [(i, (i + 1) % count) for i in range(count - 1)]
        down = [(j, i) for i, j in up]
        last = lax.slice_in_dim(shard, length - width, length, axis=dim)
        leading = lax.slice_in_dim(shard, 0, width, axis=dim)
        before = lax.ppermute(last, axis, up)
        after = lax.ppermute(leading, axis, down)
        shard = jnp.concatenate([before, shard, after], axis=dim)
    return shard


def passed_along(shard, axis, by):
    count = lax.axis_size(axis)
    pairs = [(i, i + by) for i in range(count) if 0 <= i + by < count]
    return lax.ppermute(shard, axis, pairs)


def for_sending(shard):

    def short(part):
        return part.astype(jnp.bfloat16) if part.dtype == jnp.float32 else part

    return jax.tree.map(short, shard)


def silu_slope(values):
    sigma = jax.nn.sigmoid(values)
    return sigma * (1.0 + values * (1.0 - sigma))


def spatial_forward(field_in, kernel):
    frames, tile_side = (field_in.shape[0], field_in.shape[1])
    padded = extended(field_in, (("ha", 1), ("wa", 2)), 1)
    pieces = [
        padded[:, offset // 3 : offset // 3 + tile_side, offset % 3 : offset % 3 + tile_side, :]
        for offset in range(9)
    ]
    patches = jnp.concatenate(pieces, axis=-1).reshape(frames * tile_side * tile_side, -1)
    return (patches, jnp.dot(patches, kernel, preferred_element_type=jnp.float32))


def spatial_backward(grad_out, patches, kernel):
    frames, tile_side, channels = (grad_out.shape[0], grad_out.shape[1], grad_out.shape[3])
    row_count = frames * tile_side * tile_side
    padded = extended(grad_out, (("ha", 1), ("wa", 2)), 1)
    pieces = [
        padded[
            :,
            2 - offset // 3 : 2 - offset // 3 + tile_side,
            2 - offset % 3 : 2 - offset % 3 + tile_side,
            :,
        ]
        for offset in range(9)
    ]
    stacked = jnp.concatenate(pieces, axis=-1).reshape(row_count, 9, channels)
    grad_in = jnp.einsum(
        "rkm,kcm->rc", stacked, kernel.reshape(9, -1, channels), preferred_element_type=jnp.float32
    )
    grad_kernel = jnp.einsum(
        "rk,rm->km",
        patches,
        grad_out.reshape(row_count, channels),
        preferred_element_type=jnp.float32,
    )
    return (grad_in, grad_kernel)


def temporal_forward(field_in, clip_gate, kernel):
    frames, tile_side = (field_in.shape[0], field_in.shape[1])
    gated_in = field_in * clip_gate
    earlier = passed_along(field_in[-1:], "batch", 1)
    later_frame = passed_along(gated_in[:1], "batch", -1)
    before = jnp.concatenate([earlier, field_in[:-1]], axis=0) * clip_gate
    after_tap = jnp.concatenate([gated_in[1:], later_frame], axis=0)
    joined = jnp.concatenate([before, field_in, after_tap], axis=-1).reshape(
        frames * tile_side * tile_side, -1
    )
    return (joined, jnp.dot(joined, kernel, preferred_element_type=jnp.float32))


def temporal_backward(grad_out, joined, clip_gate, kernel):
    frames, tile_side, channels = (grad_out.shape[0], grad_out.shape[1], grad_out.shape[3])
    row_count = frames * tile_side * tile_side
    gated_grad = grad_out * clip_gate
    later_frame = passed_along(gated_grad[:1], "batch", -1)
    earlier = passed_along(grad_out[-1:], "batch", 1)
    from_later = jnp.concatenate([gated_grad[1:], later_frame], axis=0)
    from_earlier = jnp.concatenate([earlier, grad_out[:-1]], axis=0) * clip_gate
    stacked = jnp.concatenate([from_later, grad_out, from_earlier], axis=-1).reshape(
        row_count, 3, channels
    )
    grad_in = jnp.einsum(
        "rkc,kmc->rm", stacked, kernel.reshape(3, -1, channels), preferred_element_type=jnp.float32
    )
    grad_kernel = jnp.einsum(
        "rk,rc->kc",
        joined,
        grad_out.reshape(row_count, channels),
        preferred_element_type=jnp.float32,
    )
    return (grad_in, grad_kernel)


def norm_forward(pre_norm, norm_gain, norm_bias, valid_rows, cell_count):
    first_sum = jnp.sum(pre_norm * valid_rows, axis=0)
    square_sum = jnp.sum(pre_norm * pre_norm * valid_rows, axis=0)
    first_sum, square_sum = lax.psum((first_sum, square_sum), ("ha", "wa", "batch"))
    mean_val = first_sum / cell_count
    inv_std = lax.rsqrt(square_sum / cell_count - mean_val * mean_val + epsilon)
    normed = (pre_norm - mean_val) * inv_std
    return (normed, inv_std, normed * norm_gain.astype(jnp.float32) + norm_bias.astype(jnp.float32))


def norm_backward(grad_norm, normed, inv_std, norm_gain, valid_rows, cell_count):
    bias_grad = jnp.sum(grad_norm, axis=0)
    gain_grad = jnp.sum(grad_norm * normed, axis=0)
    bias_grad, gain_grad = lax.psum((bias_grad, gain_grad), ("ha", "wa", "batch"))
    grad_in = (
        valid_rows
        * norm_gain.astype(jnp.float32)
        * inv_std
        * (grad_norm - bias_grad / cell_count - normed * gain_grad / cell_count)
    )
    return (grad_in, gain_grad, bias_grad)


def forward_pair(field_in, weights, clip_gate, valid_rows, cell_count):
    frames, tile_side = (field_in.shape[0], field_in.shape[1])
    patches, spatial_out = spatial_forward(field_in, weights[0])
    mid_hat, mid_scale, mid_norm = norm_forward(
        spatial_out, weights[1], weights[2], valid_rows, cell_count
    )
    hidden = (
        (jax.nn.silu(mid_norm) * valid_rows)
        .astype(jnp.bfloat16)
        .reshape(frames, tile_side, tile_side, -1)
    )
    joined, temporal_out = temporal_forward(hidden, clip_gate, weights[3])
    out_hat, out_scale, out_norm = norm_forward(
        temporal_out, weights[4], weights[5], valid_rows, cell_count
    )
    return ((patches, mid_hat, mid_scale, mid_norm, joined, out_hat, out_scale), out_norm)


def backward_pair(grad_norm, kept, weights, clip_gate, valid_rows, cell_count, tile_side):
    patches, mid_hat, mid_scale, mid_norm, joined, out_hat, out_scale = kept
    frames = clip_gate.shape[0]
    grad_time, out_gain_grad, out_bias_grad = norm_backward(
        grad_norm, out_hat, out_scale, weights[4], valid_rows, cell_count
    )
    grad_time = grad_time.astype(jnp.bfloat16).reshape(frames, tile_side, tile_side, -1)
    grad_hidden, temporal_grad = temporal_backward(grad_time, joined, clip_gate, weights[3])
    grad_mid = grad_hidden * valid_rows * silu_slope(mid_norm)
    grad_spatial, mid_gain_grad, mid_bias_grad = norm_backward(
        grad_mid, mid_hat, mid_scale, weights[1], valid_rows, cell_count
    )
    grad_spatial = grad_spatial.astype(jnp.bfloat16).reshape(frames, tile_side, tile_side, -1)
    grad_in, spatial_grad = spatial_backward(grad_spatial, patches, weights[0])
    return (
        grad_in,
        (spatial_grad, mid_gain_grad, mid_bias_grad, temporal_grad, out_gain_grad, out_bias_grad),
    )


def per_device(
    inputs,
    starts,
    first_spatial,
    first_mid_gain,
    first_mid_bias,
    first_temporal,
    first_out_gain,
    first_out_bias,
    second_spatial,
    second_mid_gain,
    second_mid_bias,
    second_temporal,
    second_out_gain,
    second_out_bias,
    cotangent,
):
    shards = (
        first_spatial,
        first_mid_gain,
        first_mid_bias,
        first_temporal,
        first_out_gain,
        first_out_bias,
        second_spatial,
        second_mid_gain,
        second_mid_bias,
        second_temporal,
        second_out_gain,
        second_out_bias,
    )
    micro_total, frames, tile_side, channels = (
        inputs.shape[0],
        inputs.shape[1],
        inputs.shape[2],
        inputs.shape[4],
    )
    row_count = frames * tile_side * tile_side
    cell_count = frames * lax.axis_size("batch") * HGT * HGT
    offsets = jnp.arange(tile_side)
    inside_h = lax.axis_index("ha") * tile_side + offsets < HGT
    inside_w = lax.axis_index("wa") * tile_side + offsets < HGT
    valid_grid = inside_h[:, None] & inside_w[None, :]
    valid_tile = valid_grid.astype(jnp.bfloat16)[None, :, :, None]
    valid_rows = jnp.broadcast_to(
        valid_grid.astype(jnp.float32)[None], (frames, tile_side, tile_side)
    ).reshape(row_count, 1)
    results = []
    input_grads = []
    kernel_total = None
    norm_total = None
    for micro_step in range(micro_total):
        gathered = (
            lax.all_gather(shards[0], "batch", axis=0, tiled=True),
            lax.all_gather(shards[1], "batch", axis=0, tiled=True),
            lax.all_gather(shards[2], "batch", axis=0, tiled=True),
            lax.all_gather(shards[3], "batch", axis=0, tiled=True),
            lax.all_gather(shards[4], "batch", axis=0, tiled=True),
            lax.all_gather(shards[5], "batch", axis=0, tiled=True),
            lax.all_gather(shards[6], "batch", axis=0, tiled=True),
            lax.all_gather(shards[7], "batch", axis=0, tiled=True),
            lax.all_gather(shards[8], "batch", axis=0, tiled=True),
            lax.all_gather(shards[9], "batch", axis=0, tiled=True),
            lax.all_gather(shards[10], "batch", axis=0, tiled=True),
            lax.all_gather(shards[11], "batch", axis=0, tiled=True),
        )
        clip_gate = (1 - starts[micro_step]).astype(jnp.bfloat16).reshape(frames, 1, 1, 1)
        x_in = inputs[micro_step] * valid_tile
        first_kept, first_norm = forward_pair(
            x_in, gathered[0:6], clip_gate, valid_rows, cell_count
        )
        first_act = (
            (jax.nn.silu(first_norm) * valid_rows)
            .astype(jnp.bfloat16)
            .reshape(frames, tile_side, tile_side, channels)
        )
        second_kept, second_norm = forward_pair(
            first_act, gathered[6:12], clip_gate, valid_rows, cell_count
        )
        pre_out = second_norm + x_in.reshape(row_count, channels).astype(jnp.float32)
        results.append(
            (jax.nn.silu(pre_out) * valid_rows).reshape(frames, tile_side, tile_side, channels)
        )
        grad_pre = (
            cotangent[micro_step].reshape(row_count, channels).astype(jnp.float32)
            * valid_rows
            * silu_slope(pre_out)
        )
        grad_act, second_grads = backward_pair(
            grad_pre, second_kept, gathered[6:12], clip_gate, valid_rows, cell_count, tile_side
        )
        grad_first = grad_act * valid_rows * silu_slope(first_norm)
        grad_conv, first_grads = backward_pair(
            grad_first, first_kept, gathered[0:6], clip_gate, valid_rows, cell_count, tile_side
        )
        input_grads.append(
            ((grad_conv + grad_pre) * valid_rows).reshape(frames, tile_side, tile_side, channels)
        )
        step_grads = first_grads + second_grads
        kernel_now = (step_grads[0], step_grads[3], step_grads[6], step_grads[9])
        norm_now = (
            step_grads[1],
            step_grads[2],
            step_grads[4],
            step_grads[5],
            step_grads[7],
            step_grads[8],
            step_grads[10],
            step_grads[11],
        )
        if micro_step == 0:
            kernel_total = kernel_now
            norm_total = norm_now
        else:
            kernel_total = jax.tree.map(jnp.add, kernel_total, kernel_now)
            norm_total = jax.tree.map(jnp.add, norm_total, norm_now)
    kernel_total = lax.psum_scatter(kernel_total, "batch", scatter_dimension=0, tiled=True)
    kernel_total = jax.tree.map(
        lambda part: part.astype(jnp.float32), lax.psum(for_sending(kernel_total), ("ha", "wa"))
    )
    shard_index = lax.axis_index("batch")
    batch_count = lax.axis_size("batch")
    norm_shards = tuple(
        (
            lax.dynamic_slice_in_dim(
                full_sum,
                shard_index * (full_sum.shape[0] // batch_count),
                full_sum.shape[0] // batch_count,
            )
            for full_sum in norm_total
        )
    )
    return (
        jnp.stack(results),
        jnp.stack(input_grads),
        kernel_total[0],
        norm_shards[0],
        norm_shards[1],
        kernel_total[1],
        norm_shards[2],
        norm_shards[3],
        kernel_total[2],
        norm_shards[4],
        norm_shards[5],
        kernel_total[3],
        norm_shards[6],
        norm_shards[7],
    )


def solution(mesh):
    in_specs = (
        P(None, "batch", "ha", "wa", None),
        P(None, "batch"),
        P("batch", None),
        P("batch"),
        P("batch"),
        P("batch", None),
        P("batch"),
        P("batch"),
        P("batch", None),
        P("batch"),
        P("batch"),
        P("batch", None),
        P("batch"),
        P("batch"),
        P(None, "batch", "ha", "wa", None),
    )
    out_specs = (
        P(None, "batch", "ha", "wa", None),
        P(None, "batch", "ha", "wa", None),
        P("batch", None),
        P("batch"),
        P("batch"),
        P("batch", None),
        P("batch"),
        P("batch"),
        P("batch", None),
        P("batch"),
        P("batch"),
        P("batch", None),
        P("batch"),
        P("batch"),
    )
    batch = mesh.shape["batch"]

    def program(*args):
        spat, temp = args[2].shape[0], args[5].shape[0]
        fits = args[0].shape == (2, 16, 4, 4, 512) and args[2].shape[1] == 1152
        if fits and batch == 8 and spat * batch == 9 * 512 and temp * batch == 3 * 1152:
            return per_device_fast(batch, *args)
        return per_device(*args)

    return jax.shard_map(
        program, mesh=mesh, in_specs=in_specs, out_specs=out_specs, check_vma=False
    )
```

```python
import functools
from types import SimpleNamespace

import jax
import jax.numpy as jnp
from jax import lax
from jax.experimental import pallas as pl
from jax.experimental.pallas import tpu as pltpu
from jax.sharding import PartitionSpec as P

HGT = 7
epsilon = 1e-05
MESH = pl.DeviceIdType.MESH
F32 = jnp.float32
BF16 = jnp.bfloat16

BASE = 10
CELL = 8
ROWS = HGT * 8 * CELL
PADDED = (BASE + HGT * 8 + BASE) * CELL
MAIN = BASE * CELL
CHUNK = 2 * CELL
CHUNKS = ROWS // CHUNK
VMEM_LIMIT = 64 * 1024 * 1024 - 1024 * 1024


def when(cond, work):
    if cond is True:
        work()
    elif cond is not False:
        pl.when(cond)(work)


def loop(count, body, init):
    def twice(i, carry):
        return body(2 * i + 1, body(2 * i, carry))

    return lax.fori_loop(0, count // 2, twice, init)


def nn(a, b):
    return jnp.dot(a, b, preferred_element_type=F32)


def nt(a, b):
    return lax.dot_general(a, b, (((1,), (1,)), ((), ())), preferred_element_type=F32)


def tn(a, b):
    return lax.dot_general(a, b, (((0,), (0,)), ((), ())), preferred_element_type=F32)


def rows_of(start, size, step=16):
    if not isinstance(start, int):
        start = pl.multiple_of(start, step)
    return pl.ds(start, size)


def per_batch(first, second, width):
    return jnp.concatenate(
        [jnp.broadcast_to(first, (CELL // 2, width)), jnp.broadcast_to(second, (CELL // 2, width))], axis=0
    )


def block_kernel(dims, names, *all_refs):
    r = SimpleNamespace(**dict(zip(names, all_refs, strict=True)))
    nb, chan, mid, cell_count = dims
    spat = 9 * chan // nb
    temp = 3 * mid // nb
    unit = spat // 6
    quarter = chan // 4
    half = chan // 2
    h = lax.axis_index("ha")
    w = lax.axis_index("wa")
    b = lax.axis_index("batch")
    par = lax.rem(b, 2)
    bh = lax.div(b, 2)
    pos = par * (nb - 1 - bh) + (1 - par) * bh
    way = 1 - 2 * h

    def at(p):
        p = lax.rem(p + 4 * nb, nb)
        upper = lax.div(p, nb // 2)
        return (1 - upper) * (2 * p) + upper * (2 * (nb - 1 - p) + 1)

    def at_group(j):
        jw = lax.div(j, 2)
        odd = lax.rem(j, 2)
        return (odd * (1 - jw) + (1 - odd) * jw, jw)

    mine = (1 - w) * h + w * (3 - h)
    sibling = (1 - h, w, b)
    beside = (h, 1 - w, b)
    onward = (h, w, at(pos + way))
    behind = (h, w, at(pos - way))
    later = lax.rem(mine + 1, 4)
    earlier = lax.rem(mine + 3, 4)
    later_dev = (*at_group(later), lax.rem(b + lax.div(mine + 1, 4), nb))
    earlier_dev = (*at_group(earlier), lax.rem(b + nb - lax.div(4 - mine, 4), nb))
    tile_group = [(lax.rem(mine + d, 4), (*at_group(lax.rem(mine + d, 4)), b)) for d in (1, 2, 3)]
    pos_b = w * 2 + par
    plane = []
    for d in (1, 2, 3):
        q = lax.rem(pos_b + d, 4)
        plane.append((q, (h, lax.div(q, 2), b - par + lax.rem(q, 2))))
    depth = nb // 2
    line = []
    for d in range(1, depth):
        q = lax.rem(bh + d, depth)
        line.append((q, (h, w, 2 * q + par)))

    def named(dev):
        return dict(ha=dev[0], wa=dev[1], batch=dev[2])

    def rc(src, dst, send, recv, dev):
        return pltpu.make_async_remote_copy(
            src_ref=src, dst_ref=dst, send_sem=send, recv_sem=recv, device_id=named(dev), device_id_type=MESH
        )

    def lc(src, dst, sem):
        return pltpu.make_async_copy(src, dst, sem)

    partners = [sibling, beside, onward, behind, later_dev, earlier_dev]
    partners += [dev for _, dev in tile_group + plane + line]
    barrier = pltpu.get_barrier_semaphore()
    for dev in partners:
        pl.semaphore_signal(barrier, inc=1, device_id=named(dev), device_id_type=MESH)
    pl.semaphore_wait(barrier, len(partners))

    shards = (r.first_spatial, r.first_temporal, r.second_spatial, r.second_temporal)
    whole = (r.w1s, r.w1t, r.w2s, r.w2t)
    shared = 2 * w + h
    shared_beside = 2 * (1 - w) + h
    own_units = (shared, 4 + h)

    def piece(i, ref, owner, u):
        if i % 2 == 0:
            return ref.at[rows_of(owner * spat + u * unit, unit), :]
        return ref.at[rows_of(owner * temp, temp), rows_of(u * quarter, quarter, 128)]

    def streams(i):
        return (0, 1) if i % 2 == 0 else (0,)

    def own_copy(i):
        rows = spat if i % 2 == 0 else temp
        return lc(shards[i], whole[i].at[rows_of(b * rows, rows), :], r.own_sem.at[i])

    def ring(i, st, s, owner, from_shard=False):
        dst = piece(i, whole[i], owner, own_units[st])
        src = piece(i, shards[i], 0, own_units[st]) if from_shard else dst
        return rc(src, dst, r.ring_send.at[i, st, s], r.ring_recv.at[i, st, s], onward)

    def cross(i, kind, s, owner, u):
        part = piece(i, whole[i], owner, u)
        return rc(part, part, r.sib_send.at[i, kind, s], r.sib_recv.at[i, kind, s], sibling)

    def over(i, s, owner, u):
        part = piece(i, whole[i], owner, u)
        return rc(part, part, r.over_send.at[i, s], r.over_recv.at[i, s], beside)

    def gather_start(i):
        for st in streams(i):
            ring(i, st, 1, b, True).start()
        own_copy(i).start()

    def gather_relay(i, s):
        owner = at(pos - way * s)
        over(i, s, owner, shared_beside).wait_recv()
        cross(i, 2, s, owner, shared_beside).start()

    def gather_pump(i, s):
        owner = at(pos - way * s)
        for st in streams(i):
            ring(i, st, s, owner).wait_recv()
            if isinstance(s, int):
                if s < nb - 1:
                    ring(i, st, s + 1, owner).start()
            else:
                pl.when(s < nb - 1)(lambda st=st: ring(i, st, s + 1, owner).start())
            cross(i, st, s, owner, own_units[st]).start()
            if st == 0:
                over(i, s, owner, shared).start()
        if isinstance(s, int):
            if s > 1:
                gather_relay(i, s - 1)
        else:
            pl.when(s > 1)(lambda: gather_relay(i, s - 1))

    def gather_finish(i):
        gather_relay(i, nb - 1)

        def body(s, _):
            owner = at(pos - way * s)
            theirs = at(pos + way * s)
            for st in streams(i):
                ring(i, st, s, owner).wait_send()
                cross(i, st, s, owner, own_units[st]).wait_send()
                cross(i, st, s, theirs, (2 * w + 1 - h, 5 - h)[st]).wait_recv()
            over(i, s, owner, shared).wait_send()
            cross(i, 2, s, owner, shared_beside).wait_send()
            cross(i, 2, s, theirs, 2 * (1 - w) + 1 - h).wait_recv()
            return 0

        lax.fori_loop(1, nb, body, 0)
        own_copy(i).wait()

    def total(k, width, value, works=()):
        slot = k % 2
        wide = value.shape[1]
        cols = pl.ds(0, wide)
        works = list(works) + [None] * 3
        pair, four, far = r.sum_a, r.sum_b, r.sum_c
        pair[slot, h, :, cols] = value
        part = pair.at[slot, h, :, cols]
        send_a = rc(part, part, r.sa_send.at[k], r.sa_recv.at[k], sibling)
        send_a.start()
        if works[0]:
            works[0]()
        part = pair.at[slot, 1 - h, :, cols]
        rc(part, part, r.sa_send.at[k], r.sa_recv.at[k], sibling).wait_recv()
        four[slot, pos_b, :, cols] = pair[slot, 0, :, cols] + pair[slot, 1, :, cols]
        sends = [send_a]
        for n, (q, dev) in enumerate(plane):
            part = four.at[slot, pos_b, :, cols]
            sends.append(rc(part, part, r.sb_send.at[k, n], r.sb_recv.at[k, pos_b], dev))
            sends[-1].start()
        if works[1]:
            works[1]()
        for n, (q, dev) in enumerate(plane):
            part = four.at[slot, q, :, cols]
            rc(part, part, r.sb_send.at[k, n], r.sb_recv.at[k, q], dev).wait_recv()
        far[slot, bh, :, cols] = (four[slot, 0, :, cols] + four[slot, 1, :, cols]) + (
            four[slot, 2, :, cols] + four[slot, 3, :, cols]
        )
        for n, (q, dev) in enumerate(line):
            part = far.at[slot, bh, :, cols]
            sends.append(rc(part, part, r.sc_send.at[k, n], r.sc_recv.at[k, bh], dev))
            sends[-1].start()
        if works[2]:
            works[2]()
        for n, (q, dev) in enumerate(line):
            part = far.at[slot, q, :, cols]
            rc(part, part, r.sc_send.at[k, n], r.sc_recv.at[k, q], dev).wait_recv()
        result = far[slot, 0, :, cols]
        for q in range(1, depth):
            result = result + far[slot, q, :, cols]
        for send in sends:
            send.wait_send()
        if wide == width:
            return result
        return jnp.concatenate([result[0:4], result[4:8, 2 * wide - width :]], axis=1)

    def chunk(ref, i, base=0, width=None):
        cols = slice(None) if width is None else pl.ds(0, width)
        value = ref[rows_of(base + i * CHUNK, CHUNK), cols]
        return value.astype(F32).reshape(2, CELL, value.shape[-1])

    def put(ref, i, value, base=0, width=None):
        cols = slice(None) if width is None else pl.ds(0, width)
        ref[rows_of(base + i * CHUNK, CHUNK), cols] = value.reshape(CHUNK, value.shape[-1]).astype(ref.dtype)

    def keep(i):
        inside = jnp.where(lax.rem(i, 4) == 3, 0.0, 1.0).astype(F32)
        first = lax.broadcasted_iota(jnp.int32, (2, 1, 1), 0) == 0
        return jnp.where(first, 1.0, inside)

    def packed(one, two, width):
        rows = [
            jnp.sum(v[k : k + CELL // 2], axis=0, keepdims=True) for v in (one, two) for k in (0, CELL // 2)
        ]
        rows = jnp.concatenate(rows, axis=0)
        wide = -(-width // 256) * 128
        return jnp.concatenate([rows[:, 0:wide], rows[:, width - wide :]], axis=0)

    def moments(ref, width):
        def body(i, carry):
            v = chunk(ref, i)
            m = v * keep(i)
            return (carry[0] + m[0] + m[1], carry[1] + m[0] * v[0] + m[1] * v[1])

        zero = jnp.zeros((CELL, width), F32)
        return loop(CHUNKS, body, (zero, zero))

    def prepare(n, sums, width):
        tile = r.tile_mid if width == mid else r.tile_out
        n2 = n // 2
        gain = r.param[2 * n : 2 * n + 1, 0:width]
        bias = r.param[2 * n + 1 : 2 * n + 2, 0:width]
        mean = sums[0:2] / cell_count
        inv = lax.rsqrt(sums[2:4] / cell_count - mean * mean + epsilon)
        scale = inv * gain
        shift = bias - mean * scale
        for k, v in enumerate((scale, shift, inv, mean * inv)):
            tile[n2, k] = per_batch(v[0:1], v[1:2], width)

    def tiles(n, width):
        tile = r.tile_mid if width == mid else r.tile_out
        return [tile[n // 2, k][None] for k in range(4)]

    def fill(ref_a, ref_b, value_of, width):
        ref_a[0:MAIN, :] = jnp.zeros((MAIN, width), BF16)
        ref_a[MAIN + ROWS : PADDED, :] = jnp.zeros((PADDED - MAIN - ROWS, width), BF16)
        ref_b[0 : MAIN - CHUNK, :] = jnp.zeros((MAIN - CHUNK, width), BF16)
        ref_b[MAIN - CHUNK + ROWS : PADDED, :] = jnp.zeros((PADDED - MAIN + CHUNK - ROWS, width), BF16)

        def body(i, before):
            v = value_of(i)
            put(ref_a, i, v, MAIN)
            pair = jnp.concatenate([before[None], v[0:1]], axis=0)
            put(ref_b, i, pair, MAIN - CHUNK)
            return v[1]

        loop(CHUNKS, body, jnp.zeros((CELL, width), F32))

    def activated(src, n, width):
        def value(i):
            scale, shift, _, _ = tiles(n, width)
            y = chunk(src, i) * scale + shift
            return y * jax.nn.sigmoid(y) * keep(i)

        return value

    def taps(ref_a, ref_b, k, size=ROWS):
        r0 = MAIN - 8 * CELL + 8 * CELL * k
        return (
            ref_b[rows_of(r0 - CHUNK, size), :],
            ref_a[rows_of(r0, size), :],
            ref_b[rows_of(r0, size), :],
        )

    def conv(ref_a, ref_b, weight, out, pump=None):
        for n, (c0, cw) in enumerate(((0, 512), (512, mid - 512))):

            def body(a, _, c0=c0, cw=cw, n=n):
                x = taps(ref_a, ref_b, a)
                acc = nn(jnp.concatenate(x, axis=1), weight[rows_of(a * 3 * chan, 3 * chan), c0 : c0 + cw])

                @pl.when(a == 0)
                def _():
                    out[:, c0 : c0 + cw] = acc

                @pl.when(a > 0)
                def _():
                    out[:, c0 : c0 + cw] += acc

                if pump is not None:
                    pump(n * 3 + a)
                return 0

            lax.fori_loop(0, 3, body, 0)

    def conv_back(ref_a, ref_b, weight, out, pump=None):
        def body(k, _):
            e = taps(ref_a, ref_b, k)
            acc = None
            for j in range(3):
                tap = 8 - 3 * k - j
                term = nt(e[j], weight[rows_of(tap * chan, chan), :])
                acc = term if acc is None else acc + term

            @pl.when(k == 0)
            def _():
                out[:, 0:chan] = acc

            @pl.when(k > 0)
            def _():
                out[:, 0:chan] += acc

            if pump is not None:
                pump(k)
            return 0

        lax.fori_loop(0, 3, body, 0)

    def send_frames(k):
        down, up = r.down, r.up
        count = ROWS // 4
        for c in range(chan // 128):
            lanes = pl.ds(128 * c, 128)
            r.halo_out[0, :, lanes] = down[c, pl.ds(CELL + 3, count, stride=4), :].astype(BF16)
            r.halo_out[1, :, lanes] = up[c, pl.ds(0, count, stride=4), :].astype(BF16)
        copies = []
        for n, dev in ((0, later_dev), (1, earlier_dev)):
            copies.append(
                rc(r.halo_out.at[n], r.halo_in.at[k, n], r.halo_send.at[k, n], r.halo_recv.at[k, n], dev)
            )
            copies[-1].start()
        return copies

    def take_frames(k, copies):
        down, up = r.down, r.up
        count = ROWS // 4
        for copy in copies:
            copy.wait()
        at_start = jnp.logical_and(mine == 0, b == 0)
        at_end = jnp.logical_and(mine == 3, b == nb - 1)
        for c in range(chan // 128):
            lanes = pl.ds(128 * c, 128)
            before = r.halo_in[k, 0, :, lanes].astype(F32)
            after = r.halo_in[k, 1, :, lanes].astype(F32)
            down[c, pl.ds(CELL - 1, count, stride=4), :] = jnp.where(at_start, 0.0, before)
            up[c, pl.ds(4, count, stride=4), :] = jnp.where(at_end, 0.0, after)

    def by_lanes(ref, rows):
        return jnp.concatenate([ref[c, rows, :] for c in range(chan // 128)], axis=1)

    def put_lanes(ref, rows, value):
        for c in range(chan // 128):
            ref[c, rows, :] = value[:, 128 * c : 128 * c + 128]

    def shifted(i):
        before = by_lanes(r.down, rows_of(i * CHUNK, CHUNK + CELL))[CELL - 1 : CELL - 1 + CHUNK]
        after = by_lanes(r.up, rows_of(i * CHUNK, CHUNK + CELL))[1 : 1 + CHUNK]
        gate = r.gate[...][None]
        return (before.reshape(2, CELL, chan) * gate, after.reshape(2, CELL, chan))

    def temporal(k, v, weight, out, works=()):
        works = list(works) + [None] * 2
        put_lanes(r.down, pl.ds(CELL, ROWS), nn(v[...], weight[0:mid, :]))
        y2 = nn(v[...], weight[2 * mid : 3 * mid, :])
        y2 = (y2.reshape(ROWS // CELL, CELL, chan) * r.gate[...][None]).reshape(ROWS, chan)
        put_lanes(r.up, pl.ds(0, ROWS), y2)
        copies = send_frames(k)
        out[...] = nn(v[...], weight[mid : 2 * mid, :])
        if works[0]:
            works[0]()
        take_frames(k, copies)

        def body(i, carry):
            before, after = shifted(i)
            value = chunk(out, i) + before + after
            put(out, i, value)
            m = value * keep(i)
            return (carry[0] + m[0] + m[1], carry[1] + m[0] * value[0] + m[1] * value[1])

        zero = jnp.zeros((CELL, chan), F32)
        return loop(CHUNKS, body, (zero, zero))

    def temporal_back(k, weight, works=()):
        works = list(works) + [None] * 2
        copies = send_frames(k)
        e3 = r.e3
        for c0, cw in ((0, 512), (512, mid - 512)):
            r.grad_mid[:, c0 : c0 + cw] = nt(e3[1], weight[mid + c0 : mid + c0 + cw, :])
        if works[0]:
            works[0]()
        take_frames(k, copies)

        def body(i, _):
            before, after = shifted(i)
            e3[0, rows_of(i * CHUNK, CHUNK), :] = after.reshape(CHUNK, chan).astype(BF16)
            e3[2, rows_of(i * CHUNK, CHUNK), :] = before.reshape(CHUNK, chan).astype(BF16)
            return 0

        loop(CHUNKS, body, 0)
        share = share_e3(k)
        for c0, cw in ((0, 512), (512, mid - 512)):
            r.grad_mid[:, c0 : c0 + cw] += nt(e3[0], weight[c0 : c0 + cw, :]) + nt(
                e3[2], weight[2 * mid + c0 : 2 * mid + c0 + cw, :]
            )
        return share

    def share(k, src, dst):
        copy = rc(src, dst, r.share_send.at[k], r.share_recv.at[k], sibling)
        copy.start()
        return copy

    outs = (r.out1s, r.out1t, r.out2s, r.out2t)

    halves = ((0, 512), (512, mid - 512))

    def e_part(n, slot):
        c0, cw = halves[n]
        return r.e_all.at[slot * ROWS : (slot + 1) * ROWS, c0 : c0 + cw]

    def e_copies(k, n):
        sems = [(r.e_send.at[k, n, m], r.e_recv.at[k, n, m]) for m in range(3)]
        return [
            rc(e_part(n, 0), e_part(n, 1), *sems[0], sibling),
            rc(e_part(n, 0), e_part(n, 2), *sems[1], beside),
            rc(e_part(n, 2), e_part(n, 3), *sems[2], sibling),
        ]

    def share_e(k):
        for n in (0, 1):
            near, over, _ = e_copies(k, n)
            over.start()
            near.start()

    def share_e_on(k, n):
        _, over, far = e_copies(k, n)
        over.wait_recv()
        far.start()

    def share_e_wait(k, n):
        near, over, far = e_copies(k, n)
        near.wait()
        over.wait_send()
        far.wait()

    def share_x(k, xa, xb, xq):
        copies = []
        for n, dev in enumerate((sibling, beside, (1 - h, 1 - w, b))):
            lanes = rows_of((2 * dev[1] + dev[0]) * quarter, quarter, 128)
            for c, ref in enumerate((xa, xb)):
                copies.append(
                    rc(ref.at[:, lanes], xq.at[n, c], r.xq_send.at[k, n, c], r.xq_recv.at[k, n, c], dev)
                )
                copies[-1].start()
        return copies

    def share_e3(k):
        return share(
            k - 2, r.e3.at[:, :, rows_of((1 - h) * half, half, 128)], r.sib_e3
        )

    def grad_tap(owner):
        return owner + jnp.where(owner > 2 * shared, 1, 0)

    spare = r.w2s

    def gq(i, row, size):
        return rows_of((mid if i == 0 else 0) + row, size)

    def inbox(i, row, size):
        return rows_of(2 * mid + (mid if i == 0 else 0) + row, size)

    def transpose_x(a, xa, xb, xq, near, far, row):
        lanes = rows_of(shared * quarter, quarter, 128)
        r0 = MAIN - 8 * CELL + 8 * CELL * a
        for j, (c, start) in enumerate(((1, r0 - CHUNK), (0, r0), (1, r0))):
            rows = rows_of(start, ROWS)
            own = (xb if c else xa)[rows, lanes]
            both = jnp.concatenate([own, xq[0, c, rows, :]], axis=0)
            near[rows_of(row + j * quarter, quarter), 0 : 2 * ROWS] = both.T
            both = jnp.concatenate([xq[1, c, rows, :], xq[2, c, rows, :]], axis=0)
            far[rows_of(row + j * quarter, quarter), 0 : 2 * ROWS] = both.T

    def spatial_part(i, near, far, row, out_row, n):
        c0, cw = halves[n]
        rows = rows_of(row, 3 * quarter)
        acc = nn(near[rows, 0 : 2 * ROWS], r.e_all[0 : 2 * ROWS, c0 : c0 + cw])
        acc += nn(far[rows, 0 : 2 * ROWS], r.e_all[2 * ROWS : 4 * ROWS, c0 : c0 + cw])
        spare[gq(i, out_row, 3 * quarter), c0 : c0 + cw] = acc.astype(BF16)

    def spatial_grad(i, xa, xb, xq):
        def body(a, _):
            low = r.xt.at[3 * quarter : 6 * quarter, :]
            transpose_x(a, xa, xb, xq, r.xt, low, 0)
            for n in (0, 1):
                spatial_part(i, r.xt, low, 0, a * 3 * quarter, n)
            return 0

        lax.fori_loop(0, 3, body, 0)

    def transpose_v(v, sv):
        for c in range(mid // 128):
            lanes = pl.ds(128 * c, 128)
            r.xt[128 * c : 128 * c + 128, :] = jnp.concatenate([v[:, lanes], sv[:, lanes]], axis=0).T

    def temporal_grad(i, k):
        e = jnp.concatenate([r.e3[k, :, rows_of(h * half, half, 128)], r.sib_e3[k]], axis=0)
        whole[i][k * mid : (k + 1) * mid, 0:half] = nn(r.xt[...], e).astype(BF16)

    def cols_of(n):
        c0, cw = halves[n]
        return pl.ds(c0, cw)

    def s_block(i, n, owner):
        return spare.at[gq(i, grad_tap(owner) * quarter, quarter), cols_of(n)]

    def s_extra(i, n, side):
        return spare.at[gq(i, (2 * shared + 1) * quarter + side * 64, 64), cols_of(n)]

    def t_block(i, owner):
        return whole[i].at[rows_of(owner * temp, temp), 0:half]

    def t_inbox(i, n):
        return whole[i].at[rows_of(n * temp, temp), half:chan]

    def parts_of(i):
        return (0, 1) if i % 2 == 0 else (0,)

    def block_of(i, n, owner):
        return s_block(i, n, owner) if i % 2 == 0 else t_block(i, owner)

    def y_box(i, n, place):
        return spare.at[inbox(i, place * quarter, quarter), cols_of(n)] if i % 2 == 0 else t_inbox(i, place)

    def z_box(i, n, place):
        return spare.at[inbox(i, 576 + place * quarter, quarter), cols_of(n)] if i % 2 == 0 else t_inbox(i, 4 + place)

    def extra_y_box(i, n):
        return spare.at[inbox(i, 4 * quarter, 64), cols_of(n)]

    def extra_z_box(i, n, place):
        return spare.at[inbox(i, 576 + 3 * quarter + place * 64, 64), cols_of(n)]

    across = (h, w, b + 1 - 2 * par)

    def add_into(dst, parts, step):
        rows, cols = dst.shape

        def body(n, _):
            at_rows = rows_of(n * step, step)
            value = dst[at_rows, :].astype(F32)
            for part in parts:
                value = value + part[at_rows, :].astype(F32)
            dst[at_rows, :] = value.astype(BF16)
            return 0

        lax.fori_loop(0, rows // step, body, 0)

    def y_copy(i, n, d):
        place = lax.rem(bh + d, depth)
        src = block_of(i, n, 2 * place + 1 - par)
        return rc(src, y_box(i, n, place), r.y_send.at[i, n, d], r.y_recv.at[i, n, place], across)

    def z_copy(i, n, d):
        place = lax.rem(bh + d, depth)
        src = block_of(i, n, 2 * place + par)
        dev = (h, w, 2 * place + par)
        return rc(src, z_box(i, n, 3 - d), r.z_send.at[i, n, d], r.z_recv.at[i, n, 3 - d], dev)

    def extra_y(i, n):
        return rc(s_extra(i, n, 1 - par), extra_y_box(i, n), r.y_send.at[i, n, 4], r.y_recv.at[i, n, 4], across)

    def extra_z(i, n):
        place = jnp.minimum(lax.rem(bh - shared + 3 + depth, depth), 2)
        dev = (h, w, 2 * shared + par)
        return rc(
            s_extra(i, n, par), extra_z_box(i, n, place), r.z_send.at[i, n, 4], r.z_recv.at[i, n, 4 + place], dev
        )

    def step_of(i):
        return 16 if i % 2 == 0 else 48

    def reduce_start(i, n):
        for d in (1, 2, 3, 0):
            y_copy(i, n, d).start()
        if i % 2 == 0:
            extra_y(i, n).start()

    def reduce_middle(i, n):
        for d in (1, 2, 3, 0):
            place = lax.rem(bh + d, depth)
            y_copy(i, n, d).wait_send()
            box = y_box(i, n, place)
            rc(box, box, r.y_send.at[i, n, d], r.y_recv.at[i, n, place], across).wait_recv()
            add_into(block_of(i, n, 2 * place + par), [box], step_of(i))
            if d:
                z_copy(i, n, d).start()
        if i % 2 == 0:
            extra_y(i, n).wait()
            add_into(s_extra(i, n, par), [extra_y_box(i, n)], 16)
            pl.when(bh != shared)(lambda: extra_z(i, n).start())

    def final_copies(i, n):
        if i % 2:
            src = t_block(i, b)
            part = outs[i].at[h]
            return lc(src, part, r.out_sem.at[i, 0, 0]), [
                (src, part, sibling, r.cast_send.at[i, 0, 0], r.cast_recv.at[i, 0, 0])
            ]
        src = s_block(i, n, b)
        start = quarter * shared - 64 * b + 512 * jnp.where(b > 2 * shared, 1, 0)
        part = outs[i].at[rows_of(start, quarter, 64), cols_of(n)]
        sends = [
            (src, part, dev, r.cast_send.at[i, n, d], r.cast_recv.at[i, n, mine])
            for d, (j, dev) in enumerate(tile_group)
        ]
        return lc(src, part, r.out_sem.at[i, n, 0]), sends

    def extra_copies(i, n):
        src = s_extra(i, n, par)
        part = outs[i].at[rows_of(512 * (1 - par), 64, 64), cols_of(n)]
        sends = [
            (src, part, dev, r.cast_send.at[i, n, 3 + d], r.cast_recv.at[i, n, 4 + mine])
            for d, (j, dev) in enumerate(tile_group)
        ]
        return lc(src, part, r.out_sem.at[i, n, 1]), sends

    def begin(copies):
        local, sends = copies
        for src, part, dev, one, two in sends:
            rc(src, part, one, two, dev).start()
        local.start()

    def beside_copy(i):
        return rc(t_block(i, b), t_inbox(i, 7), r.z_send.at[i, 0, 4], r.z_recv.at[i, 0, 4], beside)

    def reduce_last(i, n):
        for d in (1, 2, 3):
            z_copy(i, n, d).wait()
        add_into(block_of(i, n, b), [z_box(i, n, place) for place in range(3)], step_of(i))
        if i % 2:
            beside_copy(i).start()
            return
        begin(final_copies(i, n))

        @pl.when(bh != shared)
        def _():
            extra_z(i, n).wait_send()

        @pl.when(bh == shared)
        def _():
            boxes = [extra_z_box(i, n, place) for place in range(3)]
            for place, box in enumerate(boxes):
                rc(box, box, r.z_send.at[i, n, 4], r.z_recv.at[i, n, 4 + place], across).wait_recv()
            add_into(s_extra(i, n, par), boxes, 16)
            begin(extra_copies(i, n))

    def reduce_out(i):
        beside_copy(i).wait()
        add_into(t_block(i, b), [t_inbox(i, 7)], 48)
        begin(final_copies(i, 0))

    def reduce_wait(i, n):
        local, sends = final_copies(i, n)
        local.wait()
        if i % 2:
            src, part, dev, one, two = sends[0]
            rc(src, outs[i].at[1 - h], one, two, dev).wait()
            return
        for d, (j, dev) in enumerate(tile_group):
            src, part, _, one, _ = sends[d]
            rc(src, part, one, r.cast_recv.at[i, n, j], dev).wait()
        local, sends = extra_copies(i, n)

        @pl.when(bh == shared)
        def _():
            local.wait()
            for src, part, dev, one, two in sends:
                rc(src, part, one, two, dev).wait_send()

        for d, (j, dev) in enumerate(tile_group):
            jh, jw = at_group(j)

            @pl.when(bh == 2 * jw + jh)
            def _(d=d, j=j, dev=dev):
                src, part, _, one, _ = sends[d]
                rc(src, part, one, r.cast_recv.at[i, n, 4 + j], dev).wait_recv()

    def tile_of(ref, jh, jw):
        return ref.at[rows_of(jh * 4, 4, 4), rows_of(jw * 32, 32), :]

    def scatter(src, dst, n):
        copies = []
        for d, (j, dev) in enumerate(tile_group):
            copies.append(
                rc(src.at[j], tile_of(dst, h, w), r.tile_send.at[n, d], r.tile_recv.at[n, mine], dev)
            )
        return copies

    def scattered(src, dst, n):
        for d, (j, dev) in enumerate(tile_group):
            jh, jw = at_group(j)
            rc(src.at[j], tile_of(dst, jh, jw), r.tile_send.at[n, d], r.tile_recv.at[n, j], dev).wait()

    for n, (src, dst) in enumerate(((r.x_tiles, r.x_grid), (r.cot_tiles, r.cot_grid))):
        for copy in scatter(src, dst, n):
            copy.start()
        lc(src.at[mine], tile_of(dst, h, w), r.tile_own.at[n]).start()
    gather_start(0)

    xg, cg = r.x_grid, r.cot_grid
    params = total(0, mid, r.param_in[...])
    r.param[...] = params
    for n, (src, dst) in enumerate(((r.x_tiles, xg), (r.cot_tiles, cg))):
        scattered(src, dst, n)
        lc(src.at[mine], tile_of(dst, h, w), r.tile_own.at[n]).wait()

    def grid_chunk(ref, i):
        v = ref[lax.div(i, 4), rows_of(lax.rem(i, 4) * CHUNK, CHUNK), :]
        return v.astype(F32).reshape(2, CELL, chan)

    fill(r.xa, r.xb, lambda i: grid_chunk(xg, i), chan)

    def pump_loop(i, lo, hi):
        def body(s, _):
            gather_pump(i, s)
            return 0

        lax.fori_loop(lo, hi, body, 0)

    pump_loop(0, 1, nb - 1)
    gather_start(1)
    gather_pump(0, nb - 1)
    gather_start(2)
    gather_finish(0)

    def first_pump(n):
        gather_pump(1, n + 1)
        pl.when(n == 3)(lambda: gather_pump(2, 1))

    conv(r.xa, r.xb, r.w1s, r.mid1, first_pump)
    gather_pump(1, nb - 1)
    gather_finish(1)
    sums = total(
        1, mid, packed(*moments(r.mid1, mid), mid), [lambda: gather_pump(2, 2), None, lambda: gather_pump(2, 3)]
    )
    prepare(0, sums, mid)

    def hidden(src, n, dst):
        value = activated(src, n, mid)

        def body(i, _):
            put(dst, i, value(i))
            return 0

        loop(CHUNKS, body, 0)

    hidden(r.mid1, 0, r.v1)
    stats = temporal(0, r.v1, r.w1t, r.time1, [lambda: gather_pump(2, 4)])
    gather_pump(2, 5)

    def sixth():
        gather_pump(2, 6)
        gather_start(3)

    sums = total(2, chan, packed(*stats, chan), [None, None, sixth])
    prepare(1, sums, chan)
    fill(r.aa, r.ab, activated(r.time1, 1, chan), chan)
    gather_pump(2, 7)
    gather_finish(2)

    conv(r.aa, r.ab, r.w2s, r.mid2, lambda n: gather_pump(3, n + 1))
    gather_pump(3, nb - 1)
    gather_finish(3)
    sums = total(3, mid, packed(*moments(r.mid2, mid), mid))
    prepare(2, sums, mid)
    hidden(r.mid2, 2, r.v2)
    stats = temporal(1, r.v2, r.w2t, r.time2)
    shared_xq = share_x(0, r.aa, r.ab, r.xq2) + share_x(1, r.xa, r.xb, r.xq1)
    share_v2 = share(4, r.v2, r.sib_v)
    sums = total(4, chan, packed(*stats, chan))
    prepare(3, sums, chan)

    out_grid = r.out_grid

    def grid_put(ref, i, v):
        ref[lax.div(i, 4), rows_of(lax.rem(i, 4) * CHUNK, CHUNK), :] = v.reshape(CHUNK, chan)

    def slope(y, s):
        return s * (1.0 + y * (1.0 - s))

    def pre_body(i, carry):
        scale, shift, inv, offset = tiles(3, chan)
        v = chunk(r.time2, i)
        y = v * scale + shift + chunk(r.xa, i, MAIN)
        s = jax.nn.sigmoid(y)
        m = keep(i)
        grid_put(out_grid, i, y * s * m)
        d = grid_chunk(cg, i) * m * slope(y, s)
        put(r.grad_pre, i, d)
        t = d * (v * inv - offset)
        return (carry[0] + d[0] + d[1], carry[1] + t[0] + t[1])

    zero_out = jnp.zeros((CELL, chan), F32)
    zero_mid = jnp.zeros((CELL, mid), F32)
    out_grid[HGT] = jnp.zeros((8 * CELL, chan), F32)
    gg = loop(CHUNKS, pre_body, (zero_out, zero_out))

    def send_tiles(src, dst, n):
        for d, (j, dev) in enumerate(tile_group):
            jh, jw = at_group(j)
            rc(tile_of(src, jh, jw), dst.at[mine], r.tile_send.at[n, d], r.tile_recv.at[n, mine], dev).start()
        lc(tile_of(src, h, w), dst.at[mine], r.tile_own.at[n]).start()

    def sent_tiles(src, dst, n):
        for d, (j, dev) in enumerate(tile_group):
            jh, jw = at_group(j)
            rc(tile_of(src, jh, jw), dst.at[j], r.tile_send.at[n, d], r.tile_recv.at[n, j], dev).wait()
        lc(tile_of(src, h, w), dst.at[mine], r.tile_own.at[n]).wait()

    send_tiles(out_grid, r.block_out, 2)

    def norm_back(n, sums, width):
        r.norm_grads[2 * n : 2 * n + 1, 0:width] = sums[2:3] + sums[3:4]
        r.norm_grads[2 * n + 1 : 2 * n + 2, 0:width] = sums[0:1] + sums[1:2]
        back = r.back
        back[0, :, 0:width] = per_batch(sums[0:1], sums[1:2], width) / cell_count
        back[1, :, 0:width] = per_batch(sums[2:3], sums[3:4], width) / cell_count

    def through_norm(n, src, grad, i, width):
        scale, _, inv, offset = tiles(n, width)
        xhat = chunk(src, i) * inv - offset
        bias_part = r.back[0, :, 0:width][None]
        gain_part = r.back[1, :, 0:width][None]
        return scale * (chunk(grad, i, 0, width) - bias_part - xhat * gain_part) * keep(i)

    def through_act(n, src, grad, width):
        def body(i, carry):
            scale, shift, inv, offset = tiles(n, width)
            v = chunk(src, i)
            y = v * scale + shift
            s = jax.nn.sigmoid(y)
            d = chunk(grad, i, 0, width) * keep(i) * slope(y, s)
            put(grad, i, d, 0, width)
            t = d * (v * inv - offset)
            return (carry[0] + d[0] + d[1], carry[1] + t[0] + t[1])

        zero = jnp.zeros((CELL, width), F32)
        return loop(CHUNKS, body, (zero, zero))

    def to_frames(n, src, grad):
        def body(i, _):
            e = through_norm(n, src, grad, i, chan).astype(BF16)
            ef = e.astype(F32)
            r.e3[1, rows_of(i * CHUNK, CHUNK), :] = e.reshape(CHUNK, chan)
            put_lanes(r.down, rows_of(i * CHUNK + CELL, CHUNK, CELL), ef.reshape(CHUNK, chan))
            put_lanes(r.up, rows_of(i * CHUNK, CHUNK), (ef * r.gate[...][None]).reshape(CHUNK, chan))
            return 0

        loop(CHUNKS, body, 0)

    sums = total(5, chan, packed(*gg, chan))
    norm_back(3, sums, chan)
    to_frames(3, r.time2, r.grad_pre)
    shared_e3 = temporal_back(2, r.w2t)
    gg = through_act(2, r.mid2, r.grad_mid, mid)
    shared_e3.wait()
    share_v2.wait()
    def temporal_grads(i, v):
        def first():
            transpose_v(v, r.sib_v)
            temporal_grad(i, 0)

        return [first, lambda: temporal_grad(i, 1), lambda: temporal_grad(i, 2)]

    sums = total(6, mid, packed(*gg, mid), temporal_grads(3, r.v2))
    reduce_start(3, 0)
    norm_back(2, sums, mid)

    def fill_e(n, src):
        def value(i):
            v = through_norm(n, src, r.grad_mid, i, mid)
            put(r.e_all, i, v)
            return v

        fill(r.ea, r.eb, value, mid)

    fill_e(2, r.mid2)
    share_e(0)
    conv_back(r.ea, r.eb, r.w2s, r.grad_mid)
    gg = through_act(1, r.time1, r.grad_mid, chan)
    for copy in shared_xq:
        copy.wait()
    for n in (0, 1):
        share_e_on(0, n)
    for n in (0, 1):
        share_e_wait(0, n)

    def second_spatial():
        spatial_grad(2, r.aa, r.ab, r.xq2)

    sums = total(7, chan, packed(*gg, chan), [second_spatial])
    reduce_middle(3, 0)
    for n in (0, 1):
        reduce_start(2, n)
    share_v1 = share(5, r.v1, r.sib_v)
    norm_back(1, sums, chan)
    to_frames(1, r.time1, r.grad_mid)
    shared_e3 = temporal_back(3, r.w1t)
    reduce_last(3, 0)
    gg = through_act(0, r.mid1, r.grad_mid, mid)
    shared_e3.wait()
    share_v1.wait()
    sums = total(8, mid, packed(*gg, mid), temporal_grads(1, r.v1))
    reduce_start(1, 0)
    norm_back(0, sums, mid)
    fill_e(0, r.mid1)
    share_e(1)
    reduce_out(3)
    for n in (0, 1):
        reduce_middle(2, n)
    sent_tiles(out_grid, r.block_out, 2)
    conv_back(r.ea, r.eb, r.w1s, r.grad_mid)
    share_e_on(1, 0)
    near, far = r.w1s.at[0:mid, :], r.w1s.at[mid : 2 * mid, :]

    def transposes(a, _):
        transpose_x(a, r.xa, r.xb, r.xq1, near, far, a * 3 * quarter)
        return 0

    lax.fori_loop(0, 3, transposes, 0)
    for n in (0, 1):
        share_e_wait(1, n)

        def body(a, _, n=n):
            spatial_part(0, near, far, a * 3 * quarter, a * 3 * quarter, n)
            return 0

        lax.fori_loop(0, 3, body, 0)
        reduce_start(0, n)
        if n == 0:
            share_e_on(1, 1)

    def last_body(i, _):
        grid_put(out_grid, i, (chunk(r.grad_mid, i, 0, chan) + chunk(r.grad_pre, i)) * keep(i))
        return 0

    loop(CHUNKS, last_body, 0)
    send_tiles(out_grid, r.grad_input, 3)
    for n in (0, 1):
        reduce_last(2, n)
    reduce_middle(1, 0)
    reduce_middle(0, 0)
    reduce_last(1, 0)
    reduce_out(1)
    reduce_last(0, 0)
    reduce_middle(0, 1)
    reduce_last(0, 1)
    sent_tiles(out_grid, r.grad_input, 3)
    for i in (3, 2, 1, 0):
        for n in parts_of(i):
            reduce_wait(i, n)


def per_device_fast(nb, *args):
    (
        inputs,
        starts,
        first_spatial,
        first_mid_gain,
        first_mid_bias,
        first_temporal,
        first_out_gain,
        first_out_bias,
        second_spatial,
        second_mid_gain,
        second_mid_bias,
        second_temporal,
        second_out_gain,
        second_out_bias,
        cotangent,
    ) = args
    micro, frames, side, _, chan = inputs.shape
    mid = first_spatial.shape[1]
    spat, temp = first_spatial.shape[0], first_temporal.shape[0]
    few = frames // 4
    h, w, b = (lax.axis_index(name) for name in ("ha", "wa", "batch"))
    mine = (1 - w) * h + w * (3 - h)
    offsets = jnp.arange(side)
    valid = (h * side + offsets < HGT)[:, None] & (w * side + offsets < HGT)[None, :]

    def tiles(array):
        array = array * valid.astype(BF16)[None, None, :, :, None]
        array = array.reshape(micro, 4, few, side, side, chan).transpose(1, 3, 4, 0, 2, 5)
        return array.reshape(4, side, side * micro * few, chan)

    def untiled(array):
        array = array.reshape(4, side, side, micro, few, chan).transpose(3, 0, 4, 1, 2, 5)
        return array.reshape(micro, frames, side, side, chan)

    gate = (1 - lax.dynamic_slice_in_dim(starts, mine * few, few, axis=1)).astype(F32)
    gate = jnp.broadcast_to(gate.reshape(micro * few, 1), (micro * few, chan))
    here = jnp.where((h == 0) & (w == 0), 1.0, 0.0)

    def placed(shard):
        row = jnp.zeros((mid,), F32)
        return lax.dynamic_update_slice(row, shard.astype(F32) * here, (b * shard.shape[0],))

    param = jnp.stack(
        [
            placed(v)
            for v in (
                first_mid_gain,
                first_mid_bias,
                first_out_gain,
                first_out_bias,
                second_mid_gain,
                second_mid_bias,
                second_out_gain,
                second_out_bias,
            )
        ]
    )
    half = chan // 2
    few_rows = ROWS // 4

    inputs_of = dict(
        x_tiles=(tiles(inputs), pl.ANY),
        cot_tiles=(tiles(cotangent), pl.ANY),
        gate=(gate, pltpu.VMEM),
        param_in=(param, pltpu.VMEM),
        first_spatial=(first_spatial, pl.ANY),
        first_temporal=(first_temporal, pl.ANY),
        second_spatial=(second_spatial, pl.ANY),
        second_temporal=(second_temporal, pl.ANY),
    )
    outputs_of = dict(
        block_out=((4, side, side * CELL, chan), F32, pl.ANY),
        grad_input=((4, side, side * CELL, chan), F32, pl.ANY),
        norm_grads=((8, mid), F32, pltpu.VMEM),
        out1s=((spat, mid), BF16, pl.ANY),
        out1t=((2, temp, half), BF16, pl.ANY),
        out2s=((spat, mid), BF16, pl.ANY),
        out2t=((2, temp, half), BF16, pl.ANY),
    )
    dma = pltpu.SemaphoreType.DMA
    scratch_of = dict(
        w1s=pltpu.VMEM((9 * chan, mid), BF16),
        w1t=pltpu.VMEM((3 * mid, chan), BF16),
        w2s=pltpu.VMEM((9 * chan, mid), BF16),
        w2t=pltpu.VMEM((3 * mid, chan), BF16),
        x_grid=pltpu.VMEM((8, 8 * CELL, chan), BF16),
        cot_grid=pltpu.VMEM((8, 8 * CELL, chan), BF16),
        out_grid=pltpu.VMEM((8, 8 * CELL, chan), F32),
        xa=pltpu.VMEM((PADDED, chan), BF16),
        xb=pltpu.VMEM((PADDED, chan), BF16),
        aa=pltpu.VMEM((PADDED, chan), BF16),
        ab=pltpu.VMEM((PADDED, chan), BF16),
        ea=pltpu.VMEM((PADDED, mid), BF16),
        eb=pltpu.VMEM((PADDED, mid), BF16),
        mid1=pltpu.VMEM((ROWS, mid), F32),
        mid2=pltpu.VMEM((ROWS, mid), F32),
        grad_mid=pltpu.VMEM((ROWS, mid), F32),
        v1=pltpu.VMEM((ROWS, mid), BF16),
        v2=pltpu.VMEM((ROWS, mid), BF16),
        time1=pltpu.VMEM((ROWS, chan), F32),
        time2=pltpu.VMEM((ROWS, chan), F32),
        grad_pre=pltpu.VMEM((ROWS, chan), F32),
        down=pltpu.VMEM((chan // 128, ROWS + CHUNK, 128), F32),
        up=pltpu.VMEM((chan // 128, ROWS + CHUNK, 128), F32),
        e3=pltpu.VMEM((3, ROWS, chan), BF16),
        sib_e3=pltpu.VMEM((3, ROWS, half), BF16),
        halo_out=pltpu.VMEM((2, few_rows, chan), BF16),
        halo_in=pltpu.VMEM((4, 2, few_rows, chan), BF16),
        param=pltpu.VMEM((8, mid), F32),
        tile_mid=pltpu.VMEM((2, 4, CELL, mid), F32),
        tile_out=pltpu.VMEM((2, 4, CELL, chan), F32),
        back=pltpu.VMEM((2, CELL, mid), F32),
        sum_a=pltpu.VMEM((2, 2, 8, mid), F32),
        sum_b=pltpu.VMEM((2, 4, 8, mid), F32),
        sum_c=pltpu.VMEM((2, nb // 2, 8, mid), F32),
        own_sem=dma((4,)),
        ring_send=dma((4, 2, nb)),
        ring_recv=dma((4, 2, nb)),
        sib_send=dma((4, 3, nb)),
        sib_recv=dma((4, 3, nb)),
        over_send=dma((4, nb)),
        over_recv=dma((4, nb)),
        sa_send=dma((9,)),
        sa_recv=dma((9,)),
        sb_send=dma((9, 3)),
        sb_recv=dma((9, 4)),
        sc_send=dma((9, nb // 2)),
        sc_recv=dma((9, nb // 2)),
        halo_send=dma((4, 2)),
        halo_recv=dma((4, 2)),
        share_send=dma((6,)),
        share_recv=dma((6,)),
        e_all=pltpu.VMEM((4 * ROWS, mid), BF16),
        xq1=pltpu.VMEM((3, 2, PADDED, chan // 4), BF16),
        xq2=pltpu.VMEM((3, 2, PADDED, chan // 4), BF16),
        xt=pltpu.VMEM((mid, 2 * ROWS), BF16),
        sib_v=pltpu.VMEM((ROWS, mid), BF16),
        e_send=dma((2, 2, 3)),
        e_recv=dma((2, 2, 3)),
        xq_send=dma((2, 3, 2)),
        xq_recv=dma((2, 3, 2)),
        y_send=dma((4, 2, 5)),
        y_recv=dma((4, 2, 5)),
        z_send=dma((4, 2, 5)),
        z_recv=dma((4, 2, 7)),
        cast_send=dma((4, 2, 6)),
        cast_recv=dma((4, 2, 8)),
        out_sem=dma((4, 2, 2)),
        tile_send=dma((4, 3)),
        tile_recv=dma((4, 4)),
        tile_own=dma((4,)),
    )
    names = (*inputs_of, *outputs_of, *scratch_of)
    cell_count = float(frames * nb * HGT * HGT)
    results = pl.pallas_call(
        functools.partial(block_kernel, (nb, chan, mid, cell_count), names),
        out_shape=[jax.ShapeDtypeStruct(shape, dtype) for shape, dtype, _ in outputs_of.values()],
        in_specs=[pl.BlockSpec(memory_space=space) for _, space in inputs_of.values()],
        out_specs=[pl.BlockSpec(memory_space=space) for _, _, space in outputs_of.values()],
        scratch_shapes=list(scratch_of.values()),
        compiler_params=pltpu.CompilerParams(
            collective_id=0, has_side_effects=True, vmem_limit_bytes=VMEM_LIMIT
        ),
    )(*(array for array, _ in inputs_of.values()))
    got = SimpleNamespace(**dict(zip(outputs_of, results)))

    def temporal(pair):
        return jnp.concatenate([pair[0], pair[1]], axis=1).astype(F32)

    def norm(row, like):
        size = like.shape[0]
        return lax.dynamic_slice_in_dim(got.norm_grads[row], b * size, size)

    return (
        untiled(got.block_out),
        untiled(got.grad_input),
        got.out1s.astype(F32),
        norm(0, first_mid_gain),
        norm(1, first_mid_bias),
        temporal(got.out1t),
        norm(2, first_out_gain),
        norm(3, first_out_bias),
        got.out2s.astype(F32),
        norm(4, second_mid_gain),
        norm(5, second_mid_bias),
        temporal(got.out2t),
        norm(6, second_out_gain),
        norm(7, second_out_bias),
    )


def extended(shard, sides, width):
    for axis, dim in sides:
        count, length = (lax.axis_size(axis), shard.shape[dim])
        up = [(i, (i + 1) % count) for i in range(count - 1)]
        down = [(j, i) for i, j in up]
        last = lax.slice_in_dim(shard, length - width, length, axis=dim)
        leading = lax.slice_in_dim(shard, 0, width, axis=dim)
        before = lax.ppermute(last, axis, up)
        after = lax.ppermute(leading, axis, down)
        shard = jnp.concatenate([before, shard, after], axis=dim)
    return shard


def passed_along(shard, axis, by):
    count = lax.axis_size(axis)
    pairs = [(i, i + by) for i in range(count) if 0 <= i + by < count]
    return lax.ppermute(shard, axis, pairs)


def for_sending(shard):

    def short(part):
        return part.astype(jnp.bfloat16) if part.dtype == jnp.float32 else part

    return jax.tree.map(short, shard)


def silu_slope(values):
    sigma = jax.nn.sigmoid(values)
    return sigma * (1.0 + values * (1.0 - sigma))


def spatial_forward(field_in, kernel):
    frames, tile_side = (field_in.shape[0], field_in.shape[1])
    padded = extended(field_in, (("ha", 1), ("wa", 2)), 1)
    pieces = [
        padded[:, offset // 3 : offset // 3 + tile_side, offset % 3 : offset % 3 + tile_side, :]
        for offset in range(9)
    ]
    patches = jnp.concatenate(pieces, axis=-1).reshape(frames * tile_side * tile_side, -1)
    return (patches, jnp.dot(patches, kernel, preferred_element_type=jnp.float32))


def spatial_backward(grad_out, patches, kernel):
    frames, tile_side, channels = (grad_out.shape[0], grad_out.shape[1], grad_out.shape[3])
    row_count = frames * tile_side * tile_side
    padded = extended(grad_out, (("ha", 1), ("wa", 2)), 1)
    pieces = [
        padded[
            :,
            2 - offset // 3 : 2 - offset // 3 + tile_side,
            2 - offset % 3 : 2 - offset % 3 + tile_side,
            :,
        ]
        for offset in range(9)
    ]
    stacked = jnp.concatenate(pieces, axis=-1).reshape(row_count, 9, channels)
    grad_in = jnp.einsum(
        "rkm,kcm->rc", stacked, kernel.reshape(9, -1, channels), preferred_element_type=jnp.float32
    )
    grad_kernel = jnp.einsum(
        "rk,rm->km",
        patches,
        grad_out.reshape(row_count, channels),
        preferred_element_type=jnp.float32,
    )
    return (grad_in, grad_kernel)


def temporal_forward(field_in, clip_gate, kernel):
    frames, tile_side = (field_in.shape[0], field_in.shape[1])
    gated_in = field_in * clip_gate
    earlier = passed_along(field_in[-1:], "batch", 1)
    later_frame = passed_along(gated_in[:1], "batch", -1)
    before = jnp.concatenate([earlier, field_in[:-1]], axis=0) * clip_gate
    after_tap = jnp.concatenate([gated_in[1:], later_frame], axis=0)
    joined = jnp.concatenate([before, field_in, after_tap], axis=-1).reshape(
        frames * tile_side * tile_side, -1
    )
    return (joined, jnp.dot(joined, kernel, preferred_element_type=jnp.float32))


def temporal_backward(grad_out, joined, clip_gate, kernel):
    frames, tile_side, channels = (grad_out.shape[0], grad_out.shape[1], grad_out.shape[3])
    row_count = frames * tile_side * tile_side
    gated_grad = grad_out * clip_gate
    later_frame = passed_along(gated_grad[:1], "batch", -1)
    earlier = passed_along(grad_out[-1:], "batch", 1)
    from_later = jnp.concatenate([gated_grad[1:], later_frame], axis=0)
    from_earlier = jnp.concatenate([earlier, grad_out[:-1]], axis=0) * clip_gate
    stacked = jnp.concatenate([from_later, grad_out, from_earlier], axis=-1).reshape(
        row_count, 3, channels
    )
    grad_in = jnp.einsum(
        "rkc,kmc->rm", stacked, kernel.reshape(3, -1, channels), preferred_element_type=jnp.float32
    )
    grad_kernel = jnp.einsum(
        "rk,rc->kc",
        joined,
        grad_out.reshape(row_count, channels),
        preferred_element_type=jnp.float32,
    )
    return (grad_in, grad_kernel)


def norm_forward(pre_norm, norm_gain, norm_bias, valid_rows, cell_count):
    first_sum = jnp.sum(pre_norm * valid_rows, axis=0)
    square_sum = jnp.sum(pre_norm * pre_norm * valid_rows, axis=0)
    first_sum, square_sum = lax.psum((first_sum, square_sum), ("ha", "wa", "batch"))
    mean_val = first_sum / cell_count
    inv_std = lax.rsqrt(square_sum / cell_count - mean_val * mean_val + epsilon)
    normed = (pre_norm - mean_val) * inv_std
    return (normed, inv_std, normed * norm_gain.astype(jnp.float32) + norm_bias.astype(jnp.float32))


def norm_backward(grad_norm, normed, inv_std, norm_gain, valid_rows, cell_count):
    bias_grad = jnp.sum(grad_norm, axis=0)
    gain_grad = jnp.sum(grad_norm * normed, axis=0)
    bias_grad, gain_grad = lax.psum((bias_grad, gain_grad), ("ha", "wa", "batch"))
    grad_in = (
        valid_rows
        * norm_gain.astype(jnp.float32)
        * inv_std
        * (grad_norm - bias_grad / cell_count - normed * gain_grad / cell_count)
    )
    return (grad_in, gain_grad, bias_grad)


def forward_pair(field_in, weights, clip_gate, valid_rows, cell_count):
    frames, tile_side = (field_in.shape[0], field_in.shape[1])
    patches, spatial_out = spatial_forward(field_in, weights[0])
    mid_hat, mid_scale, mid_norm = norm_forward(
        spatial_out, weights[1], weights[2], valid_rows, cell_count
    )
    hidden = (
        (jax.nn.silu(mid_norm) * valid_rows)
        .astype(jnp.bfloat16)
        .reshape(frames, tile_side, tile_side, -1)
    )
    joined, temporal_out = temporal_forward(hidden, clip_gate, weights[3])
    out_hat, out_scale, out_norm = norm_forward(
        temporal_out, weights[4], weights[5], valid_rows, cell_count
    )
    return ((patches, mid_hat, mid_scale, mid_norm, joined, out_hat, out_scale), out_norm)


def backward_pair(grad_norm, kept, weights, clip_gate, valid_rows, cell_count, tile_side):
    patches, mid_hat, mid_scale, mid_norm, joined, out_hat, out_scale = kept
    frames = clip_gate.shape[0]
    grad_time, out_gain_grad, out_bias_grad = norm_backward(
        grad_norm, out_hat, out_scale, weights[4], valid_rows, cell_count
    )
    grad_time = grad_time.astype(jnp.bfloat16).reshape(frames, tile_side, tile_side, -1)
    grad_hidden, temporal_grad = temporal_backward(grad_time, joined, clip_gate, weights[3])
    grad_mid = grad_hidden * valid_rows * silu_slope(mid_norm)
    grad_spatial, mid_gain_grad, mid_bias_grad = norm_backward(
        grad_mid, mid_hat, mid_scale, weights[1], valid_rows, cell_count
    )
    grad_spatial = grad_spatial.astype(jnp.bfloat16).reshape(frames, tile_side, tile_side, -1)
    grad_in, spatial_grad = spatial_backward(grad_spatial, patches, weights[0])
    return (
        grad_in,
        (spatial_grad, mid_gain_grad, mid_bias_grad, temporal_grad, out_gain_grad, out_bias_grad),
    )


def per_device(
    inputs,
    starts,
    first_spatial,
    first_mid_gain,
    first_mid_bias,
    first_temporal,
    first_out_gain,
    first_out_bias,
    second_spatial,
    second_mid_gain,
    second_mid_bias,
    second_temporal,
    second_out_gain,
    second_out_bias,
    cotangent,
):
    shards = (
        first_spatial,
        first_mid_gain,
        first_mid_bias,
        first_temporal,
        first_out_gain,
        first_out_bias,
        second_spatial,
        second_mid_gain,
        second_mid_bias,
        second_temporal,
        second_out_gain,
        second_out_bias,
    )
    micro_total, frames, tile_side, channels = (
        inputs.shape[0],
        inputs.shape[1],
        inputs.shape[2],
        inputs.shape[4],
    )
    row_count = frames * tile_side * tile_side
    cell_count = frames * lax.axis_size("batch") * HGT * HGT
    offsets = jnp.arange(tile_side)
    inside_h = lax.axis_index("ha") * tile_side + offsets < HGT
    inside_w = lax.axis_index("wa") * tile_side + offsets < HGT
    valid_grid = inside_h[:, None] & inside_w[None, :]
    valid_tile = valid_grid.astype(jnp.bfloat16)[None, :, :, None]
    valid_rows = jnp.broadcast_to(
        valid_grid.astype(jnp.float32)[None], (frames, tile_side, tile_side)
    ).reshape(row_count, 1)
    results = []
    input_grads = []
    kernel_total = None
    norm_total = None
    for micro_step in range(micro_total):
        gathered = (
            lax.all_gather(shards[0], "batch", axis=0, tiled=True),
            lax.all_gather(shards[1], "batch", axis=0, tiled=True),
            lax.all_gather(shards[2], "batch", axis=0, tiled=True),
            lax.all_gather(shards[3], "batch", axis=0, tiled=True),
            lax.all_gather(shards[4], "batch", axis=0, tiled=True),
            lax.all_gather(shards[5], "batch", axis=0, tiled=True),
            lax.all_gather(shards[6], "batch", axis=0, tiled=True),
            lax.all_gather(shards[7], "batch", axis=0, tiled=True),
            lax.all_gather(shards[8], "batch", axis=0, tiled=True),
            lax.all_gather(shards[9], "batch", axis=0, tiled=True),
            lax.all_gather(shards[10], "batch", axis=0, tiled=True),
            lax.all_gather(shards[11], "batch", axis=0, tiled=True),
        )
        clip_gate = (1 - starts[micro_step]).astype(jnp.bfloat16).reshape(frames, 1, 1, 1)
        x_in = inputs[micro_step] * valid_tile
        first_kept, first_norm = forward_pair(
            x_in, gathered[0:6], clip_gate, valid_rows, cell_count
        )
        first_act = (
            (jax.nn.silu(first_norm) * valid_rows)
            .astype(jnp.bfloat16)
            .reshape(frames, tile_side, tile_side, channels)
        )
        second_kept, second_norm = forward_pair(
            first_act, gathered[6:12], clip_gate, valid_rows, cell_count
        )
        pre_out = second_norm + x_in.reshape(row_count, channels).astype(jnp.float32)
        results.append(
            (jax.nn.silu(pre_out) * valid_rows).reshape(frames, tile_side, tile_side, channels)
        )
        grad_pre = (
            cotangent[micro_step].reshape(row_count, channels).astype(jnp.float32)
            * valid_rows
            * silu_slope(pre_out)
        )
        grad_act, second_grads = backward_pair(
            grad_pre, second_kept, gathered[6:12], clip_gate, valid_rows, cell_count, tile_side
        )
        grad_first = grad_act * valid_rows * silu_slope(first_norm)
        grad_conv, first_grads = backward_pair(
            grad_first, first_kept, gathered[0:6], clip_gate, valid_rows, cell_count, tile_side
        )
        input_grads.append(
            ((grad_conv + grad_pre) * valid_rows).reshape(frames, tile_side, tile_side, channels)
        )
        step_grads = first_grads + second_grads
        kernel_now = (step_grads[0], step_grads[3], step_grads[6], step_grads[9])
        norm_now = (
            step_grads[1],
            step_grads[2],
            step_grads[4],
            step_grads[5],
            step_grads[7],
            step_grads[8],
            step_grads[10],
            step_grads[11],
        )
        if micro_step == 0:
            kernel_total = kernel_now
            norm_total = norm_now
        else:
            kernel_total = jax.tree.map(jnp.add, kernel_total, kernel_now)
            norm_total = jax.tree.map(jnp.add, norm_total, norm_now)
    kernel_total = lax.psum_scatter(kernel_total, "batch", scatter_dimension=0, tiled=True)
    kernel_total = jax.tree.map(
        lambda part: part.astype(jnp.float32), lax.psum(for_sending(kernel_total), ("ha", "wa"))
    )
    shard_index = lax.axis_index("batch")
    batch_count = lax.axis_size("batch")
    norm_shards = tuple(
        (
            lax.dynamic_slice_in_dim(
                full_sum,
                shard_index * (full_sum.shape[0] // batch_count),
                full_sum.shape[0] // batch_count,
            )
            for full_sum in norm_total
        )
    )
    return (
        jnp.stack(results),
        jnp.stack(input_grads),
        kernel_total[0],
        norm_shards[0],
        norm_shards[1],
        kernel_total[1],
        norm_shards[2],
        norm_shards[3],
        kernel_total[2],
        norm_shards[4],
        norm_shards[5],
        kernel_total[3],
        norm_shards[6],
        norm_shards[7],
    )


def solution(mesh):
    in_specs = (
        P(None, "batch", "ha", "wa", None),
        P(None, "batch"),
        P("batch", None),
        P("batch"),
        P("batch"),
        P("batch", None),
        P("batch"),
        P("batch"),
        P("batch", None),
        P("batch"),
        P("batch"),
        P("batch", None),
        P("batch"),
        P("batch"),
        P(None, "batch", "ha", "wa", None),
    )
    out_specs = (
        P(None, "batch", "ha", "wa", None),
        P(None, "batch", "ha", "wa", None),
        P("batch", None),
        P("batch"),
        P("batch"),
        P("batch", None),
        P("batch"),
        P("batch"),
        P("batch", None),
        P("batch"),
        P("batch"),
        P("batch", None),
        P("batch"),
        P("batch"),
    )
    batch = mesh.shape["batch"]

    def program(*args):
        spat, temp = args[2].shape[0], args[5].shape[0]
        fits = args[0].shape == (2, 16, 4, 4, 512) and args[2].shape[1] == 1152
        if fits and batch == 8 and spat * batch == 9 * 512 and temp * batch == 3 * 1152:
            return per_device_fast(batch, *args)
        return per_device(*args)

    return jax.shard_map(
        program, mesh=mesh, in_specs=in_specs, out_specs=out_specs, check_vma=False
    )
```

```python
import functools
from types import SimpleNamespace

import jax
import jax.numpy as jnp
from jax import lax
from jax.experimental import pallas as pl
from jax.experimental.pallas import tpu as pltpu
from jax.sharding import PartitionSpec as P

HGT = 7
epsilon = 1e-05
MESH = pl.DeviceIdType.MESH
F32 = jnp.float32
BF16 = jnp.bfloat16

BASE = 10
CELL = 8
ROWS = HGT * 8 * CELL
PADDED = (BASE + HGT * 8 + BASE) * CELL
MAIN = BASE * CELL
CHUNK = 2 * CELL
CHUNKS = ROWS // CHUNK
VMEM_LIMIT = 64 * 1024 * 1024 - 1024 * 1024


def when(cond, work):
    if cond is True:
        work()
    elif cond is not False:
        pl.when(cond)(work)


def loop(count, body, init):
    def twice(i, carry):
        return body(2 * i + 1, body(2 * i, carry))

    return lax.fori_loop(0, count // 2, twice, init)


def nn(a, b):
    return jnp.dot(a, b, preferred_element_type=F32)


def nt(a, b):
    return lax.dot_general(a, b, (((1,), (1,)), ((), ())), preferred_element_type=F32)


def tn(a, b):
    return lax.dot_general(a, b, (((0,), (0,)), ((), ())), preferred_element_type=F32)


def rows_of(start, size, step=16):
    if not isinstance(start, int):
        start = pl.multiple_of(start, step)
    return pl.ds(start, size)


def per_batch(first, second, width):
    return jnp.concatenate(
        [jnp.broadcast_to(first, (CELL // 2, width)), jnp.broadcast_to(second, (CELL // 2, width))], axis=0
    )


def block_kernel(dims, names, *all_refs):
    r = SimpleNamespace(**dict(zip(names, all_refs, strict=True)))
    nb, chan, mid, cell_count = dims
    spat = 9 * chan // nb
    temp = 3 * mid // nb
    unit = spat // 6
    quarter = chan // 4
    half = chan // 2
    h = lax.axis_index("ha")
    w = lax.axis_index("wa")
    b = lax.axis_index("batch")
    par = lax.rem(b, 2)
    bh = lax.div(b, 2)
    pos = par * (nb - 1 - bh) + (1 - par) * bh
    way = 1 - 2 * h

    def at(p):
        p = lax.rem(p + 4 * nb, nb)
        upper = lax.div(p, nb // 2)
        return (1 - upper) * (2 * p) + upper * (2 * (nb - 1 - p) + 1)

    def at_group(j):
        jw = lax.div(j, 2)
        odd = lax.rem(j, 2)
        return (odd * (1 - jw) + (1 - odd) * jw, jw)

    mine = (1 - w) * h + w * (3 - h)
    sibling = (1 - h, w, b)
    beside = (h, 1 - w, b)
    onward = (h, w, at(pos + way))
    behind = (h, w, at(pos - way))
    later = lax.rem(mine + 1, 4)
    earlier = lax.rem(mine + 3, 4)
    later_dev = (*at_group(later), lax.rem(b + lax.div(mine + 1, 4), nb))
    earlier_dev = (*at_group(earlier), lax.rem(b + nb - lax.div(4 - mine, 4), nb))
    tile_group = [(lax.rem(mine + d, 4), (*at_group(lax.rem(mine + d, 4)), b)) for d in (1, 2, 3)]
    pos_b = w * 2 + par
    plane = []
    for d in (1, 2, 3):
        q = lax.rem(pos_b + d, 4)
        plane.append((q, (h, lax.div(q, 2), b - par + lax.rem(q, 2))))
    depth = nb // 2
    line = []
    for d in range(1, depth):
        q = lax.rem(bh + d, depth)
        line.append((q, (h, w, 2 * q + par)))

    def named(dev):
        return dict(ha=dev[0], wa=dev[1], batch=dev[2])

    def rc(src, dst, send, recv, dev):
        return pltpu.make_async_remote_copy(
            src_ref=src, dst_ref=dst, send_sem=send, recv_sem=recv, device_id=named(dev), device_id_type=MESH
        )

    def lc(src, dst, sem):
        return pltpu.make_async_copy(src, dst, sem)

    partners = [sibling, beside, onward, behind, later_dev, earlier_dev]
    partners += [dev for _, dev in tile_group + plane + line]
    barrier = pltpu.get_barrier_semaphore()
    for dev in partners:
        pl.semaphore_signal(barrier, inc=1, device_id=named(dev), device_id_type=MESH)
    pl.semaphore_wait(barrier, len(partners))

    shards = (r.first_spatial, r.first_temporal, r.second_spatial, r.second_temporal)
    whole = (r.w1s, r.w1t, r.w2s, r.w2t)
    shared = 2 * w + h
    shared_beside = 2 * (1 - w) + h
    third = temp // 3

    def units(i, core, side):
        return (2 * side + core, 4 + core) if i % 2 == 0 else ((1 - core) * side + 2 * core,)

    def piece(i, ref, owner, u):
        if i % 2 == 0:
            return ref.at[rows_of(owner * spat + u * unit, unit), :]
        return ref.at[rows_of(owner * temp + u * third, third), :]

    def streams(i):
        return (0, 1) if i % 2 == 0 else (0,)

    def crossing(i, work):
        if i % 2 == 0:
            work()
        else:
            pl.when(h == 0)(work)

    def crossed(i, work):
        if i % 2 == 0:
            work()
        else:
            pl.when(h == 1)(work)

    def own_copy(i):
        rows = spat if i % 2 == 0 else temp
        return lc(shards[i], whole[i].at[rows_of(b * rows, rows), :], r.own_sem.at[i])

    def ring(i, st, s, owner, from_shard=False):
        u = units(i, h, w)[st]
        dst = piece(i, whole[i], owner, u)
        src = piece(i, shards[i], 0, u) if from_shard else dst
        return rc(src, dst, r.ring_send.at[i, st, s], r.ring_recv.at[i, st, s], onward)

    def cross(i, kind, s, owner, u):
        part = piece(i, whole[i], owner, u)
        return rc(part, part, r.sib_send.at[i, kind, s], r.sib_recv.at[i, kind, s], sibling)

    def over(i, s, owner, u):
        part = piece(i, whole[i], owner, u)
        return rc(part, part, r.over_send.at[i, s], r.over_recv.at[i, s], beside)

    def gather_start(i):
        for st in streams(i):
            ring(i, st, 1, b, True).start()
        own_copy(i).start()

    def gather_relay(i, s):
        owner = at(pos - way * s)

        def work():
            over(i, s, owner, units(i, h, 1 - w)[0]).wait_recv()
            cross(i, 2, s, owner, units(i, h, 1 - w)[0]).start()

        crossing(i, work)

    def gather_pump(i, s):
        owner = at(pos - way * s)
        own = units(i, h, w)
        for st in streams(i):
            ring(i, st, s, owner).wait_recv()
            if isinstance(s, int):
                if s < nb - 1:
                    ring(i, st, s + 1, owner).start()
            else:
                pl.when(s < nb - 1)(lambda st=st: ring(i, st, s + 1, owner).start())
            if st == 0:
                crossing(i, lambda: over(i, s, owner, own[0]).start())
            cross(i, st, s, owner, own[st]).start()
        if isinstance(s, int):
            if s > 1:
                gather_relay(i, s - 1)
        else:
            pl.when(s > 1)(lambda: gather_relay(i, s - 1))

    def gather_finish(i):
        gather_relay(i, nb - 1)

        def body(s, _):
            owner = at(pos - way * s)
            theirs = at(pos + way * s)
            for st in streams(i):
                ring(i, st, s, owner).wait_send()
                cross(i, st, s, owner, units(i, h, w)[st]).wait_send()
                cross(i, st, s, theirs, units(i, 1 - h, w)[st]).wait_recv()

            def sent():
                over(i, s, owner, units(i, h, w)[0]).wait_send()
                cross(i, 2, s, owner, units(i, h, 1 - w)[0]).wait_send()

            crossing(i, sent)
            crossed(i, lambda: cross(i, 2, s, theirs, units(i, 1 - h, 1 - w)[0]).wait_recv())
            return 0

        lax.fori_loop(1, nb, body, 0)
        own_copy(i).wait()

    def total(k, width, value, works=()):
        slot = k % 2
        wide = value.shape[1]
        cols = pl.ds(0, wide)
        works = list(works) + [None] * 3
        pair, four, far = r.sum_a, r.sum_b, r.sum_c
        pair[slot, h, :, cols] = value
        part = pair.at[slot, h, :, cols]
        send_a = rc(part, part, r.sa_send.at[k], r.sa_recv.at[k], sibling)
        send_a.start()
        if works[0]:
            works[0]()
        part = pair.at[slot, 1 - h, :, cols]
        rc(part, part, r.sa_send.at[k], r.sa_recv.at[k], sibling).wait_recv()
        four[slot, pos_b, :, cols] = pair[slot, 0, :, cols] + pair[slot, 1, :, cols]
        sends = [send_a]
        for n, (q, dev) in enumerate(plane):
            part = four.at[slot, pos_b, :, cols]
            sends.append(rc(part, part, r.sb_send.at[k, n], r.sb_recv.at[k, pos_b], dev))
            sends[-1].start()
        if works[1]:
            works[1]()
        for n, (q, dev) in enumerate(plane):
            part = four.at[slot, q, :, cols]
            rc(part, part, r.sb_send.at[k, n], r.sb_recv.at[k, q], dev).wait_recv()
        far[slot, bh, :, cols] = (four[slot, 0, :, cols] + four[slot, 1, :, cols]) + (
            four[slot, 2, :, cols] + four[slot, 3, :, cols]
        )
        for n, (q, dev) in enumerate(line):
            part = far.at[slot, bh, :, cols]
            sends.append(rc(part, part, r.sc_send.at[k, n], r.sc_recv.at[k, bh], dev))
            sends[-1].start()
        if works[2]:
            works[2]()
        for n, (q, dev) in enumerate(line):
            part = far.at[slot, q, :, cols]
            rc(part, part, r.sc_send.at[k, n], r.sc_recv.at[k, q], dev).wait_recv()
        result = far[slot, 0, :, cols]
        for q in range(1, depth):
            result = result + far[slot, q, :, cols]
        for send in sends:
            send.wait_send()
        if wide == width:
            return result
        return jnp.concatenate([result[0:4], result[4:8, 2 * wide - width :]], axis=1)

    def chunk(ref, i, base=0, width=None):
        cols = slice(None) if width is None else pl.ds(0, width)
        value = ref[rows_of(base + i * CHUNK, CHUNK), cols]
        return value.astype(F32).reshape(2, CELL, value.shape[-1])

    def put(ref, i, value, base=0, width=None):
        cols = slice(None) if width is None else pl.ds(0, width)
        ref[rows_of(base + i * CHUNK, CHUNK), cols] = value.reshape(CHUNK, value.shape[-1]).astype(ref.dtype)

    def keep(i):
        inside = jnp.where(lax.rem(i, 4) == 3, 0.0, 1.0).astype(F32)
        first = lax.broadcasted_iota(jnp.int32, (2, 1, 1), 0) == 0
        return jnp.where(first, 1.0, inside)

    def packed(one, two, width):
        rows = [
            jnp.sum(v[k : k + CELL // 2], axis=0, keepdims=True) for v in (one, two) for k in (0, CELL // 2)
        ]
        rows = jnp.concatenate(rows, axis=0)
        wide = -(-width // 256) * 128
        return jnp.concatenate([rows[:, 0:wide], rows[:, width - wide :]], axis=0)

    def moments(ref, width):
        def body(i, carry):
            v = chunk(ref, i)
            m = v * keep(i)
            return (carry[0] + m[0] + m[1], carry[1] + m[0] * v[0] + m[1] * v[1])

        zero = jnp.zeros((CELL, width), F32)
        return loop(CHUNKS, body, (zero, zero))

    def prepare(n, sums, width):
        tile = r.tile_mid if width == mid else r.tile_out
        n2 = n // 2
        gain = r.param[2 * n : 2 * n + 1, 0:width]
        bias = r.param[2 * n + 1 : 2 * n + 2, 0:width]
        mean = sums[0:2] / cell_count
        inv = lax.rsqrt(sums[2:4] / cell_count - mean * mean + epsilon)
        scale = inv * gain
        shift = bias - mean * scale
        for k, v in enumerate((scale, shift, inv, mean * inv)):
            tile[n2, k] = per_batch(v[0:1], v[1:2], width)

    def tiles(n, width):
        tile = r.tile_mid if width == mid else r.tile_out
        return [tile[n // 2, k][None] for k in range(4)]

    def fill(ref_a, ref_b, value_of, width):
        pads(ref_a, ref_b, width)

        def body(i, before):
            v = value_of(i)
            put(ref_a, i, v, MAIN)
            pair = jnp.concatenate([before[None], v[0:1]], axis=0)
            put(ref_b, i, pair, MAIN - CHUNK)
            return v[1]

        loop(CHUNKS, body, jnp.zeros((CELL, width), F32))

    def activated(src, n, width):
        def value(i):
            scale, shift, _, _ = tiles(n, width)
            y = chunk(src, i) * scale + shift
            return y * jax.nn.sigmoid(y) * keep(i)

        return value

    def taps(ref_a, ref_b, k, size=ROWS):
        r0 = MAIN - 8 * CELL + 8 * CELL * k
        return (
            ref_b[rows_of(r0 - CHUNK, size), :],
            ref_a[rows_of(r0, size), :],
            ref_b[rows_of(r0, size), :],
        )

    def conv(ref_a, ref_b, weight, out, pump=None):
        for n, (c0, cw) in enumerate(((0, 512), (512, mid - 512))):

            def body(a, _, c0=c0, cw=cw, n=n):
                x = taps(ref_a, ref_b, a)
                acc = nn(jnp.concatenate(x, axis=1), weight[rows_of(a * 3 * chan, 3 * chan), c0 : c0 + cw])

                @pl.when(a == 0)
                def _():
                    out[:, c0 : c0 + cw] = acc

                @pl.when(a > 0)
                def _():
                    out[:, c0 : c0 + cw] += acc

                if pump is not None:
                    pump(n * 3 + a)
                return 0

            lax.fori_loop(0, 3, body, 0)

    def conv_back(ref_a, ref_b, weight, out, pump=None):
        def body(k, _):
            e = taps(ref_a, ref_b, k)
            acc = None
            for j in range(3):
                tap = 8 - 3 * k - j
                term = nt(e[j], weight[rows_of(tap * chan, chan), :])
                acc = term if acc is None else acc + term

            @pl.when(k == 0)
            def _():
                out[:, 0:chan] = acc

            @pl.when(k > 0)
            def _():
                out[:, 0:chan] += acc

            if pump is not None:
                pump(k)
            return 0

        lax.fori_loop(0, 3, body, 0)

    def send_frames(k):
        down, up = r.down, r.up
        count = ROWS // 4
        for c in range(chan // 128):
            lanes = pl.ds(128 * c, 128)
            r.halo_out[0, :, lanes] = down[c, pl.ds(CELL + 3, count, stride=4), :].astype(BF16)
            r.halo_out[1, :, lanes] = up[c, pl.ds(0, count, stride=4), :].astype(BF16)
        copies = []
        for n, dev in ((0, later_dev), (1, earlier_dev)):
            copies.append(
                rc(r.halo_out.at[n], r.halo_in.at[k, n], r.halo_send.at[k, n], r.halo_recv.at[k, n], dev)
            )
            copies[-1].start()
        return copies

    def take_frames(k, copies):
        down, up = r.down, r.up
        count = ROWS // 4
        for copy in copies:
            copy.wait()
        at_start = jnp.logical_and(mine == 0, b == 0)
        at_end = jnp.logical_and(mine == 3, b == nb - 1)
        for c in range(chan // 128):
            lanes = pl.ds(128 * c, 128)
            before = r.halo_in[k, 0, :, lanes].astype(F32)
            after = r.halo_in[k, 1, :, lanes].astype(F32)
            down[c, pl.ds(CELL - 1, count, stride=4), :] = jnp.where(at_start, 0.0, before)
            up[c, pl.ds(4, count, stride=4), :] = jnp.where(at_end, 0.0, after)

    def by_lanes(ref, rows):
        return jnp.concatenate([ref[c, rows, :] for c in range(chan // 128)], axis=1)

    def put_lanes(ref, rows, value):
        for c in range(chan // 128):
            ref[c, rows, :] = value[:, 128 * c : 128 * c + 128]

    def shifted(i):
        before = by_lanes(r.down, rows_of(i * CHUNK, CHUNK + CELL))[CELL - 1 : CELL - 1 + CHUNK]
        after = by_lanes(r.up, rows_of(i * CHUNK, CHUNK + CELL))[1 : 1 + CHUNK]
        gate = r.gate[...][None]
        return (before.reshape(2, CELL, chan) * gate, after.reshape(2, CELL, chan))

    def temporal(k, v, weight, out, works=()):
        works = list(works) + [None] * 2
        put_lanes(r.down, pl.ds(CELL, ROWS), nn(v[...], weight[0:mid, :]))
        y2 = nn(v[...], weight[2 * mid : 3 * mid, :])
        y2 = (y2.reshape(ROWS // CELL, CELL, chan) * r.gate[...][None]).reshape(ROWS, chan)
        put_lanes(r.up, pl.ds(0, ROWS), y2)
        copies = send_frames(k)
        out[...] = nn(v[...], weight[mid : 2 * mid, :])
        if works[0]:
            works[0]()
        take_frames(k, copies)

        def body(i, carry):
            before, after = shifted(i)
            value = chunk(out, i) + before + after
            put(out, i, value)
            m = value * keep(i)
            return (carry[0] + m[0] + m[1], carry[1] + m[0] * value[0] + m[1] * value[1])

        zero = jnp.zeros((CELL, chan), F32)
        return loop(CHUNKS, body, (zero, zero))

    def temporal_back(k, weight, works=()):
        works = list(works) + [None] * 2
        copies = send_frames(k)
        e3 = r.e3
        for c0, cw in ((0, 512), (512, mid - 512)):
            r.grad_mid[:, c0 : c0 + cw] = nt(e3[1], weight[mid + c0 : mid + c0 + cw, :])
        if works[0]:
            works[0]()
        take_frames(k, copies)

        def body(i, _):
            before, after = shifted(i)
            e3[0, rows_of(i * CHUNK, CHUNK), :] = after.reshape(CHUNK, chan).astype(BF16)
            e3[2, rows_of(i * CHUNK, CHUNK), :] = before.reshape(CHUNK, chan).astype(BF16)
            return 0

        loop(CHUNKS, body, 0)
        share = share_e3(k)
        for c0, cw in ((0, 512), (512, mid - 512)):
            r.grad_mid[:, c0 : c0 + cw] += nt(e3[0], weight[c0 : c0 + cw, :]) + nt(
                e3[2], weight[2 * mid + c0 : 2 * mid + c0 + cw, :]
            )
        return share

    def share(k, src, dst):
        copy = rc(src, dst, r.share_send.at[k], r.share_recv.at[k], sibling)
        copy.start()
        return copy

    outs = (r.out1s, r.out1t, r.out2s, r.out2t)

    halves = ((0, 512), (512, mid - 512))

    def e_part(n, slot):
        c0, cw = halves[n]
        return r.e_all.at[slot * ROWS : (slot + 1) * ROWS, c0 : c0 + cw]

    def e_copies(k, n):
        sems = [(r.e_send.at[k, n, m], r.e_recv.at[k, n, m]) for m in range(3)]
        return [
            rc(e_part(n, 0), e_part(n, 1), *sems[0], sibling),
            rc(e_part(n, 0), e_part(n, 2), *sems[1], beside),
            rc(e_part(n, 2), e_part(n, 3), *sems[2], sibling),
        ]

    def share_e(k):
        for n in (0, 1):
            near, over, _ = e_copies(k, n)
            over.start()
            near.start()

    def share_e_on(k, n):
        _, over, far = e_copies(k, n)
        over.wait_recv()
        far.start()

    def share_e_wait(k, n):
        near, over, far = e_copies(k, n)
        near.wait()
        over.wait_send()
        far.wait()

    def share_x(k, xa, xq):
        copies = []
        for n, dev in enumerate((sibling, beside, (1 - h, 1 - w, b))):
            lanes = rows_of((2 * dev[1] + dev[0]) * quarter, quarter, 128)
            main = pl.ds(MAIN, ROWS)
            copies.append(
                rc(xa.at[main, lanes], xq.at[n, 0, main, :], r.xq_send.at[k, n], r.xq_recv.at[k, n], dev)
            )
            copies[-1].start()
        return copies

    def pads(ref_a, ref_b, width):
        ref_a[0:MAIN, :] = jnp.zeros((MAIN, width), BF16)
        ref_a[MAIN + ROWS : PADDED, :] = jnp.zeros((PADDED - MAIN - ROWS, width), BF16)
        ref_b[0 : MAIN - CHUNK, :] = jnp.zeros((MAIN - CHUNK, width), BF16)
        ref_b[MAIN - CHUNK + ROWS : PADDED, :] = jnp.zeros((PADDED - MAIN + CHUNK - ROWS, width), BF16)

    def spread_x(xq):
        for n in range(3):
            pads(xq.at[n, 0], xq.at[n, 1], quarter)

        def body(i, before):
            after = []
            for n in range(3):
                v = chunk(xq.at[n, 0], i, MAIN)
                put(xq.at[n, 1], i, jnp.concatenate([before[n][None], v[0:1]], axis=0), MAIN - CHUNK)
                after.append(v[1])
            return tuple(after)

        loop(CHUNKS, body, (jnp.zeros((CELL, quarter), F32),) * 3)

    def share_e3(k):
        return share(
            k - 2, r.e3.at[:, :, rows_of((1 - h) * half, half, 128)], r.sib_e3
        )

    def grad_tap(owner):
        return owner + jnp.where(owner > 2 * shared, 1, 0)

    spare = r.w2s

    def gq(i, row, size):
        return rows_of((mid if i == 0 else 0) + row, size)

    def inbox(i, row, size):
        return rows_of(2 * mid + (mid if i == 0 else 0) + row, size)

    def transpose_x(a, xa, xb, xq, near, far, row):
        lanes = rows_of(shared * quarter, quarter, 128)
        r0 = MAIN - 8 * CELL + 8 * CELL * a
        for j, (c, start) in enumerate(((1, r0 - CHUNK), (0, r0), (1, r0))):
            rows = rows_of(start, ROWS)
            own = (xb if c else xa)[rows, lanes]
            both = jnp.concatenate([own, xq[0, c, rows, :]], axis=0)
            near[rows_of(row + j * quarter, quarter), 0 : 2 * ROWS] = both.T
            both = jnp.concatenate([xq[1, c, rows, :], xq[2, c, rows, :]], axis=0)
            far[rows_of(row + j * quarter, quarter), 0 : 2 * ROWS] = both.T

    def spatial_part(i, near, far, row, out_row, n):
        c0, cw = halves[n]
        rows = rows_of(row, 3 * quarter)
        acc = nn(near[rows, 0 : 2 * ROWS], r.e_all[0 : 2 * ROWS, c0 : c0 + cw])
        acc += nn(far[rows, 0 : 2 * ROWS], r.e_all[2 * ROWS : 4 * ROWS, c0 : c0 + cw])
        spare[gq(i, out_row, 3 * quarter), c0 : c0 + cw] = acc.astype(BF16)

    def spatial_grad(i, xa, xb, xq):
        def body(a, _):
            low = r.xt.at[3 * quarter : 6 * quarter, :]
            transpose_x(a, xa, xb, xq, r.xt, low, 0)
            for n in (0, 1):
                spatial_part(i, r.xt, low, 0, a * 3 * quarter, n)
            return 0

        lax.fori_loop(0, 3, body, 0)

    def transpose_v(v, sv):
        for c in range(mid // 128):
            lanes = pl.ds(128 * c, 128)
            r.xt[128 * c : 128 * c + 128, :] = jnp.concatenate([v[:, lanes], sv[:, lanes]], axis=0).T

    def temporal_grad(i, k):
        e = jnp.concatenate([r.e3[k, :, rows_of(h * half, half, 128)], r.sib_e3[k]], axis=0)
        whole[i][k * mid : (k + 1) * mid, 0:half] = nn(r.xt[...], e).astype(BF16)

    def cols_of(n):
        c0, cw = halves[n]
        return pl.ds(c0, cw)

    def s_block(i, n, owner):
        return spare.at[gq(i, grad_tap(owner) * quarter, quarter), cols_of(n)]

    def s_extra(i, n, side):
        return spare.at[gq(i, (2 * shared + 1) * quarter + side * 64, 64), cols_of(n)]

    def t_block(i, owner):
        return whole[i].at[rows_of(owner * temp, temp), 0:half]

    def t_inbox(i, n):
        return whole[i].at[rows_of(n * temp, temp), half:chan]

    def parts_of(i):
        return (0, 1) if i % 2 == 0 else (0,)

    def block_of(i, n, owner):
        return s_block(i, n, owner) if i % 2 == 0 else t_block(i, owner)

    def y_box(i, n, place):
        return spare.at[inbox(i, place * quarter, quarter), cols_of(n)] if i % 2 == 0 else t_inbox(i, place)

    def z_box(i, n, place):
        return spare.at[inbox(i, 576 + place * quarter, quarter), cols_of(n)] if i % 2 == 0 else t_inbox(i, 4 + place)

    def extra_y_box(i, n):
        return spare.at[inbox(i, 4 * quarter, 64), cols_of(n)]

    def extra_z_box(i, n, place):
        return spare.at[inbox(i, 576 + 3 * quarter + place * 64, 64), cols_of(n)]

    across = (h, w, b + 1 - 2 * par)

    def add_into(dst, parts, step):
        rows, cols = dst.shape

        def body(n, _):
            at_rows = rows_of(n * step, step)
            value = dst[at_rows, :].astype(F32)
            for part in parts:
                value = value + part[at_rows, :].astype(F32)
            dst[at_rows, :] = value.astype(BF16)
            return 0

        lax.fori_loop(0, rows // step, body, 0)

    def y_copy(i, n, d):
        place = lax.rem(bh + d, depth)
        src = block_of(i, n, 2 * place + 1 - par)
        return rc(src, y_box(i, n, place), r.y_send.at[i, n, d], r.y_recv.at[i, n, place], across)

    def z_copy(i, n, d):
        place = lax.rem(bh + d, depth)
        src = block_of(i, n, 2 * place + par)
        dev = (h, w, 2 * place + par)
        return rc(src, z_box(i, n, 3 - d), r.z_send.at[i, n, d], r.z_recv.at[i, n, 3 - d], dev)

    def extra_y(i, n):
        return rc(s_extra(i, n, 1 - par), extra_y_box(i, n), r.y_send.at[i, n, 4], r.y_recv.at[i, n, 4], across)

    def extra_z(i, n):
        place = jnp.minimum(lax.rem(bh - shared + 3 + depth, depth), 2)
        dev = (h, w, 2 * shared + par)
        return rc(
            s_extra(i, n, par), extra_z_box(i, n, place), r.z_send.at[i, n, 4], r.z_recv.at[i, n, 4 + place], dev
        )

    def step_of(i):
        return 16 if i % 2 == 0 else 48

    def reduce_start(i, n):
        for d in (1, 2, 3, 0):
            y_copy(i, n, d).start()
        if i % 2 == 0:
            extra_y(i, n).start()

    def reduce_middle(i, n):
        for d in (1, 2, 3, 0):
            place = lax.rem(bh + d, depth)
            y_copy(i, n, d).wait_send()
            box = y_box(i, n, place)
            rc(box, box, r.y_send.at[i, n, d], r.y_recv.at[i, n, place], across).wait_recv()
            add_into(block_of(i, n, 2 * place + par), [box], step_of(i))
            if d:
                z_copy(i, n, d).start()
        if i % 2 == 0:
            extra_y(i, n).wait()
            add_into(s_extra(i, n, par), [extra_y_box(i, n)], 16)
            pl.when(bh != shared)(lambda: extra_z(i, n).start())

    def final_part(i, n, side, core):
        place = 2 * side + core
        start = quarter * place - 64 * b + 512 * jnp.where(b > 2 * place, 1, 0)
        return outs[i].at[rows_of(start, quarter, 64), cols_of(n)]

    def extra_part(i, n):
        return outs[i].at[rows_of(512 * (1 - par), 64, 64), cols_of(n)]

    def final_copies(i, n):
        if i % 2:
            src = t_block(i, b)
            part = outs[i].at[h]
            return lc(src, part, r.out_sem.at[i, 0, 0]), [
                (src, part, sibling, r.cast_send.at[i, 0, 0], r.cast_recv.at[i, 0, 0])
            ]
        src = s_block(i, n, b)
        part = final_part(i, n, w, h)
        sends = [
            (src, part, dev, r.cast_send.at[i, n, d], r.cast_recv.at[i, n, d]) for d, dev in enumerate((beside, sibling))
        ]
        return lc(src, part, r.out_sem.at[i, n, 0]), sends

    def extra_copies(i, n):
        src = s_extra(i, n, par)
        part = extra_part(i, n)
        sends = [
            (src, part, dev, r.cast_send.at[i, n, 3 + d], r.cast_recv.at[i, n, 3 + d])
            for d, dev in enumerate((beside, sibling))
        ]
        return lc(src, part, r.out_sem.at[i, n, 1]), sends

    def begin(copies):
        local, sends = copies
        for src, part, dev, one, two in sends:
            rc(src, part, one, two, dev).start()
        local.start()

    def beside_copy(i):
        return rc(t_block(i, b), t_inbox(i, 7), r.z_send.at[i, 0, 4], r.z_recv.at[i, 0, 4], beside)

    def reduce_last(i, n):
        for d in (1, 2, 3):
            z_copy(i, n, d).wait()
        add_into(block_of(i, n, b), [z_box(i, n, place) for place in range(3)], step_of(i))
        if i % 2:
            beside_copy(i).start()
            return
        begin(final_copies(i, n))

        @pl.when(bh != shared)
        def _():
            extra_z(i, n).wait_send()

        @pl.when(bh == shared)
        def _():
            boxes = [extra_z_box(i, n, place) for place in range(3)]
            for place, box in enumerate(boxes):
                rc(box, box, r.z_send.at[i, n, 4], r.z_recv.at[i, n, 4 + place], across).wait_recv()
            add_into(s_extra(i, n, par), boxes, 16)
            begin(extra_copies(i, n))

    def reduce_out(i):
        beside_copy(i).wait()
        add_into(t_block(i, b), [t_inbox(i, 7)], 48)
        begin(final_copies(i, 0))

    def final_on(i, n):
        def move(part, d):
            rc(part, part, r.cast_send.at[i, n, d], r.cast_recv.at[i, n, d], beside).wait_recv()
            rc(part, part, r.cast_send.at[i, n, d + 2], r.cast_recv.at[i, n, d + 2], sibling).start()

        move(final_part(i, n, 1 - w, h), 0)
        pl.when(bh == shared_beside)(lambda: move(extra_part(i, n), 3))

    def reduce_wait(i, n):
        local, sends = final_copies(i, n)
        local.wait()
        if i % 2:
            src, part, dev, one, two = sends[0]
            rc(src, outs[i].at[1 - h], one, two, dev).wait()
            return
        for src, part, dev, one, two in sends:
            rc(src, part, one, two, dev).wait_send()

        def far(part, d):
            return rc(part, part, r.cast_send.at[i, n, d], r.cast_recv.at[i, n, d], sibling)

        far(final_part(i, n, w, 1 - h), 1).wait_recv()
        far(final_part(i, n, 1 - w, h), 2).wait_send()
        far(final_part(i, n, 1 - w, 1 - h), 2).wait_recv()
        local, sends = extra_copies(i, n)

        @pl.when(bh == shared)
        def _():
            local.wait()
            for src, part, dev, one, two in sends:
                rc(src, part, one, two, dev).wait_send()

        pl.when(bh == shared_beside)(lambda: far(extra_part(i, n), 5).wait_send())
        pl.when(bh == 2 * w + 1 - h)(lambda: far(extra_part(i, n), 4).wait_recv())
        pl.when(bh == 2 * (1 - w) + 1 - h)(lambda: far(extra_part(i, n), 5).wait_recv())

    def tile_of(ref, jh, jw):
        return ref.at[rows_of(jh * 4, 4, 4), rows_of(jw * 32, 32), :]

    def scatter(src, dst, n):
        copies = []
        for d, (j, dev) in enumerate(tile_group):
            copies.append(
                rc(src.at[j], tile_of(dst, h, w), r.tile_send.at[n, d], r.tile_recv.at[n, mine], dev)
            )
        return copies

    def scattered(src, dst, n):
        for d, (j, dev) in enumerate(tile_group):
            jh, jw = at_group(j)
            rc(src.at[j], tile_of(dst, jh, jw), r.tile_send.at[n, d], r.tile_recv.at[n, j], dev).wait()

    def tiles_start(src, dst, n):
        for copy in scatter(src, dst, n):
            copy.start()
        lc(src.at[mine], tile_of(dst, h, w), r.tile_own.at[n]).start()

    def tiles_wait(src, dst, n):
        scattered(src, dst, n)
        lc(src.at[mine], tile_of(dst, h, w), r.tile_own.at[n]).wait()

    xg, cg = r.x_grid, r.cot_grid
    tiles_start(r.x_tiles, xg, 0)
    gather_start(0)
    r.param[...] = total(0, mid, r.param_in[...])
    tiles_wait(r.x_tiles, xg, 0)

    def grid_chunk(ref, i):
        v = ref[lax.div(i, 4), rows_of(lax.rem(i, 4) * CHUNK, CHUNK), :]
        return v.astype(F32).reshape(2, CELL, chan)

    fill(r.xa, r.xb, lambda i: grid_chunk(xg, i), chan)

    def pump_loop(i, lo, hi):
        def body(s, _):
            gather_pump(i, s)
            return 0

        lax.fori_loop(lo, hi, body, 0)

    pump_loop(0, 1, nb - 1)
    gather_start(1)
    gather_pump(0, nb - 1)
    gather_start(2)
    gather_finish(0)
    tiles_start(r.cot_tiles, cg, 1)

    def first_pump(n):
        gather_pump(1, n + 1)
        pl.when(n == 3)(lambda: gather_pump(2, 1))

    conv(r.xa, r.xb, r.w1s, r.mid1, first_pump)
    gather_pump(1, nb - 1)
    gather_finish(1)
    sums = total(
        1, mid, packed(*moments(r.mid1, mid), mid), [lambda: gather_pump(2, 2), None, lambda: gather_pump(2, 3)]
    )
    prepare(0, sums, mid)

    def hidden(src, n, dst):
        value = activated(src, n, mid)

        def body(i, _):
            put(dst, i, value(i))
            return 0

        loop(CHUNKS, body, 0)

    hidden(r.mid1, 0, r.v1)
    stats = temporal(0, r.v1, r.w1t, r.time1, [lambda: gather_pump(2, 4)])
    gather_pump(2, 5)

    def sixth():
        gather_pump(2, 6)
        gather_start(3)

    sums = total(2, chan, packed(*stats, chan), [None, None, sixth])
    prepare(1, sums, chan)
    fill(r.aa, r.ab, activated(r.time1, 1, chan), chan)
    gather_pump(2, 7)
    gather_finish(2)

    conv(r.aa, r.ab, r.w2s, r.mid2, lambda n: gather_pump(3, n + 1))
    gather_pump(3, nb - 1)
    gather_finish(3)
    sums = total(3, mid, packed(*moments(r.mid2, mid), mid))
    prepare(2, sums, mid)
    hidden(r.mid2, 2, r.v2)
    stats = temporal(1, r.v2, r.w2t, r.time2)
    shared_xq2 = share_x(0, r.aa, r.xq2)
    share_v2 = share(4, r.v2, r.sib_v)
    sums = total(4, chan, packed(*stats, chan))
    tiles_wait(r.cot_tiles, cg, 1)
    prepare(3, sums, chan)

    out_grid = r.out_grid

    def grid_put(ref, i, v):
        ref[lax.div(i, 4), rows_of(lax.rem(i, 4) * CHUNK, CHUNK), :] = v.reshape(CHUNK, chan).astype(ref.dtype)

    def slope(y, s):
        return s * (1.0 + y * (1.0 - s))

    def pre_body(i, carry):
        scale, shift, inv, offset = tiles(3, chan)
        v = chunk(r.time2, i)
        y = v * scale + shift + chunk(r.xa, i, MAIN)
        s = jax.nn.sigmoid(y)
        m = keep(i)
        grid_put(out_grid, i, y * s * m)
        d = grid_chunk(cg, i) * m * slope(y, s)
        put(r.grad_pre, i, d)
        t = d * (v * inv - offset)
        return (carry[0] + d[0] + d[1], carry[1] + t[0] + t[1])

    zero_out = jnp.zeros((CELL, chan), F32)
    zero_mid = jnp.zeros((CELL, mid), F32)
    out_grid[HGT] = jnp.zeros((8 * CELL, chan), BF16)
    gg = loop(CHUNKS, pre_body, (zero_out, zero_out))

    def send_tiles(src, dst, n):
        for d, (j, dev) in enumerate(tile_group):
            jh, jw = at_group(j)
            rc(tile_of(src, jh, jw), dst.at[mine], r.tile_send.at[n, d], r.tile_recv.at[n, mine], dev).start()
        lc(tile_of(src, h, w), dst.at[mine], r.tile_own.at[n]).start()

    def sent_tiles(src, dst, n):
        for d, (j, dev) in enumerate(tile_group):
            jh, jw = at_group(j)
            rc(tile_of(src, jh, jw), dst.at[j], r.tile_send.at[n, d], r.tile_recv.at[n, j], dev).wait()
        lc(tile_of(src, h, w), dst.at[mine], r.tile_own.at[n]).wait()

    send_tiles(out_grid, r.block_out, 2)

    def norm_back(n, sums, width):
        r.norm_grads[2 * n : 2 * n + 1, 0:width] = sums[2:3] + sums[3:4]
        r.norm_grads[2 * n + 1 : 2 * n + 2, 0:width] = sums[0:1] + sums[1:2]
        back = r.back
        back[0, :, 0:width] = per_batch(sums[0:1], sums[1:2], width) / cell_count
        back[1, :, 0:width] = per_batch(sums[2:3], sums[3:4], width) / cell_count

    def through_norm(n, src, grad, i, width):
        scale, _, inv, offset = tiles(n, width)
        xhat = chunk(src, i) * inv - offset
        bias_part = r.back[0, :, 0:width][None]
        gain_part = r.back[1, :, 0:width][None]
        return scale * (chunk(grad, i, 0, width) - bias_part - xhat * gain_part) * keep(i)

    def through_act(n, src, grad, width):
        def body(i, carry):
            scale, shift, inv, offset = tiles(n, width)
            v = chunk(src, i)
            y = v * scale + shift
            s = jax.nn.sigmoid(y)
            d = chunk(grad, i, 0, width) * keep(i) * slope(y, s)
            put(grad, i, d, 0, width)
            t = d * (v * inv - offset)
            return (carry[0] + d[0] + d[1], carry[1] + t[0] + t[1])

        zero = jnp.zeros((CELL, width), F32)
        return loop(CHUNKS, body, (zero, zero))

    def to_frames(n, src, grad):
        def body(i, _):
            e = through_norm(n, src, grad, i, chan).astype(BF16)
            ef = e.astype(F32)
            r.e3[1, rows_of(i * CHUNK, CHUNK), :] = e.reshape(CHUNK, chan)
            put_lanes(r.down, rows_of(i * CHUNK + CELL, CHUNK, CELL), ef.reshape(CHUNK, chan))
            put_lanes(r.up, rows_of(i * CHUNK, CHUNK), (ef * r.gate[...][None]).reshape(CHUNK, chan))
            return 0

        loop(CHUNKS, body, 0)

    sums = total(5, chan, packed(*gg, chan))
    norm_back(3, sums, chan)
    to_frames(3, r.time2, r.grad_pre)
    shared_e3 = temporal_back(2, r.w2t)
    gg = through_act(2, r.mid2, r.grad_mid, mid)
    shared_e3.wait()
    share_v2.wait()
    def temporal_grads(i, v):
        def first():
            transpose_v(v, r.sib_v)
            temporal_grad(i, 0)

        return [first, lambda: temporal_grad(i, 1), lambda: temporal_grad(i, 2)]

    sums = total(6, mid, packed(*gg, mid), temporal_grads(3, r.v2))
    reduce_start(3, 0)
    norm_back(2, sums, mid)

    def fill_e(n, src):
        def value(i):
            v = through_norm(n, src, r.grad_mid, i, mid)
            put(r.e_all, i, v)
            return v

        fill(r.ea, r.eb, value, mid)

    fill_e(2, r.mid2)
    share_e(0)
    conv_back(r.ea, r.eb, r.w2s, r.grad_mid)
    gg = through_act(1, r.time1, r.grad_mid, chan)
    for copy in shared_xq2:
        copy.wait()
    spread_x(r.xq2)
    for n in (0, 1):
        share_e_on(0, n)
    for n in (0, 1):
        share_e_wait(0, n)

    def second_spatial():
        spatial_grad(2, r.aa, r.ab, r.xq2)

    sums = total(7, chan, packed(*gg, chan), [second_spatial])
    reduce_middle(3, 0)
    for n in (0, 1):
        reduce_start(2, n)
    share_v1 = share(5, r.v1, r.sib_v)
    shared_xq1 = share_x(1, r.xa, r.xq1)
    norm_back(1, sums, chan)
    to_frames(1, r.time1, r.grad_mid)
    shared_e3 = temporal_back(3, r.w1t)
    reduce_last(3, 0)
    gg = through_act(0, r.mid1, r.grad_mid, mid)
    shared_e3.wait()
    share_v1.wait()
    sums = total(8, mid, packed(*gg, mid), temporal_grads(1, r.v1))
    reduce_start(1, 0)
    norm_back(0, sums, mid)
    fill_e(0, r.mid1)
    share_e(1)
    reduce_out(3)
    for n in (0, 1):
        reduce_middle(2, n)
    for copy in shared_xq1:
        copy.wait()
    spread_x(r.xq1)
    sent_tiles(out_grid, r.block_out, 2)
    conv_back(r.ea, r.eb, r.w1s, r.grad_mid)
    share_e_on(1, 0)
    near, far = r.w1s.at[0:mid, :], r.w1s.at[mid : 2 * mid, :]

    def transposes(a, _):
        transpose_x(a, r.xa, r.xb, r.xq1, near, far, a * 3 * quarter)
        return 0

    lax.fori_loop(0, 3, transposes, 0)
    for n in (0, 1):
        share_e_wait(1, n)

        def body(a, _, n=n):
            spatial_part(0, near, far, a * 3 * quarter, a * 3 * quarter, n)
            return 0

        lax.fori_loop(0, 3, body, 0)
        reduce_start(0, n)
        if n == 0:
            share_e_on(1, 1)

    def last_body(i, _):
        grid_put(out_grid, i, (chunk(r.grad_mid, i, 0, chan) + chunk(r.grad_pre, i)) * keep(i))
        return 0

    loop(CHUNKS, last_body, 0)
    send_tiles(out_grid, r.grad_input, 3)
    for n in (0, 1):
        reduce_last(2, n)
    reduce_middle(1, 0)
    for n in (0, 1):
        final_on(2, n)
    reduce_middle(0, 0)
    reduce_last(1, 0)
    reduce_out(1)
    reduce_last(0, 0)
    reduce_middle(0, 1)
    final_on(0, 0)
    reduce_last(0, 1)
    sent_tiles(out_grid, r.grad_input, 3)
    for n in (0, 1):
        reduce_wait(2, n)
    reduce_wait(3, 0)
    final_on(0, 1)
    reduce_wait(1, 0)
    for n in (0, 1):
        reduce_wait(0, n)


def per_device_fast(nb, *args):
    (
        inputs,
        starts,
        first_spatial,
        first_mid_gain,
        first_mid_bias,
        first_temporal,
        first_out_gain,
        first_out_bias,
        second_spatial,
        second_mid_gain,
        second_mid_bias,
        second_temporal,
        second_out_gain,
        second_out_bias,
        cotangent,
    ) = args
    micro, frames, side, _, chan = inputs.shape
    mid = first_spatial.shape[1]
    spat, temp = first_spatial.shape[0], first_temporal.shape[0]
    few = frames // 4
    h, w, b = (lax.axis_index(name) for name in ("ha", "wa", "batch"))
    mine = (1 - w) * h + w * (3 - h)
    offsets = jnp.arange(side)
    valid = (h * side + offsets < HGT)[:, None] & (w * side + offsets < HGT)[None, :]

    def tiles(array):
        array = array * valid.astype(BF16)[None, None, :, :, None]
        array = array.reshape(micro, 4, few, side, side, chan).transpose(1, 3, 4, 0, 2, 5)
        return array.reshape(4, side, side * micro * few, chan)

    def untiled(array):
        array = array.reshape(4, side, side, micro, few, chan).transpose(3, 0, 4, 1, 2, 5)
        return array.reshape(micro, frames, side, side, chan).astype(F32)

    gate = (1 - lax.dynamic_slice_in_dim(starts, mine * few, few, axis=1)).astype(F32)
    gate = jnp.broadcast_to(gate.reshape(micro * few, 1), (micro * few, chan))
    here = jnp.where((h == 0) & (w == 0), 1.0, 0.0)

    def placed(shard):
        row = jnp.zeros((mid,), F32)
        return lax.dynamic_update_slice(row, shard.astype(F32) * here, (b * shard.shape[0],))

    param = jnp.stack(
        [
            placed(v)
            for v in (
                first_mid_gain,
                first_mid_bias,
                first_out_gain,
                first_out_bias,
                second_mid_gain,
                second_mid_bias,
                second_out_gain,
                second_out_bias,
            )
        ]
    )
    half = chan // 2
    few_rows = ROWS // 4

    inputs_of = dict(
        x_tiles=(tiles(inputs), pl.ANY),
        cot_tiles=(tiles(cotangent), pl.ANY),
        gate=(gate, pltpu.VMEM),
        param_in=(param, pltpu.VMEM),
        first_spatial=(first_spatial, pl.ANY),
        first_temporal=(first_temporal, pl.ANY),
        second_spatial=(second_spatial, pl.ANY),
        second_temporal=(second_temporal, pl.ANY),
    )
    outputs_of = dict(
        block_out=((4, side, side * CELL, chan), BF16, pl.ANY),
        grad_input=((4, side, side * CELL, chan), BF16, pl.ANY),
        norm_grads=((8, mid), F32, pltpu.VMEM),
        out1s=((spat, mid), BF16, pl.ANY),
        out1t=((2, temp, half), BF16, pl.ANY),
        out2s=((spat, mid), BF16, pl.ANY),
        out2t=((2, temp, half), BF16, pl.ANY),
    )
    dma = pltpu.SemaphoreType.DMA
    scratch_of = dict(
        w1s=pltpu.VMEM((9 * chan, mid), BF16),
        w1t=pltpu.VMEM((3 * mid, chan), BF16),
        w2s=pltpu.VMEM((9 * chan, mid), BF16),
        w2t=pltpu.VMEM((3 * mid, chan), BF16),
        x_grid=pltpu.VMEM((8, 8 * CELL, chan), BF16),
        cot_grid=pltpu.VMEM((8, 8 * CELL, chan), BF16),
        out_grid=pltpu.VMEM((8, 8 * CELL, chan), BF16),
        xa=pltpu.VMEM((PADDED, chan), BF16),
        xb=pltpu.VMEM((PADDED, chan), BF16),
        aa=pltpu.VMEM((PADDED, chan), BF16),
        ab=pltpu.VMEM((PADDED, chan), BF16),
        ea=pltpu.VMEM((PADDED, mid), BF16),
        eb=pltpu.VMEM((PADDED, mid), BF16),
        mid1=pltpu.VMEM((ROWS, mid), F32),
        mid2=pltpu.VMEM((ROWS, mid), F32),
        grad_mid=pltpu.VMEM((ROWS, mid), F32),
        v1=pltpu.VMEM((ROWS, mid), BF16),
        v2=pltpu.VMEM((ROWS, mid), BF16),
        time1=pltpu.VMEM((ROWS, chan), F32),
        time2=pltpu.VMEM((ROWS, chan), F32),
        grad_pre=pltpu.VMEM((ROWS, chan), F32),
        down=pltpu.VMEM((chan // 128, ROWS + CHUNK, 128), F32),
        up=pltpu.VMEM((chan // 128, ROWS + CHUNK, 128), F32),
        e3=pltpu.VMEM((3, ROWS, chan), BF16),
        sib_e3=pltpu.VMEM((3, ROWS, half), BF16),
        halo_out=pltpu.VMEM((2, few_rows, chan), BF16),
        halo_in=pltpu.VMEM((4, 2, few_rows, chan), BF16),
        param=pltpu.VMEM((8, mid), F32),
        tile_mid=pltpu.VMEM((2, 4, CELL, mid), F32),
        tile_out=pltpu.VMEM((2, 4, CELL, chan), F32),
        back=pltpu.VMEM((2, CELL, mid), F32),
        sum_a=pltpu.VMEM((2, 2, 8, mid), F32),
        sum_b=pltpu.VMEM((2, 4, 8, mid), F32),
        sum_c=pltpu.VMEM((2, nb // 2, 8, mid), F32),
        own_sem=dma((4,)),
        ring_send=dma((4, 2, nb)),
        ring_recv=dma((4, 2, nb)),
        sib_send=dma((4, 3, nb)),
        sib_recv=dma((4, 3, nb)),
        over_send=dma((4, nb)),
        over_recv=dma((4, nb)),
        sa_send=dma((9,)),
        sa_recv=dma((9,)),
        sb_send=dma((9, 3)),
        sb_recv=dma((9, 4)),
        sc_send=dma((9, nb // 2)),
        sc_recv=dma((9, nb // 2)),
        halo_send=dma((4, 2)),
        halo_recv=dma((4, 2)),
        share_send=dma((6,)),
        share_recv=dma((6,)),
        e_all=pltpu.VMEM((4 * ROWS, mid), BF16),
        xq1=pltpu.VMEM((3, 2, PADDED, chan // 4), BF16),
        xq2=pltpu.VMEM((3, 2, PADDED, chan // 4), BF16),
        xt=pltpu.VMEM((mid, 2 * ROWS), BF16),
        sib_v=pltpu.VMEM((ROWS, mid), BF16),
        e_send=dma((2, 2, 3)),
        e_recv=dma((2, 2, 3)),
        xq_send=dma((2, 3)),
        xq_recv=dma((2, 3)),
        y_send=dma((4, 2, 5)),
        y_recv=dma((4, 2, 5)),
        z_send=dma((4, 2, 5)),
        z_recv=dma((4, 2, 7)),
        cast_send=dma((4, 2, 6)),
        cast_recv=dma((4, 2, 8)),
        out_sem=dma((4, 2, 2)),
        tile_send=dma((4, 3)),
        tile_recv=dma((4, 4)),
        tile_own=dma((4,)),
    )
    names = (*inputs_of, *outputs_of, *scratch_of)
    cell_count = float(frames * nb * HGT * HGT)
    results = pl.pallas_call(
        functools.partial(block_kernel, (nb, chan, mid, cell_count), names),
        out_shape=[jax.ShapeDtypeStruct(shape, dtype) for shape, dtype, _ in outputs_of.values()],
        in_specs=[pl.BlockSpec(memory_space=space) for _, space in inputs_of.values()],
        out_specs=[pl.BlockSpec(memory_space=space) for _, _, space in outputs_of.values()],
        scratch_shapes=list(scratch_of.values()),
        compiler_params=pltpu.CompilerParams(
            collective_id=0, has_side_effects=True, vmem_limit_bytes=VMEM_LIMIT
        ),
    )(*(array for array, _ in inputs_of.values()))
    got = SimpleNamespace(**dict(zip(outputs_of, results)))

    def temporal(pair):
        return jnp.concatenate([pair[0], pair[1]], axis=1).astype(F32)

    def norm(row, like):
        size = like.shape[0]
        return lax.dynamic_slice_in_dim(got.norm_grads[row], b * size, size)

    return (
        untiled(got.block_out),
        untiled(got.grad_input),
        got.out1s.astype(F32),
        norm(0, first_mid_gain),
        norm(1, first_mid_bias),
        temporal(got.out1t),
        norm(2, first_out_gain),
        norm(3, first_out_bias),
        got.out2s.astype(F32),
        norm(4, second_mid_gain),
        norm(5, second_mid_bias),
        temporal(got.out2t),
        norm(6, second_out_gain),
        norm(7, second_out_bias),
    )


def extended(shard, sides, width):
    for axis, dim in sides:
        count, length = (lax.axis_size(axis), shard.shape[dim])
        up = [(i, (i + 1) % count) for i in range(count - 1)]
        down = [(j, i) for i, j in up]
        last = lax.slice_in_dim(shard, length - width, length, axis=dim)
        leading = lax.slice_in_dim(shard, 0, width, axis=dim)
        before = lax.ppermute(last, axis, up)
        after = lax.ppermute(leading, axis, down)
        shard = jnp.concatenate([before, shard, after], axis=dim)
    return shard


def passed_along(shard, axis, by):
    count = lax.axis_size(axis)
    pairs = [(i, i + by) for i in range(count) if 0 <= i + by < count]
    return lax.ppermute(shard, axis, pairs)


def for_sending(shard):

    def short(part):
        return part.astype(jnp.bfloat16) if part.dtype == jnp.float32 else part

    return jax.tree.map(short, shard)


def silu_slope(values):
    sigma = jax.nn.sigmoid(values)
    return sigma * (1.0 + values * (1.0 - sigma))


def spatial_forward(field_in, kernel):
    frames, tile_side = (field_in.shape[0], field_in.shape[1])
    padded = extended(field_in, (("ha", 1), ("wa", 2)), 1)
    pieces = [
        padded[:, offset // 3 : offset // 3 + tile_side, offset % 3 : offset % 3 + tile_side, :]
        for offset in range(9)
    ]
    patches = jnp.concatenate(pieces, axis=-1).reshape(frames * tile_side * tile_side, -1)
    return (patches, jnp.dot(patches, kernel, preferred_element_type=jnp.float32))


def spatial_backward(grad_out, patches, kernel):
    frames, tile_side, channels = (grad_out.shape[0], grad_out.shape[1], grad_out.shape[3])
    row_count = frames * tile_side * tile_side
    padded = extended(grad_out, (("ha", 1), ("wa", 2)), 1)
    pieces = [
        padded[
            :,
            2 - offset // 3 : 2 - offset // 3 + tile_side,
            2 - offset % 3 : 2 - offset % 3 + tile_side,
            :,
        ]
        for offset in range(9)
    ]
    stacked = jnp.concatenate(pieces, axis=-1).reshape(row_count, 9, channels)
    grad_in = jnp.einsum(
        "rkm,kcm->rc", stacked, kernel.reshape(9, -1, channels), preferred_element_type=jnp.float32
    )
    grad_kernel = jnp.einsum(
        "rk,rm->km",
        patches,
        grad_out.reshape(row_count, channels),
        preferred_element_type=jnp.float32,
    )
    return (grad_in, grad_kernel)


def temporal_forward(field_in, clip_gate, kernel):
    frames, tile_side = (field_in.shape[0], field_in.shape[1])
    gated_in = field_in * clip_gate
    earlier = passed_along(field_in[-1:], "batch", 1)
    later_frame = passed_along(gated_in[:1], "batch", -1)
    before = jnp.concatenate([earlier, field_in[:-1]], axis=0) * clip_gate
    after_tap = jnp.concatenate([gated_in[1:], later_frame], axis=0)
    joined = jnp.concatenate([before, field_in, after_tap], axis=-1).reshape(
        frames * tile_side * tile_side, -1
    )
    return (joined, jnp.dot(joined, kernel, preferred_element_type=jnp.float32))


def temporal_backward(grad_out, joined, clip_gate, kernel):
    frames, tile_side, channels = (grad_out.shape[0], grad_out.shape[1], grad_out.shape[3])
    row_count = frames * tile_side * tile_side
    gated_grad = grad_out * clip_gate
    later_frame = passed_along(gated_grad[:1], "batch", -1)
    earlier = passed_along(grad_out[-1:], "batch", 1)
    from_later = jnp.concatenate([gated_grad[1:], later_frame], axis=0)
    from_earlier = jnp.concatenate([earlier, grad_out[:-1]], axis=0) * clip_gate
    stacked = jnp.concatenate([from_later, grad_out, from_earlier], axis=-1).reshape(
        row_count, 3, channels
    )
    grad_in = jnp.einsum(
        "rkc,kmc->rm", stacked, kernel.reshape(3, -1, channels), preferred_element_type=jnp.float32
    )
    grad_kernel = jnp.einsum(
        "rk,rc->kc",
        joined,
        grad_out.reshape(row_count, channels),
        preferred_element_type=jnp.float32,
    )
    return (grad_in, grad_kernel)


def norm_forward(pre_norm, norm_gain, norm_bias, valid_rows, cell_count):
    first_sum = jnp.sum(pre_norm * valid_rows, axis=0)
    square_sum = jnp.sum(pre_norm * pre_norm * valid_rows, axis=0)
    first_sum, square_sum = lax.psum((first_sum, square_sum), ("ha", "wa", "batch"))
    mean_val = first_sum / cell_count
    inv_std = lax.rsqrt(square_sum / cell_count - mean_val * mean_val + epsilon)
    normed = (pre_norm - mean_val) * inv_std
    return (normed, inv_std, normed * norm_gain.astype(jnp.float32) + norm_bias.astype(jnp.float32))


def norm_backward(grad_norm, normed, inv_std, norm_gain, valid_rows, cell_count):
    bias_grad = jnp.sum(grad_norm, axis=0)
    gain_grad = jnp.sum(grad_norm * normed, axis=0)
    bias_grad, gain_grad = lax.psum((bias_grad, gain_grad), ("ha", "wa", "batch"))
    grad_in = (
        valid_rows
        * norm_gain.astype(jnp.float32)
        * inv_std
        * (grad_norm - bias_grad / cell_count - normed * gain_grad / cell_count)
    )
    return (grad_in, gain_grad, bias_grad)


def forward_pair(field_in, weights, clip_gate, valid_rows, cell_count):
    frames, tile_side = (field_in.shape[0], field_in.shape[1])
    patches, spatial_out = spatial_forward(field_in, weights[0])
    mid_hat, mid_scale, mid_norm = norm_forward(
        spatial_out, weights[1], weights[2], valid_rows, cell_count
    )
    hidden = (
        (jax.nn.silu(mid_norm) * valid_rows)
        .astype(jnp.bfloat16)
        .reshape(frames, tile_side, tile_side, -1)
    )
    joined, temporal_out = temporal_forward(hidden, clip_gate, weights[3])
    out_hat, out_scale, out_norm = norm_forward(
        temporal_out, weights[4], weights[5], valid_rows, cell_count
    )
    return ((patches, mid_hat, mid_scale, mid_norm, joined, out_hat, out_scale), out_norm)


def backward_pair(grad_norm, kept, weights, clip_gate, valid_rows, cell_count, tile_side):
    patches, mid_hat, mid_scale, mid_norm, joined, out_hat, out_scale = kept
    frames = clip_gate.shape[0]
    grad_time, out_gain_grad, out_bias_grad = norm_backward(
        grad_norm, out_hat, out_scale, weights[4], valid_rows, cell_count
    )
    grad_time = grad_time.astype(jnp.bfloat16).reshape(frames, tile_side, tile_side, -1)
    grad_hidden, temporal_grad = temporal_backward(grad_time, joined, clip_gate, weights[3])
    grad_mid = grad_hidden * valid_rows * silu_slope(mid_norm)
    grad_spatial, mid_gain_grad, mid_bias_grad = norm_backward(
        grad_mid, mid_hat, mid_scale, weights[1], valid_rows, cell_count
    )
    grad_spatial = grad_spatial.astype(jnp.bfloat16).reshape(frames, tile_side, tile_side, -1)
    grad_in, spatial_grad = spatial_backward(grad_spatial, patches, weights[0])
    return (
        grad_in,
        (spatial_grad, mid_gain_grad, mid_bias_grad, temporal_grad, out_gain_grad, out_bias_grad),
    )


def per_device(
    inputs,
    starts,
    first_spatial,
    first_mid_gain,
    first_mid_bias,
    first_temporal,
    first_out_gain,
    first_out_bias,
    second_spatial,
    second_mid_gain,
    second_mid_bias,
    second_temporal,
    second_out_gain,
    second_out_bias,
    cotangent,
):
    shards = (
        first_spatial,
        first_mid_gain,
        first_mid_bias,
        first_temporal,
        first_out_gain,
        first_out_bias,
        second_spatial,
        second_mid_gain,
        second_mid_bias,
        second_temporal,
        second_out_gain,
        second_out_bias,
    )
    micro_total, frames, tile_side, channels = (
        inputs.shape[0],
        inputs.shape[1],
        inputs.shape[2],
        inputs.shape[4],
    )
    row_count = frames * tile_side * tile_side
    cell_count = frames * lax.axis_size("batch") * HGT * HGT
    offsets = jnp.arange(tile_side)
    inside_h = lax.axis_index("ha") * tile_side + offsets < HGT
    inside_w = lax.axis_index("wa") * tile_side + offsets < HGT
    valid_grid = inside_h[:, None] & inside_w[None, :]
    valid_tile = valid_grid.astype(jnp.bfloat16)[None, :, :, None]
    valid_rows = jnp.broadcast_to(
        valid_grid.astype(jnp.float32)[None], (frames, tile_side, tile_side)
    ).reshape(row_count, 1)
    results = []
    input_grads = []
    kernel_total = None
    norm_total = None
    for micro_step in range(micro_total):
        gathered = (
            lax.all_gather(shards[0], "batch", axis=0, tiled=True),
            lax.all_gather(shards[1], "batch", axis=0, tiled=True),
            lax.all_gather(shards[2], "batch", axis=0, tiled=True),
            lax.all_gather(shards[3], "batch", axis=0, tiled=True),
            lax.all_gather(shards[4], "batch", axis=0, tiled=True),
            lax.all_gather(shards[5], "batch", axis=0, tiled=True),
            lax.all_gather(shards[6], "batch", axis=0, tiled=True),
            lax.all_gather(shards[7], "batch", axis=0, tiled=True),
            lax.all_gather(shards[8], "batch", axis=0, tiled=True),
            lax.all_gather(shards[9], "batch", axis=0, tiled=True),
            lax.all_gather(shards[10], "batch", axis=0, tiled=True),
            lax.all_gather(shards[11], "batch", axis=0, tiled=True),
        )
        clip_gate = (1 - starts[micro_step]).astype(jnp.bfloat16).reshape(frames, 1, 1, 1)
        x_in = inputs[micro_step] * valid_tile
        first_kept, first_norm = forward_pair(
            x_in, gathered[0:6], clip_gate, valid_rows, cell_count
        )
        first_act = (
            (jax.nn.silu(first_norm) * valid_rows)
            .astype(jnp.bfloat16)
            .reshape(frames, tile_side, tile_side, channels)
        )
        second_kept, second_norm = forward_pair(
            first_act, gathered[6:12], clip_gate, valid_rows, cell_count
        )
        pre_out = second_norm + x_in.reshape(row_count, channels).astype(jnp.float32)
        results.append(
            (jax.nn.silu(pre_out) * valid_rows).reshape(frames, tile_side, tile_side, channels)
        )
        grad_pre = (
            cotangent[micro_step].reshape(row_count, channels).astype(jnp.float32)
            * valid_rows
            * silu_slope(pre_out)
        )
        grad_act, second_grads = backward_pair(
            grad_pre, second_kept, gathered[6:12], clip_gate, valid_rows, cell_count, tile_side
        )
        grad_first = grad_act * valid_rows * silu_slope(first_norm)
        grad_conv, first_grads = backward_pair(
            grad_first, first_kept, gathered[0:6], clip_gate, valid_rows, cell_count, tile_side
        )
        input_grads.append(
            ((grad_conv + grad_pre) * valid_rows).reshape(frames, tile_side, tile_side, channels)
        )
        step_grads = first_grads + second_grads
        kernel_now = (step_grads[0], step_grads[3], step_grads[6], step_grads[9])
        norm_now = (
            step_grads[1],
            step_grads[2],
            step_grads[4],
            step_grads[5],
            step_grads[7],
            step_grads[8],
            step_grads[10],
            step_grads[11],
        )
        if micro_step == 0:
            kernel_total = kernel_now
            norm_total = norm_now
        else:
            kernel_total = jax.tree.map(jnp.add, kernel_total, kernel_now)
            norm_total = jax.tree.map(jnp.add, norm_total, norm_now)
    kernel_total = lax.psum_scatter(kernel_total, "batch", scatter_dimension=0, tiled=True)
    kernel_total = jax.tree.map(
        lambda part: part.astype(jnp.float32), lax.psum(for_sending(kernel_total), ("ha", "wa"))
    )
    shard_index = lax.axis_index("batch")
    batch_count = lax.axis_size("batch")
    norm_shards = tuple(
        (
            lax.dynamic_slice_in_dim(
                full_sum,
                shard_index * (full_sum.shape[0] // batch_count),
                full_sum.shape[0] // batch_count,
            )
            for full_sum in norm_total
        )
    )
    return (
        jnp.stack(results),
        jnp.stack(input_grads),
        kernel_total[0],
        norm_shards[0],
        norm_shards[1],
        kernel_total[1],
        norm_shards[2],
        norm_shards[3],
        kernel_total[2],
        norm_shards[4],
        norm_shards[5],
        kernel_total[3],
        norm_shards[6],
        norm_shards[7],
    )


def solution(mesh):
    in_specs = (
        P(None, "batch", "ha", "wa", None),
        P(None, "batch"),
        P("batch", None),
        P("batch"),
        P("batch"),
        P("batch", None),
        P("batch"),
        P("batch"),
        P("batch", None),
        P("batch"),
        P("batch"),
        P("batch", None),
        P("batch"),
        P("batch"),
        P(None, "batch", "ha", "wa", None),
    )
    out_specs = (
        P(None, "batch", "ha", "wa", None),
        P(None, "batch", "ha", "wa", None),
        P("batch", None),
        P("batch"),
        P("batch"),
        P("batch", None),
        P("batch"),
        P("batch"),
        P("batch", None),
        P("batch"),
        P("batch"),
        P("batch", None),
        P("batch"),
        P("batch"),
    )
    batch = mesh.shape["batch"]

    def program(*args):
        spat, temp = args[2].shape[0], args[5].shape[0]
        fits = args[0].shape == (2, 16, 4, 4, 512) and args[2].shape[1] == 1152
        if fits and batch == 8 and spat * batch == 9 * 512 and temp * batch == 3 * 1152:
            return per_device_fast(batch, *args)
        return per_device(*args)

    return jax.shard_map(
        program, mesh=mesh, in_specs=in_specs, out_specs=out_specs, check_vma=False
    )
```

```python
import functools
from types import SimpleNamespace

import jax
import jax.numpy as jnp
from jax import lax
from jax.experimental import pallas as pl
from jax.experimental.pallas import tpu as pltpu
from jax.sharding import PartitionSpec as P

HGT = 7
epsilon = 1e-05
MESH = pl.DeviceIdType.MESH
F32 = jnp.float32
BF16 = jnp.bfloat16

BASE = 10
CELL = 8
ROWS = HGT * 8 * CELL
PADDED = (BASE + HGT * 8 + BASE) * CELL
MAIN = BASE * CELL
CHUNK = 2 * CELL
CHUNKS = ROWS // CHUNK
VMEM_LIMIT = 64 * 1024 * 1024 - 1024 * 1024


def when(cond, work):
    if cond is True:
        work()
    elif cond is not False:
        pl.when(cond)(work)


def loop(count, body, init):
    def twice(i, carry):
        return body(2 * i + 1, body(2 * i, carry))

    return lax.fori_loop(0, count // 2, twice, init)


def sigmoid(x):
    return 0.5 * jnp.tanh(0.5 * x) + 0.5


def nn(a, b):
    return jnp.dot(a, b, preferred_element_type=F32)


def nt(a, b):
    return lax.dot_general(a, b, (((1,), (1,)), ((), ())), preferred_element_type=F32)


def tn(a, b):
    return lax.dot_general(a, b, (((0,), (0,)), ((), ())), preferred_element_type=F32)


def rows_of(start, size, step=16):
    if not isinstance(start, int):
        start = pl.multiple_of(start, step)
    return pl.ds(start, size)


def per_batch(first, second, width):
    return jnp.concatenate(
        [jnp.broadcast_to(first, (CELL // 2, width)), jnp.broadcast_to(second, (CELL // 2, width))], axis=0
    )


def block_kernel(dims, names, *all_refs):
    r = SimpleNamespace(**dict(zip(names, all_refs, strict=True)))
    nb, chan, mid, cell_count = dims
    spat = 9 * chan // nb
    temp = 3 * mid // nb
    unit = spat // 6
    quarter = chan // 4
    half = chan // 2
    h = lax.axis_index("ha")
    w = lax.axis_index("wa")
    b = lax.axis_index("batch")
    par = lax.rem(b, 2)
    bh = lax.div(b, 2)
    pos = par * (nb - 1 - bh) + (1 - par) * bh
    way = 1 - 2 * h

    def at(p):
        p = lax.rem(p + 4 * nb, nb)
        upper = lax.div(p, nb // 2)
        return (1 - upper) * (2 * p) + upper * (2 * (nb - 1 - p) + 1)

    def at_group(j):
        jw = lax.div(j, 2)
        odd = lax.rem(j, 2)
        return (odd * (1 - jw) + (1 - odd) * jw, jw)

    mine = (1 - w) * h + w * (3 - h)
    sibling = (1 - h, w, b)
    beside = (h, 1 - w, b)
    onward = (h, w, at(pos + way))
    behind = (h, w, at(pos - way))
    later = lax.rem(mine + 1, 4)
    earlier = lax.rem(mine + 3, 4)
    later_dev = (*at_group(later), lax.rem(b + lax.div(mine + 1, 4), nb))
    earlier_dev = (*at_group(earlier), lax.rem(b + nb - lax.div(4 - mine, 4), nb))
    tile_group = [(lax.rem(mine + d, 4), (*at_group(lax.rem(mine + d, 4)), b)) for d in (1, 2, 3)]
    pos_b = w * 2 + par
    plane = []
    for d in (1, 2, 3):
        q = lax.rem(pos_b + d, 4)
        plane.append((q, (h, lax.div(q, 2), b - par + lax.rem(q, 2))))
    depth = nb // 2
    line = []
    for d in range(1, depth):
        q = lax.rem(bh + d, depth)
        line.append((q, (h, w, 2 * q + par)))

    def named(dev):
        return dict(ha=dev[0], wa=dev[1], batch=dev[2])

    def rc(src, dst, send, recv, dev):
        return pltpu.make_async_remote_copy(
            src_ref=src, dst_ref=dst, send_sem=send, recv_sem=recv, device_id=named(dev), device_id_type=MESH
        )

    def lc(src, dst, sem):
        return pltpu.make_async_copy(src, dst, sem)

    partners = [sibling, beside, onward, behind, later_dev, earlier_dev]
    partners += [dev for _, dev in tile_group + plane + line]
    barrier = pltpu.get_barrier_semaphore()
    for dev in partners:
        pl.semaphore_signal(barrier, inc=1, device_id=named(dev), device_id_type=MESH)
    pl.semaphore_wait(barrier, len(partners))

    shards = (r.first_spatial, r.first_temporal, r.second_spatial, r.second_temporal)
    whole = (r.w1s, r.w1t, r.w2s, r.w2t)
    shared = 2 * w + h
    shared_beside = 2 * (1 - w) + h
    third = temp // 3

    def units(i, core, side):
        return (2 * side + core, 4 + core) if i % 2 == 0 else ((1 - core) * side + 2 * core,)

    def piece(i, ref, owner, u):
        if i % 2 == 0:
            return ref.at[rows_of(owner * spat + u * unit, unit), :]
        return ref.at[rows_of(owner * temp + u * third, third), :]

    def streams(i):
        return (0, 1) if i % 2 == 0 else (0,)

    def crossing(i, work):
        if i % 2 == 0:
            work()
        else:
            pl.when(h == 0)(work)

    def crossed(i, work):
        if i % 2 == 0:
            work()
        else:
            pl.when(h == 1)(work)

    def own_copy(i):
        rows = spat if i % 2 == 0 else temp
        return lc(shards[i], whole[i].at[rows_of(b * rows, rows), :], r.own_sem.at[i])

    def ring(i, st, s, owner, from_shard=False):
        u = units(i, h, w)[st]
        dst = piece(i, whole[i], owner, u)
        src = piece(i, shards[i], 0, u) if from_shard else dst
        return rc(src, dst, r.ring_send.at[i, st, s], r.ring_recv.at[i, st, s], onward)

    def cross(i, kind, s, owner, u):
        part = piece(i, whole[i], owner, u)
        return rc(part, part, r.sib_send.at[i, kind, s], r.sib_recv.at[i, kind, s], sibling)

    def over(i, s, owner, u):
        part = piece(i, whole[i], owner, u)
        return rc(part, part, r.over_send.at[i, s], r.over_recv.at[i, s], beside)

    def gather_start(i):
        for st in streams(i):
            ring(i, st, 1, b, True).start()
        own_copy(i).start()

    def gather_relay(i, s):
        owner = at(pos - way * s)

        def work():
            over(i, s, owner, units(i, h, 1 - w)[0]).wait_recv()
            cross(i, 2, s, owner, units(i, h, 1 - w)[0]).start()

        crossing(i, work)

    def gather_pump(i, s):
        owner = at(pos - way * s)
        own = units(i, h, w)
        for st in streams(i):
            ring(i, st, s, owner).wait_recv()
            if isinstance(s, int):
                if s < nb - 1:
                    ring(i, st, s + 1, owner).start()
            else:
                pl.when(s < nb - 1)(lambda st=st: ring(i, st, s + 1, owner).start())
            if st == 0:
                crossing(i, lambda: over(i, s, owner, own[0]).start())
            cross(i, st, s, owner, own[st]).start()
        if isinstance(s, int):
            if s > 1:
                gather_relay(i, s - 1)
        else:
            pl.when(s > 1)(lambda: gather_relay(i, s - 1))

    def gather_finish(i):
        gather_relay(i, nb - 1)

        def body(s, _):
            owner = at(pos - way * s)
            theirs = at(pos + way * s)
            for st in streams(i):
                ring(i, st, s, owner).wait_send()
                cross(i, st, s, owner, units(i, h, w)[st]).wait_send()
                cross(i, st, s, theirs, units(i, 1 - h, w)[st]).wait_recv()

            def sent():
                over(i, s, owner, units(i, h, w)[0]).wait_send()
                cross(i, 2, s, owner, units(i, h, 1 - w)[0]).wait_send()

            crossing(i, sent)
            crossed(i, lambda: cross(i, 2, s, theirs, units(i, 1 - h, 1 - w)[0]).wait_recv())
            return 0

        lax.fori_loop(1, nb, body, 0)
        own_copy(i).wait()

    def total(k, width, value, works=()):
        slot = k % 2
        wide = value.shape[1]
        cols = pl.ds(0, wide)
        works = list(works) + [None] * 3
        pair, four, far = r.sum_a, r.sum_b, r.sum_c
        pair[slot, h, :, cols] = value
        part = pair.at[slot, h, :, cols]
        send_a = rc(part, part, r.sa_send.at[k], r.sa_recv.at[k], sibling)
        send_a.start()
        if works[0]:
            works[0]()
        part = pair.at[slot, 1 - h, :, cols]
        rc(part, part, r.sa_send.at[k], r.sa_recv.at[k], sibling).wait_recv()
        four[slot, pos_b, :, cols] = pair[slot, 0, :, cols] + pair[slot, 1, :, cols]
        sends = [send_a]
        for n, (q, dev) in enumerate(plane):
            part = four.at[slot, pos_b, :, cols]
            sends.append(rc(part, part, r.sb_send.at[k, n], r.sb_recv.at[k, pos_b], dev))
            sends[-1].start()
        if works[1]:
            works[1]()
        for n, (q, dev) in enumerate(plane):
            part = four.at[slot, q, :, cols]
            rc(part, part, r.sb_send.at[k, n], r.sb_recv.at[k, q], dev).wait_recv()
        far[slot, bh, :, cols] = (four[slot, 0, :, cols] + four[slot, 1, :, cols]) + (
            four[slot, 2, :, cols] + four[slot, 3, :, cols]
        )
        for n, (q, dev) in enumerate(line):
            part = far.at[slot, bh, :, cols]
            sends.append(rc(part, part, r.sc_send.at[k, n], r.sc_recv.at[k, bh], dev))
            sends[-1].start()
        if works[2]:
            works[2]()
        for n, (q, dev) in enumerate(line):
            part = far.at[slot, q, :, cols]
            rc(part, part, r.sc_send.at[k, n], r.sc_recv.at[k, q], dev).wait_recv()
        result = far[slot, 0, :, cols]
        for q in range(1, depth):
            result = result + far[slot, q, :, cols]
        for send in sends:
            send.wait_send()
        if wide == width:
            return result
        return jnp.concatenate([result[0:4], result[4:8, 2 * wide - width :]], axis=1)

    def chunk(ref, i, base=0, width=None):
        cols = slice(None) if width is None else pl.ds(0, width)
        value = ref[rows_of(base + i * CHUNK, CHUNK), cols]
        return value.astype(F32).reshape(2, CELL, value.shape[-1])

    def put(ref, i, value, base=0, width=None):
        cols = slice(None) if width is None else pl.ds(0, width)
        ref[rows_of(base + i * CHUNK, CHUNK), cols] = value.reshape(CHUNK, value.shape[-1]).astype(ref.dtype)

    def keep(i):
        inside = jnp.where(lax.rem(i, 4) == 3, 0.0, 1.0).astype(F32)
        first = lax.broadcasted_iota(jnp.int32, (2, 1, 1), 0) == 0
        return jnp.where(first, 1.0, inside)

    def packed(one, two, width):
        rows = [
            jnp.sum(v[k : k + CELL // 2], axis=0, keepdims=True) for v in (one, two) for k in (0, CELL // 2)
        ]
        rows = jnp.concatenate(rows, axis=0)
        wide = -(-width // 256) * 128
        return jnp.concatenate([rows[:, 0:wide], rows[:, width - wide :]], axis=0)

    def moments(ref, width):
        def body(i, carry):
            v = chunk(ref, i)
            m = v * keep(i)
            return (carry[0] + m[0] + m[1], carry[1] + m[0] * v[0] + m[1] * v[1])

        zero = jnp.zeros((CELL, width), F32)
        return loop(CHUNKS, body, (zero, zero))

    def prepare(n, sums, width):
        tile = r.tile_mid if width == mid else r.tile_out
        n2 = n // 2
        gain = r.param[2 * n : 2 * n + 1, 0:width]
        bias = r.param[2 * n + 1 : 2 * n + 2, 0:width]
        mean = sums[0:2] / cell_count
        inv = lax.rsqrt(sums[2:4] / cell_count - mean * mean + epsilon)
        scale = inv * gain
        shift = bias - mean * scale
        for k, v in enumerate((scale, shift, inv, mean * inv)):
            tile[n2, k] = per_batch(v[0:1], v[1:2], width)

    def tiles(n, width):
        tile = r.tile_mid if width == mid else r.tile_out
        return [tile[n // 2, k][None] for k in range(4)]

    def fill(ref_a, ref_b, value_of, width):
        pads(ref_a, ref_b, width)

        def body(i, before):
            v = value_of(i)
            put(ref_a, i, v, MAIN)
            pair = jnp.concatenate([before[None], v[0:1]], axis=0)
            put(ref_b, i, pair, MAIN - CHUNK)
            return v[1]

        loop(CHUNKS, body, jnp.zeros((CELL, width), F32))

    def activated(src, n, width):
        def value(i):
            scale, shift, _, _ = tiles(n, width)
            y = chunk(src, i) * scale + shift
            return y * sigmoid(y) * keep(i)

        return value

    def taps(ref_a, ref_b, k, size=ROWS):
        r0 = MAIN - 8 * CELL + 8 * CELL * k
        return (
            ref_b[rows_of(r0 - CHUNK, size), :],
            ref_a[rows_of(r0, size), :],
            ref_b[rows_of(r0, size), :],
        )

    def conv(ref_a, ref_b, weight, out, pump=None):
        for n, (c0, cw) in enumerate(((0, 512), (512, mid - 512))):

            def body(a, _, c0=c0, cw=cw, n=n):
                x = taps(ref_a, ref_b, a)
                acc = nn(jnp.concatenate(x, axis=1), weight[rows_of(a * 3 * chan, 3 * chan), c0 : c0 + cw])

                @pl.when(a == 0)
                def _():
                    out[:, c0 : c0 + cw] = acc

                @pl.when(a > 0)
                def _():
                    out[:, c0 : c0 + cw] += acc

                if pump is not None:
                    pump(n * 3 + a)
                return 0

            lax.fori_loop(0, 3, body, 0)

    def conv_back(ref_a, ref_b, weight, out, pump=None):
        def body(k, _):
            e = taps(ref_a, ref_b, k)
            acc = None
            for j in range(3):
                tap = 8 - 3 * k - j
                term = nt(e[j], weight[rows_of(tap * chan, chan), :])
                acc = term if acc is None else acc + term

            @pl.when(k == 0)
            def _():
                out[:, 0:chan] = acc

            @pl.when(k > 0)
            def _():
                out[:, 0:chan] += acc

            if pump is not None:
                pump(k)
            return 0

        lax.fori_loop(0, 3, body, 0)

    def send_frames(k):
        down, up = r.down, r.up
        count = ROWS // 4
        for c in range(chan // 128):
            lanes = pl.ds(128 * c, 128)
            r.halo_out[0, :, lanes] = down[c, pl.ds(CELL + 3, count, stride=4), :].astype(BF16)
            r.halo_out[1, :, lanes] = up[c, pl.ds(0, count, stride=4), :].astype(BF16)
        copies = []
        for n, dev in ((0, later_dev), (1, earlier_dev)):
            copies.append(
                rc(r.halo_out.at[n], r.halo_in.at[k, n], r.halo_send.at[k, n], r.halo_recv.at[k, n], dev)
            )
            copies[-1].start()
        return copies

    def take_frames(k, copies):
        down, up = r.down, r.up
        count = ROWS // 4
        for copy in copies:
            copy.wait()
        at_start = jnp.logical_and(mine == 0, b == 0)
        at_end = jnp.logical_and(mine == 3, b == nb - 1)
        for c in range(chan // 128):
            lanes = pl.ds(128 * c, 128)
            before = r.halo_in[k, 0, :, lanes].astype(F32)
            after = r.halo_in[k, 1, :, lanes].astype(F32)
            down[c, pl.ds(CELL - 1, count, stride=4), :] = jnp.where(at_start, 0.0, before)
            up[c, pl.ds(4, count, stride=4), :] = jnp.where(at_end, 0.0, after)

    def by_lanes(ref, rows):
        return jnp.concatenate([ref[c, rows, :] for c in range(chan // 128)], axis=1)

    def put_lanes(ref, rows, value):
        for c in range(chan // 128):
            ref[c, rows, :] = value[:, 128 * c : 128 * c + 128]

    def shifted(i):
        before = by_lanes(r.down, rows_of(i * CHUNK, CHUNK + CELL))[CELL - 1 : CELL - 1 + CHUNK]
        after = by_lanes(r.up, rows_of(i * CHUNK, CHUNK + CELL))[1 : 1 + CHUNK]
        gate = r.gate[...][None]
        return (before.reshape(2, CELL, chan) * gate, after.reshape(2, CELL, chan))

    def temporal(k, v, weight, out, works=()):
        works = list(works) + [None] * 2
        put_lanes(r.down, pl.ds(CELL, ROWS), nn(v[...], weight[0:mid, :]))
        y2 = nn(v[...], weight[2 * mid : 3 * mid, :])
        y2 = (y2.reshape(ROWS // CELL, CELL, chan) * r.gate[...][None]).reshape(ROWS, chan)
        put_lanes(r.up, pl.ds(0, ROWS), y2)
        copies = send_frames(k)
        out[...] = nn(v[...], weight[mid : 2 * mid, :])
        if works[0]:
            works[0]()
        take_frames(k, copies)

        def body(i, carry):
            before, after = shifted(i)
            value = chunk(out, i) + before + after
            put(out, i, value)
            m = value * keep(i)
            return (carry[0] + m[0] + m[1], carry[1] + m[0] * value[0] + m[1] * value[1])

        zero = jnp.zeros((CELL, chan), F32)
        return loop(CHUNKS, body, (zero, zero))

    def temporal_back(k, weight, works=()):
        works = list(works) + [None] * 2
        copies = send_frames(k)
        e3 = r.e3
        for c0, cw in ((0, 512), (512, mid - 512)):
            r.grad_mid[:, c0 : c0 + cw] = nt(e3[1], weight[mid + c0 : mid + c0 + cw, :])
        if works[0]:
            works[0]()
        take_frames(k, copies)

        def body(i, _):
            before, after = shifted(i)
            e3[0, rows_of(i * CHUNK, CHUNK), :] = after.reshape(CHUNK, chan).astype(BF16)
            e3[2, rows_of(i * CHUNK, CHUNK), :] = before.reshape(CHUNK, chan).astype(BF16)
            return 0

        loop(CHUNKS, body, 0)
        share = share_e3(k)
        for c0, cw in ((0, 512), (512, mid - 512)):
            r.grad_mid[:, c0 : c0 + cw] += nt(e3[0], weight[c0 : c0 + cw, :]) + nt(
                e3[2], weight[2 * mid + c0 : 2 * mid + c0 + cw, :]
            )
        return share

    def share(k, src, dst):
        copy = rc(src, dst, r.share_send.at[k], r.share_recv.at[k], sibling)
        copy.start()
        return copy

    outs = (r.out1s, r.out1t, r.out2s, r.out2t)

    halves = ((0, 512), (512, mid - 512))

    def e_part(n, slot):
        c0, cw = halves[n]
        return r.e_all.at[slot * ROWS : (slot + 1) * ROWS, c0 : c0 + cw]

    def e_copies(k, n):
        sems = [(r.e_send.at[k, n, m], r.e_recv.at[k, n, m]) for m in range(3)]
        return [
            rc(e_part(n, 0), e_part(n, 1), *sems[0], sibling),
            rc(e_part(n, 0), e_part(n, 2), *sems[1], beside),
            rc(e_part(n, 2), e_part(n, 3), *sems[2], sibling),
        ]

    def share_e(k):
        for n in (0, 1):
            near, over, _ = e_copies(k, n)
            over.start()
            near.start()

    def share_e_on(k, n):
        _, over, far = e_copies(k, n)
        over.wait_recv()
        far.start()

    def share_e_wait(k, n):
        near, over, far = e_copies(k, n)
        near.wait()
        over.wait_send()
        far.wait()

    def share_x(k, xa, xq):
        copies = []
        for n, dev in enumerate((sibling, beside, (1 - h, 1 - w, b))):
            lanes = rows_of((2 * dev[1] + dev[0]) * quarter, quarter, 128)
            main = pl.ds(MAIN, ROWS)
            copies.append(
                rc(xa.at[main, lanes], xq.at[n, 0, main, :], r.xq_send.at[k, n], r.xq_recv.at[k, n], dev)
            )
            copies[-1].start()
        return copies

    def pads(ref_a, ref_b, width):
        ref_a[0:MAIN, :] = jnp.zeros((MAIN, width), BF16)
        ref_a[MAIN + ROWS : PADDED, :] = jnp.zeros((PADDED - MAIN - ROWS, width), BF16)
        ref_b[0 : MAIN - CHUNK, :] = jnp.zeros((MAIN - CHUNK, width), BF16)
        ref_b[MAIN - CHUNK + ROWS : PADDED, :] = jnp.zeros((PADDED - MAIN + CHUNK - ROWS, width), BF16)

    def spread_x(xq):
        for n in range(3):
            pads(xq.at[n, 0], xq.at[n, 1], quarter)

        def body(i, before):
            after = []
            for n in range(3):
                v = chunk(xq.at[n, 0], i, MAIN)
                put(xq.at[n, 1], i, jnp.concatenate([before[n][None], v[0:1]], axis=0), MAIN - CHUNK)
                after.append(v[1])
            return tuple(after)

        loop(CHUNKS, body, (jnp.zeros((CELL, quarter), F32),) * 3)

    def share_e3(k):
        return share(
            k - 2, r.e3.at[:, :, rows_of((1 - h) * half, half, 128)], r.sib_e3
        )

    def grad_tap(owner):
        return owner + jnp.where(owner > 2 * shared, 1, 0)

    spare = r.w2s

    def gq(i, row, size):
        return rows_of((mid if i == 0 else 0) + row, size)

    def inbox(i, row, size):
        return rows_of(2 * mid + (mid if i == 0 else 0) + row, size)

    def transpose_x(a, xa, xb, xq, near, far, row):
        lanes = rows_of(shared * quarter, quarter, 128)
        r0 = MAIN - 8 * CELL + 8 * CELL * a
        for j, (c, start) in enumerate(((1, r0 - CHUNK), (0, r0), (1, r0))):
            rows = rows_of(start, ROWS)
            own = (xb if c else xa)[rows, lanes]
            both = jnp.concatenate([own, xq[0, c, rows, :]], axis=0)
            near[rows_of(row + j * quarter, quarter), 0 : 2 * ROWS] = both.T
            both = jnp.concatenate([xq[1, c, rows, :], xq[2, c, rows, :]], axis=0)
            far[rows_of(row + j * quarter, quarter), 0 : 2 * ROWS] = both.T

    def spatial_part(i, near, far, row, out_row, n):
        c0, cw = halves[n]
        rows = rows_of(row, 3 * quarter)
        acc = nn(near[rows, 0 : 2 * ROWS], r.e_all[0 : 2 * ROWS, c0 : c0 + cw])
        acc += nn(far[rows, 0 : 2 * ROWS], r.e_all[2 * ROWS : 4 * ROWS, c0 : c0 + cw])
        spare[gq(i, out_row, 3 * quarter), c0 : c0 + cw] = acc.astype(BF16)

    def transposes(xa, xb, xq, near, far):
        def body(a, _):
            transpose_x(a, xa, xb, xq, near, far, a * 3 * quarter)
            return 0

        lax.fori_loop(0, 3, body, 0)

    def spatial_half(i, near, far, n):
        def body(a, _):
            spatial_part(i, near, far, a * 3 * quarter, a * 3 * quarter, n)
            return 0

        lax.fori_loop(0, 3, body, 0)

    def transpose_v(v, sv):
        for c in range(mid // 128):
            lanes = pl.ds(128 * c, 128)
            r.xt[128 * c : 128 * c + 128, :] = jnp.concatenate([v[:, lanes], sv[:, lanes]], axis=0).T

    def temporal_grad(i, k):
        e = jnp.concatenate([r.e3[k, :, rows_of(h * half, half, 128)], r.sib_e3[k]], axis=0)
        whole[i][k * mid : (k + 1) * mid, 0:half] = nn(r.xt[...], e).astype(BF16)

    def cols_of(n):
        c0, cw = halves[n]
        return pl.ds(c0, cw)

    def s_block(i, n, owner):
        return spare.at[gq(i, grad_tap(owner) * quarter, quarter), cols_of(n)]

    def s_extra(i, n, side):
        return spare.at[gq(i, (2 * shared + 1) * quarter + side * 64, 64), cols_of(n)]

    def t_block(i, owner):
        return whole[i].at[rows_of(owner * temp, temp), 0:half]

    def t_inbox(i, n):
        return whole[i].at[rows_of(n * temp, temp), half:chan]

    def parts_of(i):
        return (0, 1) if i % 2 == 0 else (0,)

    def block_of(i, n, owner):
        return s_block(i, n, owner) if i % 2 == 0 else t_block(i, owner)

    def y_box(i, n, place):
        return spare.at[inbox(i, place * quarter, quarter), cols_of(n)] if i % 2 == 0 else t_inbox(i, place)

    def z_box(i, n, place):
        return spare.at[inbox(i, 576 + place * quarter, quarter), cols_of(n)] if i % 2 == 0 else t_inbox(i, 4 + place)

    def extra_y_box(i, n):
        return spare.at[inbox(i, 4 * quarter, 64), cols_of(n)]

    def extra_z_box(i, n, place):
        return spare.at[inbox(i, 576 + 3 * quarter + place * 64, 64), cols_of(n)]

    across = (h, w, b + 1 - 2 * par)

    def add_into(dst, parts, step):
        rows, cols = dst.shape

        def body(n, _):
            at_rows = rows_of(n * step, step)
            value = dst[at_rows, :].astype(F32)
            for part in parts:
                value = value + part[at_rows, :].astype(F32)
            dst[at_rows, :] = value.astype(BF16)
            return 0

        lax.fori_loop(0, rows // step, body, 0)

    def y_copy(i, n, d):
        place = lax.rem(bh + d, depth)
        src = block_of(i, n, 2 * place + 1 - par)
        return rc(src, y_box(i, n, place), r.y_send.at[i, n, d], r.y_recv.at[i, n, place], across)

    def z_copy(i, n, d):
        place = lax.rem(bh + d, depth)
        src = block_of(i, n, 2 * place + par)
        dev = (h, w, 2 * place + par)
        return rc(src, z_box(i, n, 3 - d), r.z_send.at[i, n, d], r.z_recv.at[i, n, 3 - d], dev)

    def extra_y(i, n):
        return rc(s_extra(i, n, 1 - par), extra_y_box(i, n), r.y_send.at[i, n, 4], r.y_recv.at[i, n, 4], across)

    def extra_z(i, n):
        place = jnp.minimum(lax.rem(bh - shared + 3 + depth, depth), 2)
        dev = (h, w, 2 * shared + par)
        return rc(
            s_extra(i, n, par), extra_z_box(i, n, place), r.z_send.at[i, n, 4], r.z_recv.at[i, n, 4 + place], dev
        )

    def step_of(i):
        return 16 if i % 2 == 0 else 48

    def reduce_start(i, n):
        for d in (1, 2, 3, 0):
            y_copy(i, n, d).start()
        if i % 2 == 0:
            extra_y(i, n).start()

    def reduce_middle(i, n):
        for d in (1, 2, 3, 0):
            place = lax.rem(bh + d, depth)
            y_copy(i, n, d).wait_send()
            box = y_box(i, n, place)
            rc(box, box, r.y_send.at[i, n, d], r.y_recv.at[i, n, place], across).wait_recv()
            add_into(block_of(i, n, 2 * place + par), [box], step_of(i))
            if d:
                z_copy(i, n, d).start()
        if i % 2 == 0:
            extra_y(i, n).wait()
            add_into(s_extra(i, n, par), [extra_y_box(i, n)], 16)
            pl.when(bh != shared)(lambda: extra_z(i, n).start())

    def final_part(i, n, side, core):
        place = 2 * side + core
        start = quarter * place - 64 * b + 512 * jnp.where(b > 2 * place, 1, 0)
        return outs[i].at[rows_of(start, quarter, 64), cols_of(n)]

    def extra_part(i, n):
        return outs[i].at[rows_of(512 * (1 - par), 64, 64), cols_of(n)]

    def final_copies(i, n):
        if i % 2:
            src = t_block(i, b)
            part = outs[i].at[h]
            return lc(src, part, r.out_sem.at[i, 0, 0]), [
                (src, part, sibling, r.cast_send.at[i, 0, 0], r.cast_recv.at[i, 0, 0])
            ]
        src = s_block(i, n, b)
        part = final_part(i, n, w, h)
        sends = [
            (src, part, dev, r.cast_send.at[i, n, d], r.cast_recv.at[i, n, d]) for d, dev in enumerate((beside, sibling))
        ]
        return lc(src, part, r.out_sem.at[i, n, 0]), sends

    def extra_copies(i, n):
        src = s_extra(i, n, par)
        part = extra_part(i, n)
        sends = [
            (src, part, dev, r.cast_send.at[i, n, 3 + d], r.cast_recv.at[i, n, 3 + d])
            for d, dev in enumerate((beside, sibling))
        ]
        return lc(src, part, r.out_sem.at[i, n, 1]), sends

    def begin(copies):
        local, sends = copies
        for src, part, dev, one, two in sends:
            rc(src, part, one, two, dev).start()
        local.start()

    def beside_copy(i):
        return rc(t_block(i, b), t_inbox(i, 7), r.z_send.at[i, 0, 4], r.z_recv.at[i, 0, 4], beside)

    def reduce_last(i, n):
        for d in (1, 2, 3):
            z_copy(i, n, d).wait()
        add_into(block_of(i, n, b), [z_box(i, n, place) for place in range(3)], step_of(i))
        if i % 2:
            beside_copy(i).start()
            return
        begin(final_copies(i, n))

        @pl.when(bh != shared)
        def _():
            extra_z(i, n).wait_send()

        @pl.when(bh == shared)
        def _():
            boxes = [extra_z_box(i, n, place) for place in range(3)]
            for place, box in enumerate(boxes):
                rc(box, box, r.z_send.at[i, n, 4], r.z_recv.at[i, n, 4 + place], across).wait_recv()
            add_into(s_extra(i, n, par), boxes, 16)
            begin(extra_copies(i, n))

    def reduce_out(i):
        beside_copy(i).wait()
        add_into(t_block(i, b), [t_inbox(i, 7)], 48)
        begin(final_copies(i, 0))

    def final_on(i, n):
        def move(part, d):
            rc(part, part, r.cast_send.at[i, n, d], r.cast_recv.at[i, n, d], beside).wait_recv()
            rc(part, part, r.cast_send.at[i, n, d + 2], r.cast_recv.at[i, n, d + 2], sibling).start()

        move(final_part(i, n, 1 - w, h), 0)
        pl.when(bh == shared_beside)(lambda: move(extra_part(i, n), 3))

    def reduce_wait(i, n):
        local, sends = final_copies(i, n)
        local.wait()
        if i % 2:
            src, part, dev, one, two = sends[0]
            rc(src, outs[i].at[1 - h], one, two, dev).wait()
            return
        for src, part, dev, one, two in sends:
            rc(src, part, one, two, dev).wait_send()

        def far(part, d):
            return rc(part, part, r.cast_send.at[i, n, d], r.cast_recv.at[i, n, d], sibling)

        far(final_part(i, n, w, 1 - h), 1).wait_recv()
        far(final_part(i, n, 1 - w, h), 2).wait_send()
        far(final_part(i, n, 1 - w, 1 - h), 2).wait_recv()
        local, sends = extra_copies(i, n)

        @pl.when(bh == shared)
        def _():
            local.wait()
            for src, part, dev, one, two in sends:
                rc(src, part, one, two, dev).wait_send()

        pl.when(bh == shared_beside)(lambda: far(extra_part(i, n), 5).wait_send())
        pl.when(bh == 2 * w + 1 - h)(lambda: far(extra_part(i, n), 4).wait_recv())
        pl.when(bh == 2 * (1 - w) + 1 - h)(lambda: far(extra_part(i, n), 5).wait_recv())

    def tile_of(ref, jh, jw):
        return ref.at[rows_of(jh * 4, 4, 4), rows_of(jw * 32, 32), :]

    def scatter(src, dst, n):
        copies = []
        for d, (j, dev) in enumerate(tile_group):
            copies.append(
                rc(src.at[j], tile_of(dst, h, w), r.tile_send.at[n, d], r.tile_recv.at[n, mine], dev)
            )
        return copies

    def scattered(src, dst, n):
        for d, (j, dev) in enumerate(tile_group):
            jh, jw = at_group(j)
            rc(src.at[j], tile_of(dst, jh, jw), r.tile_send.at[n, d], r.tile_recv.at[n, j], dev).wait()

    def tiles_start(src, dst, n):
        for copy in scatter(src, dst, n):
            copy.start()
        lc(src.at[mine], tile_of(dst, h, w), r.tile_own.at[n]).start()

    def tiles_wait(src, dst, n):
        scattered(src, dst, n)
        lc(src.at[mine], tile_of(dst, h, w), r.tile_own.at[n]).wait()

    xg, cg = r.x_grid, r.cot_grid
    tiles_start(r.x_tiles, xg, 0)
    gather_start(0)
    r.param[...] = total(0, mid, r.param_in[...])
    tiles_wait(r.x_tiles, xg, 0)

    def grid_chunk(ref, i):
        v = ref[lax.div(i, 4), rows_of(lax.rem(i, 4) * CHUNK, CHUNK), :]
        return v.astype(F32).reshape(2, CELL, chan)

    fill(r.xa, r.xb, lambda i: grid_chunk(xg, i), chan)

    def pump_loop(i, lo, hi):
        def body(s, _):
            gather_pump(i, s)
            return 0

        lax.fori_loop(lo, hi, body, 0)

    pump_loop(0, 1, nb - 2)
    gather_start(1)
    gather_pump(0, nb - 2)
    gather_start(2)
    gather_pump(0, nb - 1)
    gather_pump(1, 1)
    gather_pump(2, 1)
    gather_pump(1, 2)
    gather_finish(0)

    def first_pump(n):
        pl.when(lax.rem(n, 2) == 0)(lambda: gather_pump(1, 3 + lax.div(n, 2)))
        pl.when(n == 3)(lambda: gather_pump(2, 2))

    conv(r.xa, r.xb, r.w1s, r.mid1, first_pump)
    sums = total(
        1,
        mid,
        packed(*moments(r.mid1, mid), mid),
        [lambda: gather_pump(1, nb - 2), lambda: gather_pump(2, 3), lambda: gather_pump(1, nb - 1)],
    )
    prepare(0, sums, mid)

    def hidden(src, n, dst):
        value = activated(src, n, mid)

        def body(i, _):
            put(dst, i, value(i))
            return 0

        loop(CHUNKS, body, 0)

    hidden(r.mid1, 0, r.v1)
    gather_pump(2, 4)
    gather_finish(1)
    stats = temporal(0, r.v1, r.w1t, r.time1, [lambda: gather_pump(2, 5)])

    def sixth():
        gather_pump(2, 6)

    sums = total(2, chan, packed(*stats, chan), [lambda: gather_start(3), None, sixth])
    prepare(1, sums, chan)
    fill(r.aa, r.ab, activated(r.time1, 1, chan), chan)
    gather_pump(3, 1)
    gather_pump(2, nb - 1)
    gather_pump(3, 2)
    gather_finish(2)
    tiles_start(r.cot_tiles, cg, 1)

    def second_pump(n):
        pl.when(n < nb - 3)(lambda: gather_pump(3, 3 + n))

    conv(r.aa, r.ab, r.w2s, r.mid2, second_pump)
    sums = total(3, mid, packed(*moments(r.mid2, mid), mid), [lambda: gather_finish(3)])
    prepare(2, sums, mid)
    hidden(r.mid2, 2, r.v2)
    stats = temporal(1, r.v2, r.w2t, r.time2)
    shared_xq2 = share_x(0, r.aa, r.xq2)
    share_v2 = share(4, r.v2, r.sib_v)
    sums = total(4, chan, packed(*stats, chan))
    tiles_wait(r.cot_tiles, cg, 1)
    prepare(3, sums, chan)

    out_grid = r.out_grid

    def grid_put(ref, i, v):
        ref[lax.div(i, 4), rows_of(lax.rem(i, 4) * CHUNK, CHUNK), :] = v.reshape(CHUNK, chan).astype(ref.dtype)

    def slope(y, s):
        return s * (1.0 + y * (1.0 - s))

    def pre_body(i, carry):
        scale, shift, inv, offset = tiles(3, chan)
        v = chunk(r.time2, i)
        y = v * scale + shift + chunk(r.xa, i, MAIN)
        s = sigmoid(y)
        m = keep(i)
        grid_put(out_grid, i, y * s * m)
        d = grid_chunk(cg, i) * m * slope(y, s)
        put(r.grad_pre, i, d)
        t = d * (v * inv - offset)
        return (carry[0] + d[0] + d[1], carry[1] + t[0] + t[1])

    zero_out = jnp.zeros((CELL, chan), F32)
    zero_mid = jnp.zeros((CELL, mid), F32)
    out_grid[HGT] = jnp.zeros((8 * CELL, chan), BF16)
    gg = loop(CHUNKS, pre_body, (zero_out, zero_out))

    def send_tiles(src, dst, n):
        for d, (j, dev) in enumerate(tile_group):
            jh, jw = at_group(j)
            rc(tile_of(src, jh, jw), dst.at[mine], r.tile_send.at[n, d], r.tile_recv.at[n, mine], dev).start()
        lc(tile_of(src, h, w), dst.at[mine], r.tile_own.at[n]).start()

    def sent_tiles(src, dst, n):
        for d, (j, dev) in enumerate(tile_group):
            jh, jw = at_group(j)
            rc(tile_of(src, jh, jw), dst.at[j], r.tile_send.at[n, d], r.tile_recv.at[n, j], dev).wait()
        lc(tile_of(src, h, w), dst.at[mine], r.tile_own.at[n]).wait()

    send_tiles(out_grid, r.block_out, 2)

    def norm_back(n, sums, width):
        r.norm_grads[2 * n : 2 * n + 1, 0:width] = sums[2:3] + sums[3:4]
        r.norm_grads[2 * n + 1 : 2 * n + 2, 0:width] = sums[0:1] + sums[1:2]
        back = r.back
        back[0, :, 0:width] = per_batch(sums[0:1], sums[1:2], width) / cell_count
        back[1, :, 0:width] = per_batch(sums[2:3], sums[3:4], width) / cell_count

    def through_norm(n, src, grad, i, width):
        scale, _, inv, offset = tiles(n, width)
        xhat = chunk(src, i) * inv - offset
        bias_part = r.back[0, :, 0:width][None]
        gain_part = r.back[1, :, 0:width][None]
        return scale * (chunk(grad, i, 0, width) - bias_part - xhat * gain_part) * keep(i)

    def through_act(n, src, grad, width):
        def body(i, carry):
            scale, shift, inv, offset = tiles(n, width)
            v = chunk(src, i)
            y = v * scale + shift
            s = sigmoid(y)
            d = chunk(grad, i, 0, width) * keep(i) * slope(y, s)
            put(grad, i, d, 0, width)
            t = d * (v * inv - offset)
            return (carry[0] + d[0] + d[1], carry[1] + t[0] + t[1])

        zero = jnp.zeros((CELL, width), F32)
        return loop(CHUNKS, body, (zero, zero))

    def to_frames(n, src, grad):
        def body(i, _):
            e = through_norm(n, src, grad, i, chan).astype(BF16)
            ef = e.astype(F32)
            r.e3[1, rows_of(i * CHUNK, CHUNK), :] = e.reshape(CHUNK, chan)
            put_lanes(r.down, rows_of(i * CHUNK + CELL, CHUNK, CELL), ef.reshape(CHUNK, chan))
            put_lanes(r.up, rows_of(i * CHUNK, CHUNK), (ef * r.gate[...][None]).reshape(CHUNK, chan))
            return 0

        loop(CHUNKS, body, 0)

    sums = total(5, chan, packed(*gg, chan))
    norm_back(3, sums, chan)
    to_frames(3, r.time2, r.grad_pre)
    shared_e3 = temporal_back(2, r.w2t)
    gg = through_act(2, r.mid2, r.grad_mid, mid)
    shared_e3.wait()
    share_v2.wait()
    def temporal_grads(i, v):
        def first():
            transpose_v(v, r.sib_v)
            temporal_grad(i, 0)

        return [first, lambda: temporal_grad(i, 1), lambda: temporal_grad(i, 2)]

    sums = total(6, mid, packed(*gg, mid), temporal_grads(3, r.v2))
    reduce_start(3, 0)
    norm_back(2, sums, mid)

    def fill_e(n, src):
        def value(i):
            v = through_norm(n, src, r.grad_mid, i, mid)
            put(r.e_all, i, v)
            return v

        fill(r.ea, r.eb, value, mid)

    fill_e(2, r.mid2)
    share_e(0)
    conv_back(r.ea, r.eb, r.w2s, r.grad_mid)
    share_e_on(0, 0)
    gg = through_act(1, r.time1, r.grad_mid, chan)
    for copy in shared_xq2:
        copy.wait()
    near, far = spare.at[mid : 2 * mid, :], spare.at[3 * mid : 4 * mid, :]

    def spread_and_turn():
        spread_x(r.xq2)
        transposes(r.aa, r.ab, r.xq2, near, far)

    def first_half():
        share_e_wait(0, 0)
        spatial_half(2, near, far, 0)

    sums = total(7, chan, packed(*gg, chan), [spread_and_turn, first_half, lambda: share_e_on(0, 1)])
    reduce_start(2, 0)
    reduce_middle(3, 0)
    share_v1 = share(5, r.v1, r.sib_v)
    shared_xq1 = share_x(1, r.xa, r.xq1)
    norm_back(1, sums, chan)
    to_frames(1, r.time1, r.grad_mid)

    def second_half():
        share_e_wait(0, 1)
        spatial_half(2, near, far, 1)
        reduce_start(2, 1)

    shared_e3 = temporal_back(3, r.w1t, [second_half])
    reduce_last(3, 0)
    gg = through_act(0, r.mid1, r.grad_mid, mid)
    shared_e3.wait()
    share_v1.wait()
    sums = total(8, mid, packed(*gg, mid), temporal_grads(1, r.v1))
    reduce_start(1, 0)
    norm_back(0, sums, mid)
    fill_e(0, r.mid1)
    share_e(1)
    reduce_out(3)
    for n in (0, 1):
        reduce_middle(2, n)
    for copy in shared_xq1:
        copy.wait()
    spread_x(r.xq1)
    sent_tiles(out_grid, r.block_out, 2)
    conv_back(r.ea, r.eb, r.w1s, r.grad_mid)
    share_e_on(1, 0)
    near, far = r.w1s.at[0:mid, :], r.w1s.at[mid : 2 * mid, :]
    transposes(r.xa, r.xb, r.xq1, near, far)
    share_e_wait(1, 0)
    spatial_half(0, near, far, 0)
    reduce_start(0, 0)
    share_e_on(1, 1)
    share_e_wait(1, 1)
    spatial_half(0, near, far, 1)
    reduce_start(0, 1)

    def last_body(i, _):
        grid_put(out_grid, i, (chunk(r.grad_mid, i, 0, chan) + chunk(r.grad_pre, i)) * keep(i))
        return 0

    loop(CHUNKS, last_body, 0)
    send_tiles(out_grid, r.grad_input, 3)
    for n in (0, 1):
        reduce_last(2, n)
    reduce_middle(1, 0)
    for n in (0, 1):
        final_on(2, n)
    reduce_middle(0, 0)
    reduce_last(1, 0)
    reduce_out(1)
    reduce_last(0, 0)
    reduce_middle(0, 1)
    final_on(0, 0)
    reduce_last(0, 1)
    sent_tiles(out_grid, r.grad_input, 3)
    for n in (0, 1):
        reduce_wait(2, n)
    reduce_wait(3, 0)
    final_on(0, 1)
    reduce_wait(1, 0)
    for n in (0, 1):
        reduce_wait(0, n)


def per_device_fast(nb, *args):
    (
        inputs,
        starts,
        first_spatial,
        first_mid_gain,
        first_mid_bias,
        first_temporal,
        first_out_gain,
        first_out_bias,
        second_spatial,
        second_mid_gain,
        second_mid_bias,
        second_temporal,
        second_out_gain,
        second_out_bias,
        cotangent,
    ) = args
    micro, frames, side, _, chan = inputs.shape
    mid = first_spatial.shape[1]
    spat, temp = first_spatial.shape[0], first_temporal.shape[0]
    few = frames // 4
    h, w, b = (lax.axis_index(name) for name in ("ha", "wa", "batch"))
    mine = (1 - w) * h + w * (3 - h)
    offsets = jnp.arange(side)
    valid = (h * side + offsets < HGT)[:, None] & (w * side + offsets < HGT)[None, :]

    def tiles(array):
        array = array * valid.astype(BF16)[None, None, :, :, None]
        array = array.reshape(micro, 4, few, side, side, chan).transpose(1, 3, 4, 0, 2, 5)
        return array.reshape(4, side, side * micro * few, chan)

    def untiled(array):
        array = array.reshape(4, side, side, micro, few, chan).transpose(3, 0, 4, 1, 2, 5)
        return array.reshape(micro, frames, side, side, chan).astype(F32)

    gate = (1 - lax.dynamic_slice_in_dim(starts, mine * few, few, axis=1)).astype(F32)
    gate = jnp.broadcast_to(gate.reshape(micro * few, 1), (micro * few, chan))
    here = jnp.where((h == 0) & (w == 0), 1.0, 0.0)

    def placed(shard):
        row = jnp.zeros((mid,), F32)
        return lax.dynamic_update_slice(row, shard.astype(F32) * here, (b * shard.shape[0],))

    param = jnp.stack(
        [
            placed(v)
            for v in (
                first_mid_gain,
                first_mid_bias,
                first_out_gain,
                first_out_bias,
                second_mid_gain,
                second_mid_bias,
                second_out_gain,
                second_out_bias,
            )
        ]
    )
    half = chan // 2
    few_rows = ROWS // 4

    inputs_of = dict(
        x_tiles=(tiles(inputs), pl.ANY),
        cot_tiles=(tiles(cotangent), pl.ANY),
        gate=(gate, pltpu.VMEM),
        param_in=(param, pltpu.VMEM),
        first_spatial=(first_spatial, pl.ANY),
        first_temporal=(first_temporal, pl.ANY),
        second_spatial=(second_spatial, pl.ANY),
        second_temporal=(second_temporal, pl.ANY),
    )
    outputs_of = dict(
        block_out=((4, side, side * CELL, chan), BF16, pl.ANY),
        grad_input=((4, side, side * CELL, chan), BF16, pl.ANY),
        norm_grads=((8, mid), F32, pltpu.VMEM),
        out1s=((spat, mid), BF16, pl.ANY),
        out1t=((2, temp, half), BF16, pl.ANY),
        out2s=((spat, mid), BF16, pl.ANY),
        out2t=((2, temp, half), BF16, pl.ANY),
    )
    dma = pltpu.SemaphoreType.DMA
    scratch_of = dict(
        w1s=pltpu.VMEM((9 * chan, mid), BF16),
        w1t=pltpu.VMEM((3 * mid, chan), BF16),
        w2s=pltpu.VMEM((9 * chan, mid), BF16),
        w2t=pltpu.VMEM((3 * mid, chan), BF16),
        x_grid=pltpu.VMEM((8, 8 * CELL, chan), BF16),
        cot_grid=pltpu.VMEM((8, 8 * CELL, chan), BF16),
        out_grid=pltpu.VMEM((8, 8 * CELL, chan), BF16),
        xa=pltpu.VMEM((PADDED, chan), BF16),
        xb=pltpu.VMEM((PADDED, chan), BF16),
        aa=pltpu.VMEM((PADDED, chan), BF16),
        ab=pltpu.VMEM((PADDED, chan), BF16),
        ea=pltpu.VMEM((PADDED, mid), BF16),
        eb=pltpu.VMEM((PADDED, mid), BF16),
        mid1=pltpu.VMEM((ROWS, mid), F32),
        mid2=pltpu.VMEM((ROWS, mid), F32),
        grad_mid=pltpu.VMEM((ROWS, mid), F32),
        v1=pltpu.VMEM((ROWS, mid), BF16),
        v2=pltpu.VMEM((ROWS, mid), BF16),
        time1=pltpu.VMEM((ROWS, chan), F32),
        time2=pltpu.VMEM((ROWS, chan), F32),
        grad_pre=pltpu.VMEM((ROWS, chan), F32),
        down=pltpu.VMEM((chan // 128, ROWS + CHUNK, 128), F32),
        up=pltpu.VMEM((chan // 128, ROWS + CHUNK, 128), F32),
        e3=pltpu.VMEM((3, ROWS, chan), BF16),
        sib_e3=pltpu.VMEM((3, ROWS, half), BF16),
        halo_out=pltpu.VMEM((2, few_rows, chan), BF16),
        halo_in=pltpu.VMEM((4, 2, few_rows, chan), BF16),
        param=pltpu.VMEM((8, mid), F32),
        tile_mid=pltpu.VMEM((2, 4, CELL, mid), F32),
        tile_out=pltpu.VMEM((2, 4, CELL, chan), F32),
        back=pltpu.VMEM((2, CELL, mid), F32),
        sum_a=pltpu.VMEM((2, 2, 8, mid), F32),
        sum_b=pltpu.VMEM((2, 4, 8, mid), F32),
        sum_c=pltpu.VMEM((2, nb // 2, 8, mid), F32),
        own_sem=dma((4,)),
        ring_send=dma((4, 2, nb)),
        ring_recv=dma((4, 2, nb)),
        sib_send=dma((4, 3, nb)),
        sib_recv=dma((4, 3, nb)),
        over_send=dma((4, nb)),
        over_recv=dma((4, nb)),
        sa_send=dma((9,)),
        sa_recv=dma((9,)),
        sb_send=dma((9, 3)),
        sb_recv=dma((9, 4)),
        sc_send=dma((9, nb // 2)),
        sc_recv=dma((9, nb // 2)),
        halo_send=dma((4, 2)),
        halo_recv=dma((4, 2)),
        share_send=dma((6,)),
        share_recv=dma((6,)),
        e_all=pltpu.VMEM((4 * ROWS, mid), BF16),
        xq1=pltpu.VMEM((3, 2, PADDED, chan // 4), BF16),
        xq2=pltpu.VMEM((3, 2, PADDED, chan // 4), BF16),
        xt=pltpu.VMEM((mid, 2 * ROWS), BF16),
        sib_v=pltpu.VMEM((ROWS, mid), BF16),
        e_send=dma((2, 2, 3)),
        e_recv=dma((2, 2, 3)),
        xq_send=dma((2, 3)),
        xq_recv=dma((2, 3)),
        y_send=dma((4, 2, 5)),
        y_recv=dma((4, 2, 5)),
        z_send=dma((4, 2, 5)),
        z_recv=dma((4, 2, 7)),
        cast_send=dma((4, 2, 6)),
        cast_recv=dma((4, 2, 8)),
        out_sem=dma((4, 2, 2)),
        tile_send=dma((4, 3)),
        tile_recv=dma((4, 4)),
        tile_own=dma((4,)),
    )
    names = (*inputs_of, *outputs_of, *scratch_of)
    cell_count = float(frames * nb * HGT * HGT)
    results = pl.pallas_call(
        functools.partial(block_kernel, (nb, chan, mid, cell_count), names),
        out_shape=[jax.ShapeDtypeStruct(shape, dtype) for shape, dtype, _ in outputs_of.values()],
        in_specs=[pl.BlockSpec(memory_space=space) for _, space in inputs_of.values()],
        out_specs=[pl.BlockSpec(memory_space=space) for _, _, space in outputs_of.values()],
        scratch_shapes=list(scratch_of.values()),
        compiler_params=pltpu.CompilerParams(
            collective_id=0, has_side_effects=True, vmem_limit_bytes=VMEM_LIMIT
        ),
    )(*(array for array, _ in inputs_of.values()))
    got = SimpleNamespace(**dict(zip(outputs_of, results)))

    def temporal(pair):
        return jnp.concatenate([pair[0], pair[1]], axis=1).astype(F32)

    def norm(row, like):
        size = like.shape[0]
        return lax.dynamic_slice_in_dim(got.norm_grads[row], b * size, size)

    return (
        untiled(got.block_out),
        untiled(got.grad_input),
        got.out1s.astype(F32),
        norm(0, first_mid_gain),
        norm(1, first_mid_bias),
        temporal(got.out1t),
        norm(2, first_out_gain),
        norm(3, first_out_bias),
        got.out2s.astype(F32),
        norm(4, second_mid_gain),
        norm(5, second_mid_bias),
        temporal(got.out2t),
        norm(6, second_out_gain),
        norm(7, second_out_bias),
    )


def extended(shard, sides, width):
    for axis, dim in sides:
        count, length = (lax.axis_size(axis), shard.shape[dim])
        up = [(i, (i + 1) % count) for i in range(count - 1)]
        down = [(j, i) for i, j in up]
        last = lax.slice_in_dim(shard, length - width, length, axis=dim)
        leading = lax.slice_in_dim(shard, 0, width, axis=dim)
        before = lax.ppermute(last, axis, up)
        after = lax.ppermute(leading, axis, down)
        shard = jnp.concatenate([before, shard, after], axis=dim)
    return shard


def passed_along(shard, axis, by):
    count = lax.axis_size(axis)
    pairs = [(i, i + by) for i in range(count) if 0 <= i + by < count]
    return lax.ppermute(shard, axis, pairs)


def for_sending(shard):

    def short(part):
        return part.astype(jnp.bfloat16) if part.dtype == jnp.float32 else part

    return jax.tree.map(short, shard)


def silu_slope(values):
    sigma = jax.nn.sigmoid(values)
    return sigma * (1.0 + values * (1.0 - sigma))


def spatial_forward(field_in, kernel):
    frames, tile_side = (field_in.shape[0], field_in.shape[1])
    padded = extended(field_in, (("ha", 1), ("wa", 2)), 1)
    pieces = [
        padded[:, offset // 3 : offset // 3 + tile_side, offset % 3 : offset % 3 + tile_side, :]
        for offset in range(9)
    ]
    patches = jnp.concatenate(pieces, axis=-1).reshape(frames * tile_side * tile_side, -1)
    return (patches, jnp.dot(patches, kernel, preferred_element_type=jnp.float32))


def spatial_backward(grad_out, patches, kernel):
    frames, tile_side, channels = (grad_out.shape[0], grad_out.shape[1], grad_out.shape[3])
    row_count = frames * tile_side * tile_side
    padded = extended(grad_out, (("ha", 1), ("wa", 2)), 1)
    pieces = [
        padded[
            :,
            2 - offset // 3 : 2 - offset // 3 + tile_side,
            2 - offset % 3 : 2 - offset % 3 + tile_side,
            :,
        ]
        for offset in range(9)
    ]
    stacked = jnp.concatenate(pieces, axis=-1).reshape(row_count, 9, channels)
    grad_in = jnp.einsum(
        "rkm,kcm->rc", stacked, kernel.reshape(9, -1, channels), preferred_element_type=jnp.float32
    )
    grad_kernel = jnp.einsum(
        "rk,rm->km",
        patches,
        grad_out.reshape(row_count, channels),
        preferred_element_type=jnp.float32,
    )
    return (grad_in, grad_kernel)


def temporal_forward(field_in, clip_gate, kernel):
    frames, tile_side = (field_in.shape[0], field_in.shape[1])
    gated_in = field_in * clip_gate
    earlier = passed_along(field_in[-1:], "batch", 1)
    later_frame = passed_along(gated_in[:1], "batch", -1)
    before = jnp.concatenate([earlier, field_in[:-1]], axis=0) * clip_gate
    after_tap = jnp.concatenate([gated_in[1:], later_frame], axis=0)
    joined = jnp.concatenate([before, field_in, after_tap], axis=-1).reshape(
        frames * tile_side * tile_side, -1
    )
    return (joined, jnp.dot(joined, kernel, preferred_element_type=jnp.float32))


def temporal_backward(grad_out, joined, clip_gate, kernel):
    frames, tile_side, channels = (grad_out.shape[0], grad_out.shape[1], grad_out.shape[3])
    row_count = frames * tile_side * tile_side
    gated_grad = grad_out * clip_gate
    later_frame = passed_along(gated_grad[:1], "batch", -1)
    earlier = passed_along(grad_out[-1:], "batch", 1)
    from_later = jnp.concatenate([gated_grad[1:], later_frame], axis=0)
    from_earlier = jnp.concatenate([earlier, grad_out[:-1]], axis=0) * clip_gate
    stacked = jnp.concatenate([from_later, grad_out, from_earlier], axis=-1).reshape(
        row_count, 3, channels
    )
    grad_in = jnp.einsum(
        "rkc,kmc->rm", stacked, kernel.reshape(3, -1, channels), preferred_element_type=jnp.float32
    )
    grad_kernel = jnp.einsum(
        "rk,rc->kc",
        joined,
        grad_out.reshape(row_count, channels),
        preferred_element_type=jnp.float32,
    )
    return (grad_in, grad_kernel)


def norm_forward(pre_norm, norm_gain, norm_bias, valid_rows, cell_count):
    first_sum = jnp.sum(pre_norm * valid_rows, axis=0)
    square_sum = jnp.sum(pre_norm * pre_norm * valid_rows, axis=0)
    first_sum, square_sum = lax.psum((first_sum, square_sum), ("ha", "wa", "batch"))
    mean_val = first_sum / cell_count
    inv_std = lax.rsqrt(square_sum / cell_count - mean_val * mean_val + epsilon)
    normed = (pre_norm - mean_val) * inv_std
    return (normed, inv_std, normed * norm_gain.astype(jnp.float32) + norm_bias.astype(jnp.float32))


def norm_backward(grad_norm, normed, inv_std, norm_gain, valid_rows, cell_count):
    bias_grad = jnp.sum(grad_norm, axis=0)
    gain_grad = jnp.sum(grad_norm * normed, axis=0)
    bias_grad, gain_grad = lax.psum((bias_grad, gain_grad), ("ha", "wa", "batch"))
    grad_in = (
        valid_rows
        * norm_gain.astype(jnp.float32)
        * inv_std
        * (grad_norm - bias_grad / cell_count - normed * gain_grad / cell_count)
    )
    return (grad_in, gain_grad, bias_grad)


def forward_pair(field_in, weights, clip_gate, valid_rows, cell_count):
    frames, tile_side = (field_in.shape[0], field_in.shape[1])
    patches, spatial_out = spatial_forward(field_in, weights[0])
    mid_hat, mid_scale, mid_norm = norm_forward(
        spatial_out, weights[1], weights[2], valid_rows, cell_count
    )
    hidden = (
        (jax.nn.silu(mid_norm) * valid_rows)
        .astype(jnp.bfloat16)
        .reshape(frames, tile_side, tile_side, -1)
    )
    joined, temporal_out = temporal_forward(hidden, clip_gate, weights[3])
    out_hat, out_scale, out_norm = norm_forward(
        temporal_out, weights[4], weights[5], valid_rows, cell_count
    )
    return ((patches, mid_hat, mid_scale, mid_norm, joined, out_hat, out_scale), out_norm)


def backward_pair(grad_norm, kept, weights, clip_gate, valid_rows, cell_count, tile_side):
    patches, mid_hat, mid_scale, mid_norm, joined, out_hat, out_scale = kept
    frames = clip_gate.shape[0]
    grad_time, out_gain_grad, out_bias_grad = norm_backward(
        grad_norm, out_hat, out_scale, weights[4], valid_rows, cell_count
    )
    grad_time = grad_time.astype(jnp.bfloat16).reshape(frames, tile_side, tile_side, -1)
    grad_hidden, temporal_grad = temporal_backward(grad_time, joined, clip_gate, weights[3])
    grad_mid = grad_hidden * valid_rows * silu_slope(mid_norm)
    grad_spatial, mid_gain_grad, mid_bias_grad = norm_backward(
        grad_mid, mid_hat, mid_scale, weights[1], valid_rows, cell_count
    )
    grad_spatial = grad_spatial.astype(jnp.bfloat16).reshape(frames, tile_side, tile_side, -1)
    grad_in, spatial_grad = spatial_backward(grad_spatial, patches, weights[0])
    return (
        grad_in,
        (spatial_grad, mid_gain_grad, mid_bias_grad, temporal_grad, out_gain_grad, out_bias_grad),
    )


def per_device(
    inputs,
    starts,
    first_spatial,
    first_mid_gain,
    first_mid_bias,
    first_temporal,
    first_out_gain,
    first_out_bias,
    second_spatial,
    second_mid_gain,
    second_mid_bias,
    second_temporal,
    second_out_gain,
    second_out_bias,
    cotangent,
):
    shards = (
        first_spatial,
        first_mid_gain,
        first_mid_bias,
        first_temporal,
        first_out_gain,
        first_out_bias,
        second_spatial,
        second_mid_gain,
        second_mid_bias,
        second_temporal,
        second_out_gain,
        second_out_bias,
    )
    micro_total, frames, tile_side, channels = (
        inputs.shape[0],
        inputs.shape[1],
        inputs.shape[2],
        inputs.shape[4],
    )
    row_count = frames * tile_side * tile_side
    cell_count = frames * lax.axis_size("batch") * HGT * HGT
    offsets = jnp.arange(tile_side)
    inside_h = lax.axis_index("ha") * tile_side + offsets < HGT
    inside_w = lax.axis_index("wa") * tile_side + offsets < HGT
    valid_grid = inside_h[:, None] & inside_w[None, :]
    valid_tile = valid_grid.astype(jnp.bfloat16)[None, :, :, None]
    valid_rows = jnp.broadcast_to(
        valid_grid.astype(jnp.float32)[None], (frames, tile_side, tile_side)
    ).reshape(row_count, 1)
    results = []
    input_grads = []
    kernel_total = None
    norm_total = None
    for micro_step in range(micro_total):
        gathered = (
            lax.all_gather(shards[0], "batch", axis=0, tiled=True),
            lax.all_gather(shards[1], "batch", axis=0, tiled=True),
            lax.all_gather(shards[2], "batch", axis=0, tiled=True),
            lax.all_gather(shards[3], "batch", axis=0, tiled=True),
            lax.all_gather(shards[4], "batch", axis=0, tiled=True),
            lax.all_gather(shards[5], "batch", axis=0, tiled=True),
            lax.all_gather(shards[6], "batch", axis=0, tiled=True),
            lax.all_gather(shards[7], "batch", axis=0, tiled=True),
            lax.all_gather(shards[8], "batch", axis=0, tiled=True),
            lax.all_gather(shards[9], "batch", axis=0, tiled=True),
            lax.all_gather(shards[10], "batch", axis=0, tiled=True),
            lax.all_gather(shards[11], "batch", axis=0, tiled=True),
        )
        clip_gate = (1 - starts[micro_step]).astype(jnp.bfloat16).reshape(frames, 1, 1, 1)
        x_in = inputs[micro_step] * valid_tile
        first_kept, first_norm = forward_pair(
            x_in, gathered[0:6], clip_gate, valid_rows, cell_count
        )
        first_act = (
            (jax.nn.silu(first_norm) * valid_rows)
            .astype(jnp.bfloat16)
            .reshape(frames, tile_side, tile_side, channels)
        )
        second_kept, second_norm = forward_pair(
            first_act, gathered[6:12], clip_gate, valid_rows, cell_count
        )
        pre_out = second_norm + x_in.reshape(row_count, channels).astype(jnp.float32)
        results.append(
            (jax.nn.silu(pre_out) * valid_rows).reshape(frames, tile_side, tile_side, channels)
        )
        grad_pre = (
            cotangent[micro_step].reshape(row_count, channels).astype(jnp.float32)
            * valid_rows
            * silu_slope(pre_out)
        )
        grad_act, second_grads = backward_pair(
            grad_pre, second_kept, gathered[6:12], clip_gate, valid_rows, cell_count, tile_side
        )
        grad_first = grad_act * valid_rows * silu_slope(first_norm)
        grad_conv, first_grads = backward_pair(
            grad_first, first_kept, gathered[0:6], clip_gate, valid_rows, cell_count, tile_side
        )
        input_grads.append(
            ((grad_conv + grad_pre) * valid_rows).reshape(frames, tile_side, tile_side, channels)
        )
        step_grads = first_grads + second_grads
        kernel_now = (step_grads[0], step_grads[3], step_grads[6], step_grads[9])
        norm_now = (
            step_grads[1],
            step_grads[2],
            step_grads[4],
            step_grads[5],
            step_grads[7],
            step_grads[8],
            step_grads[10],
            step_grads[11],
        )
        if micro_step == 0:
            kernel_total = kernel_now
            norm_total = norm_now
        else:
            kernel_total = jax.tree.map(jnp.add, kernel_total, kernel_now)
            norm_total = jax.tree.map(jnp.add, norm_total, norm_now)
    kernel_total = lax.psum_scatter(kernel_total, "batch", scatter_dimension=0, tiled=True)
    kernel_total = jax.tree.map(
        lambda part: part.astype(jnp.float32), lax.psum(for_sending(kernel_total), ("ha", "wa"))
    )
    shard_index = lax.axis_index("batch")
    batch_count = lax.axis_size("batch")
    norm_shards = tuple(
        (
            lax.dynamic_slice_in_dim(
                full_sum,
                shard_index * (full_sum.shape[0] // batch_count),
                full_sum.shape[0] // batch_count,
            )
            for full_sum in norm_total
        )
    )
    return (
        jnp.stack(results),
        jnp.stack(input_grads),
        kernel_total[0],
        norm_shards[0],
        norm_shards[1],
        kernel_total[1],
        norm_shards[2],
        norm_shards[3],
        kernel_total[2],
        norm_shards[4],
        norm_shards[5],
        kernel_total[3],
        norm_shards[6],
        norm_shards[7],
    )


def solution(mesh):
    in_specs = (
        P(None, "batch", "ha", "wa", None),
        P(None, "batch"),
        P("batch", None),
        P("batch"),
        P("batch"),
        P("batch", None),
        P("batch"),
        P("batch"),
        P("batch", None),
        P("batch"),
        P("batch"),
        P("batch", None),
        P("batch"),
        P("batch"),
        P(None, "batch", "ha", "wa", None),
    )
    out_specs = (
        P(None, "batch", "ha", "wa", None),
        P(None, "batch", "ha", "wa", None),
        P("batch", None),
        P("batch"),
        P("batch"),
        P("batch", None),
        P("batch"),
        P("batch"),
        P("batch", None),
        P("batch"),
        P("batch"),
        P("batch", None),
        P("batch"),
        P("batch"),
    )
    batch = mesh.shape["batch"]

    def program(*args):
        spat, temp = args[2].shape[0], args[5].shape[0]
        fits = args[0].shape == (2, 16, 4, 4, 512) and args[2].shape[1] == 1152
        if fits and batch == 8 and spat * batch == 9 * 512 and temp * batch == 3 * 1152:
            return per_device_fast(batch, *args)
        return per_device(*args)

    return jax.shard_map(
        program, mesh=mesh, in_specs=in_specs, out_specs=out_specs, check_vma=False
    )
```

```python
import functools
from types import SimpleNamespace

import jax
import jax.numpy as jnp
from jax import lax
from jax.experimental import pallas as pl
from jax.experimental.pallas import tpu as pltpu
from jax.sharding import PartitionSpec as P

HGT = 7
epsilon = 1e-05
MESH = pl.DeviceIdType.MESH
F32 = jnp.float32
BF16 = jnp.bfloat16

BASE = 10
CELL = 8
ROWS = HGT * 8 * CELL
PADDED = (BASE + HGT * 8 + BASE) * CELL
MAIN = BASE * CELL
CHUNK = 2 * CELL
CHUNKS = ROWS // CHUNK
VMEM_LIMIT = 64 * 1024 * 1024 - 1024 * 1024


def when(cond, work):
    if cond is True:
        work()
    elif cond is not False:
        pl.when(cond)(work)


def loop(count, body, init):
    def twice(i, carry):
        return body(2 * i + 1, body(2 * i, carry))

    return lax.fori_loop(0, count // 2, twice, init)


def sigmoid(x):
    return 0.5 * jnp.tanh(0.5 * x) + 0.5


def nn(a, b):
    return jnp.dot(a, b, preferred_element_type=F32)


def nt(a, b):
    return lax.dot_general(a, b, (((1,), (1,)), ((), ())), preferred_element_type=F32)


def tn(a, b):
    return lax.dot_general(a, b, (((0,), (0,)), ((), ())), preferred_element_type=F32)


def rows_of(start, size, step=16):
    if not isinstance(start, int):
        start = pl.multiple_of(start, step)
    return pl.ds(start, size)


def per_batch(first, second, width):
    return jnp.concatenate(
        [jnp.broadcast_to(first, (CELL // 2, width)), jnp.broadcast_to(second, (CELL // 2, width))], axis=0
    )


def block_kernel(dims, names, *all_refs):
    r = SimpleNamespace(**dict(zip(names, all_refs, strict=True)))
    nb, chan, mid, cell_count = dims
    spat = 9 * chan // nb
    temp = 3 * mid // nb
    unit = spat // 6
    quarter = chan // 4
    half = chan // 2
    h = lax.axis_index("ha")
    w = lax.axis_index("wa")
    b = lax.axis_index("batch")
    par = lax.rem(b, 2)
    bh = lax.div(b, 2)
    pos = par * (nb - 1 - bh) + (1 - par) * bh
    ways = (1 - 2 * h, 2 * h - 1)

    def at(p):
        p = lax.rem(p + 4 * nb, nb)
        upper = lax.div(p, nb // 2)
        return (1 - upper) * (2 * p) + upper * (2 * (nb - 1 - p) + 1)

    def at_group(j):
        jw = lax.div(j, 2)
        odd = lax.rem(j, 2)
        return (odd * (1 - jw) + (1 - odd) * jw, jw)

    mine = (1 - w) * h + w * (3 - h)
    sibling = (1 - h, w, b)
    beside = (h, 1 - w, b)
    onward = [(h, w, at(pos + way)) for way in ways]
    later = lax.rem(mine + 1, 4)
    earlier = lax.rem(mine + 3, 4)
    later_dev = (*at_group(later), lax.rem(b + lax.div(mine + 1, 4), nb))
    earlier_dev = (*at_group(earlier), lax.rem(b + nb - lax.div(4 - mine, 4), nb))
    tile_group = [(lax.rem(mine + d, 4), (*at_group(lax.rem(mine + d, 4)), b)) for d in (1, 2, 3)]
    pos_b = w * 2 + par
    plane = []
    for d in (1, 2, 3):
        q = lax.rem(pos_b + d, 4)
        plane.append((q, (h, lax.div(q, 2), b - par + lax.rem(q, 2))))
    depth = nb // 2
    line = []
    for d in range(1, depth):
        q = lax.rem(bh + d, depth)
        line.append((q, (h, w, 2 * q + par)))

    def named(dev):
        return dict(ha=dev[0], wa=dev[1], batch=dev[2])

    def rc(src, dst, send, recv, dev):
        return pltpu.make_async_remote_copy(
            src_ref=src, dst_ref=dst, send_sem=send, recv_sem=recv, device_id=named(dev), device_id_type=MESH
        )

    def lc(src, dst, sem):
        return pltpu.make_async_copy(src, dst, sem)

    partners = [sibling, beside, *onward, later_dev, earlier_dev]
    partners += [dev for _, dev in tile_group + plane + line]
    barrier = pltpu.get_barrier_semaphore()
    for dev in partners:
        pl.semaphore_signal(barrier, inc=1, device_id=named(dev), device_id_type=MESH)
    pl.semaphore_wait(barrier, len(partners))

    shards = (r.first_spatial, r.first_temporal, r.second_spatial, r.second_temporal)
    whole = (r.w1s, r.w1t, r.w2s, r.w2t)
    shared = 2 * w + h
    shared_beside = 2 * (1 - w) + h
    third = temp // 3

    def units(i, core, side):
        return (2 * side + core, 4 + core) if i % 2 == 0 else ((1 - core) * side + 2 * core,)

    def piece(i, ref, owner, u):
        if i % 2 == 0:
            return ref.at[rows_of(owner * spat + u * unit, unit), :]
        return ref.at[rows_of(owner * temp + u * third, third), :]

    def streams(i):
        return (0, 1) if i % 2 == 0 else (0,)

    def crossing(i, work):
        if i % 2 == 0:
            work()
        else:
            pl.when(h == 0)(work)

    def crossed(i, work):
        if i % 2 == 0:
            work()
        else:
            pl.when(h == 1)(work)

    def own_copy(i):
        rows = spat if i % 2 == 0 else temp
        return lc(shards[i], whole[i].at[rows_of(b * rows, rows), :], r.own_sem.at[i])

    def ring(i, st, s, owner, from_shard=False):
        u = units(i, h, w)[st]
        dst = piece(i, whole[i], owner, u)
        src = piece(i, shards[i], 0, u) if from_shard else dst
        return rc(src, dst, r.ring_send.at[i, st, s], r.ring_recv.at[i, st, s], onward[st])

    def cross(i, kind, s, owner, u):
        part = piece(i, whole[i], owner, u)
        return rc(part, part, r.sib_send.at[i, kind, s], r.sib_recv.at[i, kind, s], sibling)

    def over(i, s, owner, u):
        part = piece(i, whole[i], owner, u)
        return rc(part, part, r.over_send.at[i, s], r.over_recv.at[i, s], beside)

    def gather_start(i):
        for st in streams(i):
            ring(i, st, 1, b, True).start()
        own_copy(i).start()

    def gather_relay(i, s):
        owner = at(pos - ways[0] * s)

        def work():
            over(i, s, owner, units(i, h, 1 - w)[0]).wait_recv()
            cross(i, 2, s, owner, units(i, h, 1 - w)[0]).start()

        crossing(i, work)

    def gather_pump(i, s):
        own = units(i, h, w)
        for st in streams(i):
            owner = at(pos - ways[st] * s)
            ring(i, st, s, owner).wait_recv()
            if isinstance(s, int):
                if s < nb - 1:
                    ring(i, st, s + 1, owner).start()
            else:
                pl.when(s < nb - 1)(lambda st=st, owner=owner: ring(i, st, s + 1, owner).start())
            if st == 0:
                crossing(i, lambda owner=owner: over(i, s, owner, own[0]).start())
            cross(i, st, s, owner, own[st]).start()
        if isinstance(s, int):
            if s > 1:
                gather_relay(i, s - 1)
        else:
            pl.when(s > 1)(lambda: gather_relay(i, s - 1))

    def gather_finish(i):
        gather_relay(i, nb - 1)

        def body(s, _):
            for st in streams(i):
                cross(i, st, s, at(pos + ways[st] * s), units(i, 1 - h, w)[st]).wait_recv()
            theirs = at(pos + ways[0] * s)
            crossed(i, lambda: cross(i, 2, s, theirs, units(i, 1 - h, 1 - w)[0]).wait_recv())
            return 0

        lax.fori_loop(1, nb, body, 0)
        own_copy(i).wait()

    def gather_sent(i):
        def body(s, _):
            for st in streams(i):
                owner = at(pos - ways[st] * s)
                ring(i, st, s, owner).wait_send()
                cross(i, st, s, owner, units(i, h, w)[st]).wait_send()

            def sent():
                owner = at(pos - ways[0] * s)
                over(i, s, owner, units(i, h, w)[0]).wait_send()
                cross(i, 2, s, owner, units(i, h, 1 - w)[0]).wait_send()

            crossing(i, sent)
            return 0

        lax.fori_loop(1, nb, body, 0)

    def total(k, width, value, works=()):
        slot = k % 2
        wide = value.shape[1]
        cols = pl.ds(0, wide)
        works = list(works) + [None] * 3
        pair, four, far = r.sum_a, r.sum_b, r.sum_c
        pair[slot, h, :, cols] = value
        part = pair.at[slot, h, :, cols]
        send_a = rc(part, part, r.sa_send.at[k], r.sa_recv.at[k], sibling)
        send_a.start()
        if works[0]:
            works[0]()
        part = pair.at[slot, 1 - h, :, cols]
        rc(part, part, r.sa_send.at[k], r.sa_recv.at[k], sibling).wait_recv()
        four[slot, pos_b, :, cols] = pair[slot, 0, :, cols] + pair[slot, 1, :, cols]
        sends = [send_a]
        for n, (q, dev) in enumerate(plane):
            part = four.at[slot, pos_b, :, cols]
            sends.append(rc(part, part, r.sb_send.at[k, n], r.sb_recv.at[k, pos_b], dev))
            sends[-1].start()
        if works[1]:
            works[1]()
        for n, (q, dev) in enumerate(plane):
            part = four.at[slot, q, :, cols]
            rc(part, part, r.sb_send.at[k, n], r.sb_recv.at[k, q], dev).wait_recv()
        far[slot, bh, :, cols] = (four[slot, 0, :, cols] + four[slot, 1, :, cols]) + (
            four[slot, 2, :, cols] + four[slot, 3, :, cols]
        )
        for n, (q, dev) in enumerate(line):
            part = far.at[slot, bh, :, cols]
            sends.append(rc(part, part, r.sc_send.at[k, n], r.sc_recv.at[k, bh], dev))
            sends[-1].start()
        if works[2]:
            works[2]()
        for n, (q, dev) in enumerate(line):
            part = far.at[slot, q, :, cols]
            rc(part, part, r.sc_send.at[k, n], r.sc_recv.at[k, q], dev).wait_recv()
        result = far[slot, 0, :, cols]
        for q in range(1, depth):
            result = result + far[slot, q, :, cols]
        for send in sends:
            send.wait_send()
        if wide == width:
            return result
        return jnp.concatenate([result[0:4], result[4:8, 2 * wide - width :]], axis=1)

    def chunk(ref, i, base=0, width=None):
        cols = slice(None) if width is None else pl.ds(0, width)
        value = ref[rows_of(base + i * CHUNK, CHUNK), cols]
        return value.astype(F32).reshape(2, CELL, value.shape[-1])

    def put(ref, i, value, base=0, width=None):
        cols = slice(None) if width is None else pl.ds(0, width)
        ref[rows_of(base + i * CHUNK, CHUNK), cols] = value.reshape(CHUNK, value.shape[-1]).astype(ref.dtype)

    def keep(i):
        inside = jnp.where(lax.rem(i, 4) == 3, 0.0, 1.0).astype(F32)
        first = lax.broadcasted_iota(jnp.int32, (2, 1, 1), 0) == 0
        return jnp.where(first, 1.0, inside)

    def packed(one, two, width):
        rows = [
            jnp.sum(v[k : k + CELL // 2], axis=0, keepdims=True) for v in (one, two) for k in (0, CELL // 2)
        ]
        rows = jnp.concatenate(rows, axis=0)
        wide = -(-width // 256) * 128
        return jnp.concatenate([rows[:, 0:wide], rows[:, width - wide :]], axis=0)

    def moments(ref, width):
        def body(i, carry):
            v = chunk(ref, i)
            m = v * keep(i)
            return (carry[0] + m[0] + m[1], carry[1] + m[0] * v[0] + m[1] * v[1])

        zero = jnp.zeros((CELL, width), F32)
        return loop(CHUNKS, body, (zero, zero))

    def prepare(n, sums, width):
        tile = r.tile_mid if width == mid else r.tile_out
        n2 = n // 2
        gain = r.param[2 * n : 2 * n + 1, 0:width]
        bias = r.param[2 * n + 1 : 2 * n + 2, 0:width]
        mean = sums[0:2] / cell_count
        inv = lax.rsqrt(sums[2:4] / cell_count - mean * mean + epsilon)
        scale = inv * gain
        shift = bias - mean * scale
        for k, v in enumerate((scale, shift, inv, mean * inv)):
            tile[n2, k] = per_batch(v[0:1], v[1:2], width)

    def tiles(n, width):
        tile = r.tile_mid if width == mid else r.tile_out
        return [tile[n // 2, k][None] for k in range(4)]

    def fill(ref_a, ref_b, value_of, width):
        pads(ref_a, ref_b, width)

        def body(i, before):
            v = value_of(i)
            put(ref_a, i, v, MAIN)
            pair = jnp.concatenate([before[None], v[0:1]], axis=0)
            put(ref_b, i, pair, MAIN - CHUNK)
            return v[1]

        loop(CHUNKS, body, jnp.zeros((CELL, width), F32))

    def activated(src, n, width):
        def value(i):
            scale, shift, _, _ = tiles(n, width)
            y = chunk(src, i) * scale + shift
            return y * sigmoid(y) * keep(i)

        return value

    def taps(ref_a, ref_b, k, size=ROWS):
        r0 = MAIN - 8 * CELL + 8 * CELL * k
        return (
            ref_b[rows_of(r0 - CHUNK, size), :],
            ref_a[rows_of(r0, size), :],
            ref_b[rows_of(r0, size), :],
        )

    def conv(ref_a, ref_b, weight, out, pump=None):
        for n, (c0, cw) in enumerate(((0, 512), (512, mid - 512))):

            def body(a, _, c0=c0, cw=cw, n=n):
                x = taps(ref_a, ref_b, a)
                acc = nn(jnp.concatenate(x, axis=1), weight[rows_of(a * 3 * chan, 3 * chan), c0 : c0 + cw])

                @pl.when(a == 0)
                def _():
                    out[:, c0 : c0 + cw] = acc

                @pl.when(a > 0)
                def _():
                    out[:, c0 : c0 + cw] += acc

                if pump is not None:
                    pump(n * 3 + a)
                return 0

            lax.fori_loop(0, 3, body, 0)

    def conv_back(ref_a, ref_b, weight, out, pump=None):
        def body(k, _):
            e = taps(ref_a, ref_b, k)
            acc = None
            for j in range(3):
                tap = 8 - 3 * k - j
                term = nt(e[j], weight[rows_of(tap * chan, chan), :])
                acc = term if acc is None else acc + term

            @pl.when(k == 0)
            def _():
                out[:, 0:chan] = acc

            @pl.when(k > 0)
            def _():
                out[:, 0:chan] += acc

            if pump is not None:
                pump(k)
            return 0

        lax.fori_loop(0, 3, body, 0)

    def send_frames(k):
        down, up = r.down, r.up
        count = ROWS // 4
        for c in range(chan // 128):
            lanes = pl.ds(128 * c, 128)
            r.halo_out[0, :, lanes] = down[c, pl.ds(CELL + 3, count, stride=4), :].astype(BF16)
            r.halo_out[1, :, lanes] = up[c, pl.ds(0, count, stride=4), :].astype(BF16)
        copies = []
        for n, dev in ((0, later_dev), (1, earlier_dev)):
            copies.append(
                rc(r.halo_out.at[n], r.halo_in.at[k, n], r.halo_send.at[k, n], r.halo_recv.at[k, n], dev)
            )
            copies[-1].start()
        return copies

    def take_frames(k, copies):
        down, up = r.down, r.up
        count = ROWS // 4
        for copy in copies:
            copy.wait()
        at_start = jnp.logical_and(mine == 0, b == 0)
        at_end = jnp.logical_and(mine == 3, b == nb - 1)
        for c in range(chan // 128):
            lanes = pl.ds(128 * c, 128)
            before = r.halo_in[k, 0, :, lanes].astype(F32)
            after = r.halo_in[k, 1, :, lanes].astype(F32)
            down[c, pl.ds(CELL - 1, count, stride=4), :] = jnp.where(at_start, 0.0, before)
            up[c, pl.ds(4, count, stride=4), :] = jnp.where(at_end, 0.0, after)

    def by_lanes(ref, rows):
        return jnp.concatenate([ref[c, rows, :] for c in range(chan // 128)], axis=1)

    def put_lanes(ref, rows, value):
        for c in range(chan // 128):
            ref[c, rows, :] = value[:, 128 * c : 128 * c + 128]

    def shifted(i):
        before = by_lanes(r.down, rows_of(i * CHUNK, CHUNK + CELL))[CELL - 1 : CELL - 1 + CHUNK]
        after = by_lanes(r.up, rows_of(i * CHUNK, CHUNK + CELL))[1 : 1 + CHUNK]
        gate = r.gate[...][None]
        return (before.reshape(2, CELL, chan) * gate, after.reshape(2, CELL, chan))

    def temporal(k, v, weight, out, works=()):
        works = list(works) + [None] * 2
        put_lanes(r.down, pl.ds(CELL, ROWS), nn(v[...], weight[0:mid, :]))
        y2 = nn(v[...], weight[2 * mid : 3 * mid, :])
        y2 = (y2.reshape(ROWS // CELL, CELL, chan) * r.gate[...][None]).reshape(ROWS, chan)
        put_lanes(r.up, pl.ds(0, ROWS), y2)
        copies = send_frames(k)
        out[...] = nn(v[...], weight[mid : 2 * mid, :])
        if works[0]:
            works[0]()
        take_frames(k, copies)

        def body(i, carry):
            before, after = shifted(i)
            value = chunk(out, i) + before + after
            put(out, i, value)
            m = value * keep(i)
            return (carry[0] + m[0] + m[1], carry[1] + m[0] * value[0] + m[1] * value[1])

        zero = jnp.zeros((CELL, chan), F32)
        return loop(CHUNKS, body, (zero, zero))

    def temporal_back(k, weight, works=()):
        works = list(works) + [None] * 2
        copies = send_frames(k)
        e3 = r.e3
        for c0, cw in ((0, 512), (512, mid - 512)):
            r.grad_mid[:, c0 : c0 + cw] = nt(e3[1], weight[mid + c0 : mid + c0 + cw, :])
        if works[0]:
            works[0]()
        take_frames(k, copies)

        def body(i, _):
            before, after = shifted(i)
            e3[0, rows_of(i * CHUNK, CHUNK), :] = after.reshape(CHUNK, chan).astype(BF16)
            e3[2, rows_of(i * CHUNK, CHUNK), :] = before.reshape(CHUNK, chan).astype(BF16)
            return 0

        loop(CHUNKS, body, 0)
        share = share_e3(k)
        for c0, cw in ((0, 512), (512, mid - 512)):
            r.grad_mid[:, c0 : c0 + cw] += nt(e3[0], weight[c0 : c0 + cw, :]) + nt(
                e3[2], weight[2 * mid + c0 : 2 * mid + c0 + cw, :]
            )
        return share

    def share(k, src, dst):
        copy = rc(src, dst, r.share_send.at[k], r.share_recv.at[k], sibling)
        copy.start()
        return copy

    outs = (r.out1s, r.out1t, r.out2s, r.out2t)

    halves = ((0, 512), (512, mid - 512))

    def e_part(n, slot):
        c0, cw = halves[n]
        return r.e_all.at[slot * ROWS : (slot + 1) * ROWS, c0 : c0 + cw]

    def e_copies(k, n):
        sems = [(r.e_send.at[k, n, m], r.e_recv.at[k, n, m]) for m in range(3)]
        return [
            rc(e_part(n, 0), e_part(n, 1), *sems[0], sibling),
            rc(e_part(n, 0), e_part(n, 2), *sems[1], beside),
            rc(e_part(n, 2), e_part(n, 3), *sems[2], sibling),
        ]

    def share_e(k):
        for n in (0, 1):
            near, over, _ = e_copies(k, n)
            over.start()
            near.start()

    def share_e_on(k, n):
        _, over, far = e_copies(k, n)
        over.wait_recv()
        far.start()

    def share_e_wait(k, n):
        near, over, far = e_copies(k, n)
        near.wait()
        over.wait_send()
        far.wait()

    def share_x(k, xa, xq):
        copies = []
        for n, dev in enumerate((sibling, beside, (1 - h, 1 - w, b))):
            lanes = rows_of((2 * dev[1] + dev[0]) * quarter, quarter, 128)
            main = pl.ds(MAIN, ROWS)
            copies.append(
                rc(xa.at[main, lanes], xq.at[n, 0, main, :], r.xq_send.at[k, n], r.xq_recv.at[k, n], dev)
            )
            copies[-1].start()
        return copies

    def pads(ref_a, ref_b, width):
        ref_a[0:MAIN, :] = jnp.zeros((MAIN, width), BF16)
        ref_a[MAIN + ROWS : PADDED, :] = jnp.zeros((PADDED - MAIN - ROWS, width), BF16)
        ref_b[0 : MAIN - CHUNK, :] = jnp.zeros((MAIN - CHUNK, width), BF16)
        ref_b[MAIN - CHUNK + ROWS : PADDED, :] = jnp.zeros((PADDED - MAIN + CHUNK - ROWS, width), BF16)

    def spread_x(xq):
        for n in range(3):
            pads(xq.at[n, 0], xq.at[n, 1], quarter)

        def body(i, before):
            after = []
            for n in range(3):
                v = chunk(xq.at[n, 0], i, MAIN)
                put(xq.at[n, 1], i, jnp.concatenate([before[n][None], v[0:1]], axis=0), MAIN - CHUNK)
                after.append(v[1])
            return tuple(after)

        loop(CHUNKS, body, (jnp.zeros((CELL, quarter), F32),) * 3)

    def share_e3(k):
        return share(
            k - 2, r.e3.at[:, :, rows_of((1 - h) * half, half, 128)], r.sib_e3
        )

    def grad_tap(owner):
        return owner + jnp.where(owner > 2 * shared, 1, 0)

    spare = r.w2s

    def gq(i, row, size):
        return rows_of((mid if i == 0 else 0) + row, size)

    def inbox(i, row, size):
        return rows_of(2 * mid + (mid if i == 0 else 0) + row, size)

    def transpose_x(a, xa, xb, xq, near, far, row):
        lanes = rows_of(shared * quarter, quarter, 128)
        r0 = MAIN - 8 * CELL + 8 * CELL * a
        for j, (c, start) in enumerate(((1, r0 - CHUNK), (0, r0), (1, r0))):
            rows = rows_of(start, ROWS)
            own = (xb if c else xa)[rows, lanes]
            both = jnp.concatenate([own, xq[0, c, rows, :]], axis=0)
            near[rows_of(row + j * quarter, quarter), 0 : 2 * ROWS] = both.T
            both = jnp.concatenate([xq[1, c, rows, :], xq[2, c, rows, :]], axis=0)
            far[rows_of(row + j * quarter, quarter), 0 : 2 * ROWS] = both.T

    def spatial_part(i, near, far, row, out_row, n):
        c0, cw = halves[n]
        rows = rows_of(row, 3 * quarter)
        acc = nn(near[rows, 0 : 2 * ROWS], r.e_all[0 : 2 * ROWS, c0 : c0 + cw])
        acc += nn(far[rows, 0 : 2 * ROWS], r.e_all[2 * ROWS : 4 * ROWS, c0 : c0 + cw])
        spare[gq(i, out_row, 3 * quarter), c0 : c0 + cw] = acc.astype(BF16)

    def transposes(xa, xb, xq, near, far):
        def body(a, _):
            transpose_x(a, xa, xb, xq, near, far, a * 3 * quarter)
            return 0

        lax.fori_loop(0, 3, body, 0)

    def spatial_half(i, near, far, n):
        def body(a, _):
            spatial_part(i, near, far, a * 3 * quarter, a * 3 * quarter, n)
            return 0

        lax.fori_loop(0, 3, body, 0)

    def transpose_v(v, sv):
        for c in range(mid // 128):
            lanes = pl.ds(128 * c, 128)
            r.xt[128 * c : 128 * c + 128, :] = jnp.concatenate([v[:, lanes], sv[:, lanes]], axis=0).T

    def temporal_grad(i, k):
        e = jnp.concatenate([r.e3[k, :, rows_of(h * half, half, 128)], r.sib_e3[k]], axis=0)
        whole[i][k * mid : (k + 1) * mid, 0:half] = nn(r.xt[...], e).astype(BF16)

    def cols_of(n):
        c0, cw = halves[n]
        return pl.ds(c0, cw)

    def s_block(i, n, owner):
        return spare.at[gq(i, grad_tap(owner) * quarter, quarter), cols_of(n)]

    def s_extra(i, n, side):
        return spare.at[gq(i, (2 * shared + 1) * quarter + side * 64, 64), cols_of(n)]

    def t_block(i, owner):
        return whole[i].at[rows_of(owner * temp, temp), 0:half]

    def t_inbox(i, n):
        return whole[i].at[rows_of(n * temp, temp), half:chan]

    def parts_of(i):
        return (0, 1) if i % 2 == 0 else (0,)

    def block_of(i, n, owner):
        return s_block(i, n, owner) if i % 2 == 0 else t_block(i, owner)

    def y_box(i, n, place):
        return spare.at[inbox(i, place * quarter, quarter), cols_of(n)] if i % 2 == 0 else t_inbox(i, place)

    def z_box(i, n, place):
        return spare.at[inbox(i, 576 + place * quarter, quarter), cols_of(n)] if i % 2 == 0 else t_inbox(i, 4 + place)

    def extra_y_box(i, n):
        return spare.at[inbox(i, 4 * quarter, 64), cols_of(n)]

    def extra_z_box(i, n, place):
        return spare.at[inbox(i, 576 + 3 * quarter + place * 64, 64), cols_of(n)]

    across = (h, w, b + 1 - 2 * par)

    def add_into(dst, parts, step):
        rows, cols = dst.shape

        def body(n, _):
            at_rows = rows_of(n * step, step)
            value = dst[at_rows, :].astype(F32)
            for part in parts:
                value = value + part[at_rows, :].astype(F32)
            dst[at_rows, :] = value.astype(BF16)
            return 0

        lax.fori_loop(0, rows // step, body, 0)

    def y_copy(i, n, d):
        place = lax.rem(bh + d, depth)
        src = block_of(i, n, 2 * place + 1 - par)
        return rc(src, y_box(i, n, place), r.y_send.at[i, n, d], r.y_recv.at[i, n, place], across)

    def z_copy(i, n, d):
        place = lax.rem(bh + d, depth)
        src = block_of(i, n, 2 * place + par)
        dev = (h, w, 2 * place + par)
        return rc(src, z_box(i, n, 3 - d), r.z_send.at[i, n, d], r.z_recv.at[i, n, 3 - d], dev)

    def extra_y(i, n):
        return rc(s_extra(i, n, 1 - par), extra_y_box(i, n), r.y_send.at[i, n, 4], r.y_recv.at[i, n, 4], across)

    def extra_z(i, n):
        place = jnp.minimum(lax.rem(bh - shared + 3 + depth, depth), 2)
        dev = (h, w, 2 * shared + par)
        return rc(
            s_extra(i, n, par), extra_z_box(i, n, place), r.z_send.at[i, n, 4], r.z_recv.at[i, n, 4 + place], dev
        )

    def step_of(i):
        return 16 if i % 2 == 0 else 48

    def reduce_start(i, n):
        for d in (1, 2, 3, 0):
            y_copy(i, n, d).start()
        if i % 2 == 0:
            extra_y(i, n).start()

    def reduce_middle(i, n):
        for d in (1, 2, 3, 0):
            place = lax.rem(bh + d, depth)
            y_copy(i, n, d).wait_send()
            box = y_box(i, n, place)
            rc(box, box, r.y_send.at[i, n, d], r.y_recv.at[i, n, place], across).wait_recv()
            add_into(block_of(i, n, 2 * place + par), [box], step_of(i))
            if d:
                z_copy(i, n, d).start()
        if i % 2 == 0:
            extra_y(i, n).wait()
            add_into(s_extra(i, n, par), [extra_y_box(i, n)], 16)
            pl.when(bh != shared)(lambda: extra_z(i, n).start())

    def final_part(i, n, side, core):
        place = 2 * side + core
        start = quarter * place - 64 * b + 512 * jnp.where(b > 2 * place, 1, 0)
        return outs[i].at[rows_of(start, quarter, 64), cols_of(n)]

    def extra_part(i, n):
        return outs[i].at[rows_of(512 * (1 - par), 64, 64), cols_of(n)]

    def final_copies(i, n):
        if i % 2:
            src = t_block(i, b)
            part = outs[i].at[h]
            return lc(src, part, r.out_sem.at[i, 0, 0]), [
                (src, part, sibling, r.cast_send.at[i, 0, 0], r.cast_recv.at[i, 0, 0])
            ]
        src = s_block(i, n, b)
        part = final_part(i, n, w, h)
        sends = [
            (src, part, dev, r.cast_send.at[i, n, d], r.cast_recv.at[i, n, d]) for d, dev in enumerate((beside, sibling))
        ]
        return lc(src, part, r.out_sem.at[i, n, 0]), sends

    def extra_copies(i, n):
        src = s_extra(i, n, par)
        part = extra_part(i, n)
        sends = [
            (src, part, dev, r.cast_send.at[i, n, 3 + d], r.cast_recv.at[i, n, 3 + d])
            for d, dev in enumerate((beside, sibling))
        ]
        return lc(src, part, r.out_sem.at[i, n, 1]), sends

    def begin(copies):
        local, sends = copies
        for src, part, dev, one, two in sends:
            rc(src, part, one, two, dev).start()
        local.start()

    def beside_copy(i):
        return rc(t_block(i, b), t_inbox(i, 7), r.z_send.at[i, 0, 4], r.z_recv.at[i, 0, 4], beside)

    def reduce_last(i, n):
        for d in (1, 2, 3):
            z_copy(i, n, d).wait()
        add_into(block_of(i, n, b), [z_box(i, n, place) for place in range(3)], step_of(i))
        if i % 2:
            beside_copy(i).start()
            return
        begin(final_copies(i, n))

        @pl.when(bh != shared)
        def _():
            extra_z(i, n).wait_send()

        @pl.when(bh == shared)
        def _():
            boxes = [extra_z_box(i, n, place) for place in range(3)]
            for place, box in enumerate(boxes):
                rc(box, box, r.z_send.at[i, n, 4], r.z_recv.at[i, n, 4 + place], across).wait_recv()
            add_into(s_extra(i, n, par), boxes, 16)
            begin(extra_copies(i, n))

    def reduce_out(i):
        beside_copy(i).wait()
        add_into(t_block(i, b), [t_inbox(i, 7)], 48)
        begin(final_copies(i, 0))

    def final_on(i, n):
        def move(part, d):
            rc(part, part, r.cast_send.at[i, n, d], r.cast_recv.at[i, n, d], beside).wait_recv()
            rc(part, part, r.cast_send.at[i, n, d + 2], r.cast_recv.at[i, n, d + 2], sibling).start()

        move(final_part(i, n, 1 - w, h), 0)
        pl.when(bh == shared_beside)(lambda: move(extra_part(i, n), 3))

    def reduce_wait(i, n):
        local, sends = final_copies(i, n)
        local.wait()
        if i % 2:
            src, part, dev, one, two = sends[0]
            rc(src, outs[i].at[1 - h], one, two, dev).wait()
            return
        for src, part, dev, one, two in sends:
            rc(src, part, one, two, dev).wait_send()

        def far(part, d):
            return rc(part, part, r.cast_send.at[i, n, d], r.cast_recv.at[i, n, d], sibling)

        far(final_part(i, n, w, 1 - h), 1).wait_recv()
        far(final_part(i, n, 1 - w, h), 2).wait_send()
        far(final_part(i, n, 1 - w, 1 - h), 2).wait_recv()
        local, sends = extra_copies(i, n)

        @pl.when(bh == shared)
        def _():
            local.wait()
            for src, part, dev, one, two in sends:
                rc(src, part, one, two, dev).wait_send()

        pl.when(bh == shared_beside)(lambda: far(extra_part(i, n), 5).wait_send())
        pl.when(bh == 2 * w + 1 - h)(lambda: far(extra_part(i, n), 4).wait_recv())
        pl.when(bh == 2 * (1 - w) + 1 - h)(lambda: far(extra_part(i, n), 5).wait_recv())

    def tile_of(ref, jh, jw):
        return ref.at[rows_of(jh * 4, 4, 4), rows_of(jw * 32, 32), :]

    def scatter(src, dst, n):
        copies = []
        for d, (j, dev) in enumerate(tile_group):
            copies.append(
                rc(src.at[j], tile_of(dst, h, w), r.tile_send.at[n, d], r.tile_recv.at[n, mine], dev)
            )
        return copies

    def scattered(src, dst, n):
        for d, (j, dev) in enumerate(tile_group):
            jh, jw = at_group(j)
            rc(src.at[j], tile_of(dst, jh, jw), r.tile_send.at[n, d], r.tile_recv.at[n, j], dev).wait()

    def tiles_start(src, dst, n):
        for copy in scatter(src, dst, n):
            copy.start()
        lc(src.at[mine], tile_of(dst, h, w), r.tile_own.at[n]).start()

    def tiles_wait(src, dst, n):
        scattered(src, dst, n)
        lc(src.at[mine], tile_of(dst, h, w), r.tile_own.at[n]).wait()

    xg, cg = r.x_grid, r.cot_grid
    tiles_start(r.x_tiles, xg, 0)
    gather_start(0)
    r.param[...] = total(0, mid, r.param_in[...])
    tiles_wait(r.x_tiles, xg, 0)

    def grid_chunk(ref, i):
        v = ref[lax.div(i, 4), rows_of(lax.rem(i, 4) * CHUNK, CHUNK), :]
        return v.astype(F32).reshape(2, CELL, chan)

    fill(r.xa, r.xb, lambda i: grid_chunk(xg, i), chan)

    def pump_loop(i, lo, hi):
        def body(s, _):
            gather_pump(i, s)
            return 0

        lax.fori_loop(lo, hi, body, 0)

    pump_loop(0, 1, nb - 3)
    gather_start(1)
    pump_loop(0, nb - 3, nb - 1)
    gather_start(2)
    gather_pump(0, nb - 1)
    gather_pump(1, 1)
    gather_pump(2, 1)
    gather_pump(1, 2)
    gather_finish(0)

    def first_pump(n):
        pl.when(lax.rem(n, 2) == 0)(lambda: gather_pump(1, 3 + lax.div(n, 2)))
        pl.when(n == 3)(lambda: gather_pump(2, 2))

    conv(r.xa, r.xb, r.w1s, r.mid1, first_pump)
    sums = total(
        1,
        mid,
        packed(*moments(r.mid1, mid), mid),
        [lambda: gather_pump(1, nb - 2), lambda: gather_pump(2, 3), lambda: gather_pump(1, nb - 1)],
    )
    prepare(0, sums, mid)

    def hidden(src, n, dst):
        value = activated(src, n, mid)

        def body(i, _):
            put(dst, i, value(i))
            return 0

        loop(CHUNKS, body, 0)

    hidden(r.mid1, 0, r.v1)
    gather_pump(2, 4)
    gather_finish(1)
    stats = temporal(0, r.v1, r.w1t, r.time1, [lambda: gather_pump(2, 5)])

    def sixth():
        gather_pump(2, 6)

    sums = total(2, chan, packed(*stats, chan), [lambda: gather_start(3), None, sixth])
    prepare(1, sums, chan)
    fill(r.aa, r.ab, activated(r.time1, 1, chan), chan)
    gather_pump(3, 1)
    gather_pump(2, nb - 1)
    gather_pump(3, 2)
    gather_finish(2)
    tiles_start(r.cot_tiles, cg, 1)

    def second_pump(n):
        pl.when(n < nb - 3)(lambda: gather_pump(3, 3 + n))

    conv(r.aa, r.ab, r.w2s, r.mid2, second_pump)
    sums = total(3, mid, packed(*moments(r.mid2, mid), mid), [lambda: gather_finish(3)])
    prepare(2, sums, mid)
    hidden(r.mid2, 2, r.v2)
    stats = temporal(1, r.v2, r.w2t, r.time2)
    shared_xq2 = share_x(0, r.aa, r.xq2)
    shared_xq1 = share_x(1, r.xa, r.xq1)
    for i in range(4):
        gather_sent(i)
    share_v2 = share(4, r.v2, r.sib_v)
    sums = total(4, chan, packed(*stats, chan))
    tiles_wait(r.cot_tiles, cg, 1)
    prepare(3, sums, chan)

    out_grid = r.out_grid

    def grid_put(ref, i, v):
        ref[lax.div(i, 4), rows_of(lax.rem(i, 4) * CHUNK, CHUNK), :] = v.reshape(CHUNK, chan).astype(ref.dtype)

    def slope(y, s):
        return s * (1.0 + y * (1.0 - s))

    def pre_body(i, carry):
        scale, shift, inv, offset = tiles(3, chan)
        v = chunk(r.time2, i)
        y = v * scale + shift + chunk(r.xa, i, MAIN)
        s = sigmoid(y)
        m = keep(i)
        grid_put(out_grid, i, y * s * m)
        d = grid_chunk(cg, i) * m * slope(y, s)
        put(r.grad_pre, i, d)
        t = d * (v * inv - offset)
        return (carry[0] + d[0] + d[1], carry[1] + t[0] + t[1])

    zero_out = jnp.zeros((CELL, chan), F32)
    zero_mid = jnp.zeros((CELL, mid), F32)
    out_grid[HGT] = jnp.zeros((8 * CELL, chan), BF16)
    gg = loop(CHUNKS, pre_body, (zero_out, zero_out))

    def send_tiles(src, dst, n):
        for d, (j, dev) in enumerate(tile_group):
            jh, jw = at_group(j)
            rc(tile_of(src, jh, jw), dst.at[mine], r.tile_send.at[n, d], r.tile_recv.at[n, mine], dev).start()
        lc(tile_of(src, h, w), dst.at[mine], r.tile_own.at[n]).start()

    def sent_tiles(src, dst, n):
        for d, (j, dev) in enumerate(tile_group):
            jh, jw = at_group(j)
            rc(tile_of(src, jh, jw), dst.at[j], r.tile_send.at[n, d], r.tile_recv.at[n, j], dev).wait()
        lc(tile_of(src, h, w), dst.at[mine], r.tile_own.at[n]).wait()

    send_tiles(out_grid, r.block_out, 2)

    def norm_back(n, sums, width):
        r.norm_grads[2 * n : 2 * n + 1, 0:width] = sums[2:3] + sums[3:4]
        r.norm_grads[2 * n + 1 : 2 * n + 2, 0:width] = sums[0:1] + sums[1:2]
        back = r.back
        back[0, :, 0:width] = per_batch(sums[0:1], sums[1:2], width) / cell_count
        back[1, :, 0:width] = per_batch(sums[2:3], sums[3:4], width) / cell_count

    def through_norm(n, src, grad, i, width):
        scale, _, inv, offset = tiles(n, width)
        xhat = chunk(src, i) * inv - offset
        bias_part = r.back[0, :, 0:width][None]
        gain_part = r.back[1, :, 0:width][None]
        return scale * (chunk(grad, i, 0, width) - bias_part - xhat * gain_part) * keep(i)

    def through_act(n, src, grad, width):
        def body(i, carry):
            scale, shift, inv, offset = tiles(n, width)
            v = chunk(src, i)
            y = v * scale + shift
            s = sigmoid(y)
            d = chunk(grad, i, 0, width) * keep(i) * slope(y, s)
            put(grad, i, d, 0, width)
            t = d * (v * inv - offset)
            return (carry[0] + d[0] + d[1], carry[1] + t[0] + t[1])

        zero = jnp.zeros((CELL, width), F32)
        return loop(CHUNKS, body, (zero, zero))

    def to_frames(n, src, grad):
        def body(i, _):
            e = through_norm(n, src, grad, i, chan).astype(BF16)
            ef = e.astype(F32)
            r.e3[1, rows_of(i * CHUNK, CHUNK), :] = e.reshape(CHUNK, chan)
            put_lanes(r.down, rows_of(i * CHUNK + CELL, CHUNK, CELL), ef.reshape(CHUNK, chan))
            put_lanes(r.up, rows_of(i * CHUNK, CHUNK), (ef * r.gate[...][None]).reshape(CHUNK, chan))
            return 0

        loop(CHUNKS, body, 0)

    sums = total(5, chan, packed(*gg, chan))
    norm_back(3, sums, chan)
    to_frames(3, r.time2, r.grad_pre)
    shared_e3 = temporal_back(2, r.w2t)
    gg = through_act(2, r.mid2, r.grad_mid, mid)
    shared_e3.wait()
    share_v2.wait()
    def temporal_grads(i, v):
        def first():
            transpose_v(v, r.sib_v)
            temporal_grad(i, 0)

        return [first, lambda: temporal_grad(i, 1), lambda: temporal_grad(i, 2)]

    sums = total(6, mid, packed(*gg, mid), temporal_grads(3, r.v2))
    reduce_start(3, 0)
    norm_back(2, sums, mid)

    def fill_e(n, src):
        def value(i):
            v = through_norm(n, src, r.grad_mid, i, mid)
            put(r.e_all, i, v)
            return v

        fill(r.ea, r.eb, value, mid)

    fill_e(2, r.mid2)
    share_e(0)
    conv_back(r.ea, r.eb, r.w2s, r.grad_mid)
    share_e_on(0, 0)
    gg = through_act(1, r.time1, r.grad_mid, chan)
    for copy in shared_xq2:
        copy.wait()
    near, far = spare.at[mid : 2 * mid, :], spare.at[3 * mid : 4 * mid, :]

    def spread_and_turn():
        spread_x(r.xq2)
        transposes(r.aa, r.ab, r.xq2, near, far)

    def first_half():
        share_e_wait(0, 0)
        spatial_half(2, near, far, 0)

    sums = total(7, chan, packed(*gg, chan), [spread_and_turn, first_half, lambda: share_e_on(0, 1)])
    reduce_start(2, 0)
    reduce_middle(3, 0)
    share_v1 = share(5, r.v1, r.sib_v)
    norm_back(1, sums, chan)
    to_frames(1, r.time1, r.grad_mid)

    def second_half():
        share_e_wait(0, 1)
        spatial_half(2, near, far, 1)
        reduce_start(2, 1)

    shared_e3 = temporal_back(3, r.w1t, [second_half])
    reduce_last(3, 0)
    gg = through_act(0, r.mid1, r.grad_mid, mid)
    shared_e3.wait()
    share_v1.wait()
    sums = total(8, mid, packed(*gg, mid), temporal_grads(1, r.v1))
    reduce_start(1, 0)
    norm_back(0, sums, mid)
    fill_e(0, r.mid1)
    share_e(1)
    reduce_out(3)
    for n in (0, 1):
        reduce_middle(2, n)
    for copy in shared_xq1:
        copy.wait()
    spread_x(r.xq1)
    sent_tiles(out_grid, r.block_out, 2)
    conv_back(r.ea, r.eb, r.w1s, r.grad_mid)
    share_e_on(1, 0)
    near, far = r.w1s.at[0:mid, :], r.w1s.at[mid : 2 * mid, :]
    transposes(r.xa, r.xb, r.xq1, near, far)
    share_e_wait(1, 0)
    spatial_half(0, near, far, 0)
    reduce_start(0, 0)
    share_e_on(1, 1)
    share_e_wait(1, 1)
    spatial_half(0, near, far, 1)
    reduce_start(0, 1)

    def last_body(i, _):
        grid_put(out_grid, i, (chunk(r.grad_mid, i, 0, chan) + chunk(r.grad_pre, i)) * keep(i))
        return 0

    loop(CHUNKS, last_body, 0)
    send_tiles(out_grid, r.grad_input, 3)
    for n in (0, 1):
        reduce_last(2, n)
    reduce_middle(1, 0)
    for n in (0, 1):
        final_on(2, n)
    reduce_middle(0, 0)
    reduce_last(1, 0)
    reduce_out(1)
    reduce_last(0, 0)
    reduce_middle(0, 1)
    final_on(0, 0)
    reduce_last(0, 1)
    sent_tiles(out_grid, r.grad_input, 3)
    for n in (0, 1):
        reduce_wait(2, n)
    reduce_wait(3, 0)
    final_on(0, 1)
    reduce_wait(1, 0)
    for n in (0, 1):
        reduce_wait(0, n)


def per_device_fast(nb, *args):
    (
        inputs,
        starts,
        first_spatial,
        first_mid_gain,
        first_mid_bias,
        first_temporal,
        first_out_gain,
        first_out_bias,
        second_spatial,
        second_mid_gain,
        second_mid_bias,
        second_temporal,
        second_out_gain,
        second_out_bias,
        cotangent,
    ) = args
    micro, frames, side, _, chan = inputs.shape
    mid = first_spatial.shape[1]
    spat, temp = first_spatial.shape[0], first_temporal.shape[0]
    few = frames // 4
    h, w, b = (lax.axis_index(name) for name in ("ha", "wa", "batch"))
    mine = (1 - w) * h + w * (3 - h)
    offsets = jnp.arange(side)
    valid = (h * side + offsets < HGT)[:, None] & (w * side + offsets < HGT)[None, :]

    def tiles(array):
        array = array * valid.astype(BF16)[None, None, :, :, None]
        array = array.reshape(micro, 4, few, side, side, chan).transpose(1, 3, 4, 0, 2, 5)
        return array.reshape(4, side, side * micro * few, chan)

    def untiled(array):
        array = array.reshape(4, side, side, micro, few, chan).transpose(3, 0, 4, 1, 2, 5)
        return array.reshape(micro, frames, side, side, chan).astype(F32)

    gate = (1 - lax.dynamic_slice_in_dim(starts, mine * few, few, axis=1)).astype(F32)
    gate = jnp.broadcast_to(gate.reshape(micro * few, 1), (micro * few, chan))
    here = jnp.where((h == 0) & (w == 0), 1.0, 0.0)

    def placed(shard):
        row = jnp.zeros((mid,), F32)
        return lax.dynamic_update_slice(row, shard.astype(F32) * here, (b * shard.shape[0],))

    param = jnp.stack(
        [
            placed(v)
            for v in (
                first_mid_gain,
                first_mid_bias,
                first_out_gain,
                first_out_bias,
                second_mid_gain,
                second_mid_bias,
                second_out_gain,
                second_out_bias,
            )
        ]
    )
    half = chan // 2
    few_rows = ROWS // 4

    inputs_of = dict(
        x_tiles=(tiles(inputs), pl.ANY),
        cot_tiles=(tiles(cotangent), pl.ANY),
        gate=(gate, pltpu.VMEM),
        param_in=(param, pltpu.VMEM),
        first_spatial=(first_spatial, pl.ANY),
        first_temporal=(first_temporal, pl.ANY),
        second_spatial=(second_spatial, pl.ANY),
        second_temporal=(second_temporal, pl.ANY),
    )
    outputs_of = dict(
        block_out=((4, side, side * CELL, chan), BF16, pl.ANY),
        grad_input=((4, side, side * CELL, chan), BF16, pl.ANY),
        norm_grads=((8, mid), F32, pltpu.VMEM),
        out1s=((spat, mid), BF16, pl.ANY),
        out1t=((2, temp, half), BF16, pl.ANY),
        out2s=((spat, mid), BF16, pl.ANY),
        out2t=((2, temp, half), BF16, pl.ANY),
    )
    dma = pltpu.SemaphoreType.DMA
    scratch_of = dict(
        w1s=pltpu.VMEM((9 * chan, mid), BF16),
        w1t=pltpu.VMEM((3 * mid, chan), BF16),
        w2s=pltpu.VMEM((9 * chan, mid), BF16),
        w2t=pltpu.VMEM((3 * mid, chan), BF16),
        x_grid=pltpu.VMEM((8, 8 * CELL, chan), BF16),
        cot_grid=pltpu.VMEM((8, 8 * CELL, chan), BF16),
        out_grid=pltpu.VMEM((8, 8 * CELL, chan), BF16),
        xa=pltpu.VMEM((PADDED, chan), BF16),
        xb=pltpu.VMEM((PADDED, chan), BF16),
        aa=pltpu.VMEM((PADDED, chan), BF16),
        ab=pltpu.VMEM((PADDED, chan), BF16),
        ea=pltpu.VMEM((PADDED, mid), BF16),
        eb=pltpu.VMEM((PADDED, mid), BF16),
        mid1=pltpu.VMEM((ROWS, mid), F32),
        mid2=pltpu.VMEM((ROWS, mid), F32),
        grad_mid=pltpu.VMEM((ROWS, mid), F32),
        v1=pltpu.VMEM((ROWS, mid), BF16),
        v2=pltpu.VMEM((ROWS, mid), BF16),
        time1=pltpu.VMEM((ROWS, chan), F32),
        time2=pltpu.VMEM((ROWS, chan), F32),
        grad_pre=pltpu.VMEM((ROWS, chan), F32),
        down=pltpu.VMEM((chan // 128, ROWS + CHUNK, 128), F32),
        up=pltpu.VMEM((chan // 128, ROWS + CHUNK, 128), F32),
        e3=pltpu.VMEM((3, ROWS, chan), BF16),
        sib_e3=pltpu.VMEM((3, ROWS, half), BF16),
        halo_out=pltpu.VMEM((2, few_rows, chan), BF16),
        halo_in=pltpu.VMEM((4, 2, few_rows, chan), BF16),
        param=pltpu.VMEM((8, mid), F32),
        tile_mid=pltpu.VMEM((2, 4, CELL, mid), F32),
        tile_out=pltpu.VMEM((2, 4, CELL, chan), F32),
        back=pltpu.VMEM((2, CELL, mid), F32),
        sum_a=pltpu.VMEM((2, 2, 8, mid), F32),
        sum_b=pltpu.VMEM((2, 4, 8, mid), F32),
        sum_c=pltpu.VMEM((2, nb // 2, 8, mid), F32),
        own_sem=dma((4,)),
        ring_send=dma((4, 2, nb)),
        ring_recv=dma((4, 2, nb)),
        sib_send=dma((4, 3, nb)),
        sib_recv=dma((4, 3, nb)),
        over_send=dma((4, nb)),
        over_recv=dma((4, nb)),
        sa_send=dma((9,)),
        sa_recv=dma((9,)),
        sb_send=dma((9, 3)),
        sb_recv=dma((9, 4)),
        sc_send=dma((9, nb // 2)),
        sc_recv=dma((9, nb // 2)),
        halo_send=dma((4, 2)),
        halo_recv=dma((4, 2)),
        share_send=dma((6,)),
        share_recv=dma((6,)),
        e_all=pltpu.VMEM((4 * ROWS, mid), BF16),
        xq1=pltpu.VMEM((3, 2, PADDED, chan // 4), BF16),
        xq2=pltpu.VMEM((3, 2, PADDED, chan // 4), BF16),
        xt=pltpu.VMEM((mid, 2 * ROWS), BF16),
        sib_v=pltpu.VMEM((ROWS, mid), BF16),
        e_send=dma((2, 2, 3)),
        e_recv=dma((2, 2, 3)),
        xq_send=dma((2, 3)),
        xq_recv=dma((2, 3)),
        y_send=dma((4, 2, 5)),
        y_recv=dma((4, 2, 5)),
        z_send=dma((4, 2, 5)),
        z_recv=dma((4, 2, 7)),
        cast_send=dma((4, 2, 6)),
        cast_recv=dma((4, 2, 8)),
        out_sem=dma((4, 2, 2)),
        tile_send=dma((4, 3)),
        tile_recv=dma((4, 4)),
        tile_own=dma((4,)),
    )
    names = (*inputs_of, *outputs_of, *scratch_of)
    cell_count = float(frames * nb * HGT * HGT)
    results = pl.pallas_call(
        functools.partial(block_kernel, (nb, chan, mid, cell_count), names),
        out_shape=[jax.ShapeDtypeStruct(shape, dtype) for shape, dtype, _ in outputs_of.values()],
        in_specs=[pl.BlockSpec(memory_space=space) for _, space in inputs_of.values()],
        out_specs=[pl.BlockSpec(memory_space=space) for _, _, space in outputs_of.values()],
        scratch_shapes=list(scratch_of.values()),
        compiler_params=pltpu.CompilerParams(
            collective_id=0, has_side_effects=True, vmem_limit_bytes=VMEM_LIMIT
        ),
    )(*(array for array, _ in inputs_of.values()))
    got = SimpleNamespace(**dict(zip(outputs_of, results)))

    def temporal(pair):
        return jnp.concatenate([pair[0], pair[1]], axis=1).astype(F32)

    def norm(row, like):
        size = like.shape[0]
        return lax.dynamic_slice_in_dim(got.norm_grads[row], b * size, size)

    return (
        untiled(got.block_out),
        untiled(got.grad_input),
        got.out1s.astype(F32),
        norm(0, first_mid_gain),
        norm(1, first_mid_bias),
        temporal(got.out1t),
        norm(2, first_out_gain),
        norm(3, first_out_bias),
        got.out2s.astype(F32),
        norm(4, second_mid_gain),
        norm(5, second_mid_bias),
        temporal(got.out2t),
        norm(6, second_out_gain),
        norm(7, second_out_bias),
    )


def extended(shard, sides, width):
    for axis, dim in sides:
        count, length = (lax.axis_size(axis), shard.shape[dim])
        up = [(i, (i + 1) % count) for i in range(count - 1)]
        down = [(j, i) for i, j in up]
        last = lax.slice_in_dim(shard, length - width, length, axis=dim)
        leading = lax.slice_in_dim(shard, 0, width, axis=dim)
        before = lax.ppermute(last, axis, up)
        after = lax.ppermute(leading, axis, down)
        shard = jnp.concatenate([before, shard, after], axis=dim)
    return shard


def passed_along(shard, axis, by):
    count = lax.axis_size(axis)
    pairs = [(i, i + by) for i in range(count) if 0 <= i + by < count]
    return lax.ppermute(shard, axis, pairs)


def for_sending(shard):

    def short(part):
        return part.astype(jnp.bfloat16) if part.dtype == jnp.float32 else part

    return jax.tree.map(short, shard)


def silu_slope(values):
    sigma = jax.nn.sigmoid(values)
    return sigma * (1.0 + values * (1.0 - sigma))


def spatial_forward(field_in, kernel):
    frames, tile_side = (field_in.shape[0], field_in.shape[1])
    padded = extended(field_in, (("ha", 1), ("wa", 2)), 1)
    pieces = [
        padded[:, offset // 3 : offset // 3 + tile_side, offset % 3 : offset % 3 + tile_side, :]
        for offset in range(9)
    ]
    patches = jnp.concatenate(pieces, axis=-1).reshape(frames * tile_side * tile_side, -1)
    return (patches, jnp.dot(patches, kernel, preferred_element_type=jnp.float32))


def spatial_backward(grad_out, patches, kernel):
    frames, tile_side, channels = (grad_out.shape[0], grad_out.shape[1], grad_out.shape[3])
    row_count = frames * tile_side * tile_side
    padded = extended(grad_out, (("ha", 1), ("wa", 2)), 1)
    pieces = [
        padded[
            :,
            2 - offset // 3 : 2 - offset // 3 + tile_side,
            2 - offset % 3 : 2 - offset % 3 + tile_side,
            :,
        ]
        for offset in range(9)
    ]
    stacked = jnp.concatenate(pieces, axis=-1).reshape(row_count, 9, channels)
    grad_in = jnp.einsum(
        "rkm,kcm->rc", stacked, kernel.reshape(9, -1, channels), preferred_element_type=jnp.float32
    )
    grad_kernel = jnp.einsum(
        "rk,rm->km",
        patches,
        grad_out.reshape(row_count, channels),
        preferred_element_type=jnp.float32,
    )
    return (grad_in, grad_kernel)


def temporal_forward(field_in, clip_gate, kernel):
    frames, tile_side = (field_in.shape[0], field_in.shape[1])
    gated_in = field_in * clip_gate
    earlier = passed_along(field_in[-1:], "batch", 1)
    later_frame = passed_along(gated_in[:1], "batch", -1)
    before = jnp.concatenate([earlier, field_in[:-1]], axis=0) * clip_gate
    after_tap = jnp.concatenate([gated_in[1:], later_frame], axis=0)
    joined = jnp.concatenate([before, field_in, after_tap], axis=-1).reshape(
        frames * tile_side * tile_side, -1
    )
    return (joined, jnp.dot(joined, kernel, preferred_element_type=jnp.float32))


def temporal_backward(grad_out, joined, clip_gate, kernel):
    frames, tile_side, channels = (grad_out.shape[0], grad_out.shape[1], grad_out.shape[3])
    row_count = frames * tile_side * tile_side
    gated_grad = grad_out * clip_gate
    later_frame = passed_along(gated_grad[:1], "batch", -1)
    earlier = passed_along(grad_out[-1:], "batch", 1)
    from_later = jnp.concatenate([gated_grad[1:], later_frame], axis=0)
    from_earlier = jnp.concatenate([earlier, grad_out[:-1]], axis=0) * clip_gate
    stacked = jnp.concatenate([from_later, grad_out, from_earlier], axis=-1).reshape(
        row_count, 3, channels
    )
    grad_in = jnp.einsum(
        "rkc,kmc->rm", stacked, kernel.reshape(3, -1, channels), preferred_element_type=jnp.float32
    )
    grad_kernel = jnp.einsum(
        "rk,rc->kc",
        joined,
        grad_out.reshape(row_count, channels),
        preferred_element_type=jnp.float32,
    )
    return (grad_in, grad_kernel)


def norm_forward(pre_norm, norm_gain, norm_bias, valid_rows, cell_count):
    first_sum = jnp.sum(pre_norm * valid_rows, axis=0)
    square_sum = jnp.sum(pre_norm * pre_norm * valid_rows, axis=0)
    first_sum, square_sum = lax.psum((first_sum, square_sum), ("ha", "wa", "batch"))
    mean_val = first_sum / cell_count
    inv_std = lax.rsqrt(square_sum / cell_count - mean_val * mean_val + epsilon)
    normed = (pre_norm - mean_val) * inv_std
    return (normed, inv_std, normed * norm_gain.astype(jnp.float32) + norm_bias.astype(jnp.float32))


def norm_backward(grad_norm, normed, inv_std, norm_gain, valid_rows, cell_count):
    bias_grad = jnp.sum(grad_norm, axis=0)
    gain_grad = jnp.sum(grad_norm * normed, axis=0)
    bias_grad, gain_grad = lax.psum((bias_grad, gain_grad), ("ha", "wa", "batch"))
    grad_in = (
        valid_rows
        * norm_gain.astype(jnp.float32)
        * inv_std
        * (grad_norm - bias_grad / cell_count - normed * gain_grad / cell_count)
    )
    return (grad_in, gain_grad, bias_grad)


def forward_pair(field_in, weights, clip_gate, valid_rows, cell_count):
    frames, tile_side = (field_in.shape[0], field_in.shape[1])
    patches, spatial_out = spatial_forward(field_in, weights[0])
    mid_hat, mid_scale, mid_norm = norm_forward(
        spatial_out, weights[1], weights[2], valid_rows, cell_count
    )
    hidden = (
        (jax.nn.silu(mid_norm) * valid_rows)
        .astype(jnp.bfloat16)
        .reshape(frames, tile_side, tile_side, -1)
    )
    joined, temporal_out = temporal_forward(hidden, clip_gate, weights[3])
    out_hat, out_scale, out_norm = norm_forward(
        temporal_out, weights[4], weights[5], valid_rows, cell_count
    )
    return ((patches, mid_hat, mid_scale, mid_norm, joined, out_hat, out_scale), out_norm)


def backward_pair(grad_norm, kept, weights, clip_gate, valid_rows, cell_count, tile_side):
    patches, mid_hat, mid_scale, mid_norm, joined, out_hat, out_scale = kept
    frames = clip_gate.shape[0]
    grad_time, out_gain_grad, out_bias_grad = norm_backward(
        grad_norm, out_hat, out_scale, weights[4], valid_rows, cell_count
    )
    grad_time = grad_time.astype(jnp.bfloat16).reshape(frames, tile_side, tile_side, -1)
    grad_hidden, temporal_grad = temporal_backward(grad_time, joined, clip_gate, weights[3])
    grad_mid = grad_hidden * valid_rows * silu_slope(mid_norm)
    grad_spatial, mid_gain_grad, mid_bias_grad = norm_backward(
        grad_mid, mid_hat, mid_scale, weights[1], valid_rows, cell_count
    )
    grad_spatial = grad_spatial.astype(jnp.bfloat16).reshape(frames, tile_side, tile_side, -1)
    grad_in, spatial_grad = spatial_backward(grad_spatial, patches, weights[0])
    return (
        grad_in,
        (spatial_grad, mid_gain_grad, mid_bias_grad, temporal_grad, out_gain_grad, out_bias_grad),
    )


def per_device(
    inputs,
    starts,
    first_spatial,
    first_mid_gain,
    first_mid_bias,
    first_temporal,
    first_out_gain,
    first_out_bias,
    second_spatial,
    second_mid_gain,
    second_mid_bias,
    second_temporal,
    second_out_gain,
    second_out_bias,
    cotangent,
):
    shards = (
        first_spatial,
        first_mid_gain,
        first_mid_bias,
        first_temporal,
        first_out_gain,
        first_out_bias,
        second_spatial,
        second_mid_gain,
        second_mid_bias,
        second_temporal,
        second_out_gain,
        second_out_bias,
    )
    micro_total, frames, tile_side, channels = (
        inputs.shape[0],
        inputs.shape[1],
        inputs.shape[2],
        inputs.shape[4],
    )
    row_count = frames * tile_side * tile_side
    cell_count = frames * lax.axis_size("batch") * HGT * HGT
    offsets = jnp.arange(tile_side)
    inside_h = lax.axis_index("ha") * tile_side + offsets < HGT
    inside_w = lax.axis_index("wa") * tile_side + offsets < HGT
    valid_grid = inside_h[:, None] & inside_w[None, :]
    valid_tile = valid_grid.astype(jnp.bfloat16)[None, :, :, None]
    valid_rows = jnp.broadcast_to(
        valid_grid.astype(jnp.float32)[None], (frames, tile_side, tile_side)
    ).reshape(row_count, 1)
    results = []
    input_grads = []
    kernel_total = None
    norm_total = None
    for micro_step in range(micro_total):
        gathered = (
            lax.all_gather(shards[0], "batch", axis=0, tiled=True),
            lax.all_gather(shards[1], "batch", axis=0, tiled=True),
            lax.all_gather(shards[2], "batch", axis=0, tiled=True),
            lax.all_gather(shards[3], "batch", axis=0, tiled=True),
            lax.all_gather(shards[4], "batch", axis=0, tiled=True),
            lax.all_gather(shards[5], "batch", axis=0, tiled=True),
            lax.all_gather(shards[6], "batch", axis=0, tiled=True),
            lax.all_gather(shards[7], "batch", axis=0, tiled=True),
            lax.all_gather(shards[8], "batch", axis=0, tiled=True),
            lax.all_gather(shards[9], "batch", axis=0, tiled=True),
            lax.all_gather(shards[10], "batch", axis=0, tiled=True),
            lax.all_gather(shards[11], "batch", axis=0, tiled=True),
        )
        clip_gate = (1 - starts[micro_step]).astype(jnp.bfloat16).reshape(frames, 1, 1, 1)
        x_in = inputs[micro_step] * valid_tile
        first_kept, first_norm = forward_pair(
            x_in, gathered[0:6], clip_gate, valid_rows, cell_count
        )
        first_act = (
            (jax.nn.silu(first_norm) * valid_rows)
            .astype(jnp.bfloat16)
            .reshape(frames, tile_side, tile_side, channels)
        )
        second_kept, second_norm = forward_pair(
            first_act, gathered[6:12], clip_gate, valid_rows, cell_count
        )
        pre_out = second_norm + x_in.reshape(row_count, channels).astype(jnp.float32)
        results.append(
            (jax.nn.silu(pre_out) * valid_rows).reshape(frames, tile_side, tile_side, channels)
        )
        grad_pre = (
            cotangent[micro_step].reshape(row_count, channels).astype(jnp.float32)
            * valid_rows
            * silu_slope(pre_out)
        )
        grad_act, second_grads = backward_pair(
            grad_pre, second_kept, gathered[6:12], clip_gate, valid_rows, cell_count, tile_side
        )
        grad_first = grad_act * valid_rows * silu_slope(first_norm)
        grad_conv, first_grads = backward_pair(
            grad_first, first_kept, gathered[0:6], clip_gate, valid_rows, cell_count, tile_side
        )
        input_grads.append(
            ((grad_conv + grad_pre) * valid_rows).reshape(frames, tile_side, tile_side, channels)
        )
        step_grads = first_grads + second_grads
        kernel_now = (step_grads[0], step_grads[3], step_grads[6], step_grads[9])
        norm_now = (
            step_grads[1],
            step_grads[2],
            step_grads[4],
            step_grads[5],
            step_grads[7],
            step_grads[8],
            step_grads[10],
            step_grads[11],
        )
        if micro_step == 0:
            kernel_total = kernel_now
            norm_total = norm_now
        else:
            kernel_total = jax.tree.map(jnp.add, kernel_total, kernel_now)
            norm_total = jax.tree.map(jnp.add, norm_total, norm_now)
    kernel_total = lax.psum_scatter(kernel_total, "batch", scatter_dimension=0, tiled=True)
    kernel_total = jax.tree.map(
        lambda part: part.astype(jnp.float32), lax.psum(for_sending(kernel_total), ("ha", "wa"))
    )
    shard_index = lax.axis_index("batch")
    batch_count = lax.axis_size("batch")
    norm_shards = tuple(
        (
            lax.dynamic_slice_in_dim(
                full_sum,
                shard_index * (full_sum.shape[0] // batch_count),
                full_sum.shape[0] // batch_count,
            )
            for full_sum in norm_total
        )
    )
    return (
        jnp.stack(results),
        jnp.stack(input_grads),
        kernel_total[0],
        norm_shards[0],
        norm_shards[1],
        kernel_total[1],
        norm_shards[2],
        norm_shards[3],
        kernel_total[2],
        norm_shards[4],
        norm_shards[5],
        kernel_total[3],
        norm_shards[6],
        norm_shards[7],
    )


def solution(mesh):
    in_specs = (
        P(None, "batch", "ha", "wa", None),
        P(None, "batch"),
        P("batch", None),
        P("batch"),
        P("batch"),
        P("batch", None),
        P("batch"),
        P("batch"),
        P("batch", None),
        P("batch"),
        P("batch"),
        P("batch", None),
        P("batch"),
        P("batch"),
        P(None, "batch", "ha", "wa", None),
    )
    out_specs = (
        P(None, "batch", "ha", "wa", None),
        P(None, "batch", "ha", "wa", None),
        P("batch", None),
        P("batch"),
        P("batch"),
        P("batch", None),
        P("batch"),
        P("batch"),
        P("batch", None),
        P("batch"),
        P("batch"),
        P("batch", None),
        P("batch"),
        P("batch"),
    )
    batch = mesh.shape["batch"]

    def program(*args):
        spat, temp = args[2].shape[0], args[5].shape[0]
        fits = args[0].shape == (2, 16, 4, 4, 512) and args[2].shape[1] == 1152
        if fits and batch == 8 and spat * batch == 9 * 512 and temp * batch == 3 * 1152:
            return per_device_fast(batch, *args)
        return per_device(*args)

    return jax.shard_map(
        program, mesh=mesh, in_specs=in_specs, out_specs=out_specs, check_vma=False
    )
```

```python
import functools
from types import SimpleNamespace

import jax
import jax.numpy as jnp
from jax import lax
from jax.experimental import pallas as pl
from jax.experimental.pallas import tpu as pltpu
from jax.sharding import PartitionSpec as P

HGT = 7
epsilon = 1e-05
MESH = pl.DeviceIdType.MESH
F32 = jnp.float32
BF16 = jnp.bfloat16

BASE = 10
CELL = 8
ROWS = HGT * 8 * CELL
PADDED = (BASE + HGT * 8 + BASE) * CELL
MAIN = BASE * CELL
CHUNK = 2 * CELL
CHUNKS = ROWS // CHUNK
VMEM_LIMIT = 64 * 1024 * 1024 - 1024 * 1024


def when(cond, work):
    if cond is True:
        work()
    elif cond is not False:
        pl.when(cond)(work)


def loop(count, body, init):
    def twice(i, carry):
        return body(2 * i + 1, body(2 * i, carry))

    return lax.fori_loop(0, count // 2, twice, init)


def sigmoid(x):
    return 0.5 * jnp.tanh(0.5 * x) + 0.5


def nn(a, b):
    return jnp.dot(a, b, preferred_element_type=F32)


def nt(a, b):
    return lax.dot_general(a, b, (((1,), (1,)), ((), ())), preferred_element_type=F32)


def tn(a, b):
    return lax.dot_general(a, b, (((0,), (0,)), ((), ())), preferred_element_type=F32)


def rows_of(start, size, step=16):
    if not isinstance(start, int):
        start = pl.multiple_of(start, step)
    return pl.ds(start, size)


def per_batch(first, second, width):
    return jnp.concatenate(
        [jnp.broadcast_to(first, (CELL // 2, width)), jnp.broadcast_to(second, (CELL // 2, width))], axis=0
    )


def block_kernel(dims, names, *all_refs):
    r = SimpleNamespace(**dict(zip(names, all_refs, strict=True)))
    nb, chan, mid, cell_count = dims
    spat = 9 * chan // nb
    temp = 3 * mid // nb
    unit = spat // 6
    quarter = chan // 4
    half = chan // 2
    h = lax.axis_index("ha")
    w = lax.axis_index("wa")
    b = lax.axis_index("batch")
    par = lax.rem(b, 2)
    bh = lax.div(b, 2)
    pos = par * (nb - 1 - bh) + (1 - par) * bh
    ways = (1 - 2 * h, 2 * h - 1)

    def at(p):
        p = lax.rem(p + 4 * nb, nb)
        upper = lax.div(p, nb // 2)
        return (1 - upper) * (2 * p) + upper * (2 * (nb - 1 - p) + 1)

    def at_group(j):
        jw = lax.div(j, 2)
        odd = lax.rem(j, 2)
        return (odd * (1 - jw) + (1 - odd) * jw, jw)

    mine = (1 - w) * h + w * (3 - h)
    sibling = (1 - h, w, b)
    beside = (h, 1 - w, b)
    onward = [(h, w, at(pos + way)) for way in ways]
    later = lax.rem(mine + 1, 4)
    earlier = lax.rem(mine + 3, 4)
    later_dev = (*at_group(later), lax.rem(b + lax.div(mine + 1, 4), nb))
    earlier_dev = (*at_group(earlier), lax.rem(b + nb - lax.div(4 - mine, 4), nb))
    tile_group = [(lax.rem(mine + d, 4), (*at_group(lax.rem(mine + d, 4)), b)) for d in (1, 2, 3)]
    pos_b = w * 2 + par
    plane = []
    for d in (1, 2, 3):
        q = lax.rem(pos_b + d, 4)
        plane.append((q, (h, lax.div(q, 2), b - par + lax.rem(q, 2))))
    depth = nb // 2
    line = []
    for d in range(1, depth):
        q = lax.rem(bh + d, depth)
        line.append((q, (h, w, 2 * q + par)))

    def named(dev):
        return dict(ha=dev[0], wa=dev[1], batch=dev[2])

    def rc(src, dst, send, recv, dev):
        return pltpu.make_async_remote_copy(
            src_ref=src, dst_ref=dst, send_sem=send, recv_sem=recv, device_id=named(dev), device_id_type=MESH
        )

    def lc(src, dst, sem):
        return pltpu.make_async_copy(src, dst, sem)

    partners = [sibling, beside, *onward, later_dev, earlier_dev]
    partners += [dev for _, dev in tile_group + plane + line]
    barrier = pltpu.get_barrier_semaphore()
    for dev in partners:
        pl.semaphore_signal(barrier, inc=1, device_id=named(dev), device_id_type=MESH)
    pl.semaphore_wait(barrier, len(partners))

    shards = (r.first_spatial, r.first_temporal, r.second_spatial, r.second_temporal)
    whole = (r.w1s, r.w1t, r.w2s, r.w2t)
    shared = 2 * w + h
    shared_beside = 2 * (1 - w) + h
    third = temp // 3

    def units(i, core, side):
        return (2 * side + core, 4 + core) if i % 2 == 0 else ((1 - core) * side + 2 * core,)

    def piece(i, ref, owner, u):
        if i % 2 == 0:
            return ref.at[rows_of(owner * spat + u * unit, unit), :]
        return ref.at[rows_of(owner * temp + u * third, third), :]

    def streams(i):
        return (0, 1) if i % 2 == 0 else (0,)

    def crossing(i, work):
        if i % 2 == 0:
            work()
        else:
            pl.when(h == 0)(work)

    def crossed(i, work):
        if i % 2 == 0:
            work()
        else:
            pl.when(h == 1)(work)

    def own_copy(i):
        rows = spat if i % 2 == 0 else temp
        return lc(shards[i], whole[i].at[rows_of(b * rows, rows), :], r.own_sem.at[i])

    def ring(i, st, s, owner, from_shard=False):
        u = units(i, h, w)[st]
        dst = piece(i, whole[i], owner, u)
        src = piece(i, shards[i], 0, u) if from_shard else dst
        return rc(src, dst, r.ring_send.at[i, st, s], r.ring_recv.at[i, st, s], onward[st])

    def cross(i, kind, s, owner, u):
        part = piece(i, whole[i], owner, u)
        return rc(part, part, r.sib_send.at[i, kind, s], r.sib_recv.at[i, kind, s], sibling)

    def over(i, s, owner, u):
        part = piece(i, whole[i], owner, u)
        return rc(part, part, r.over_send.at[i, s], r.over_recv.at[i, s], beside)

    def gather_start(i):
        for st in streams(i):
            ring(i, st, 1, b, True).start()
        own_copy(i).start()

    def gather_relay(i, s):
        owner = at(pos - ways[0] * s)

        def work():
            over(i, s, owner, units(i, h, 1 - w)[0]).wait_recv()
            cross(i, 2, s, owner, units(i, h, 1 - w)[0]).start()

        crossing(i, work)

    def gather_pump(i, s):
        own = units(i, h, w)
        for st in streams(i):
            owner = at(pos - ways[st] * s)
            ring(i, st, s, owner).wait_recv()
            if isinstance(s, int):
                if s < nb - 1:
                    ring(i, st, s + 1, owner).start()
            else:
                pl.when(s < nb - 1)(lambda st=st, owner=owner: ring(i, st, s + 1, owner).start())
            if st == 0:
                crossing(i, lambda owner=owner: over(i, s, owner, own[0]).start())
            cross(i, st, s, owner, own[st]).start()
        if isinstance(s, int):
            if s > 1:
                gather_relay(i, s - 1)
        else:
            pl.when(s > 1)(lambda: gather_relay(i, s - 1))

    def gather_finish(i):
        gather_relay(i, nb - 1)

        def body(s, _):
            for st in streams(i):
                cross(i, st, s, at(pos + ways[st] * s), units(i, 1 - h, w)[st]).wait_recv()
            theirs = at(pos + ways[0] * s)
            crossed(i, lambda: cross(i, 2, s, theirs, units(i, 1 - h, 1 - w)[0]).wait_recv())
            return 0

        lax.fori_loop(1, nb, body, 0)
        own_copy(i).wait()

    def gather_sent(i):
        def body(s, _):
            for st in streams(i):
                owner = at(pos - ways[st] * s)
                ring(i, st, s, owner).wait_send()
                cross(i, st, s, owner, units(i, h, w)[st]).wait_send()

            def sent():
                owner = at(pos - ways[0] * s)
                over(i, s, owner, units(i, h, w)[0]).wait_send()
                cross(i, 2, s, owner, units(i, h, 1 - w)[0]).wait_send()

            crossing(i, sent)
            return 0

        lax.fori_loop(1, nb, body, 0)

    def total(k, width, value, works=()):
        slot = k % 2
        wide = value.shape[1]
        cols = pl.ds(0, wide)
        works = list(works) + [None] * 3
        pair, four, far = r.sum_a, r.sum_b, r.sum_c
        pair[slot, h, :, cols] = value
        part = pair.at[slot, h, :, cols]
        send_a = rc(part, part, r.sa_send.at[k], r.sa_recv.at[k], sibling)
        send_a.start()
        if works[0]:
            works[0]()
        part = pair.at[slot, 1 - h, :, cols]
        rc(part, part, r.sa_send.at[k], r.sa_recv.at[k], sibling).wait_recv()
        four[slot, pos_b, :, cols] = pair[slot, 0, :, cols] + pair[slot, 1, :, cols]
        sends = [send_a]
        for n, (q, dev) in enumerate(plane):
            part = four.at[slot, pos_b, :, cols]
            sends.append(rc(part, part, r.sb_send.at[k, n], r.sb_recv.at[k, pos_b], dev))
            sends[-1].start()
        if works[1]:
            works[1]()
        for n, (q, dev) in enumerate(plane):
            part = four.at[slot, q, :, cols]
            rc(part, part, r.sb_send.at[k, n], r.sb_recv.at[k, q], dev).wait_recv()
        far[slot, bh, :, cols] = (four[slot, 0, :, cols] + four[slot, 1, :, cols]) + (
            four[slot, 2, :, cols] + four[slot, 3, :, cols]
        )
        for n, (q, dev) in enumerate(line):
            part = far.at[slot, bh, :, cols]
            sends.append(rc(part, part, r.sc_send.at[k, n], r.sc_recv.at[k, bh], dev))
            sends[-1].start()
        if works[2]:
            works[2]()
        for n, (q, dev) in enumerate(line):
            part = far.at[slot, q, :, cols]
            rc(part, part, r.sc_send.at[k, n], r.sc_recv.at[k, q], dev).wait_recv()
        result = far[slot, 0, :, cols]
        for q in range(1, depth):
            result = result + far[slot, q, :, cols]
        for send in sends:
            send.wait_send()
        if wide == width:
            return result
        return jnp.concatenate([result[0:4], result[4:8, 2 * wide - width :]], axis=1)

    def chunk(ref, i, base=0, width=None):
        cols = slice(None) if width is None else pl.ds(0, width)
        value = ref[rows_of(base + i * CHUNK, CHUNK), cols]
        return value.astype(F32).reshape(2, CELL, value.shape[-1])

    def put(ref, i, value, base=0, width=None):
        cols = slice(None) if width is None else pl.ds(0, width)
        ref[rows_of(base + i * CHUNK, CHUNK), cols] = value.reshape(CHUNK, value.shape[-1]).astype(ref.dtype)

    def keep(i):
        inside = jnp.where(lax.rem(i, 4) == 3, 0.0, 1.0).astype(F32)
        first = lax.broadcasted_iota(jnp.int32, (2, 1, 1), 0) == 0
        return jnp.where(first, 1.0, inside)

    def packed(one, two, width):
        rows = [
            jnp.sum(v[k : k + CELL // 2], axis=0, keepdims=True) for v in (one, two) for k in (0, CELL // 2)
        ]
        rows = jnp.concatenate(rows, axis=0)
        wide = -(-width // 256) * 128
        return jnp.concatenate([rows[:, 0:wide], rows[:, width - wide :]], axis=0)

    def moments(ref, width):
        def body(i, carry):
            v = chunk(ref, i)
            m = v * keep(i)
            return (carry[0] + m[0] + m[1], carry[1] + m[0] * v[0] + m[1] * v[1])

        zero = jnp.zeros((CELL, width), F32)
        return loop(CHUNKS, body, (zero, zero))

    def prepare(n, sums, width):
        tile = r.tile_mid if width == mid else r.tile_out
        n2 = n // 2
        gain = r.param[2 * n : 2 * n + 1, 0:width]
        bias = r.param[2 * n + 1 : 2 * n + 2, 0:width]
        mean = sums[0:2] / cell_count
        inv = lax.rsqrt(sums[2:4] / cell_count - mean * mean + epsilon)
        scale = inv * gain
        shift = bias - mean * scale
        for k, v in enumerate((scale, shift, inv, mean * inv)):
            tile[n2, k] = per_batch(v[0:1], v[1:2], width)

    def tiles(n, width):
        tile = r.tile_mid if width == mid else r.tile_out
        return [tile[n // 2, k][None] for k in range(4)]

    def fill(ref_a, ref_b, value_of, width):
        pads(ref_a, ref_b, width)

        def body(i, before):
            v = value_of(i)
            put(ref_a, i, v, MAIN)
            pair = jnp.concatenate([before[None], v[0:1]], axis=0)
            put(ref_b, i, pair, MAIN - CHUNK)
            return v[1]

        loop(CHUNKS, body, jnp.zeros((CELL, width), F32))

    def activated(src, n, width):
        def value(i):
            scale, shift, _, _ = tiles(n, width)
            y = chunk(src, i) * scale + shift
            return y * sigmoid(y) * keep(i)

        return value

    def taps(ref_a, ref_b, k, size=ROWS):
        r0 = MAIN - 8 * CELL + 8 * CELL * k
        return (
            ref_b[rows_of(r0 - CHUNK, size), :],
            ref_a[rows_of(r0, size), :],
            ref_b[rows_of(r0, size), :],
        )

    def conv(ref_a, ref_b, weight, out, pump=None):
        for n, (c0, cw) in enumerate(((0, 512), (512, mid - 512))):

            def body(a, _, c0=c0, cw=cw, n=n):
                x = taps(ref_a, ref_b, a)
                acc = nn(jnp.concatenate(x, axis=1), weight[rows_of(a * 3 * chan, 3 * chan), c0 : c0 + cw])

                @pl.when(a == 0)
                def _():
                    out[:, c0 : c0 + cw] = acc

                @pl.when(a > 0)
                def _():
                    out[:, c0 : c0 + cw] += acc

                if pump is not None:
                    pump(n * 3 + a)
                return 0

            lax.fori_loop(0, 3, body, 0)

    def conv_back(ref_a, ref_b, weight, out, pump=None):
        def body(k, _):
            e = taps(ref_a, ref_b, k)
            acc = None
            for j in range(3):
                tap = 8 - 3 * k - j
                term = nt(e[j], weight[rows_of(tap * chan, chan), :])
                acc = term if acc is None else acc + term

            @pl.when(k == 0)
            def _():
                out[:, 0:chan] = acc

            @pl.when(k > 0)
            def _():
                out[:, 0:chan] += acc

            if pump is not None:
                pump(k)
            return 0

        lax.fori_loop(0, 3, body, 0)

    def send_frames(k):
        down, up = r.down, r.up
        count = ROWS // 4
        for c in range(chan // 128):
            lanes = pl.ds(128 * c, 128)
            r.halo_out[0, :, lanes] = down[c, pl.ds(CELL + 3, count, stride=4), :].astype(BF16)
            r.halo_out[1, :, lanes] = up[c, pl.ds(0, count, stride=4), :].astype(BF16)
        copies = []
        for n, dev in ((0, later_dev), (1, earlier_dev)):
            copies.append(
                rc(r.halo_out.at[n], r.halo_in.at[k, n], r.halo_send.at[k, n], r.halo_recv.at[k, n], dev)
            )
            copies[-1].start()
        return copies

    def take_frames(k, copies):
        down, up = r.down, r.up
        count = ROWS // 4
        for copy in copies:
            copy.wait()
        at_start = jnp.logical_and(mine == 0, b == 0)
        at_end = jnp.logical_and(mine == 3, b == nb - 1)
        for c in range(chan // 128):
            lanes = pl.ds(128 * c, 128)
            before = r.halo_in[k, 0, :, lanes].astype(F32)
            after = r.halo_in[k, 1, :, lanes].astype(F32)
            down[c, pl.ds(CELL - 1, count, stride=4), :] = jnp.where(at_start, 0.0, before)
            up[c, pl.ds(4, count, stride=4), :] = jnp.where(at_end, 0.0, after)

    def by_lanes(ref, rows):
        return jnp.concatenate([ref[c, rows, :] for c in range(chan // 128)], axis=1)

    def put_lanes(ref, rows, value):
        for c in range(chan // 128):
            ref[c, rows, :] = value[:, 128 * c : 128 * c + 128]

    def shifted(i):
        before = by_lanes(r.down, rows_of(i * CHUNK, CHUNK + CELL))[CELL - 1 : CELL - 1 + CHUNK]
        after = by_lanes(r.up, rows_of(i * CHUNK, CHUNK + CELL))[1 : 1 + CHUNK]
        gate = r.gate[...][None]
        return (before.reshape(2, CELL, chan) * gate, after.reshape(2, CELL, chan))

    def temporal(k, v, weight, out, works=()):
        works = list(works) + [None] * 2
        put_lanes(r.down, pl.ds(CELL, ROWS), nn(v[...], weight[0:mid, :]))
        y2 = nn(v[...], weight[2 * mid : 3 * mid, :])
        y2 = (y2.reshape(ROWS // CELL, CELL, chan) * r.gate[...][None]).reshape(ROWS, chan)
        put_lanes(r.up, pl.ds(0, ROWS), y2)
        copies = send_frames(k)
        out[...] = nn(v[...], weight[mid : 2 * mid, :])
        if works[0]:
            works[0]()
        take_frames(k, copies)

        def body(i, carry):
            before, after = shifted(i)
            value = chunk(out, i) + before + after
            put(out, i, value)
            m = value * keep(i)
            return (carry[0] + m[0] + m[1], carry[1] + m[0] * value[0] + m[1] * value[1])

        zero = jnp.zeros((CELL, chan), F32)
        return loop(CHUNKS, body, (zero, zero))

    def temporal_back(k, weight, works=()):
        works = list(works) + [None] * 2
        copies = send_frames(k)
        e3 = r.e3
        for c0, cw in ((0, 512), (512, mid - 512)):
            r.grad_mid[:, c0 : c0 + cw] = nt(e3[1], weight[mid + c0 : mid + c0 + cw, :])
        if works[0]:
            works[0]()
        take_frames(k, copies)

        def body(i, _):
            before, after = shifted(i)
            e3[0, rows_of(i * CHUNK, CHUNK), :] = after.reshape(CHUNK, chan).astype(BF16)
            e3[2, rows_of(i * CHUNK, CHUNK), :] = before.reshape(CHUNK, chan).astype(BF16)
            return 0

        loop(CHUNKS, body, 0)
        share = share_e3(k)
        for c0, cw in ((0, 512), (512, mid - 512)):
            r.grad_mid[:, c0 : c0 + cw] += nt(e3[0], weight[c0 : c0 + cw, :]) + nt(
                e3[2], weight[2 * mid + c0 : 2 * mid + c0 + cw, :]
            )
        return share

    def share(k, src, dst):
        copy = rc(src, dst, r.share_send.at[k], r.share_recv.at[k], sibling)
        copy.start()
        return copy

    outs = (r.out1s, r.out1t, r.out2s, r.out2t)

    halves = ((0, 512), (512, mid - 512))

    def e_part(n, slot):
        c0, cw = halves[n]
        return r.e_all.at[slot * ROWS : (slot + 1) * ROWS, c0 : c0 + cw]

    def e_copies(k, n):
        sems = [(r.e_send.at[k, n, m], r.e_recv.at[k, n, m]) for m in range(3)]
        return [
            rc(e_part(n, 0), e_part(n, 1), *sems[0], sibling),
            rc(e_part(n, 0), e_part(n, 2), *sems[1], beside),
            rc(e_part(n, 2), e_part(n, 3), *sems[2], sibling),
        ]

    def share_e(k, n):
        near, over, _ = e_copies(k, n)
        over.start()
        near.start()

    def share_e_on(k, n):
        _, over, far = e_copies(k, n)
        over.wait_recv()
        far.start()

    def share_e_wait(k, n):
        near, over, far = e_copies(k, n)
        near.wait()
        over.wait_send()
        far.wait()

    def share_x(k, xa, xq):
        copies = []
        for n, dev in enumerate((sibling, beside, (1 - h, 1 - w, b))):
            lanes = rows_of((2 * dev[1] + dev[0]) * quarter, quarter, 128)
            main = pl.ds(MAIN, ROWS)
            copies.append(
                rc(xa.at[main, lanes], xq.at[n, 0, main, :], r.xq_send.at[k, n], r.xq_recv.at[k, n], dev)
            )
            copies[-1].start()
        return copies

    def pads(ref_a, ref_b, width):
        ref_a[0:MAIN, :] = jnp.zeros((MAIN, width), BF16)
        ref_a[MAIN + ROWS : PADDED, :] = jnp.zeros((PADDED - MAIN - ROWS, width), BF16)
        ref_b[0 : MAIN - CHUNK, :] = jnp.zeros((MAIN - CHUNK, width), BF16)
        ref_b[MAIN - CHUNK + ROWS : PADDED, :] = jnp.zeros((PADDED - MAIN + CHUNK - ROWS, width), BF16)

    def spread_x(xq):
        for n in range(3):
            pads(xq.at[n, 0], xq.at[n, 1], quarter)

        def body(i, before):
            after = []
            for n in range(3):
                v = chunk(xq.at[n, 0], i, MAIN)
                put(xq.at[n, 1], i, jnp.concatenate([before[n][None], v[0:1]], axis=0), MAIN - CHUNK)
                after.append(v[1])
            return tuple(after)

        loop(CHUNKS, body, (jnp.zeros((CELL, quarter), F32),) * 3)

    def share_e3(k):
        return share(
            k - 2, r.e3.at[:, :, rows_of((1 - h) * half, half, 128)], r.sib_e3
        )

    def grad_tap(owner):
        return owner + jnp.where(owner > 2 * shared, 1, 0)

    spare = r.w2s

    def gq(i, row, size):
        return rows_of((mid if i == 0 else 0) + row, size)

    def inbox(i, row, size):
        return rows_of(2 * mid + (mid if i == 0 else 0) + row, size)

    def transpose_x(a, xa, xb, xq, near, far, row):
        lanes = rows_of(shared * quarter, quarter, 128)
        r0 = MAIN - 8 * CELL + 8 * CELL * a
        for j, (c, start) in enumerate(((1, r0 - CHUNK), (0, r0), (1, r0))):
            rows = rows_of(start, ROWS)
            own = (xb if c else xa)[rows, lanes]
            both = jnp.concatenate([own, xq[0, c, rows, :]], axis=0)
            near[rows_of(row + j * quarter, quarter), 0 : 2 * ROWS] = both.T
            both = jnp.concatenate([xq[1, c, rows, :], xq[2, c, rows, :]], axis=0)
            far[rows_of(row + j * quarter, quarter), 0 : 2 * ROWS] = both.T

    def spatial_part(i, near, far, row, out_row, n):
        c0, cw = halves[n]
        rows = rows_of(row, 3 * quarter)
        acc = nn(near[rows, 0 : 2 * ROWS], r.e_all[0 : 2 * ROWS, c0 : c0 + cw])
        acc += nn(far[rows, 0 : 2 * ROWS], r.e_all[2 * ROWS : 4 * ROWS, c0 : c0 + cw])
        spare[gq(i, out_row, 3 * quarter), c0 : c0 + cw] = acc.astype(BF16)

    def transposes(xa, xb, xq, near, far):
        def body(a, _):
            transpose_x(a, xa, xb, xq, near, far, a * 3 * quarter)
            return 0

        lax.fori_loop(0, 3, body, 0)

    def spatial_half(i, near, far, n):
        def body(a, _):
            spatial_part(i, near, far, a * 3 * quarter, a * 3 * quarter, n)
            return 0

        lax.fori_loop(0, 3, body, 0)

    def transpose_v(v, sv):
        for c in range(mid // 128):
            lanes = pl.ds(128 * c, 128)
            r.xt[128 * c : 128 * c + 128, :] = jnp.concatenate([v[:, lanes], sv[:, lanes]], axis=0).T

    def temporal_grad(i, k):
        e = jnp.concatenate([r.e3[k, :, rows_of(h * half, half, 128)], r.sib_e3[k]], axis=0)
        whole[i][k * mid : (k + 1) * mid, 0:half] = nn(r.xt[...], e).astype(BF16)

    def cols_of(n):
        c0, cw = halves[n]
        return pl.ds(c0, cw)

    def s_block(i, n, owner):
        return spare.at[gq(i, grad_tap(owner) * quarter, quarter), cols_of(n)]

    def s_extra(i, n, side):
        return spare.at[gq(i, (2 * shared + 1) * quarter + side * 64, 64), cols_of(n)]

    def t_block(i, owner):
        return whole[i].at[rows_of(owner * temp, temp), 0:half]

    def t_inbox(i, n):
        return whole[i].at[rows_of(n * temp, temp), half:chan]

    def parts_of(i):
        return (0, 1) if i % 2 == 0 else (0,)

    def block_of(i, n, owner):
        return s_block(i, n, owner) if i % 2 == 0 else t_block(i, owner)

    def y_box(i, n, place):
        return spare.at[inbox(i, place * quarter, quarter), cols_of(n)] if i % 2 == 0 else t_inbox(i, place)

    def z_box(i, n, place):
        return spare.at[inbox(i, 576 + place * quarter, quarter), cols_of(n)] if i % 2 == 0 else t_inbox(i, 4 + place)

    def extra_y_box(i, n):
        return spare.at[inbox(i, 4 * quarter, 64), cols_of(n)]

    def extra_z_box(i, n, place):
        return spare.at[inbox(i, 576 + 3 * quarter + place * 64, 64), cols_of(n)]

    across = (h, w, b + 1 - 2 * par)

    def add_into(dst, parts, step):
        rows, cols = dst.shape

        def body(n, _):
            at_rows = rows_of(n * step, step)
            value = dst[at_rows, :].astype(F32)
            for part in parts:
                value = value + part[at_rows, :].astype(F32)
            dst[at_rows, :] = value.astype(BF16)
            return 0

        lax.fori_loop(0, rows // step, body, 0)

    def y_copy(i, n, d):
        place = lax.rem(bh + d, depth)
        src = block_of(i, n, 2 * place + 1 - par)
        return rc(src, y_box(i, n, place), r.y_send.at[i, n, d], r.y_recv.at[i, n, place], across)

    def z_copy(i, n, d):
        place = lax.rem(bh + d, depth)
        src = block_of(i, n, 2 * place + par)
        dev = (h, w, 2 * place + par)
        return rc(src, z_box(i, n, 3 - d), r.z_send.at[i, n, d], r.z_recv.at[i, n, 3 - d], dev)

    def extra_y(i, n):
        return rc(s_extra(i, n, 1 - par), extra_y_box(i, n), r.y_send.at[i, n, 4], r.y_recv.at[i, n, 4], across)

    def extra_z(i, n):
        place = jnp.minimum(lax.rem(bh - shared + 3 + depth, depth), 2)
        dev = (h, w, 2 * shared + par)
        return rc(
            s_extra(i, n, par), extra_z_box(i, n, place), r.z_send.at[i, n, 4], r.z_recv.at[i, n, 4 + place], dev
        )

    def step_of(i):
        return 16 if i % 2 == 0 else 48

    def reduce_start(i, n):
        for d in (1, 2, 3, 0):
            y_copy(i, n, d).start()
        if i % 2 == 0:
            extra_y(i, n).start()

    def reduce_middle(i, n):
        for d in (1, 2, 3, 0):
            place = lax.rem(bh + d, depth)
            y_copy(i, n, d).wait_send()
            box = y_box(i, n, place)
            rc(box, box, r.y_send.at[i, n, d], r.y_recv.at[i, n, place], across).wait_recv()
            add_into(block_of(i, n, 2 * place + par), [box], step_of(i))
            if d:
                z_copy(i, n, d).start()
        if i % 2 == 0:
            extra_y(i, n).wait()
            add_into(s_extra(i, n, par), [extra_y_box(i, n)], 16)
            pl.when(bh != shared)(lambda: extra_z(i, n).start())

    def final_part(i, n, side, core):
        place = 2 * side + core
        start = quarter * place - 64 * b + 512 * jnp.where(b > 2 * place, 1, 0)
        return outs[i].at[rows_of(start, quarter, 64), cols_of(n)]

    def extra_part(i, n):
        return outs[i].at[rows_of(512 * (1 - par), 64, 64), cols_of(n)]

    def final_copies(i, n):
        if i % 2:
            src = t_block(i, b)
            part = outs[i].at[h]
            return lc(src, part, r.out_sem.at[i, 0, 0]), [
                (src, part, sibling, r.cast_send.at[i, 0, 0], r.cast_recv.at[i, 0, 0])
            ]
        src = s_block(i, n, b)
        part = final_part(i, n, w, h)
        sends = [
            (src, part, dev, r.cast_send.at[i, n, d], r.cast_recv.at[i, n, d]) for d, dev in enumerate((beside, sibling))
        ]
        return lc(src, part, r.out_sem.at[i, n, 0]), sends

    def extra_copies(i, n):
        src = s_extra(i, n, par)
        part = extra_part(i, n)
        sends = [
            (src, part, dev, r.cast_send.at[i, n, 3 + d], r.cast_recv.at[i, n, 3 + d])
            for d, dev in enumerate((beside, sibling))
        ]
        return lc(src, part, r.out_sem.at[i, n, 1]), sends

    def begin(copies):
        local, sends = copies
        for src, part, dev, one, two in sends:
            rc(src, part, one, two, dev).start()
        local.start()

    def beside_copy(i):
        return rc(t_block(i, b), t_inbox(i, 7), r.z_send.at[i, 0, 4], r.z_recv.at[i, 0, 4], beside)

    def reduce_last(i, n):
        for d in (1, 2, 3):
            z_copy(i, n, d).wait()
        add_into(block_of(i, n, b), [z_box(i, n, place) for place in range(3)], step_of(i))
        if i % 2:
            beside_copy(i).start()
            return
        begin(final_copies(i, n))

        @pl.when(bh != shared)
        def _():
            extra_z(i, n).wait_send()

        @pl.when(bh == shared)
        def _():
            boxes = [extra_z_box(i, n, place) for place in range(3)]
            for place, box in enumerate(boxes):
                rc(box, box, r.z_send.at[i, n, 4], r.z_recv.at[i, n, 4 + place], across).wait_recv()
            add_into(s_extra(i, n, par), boxes, 16)
            begin(extra_copies(i, n))

    def reduce_out(i):
        beside_copy(i).wait()
        add_into(t_block(i, b), [t_inbox(i, 7)], 48)
        begin(final_copies(i, 0))

    def final_on(i, n):
        def move(part, d):
            rc(part, part, r.cast_send.at[i, n, d], r.cast_recv.at[i, n, d], beside).wait_recv()
            rc(part, part, r.cast_send.at[i, n, d + 2], r.cast_recv.at[i, n, d + 2], sibling).start()

        move(final_part(i, n, 1 - w, h), 0)
        pl.when(bh == shared_beside)(lambda: move(extra_part(i, n), 3))

    def reduce_wait(i, n):
        local, sends = final_copies(i, n)
        local.wait()
        if i % 2:
            src, part, dev, one, two = sends[0]
            rc(src, outs[i].at[1 - h], one, two, dev).wait()
            return
        for src, part, dev, one, two in sends:
            rc(src, part, one, two, dev).wait_send()

        def far(part, d):
            return rc(part, part, r.cast_send.at[i, n, d], r.cast_recv.at[i, n, d], sibling)

        far(final_part(i, n, w, 1 - h), 1).wait_recv()
        far(final_part(i, n, 1 - w, h), 2).wait_send()
        far(final_part(i, n, 1 - w, 1 - h), 2).wait_recv()
        local, sends = extra_copies(i, n)

        @pl.when(bh == shared)
        def _():
            local.wait()
            for src, part, dev, one, two in sends:
                rc(src, part, one, two, dev).wait_send()

        pl.when(bh == shared_beside)(lambda: far(extra_part(i, n), 5).wait_send())
        pl.when(bh == 2 * w + 1 - h)(lambda: far(extra_part(i, n), 4).wait_recv())
        pl.when(bh == 2 * (1 - w) + 1 - h)(lambda: far(extra_part(i, n), 5).wait_recv())

    def tile_of(ref, jh, jw):
        return ref.at[rows_of(jh * 4, 4, 4), rows_of(jw * 32, 32), :]

    def scatter(src, dst, n):
        copies = []
        for d, (j, dev) in enumerate(tile_group):
            copies.append(
                rc(src.at[j], tile_of(dst, h, w), r.tile_send.at[n, d], r.tile_recv.at[n, mine], dev)
            )
        return copies

    def scattered(src, dst, n):
        for d, (j, dev) in enumerate(tile_group):
            jh, jw = at_group(j)
            rc(src.at[j], tile_of(dst, jh, jw), r.tile_send.at[n, d], r.tile_recv.at[n, j], dev).wait()

    def tiles_start(src, dst, n):
        for copy in scatter(src, dst, n):
            copy.start()
        lc(src.at[mine], tile_of(dst, h, w), r.tile_own.at[n]).start()

    def tiles_wait(src, dst, n):
        scattered(src, dst, n)
        lc(src.at[mine], tile_of(dst, h, w), r.tile_own.at[n]).wait()

    xg, cg = r.x_grid, r.cot_grid
    tiles_start(r.x_tiles, xg, 0)
    gather_start(0)
    r.param[...] = total(0, mid, r.param_in[...])
    tiles_wait(r.x_tiles, xg, 0)

    def grid_chunk(ref, i):
        v = ref[lax.div(i, 4), rows_of(lax.rem(i, 4) * CHUNK, CHUNK), :]
        return v.astype(F32).reshape(2, CELL, chan)

    fill(r.xa, r.xb, lambda i: grid_chunk(xg, i), chan)

    def pump_loop(i, lo, hi):
        def body(s, _):
            gather_pump(i, s)
            return 0

        lax.fori_loop(lo, hi, body, 0)

    pump_loop(0, 1, nb - 3)
    gather_start(1)
    pump_loop(0, nb - 3, nb - 1)
    gather_start(2)
    gather_pump(0, nb - 1)
    gather_pump(1, 1)
    gather_pump(2, 1)
    gather_pump(1, 2)
    gather_finish(0)

    def first_pump(n):
        pl.when(n < 4)(lambda: gather_pump(1, 3 + n))
        pl.when(n == 1)(lambda: gather_pump(2, 2))

    conv(r.xa, r.xb, r.w1s, r.mid1, first_pump)
    sums = total(1, mid, packed(*moments(r.mid1, mid), mid))
    gather_pump(2, 3)
    gather_pump(1, nb - 1)
    prepare(0, sums, mid)

    def hidden(src, n, dst):
        value = activated(src, n, mid)

        def body(i, _):
            put(dst, i, value(i))
            return 0

        loop(CHUNKS, body, 0)

    hidden(r.mid1, 0, r.v1)
    gather_finish(1)
    gather_pump(2, 4)
    stats = temporal(0, r.v1, r.w1t, r.time1)
    sums = total(2, chan, packed(*stats, chan))
    gather_pump(2, 5)
    gather_start(3)
    prepare(1, sums, chan)
    fill(r.aa, r.ab, activated(r.time1, 1, chan), chan)
    gather_pump(2, 6)
    gather_pump(3, 1)
    gather_pump(2, nb - 1)
    gather_pump(3, 2)
    gather_finish(2)
    tiles_start(r.cot_tiles, cg, 1)

    def second_pump(n):
        pl.when(n < nb - 3)(lambda: gather_pump(3, 3 + n))

    conv(r.aa, r.ab, r.w2s, r.mid2, second_pump)
    sums = total(3, mid, packed(*moments(r.mid2, mid), mid), [lambda: gather_finish(3)])
    prepare(2, sums, mid)
    hidden(r.mid2, 2, r.v2)
    stats = temporal(1, r.v2, r.w2t, r.time2)
    shared_xq2 = share_x(0, r.aa, r.xq2)
    shared_xq1 = share_x(1, r.xa, r.xq1)
    for i in range(4):
        gather_sent(i)
    share_v2 = share(4, r.v2, r.sib_v)
    sums = total(4, chan, packed(*stats, chan))
    tiles_wait(r.cot_tiles, cg, 1)
    prepare(3, sums, chan)

    out_grid = r.out_grid

    def grid_put(ref, i, v):
        ref[lax.div(i, 4), rows_of(lax.rem(i, 4) * CHUNK, CHUNK), :] = v.reshape(CHUNK, chan).astype(ref.dtype)

    def slope(y, s):
        return s * (1.0 + y * (1.0 - s))

    def pre_body(i, carry):
        scale, shift, inv, offset = tiles(3, chan)
        v = chunk(r.time2, i)
        y = v * scale + shift + chunk(r.xa, i, MAIN)
        s = sigmoid(y)
        m = keep(i)
        grid_put(out_grid, i, y * s * m)
        d = grid_chunk(cg, i) * m * slope(y, s)
        put(r.grad_pre, i, d)
        t = d * (v * inv - offset)
        return (carry[0] + d[0] + d[1], carry[1] + t[0] + t[1])

    zero_out = jnp.zeros((CELL, chan), F32)
    zero_mid = jnp.zeros((CELL, mid), F32)
    out_grid[HGT] = jnp.zeros((8 * CELL, chan), BF16)
    gg = loop(CHUNKS, pre_body, (zero_out, zero_out))

    def send_tiles(src, dst, n):
        for d, (j, dev) in enumerate(tile_group):
            jh, jw = at_group(j)
            rc(tile_of(src, jh, jw), dst.at[mine], r.tile_send.at[n, d], r.tile_recv.at[n, mine], dev).start()
        lc(tile_of(src, h, w), dst.at[mine], r.tile_own.at[n]).start()

    def sent_tiles(src, dst, n):
        for d, (j, dev) in enumerate(tile_group):
            jh, jw = at_group(j)
            rc(tile_of(src, jh, jw), dst.at[j], r.tile_send.at[n, d], r.tile_recv.at[n, j], dev).wait()
        lc(tile_of(src, h, w), dst.at[mine], r.tile_own.at[n]).wait()

    send_tiles(out_grid, r.block_out, 2)

    def norm_back(n, sums, width):
        r.norm_grads[2 * n : 2 * n + 1, 0:width] = sums[2:3] + sums[3:4]
        r.norm_grads[2 * n + 1 : 2 * n + 2, 0:width] = sums[0:1] + sums[1:2]
        back = r.back
        back[0, :, 0:width] = per_batch(sums[0:1], sums[1:2], width) / cell_count
        back[1, :, 0:width] = per_batch(sums[2:3], sums[3:4], width) / cell_count

    def through_norm(n, src, grad, i, width):
        scale, _, inv, offset = tiles(n, width)
        xhat = chunk(src, i) * inv - offset
        bias_part = r.back[0, :, 0:width][None]
        gain_part = r.back[1, :, 0:width][None]
        return scale * (chunk(grad, i, 0, width) - bias_part - xhat * gain_part) * keep(i)

    def through_act(n, src, grad, width):
        def body(i, carry):
            scale, shift, inv, offset = tiles(n, width)
            v = chunk(src, i)
            y = v * scale + shift
            s = sigmoid(y)
            d = chunk(grad, i, 0, width) * keep(i) * slope(y, s)
            put(grad, i, d, 0, width)
            t = d * (v * inv - offset)
            return (carry[0] + d[0] + d[1], carry[1] + t[0] + t[1])

        zero = jnp.zeros((CELL, width), F32)
        return loop(CHUNKS, body, (zero, zero))

    def to_frames(n, src, grad):
        def body(i, _):
            e = through_norm(n, src, grad, i, chan).astype(BF16)
            ef = e.astype(F32)
            r.e3[1, rows_of(i * CHUNK, CHUNK), :] = e.reshape(CHUNK, chan)
            put_lanes(r.down, rows_of(i * CHUNK + CELL, CHUNK, CELL), ef.reshape(CHUNK, chan))
            put_lanes(r.up, rows_of(i * CHUNK, CHUNK), (ef * r.gate[...][None]).reshape(CHUNK, chan))
            return 0

        loop(CHUNKS, body, 0)

    sums = total(5, chan, packed(*gg, chan))
    norm_back(3, sums, chan)
    to_frames(3, r.time2, r.grad_pre)
    shared_e3 = temporal_back(2, r.w2t)
    gg = through_act(2, r.mid2, r.grad_mid, mid)
    shared_e3.wait()
    share_v2.wait()
    def temporal_grads(i, v):
        def first():
            transpose_v(v, r.sib_v)
            temporal_grad(i, 0)

        return [first, lambda: temporal_grad(i, 1), lambda: temporal_grad(i, 2)]

    sums = total(6, mid, packed(*gg, mid), temporal_grads(3, r.v2))
    reduce_start(3, 0)
    norm_back(2, sums, mid)

    def fill_e(n, src):
        def value(i):
            v = through_norm(n, src, r.grad_mid, i, mid)
            put(r.e_all, i, v)
            return v

        fill(r.ea, r.eb, value, mid)

    fill_e(2, r.mid2)
    share_e(0, 0)
    conv_back(r.ea, r.eb, r.w2s, r.grad_mid)
    share_e_on(0, 0)
    gg = through_act(1, r.time1, r.grad_mid, chan)
    for copy in shared_xq2:
        copy.wait()
    near, far = spare.at[mid : 2 * mid, :], spare.at[3 * mid : 4 * mid, :]

    def spread_and_turn():
        spread_x(r.xq2)
        transposes(r.aa, r.ab, r.xq2, near, far)

    def first_half():
        share_e_wait(0, 0)
        spatial_half(2, near, far, 0)

    sums = total(7, chan, packed(*gg, chan), [spread_and_turn, first_half])
    share_e(0, 1)
    reduce_start(2, 0)
    reduce_middle(3, 0)
    share_v1 = share(5, r.v1, r.sib_v)
    norm_back(1, sums, chan)
    to_frames(1, r.time1, r.grad_mid)

    shared_e3 = temporal_back(3, r.w1t)
    share_e_on(0, 1)
    reduce_last(3, 0)
    gg = through_act(0, r.mid1, r.grad_mid, mid)
    shared_e3.wait()
    share_v1.wait()
    share_e_wait(0, 1)
    spatial_half(2, near, far, 1)
    sums = total(8, mid, packed(*gg, mid), temporal_grads(1, r.v1))
    reduce_start(2, 1)
    reduce_start(1, 0)
    norm_back(0, sums, mid)
    fill_e(0, r.mid1)
    share_e(1, 0)
    share_e(1, 1)
    reduce_out(3)
    for n in (0, 1):
        reduce_middle(2, n)
    for copy in shared_xq1:
        copy.wait()
    spread_x(r.xq1)
    sent_tiles(out_grid, r.block_out, 2)
    conv_back(r.ea, r.eb, r.w1s, r.grad_mid)
    share_e_on(1, 0)
    near, far = r.w1s.at[0:mid, :], r.w1s.at[mid : 2 * mid, :]
    transposes(r.xa, r.xb, r.xq1, near, far)
    share_e_wait(1, 0)
    spatial_half(0, near, far, 0)
    reduce_start(0, 0)
    share_e_on(1, 1)
    share_e_wait(1, 1)
    spatial_half(0, near, far, 1)
    reduce_start(0, 1)

    def last_body(i, _):
        grid_put(out_grid, i, (chunk(r.grad_mid, i, 0, chan) + chunk(r.grad_pre, i)) * keep(i))
        return 0

    loop(CHUNKS, last_body, 0)
    send_tiles(out_grid, r.grad_input, 3)
    for n in (0, 1):
        reduce_last(2, n)
    reduce_middle(1, 0)
    for n in (0, 1):
        final_on(2, n)
    reduce_middle(0, 0)
    reduce_last(1, 0)
    reduce_out(1)
    reduce_last(0, 0)
    reduce_middle(0, 1)
    final_on(0, 0)
    reduce_last(0, 1)
    sent_tiles(out_grid, r.grad_input, 3)
    for n in (0, 1):
        reduce_wait(2, n)
    reduce_wait(3, 0)
    final_on(0, 1)
    reduce_wait(1, 0)
    for n in (0, 1):
        reduce_wait(0, n)


def per_device_fast(nb, *args):
    (
        inputs,
        starts,
        first_spatial,
        first_mid_gain,
        first_mid_bias,
        first_temporal,
        first_out_gain,
        first_out_bias,
        second_spatial,
        second_mid_gain,
        second_mid_bias,
        second_temporal,
        second_out_gain,
        second_out_bias,
        cotangent,
    ) = args
    micro, frames, side, _, chan = inputs.shape
    mid = first_spatial.shape[1]
    spat, temp = first_spatial.shape[0], first_temporal.shape[0]
    few = frames // 4
    h, w, b = (lax.axis_index(name) for name in ("ha", "wa", "batch"))
    mine = (1 - w) * h + w * (3 - h)
    offsets = jnp.arange(side)
    valid = (h * side + offsets < HGT)[:, None] & (w * side + offsets < HGT)[None, :]

    def tiles(array):
        array = array * valid.astype(BF16)[None, None, :, :, None]
        array = array.reshape(micro, 4, few, side, side, chan).transpose(1, 3, 4, 0, 2, 5)
        return array.reshape(4, side, side * micro * few, chan)

    def untiled(array):
        array = array.reshape(4, side, side, micro, few, chan).transpose(3, 0, 4, 1, 2, 5)
        return array.reshape(micro, frames, side, side, chan).astype(F32)

    gate = (1 - lax.dynamic_slice_in_dim(starts, mine * few, few, axis=1)).astype(F32)
    gate = jnp.broadcast_to(gate.reshape(micro * few, 1), (micro * few, chan))
    here = jnp.where((h == 0) & (w == 0), 1.0, 0.0)

    def placed(shard):
        row = jnp.zeros((mid,), F32)
        return lax.dynamic_update_slice(row, shard.astype(F32) * here, (b * shard.shape[0],))

    param = jnp.stack(
        [
            placed(v)
            for v in (
                first_mid_gain,
                first_mid_bias,
                first_out_gain,
                first_out_bias,
                second_mid_gain,
                second_mid_bias,
                second_out_gain,
                second_out_bias,
            )
        ]
    )
    half = chan // 2
    few_rows = ROWS // 4

    inputs_of = dict(
        x_tiles=(tiles(inputs), pl.ANY),
        cot_tiles=(tiles(cotangent), pl.ANY),
        gate=(gate, pltpu.VMEM),
        param_in=(param, pltpu.VMEM),
        first_spatial=(first_spatial, pl.ANY),
        first_temporal=(first_temporal, pl.ANY),
        second_spatial=(second_spatial, pl.ANY),
        second_temporal=(second_temporal, pl.ANY),
    )
    outputs_of = dict(
        block_out=((4, side, side * CELL, chan), BF16, pl.ANY),
        grad_input=((4, side, side * CELL, chan), BF16, pl.ANY),
        norm_grads=((8, mid), F32, pltpu.VMEM),
        out1s=((spat, mid), BF16, pl.ANY),
        out1t=((2, temp, half), BF16, pl.ANY),
        out2s=((spat, mid), BF16, pl.ANY),
        out2t=((2, temp, half), BF16, pl.ANY),
    )
    dma = pltpu.SemaphoreType.DMA
    scratch_of = dict(
        w1s=pltpu.VMEM((9 * chan, mid), BF16),
        w1t=pltpu.VMEM((3 * mid, chan), BF16),
        w2s=pltpu.VMEM((9 * chan, mid), BF16),
        w2t=pltpu.VMEM((3 * mid, chan), BF16),
        x_grid=pltpu.VMEM((8, 8 * CELL, chan), BF16),
        cot_grid=pltpu.VMEM((8, 8 * CELL, chan), BF16),
        out_grid=pltpu.VMEM((8, 8 * CELL, chan), BF16),
        xa=pltpu.VMEM((PADDED, chan), BF16),
        xb=pltpu.VMEM((PADDED, chan), BF16),
        aa=pltpu.VMEM((PADDED, chan), BF16),
        ab=pltpu.VMEM((PADDED, chan), BF16),
        ea=pltpu.VMEM((PADDED, mid), BF16),
        eb=pltpu.VMEM((PADDED, mid), BF16),
        mid1=pltpu.VMEM((ROWS, mid), F32),
        mid2=pltpu.VMEM((ROWS, mid), F32),
        grad_mid=pltpu.VMEM((ROWS, mid), F32),
        v1=pltpu.VMEM((ROWS, mid), BF16),
        v2=pltpu.VMEM((ROWS, mid), BF16),
        time1=pltpu.VMEM((ROWS, chan), F32),
        time2=pltpu.VMEM((ROWS, chan), F32),
        grad_pre=pltpu.VMEM((ROWS, chan), F32),
        down=pltpu.VMEM((chan // 128, ROWS + CHUNK, 128), F32),
        up=pltpu.VMEM((chan // 128, ROWS + CHUNK, 128), F32),
        e3=pltpu.VMEM((3, ROWS, chan), BF16),
        sib_e3=pltpu.VMEM((3, ROWS, half), BF16),
        halo_out=pltpu.VMEM((2, few_rows, chan), BF16),
        halo_in=pltpu.VMEM((4, 2, few_rows, chan), BF16),
        param=pltpu.VMEM((8, mid), F32),
        tile_mid=pltpu.VMEM((2, 4, CELL, mid), F32),
        tile_out=pltpu.VMEM((2, 4, CELL, chan), F32),
        back=pltpu.VMEM((2, CELL, mid), F32),
        sum_a=pltpu.VMEM((2, 2, 8, mid), F32),
        sum_b=pltpu.VMEM((2, 4, 8, mid), F32),
        sum_c=pltpu.VMEM((2, nb // 2, 8, mid), F32),
        own_sem=dma((4,)),
        ring_send=dma((4, 2, nb)),
        ring_recv=dma((4, 2, nb)),
        sib_send=dma((4, 3, nb)),
        sib_recv=dma((4, 3, nb)),
        over_send=dma((4, nb)),
        over_recv=dma((4, nb)),
        sa_send=dma((9,)),
        sa_recv=dma((9,)),
        sb_send=dma((9, 3)),
        sb_recv=dma((9, 4)),
        sc_send=dma((9, nb // 2)),
        sc_recv=dma((9, nb // 2)),
        halo_send=dma((4, 2)),
        halo_recv=dma((4, 2)),
        share_send=dma((6,)),
        share_recv=dma((6,)),
        e_all=pltpu.VMEM((4 * ROWS, mid), BF16),
        xq1=pltpu.VMEM((3, 2, PADDED, chan // 4), BF16),
        xq2=pltpu.VMEM((3, 2, PADDED, chan // 4), BF16),
        xt=pltpu.VMEM((mid, 2 * ROWS), BF16),
        sib_v=pltpu.VMEM((ROWS, mid), BF16),
        e_send=dma((2, 2, 3)),
        e_recv=dma((2, 2, 3)),
        xq_send=dma((2, 3)),
        xq_recv=dma((2, 3)),
        y_send=dma((4, 2, 5)),
        y_recv=dma((4, 2, 5)),
        z_send=dma((4, 2, 5)),
        z_recv=dma((4, 2, 7)),
        cast_send=dma((4, 2, 6)),
        cast_recv=dma((4, 2, 8)),
        out_sem=dma((4, 2, 2)),
        tile_send=dma((4, 3)),
        tile_recv=dma((4, 4)),
        tile_own=dma((4,)),
    )
    names = (*inputs_of, *outputs_of, *scratch_of)
    cell_count = float(frames * nb * HGT * HGT)
    results = pl.pallas_call(
        functools.partial(block_kernel, (nb, chan, mid, cell_count), names),
        out_shape=[jax.ShapeDtypeStruct(shape, dtype) for shape, dtype, _ in outputs_of.values()],
        in_specs=[pl.BlockSpec(memory_space=space) for _, space in inputs_of.values()],
        out_specs=[pl.BlockSpec(memory_space=space) for _, _, space in outputs_of.values()],
        scratch_shapes=list(scratch_of.values()),
        compiler_params=pltpu.CompilerParams(
            collective_id=0, has_side_effects=True, vmem_limit_bytes=VMEM_LIMIT
        ),
    )(*(array for array, _ in inputs_of.values()))
    got = SimpleNamespace(**dict(zip(outputs_of, results)))

    def temporal(pair):
        return jnp.concatenate([pair[0], pair[1]], axis=1).astype(F32)

    def norm(row, like):
        size = like.shape[0]
        return lax.dynamic_slice_in_dim(got.norm_grads[row], b * size, size)

    return (
        untiled(got.block_out),
        untiled(got.grad_input),
        got.out1s.astype(F32),
        norm(0, first_mid_gain),
        norm(1, first_mid_bias),
        temporal(got.out1t),
        norm(2, first_out_gain),
        norm(3, first_out_bias),
        got.out2s.astype(F32),
        norm(4, second_mid_gain),
        norm(5, second_mid_bias),
        temporal(got.out2t),
        norm(6, second_out_gain),
        norm(7, second_out_bias),
    )


def extended(shard, sides, width):
    for axis, dim in sides:
        count, length = (lax.axis_size(axis), shard.shape[dim])
        up = [(i, (i + 1) % count) for i in range(count - 1)]
        down = [(j, i) for i, j in up]
        last = lax.slice_in_dim(shard, length - width, length, axis=dim)
        leading = lax.slice_in_dim(shard, 0, width, axis=dim)
        before = lax.ppermute(last, axis, up)
        after = lax.ppermute(leading, axis, down)
        shard = jnp.concatenate([before, shard, after], axis=dim)
    return shard


def passed_along(shard, axis, by):
    count = lax.axis_size(axis)
    pairs = [(i, i + by) for i in range(count) if 0 <= i + by < count]
    return lax.ppermute(shard, axis, pairs)


def for_sending(shard):

    def short(part):
        return part.astype(jnp.bfloat16) if part.dtype == jnp.float32 else part

    return jax.tree.map(short, shard)


def silu_slope(values):
    sigma = jax.nn.sigmoid(values)
    return sigma * (1.0 + values * (1.0 - sigma))


def spatial_forward(field_in, kernel):
    frames, tile_side = (field_in.shape[0], field_in.shape[1])
    padded = extended(field_in, (("ha", 1), ("wa", 2)), 1)
    pieces = [
        padded[:, offset // 3 : offset // 3 + tile_side, offset % 3 : offset % 3 + tile_side, :]
        for offset in range(9)
    ]
    patches = jnp.concatenate(pieces, axis=-1).reshape(frames * tile_side * tile_side, -1)
    return (patches, jnp.dot(patches, kernel, preferred_element_type=jnp.float32))


def spatial_backward(grad_out, patches, kernel):
    frames, tile_side, channels = (grad_out.shape[0], grad_out.shape[1], grad_out.shape[3])
    row_count = frames * tile_side * tile_side
    padded = extended(grad_out, (("ha", 1), ("wa", 2)), 1)
    pieces = [
        padded[
            :,
            2 - offset // 3 : 2 - offset // 3 + tile_side,
            2 - offset % 3 : 2 - offset % 3 + tile_side,
            :,
        ]
        for offset in range(9)
    ]
    stacked = jnp.concatenate(pieces, axis=-1).reshape(row_count, 9, channels)
    grad_in = jnp.einsum(
        "rkm,kcm->rc", stacked, kernel.reshape(9, -1, channels), preferred_element_type=jnp.float32
    )
    grad_kernel = jnp.einsum(
        "rk,rm->km",
        patches,
        grad_out.reshape(row_count, channels),
        preferred_element_type=jnp.float32,
    )
    return (grad_in, grad_kernel)


def temporal_forward(field_in, clip_gate, kernel):
    frames, tile_side = (field_in.shape[0], field_in.shape[1])
    gated_in = field_in * clip_gate
    earlier = passed_along(field_in[-1:], "batch", 1)
    later_frame = passed_along(gated_in[:1], "batch", -1)
    before = jnp.concatenate([earlier, field_in[:-1]], axis=0) * clip_gate
    after_tap = jnp.concatenate([gated_in[1:], later_frame], axis=0)
    joined = jnp.concatenate([before, field_in, after_tap], axis=-1).reshape(
        frames * tile_side * tile_side, -1
    )
    return (joined, jnp.dot(joined, kernel, preferred_element_type=jnp.float32))


def temporal_backward(grad_out, joined, clip_gate, kernel):
    frames, tile_side, channels = (grad_out.shape[0], grad_out.shape[1], grad_out.shape[3])
    row_count = frames * tile_side * tile_side
    gated_grad = grad_out * clip_gate
    later_frame = passed_along(gated_grad[:1], "batch", -1)
    earlier = passed_along(grad_out[-1:], "batch", 1)
    from_later = jnp.concatenate([gated_grad[1:], later_frame], axis=0)
    from_earlier = jnp.concatenate([earlier, grad_out[:-1]], axis=0) * clip_gate
    stacked = jnp.concatenate([from_later, grad_out, from_earlier], axis=-1).reshape(
        row_count, 3, channels
    )
    grad_in = jnp.einsum(
        "rkc,kmc->rm", stacked, kernel.reshape(3, -1, channels), preferred_element_type=jnp.float32
    )
    grad_kernel = jnp.einsum(
        "rk,rc->kc",
        joined,
        grad_out.reshape(row_count, channels),
        preferred_element_type=jnp.float32,
    )
    return (grad_in, grad_kernel)


def norm_forward(pre_norm, norm_gain, norm_bias, valid_rows, cell_count):
    first_sum = jnp.sum(pre_norm * valid_rows, axis=0)
    square_sum = jnp.sum(pre_norm * pre_norm * valid_rows, axis=0)
    first_sum, square_sum = lax.psum((first_sum, square_sum), ("ha", "wa", "batch"))
    mean_val = first_sum / cell_count
    inv_std = lax.rsqrt(square_sum / cell_count - mean_val * mean_val + epsilon)
    normed = (pre_norm - mean_val) * inv_std
    return (normed, inv_std, normed * norm_gain.astype(jnp.float32) + norm_bias.astype(jnp.float32))


def norm_backward(grad_norm, normed, inv_std, norm_gain, valid_rows, cell_count):
    bias_grad = jnp.sum(grad_norm, axis=0)
    gain_grad = jnp.sum(grad_norm * normed, axis=0)
    bias_grad, gain_grad = lax.psum((bias_grad, gain_grad), ("ha", "wa", "batch"))
    grad_in = (
        valid_rows
        * norm_gain.astype(jnp.float32)
        * inv_std
        * (grad_norm - bias_grad / cell_count - normed * gain_grad / cell_count)
    )
    return (grad_in, gain_grad, bias_grad)


def forward_pair(field_in, weights, clip_gate, valid_rows, cell_count):
    frames, tile_side = (field_in.shape[0], field_in.shape[1])
    patches, spatial_out = spatial_forward(field_in, weights[0])
    mid_hat, mid_scale, mid_norm = norm_forward(
        spatial_out, weights[1], weights[2], valid_rows, cell_count
    )
    hidden = (
        (jax.nn.silu(mid_norm) * valid_rows)
        .astype(jnp.bfloat16)
        .reshape(frames, tile_side, tile_side, -1)
    )
    joined, temporal_out = temporal_forward(hidden, clip_gate, weights[3])
    out_hat, out_scale, out_norm = norm_forward(
        temporal_out, weights[4], weights[5], valid_rows, cell_count
    )
    return ((patches, mid_hat, mid_scale, mid_norm, joined, out_hat, out_scale), out_norm)


def backward_pair(grad_norm, kept, weights, clip_gate, valid_rows, cell_count, tile_side):
    patches, mid_hat, mid_scale, mid_norm, joined, out_hat, out_scale = kept
    frames = clip_gate.shape[0]
    grad_time, out_gain_grad, out_bias_grad = norm_backward(
        grad_norm, out_hat, out_scale, weights[4], valid_rows, cell_count
    )
    grad_time = grad_time.astype(jnp.bfloat16).reshape(frames, tile_side, tile_side, -1)
    grad_hidden, temporal_grad = temporal_backward(grad_time, joined, clip_gate, weights[3])
    grad_mid = grad_hidden * valid_rows * silu_slope(mid_norm)
    grad_spatial, mid_gain_grad, mid_bias_grad = norm_backward(
        grad_mid, mid_hat, mid_scale, weights[1], valid_rows, cell_count
    )
    grad_spatial = grad_spatial.astype(jnp.bfloat16).reshape(frames, tile_side, tile_side, -1)
    grad_in, spatial_grad = spatial_backward(grad_spatial, patches, weights[0])
    return (
        grad_in,
        (spatial_grad, mid_gain_grad, mid_bias_grad, temporal_grad, out_gain_grad, out_bias_grad),
    )


def per_device(
    inputs,
    starts,
    first_spatial,
    first_mid_gain,
    first_mid_bias,
    first_temporal,
    first_out_gain,
    first_out_bias,
    second_spatial,
    second_mid_gain,
    second_mid_bias,
    second_temporal,
    second_out_gain,
    second_out_bias,
    cotangent,
):
    shards = (
        first_spatial,
        first_mid_gain,
        first_mid_bias,
        first_temporal,
        first_out_gain,
        first_out_bias,
        second_spatial,
        second_mid_gain,
        second_mid_bias,
        second_temporal,
        second_out_gain,
        second_out_bias,
    )
    micro_total, frames, tile_side, channels = (
        inputs.shape[0],
        inputs.shape[1],
        inputs.shape[2],
        inputs.shape[4],
    )
    row_count = frames * tile_side * tile_side
    cell_count = frames * lax.axis_size("batch") * HGT * HGT
    offsets = jnp.arange(tile_side)
    inside_h = lax.axis_index("ha") * tile_side + offsets < HGT
    inside_w = lax.axis_index("wa") * tile_side + offsets < HGT
    valid_grid = inside_h[:, None] & inside_w[None, :]
    valid_tile = valid_grid.astype(jnp.bfloat16)[None, :, :, None]
    valid_rows = jnp.broadcast_to(
        valid_grid.astype(jnp.float32)[None], (frames, tile_side, tile_side)
    ).reshape(row_count, 1)
    results = []
    input_grads = []
    kernel_total = None
    norm_total = None
    for micro_step in range(micro_total):
        gathered = (
            lax.all_gather(shards[0], "batch", axis=0, tiled=True),
            lax.all_gather(shards[1], "batch", axis=0, tiled=True),
            lax.all_gather(shards[2], "batch", axis=0, tiled=True),
            lax.all_gather(shards[3], "batch", axis=0, tiled=True),
            lax.all_gather(shards[4], "batch", axis=0, tiled=True),
            lax.all_gather(shards[5], "batch", axis=0, tiled=True),
            lax.all_gather(shards[6], "batch", axis=0, tiled=True),
            lax.all_gather(shards[7], "batch", axis=0, tiled=True),
            lax.all_gather(shards[8], "batch", axis=0, tiled=True),
            lax.all_gather(shards[9], "batch", axis=0, tiled=True),
            lax.all_gather(shards[10], "batch", axis=0, tiled=True),
            lax.all_gather(shards[11], "batch", axis=0, tiled=True),
        )
        clip_gate = (1 - starts[micro_step]).astype(jnp.bfloat16).reshape(frames, 1, 1, 1)
        x_in = inputs[micro_step] * valid_tile
        first_kept, first_norm = forward_pair(
            x_in, gathered[0:6], clip_gate, valid_rows, cell_count
        )
        first_act = (
            (jax.nn.silu(first_norm) * valid_rows)
            .astype(jnp.bfloat16)
            .reshape(frames, tile_side, tile_side, channels)
        )
        second_kept, second_norm = forward_pair(
            first_act, gathered[6:12], clip_gate, valid_rows, cell_count
        )
        pre_out = second_norm + x_in.reshape(row_count, channels).astype(jnp.float32)
        results.append(
            (jax.nn.silu(pre_out) * valid_rows).reshape(frames, tile_side, tile_side, channels)
        )
        grad_pre = (
            cotangent[micro_step].reshape(row_count, channels).astype(jnp.float32)
            * valid_rows
            * silu_slope(pre_out)
        )
        grad_act, second_grads = backward_pair(
            grad_pre, second_kept, gathered[6:12], clip_gate, valid_rows, cell_count, tile_side
        )
        grad_first = grad_act * valid_rows * silu_slope(first_norm)
        grad_conv, first_grads = backward_pair(
            grad_first, first_kept, gathered[0:6], clip_gate, valid_rows, cell_count, tile_side
        )
        input_grads.append(
            ((grad_conv + grad_pre) * valid_rows).reshape(frames, tile_side, tile_side, channels)
        )
        step_grads = first_grads + second_grads
        kernel_now = (step_grads[0], step_grads[3], step_grads[6], step_grads[9])
        norm_now = (
            step_grads[1],
            step_grads[2],
            step_grads[4],
            step_grads[5],
            step_grads[7],
            step_grads[8],
            step_grads[10],
            step_grads[11],
        )
        if micro_step == 0:
            kernel_total = kernel_now
            norm_total = norm_now
        else:
            kernel_total = jax.tree.map(jnp.add, kernel_total, kernel_now)
            norm_total = jax.tree.map(jnp.add, norm_total, norm_now)
    kernel_total = lax.psum_scatter(kernel_total, "batch", scatter_dimension=0, tiled=True)
    kernel_total = jax.tree.map(
        lambda part: part.astype(jnp.float32), lax.psum(for_sending(kernel_total), ("ha", "wa"))
    )
    shard_index = lax.axis_index("batch")
    batch_count = lax.axis_size("batch")
    norm_shards = tuple(
        (
            lax.dynamic_slice_in_dim(
                full_sum,
                shard_index * (full_sum.shape[0] // batch_count),
                full_sum.shape[0] // batch_count,
            )
            for full_sum in norm_total
        )
    )
    return (
        jnp.stack(results),
        jnp.stack(input_grads),
        kernel_total[0],
        norm_shards[0],
        norm_shards[1],
        kernel_total[1],
        norm_shards[2],
        norm_shards[3],
        kernel_total[2],
        norm_shards[4],
        norm_shards[5],
        kernel_total[3],
        norm_shards[6],
        norm_shards[7],
    )


def solution(mesh):
    in_specs = (
        P(None, "batch", "ha", "wa", None),
        P(None, "batch"),
        P("batch", None),
        P("batch"),
        P("batch"),
        P("batch", None),
        P("batch"),
        P("batch"),
        P("batch", None),
        P("batch"),
        P("batch"),
        P("batch", None),
        P("batch"),
        P("batch"),
        P(None, "batch", "ha", "wa", None),
    )
    out_specs = (
        P(None, "batch", "ha", "wa", None),
        P(None, "batch", "ha", "wa", None),
        P("batch", None),
        P("batch"),
        P("batch"),
        P("batch", None),
        P("batch"),
        P("batch"),
        P("batch", None),
        P("batch"),
        P("batch"),
        P("batch", None),
        P("batch"),
        P("batch"),
    )
    batch = mesh.shape["batch"]

    def program(*args):
        spat, temp = args[2].shape[0], args[5].shape[0]
        fits = args[0].shape == (2, 16, 4, 4, 512) and args[2].shape[1] == 1152
        if fits and batch == 8 and spat * batch == 9 * 512 and temp * batch == 3 * 1152:
            return per_device_fast(batch, *args)
        return per_device(*args)

    return jax.shard_map(
        program, mesh=mesh, in_specs=in_specs, out_specs=out_specs, check_vma=False
    )
```

```python
import functools
from types import SimpleNamespace

import jax
import jax.numpy as jnp
from jax import lax
from jax.experimental import pallas as pl
from jax.experimental.pallas import tpu as pltpu
from jax.sharding import PartitionSpec as P

HGT = 7
epsilon = 1e-05
MESH = pl.DeviceIdType.MESH
F32 = jnp.float32
BF16 = jnp.bfloat16

BASE = 10
CELL = 8
ROWS = HGT * 8 * CELL
PADDED = (BASE + HGT * 8 + BASE) * CELL
MAIN = BASE * CELL
CHUNK = 2 * CELL
CHUNKS = ROWS // CHUNK
VMEM_LIMIT = 64 * 1024 * 1024 - 1024 * 1024


def when(cond, work):
    if cond is True:
        work()
    elif cond is not False:
        pl.when(cond)(work)


def loop(count, body, init):
    def twice(i, carry):
        return body(2 * i + 1, body(2 * i, carry))

    return lax.fori_loop(0, count // 2, twice, init)


def sigmoid(x):
    return 0.5 * jnp.tanh(0.5 * x) + 0.5


def nn(a, b):
    return jnp.dot(a, b, preferred_element_type=F32)


def nt(a, b):
    return lax.dot_general(a, b, (((1,), (1,)), ((), ())), preferred_element_type=F32)


def tn(a, b):
    return lax.dot_general(a, b, (((0,), (0,)), ((), ())), preferred_element_type=F32)


def rows_of(start, size, step=16):
    if not isinstance(start, int):
        start = pl.multiple_of(start, step)
    return pl.ds(start, size)


def block_kernel(dims, names, *all_refs):
    r = SimpleNamespace(**dict(zip(names, all_refs, strict=True)))
    nb, chan, mid, cell_count = dims
    spat = 9 * chan // nb
    temp = 3 * mid // nb
    unit = spat // 6
    quarter = chan // 4
    half = chan // 2
    h = lax.axis_index("ha")
    w = lax.axis_index("wa")
    b = lax.axis_index("batch")
    par = lax.rem(b, 2)
    bh = lax.div(b, 2)
    pos = par * (nb - 1 - bh) + (1 - par) * bh
    ways = (1 - 2 * h, 2 * h - 1)

    def at(p):
        p = lax.rem(p + 4 * nb, nb)
        upper = lax.div(p, nb // 2)
        return (1 - upper) * (2 * p) + upper * (2 * (nb - 1 - p) + 1)

    def at_group(j):
        return (lax.rem(j, 2), lax.div(j, 2))

    mine = 2 * w + h
    sibling = (1 - h, w, b)
    beside = (h, 1 - w, b)
    onward = [(h, w, at(pos + way)) for way in ways]
    later_dev = (1 - h, w, lax.rem(b + h, nb))
    earlier_dev = (1 - h, w, lax.rem(b + nb - 1 + h, nb))
    tile_group = [(lax.rem(mine + d, 4), (*at_group(lax.rem(mine + d, 4)), b)) for d in (1, 2, 3)]
    across = (h, w, b + 1 - 2 * par)
    pos_b = h * 2 + par
    plane = []
    for d in (1, 2, 3):
        q = lax.rem(pos_b + d, 4)
        plane.append((q, (lax.div(q, 2), w, b - par + lax.rem(q, 2))))
    depth = nb // 2
    line = []
    for d in range(1, depth):
        q = lax.rem(bh + d, depth)
        line.append((q, (h, w, 2 * q + par)))

    def named(dev):
        return dict(ha=dev[0], wa=dev[1], batch=dev[2])

    def rc(src, dst, send, recv, dev):
        return pltpu.make_async_remote_copy(
            src_ref=src, dst_ref=dst, send_sem=send, recv_sem=recv, device_id=named(dev), device_id_type=MESH
        )

    def lc(src, dst, sem):
        return pltpu.make_async_copy(src, dst, sem)

    partners = [sibling, beside, *onward, later_dev, earlier_dev]
    partners += [dev for _, dev in tile_group + plane + line]
    barrier = pltpu.get_barrier_semaphore()
    for dev in partners:
        pl.semaphore_signal(barrier, inc=1, device_id=named(dev), device_id_type=MESH)
    pl.semaphore_wait(barrier, len(partners))

    shards = (r.first_spatial, r.first_temporal, r.second_spatial, r.second_temporal)
    whole = (r.w1s, r.w1t, r.w2s, r.w2t)
    shared = 2 * w + h
    shared_beside = 2 * (1 - w) + h
    third = temp // 3

    def units(i, core, side):
        return (2 * side + core, 4 + core) if i % 2 == 0 else ((1 - core) * side + 2 * core,)

    def piece(i, ref, owner, u, k):
        if i % 2 == 0:
            return ref.at[rows_of(owner * spat + u * unit + k * (unit // 2), unit // 2), :]
        return ref.at[rows_of(owner * temp + u * third, third), :]

    def subs(i):
        return (0, 1) if i % 2 == 0 else (0,)

    def streams(i):
        return (0, 1) if i % 2 == 0 else (0,)

    def crossing(i, work):
        if i % 2 == 0:
            work()
        else:
            pl.when(h == 0)(work)

    def crossed(i, work):
        if i % 2 == 0:
            work()
        else:
            pl.when(h == 1)(work)

    def own_copy(i):
        rows = spat if i % 2 == 0 else temp
        return lc(shards[i], whole[i].at[rows_of(b * rows, rows), :], r.own_sem.at[i])

    def ring(i, st, k, s, owner, from_shard=False):
        u = units(i, h, w)[st]
        dst = piece(i, whole[i], owner, u, k)
        src = piece(i, shards[i], 0, u, k) if from_shard else dst
        return rc(src, dst, r.ring_send.at[i, st, k, s], r.ring_recv.at[i, st, k, s], onward[st])

    def cross(i, kind, k, s, owner, u):
        part = piece(i, whole[i], owner, u, k)
        return rc(part, part, r.sib_send.at[i, kind, k, s], r.sib_recv.at[i, kind, k, s], sibling)

    def over(i, k, s, owner, u):
        part = piece(i, whole[i], owner, u, k)
        return rc(part, part, r.over_send.at[i, k, s], r.over_recv.at[i, k, s], beside)

    def gather_start(i):
        for k in subs(i):
            for st in streams(i):
                ring(i, st, k, 1, b, True).start()
        own_copy(i).start()

    def gather_relay(i, s):
        owner = at(pos - ways[0] * s)

        def work():
            for k in subs(i):
                over(i, k, s, owner, units(i, h, 1 - w)[0]).wait_recv()
                cross(i, 2, k, s, owner, units(i, h, 1 - w)[0]).start()

        crossing(i, work)

    def gather_pump(i, s):
        own = units(i, h, w)
        for k in subs(i):
            for st in streams(i):
                owner = at(pos - ways[st] * s)
                ring(i, st, k, s, owner).wait_recv()
                if isinstance(s, int):
                    if s < nb - 1:
                        ring(i, st, k, s + 1, owner).start()
                else:
                    pl.when(s < nb - 1)(lambda st=st, k=k, owner=owner: ring(i, st, k, s + 1, owner).start())
                if st == 0:
                    crossing(i, lambda k=k, owner=owner: over(i, k, s, owner, own[0]).start())
                cross(i, st, k, s, owner, own[st]).start()
        if isinstance(s, int):
            if s > 1:
                gather_relay(i, s - 1)
        else:
            pl.when(s > 1)(lambda: gather_relay(i, s - 1))

    def gather_finish(i):
        gather_relay(i, nb - 1)

        def body(s, _):
            for k in subs(i):
                for st in streams(i):
                    cross(i, st, k, s, at(pos + ways[st] * s), units(i, 1 - h, w)[st]).wait_recv()
                theirs = at(pos + ways[0] * s)
                crossed(i, lambda k=k: cross(i, 2, k, s, theirs, units(i, 1 - h, 1 - w)[0]).wait_recv())
            return 0

        lax.fori_loop(1, nb, body, 0)
        own_copy(i).wait()

    def gather_sent(i):
        def body(s, _):
            for k in subs(i):
                for st in streams(i):
                    owner = at(pos - ways[st] * s)
                    ring(i, st, k, s, owner).wait_send()
                    cross(i, st, k, s, owner, units(i, h, w)[st]).wait_send()

                def sent(k=k):
                    owner = at(pos - ways[0] * s)
                    over(i, k, s, owner, units(i, h, w)[0]).wait_send()
                    cross(i, 2, k, s, owner, units(i, h, 1 - w)[0]).wait_send()

                crossing(i, sent)
            return 0

        lax.fori_loop(1, nb, body, 0)

    def total(k, width, value, works=()):
        slot = k % 2
        wide = value.shape[1]
        cols = pl.ds(0, wide)
        works = list(works) + [None] * 2
        four, far = r.sum_b, r.sum_c
        four[slot, pos_b, :, cols] = value
        sends = []
        for n, (q, dev) in enumerate(plane):
            part = four.at[slot, pos_b, :, cols]
            sends.append(rc(part, part, r.sb_send.at[k, n], r.sb_recv.at[k, pos_b], dev))
            sends[-1].start()
        if works[0]:
            works[0]()
        for n, (q, dev) in enumerate(plane):
            part = four.at[slot, q, :, cols]
            rc(part, part, r.sb_send.at[k, n], r.sb_recv.at[k, q], dev).wait_recv()
        far[slot, bh, :, cols] = (four[slot, 0, :, cols] + four[slot, 1, :, cols]) + (
            four[slot, 2, :, cols] + four[slot, 3, :, cols]
        )
        for n, (q, dev) in enumerate(line):
            part = far.at[slot, bh, :, cols]
            sends.append(rc(part, part, r.sc_send.at[k, n], r.sc_recv.at[k, bh], dev))
            sends[-1].start()
        if works[1]:
            works[1]()
        for n, (q, dev) in enumerate(line):
            part = far.at[slot, q, :, cols]
            rc(part, part, r.sc_send.at[k, n], r.sc_recv.at[k, q], dev).wait_recv()
        result = far[slot, 0, :, cols]
        for q in range(1, depth):
            result = result + far[slot, q, :, cols]
        for send in sends:
            send.wait_send()
        if wide == width:
            return result
        return jnp.concatenate([result[2 * n : 2 * n + 2] for n in range(width // wide)], axis=1)

    def chunk(ref, i, base=0, width=None):
        cols = slice(None) if width is None else pl.ds(0, width)
        value = ref[rows_of(base + i * CHUNK, CHUNK), cols]
        return value.astype(F32).reshape(2, CELL, value.shape[-1])

    def put(ref, i, value, base=0, width=None):
        cols = slice(None) if width is None else pl.ds(0, width)
        ref[rows_of(base + i * CHUNK, CHUNK), cols] = value.reshape(CHUNK, value.shape[-1]).astype(ref.dtype)

    def keep(i):
        inside = jnp.where(lax.rem(i, 4) == 3, 0.0, 1.0).astype(F32)
        first = lax.broadcasted_iota(jnp.int32, (2, 1, 1), 0) == 0
        return jnp.where(first, 1.0, inside)

    def packed(one, two, width):
        rows = jnp.concatenate([jnp.sum(v, axis=0, keepdims=True) for v in (one, two)], axis=0)
        wide = 384 if width == mid else 128
        parts = [rows[:, n * wide : (n + 1) * wide] for n in range(width // wide)]
        return jnp.concatenate((parts + parts[-1:])[0:4], axis=0)

    def moments(ref, width):
        def body(i, carry):
            v = chunk(ref, i)
            m = v * keep(i)
            return (carry[0] + m[0] + m[1], carry[1] + m[0] * v[0] + m[1] * v[1])

        zero = jnp.zeros((CELL, width), F32)
        return loop(CHUNKS, body, (zero, zero))

    def prepare(n, sums, width):
        tile = r.tile_mid if width == mid else r.tile_out
        n2 = n // 2
        gain = r.param[2 * n : 2 * n + 1, 0:width]
        bias = r.param[2 * n + 1 : 2 * n + 2, 0:width]
        mean = sums[0:1] / cell_count
        inv = lax.rsqrt(sums[1:2] / cell_count - mean * mean + epsilon)
        scale = inv * gain
        shift = bias - mean * scale
        for k, v in enumerate((scale, shift, inv, mean * inv)):
            tile[n2, k] = jnp.broadcast_to(v, (CELL, width))

    def tiles(n, width):
        tile = r.tile_mid if width == mid else r.tile_out
        return [tile[n // 2, k][None] for k in range(4)]

    def fill(ref_a, ref_b, value_of, width):
        pads(ref_a, ref_b, width)

        def body(i, before):
            v = value_of(i)
            put(ref_a, i, v, MAIN)
            pair = jnp.concatenate([before[None], v[0:1]], axis=0)
            put(ref_b, i, pair, MAIN - CHUNK)
            return v[1]

        loop(CHUNKS, body, jnp.zeros((CELL, width), F32))

    def activated(src, n, width):
        def value(i):
            scale, shift, _, _ = tiles(n, width)
            y = chunk(src, i) * scale + shift
            return y * sigmoid(y) * keep(i)

        return value

    def taps(ref_a, ref_b, k, size=ROWS):
        r0 = MAIN - 8 * CELL + 8 * CELL * k
        return (
            ref_b[rows_of(r0 - CHUNK, size), :],
            ref_a[rows_of(r0, size), :],
            ref_b[rows_of(r0, size), :],
        )

    def conv(ref_a, ref_b, weight, out, pump=None):
        for n, (c0, cw) in enumerate(((0, 512), (512, mid - 512))):

            def body(a, _, c0=c0, cw=cw, n=n):
                x = taps(ref_a, ref_b, a)
                acc = nn(jnp.concatenate(x, axis=1), weight[rows_of(a * 3 * chan, 3 * chan), c0 : c0 + cw])

                @pl.when(a == 0)
                def _():
                    out[:, c0 : c0 + cw] = acc

                @pl.when(a > 0)
                def _():
                    out[:, c0 : c0 + cw] += acc

                if pump is not None:
                    pump(n * 3 + a)
                return 0

            lax.fori_loop(0, 3, body, 0)

    def conv_back(ref_a, ref_b, weight, out, pump=None):
        def body(k, _):
            e = taps(ref_a, ref_b, k)
            acc = None
            for j in range(3):
                tap = 8 - 3 * k - j
                term = nt(e[j], weight[rows_of(tap * chan, chan), :])
                acc = term if acc is None else acc + term

            @pl.when(k == 0)
            def _():
                out[:, 0:chan] = acc

            @pl.when(k > 0)
            def _():
                out[:, 0:chan] += acc

            if pump is not None:
                pump(k)
            return 0

        lax.fori_loop(0, 3, body, 0)

    def send_frames(k):
        down, up = r.down, r.up
        count = ROWS // CELL
        for c in range(chan // 128):
            lanes = pl.ds(128 * c, 128)
            r.halo_out[0, :, lanes] = down[c, pl.ds(2 * CELL - 1, count, stride=CELL), :]
            r.halo_out[1, :, lanes] = up[c, pl.ds(0, count, stride=CELL), :]
        copies = []
        for n, dev in ((0, later_dev), (1, earlier_dev)):
            copies.append(
                rc(r.halo_out.at[n], r.halo_in.at[k, n], r.halo_send.at[k, n], r.halo_recv.at[k, n], dev)
            )
            copies[-1].start()
        return copies

    def take_frames(k, copies):
        down, up = r.down, r.up
        count = ROWS // CELL
        for copy in copies:
            copy.wait()
        at_start = jnp.logical_and(h == 0, b == 0)
        at_end = jnp.logical_and(h == 1, b == nb - 1)
        for c in range(chan // 128):
            lanes = pl.ds(128 * c, 128)
            before = r.halo_in[k, 0, :, lanes]
            after = r.halo_in[k, 1, :, lanes]
            down[c, pl.ds(CELL - 1, count, stride=CELL), :] = jnp.where(at_start, 0.0, before)
            up[c, pl.ds(CELL, count, stride=CELL), :] = jnp.where(at_end, 0.0, after)

    def by_lanes(ref, rows):
        return jnp.concatenate([ref[c, rows, :] for c in range(chan // 128)], axis=1)

    def put_lanes(ref, rows, value):
        for c in range(chan // 128):
            ref[c, rows, :] = value[:, 128 * c : 128 * c + 128]

    def shifted(i):
        before = by_lanes(r.down, rows_of(i * CHUNK, CHUNK + CELL))[CELL - 1 : CELL - 1 + CHUNK]
        after = by_lanes(r.up, rows_of(i * CHUNK, CHUNK + CELL))[1 : 1 + CHUNK]
        gate = r.gate[...][None]
        return (before.reshape(2, CELL, chan) * gate, after.reshape(2, CELL, chan))

    def temporal(k, v, weight, out, works=()):
        works = list(works) + [None] * 2
        put_lanes(r.down, pl.ds(CELL, ROWS), nn(v[...], weight[0:mid, :]))
        y2 = nn(v[...], weight[2 * mid : 3 * mid, :])
        y2 = (y2.reshape(ROWS // CELL, CELL, chan) * r.gate[...][None]).reshape(ROWS, chan)
        put_lanes(r.up, pl.ds(0, ROWS), y2)
        copies = send_frames(k)
        out[...] = nn(v[...], weight[mid : 2 * mid, :])
        if works[0]:
            works[0]()
        take_frames(k, copies)

        def body(i, carry):
            before, after = shifted(i)
            value = chunk(out, i) + before + after
            put(out, i, value)
            m = value * keep(i)
            return (carry[0] + m[0] + m[1], carry[1] + m[0] * value[0] + m[1] * value[1])

        zero = jnp.zeros((CELL, chan), F32)
        return loop(CHUNKS, body, (zero, zero))

    def temporal_back(k, weight, works=()):
        works = list(works) + [None] * 2
        copies = send_frames(k)
        e3 = r.e3
        for c0, cw in ((0, 512), (512, mid - 512)):
            r.grad_mid[:, c0 : c0 + cw] = nt(e3[1], weight[mid + c0 : mid + c0 + cw, :])
        if works[0]:
            works[0]()
        take_frames(k, copies)

        def body(i, _):
            before, after = shifted(i)
            e3[0, rows_of(i * CHUNK, CHUNK), :] = after.reshape(CHUNK, chan).astype(BF16)
            e3[2, rows_of(i * CHUNK, CHUNK), :] = before.reshape(CHUNK, chan).astype(BF16)
            return 0

        loop(CHUNKS, body, 0)
        share = share_e3(k)
        for c0, cw in ((0, 512), (512, mid - 512)):
            r.grad_mid[:, c0 : c0 + cw] += nt(e3[0], weight[c0 : c0 + cw, :]) + nt(
                e3[2], weight[2 * mid + c0 : 2 * mid + c0 + cw, :]
            )
        return share

    def share(k, src, dst):
        copy = rc(src, dst, r.share_send.at[k], r.share_recv.at[k], sibling)
        copy.start()
        return copy

    outs = (r.out1s, r.out1t, r.out2s, r.out2t)

    halves = ((0, 512), (512, mid - 512))

    def e_part(n, slot):
        c0, cw = halves[n]
        return r.e_all.at[slot * ROWS : (slot + 1) * ROWS, c0 : c0 + cw]

    def e_copies(k, n):
        sems = [(r.e_send.at[k, n, m], r.e_recv.at[k, n, m]) for m in range(3)]
        return [
            rc(e_part(n, 0), e_part(n, 1), *sems[0], sibling),
            rc(e_part(n, 0), e_part(n, 2), *sems[1], beside),
            rc(e_part(n, 2), e_part(n, 3), *sems[2], sibling),
        ]

    def share_e(k):
        for n in (0, 1):
            near, over, _ = e_copies(k, n)
            over.start()
            near.start()

    def share_e_on(k, n):
        _, over, far = e_copies(k, n)
        over.wait_recv()
        far.start()

    def share_e_wait(k, n):
        near, over, far = e_copies(k, n)
        near.wait()
        over.wait_send()
        far.wait()

    def share_x(k, xa, xq):
        copies = []
        for n, dev in enumerate((sibling, beside, (1 - h, 1 - w, b))):
            lanes = rows_of((2 * dev[1] + dev[0]) * quarter, quarter, 128)
            main = pl.ds(MAIN, ROWS)
            copies.append(
                rc(xa.at[main, lanes], xq.at[n, 0, main, :], r.xq_send.at[k, n], r.xq_recv.at[k, n], dev)
            )
            copies[-1].start()
        return copies

    def pads(ref_a, ref_b, width):
        ref_a[0:MAIN, :] = jnp.zeros((MAIN, width), BF16)
        ref_a[MAIN + ROWS : PADDED, :] = jnp.zeros((PADDED - MAIN - ROWS, width), BF16)
        ref_b[0 : MAIN - CHUNK, :] = jnp.zeros((MAIN - CHUNK, width), BF16)
        ref_b[MAIN - CHUNK + ROWS : PADDED, :] = jnp.zeros((PADDED - MAIN + CHUNK - ROWS, width), BF16)

    def spread_x(xq):
        for n in range(3):
            pads(xq.at[n, 0], xq.at[n, 1], quarter)

        def body(i, before):
            after = []
            for n in range(3):
                v = chunk(xq.at[n, 0], i, MAIN)
                put(xq.at[n, 1], i, jnp.concatenate([before[n][None], v[0:1]], axis=0), MAIN - CHUNK)
                after.append(v[1])
            return tuple(after)

        loop(CHUNKS, body, (jnp.zeros((CELL, quarter), F32),) * 3)

    def share_e3(k):
        return share(
            k - 2, r.e3.at[:, :, rows_of((1 - h) * half, half, 128)], r.sib_e3
        )

    def grad_tap(owner):
        return owner + jnp.where(owner > 2 * shared, 1, 0)

    spare = r.w2s

    def gq(i, row, size):
        return rows_of((mid if i == 0 else 0) + row, size)

    def inbox(i, row, size):
        return rows_of(2 * mid + (mid if i == 0 else 0) + row, size)

    def transpose_x(a, xa, xb, xq, near, far, row):
        lanes = rows_of(shared * quarter, quarter, 128)
        r0 = MAIN - 8 * CELL + 8 * CELL * a
        for j, (c, start) in enumerate(((1, r0 - CHUNK), (0, r0), (1, r0))):
            rows = rows_of(start, ROWS)
            own = (xb if c else xa)[rows, lanes]
            both = jnp.concatenate([own, xq[0, c, rows, :]], axis=0)
            near[rows_of(row + j * quarter, quarter), 0 : 2 * ROWS] = both.T
            both = jnp.concatenate([xq[1, c, rows, :], xq[2, c, rows, :]], axis=0)
            far[rows_of(row + j * quarter, quarter), 0 : 2 * ROWS] = both.T

    def spatial_part(i, near, far, row, out_row, n):
        c0, cw = halves[n]
        rows = rows_of(row, 3 * quarter)
        acc = nn(near[rows, 0 : 2 * ROWS], r.e_all[0 : 2 * ROWS, c0 : c0 + cw])
        acc += nn(far[rows, 0 : 2 * ROWS], r.e_all[2 * ROWS : 4 * ROWS, c0 : c0 + cw])
        spare[gq(i, out_row, 3 * quarter), c0 : c0 + cw] = acc.astype(BF16)

    def transposes(xa, xb, xq, near, far):
        def body(a, _):
            transpose_x(a, xa, xb, xq, near, far, a * 3 * quarter)
            return 0

        lax.fori_loop(0, 3, body, 0)

    def spatial_half(i, near, far, n):
        def body(a, _):
            spatial_part(i, near, far, a * 3 * quarter, a * 3 * quarter, n)
            return 0

        lax.fori_loop(0, 3, body, 0)

    def transpose_v(v, sv):
        for c in range(mid // 128):
            lanes = pl.ds(128 * c, 128)
            r.xt[128 * c : 128 * c + 128, :] = jnp.concatenate([v[:, lanes], sv[:, lanes]], axis=0).T

    def temporal_grad(i, k):
        e = jnp.concatenate([r.e3[k, :, rows_of(h * half, half, 128)], r.sib_e3[k]], axis=0)
        whole[i][k * mid : (k + 1) * mid, 0:half] = nn(r.xt[...], e).astype(BF16)

    def cols_of(n):
        c0, cw = halves[n]
        return pl.ds(c0, cw)

    def s_block(i, n, owner):
        return spare.at[gq(i, grad_tap(owner) * quarter, quarter), cols_of(n)]

    def s_extra(i, n, side):
        return spare.at[gq(i, (2 * shared + 1) * quarter + side * 64, 64), cols_of(n)]

    def t_block(i, owner):
        return whole[i].at[rows_of(owner * temp, temp), 0:half]

    def t_inbox(i, n):
        return whole[i].at[rows_of(n * temp, temp), half:chan]

    def parts_of(i):
        return (0, 1) if i % 2 == 0 else (0,)

    def block_of(i, n, owner):
        return s_block(i, n, owner) if i % 2 == 0 else t_block(i, owner)

    def y_box(i, n, place):
        return spare.at[inbox(i, place * quarter, quarter), cols_of(n)] if i % 2 == 0 else t_inbox(i, place)

    def z_box(i, n, place):
        return spare.at[inbox(i, 576 + place * quarter, quarter), cols_of(n)] if i % 2 == 0 else t_inbox(i, 4 + place)

    def extra_y_box(i, n):
        return spare.at[inbox(i, 4 * quarter, 64), cols_of(n)]

    def extra_z_box(i, n, place):
        return spare.at[inbox(i, 576 + 3 * quarter + place * 64, 64), cols_of(n)]

    def add_into(dst, parts, step):
        rows, cols = dst.shape

        def body(n, _):
            at_rows = rows_of(n * step, step)
            value = dst[at_rows, :].astype(F32)
            for part in parts:
                value = value + part[at_rows, :].astype(F32)
            dst[at_rows, :] = value.astype(BF16)
            return 0

        lax.fori_loop(0, rows // step, body, 0)

    def y_copy(i, n, d):
        place = lax.rem(bh + d, depth)
        src = block_of(i, n, 2 * place + 1 - par)
        return rc(src, y_box(i, n, place), r.y_send.at[i, n, d], r.y_recv.at[i, n, place], across)

    def z_copy(i, n, d):
        place = lax.rem(bh + d, depth)
        src = block_of(i, n, 2 * place + par)
        dev = (h, w, 2 * place + par)
        return rc(src, z_box(i, n, 3 - d), r.z_send.at[i, n, d], r.z_recv.at[i, n, 3 - d], dev)

    def extra_y(i, n):
        return rc(s_extra(i, n, 1 - par), extra_y_box(i, n), r.y_send.at[i, n, 4], r.y_recv.at[i, n, 4], across)

    def extra_z(i, n):
        place = jnp.minimum(lax.rem(bh - shared + 3 + depth, depth), 2)
        dev = (h, w, 2 * shared + par)
        return rc(
            s_extra(i, n, par), extra_z_box(i, n, place), r.z_send.at[i, n, 4], r.z_recv.at[i, n, 4 + place], dev
        )

    def step_of(i):
        return 16 if i % 2 == 0 else 48

    def reduce_start(i, n):
        for d in (1, 2, 3, 0):
            y_copy(i, n, d).start()
        if i % 2 == 0:
            extra_y(i, n).start()

    def reduce_middle(i, n):
        for d in (1, 2, 3, 0):
            place = lax.rem(bh + d, depth)
            y_copy(i, n, d).wait_send()
            box = y_box(i, n, place)
            rc(box, box, r.y_send.at[i, n, d], r.y_recv.at[i, n, place], across).wait_recv()
            add_into(block_of(i, n, 2 * place + par), [box], step_of(i))
            if d:
                z_copy(i, n, d).start()
        if i % 2 == 0:
            extra_y(i, n).wait()
            add_into(s_extra(i, n, par), [extra_y_box(i, n)], 16)
            pl.when(bh != shared)(lambda: extra_z(i, n).start())

    def final_part(i, n, side, core):
        place = 2 * side + core
        start = quarter * place - 64 * b + 512 * jnp.where(b > 2 * place, 1, 0)
        return outs[i].at[rows_of(start, quarter, 64), cols_of(n)]

    def extra_part(i, n):
        return outs[i].at[rows_of(512 * (1 - par), 64, 64), cols_of(n)]

    def final_copies(i, n):
        if i % 2:
            src = t_block(i, b)
            part = outs[i].at[h]
            return lc(src, part, r.out_sem.at[i, 0, 0]), [
                (src, part, sibling, r.cast_send.at[i, 0, 0], r.cast_recv.at[i, 0, 0])
            ]
        src = s_block(i, n, b)
        part = final_part(i, n, w, h)
        sends = [
            (src, part, dev, r.cast_send.at[i, n, d], r.cast_recv.at[i, n, d]) for d, dev in enumerate((beside, sibling))
        ]
        return lc(src, part, r.out_sem.at[i, n, 0]), sends

    def extra_copies(i, n):
        src = s_extra(i, n, par)
        part = extra_part(i, n)
        sends = [
            (src, part, dev, r.cast_send.at[i, n, 3 + d], r.cast_recv.at[i, n, 3 + d])
            for d, dev in enumerate((beside, sibling))
        ]
        return lc(src, part, r.out_sem.at[i, n, 1]), sends

    def begin(copies):
        local, sends = copies
        for src, part, dev, one, two in sends:
            rc(src, part, one, two, dev).start()
        local.start()

    def credit(n):
        pl.semaphore_signal(r.credit.at[n], inc=1, device_id=named(beside), device_id_type=MESH)

    def credited(n):
        pl.semaphore_wait(r.credit.at[n], 1)

    def beside_copy(i):
        return rc(t_block(i, b), t_inbox(i, 7), r.z_send.at[i, 0, 4], r.z_recv.at[i, 0, 4], beside)

    def reduce_last(i, n):
        for d in (1, 2, 3):
            z_copy(i, n, d).wait()
        add_into(block_of(i, n, b), [z_box(i, n, place) for place in range(3)], step_of(i))
        if i % 2:
            credited(i // 2)
            beside_copy(i).start()
            return
        begin(final_copies(i, n))

        @pl.when(bh != shared)
        def _():
            extra_z(i, n).wait_send()

        @pl.when(bh == shared)
        def _():
            boxes = [extra_z_box(i, n, place) for place in range(3)]
            for place, box in enumerate(boxes):
                rc(box, box, r.z_send.at[i, n, 4], r.z_recv.at[i, n, 4 + place], across).wait_recv()
            add_into(s_extra(i, n, par), boxes, 16)
            begin(extra_copies(i, n))

    def reduce_out(i):
        beside_copy(i).wait()
        add_into(t_block(i, b), [t_inbox(i, 7)], 48)
        begin(final_copies(i, 0))

    def final_on(i, n):
        def move(part, d):
            rc(part, part, r.cast_send.at[i, n, d], r.cast_recv.at[i, n, d], beside).wait_recv()
            rc(part, part, r.cast_send.at[i, n, d + 2], r.cast_recv.at[i, n, d + 2], sibling).start()

        move(final_part(i, n, 1 - w, h), 0)
        pl.when(bh == shared_beside)(lambda: move(extra_part(i, n), 3))

    def reduce_wait(i, n):
        local, sends = final_copies(i, n)
        local.wait()
        if i % 2:
            src, part, dev, one, two = sends[0]
            rc(src, outs[i].at[1 - h], one, two, dev).wait()
            return
        for src, part, dev, one, two in sends:
            rc(src, part, one, two, dev).wait_send()

        def far(part, d):
            return rc(part, part, r.cast_send.at[i, n, d], r.cast_recv.at[i, n, d], sibling)

        far(final_part(i, n, w, 1 - h), 1).wait_recv()
        far(final_part(i, n, 1 - w, h), 2).wait_send()
        far(final_part(i, n, 1 - w, 1 - h), 2).wait_recv()
        local, sends = extra_copies(i, n)

        @pl.when(bh == shared)
        def _():
            local.wait()
            for src, part, dev, one, two in sends:
                rc(src, part, one, two, dev).wait_send()

        pl.when(bh == shared_beside)(lambda: far(extra_part(i, n), 5).wait_send())
        pl.when(bh == 2 * w + 1 - h)(lambda: far(extra_part(i, n), 4).wait_recv())
        pl.when(bh == 2 * (1 - w) + 1 - h)(lambda: far(extra_part(i, n), 5).wait_recv())

    def tile_of(ref, jh, jw):
        return ref.at[rows_of(jh * 4, 4, 4), rows_of(jw * 32, 32), :]

    def scatter(src, dst, n):
        copies = []
        for d, (j, dev) in enumerate(tile_group):
            copies.append(
                rc(src.at[j], tile_of(dst, h, w), r.tile_send.at[n, d], r.tile_recv.at[n, mine], dev)
            )
        return copies

    def scattered(src, dst, n):
        for d, (j, dev) in enumerate(tile_group):
            jh, jw = at_group(j)
            rc(src.at[j], tile_of(dst, jh, jw), r.tile_send.at[n, d], r.tile_recv.at[n, j], dev).wait()

    def tiles_start(src, dst, n):
        for copy in scatter(src, dst, n):
            copy.start()
        lc(src.at[mine], tile_of(dst, h, w), r.tile_own.at[n]).start()

    def tiles_wait(src, dst, n):
        scattered(src, dst, n)
        lc(src.at[mine], tile_of(dst, h, w), r.tile_own.at[n]).wait()

    xg, cg = r.x_grid, r.cot_grid
    tiles_start(r.x_tiles, xg, 0)
    gather_start(0)
    r.param[...] = total(0, mid, r.param_in[...])
    tiles_wait(r.x_tiles, xg, 0)

    def grid_chunk(ref, i):
        v = ref[lax.div(i, 4), rows_of(lax.rem(i, 4) * CHUNK, CHUNK), :]
        return v.astype(F32).reshape(2, CELL, chan)

    fill(r.xa, r.xb, lambda i: grid_chunk(xg, i), chan)

    def pump_loop(i, lo, hi):
        def body(s, _):
            gather_pump(i, s)
            return 0

        lax.fori_loop(lo, hi, body, 0)

    pump_loop(0, 1, nb - 3)
    gather_start(1)
    pump_loop(0, nb - 3, nb - 1)
    gather_start(2)
    gather_pump(0, nb - 1)
    gather_pump(1, 1)
    gather_pump(2, 1)
    gather_pump(1, 2)
    gather_finish(0)

    def first_pump(n):
        pl.when(lax.rem(n, 2) == 0)(lambda: gather_pump(1, 3 + lax.div(n, 2)))
        pl.when(n == 3)(lambda: gather_pump(2, 2))

    conv(r.xa, r.xb, r.w1s, r.mid1, first_pump)
    def first_last():
        gather_pump(2, 3)
        gather_pump(1, nb - 1)

    sums = total(
        1,
        mid,
        packed(*moments(r.mid1, mid), mid),
        [lambda: gather_pump(1, nb - 2), first_last],
    )
    prepare(0, sums, mid)

    def hidden(src, n, dst):
        value = activated(src, n, mid)

        def body(i, _):
            put(dst, i, value(i))
            return 0

        loop(CHUNKS, body, 0)

    hidden(r.mid1, 0, r.v1)
    gather_pump(2, 4)
    gather_finish(1)
    stats = temporal(0, r.v1, r.w1t, r.time1, [lambda: gather_pump(2, 5)])

    def sixth():
        gather_pump(2, 6)

    sums = total(2, chan, packed(*stats, chan), [lambda: gather_start(3), sixth])
    prepare(1, sums, chan)
    fill(r.aa, r.ab, activated(r.time1, 1, chan), chan)
    gather_pump(3, 1)
    gather_pump(2, nb - 1)
    gather_pump(3, 2)
    gather_finish(2)
    tiles_start(r.cot_tiles, cg, 1)

    def second_pump(n):
        pl.when(n < nb - 3)(lambda: gather_pump(3, 3 + n))

    conv(r.aa, r.ab, r.w2s, r.mid2, second_pump)
    sums = total(3, mid, packed(*moments(r.mid2, mid), mid), [lambda: gather_finish(3)])
    prepare(2, sums, mid)
    hidden(r.mid2, 2, r.v2)
    stats = temporal(1, r.v2, r.w2t, r.time2)
    shared_xq2 = share_x(0, r.aa, r.xq2)
    shared_xq1 = share_x(1, r.xa, r.xq1)
    for i in range(4):
        gather_sent(i)
    share_v2 = share(4, r.v2, r.sib_v)
    sums = total(4, chan, packed(*stats, chan))
    tiles_wait(r.cot_tiles, cg, 1)
    prepare(3, sums, chan)

    out_grid = r.out_grid

    def grid_put(ref, i, v):
        ref[lax.div(i, 4), rows_of(lax.rem(i, 4) * CHUNK, CHUNK), :] = v.reshape(CHUNK, chan).astype(ref.dtype)

    def slope(y, s):
        return s * (1.0 + y * (1.0 - s))

    def pre_body(i, carry):
        scale, shift, inv, offset = tiles(3, chan)
        v = chunk(r.time2, i)
        y = v * scale + shift + chunk(r.xa, i, MAIN)
        s = sigmoid(y)
        m = keep(i)
        grid_put(out_grid, i, y * s * m)
        d = grid_chunk(cg, i) * m * slope(y, s)
        put(r.grad_pre, i, d)
        t = d * (v * inv - offset)
        return (carry[0] + d[0] + d[1], carry[1] + t[0] + t[1])

    zero_out = jnp.zeros((CELL, chan), F32)
    zero_mid = jnp.zeros((CELL, mid), F32)
    out_grid[HGT] = jnp.zeros((8 * CELL, chan), BF16)
    gg = loop(CHUNKS, pre_body, (zero_out, zero_out))

    def send_tiles(src, dst, n):
        for d, (j, dev) in enumerate(tile_group):
            jh, jw = at_group(j)
            rc(tile_of(src, jh, jw), dst.at[mine], r.tile_send.at[n, d], r.tile_recv.at[n, mine], dev).start()
        lc(tile_of(src, h, w), dst.at[mine], r.tile_own.at[n]).start()

    def sent_tiles(src, dst, n):
        for d, (j, dev) in enumerate(tile_group):
            jh, jw = at_group(j)
            rc(tile_of(src, jh, jw), dst.at[j], r.tile_send.at[n, d], r.tile_recv.at[n, j], dev).wait()
        lc(tile_of(src, h, w), dst.at[mine], r.tile_own.at[n]).wait()

    send_tiles(out_grid, r.block_out, 2)

    def norm_back(n, sums, width):
        r.norm_part[0, 2 * n : 2 * n + 1, 0:width] = sums[1:2]
        r.norm_part[0, 2 * n + 1 : 2 * n + 2, 0:width] = sums[0:1]
        back = r.back
        back[0, :, 0:width] = jnp.broadcast_to(sums[0:1] / cell_count, (CELL, width))
        back[1, :, 0:width] = jnp.broadcast_to(sums[1:2] / cell_count, (CELL, width))

    def through_norm(n, src, grad, i, width):
        scale, _, inv, offset = tiles(n, width)
        xhat = chunk(src, i) * inv - offset
        bias_part = r.back[0, :, 0:width][None]
        gain_part = r.back[1, :, 0:width][None]
        return scale * (chunk(grad, i, 0, width) - bias_part - xhat * gain_part) * keep(i)

    def through_act(n, src, grad, width):
        def body(i, carry):
            scale, shift, inv, offset = tiles(n, width)
            v = chunk(src, i)
            y = v * scale + shift
            s = sigmoid(y)
            d = chunk(grad, i, 0, width) * keep(i) * slope(y, s)
            put(grad, i, d, 0, width)
            t = d * (v * inv - offset)
            return (carry[0] + d[0] + d[1], carry[1] + t[0] + t[1])

        zero = jnp.zeros((CELL, width), F32)
        return loop(CHUNKS, body, (zero, zero))

    def to_frames(n, src, grad):
        def body(i, _):
            e = through_norm(n, src, grad, i, chan).astype(BF16)
            ef = e.astype(F32)
            r.e3[1, rows_of(i * CHUNK, CHUNK), :] = e.reshape(CHUNK, chan)
            put_lanes(r.down, rows_of(i * CHUNK + CELL, CHUNK, CELL), ef.reshape(CHUNK, chan))
            put_lanes(r.up, rows_of(i * CHUNK, CHUNK), (ef * r.gate[...][None]).reshape(CHUNK, chan))
            return 0

        loop(CHUNKS, body, 0)

    sums = total(5, chan, packed(*gg, chan))
    norm_back(3, sums, chan)
    to_frames(3, r.time2, r.grad_pre)
    shared_e3 = temporal_back(2, r.w2t)
    credit(1)
    gg = through_act(2, r.mid2, r.grad_mid, mid)
    shared_e3.wait()
    share_v2.wait()
    def temporal_grads(i, v):
        def first():
            transpose_v(v, r.sib_v)
            temporal_grad(i, 0)

        def others():
            temporal_grad(i, 1)
            temporal_grad(i, 2)

        return [first, others]

    sums = total(6, mid, packed(*gg, mid), temporal_grads(3, r.v2))
    reduce_start(3, 0)
    norm_back(2, sums, mid)

    def fill_e(n, src):
        def value(i):
            v = through_norm(n, src, r.grad_mid, i, mid)
            put(r.e_all, i, v)
            return v

        fill(r.ea, r.eb, value, mid)

    fill_e(2, r.mid2)
    share_e(0)
    conv_back(r.ea, r.eb, r.w2s, r.grad_mid)
    share_e_on(0, 0)
    gg = through_act(1, r.time1, r.grad_mid, chan)
    for copy in shared_xq2:
        copy.wait()
    near, far = spare.at[mid : 2 * mid, :], spare.at[3 * mid : 4 * mid, :]

    def spread_and_turn():
        spread_x(r.xq2)
        transposes(r.aa, r.ab, r.xq2, near, far)

    def first_half():
        share_e_wait(0, 0)
        spatial_half(2, near, far, 0)

    sums = total(7, chan, packed(*gg, chan), [spread_and_turn, first_half])
    share_e_on(0, 1)
    reduce_start(2, 0)
    reduce_middle(3, 0)
    share_v1 = share(5, r.v1, r.sib_v)
    norm_back(1, sums, chan)
    to_frames(1, r.time1, r.grad_mid)

    def second_half():
        share_e_wait(0, 1)
        spatial_half(2, near, far, 1)
        credit(2)
        reduce_start(2, 1)

    shared_e3 = temporal_back(3, r.w1t, [second_half])
    credit(0)
    reduce_last(3, 0)
    gg = through_act(0, r.mid1, r.grad_mid, mid)
    shared_e3.wait()
    share_v1.wait()
    sums = total(8, mid, packed(*gg, mid), temporal_grads(1, r.v1))
    reduce_start(1, 0)
    norm_back(0, sums, mid)
    fill_e(0, r.mid1)
    credited(2)
    share_e(1)
    reduce_out(3)
    for n in (0, 1):
        reduce_middle(2, n)
    for copy in shared_xq1:
        copy.wait()
    spread_x(r.xq1)
    sent_tiles(out_grid, r.block_out, 2)
    conv_back(r.ea, r.eb, r.w1s, r.grad_mid)
    share_e_on(1, 0)
    near, far = r.w1s.at[0:mid, :], r.w1s.at[mid : 2 * mid, :]
    transposes(r.xa, r.xb, r.xq1, near, far)
    share_e_wait(1, 0)
    spatial_half(0, near, far, 0)
    reduce_start(0, 0)
    share_e_on(1, 1)
    share_e_wait(1, 1)
    spatial_half(0, near, far, 1)
    reduce_start(0, 1)

    norm_copy = rc(r.norm_part.at[0], r.norm_part.at[1], r.norm_sem.at[0], r.norm_sem.at[1], beside)
    norm_copy.start()

    def last_body(i, _):
        grid_put(out_grid, i, (chunk(r.grad_mid, i, 0, chan) + chunk(r.grad_pre, i)) * keep(i))
        return 0

    loop(CHUNKS, last_body, 0)
    send_tiles(out_grid, r.grad_input, 3)
    for n in (0, 1):
        reduce_last(2, n)
    reduce_middle(1, 0)
    for n in (0, 1):
        final_on(2, n)
    reduce_middle(0, 0)
    reduce_last(1, 0)
    reduce_out(1)
    reduce_last(0, 0)
    reduce_middle(0, 1)
    final_on(0, 0)
    reduce_last(0, 1)
    norm_copy.wait()
    r.norm_grads[...] = r.norm_part[0] + r.norm_part[1]
    sent_tiles(out_grid, r.grad_input, 3)
    for n in (0, 1):
        reduce_wait(2, n)
    reduce_wait(3, 0)
    final_on(0, 1)
    reduce_wait(1, 0)
    for n in (0, 1):
        reduce_wait(0, n)


def per_device_fast(nb, *args):
    (
        inputs,
        starts,
        first_spatial,
        first_mid_gain,
        first_mid_bias,
        first_temporal,
        first_out_gain,
        first_out_bias,
        second_spatial,
        second_mid_gain,
        second_mid_bias,
        second_temporal,
        second_out_gain,
        second_out_bias,
        cotangent,
    ) = args
    micro, frames, side, _, chan = inputs.shape
    mid = first_spatial.shape[1]
    spat, temp = first_spatial.shape[0], first_temporal.shape[0]
    h, w, b = (lax.axis_index(name) for name in ("ha", "wa", "batch"))
    few = frames // 2
    offsets = jnp.arange(side)
    valid = (h * side + offsets < HGT)[:, None] & (w * side + offsets < HGT)[None, :]

    def tiles(array):
        array = array * valid.astype(BF16)[None, None, :, :, None]
        array = array.reshape(micro, 2, few, side, side, chan).transpose(0, 1, 3, 4, 2, 5)
        return array.reshape(4, side, side * few, chan)

    def untiled(array):
        array = array.reshape(micro, 2, side, side, few, chan).transpose(0, 1, 4, 2, 3, 5)
        return array.reshape(micro, frames, side, side, chan).astype(F32)

    gate = (1 - lax.dynamic_slice(starts, (w, h * few), (1, few))).astype(F32)
    gate = jnp.broadcast_to(gate.reshape(few, 1), (few, chan))
    here = jnp.where(h == 0, 1.0, 0.0)

    def placed(shard):
        row = jnp.zeros((mid,), F32)
        return lax.dynamic_update_slice(row, shard.astype(F32) * here, (b * shard.shape[0],))

    param = jnp.stack(
        [
            placed(v)
            for v in (
                first_mid_gain,
                first_mid_bias,
                first_out_gain,
                first_out_bias,
                second_mid_gain,
                second_mid_bias,
                second_out_gain,
                second_out_bias,
            )
        ]
    )
    half = chan // 2
    few_rows = ROWS // CELL

    inputs_of = dict(
        x_tiles=(tiles(inputs), pl.ANY),
        cot_tiles=(tiles(cotangent), pl.ANY),
        gate=(gate, pltpu.VMEM),
        param_in=(param, pltpu.VMEM),
        first_spatial=(first_spatial, pl.ANY),
        first_temporal=(first_temporal, pl.ANY),
        second_spatial=(second_spatial, pl.ANY),
        second_temporal=(second_temporal, pl.ANY),
    )
    outputs_of = dict(
        block_out=((4, side, side * CELL, chan), BF16, pl.ANY),
        grad_input=((4, side, side * CELL, chan), BF16, pl.ANY),
        norm_grads=((8, mid), F32, pltpu.VMEM),
        out1s=((spat, mid), BF16, pl.ANY),
        out1t=((2, temp, half), BF16, pl.ANY),
        out2s=((spat, mid), BF16, pl.ANY),
        out2t=((2, temp, half), BF16, pl.ANY),
    )
    dma = pltpu.SemaphoreType.DMA
    scratch_of = dict(
        w1s=pltpu.VMEM((9 * chan, mid), BF16),
        w1t=pltpu.VMEM((3 * mid, chan), BF16),
        w2s=pltpu.VMEM((9 * chan, mid), BF16),
        w2t=pltpu.VMEM((3 * mid, chan), BF16),
        x_grid=pltpu.VMEM((8, 8 * CELL, chan), BF16),
        cot_grid=pltpu.VMEM((8, 8 * CELL, chan), BF16),
        out_grid=pltpu.VMEM((8, 8 * CELL, chan), BF16),
        xa=pltpu.VMEM((PADDED, chan), BF16),
        xb=pltpu.VMEM((PADDED, chan), BF16),
        aa=pltpu.VMEM((PADDED, chan), BF16),
        ab=pltpu.VMEM((PADDED, chan), BF16),
        ea=pltpu.VMEM((PADDED, mid), BF16),
        eb=pltpu.VMEM((PADDED, mid), BF16),
        mid1=pltpu.VMEM((ROWS, mid), F32),
        mid2=pltpu.VMEM((ROWS, mid), F32),
        grad_mid=pltpu.VMEM((ROWS, mid), F32),
        v1=pltpu.VMEM((ROWS, mid), BF16),
        v2=pltpu.VMEM((ROWS, mid), BF16),
        time1=pltpu.VMEM((ROWS, chan), F32),
        time2=pltpu.VMEM((ROWS, chan), F32),
        grad_pre=pltpu.VMEM((ROWS, chan), F32),
        down=pltpu.VMEM((chan // 128, ROWS + CHUNK, 128), F32),
        up=pltpu.VMEM((chan // 128, ROWS + CHUNK, 128), F32),
        e3=pltpu.VMEM((3, ROWS, chan), BF16),
        sib_e3=pltpu.VMEM((3, ROWS, half), BF16),
        halo_out=pltpu.VMEM((2, few_rows, chan), F32),
        halo_in=pltpu.VMEM((4, 2, few_rows, chan), F32),
        param=pltpu.VMEM((8, mid), F32),
        tile_mid=pltpu.VMEM((2, 4, CELL, mid), F32),
        tile_out=pltpu.VMEM((2, 4, CELL, chan), F32),
        back=pltpu.VMEM((2, CELL, mid), F32),
        norm_part=pltpu.VMEM((2, 8, mid), F32),
        sum_b=pltpu.VMEM((2, 4, 8, mid), F32),
        sum_c=pltpu.VMEM((2, nb // 2, 8, mid), F32),
        own_sem=dma((4,)),
        ring_send=dma((4, 2, 2, nb)),
        ring_recv=dma((4, 2, 2, nb)),
        sib_send=dma((4, 3, 2, nb)),
        sib_recv=dma((4, 3, 2, nb)),
        over_send=dma((4, 2, nb)),
        over_recv=dma((4, 2, nb)),
        norm_sem=dma((2,)),
        credit=pltpu.SemaphoreType.REGULAR((3,)),
        sb_send=dma((9, 3)),
        sb_recv=dma((9, 4)),
        sc_send=dma((9, nb // 2)),
        sc_recv=dma((9, nb // 2)),
        halo_send=dma((4, 2)),
        halo_recv=dma((4, 2)),
        share_send=dma((6,)),
        share_recv=dma((6,)),
        e_all=pltpu.VMEM((4 * ROWS, mid), BF16),
        xq1=pltpu.VMEM((3, 2, PADDED, chan // 4), BF16),
        xq2=pltpu.VMEM((3, 2, PADDED, chan // 4), BF16),
        xt=pltpu.VMEM((mid, 2 * ROWS), BF16),
        sib_v=pltpu.VMEM((ROWS, mid), BF16),
        e_send=dma((2, 2, 3)),
        e_recv=dma((2, 2, 3)),
        xq_send=dma((2, 3)),
        xq_recv=dma((2, 3)),
        y_send=dma((4, 2, 5)),
        y_recv=dma((4, 2, 5)),
        z_send=dma((4, 2, 5)),
        z_recv=dma((4, 2, 7)),
        cast_send=dma((4, 2, 6)),
        cast_recv=dma((4, 2, 8)),
        out_sem=dma((4, 2, 2)),
        tile_send=dma((4, 3)),
        tile_recv=dma((4, 4)),
        tile_own=dma((4,)),
    )
    names = (*inputs_of, *outputs_of, *scratch_of)
    cell_count = float(frames * nb * HGT * HGT)
    results = pl.pallas_call(
        functools.partial(block_kernel, (nb, chan, mid, cell_count), names),
        out_shape=[jax.ShapeDtypeStruct(shape, dtype) for shape, dtype, _ in outputs_of.values()],
        in_specs=[pl.BlockSpec(memory_space=space) for _, space in inputs_of.values()],
        out_specs=[pl.BlockSpec(memory_space=space) for _, _, space in outputs_of.values()],
        scratch_shapes=list(scratch_of.values()),
        compiler_params=pltpu.CompilerParams(
            collective_id=0, has_side_effects=True, vmem_limit_bytes=VMEM_LIMIT
        ),
    )(*(array for array, _ in inputs_of.values()))
    got = SimpleNamespace(**dict(zip(outputs_of, results)))

    def temporal(pair):
        return jnp.concatenate([pair[0], pair[1]], axis=1).astype(F32)

    def norm(row, like):
        size = like.shape[0]
        return lax.dynamic_slice_in_dim(got.norm_grads[row], b * size, size)

    return (
        untiled(got.block_out),
        untiled(got.grad_input),
        got.out1s.astype(F32),
        norm(0, first_mid_gain),
        norm(1, first_mid_bias),
        temporal(got.out1t),
        norm(2, first_out_gain),
        norm(3, first_out_bias),
        got.out2s.astype(F32),
        norm(4, second_mid_gain),
        norm(5, second_mid_bias),
        temporal(got.out2t),
        norm(6, second_out_gain),
        norm(7, second_out_bias),
    )


def extended(shard, sides, width):
    for axis, dim in sides:
        count, length = (lax.axis_size(axis), shard.shape[dim])
        up = [(i, (i + 1) % count) for i in range(count - 1)]
        down = [(j, i) for i, j in up]
        last = lax.slice_in_dim(shard, length - width, length, axis=dim)
        leading = lax.slice_in_dim(shard, 0, width, axis=dim)
        before = lax.ppermute(last, axis, up)
        after = lax.ppermute(leading, axis, down)
        shard = jnp.concatenate([before, shard, after], axis=dim)
    return shard


def passed_along(shard, axis, by):
    count = lax.axis_size(axis)
    pairs = [(i, i + by) for i in range(count) if 0 <= i + by < count]
    return lax.ppermute(shard, axis, pairs)


def for_sending(shard):

    def short(part):
        return part.astype(jnp.bfloat16) if part.dtype == jnp.float32 else part

    return jax.tree.map(short, shard)


def silu_slope(values):
    sigma = jax.nn.sigmoid(values)
    return sigma * (1.0 + values * (1.0 - sigma))


def spatial_forward(field_in, kernel):
    frames, tile_side = (field_in.shape[0], field_in.shape[1])
    padded = extended(field_in, (("ha", 1), ("wa", 2)), 1)
    pieces = [
        padded[:, offset // 3 : offset // 3 + tile_side, offset % 3 : offset % 3 + tile_side, :]
        for offset in range(9)
    ]
    patches = jnp.concatenate(pieces, axis=-1).reshape(frames * tile_side * tile_side, -1)
    return (patches, jnp.dot(patches, kernel, preferred_element_type=jnp.float32))


def spatial_backward(grad_out, patches, kernel):
    frames, tile_side, channels = (grad_out.shape[0], grad_out.shape[1], grad_out.shape[3])
    row_count = frames * tile_side * tile_side
    padded = extended(grad_out, (("ha", 1), ("wa", 2)), 1)
    pieces = [
        padded[
            :,
            2 - offset // 3 : 2 - offset // 3 + tile_side,
            2 - offset % 3 : 2 - offset % 3 + tile_side,
            :,
        ]
        for offset in range(9)
    ]
    stacked = jnp.concatenate(pieces, axis=-1).reshape(row_count, 9, channels)
    grad_in = jnp.einsum(
        "rkm,kcm->rc", stacked, kernel.reshape(9, -1, channels), preferred_element_type=jnp.float32
    )
    grad_kernel = jnp.einsum(
        "rk,rm->km",
        patches,
        grad_out.reshape(row_count, channels),
        preferred_element_type=jnp.float32,
    )
    return (grad_in, grad_kernel)


def temporal_forward(field_in, clip_gate, kernel):
    frames, tile_side = (field_in.shape[0], field_in.shape[1])
    gated_in = field_in * clip_gate
    earlier = passed_along(field_in[-1:], "batch", 1)
    later_frame = passed_along(gated_in[:1], "batch", -1)
    before = jnp.concatenate([earlier, field_in[:-1]], axis=0) * clip_gate
    after_tap = jnp.concatenate([gated_in[1:], later_frame], axis=0)
    joined = jnp.concatenate([before, field_in, after_tap], axis=-1).reshape(
        frames * tile_side * tile_side, -1
    )
    return (joined, jnp.dot(joined, kernel, preferred_element_type=jnp.float32))


def temporal_backward(grad_out, joined, clip_gate, kernel):
    frames, tile_side, channels = (grad_out.shape[0], grad_out.shape[1], grad_out.shape[3])
    row_count = frames * tile_side * tile_side
    gated_grad = grad_out * clip_gate
    later_frame = passed_along(gated_grad[:1], "batch", -1)
    earlier = passed_along(grad_out[-1:], "batch", 1)
    from_later = jnp.concatenate([gated_grad[1:], later_frame], axis=0)
    from_earlier = jnp.concatenate([earlier, grad_out[:-1]], axis=0) * clip_gate
    stacked = jnp.concatenate([from_later, grad_out, from_earlier], axis=-1).reshape(
        row_count, 3, channels
    )
    grad_in = jnp.einsum(
        "rkc,kmc->rm", stacked, kernel.reshape(3, -1, channels), preferred_element_type=jnp.float32
    )
    grad_kernel = jnp.einsum(
        "rk,rc->kc",
        joined,
        grad_out.reshape(row_count, channels),
        preferred_element_type=jnp.float32,
    )
    return (grad_in, grad_kernel)


def norm_forward(pre_norm, norm_gain, norm_bias, valid_rows, cell_count):
    first_sum = jnp.sum(pre_norm * valid_rows, axis=0)
    square_sum = jnp.sum(pre_norm * pre_norm * valid_rows, axis=0)
    first_sum, square_sum = lax.psum((first_sum, square_sum), ("ha", "wa", "batch"))
    mean_val = first_sum / cell_count
    inv_std = lax.rsqrt(square_sum / cell_count - mean_val * mean_val + epsilon)
    normed = (pre_norm - mean_val) * inv_std
    return (normed, inv_std, normed * norm_gain.astype(jnp.float32) + norm_bias.astype(jnp.float32))


def norm_backward(grad_norm, normed, inv_std, norm_gain, valid_rows, cell_count):
    bias_grad = jnp.sum(grad_norm, axis=0)
    gain_grad = jnp.sum(grad_norm * normed, axis=0)
    bias_grad, gain_grad = lax.psum((bias_grad, gain_grad), ("ha", "wa", "batch"))
    grad_in = (
        valid_rows
        * norm_gain.astype(jnp.float32)
        * inv_std
        * (grad_norm - bias_grad / cell_count - normed * gain_grad / cell_count)
    )
    return (grad_in, gain_grad, bias_grad)


def forward_pair(field_in, weights, clip_gate, valid_rows, cell_count):
    frames, tile_side = (field_in.shape[0], field_in.shape[1])
    patches, spatial_out = spatial_forward(field_in, weights[0])
    mid_hat, mid_scale, mid_norm = norm_forward(
        spatial_out, weights[1], weights[2], valid_rows, cell_count
    )
    hidden = (
        (jax.nn.silu(mid_norm) * valid_rows)
        .astype(jnp.bfloat16)
        .reshape(frames, tile_side, tile_side, -1)
    )
    joined, temporal_out = temporal_forward(hidden, clip_gate, weights[3])
    out_hat, out_scale, out_norm = norm_forward(
        temporal_out, weights[4], weights[5], valid_rows, cell_count
    )
    return ((patches, mid_hat, mid_scale, mid_norm, joined, out_hat, out_scale), out_norm)


def backward_pair(grad_norm, kept, weights, clip_gate, valid_rows, cell_count, tile_side):
    patches, mid_hat, mid_scale, mid_norm, joined, out_hat, out_scale = kept
    frames = clip_gate.shape[0]
    grad_time, out_gain_grad, out_bias_grad = norm_backward(
        grad_norm, out_hat, out_scale, weights[4], valid_rows, cell_count
    )
    grad_time = grad_time.astype(jnp.bfloat16).reshape(frames, tile_side, tile_side, -1)
    grad_hidden, temporal_grad = temporal_backward(grad_time, joined, clip_gate, weights[3])
    grad_mid = grad_hidden * valid_rows * silu_slope(mid_norm)
    grad_spatial, mid_gain_grad, mid_bias_grad = norm_backward(
        grad_mid, mid_hat, mid_scale, weights[1], valid_rows, cell_count
    )
    grad_spatial = grad_spatial.astype(jnp.bfloat16).reshape(frames, tile_side, tile_side, -1)
    grad_in, spatial_grad = spatial_backward(grad_spatial, patches, weights[0])
    return (
        grad_in,
        (spatial_grad, mid_gain_grad, mid_bias_grad, temporal_grad, out_gain_grad, out_bias_grad),
    )


def per_device(
    inputs,
    starts,
    first_spatial,
    first_mid_gain,
    first_mid_bias,
    first_temporal,
    first_out_gain,
    first_out_bias,
    second_spatial,
    second_mid_gain,
    second_mid_bias,
    second_temporal,
    second_out_gain,
    second_out_bias,
    cotangent,
):
    shards = (
        first_spatial,
        first_mid_gain,
        first_mid_bias,
        first_temporal,
        first_out_gain,
        first_out_bias,
        second_spatial,
        second_mid_gain,
        second_mid_bias,
        second_temporal,
        second_out_gain,
        second_out_bias,
    )
    micro_total, frames, tile_side, channels = (
        inputs.shape[0],
        inputs.shape[1],
        inputs.shape[2],
        inputs.shape[4],
    )
    row_count = frames * tile_side * tile_side
    cell_count = frames * lax.axis_size("batch") * HGT * HGT
    offsets = jnp.arange(tile_side)
    inside_h = lax.axis_index("ha") * tile_side + offsets < HGT
    inside_w = lax.axis_index("wa") * tile_side + offsets < HGT
    valid_grid = inside_h[:, None] & inside_w[None, :]
    valid_tile = valid_grid.astype(jnp.bfloat16)[None, :, :, None]
    valid_rows = jnp.broadcast_to(
        valid_grid.astype(jnp.float32)[None], (frames, tile_side, tile_side)
    ).reshape(row_count, 1)
    results = []
    input_grads = []
    kernel_total = None
    norm_total = None
    for micro_step in range(micro_total):
        gathered = (
            lax.all_gather(shards[0], "batch", axis=0, tiled=True),
            lax.all_gather(shards[1], "batch", axis=0, tiled=True),
            lax.all_gather(shards[2], "batch", axis=0, tiled=True),
            lax.all_gather(shards[3], "batch", axis=0, tiled=True),
            lax.all_gather(shards[4], "batch", axis=0, tiled=True),
            lax.all_gather(shards[5], "batch", axis=0, tiled=True),
            lax.all_gather(shards[6], "batch", axis=0, tiled=True),
            lax.all_gather(shards[7], "batch", axis=0, tiled=True),
            lax.all_gather(shards[8], "batch", axis=0, tiled=True),
            lax.all_gather(shards[9], "batch", axis=0, tiled=True),
            lax.all_gather(shards[10], "batch", axis=0, tiled=True),
            lax.all_gather(shards[11], "batch", axis=0, tiled=True),
        )
        clip_gate = (1 - starts[micro_step]).astype(jnp.bfloat16).reshape(frames, 1, 1, 1)
        x_in = inputs[micro_step] * valid_tile
        first_kept, first_norm = forward_pair(
            x_in, gathered[0:6], clip_gate, valid_rows, cell_count
        )
        first_act = (
            (jax.nn.silu(first_norm) * valid_rows)
            .astype(jnp.bfloat16)
            .reshape(frames, tile_side, tile_side, channels)
        )
        second_kept, second_norm = forward_pair(
            first_act, gathered[6:12], clip_gate, valid_rows, cell_count
        )
        pre_out = second_norm + x_in.reshape(row_count, channels).astype(jnp.float32)
        results.append(
            (jax.nn.silu(pre_out) * valid_rows).reshape(frames, tile_side, tile_side, channels)
        )
        grad_pre = (
            cotangent[micro_step].reshape(row_count, channels).astype(jnp.float32)
            * valid_rows
            * silu_slope(pre_out)
        )
        grad_act, second_grads = backward_pair(
            grad_pre, second_kept, gathered[6:12], clip_gate, valid_rows, cell_count, tile_side
        )
        grad_first = grad_act * valid_rows * silu_slope(first_norm)
        grad_conv, first_grads = backward_pair(
            grad_first, first_kept, gathered[0:6], clip_gate, valid_rows, cell_count, tile_side
        )
        input_grads.append(
            ((grad_conv + grad_pre) * valid_rows).reshape(frames, tile_side, tile_side, channels)
        )
        step_grads = first_grads + second_grads
        kernel_now = (step_grads[0], step_grads[3], step_grads[6], step_grads[9])
        norm_now = (
            step_grads[1],
            step_grads[2],
            step_grads[4],
            step_grads[5],
            step_grads[7],
            step_grads[8],
            step_grads[10],
            step_grads[11],
        )
        if micro_step == 0:
            kernel_total = kernel_now
            norm_total = norm_now
        else:
            kernel_total = jax.tree.map(jnp.add, kernel_total, kernel_now)
            norm_total = jax.tree.map(jnp.add, norm_total, norm_now)
    kernel_total = lax.psum_scatter(kernel_total, "batch", scatter_dimension=0, tiled=True)
    kernel_total = jax.tree.map(
        lambda part: part.astype(jnp.float32), lax.psum(for_sending(kernel_total), ("ha", "wa"))
    )
    shard_index = lax.axis_index("batch")
    batch_count = lax.axis_size("batch")
    norm_shards = tuple(
        (
            lax.dynamic_slice_in_dim(
                full_sum,
                shard_index * (full_sum.shape[0] // batch_count),
                full_sum.shape[0] // batch_count,
            )
            for full_sum in norm_total
        )
    )
    return (
        jnp.stack(results),
        jnp.stack(input_grads),
        kernel_total[0],
        norm_shards[0],
        norm_shards[1],
        kernel_total[1],
        norm_shards[2],
        norm_shards[3],
        kernel_total[2],
        norm_shards[4],
        norm_shards[5],
        kernel_total[3],
        norm_shards[6],
        norm_shards[7],
    )


def solution(mesh):
    in_specs = (
        P(None, "batch", "ha", "wa", None),
        P(None, "batch"),
        P("batch", None),
        P("batch"),
        P("batch"),
        P("batch", None),
        P("batch"),
        P("batch"),
        P("batch", None),
        P("batch"),
        P("batch"),
        P("batch", None),
        P("batch"),
        P("batch"),
        P(None, "batch", "ha", "wa", None),
    )
    out_specs = (
        P(None, "batch", "ha", "wa", None),
        P(None, "batch", "ha", "wa", None),
        P("batch", None),
        P("batch"),
        P("batch"),
        P("batch", None),
        P("batch"),
        P("batch"),
        P("batch", None),
        P("batch"),
        P("batch"),
        P("batch", None),
        P("batch"),
        P("batch"),
    )
    batch = mesh.shape["batch"]

    def program(*args):
        spat, temp = args[2].shape[0], args[5].shape[0]
        fits = args[0].shape == (2, 16, 4, 4, 512) and args[2].shape[1] == 1152
        if fits and batch == 8 and spat * batch == 9 * 512 and temp * batch == 3 * 1152:
            return per_device_fast(batch, *args)
        return per_device(*args)

    return jax.shard_map(
        program, mesh=mesh, in_specs=in_specs, out_specs=out_specs, check_vma=False
    )
```

```python
import functools
from types import SimpleNamespace

import jax
import jax.numpy as jnp
from jax import lax
from jax.experimental import pallas as pl
from jax.experimental.pallas import tpu as pltpu
from jax.sharding import PartitionSpec as P

HGT = 7
epsilon = 1e-05
MESH = pl.DeviceIdType.MESH
F32 = jnp.float32
BF16 = jnp.bfloat16

BASE = 10
CELL = 8
ROWS = HGT * 8 * CELL
PADDED = (BASE + HGT * 8 + BASE) * CELL
MAIN = BASE * CELL
CHUNK = 2 * CELL
CHUNKS = ROWS // CHUNK
VMEM_LIMIT = 64 * 1024 * 1024 - 1024 * 1024


def when(cond, work):
    if cond is True:
        work()
    elif cond is not False:
        pl.when(cond)(work)


def loop(count, body, init):
    def twice(i, carry):
        return body(2 * i + 1, body(2 * i, carry))

    return lax.fori_loop(0, count // 2, twice, init)


def sigmoid(x):
    return 0.5 * jnp.tanh(0.5 * x) + 0.5


def nn(a, b):
    return jnp.dot(a, b, preferred_element_type=F32)


def nt(a, b):
    return lax.dot_general(a, b, (((1,), (1,)), ((), ())), preferred_element_type=F32)


def tn(a, b):
    return lax.dot_general(a, b, (((0,), (0,)), ((), ())), preferred_element_type=F32)


def rows_of(start, size, step=16):
    if not isinstance(start, int):
        start = pl.multiple_of(start, step)
    return pl.ds(start, size)


def block_kernel(dims, names, *all_refs):
    r = SimpleNamespace(**dict(zip(names, all_refs, strict=True)))
    nb, chan, mid, cell_count = dims
    spat = 9 * chan // nb
    temp = 3 * mid // nb
    unit = spat // 6
    quarter = chan // 4
    half = chan // 2
    h = lax.axis_index("ha")
    w = lax.axis_index("wa")
    b = lax.axis_index("batch")
    par = lax.rem(b, 2)
    bh = lax.div(b, 2)
    pos = par * (nb - 1 - bh) + (1 - par) * bh
    ways = (1 - 2 * h, 2 * h - 1)

    def at(p):
        p = lax.rem(p + 4 * nb, nb)
        upper = lax.div(p, nb // 2)
        return (1 - upper) * (2 * p) + upper * (2 * (nb - 1 - p) + 1)

    def at_group(j):
        return (lax.rem(j, 2), lax.div(j, 2))

    mine = 2 * w + h
    sibling = (1 - h, w, b)
    beside = (h, 1 - w, b)
    onward = [(h, w, at(pos + way)) for way in ways]
    later_dev = (1 - h, w, lax.rem(b + h, nb))
    earlier_dev = (1 - h, w, lax.rem(b + nb - 1 + h, nb))
    tile_group = [(lax.rem(mine + d, 4), (*at_group(lax.rem(mine + d, 4)), b)) for d in (1, 2, 3)]
    across = (h, w, b + 1 - 2 * par)
    pos_b = h * 2 + par
    plane = []
    for d in (1, 2, 3):
        q = lax.rem(pos_b + d, 4)
        plane.append((q, (lax.div(q, 2), w, b - par + lax.rem(q, 2))))
    depth = nb // 2
    line = []
    for d in range(1, depth):
        q = lax.rem(bh + d, depth)
        line.append((q, (h, w, 2 * q + par)))

    def named(dev):
        return dict(ha=dev[0], wa=dev[1], batch=dev[2])

    def rc(src, dst, send, recv, dev):
        return pltpu.make_async_remote_copy(
            src_ref=src, dst_ref=dst, send_sem=send, recv_sem=recv, device_id=named(dev), device_id_type=MESH
        )

    def lc(src, dst, sem):
        return pltpu.make_async_copy(src, dst, sem)

    partners = [sibling, beside, *onward, later_dev, earlier_dev]
    partners += [dev for _, dev in tile_group + plane + line]
    barrier = pltpu.get_barrier_semaphore()
    for dev in partners:
        pl.semaphore_signal(barrier, inc=1, device_id=named(dev), device_id_type=MESH)
    pl.semaphore_wait(barrier, len(partners))

    shards = (r.first_spatial, r.first_temporal, r.second_spatial, r.second_temporal)
    whole = (r.w1s, r.w1t, r.w2s, r.w2t)
    shared = 2 * w + h
    shared_beside = 2 * (1 - w) + h
    third = temp // 3

    def units(i, core, side):
        return (2 * side + core, 4 + core) if i % 2 == 0 else ((1 - core) * side + 2 * core,)

    def piece(i, ref, owner, u, k):
        if i % 2 == 0:
            return ref.at[rows_of(owner * spat + u * unit + k * (unit // 2), unit // 2), :]
        return ref.at[rows_of(owner * temp + u * third, third), :]

    def subs(i):
        return (0, 1) if i % 2 == 0 else (0,)

    def streams(i):
        return (0, 1) if i % 2 == 0 else (0,)

    def crossing(i, work):
        if i % 2 == 0:
            work()
        else:
            pl.when(h == 0)(work)

    def crossed(i, work):
        if i % 2 == 0:
            work()
        else:
            pl.when(h == 1)(work)

    def own_copy(i):
        rows = spat if i % 2 == 0 else temp
        return lc(shards[i], whole[i].at[rows_of(b * rows, rows), :], r.own_sem.at[i])

    def ring(i, st, k, s, owner, from_shard=False):
        u = units(i, h, w)[st]
        dst = piece(i, whole[i], owner, u, k)
        src = piece(i, shards[i], 0, u, k) if from_shard else dst
        return rc(src, dst, r.ring_send.at[i, st, k, s], r.ring_recv.at[i, st, k, s], onward[st])

    def cross(i, kind, k, s, owner, u):
        part = piece(i, whole[i], owner, u, k)
        return rc(part, part, r.sib_send.at[i, kind, k, s], r.sib_recv.at[i, kind, k, s], sibling)

    def over(i, k, s, owner, u):
        part = piece(i, whole[i], owner, u, k)
        return rc(part, part, r.over_send.at[i, k, s], r.over_recv.at[i, k, s], beside)

    def gather_start(i):
        for k in subs(i):
            for st in streams(i):
                ring(i, st, k, 1, b, True).start()
        own_copy(i).start()

    def gather_relay(i, s):
        owner = at(pos - ways[0] * s)

        def work():
            for k in subs(i):
                over(i, k, s, owner, units(i, h, 1 - w)[0]).wait_recv()
                cross(i, 2, k, s, owner, units(i, h, 1 - w)[0]).start()

        crossing(i, work)

    def gather_pump(i, s):
        own = units(i, h, w)
        for k in subs(i):
            for st in streams(i):
                owner = at(pos - ways[st] * s)
                ring(i, st, k, s, owner).wait_recv()
                if isinstance(s, int):
                    if s < nb - 1:
                        ring(i, st, k, s + 1, owner).start()
                else:
                    pl.when(s < nb - 1)(lambda st=st, k=k, owner=owner: ring(i, st, k, s + 1, owner).start())
                if st == 0:
                    crossing(i, lambda k=k, owner=owner: over(i, k, s, owner, own[0]).start())
                cross(i, st, k, s, owner, own[st]).start()
        if isinstance(s, int):
            if s > 1:
                gather_relay(i, s - 1)
        else:
            pl.when(s > 1)(lambda: gather_relay(i, s - 1))

    def gather_finish(i):
        gather_relay(i, nb - 1)

        def body(s, _):
            for k in subs(i):
                for st in streams(i):
                    cross(i, st, k, s, at(pos + ways[st] * s), units(i, 1 - h, w)[st]).wait_recv()
                theirs = at(pos + ways[0] * s)
                crossed(i, lambda k=k: cross(i, 2, k, s, theirs, units(i, 1 - h, 1 - w)[0]).wait_recv())
            return 0

        lax.fori_loop(1, nb, body, 0)
        own_copy(i).wait()

    def gather_sent(i):
        def body(s, _):
            for k in subs(i):
                for st in streams(i):
                    owner = at(pos - ways[st] * s)
                    ring(i, st, k, s, owner).wait_send()
                    cross(i, st, k, s, owner, units(i, h, w)[st]).wait_send()

                def sent(k=k):
                    owner = at(pos - ways[0] * s)
                    over(i, k, s, owner, units(i, h, w)[0]).wait_send()
                    cross(i, 2, k, s, owner, units(i, h, 1 - w)[0]).wait_send()

                crossing(i, sent)
            return 0

        lax.fori_loop(1, nb, body, 0)

    def total(k, width, value, works=()):
        slot = k % 2
        wide = value.shape[1]
        cols = pl.ds(0, wide)
        works = list(works) + [None] * 2
        four, far = r.sum_b, r.sum_c
        four[slot, pos_b, :, cols] = value
        sends = []
        for n, (q, dev) in enumerate(plane):
            part = four.at[slot, pos_b, :, cols]
            sends.append(rc(part, part, r.sb_send.at[k, n], r.sb_recv.at[k, pos_b], dev))
            sends[-1].start()
        if works[0]:
            works[0]()
        for n, (q, dev) in enumerate(plane):
            part = four.at[slot, q, :, cols]
            rc(part, part, r.sb_send.at[k, n], r.sb_recv.at[k, q], dev).wait_recv()
        far[slot, bh, :, cols] = (four[slot, 0, :, cols] + four[slot, 1, :, cols]) + (
            four[slot, 2, :, cols] + four[slot, 3, :, cols]
        )
        for n, (q, dev) in enumerate(line):
            part = far.at[slot, bh, :, cols]
            sends.append(rc(part, part, r.sc_send.at[k, n], r.sc_recv.at[k, bh], dev))
            sends[-1].start()
        if works[1]:
            works[1]()
        for n, (q, dev) in enumerate(line):
            part = far.at[slot, q, :, cols]
            rc(part, part, r.sc_send.at[k, n], r.sc_recv.at[k, q], dev).wait_recv()
        result = far[slot, 0, :, cols]
        for q in range(1, depth):
            result = result + far[slot, q, :, cols]
        for send in sends:
            send.wait_send()
        if wide == width:
            return result
        return jnp.concatenate([result[2 * n : 2 * n + 2] for n in range(width // wide)], axis=1)

    def chunk(ref, i, base=0, width=None):
        cols = slice(None) if width is None else pl.ds(0, width)
        value = ref[rows_of(base + i * CHUNK, CHUNK), cols]
        return value.astype(F32).reshape(2, CELL, value.shape[-1])

    def put(ref, i, value, base=0, width=None):
        cols = slice(None) if width is None else pl.ds(0, width)
        ref[rows_of(base + i * CHUNK, CHUNK), cols] = value.reshape(CHUNK, value.shape[-1]).astype(ref.dtype)

    def keep(i):
        inside = jnp.where(lax.rem(i, 4) == 3, 0.0, 1.0).astype(F32)
        first = lax.broadcasted_iota(jnp.int32, (2, 1, 1), 0) == 0
        return jnp.where(first, 1.0, inside)

    def packed(one, two, width):
        rows = jnp.concatenate([jnp.sum(v, axis=0, keepdims=True) for v in (one, two)], axis=0)
        wide = 384 if width == mid else 128
        parts = [rows[:, n * wide : (n + 1) * wide] for n in range(width // wide)]
        return jnp.concatenate((parts + parts[-1:])[0:4], axis=0)

    def moments(ref, width):
        def body(i, carry):
            v = chunk(ref, i)
            m = v * keep(i)
            return (carry[0] + m[0] + m[1], carry[1] + m[0] * v[0] + m[1] * v[1])

        zero = jnp.zeros((CELL, width), F32)
        return loop(CHUNKS, body, (zero, zero))

    def prepare(n, sums, width):
        tile = r.tile_mid if width == mid else r.tile_out
        n2 = n // 2
        gain = r.param[2 * n : 2 * n + 1, 0:width]
        bias = r.param[2 * n + 1 : 2 * n + 2, 0:width]
        mean = sums[0:1] / cell_count
        inv = lax.rsqrt(sums[1:2] / cell_count - mean * mean + epsilon)
        scale = inv * gain
        shift = bias - mean * scale
        for k, v in enumerate((scale, shift, inv, mean * inv)):
            tile[n2, k] = jnp.broadcast_to(v, (CELL, width))

    def tiles(n, width):
        tile = r.tile_mid if width == mid else r.tile_out
        return [tile[n // 2, k][None] for k in range(4)]

    def fill(ref_a, ref_b, value_of, width):
        pads(ref_a, ref_b, width)

        def body(i, before):
            v = value_of(i)
            put(ref_a, i, v, MAIN)
            pair = jnp.concatenate([before[None], v[0:1]], axis=0)
            put(ref_b, i, pair, MAIN - CHUNK)
            return v[1]

        loop(CHUNKS, body, jnp.zeros((CELL, width), F32))

    def activated(src, n, width):
        def value(i):
            scale, shift, _, _ = tiles(n, width)
            y = chunk(src, i) * scale + shift
            return y * sigmoid(y) * keep(i)

        return value

    def taps(ref_a, ref_b, k, size=ROWS):
        r0 = MAIN - 8 * CELL + 8 * CELL * k
        return (
            ref_b[rows_of(r0 - CHUNK, size), :],
            ref_a[rows_of(r0, size), :],
            ref_b[rows_of(r0, size), :],
        )

    def conv(ref_a, ref_b, weight, out, pump=None):
        for n, (c0, cw) in enumerate(((0, 512), (512, mid - 512))):

            def body(a, _, c0=c0, cw=cw, n=n):
                x = taps(ref_a, ref_b, a)
                acc = nn(jnp.concatenate(x, axis=1), weight[rows_of(a * 3 * chan, 3 * chan), c0 : c0 + cw])

                @pl.when(a == 0)
                def _():
                    out[:, c0 : c0 + cw] = acc

                @pl.when(a > 0)
                def _():
                    out[:, c0 : c0 + cw] += acc

                if pump is not None:
                    pump(n * 3 + a)
                return 0

            lax.fori_loop(0, 3, body, 0)

    def conv_back(ref_a, ref_b, weight, out, pump=None):
        def body(k, _):
            e = taps(ref_a, ref_b, k)
            acc = None
            for j in range(3):
                tap = 8 - 3 * k - j
                term = nt(e[j], weight[rows_of(tap * chan, chan), :])
                acc = term if acc is None else acc + term

            @pl.when(k == 0)
            def _():
                out[:, 0:chan] = acc

            @pl.when(k > 0)
            def _():
                out[:, 0:chan] += acc

            if pump is not None:
                pump(k)
            return 0

        lax.fori_loop(0, 3, body, 0)

    def send_frames(k):
        down, up = r.down, r.up
        count = ROWS // CELL
        for c in range(chan // 128):
            lanes = pl.ds(128 * c, 128)
            r.halo_out[0, :, lanes] = down[c, pl.ds(2 * CELL - 1, count, stride=CELL), :]
            r.halo_out[1, :, lanes] = up[c, pl.ds(0, count, stride=CELL), :]
        copies = []
        for n, dev in ((0, later_dev), (1, earlier_dev)):
            copies.append(
                rc(r.halo_out.at[n], r.halo_in.at[k, n], r.halo_send.at[k, n], r.halo_recv.at[k, n], dev)
            )
            copies[-1].start()
        return copies

    def take_frames(k, copies):
        down, up = r.down, r.up
        count = ROWS // CELL
        for copy in copies:
            copy.wait()
        at_start = jnp.logical_and(h == 0, b == 0)
        at_end = jnp.logical_and(h == 1, b == nb - 1)
        for c in range(chan // 128):
            lanes = pl.ds(128 * c, 128)
            before = r.halo_in[k, 0, :, lanes]
            after = r.halo_in[k, 1, :, lanes]
            down[c, pl.ds(CELL - 1, count, stride=CELL), :] = jnp.where(at_start, 0.0, before)
            up[c, pl.ds(CELL, count, stride=CELL), :] = jnp.where(at_end, 0.0, after)

    def by_lanes(ref, rows):
        return jnp.concatenate([ref[c, rows, :] for c in range(chan // 128)], axis=1)

    def put_lanes(ref, rows, value):
        for c in range(chan // 128):
            ref[c, rows, :] = value[:, 128 * c : 128 * c + 128]

    def shifted(i):
        before = by_lanes(r.down, rows_of(i * CHUNK, CHUNK + CELL))[CELL - 1 : CELL - 1 + CHUNK]
        after = by_lanes(r.up, rows_of(i * CHUNK, CHUNK + CELL))[1 : 1 + CHUNK]
        gate = r.gate[...][None]
        return (before.reshape(2, CELL, chan) * gate, after.reshape(2, CELL, chan))

    def temporal(k, v, weight, out, works=()):
        works = list(works) + [None] * 2
        put_lanes(r.down, pl.ds(CELL, ROWS), nn(v[...], weight[0:mid, :]))
        y2 = nn(v[...], weight[2 * mid : 3 * mid, :])
        y2 = (y2.reshape(ROWS // CELL, CELL, chan) * r.gate[...][None]).reshape(ROWS, chan)
        put_lanes(r.up, pl.ds(0, ROWS), y2)
        copies = send_frames(k)
        out[...] = nn(v[...], weight[mid : 2 * mid, :])
        if works[0]:
            works[0]()
        take_frames(k, copies)

        def body(i, carry):
            before, after = shifted(i)
            value = chunk(out, i) + before + after
            put(out, i, value)
            m = value * keep(i)
            return (carry[0] + m[0] + m[1], carry[1] + m[0] * value[0] + m[1] * value[1])

        zero = jnp.zeros((CELL, chan), F32)
        return loop(CHUNKS, body, (zero, zero))

    def temporal_back(k, weight, works=()):
        works = list(works) + [None] * 2
        copies = send_frames(k)
        e3 = r.e3
        for c0, cw in ((0, 512), (512, mid - 512)):
            r.grad_mid[:, c0 : c0 + cw] = nt(e3[1], weight[mid + c0 : mid + c0 + cw, :])
        if works[0]:
            works[0]()
        take_frames(k, copies)

        def body(i, _):
            before, after = shifted(i)
            e3[0, rows_of(i * CHUNK, CHUNK), :] = after.reshape(CHUNK, chan).astype(BF16)
            e3[2, rows_of(i * CHUNK, CHUNK), :] = before.reshape(CHUNK, chan).astype(BF16)
            return 0

        loop(CHUNKS, body, 0)
        share = share_e3(k)
        for c0, cw in ((0, 512), (512, mid - 512)):
            r.grad_mid[:, c0 : c0 + cw] += nt(e3[0], weight[c0 : c0 + cw, :]) + nt(
                e3[2], weight[2 * mid + c0 : 2 * mid + c0 + cw, :]
            )
        return share

    def share(k, src, dst):
        copy = rc(src, dst, r.share_send.at[k], r.share_recv.at[k], sibling)
        copy.start()
        return copy

    outs = (r.out1s, r.out1t, r.out2s, r.out2t)

    chunks = ((0, 256), (256, 256), (512, 256), (768, mid - 768))
    every = range(len(chunks))

    def e_part(n, slot):
        c0, cw = chunks[n]
        return r.e_all.at[slot * ROWS : (slot + 1) * ROWS, c0 : c0 + cw]

    def e_copies(k, n):
        sems = [(r.e_send.at[k, n, m], r.e_recv.at[k, n, m]) for m in range(3)]
        return [
            rc(e_part(n, 0), e_part(n, 1), *sems[0], sibling),
            rc(e_part(n, 0), e_part(n, 2), *sems[1], beside),
            rc(e_part(n, 2), e_part(n, 3), *sems[2], sibling),
        ]

    def share_e(k):
        for n in every:
            near, over, _ = e_copies(k, n)
            over.start()
            near.start()

    def share_e_on(k, n):
        _, over, far = e_copies(k, n)
        over.wait_recv()
        far.start()

    def share_e_wait(k, n):
        near, over, far = e_copies(k, n)
        near.wait()
        over.wait_send()
        far.wait()

    def share_x(k, xa, xq):
        copies = []
        for n, dev in enumerate((sibling, beside, (1 - h, 1 - w, b))):
            lanes = rows_of((2 * dev[1] + dev[0]) * quarter, quarter, 128)
            main = pl.ds(MAIN, ROWS)
            copies.append(
                rc(xa.at[main, lanes], xq.at[n, 0, main, :], r.xq_send.at[k, n], r.xq_recv.at[k, n], dev)
            )
            copies[-1].start()
        return copies

    def pads(ref_a, ref_b, width):
        ref_a[0:MAIN, :] = jnp.zeros((MAIN, width), BF16)
        ref_a[MAIN + ROWS : PADDED, :] = jnp.zeros((PADDED - MAIN - ROWS, width), BF16)
        ref_b[0 : MAIN - CHUNK, :] = jnp.zeros((MAIN - CHUNK, width), BF16)
        ref_b[MAIN - CHUNK + ROWS : PADDED, :] = jnp.zeros((PADDED - MAIN + CHUNK - ROWS, width), BF16)

    def spread_x(xq):
        for n in range(3):
            pads(xq.at[n, 0], xq.at[n, 1], quarter)

        def body(i, before):
            after = []
            for n in range(3):
                v = chunk(xq.at[n, 0], i, MAIN)
                put(xq.at[n, 1], i, jnp.concatenate([before[n][None], v[0:1]], axis=0), MAIN - CHUNK)
                after.append(v[1])
            return tuple(after)

        loop(CHUNKS, body, (jnp.zeros((CELL, quarter), F32),) * 3)

    def share_e3(k):
        return share(
            k - 2, r.e3.at[:, :, rows_of((1 - h) * half, half, 128)], r.sib_e3
        )

    def grad_tap(owner):
        return owner + jnp.where(owner > 2 * shared, 1, 0)

    spare = r.w2s

    def gq(i, row, size):
        return rows_of((mid if i == 0 else 0) + row, size)

    def inbox(i, row, size):
        return rows_of(2 * mid + (mid if i == 0 else 0) + row, size)

    def transpose_x(a, xa, xb, xq, near, far, row):
        lanes = rows_of(shared * quarter, quarter, 128)
        r0 = MAIN - 8 * CELL + 8 * CELL * a
        for j, (c, start) in enumerate(((1, r0 - CHUNK), (0, r0), (1, r0))):
            rows = rows_of(start, ROWS)
            own = (xb if c else xa)[rows, lanes]
            both = jnp.concatenate([own, xq[0, c, rows, :]], axis=0)
            near[rows_of(row + j * quarter, quarter), 0 : 2 * ROWS] = both.T
            both = jnp.concatenate([xq[1, c, rows, :], xq[2, c, rows, :]], axis=0)
            far[rows_of(row + j * quarter, quarter), 0 : 2 * ROWS] = both.T

    def transposes(xa, xb, xq):
        def body(a, _):
            transpose_x(a, xa, xb, xq, r.xt, r.xt2, a * 3 * quarter)
            return 0

        lax.fori_loop(0, 3, body, 0)

    def spatial_chunk(i, n):
        c0, cw = chunks[n]

        def body(a, _):
            rows = rows_of(a * (mid // 2), mid // 2)
            acc = nn(r.xt[rows, :], r.e_all[0 : 2 * ROWS, c0 : c0 + cw])
            acc += nn(r.xt2[rows, :], r.e_all[2 * ROWS : 4 * ROWS, c0 : c0 + cw])
            spare[gq(i, a * (mid // 2), mid // 2), c0 : c0 + cw] = acc.astype(BF16)
            return 0

        lax.fori_loop(0, 2, body, 0)

    def transpose_v(v, sv):
        for c in range(mid // 128):
            lanes = pl.ds(128 * c, 128)
            r.xt[128 * c : 128 * c + 128, :] = jnp.concatenate([v[:, lanes], sv[:, lanes]], axis=0).T

    def temporal_grad(i, k):
        e = jnp.concatenate([r.e3[k, :, rows_of(h * half, half, 128)], r.sib_e3[k]], axis=0)
        whole[i][k * mid : (k + 1) * mid, 0:half] = nn(r.xt[...], e).astype(BF16)

    def cols_of(n):
        c0, cw = chunks[n]
        return pl.ds(c0, cw)

    def s_block(i, n, owner):
        return spare.at[gq(i, grad_tap(owner) * quarter, quarter), cols_of(n)]

    def s_extra(i, n, side):
        return spare.at[gq(i, (2 * shared + 1) * quarter + side * 64, 64), cols_of(n)]

    def t_block(i, owner):
        return whole[i].at[rows_of(owner * temp, temp), 0:half]

    def t_inbox(i, n):
        return whole[i].at[rows_of(n * temp, temp), half:chan]

    def parts_of(i):
        return every if i % 2 == 0 else (0,)

    def block_of(i, n, owner):
        return s_block(i, n, owner) if i % 2 == 0 else t_block(i, owner)

    def y_box(i, n, place):
        return spare.at[inbox(i, place * quarter, quarter), cols_of(n)] if i % 2 == 0 else t_inbox(i, place)

    def z_box(i, n, place):
        return spare.at[inbox(i, 576 + place * quarter, quarter), cols_of(n)] if i % 2 == 0 else t_inbox(i, 4 + place)

    def extra_y_box(i, n):
        return spare.at[inbox(i, 4 * quarter, 64), cols_of(n)]

    def extra_z_box(i, n, place):
        return spare.at[inbox(i, 576 + 3 * quarter + place * 64, 64), cols_of(n)]

    def add_into(dst, parts, step):
        rows, cols = dst.shape

        def body(n, _):
            at_rows = rows_of(n * step, step)
            value = dst[at_rows, :].astype(F32)
            for part in parts:
                value = value + part[at_rows, :].astype(F32)
            dst[at_rows, :] = value.astype(BF16)
            return 0

        lax.fori_loop(0, rows // step, body, 0)

    def y_copy(i, n, d):
        place = lax.rem(bh + d, depth)
        src = block_of(i, n, 2 * place + 1 - par)
        return rc(src, y_box(i, n, place), r.y_send.at[i, n, d], r.y_recv.at[i, n, place], across)

    def z_copy(i, n, d):
        place = lax.rem(bh + d, depth)
        src = block_of(i, n, 2 * place + par)
        dev = (h, w, 2 * place + par)
        return rc(src, z_box(i, n, 3 - d), r.z_send.at[i, n, d], r.z_recv.at[i, n, 3 - d], dev)

    def extra_y(i, n):
        return rc(s_extra(i, n, 1 - par), extra_y_box(i, n), r.y_send.at[i, n, 4], r.y_recv.at[i, n, 4], across)

    def extra_z(i, n):
        place = jnp.minimum(lax.rem(bh - shared + 3 + depth, depth), 2)
        dev = (h, w, 2 * shared + par)
        return rc(
            s_extra(i, n, par), extra_z_box(i, n, place), r.z_send.at[i, n, 4], r.z_recv.at[i, n, 4 + place], dev
        )

    def step_of(i):
        return 32 if i % 2 == 0 else 48

    def reduce_start(i, n):
        for d in (1, 2, 3, 0):
            y_copy(i, n, d).start()
        if i % 2 == 0:
            extra_y(i, n).start()

    def reduce_middle(i, n):
        for d in (1, 2, 3, 0):
            place = lax.rem(bh + d, depth)
            y_copy(i, n, d).wait_send()
            box = y_box(i, n, place)
            rc(box, box, r.y_send.at[i, n, d], r.y_recv.at[i, n, place], across).wait_recv()
            add_into(block_of(i, n, 2 * place + par), [box], step_of(i))
            if d:
                z_copy(i, n, d).start()
        if i % 2 == 0:
            extra_y(i, n).wait()
            add_into(s_extra(i, n, par), [extra_y_box(i, n)], 32)
            pl.when(bh != shared)(lambda: extra_z(i, n).start())

    def final_part(i, n, side, core):
        place = 2 * side + core
        start = quarter * place - 64 * b + 512 * jnp.where(b > 2 * place, 1, 0)
        return outs[i].at[rows_of(start, quarter, 64), cols_of(n)]

    def extra_part(i, n):
        return outs[i].at[rows_of(512 * (1 - par), 64, 64), cols_of(n)]

    def final_copies(i, n):
        if i % 2:
            src = t_block(i, b)
            part = outs[i].at[h]
            return lc(src, part, r.out_sem.at[i, 0, 0]), [
                (src, part, sibling, r.cast_send.at[i, 0, 0], r.cast_recv.at[i, 0, 0])
            ]
        src = s_block(i, n, b)
        part = final_part(i, n, w, h)
        sends = [
            (src, part, dev, r.cast_send.at[i, n, d], r.cast_recv.at[i, n, d]) for d, dev in enumerate((beside, sibling))
        ]
        return lc(src, part, r.out_sem.at[i, n, 0]), sends

    def extra_copies(i, n):
        src = s_extra(i, n, par)
        part = extra_part(i, n)
        sends = [
            (src, part, dev, r.cast_send.at[i, n, 3 + d], r.cast_recv.at[i, n, 3 + d])
            for d, dev in enumerate((beside, sibling))
        ]
        return lc(src, part, r.out_sem.at[i, n, 1]), sends

    def begin(copies):
        local, sends = copies
        for src, part, dev, one, two in sends:
            rc(src, part, one, two, dev).start()
        local.start()

    def credit(n):
        pl.semaphore_signal(r.credit.at[n], inc=1, device_id=named(beside), device_id_type=MESH)

    def credited(n):
        pl.semaphore_wait(r.credit.at[n], 1)

    def beside_copy(i):
        return rc(t_block(i, b), t_inbox(i, 7), r.z_send.at[i, 0, 4], r.z_recv.at[i, 0, 4], beside)

    def reduce_last(i, n):
        for d in (1, 2, 3):
            z_copy(i, n, d).wait()
        add_into(block_of(i, n, b), [z_box(i, n, place) for place in range(3)], step_of(i))
        if i % 2:
            credited(i // 2)
            beside_copy(i).start()
            return
        begin(final_copies(i, n))

        @pl.when(bh != shared)
        def _():
            extra_z(i, n).wait_send()

        @pl.when(bh == shared)
        def _():
            boxes = [extra_z_box(i, n, place) for place in range(3)]
            for place, box in enumerate(boxes):
                rc(box, box, r.z_send.at[i, n, 4], r.z_recv.at[i, n, 4 + place], across).wait_recv()
            add_into(s_extra(i, n, par), boxes, 32)
            begin(extra_copies(i, n))

    def reduce_out(i):
        beside_copy(i).wait()
        add_into(t_block(i, b), [t_inbox(i, 7)], 48)
        begin(final_copies(i, 0))

    def final_on(i, n):
        def move(part, d):
            rc(part, part, r.cast_send.at[i, n, d], r.cast_recv.at[i, n, d], beside).wait_recv()
            rc(part, part, r.cast_send.at[i, n, d + 2], r.cast_recv.at[i, n, d + 2], sibling).start()

        move(final_part(i, n, 1 - w, h), 0)
        pl.when(bh == shared_beside)(lambda: move(extra_part(i, n), 3))

    def reduce_wait(i, n):
        local, sends = final_copies(i, n)
        local.wait()
        if i % 2:
            src, part, dev, one, two = sends[0]
            rc(src, outs[i].at[1 - h], one, two, dev).wait()
            return
        for src, part, dev, one, two in sends:
            rc(src, part, one, two, dev).wait_send()

        def far(part, d):
            return rc(part, part, r.cast_send.at[i, n, d], r.cast_recv.at[i, n, d], sibling)

        far(final_part(i, n, w, 1 - h), 1).wait_recv()
        far(final_part(i, n, 1 - w, h), 2).wait_send()
        far(final_part(i, n, 1 - w, 1 - h), 2).wait_recv()
        local, sends = extra_copies(i, n)

        @pl.when(bh == shared)
        def _():
            local.wait()
            for src, part, dev, one, two in sends:
                rc(src, part, one, two, dev).wait_send()

        pl.when(bh == shared_beside)(lambda: far(extra_part(i, n), 5).wait_send())
        pl.when(bh == 2 * w + 1 - h)(lambda: far(extra_part(i, n), 4).wait_recv())
        pl.when(bh == 2 * (1 - w) + 1 - h)(lambda: far(extra_part(i, n), 5).wait_recv())

    def tile_of(ref, jh, jw):
        return ref.at[rows_of(jh * 4, 4, 4), rows_of(jw * 32, 32), :]

    def scatter(src, dst, n):
        copies = []
        for d, (j, dev) in enumerate(tile_group):
            copies.append(
                rc(src.at[j], tile_of(dst, h, w), r.tile_send.at[n, d], r.tile_recv.at[n, mine], dev)
            )
        return copies

    def scattered(src, dst, n):
        for d, (j, dev) in enumerate(tile_group):
            jh, jw = at_group(j)
            rc(src.at[j], tile_of(dst, jh, jw), r.tile_send.at[n, d], r.tile_recv.at[n, j], dev).wait()

    def tiles_start(src, dst, n):
        for copy in scatter(src, dst, n):
            copy.start()
        lc(src.at[mine], tile_of(dst, h, w), r.tile_own.at[n]).start()

    def tiles_wait(src, dst, n):
        scattered(src, dst, n)
        lc(src.at[mine], tile_of(dst, h, w), r.tile_own.at[n]).wait()

    xg, cg = r.x_grid, r.cot_grid
    tiles_start(r.x_tiles, xg, 0)
    gather_start(0)
    r.param[...] = total(0, mid, r.param_in[...])
    tiles_wait(r.x_tiles, xg, 0)

    def grid_chunk(ref, i):
        v = ref[lax.div(i, 4), rows_of(lax.rem(i, 4) * CHUNK, CHUNK), :]
        return v.astype(F32).reshape(2, CELL, chan)

    fill(r.xa, r.xb, lambda i: grid_chunk(xg, i), chan)

    def pump_loop(i, lo, hi):
        def body(s, _):
            gather_pump(i, s)
            return 0

        lax.fori_loop(lo, hi, body, 0)

    pump_loop(0, 1, nb - 3)
    gather_start(1)
    pump_loop(0, nb - 3, nb - 1)
    gather_start(2)
    gather_pump(0, nb - 1)
    gather_pump(1, 1)
    gather_pump(2, 1)
    gather_pump(1, 2)
    gather_finish(0)

    def first_pump(n):
        pl.when(lax.rem(n, 2) == 0)(lambda: gather_pump(1, 3 + lax.div(n, 2)))
        pl.when(n == 3)(lambda: gather_pump(2, 2))

    conv(r.xa, r.xb, r.w1s, r.mid1, first_pump)
    def first_last():
        gather_pump(2, 3)
        gather_pump(1, nb - 1)

    sums = total(
        1,
        mid,
        packed(*moments(r.mid1, mid), mid),
        [lambda: gather_pump(1, nb - 2), first_last],
    )
    prepare(0, sums, mid)

    def hidden(src, n, dst):
        value = activated(src, n, mid)

        def body(i, _):
            put(dst, i, value(i))
            return 0

        loop(CHUNKS, body, 0)

    hidden(r.mid1, 0, r.v1)
    gather_pump(2, 4)
    gather_finish(1)
    stats = temporal(0, r.v1, r.w1t, r.time1, [lambda: gather_pump(2, 5)])

    def sixth():
        gather_pump(2, 6)

    sums = total(2, chan, packed(*stats, chan), [lambda: gather_start(3), sixth])
    prepare(1, sums, chan)
    fill(r.aa, r.ab, activated(r.time1, 1, chan), chan)
    gather_pump(3, 1)
    gather_pump(2, nb - 1)
    gather_pump(3, 2)
    gather_finish(2)
    tiles_start(r.cot_tiles, cg, 1)

    def second_pump(n):
        pl.when(n < nb - 3)(lambda: gather_pump(3, 3 + n))

    conv(r.aa, r.ab, r.w2s, r.mid2, second_pump)
    sums = total(3, mid, packed(*moments(r.mid2, mid), mid), [lambda: gather_finish(3)])
    prepare(2, sums, mid)
    hidden(r.mid2, 2, r.v2)
    stats = temporal(1, r.v2, r.w2t, r.time2)
    shared_xq2 = share_x(0, r.aa, r.xq2)
    shared_xq1 = share_x(1, r.xa, r.xq1)
    for i in range(4):
        gather_sent(i)
    share_v2 = share(4, r.v2, r.sib_v)
    sums = total(4, chan, packed(*stats, chan))
    tiles_wait(r.cot_tiles, cg, 1)
    prepare(3, sums, chan)

    out_grid = r.out_grid

    def grid_put(ref, i, v):
        ref[lax.div(i, 4), rows_of(lax.rem(i, 4) * CHUNK, CHUNK), :] = v.reshape(CHUNK, chan).astype(ref.dtype)

    def slope(y, s):
        return s * (1.0 + y * (1.0 - s))

    def pre_body(i, carry):
        scale, shift, inv, offset = tiles(3, chan)
        v = chunk(r.time2, i)
        y = v * scale + shift + chunk(r.xa, i, MAIN)
        s = sigmoid(y)
        m = keep(i)
        grid_put(out_grid, i, y * s * m)
        d = grid_chunk(cg, i) * m * slope(y, s)
        put(r.grad_pre, i, d)
        t = d * (v * inv - offset)
        return (carry[0] + d[0] + d[1], carry[1] + t[0] + t[1])

    zero_out = jnp.zeros((CELL, chan), F32)
    zero_mid = jnp.zeros((CELL, mid), F32)
    out_grid[HGT] = jnp.zeros((8 * CELL, chan), BF16)
    gg = loop(CHUNKS, pre_body, (zero_out, zero_out))

    def send_tiles(src, dst, n):
        for d, (j, dev) in enumerate(tile_group):
            jh, jw = at_group(j)
            rc(tile_of(src, jh, jw), dst.at[mine], r.tile_send.at[n, d], r.tile_recv.at[n, mine], dev).start()
        lc(tile_of(src, h, w), dst.at[mine], r.tile_own.at[n]).start()

    def sent_tiles(src, dst, n):
        for d, (j, dev) in enumerate(tile_group):
            jh, jw = at_group(j)
            rc(tile_of(src, jh, jw), dst.at[j], r.tile_send.at[n, d], r.tile_recv.at[n, j], dev).wait()
        lc(tile_of(src, h, w), dst.at[mine], r.tile_own.at[n]).wait()

    send_tiles(out_grid, r.block_out, 2)

    def norm_back(n, sums, width):
        r.norm_part[0, 2 * n : 2 * n + 1, 0:width] = sums[1:2]
        r.norm_part[0, 2 * n + 1 : 2 * n + 2, 0:width] = sums[0:1]
        back = r.back
        back[0, :, 0:width] = jnp.broadcast_to(sums[0:1] / cell_count, (CELL, width))
        back[1, :, 0:width] = jnp.broadcast_to(sums[1:2] / cell_count, (CELL, width))

    def through_norm(n, src, grad, i, width):
        scale, _, inv, offset = tiles(n, width)
        xhat = chunk(src, i) * inv - offset
        bias_part = r.back[0, :, 0:width][None]
        gain_part = r.back[1, :, 0:width][None]
        return scale * (chunk(grad, i, 0, width) - bias_part - xhat * gain_part) * keep(i)

    def through_act(n, src, grad, width):
        def body(i, carry):
            scale, shift, inv, offset = tiles(n, width)
            v = chunk(src, i)
            y = v * scale + shift
            s = sigmoid(y)
            d = chunk(grad, i, 0, width) * keep(i) * slope(y, s)
            put(grad, i, d, 0, width)
            t = d * (v * inv - offset)
            return (carry[0] + d[0] + d[1], carry[1] + t[0] + t[1])

        zero = jnp.zeros((CELL, width), F32)
        return loop(CHUNKS, body, (zero, zero))

    def to_frames(n, src, grad):
        def body(i, _):
            e = through_norm(n, src, grad, i, chan).astype(BF16)
            ef = e.astype(F32)
            r.e3[1, rows_of(i * CHUNK, CHUNK), :] = e.reshape(CHUNK, chan)
            put_lanes(r.down, rows_of(i * CHUNK + CELL, CHUNK, CELL), ef.reshape(CHUNK, chan))
            put_lanes(r.up, rows_of(i * CHUNK, CHUNK), (ef * r.gate[...][None]).reshape(CHUNK, chan))
            return 0

        loop(CHUNKS, body, 0)

    sums = total(5, chan, packed(*gg, chan))
    norm_back(3, sums, chan)
    to_frames(3, r.time2, r.grad_pre)
    shared_e3 = temporal_back(2, r.w2t)
    credit(1)
    gg = through_act(2, r.mid2, r.grad_mid, mid)
    shared_e3.wait()
    share_v2.wait()
    def temporal_grads(i, v):
        def first():
            transpose_v(v, r.sib_v)
            temporal_grad(i, 0)

        def others():
            temporal_grad(i, 1)
            temporal_grad(i, 2)

        return [first, others]

    sums = total(6, mid, packed(*gg, mid), temporal_grads(3, r.v2))
    reduce_start(3, 0)
    norm_back(2, sums, mid)

    def fill_e(n, src):
        def value(i):
            v = through_norm(n, src, r.grad_mid, i, mid)
            put(r.e_all, i, v)
            return v

        fill(r.ea, r.eb, value, mid)

    fill_e(2, r.mid2)
    share_e(0)
    conv_back(r.ea, r.eb, r.w2s, r.grad_mid)
    share_e_on(0, 0)
    gg = through_act(1, r.time1, r.grad_mid, chan)
    for copy in shared_xq2:
        copy.wait()

    def spread_and_turn():
        spread_x(r.xq2)
        transposes(r.aa, r.ab, r.xq2)

    def first_chunk():
        share_e_wait(0, 0)
        spatial_chunk(2, 0)
        share_e_on(0, 1)

    sums = total(7, chan, packed(*gg, chan), [spread_and_turn, first_chunk])
    share_e_on(0, 2)
    reduce_start(2, 0)
    reduce_middle(3, 0)
    share_v1 = share(5, r.v1, r.sib_v)
    norm_back(1, sums, chan)
    to_frames(1, r.time1, r.grad_mid)

    def other_chunks():
        for n in every[1:]:
            if n + 1 in every[3:]:
                share_e_on(0, n + 1)
            share_e_wait(0, n)
            spatial_chunk(2, n)
            reduce_start(2, n)
        credit(2)

    shared_e3 = temporal_back(3, r.w1t, [other_chunks])
    credit(0)
    reduce_last(3, 0)
    gg = through_act(0, r.mid1, r.grad_mid, mid)
    shared_e3.wait()
    share_v1.wait()
    sums = total(8, mid, packed(*gg, mid), temporal_grads(1, r.v1))
    reduce_start(1, 0)
    norm_back(0, sums, mid)
    fill_e(0, r.mid1)
    credited(2)
    share_e(1)
    for copy in shared_xq1:
        copy.wait()
    spread_x(r.xq1)
    transposes(r.xa, r.xb, r.xq1)
    share_e_on(1, 0)
    reduce_out(3)
    sent_tiles(out_grid, r.block_out, 2)
    for n in every:
        share_e_wait(1, n)
        spatial_chunk(0, n)
        reduce_start(0, n)
        if n + 1 in every:
            share_e_on(1, n + 1)
        reduce_middle(2, n)
    reduce_middle(1, 0)

    def back_pump(k):
        for n in (0, 1):
            pl.when(k == n + 1)(lambda n=n: reduce_middle(0, n))

    conv_back(r.ea, r.eb, r.w1s, r.grad_mid, back_pump)

    norm_copy = rc(r.norm_part.at[0], r.norm_part.at[1], r.norm_sem.at[0], r.norm_sem.at[1], beside)
    norm_copy.start()

    def last_body(i, _):
        grid_put(out_grid, i, (chunk(r.grad_mid, i, 0, chan) + chunk(r.grad_pre, i)) * keep(i))
        return 0

    loop(CHUNKS, last_body, 0)
    send_tiles(out_grid, r.grad_input, 3)
    for n in every:
        reduce_last(2, n)
    reduce_last(1, 0)
    for n in every:
        final_on(2, n)
    reduce_middle(0, 2)
    reduce_out(1)
    reduce_last(0, 0)
    reduce_last(0, 1)
    reduce_middle(0, 3)
    final_on(0, 0)
    reduce_last(0, 2)
    final_on(0, 1)
    norm_copy.wait()
    r.norm_grads[...] = r.norm_part[0] + r.norm_part[1]
    reduce_last(0, 3)
    final_on(0, 2)
    sent_tiles(out_grid, r.grad_input, 3)
    for n in every:
        reduce_wait(2, n)
    reduce_wait(3, 0)
    reduce_wait(1, 0)
    final_on(0, 3)
    for n in every:
        reduce_wait(0, n)


def per_device_fast(nb, *args):
    (
        inputs,
        starts,
        first_spatial,
        first_mid_gain,
        first_mid_bias,
        first_temporal,
        first_out_gain,
        first_out_bias,
        second_spatial,
        second_mid_gain,
        second_mid_bias,
        second_temporal,
        second_out_gain,
        second_out_bias,
        cotangent,
    ) = args
    micro, frames, side, _, chan = inputs.shape
    mid = first_spatial.shape[1]
    spat, temp = first_spatial.shape[0], first_temporal.shape[0]
    h, w, b = (lax.axis_index(name) for name in ("ha", "wa", "batch"))
    few = frames // 2
    offsets = jnp.arange(side)
    valid = (h * side + offsets < HGT)[:, None] & (w * side + offsets < HGT)[None, :]

    def tiles(array):
        array = array * valid.astype(BF16)[None, None, :, :, None]
        array = array.reshape(micro, 2, few, side, side, chan).transpose(0, 1, 3, 4, 2, 5)
        return array.reshape(4, side, side * few, chan)

    def untiled(array):
        array = array.reshape(micro, 2, side, side, few, chan).transpose(0, 1, 4, 2, 3, 5)
        return array.reshape(micro, frames, side, side, chan).astype(F32)

    gate = (1 - lax.dynamic_slice(starts, (w, h * few), (1, few))).astype(F32)
    gate = jnp.broadcast_to(gate.reshape(few, 1), (few, chan))
    here = jnp.where(h == 0, 1.0, 0.0)

    def placed(shard):
        row = jnp.zeros((mid,), F32)
        return lax.dynamic_update_slice(row, shard.astype(F32) * here, (b * shard.shape[0],))

    param = jnp.stack(
        [
            placed(v)
            for v in (
                first_mid_gain,
                first_mid_bias,
                first_out_gain,
                first_out_bias,
                second_mid_gain,
                second_mid_bias,
                second_out_gain,
                second_out_bias,
            )
        ]
    )
    half = chan // 2
    few_rows = ROWS // CELL

    inputs_of = dict(
        x_tiles=(tiles(inputs), pl.ANY),
        cot_tiles=(tiles(cotangent), pl.ANY),
        gate=(gate, pltpu.VMEM),
        param_in=(param, pltpu.VMEM),
        first_spatial=(first_spatial, pl.ANY),
        first_temporal=(first_temporal, pl.ANY),
        second_spatial=(second_spatial, pl.ANY),
        second_temporal=(second_temporal, pl.ANY),
    )
    outputs_of = dict(
        block_out=((4, side, side * CELL, chan), BF16, pl.ANY),
        grad_input=((4, side, side * CELL, chan), BF16, pl.ANY),
        norm_grads=((8, mid), F32, pltpu.VMEM),
        out1s=((spat, mid), BF16, pl.ANY),
        out1t=((2, temp, half), BF16, pl.ANY),
        out2s=((spat, mid), BF16, pl.ANY),
        out2t=((2, temp, half), BF16, pl.ANY),
    )
    dma = pltpu.SemaphoreType.DMA
    scratch_of = dict(
        w1s=pltpu.VMEM((9 * chan, mid), BF16),
        w1t=pltpu.VMEM((3 * mid, chan), BF16),
        w2s=pltpu.VMEM((9 * chan, mid), BF16),
        w2t=pltpu.VMEM((3 * mid, chan), BF16),
        x_grid=pltpu.VMEM((8, 8 * CELL, chan), BF16),
        cot_grid=pltpu.VMEM((8, 8 * CELL, chan), BF16),
        out_grid=pltpu.VMEM((8, 8 * CELL, chan), BF16),
        xa=pltpu.VMEM((PADDED, chan), BF16),
        xb=pltpu.VMEM((PADDED, chan), BF16),
        aa=pltpu.VMEM((PADDED, chan), BF16),
        ab=pltpu.VMEM((PADDED, chan), BF16),
        ea=pltpu.VMEM((PADDED, mid), BF16),
        eb=pltpu.VMEM((PADDED, mid), BF16),
        mid1=pltpu.VMEM((ROWS, mid), F32),
        mid2=pltpu.VMEM((ROWS, mid), F32),
        grad_mid=pltpu.VMEM((ROWS, mid), F32),
        v1=pltpu.VMEM((ROWS, mid), BF16),
        v2=pltpu.VMEM((ROWS, mid), BF16),
        time1=pltpu.VMEM((ROWS, chan), F32),
        time2=pltpu.VMEM((ROWS, chan), F32),
        grad_pre=pltpu.VMEM((ROWS, chan), F32),
        down=pltpu.VMEM((chan // 128, ROWS + CHUNK, 128), F32),
        up=pltpu.VMEM((chan // 128, ROWS + CHUNK, 128), F32),
        e3=pltpu.VMEM((3, ROWS, chan), BF16),
        sib_e3=pltpu.VMEM((3, ROWS, half), BF16),
        halo_out=pltpu.VMEM((2, few_rows, chan), F32),
        halo_in=pltpu.VMEM((4, 2, few_rows, chan), F32),
        param=pltpu.VMEM((8, mid), F32),
        tile_mid=pltpu.VMEM((2, 4, CELL, mid), F32),
        tile_out=pltpu.VMEM((2, 4, CELL, chan), F32),
        back=pltpu.VMEM((2, CELL, mid), F32),
        norm_part=pltpu.VMEM((2, 8, mid), F32),
        sum_b=pltpu.VMEM((2, 4, 8, mid), F32),
        sum_c=pltpu.VMEM((2, nb // 2, 8, mid), F32),
        own_sem=dma((4,)),
        ring_send=dma((4, 2, 2, nb)),
        ring_recv=dma((4, 2, 2, nb)),
        sib_send=dma((4, 3, 2, nb)),
        sib_recv=dma((4, 3, 2, nb)),
        over_send=dma((4, 2, nb)),
        over_recv=dma((4, 2, nb)),
        norm_sem=dma((2,)),
        credit=pltpu.SemaphoreType.REGULAR((3,)),
        sb_send=dma((9, 3)),
        sb_recv=dma((9, 4)),
        sc_send=dma((9, nb // 2)),
        sc_recv=dma((9, nb // 2)),
        halo_send=dma((4, 2)),
        halo_recv=dma((4, 2)),
        share_send=dma((6,)),
        share_recv=dma((6,)),
        e_all=pltpu.VMEM((4 * ROWS, mid), BF16),
        xq1=pltpu.VMEM((3, 2, PADDED, chan // 4), BF16),
        xq2=pltpu.VMEM((3, 2, PADDED, chan // 4), BF16),
        xt=pltpu.VMEM((mid, 2 * ROWS), BF16),
        xt2=pltpu.VMEM((mid, 2 * ROWS), BF16),
        sib_v=pltpu.VMEM((ROWS, mid), BF16),
        e_send=dma((2, 4, 3)),
        e_recv=dma((2, 4, 3)),
        xq_send=dma((2, 3)),
        xq_recv=dma((2, 3)),
        y_send=dma((4, 4, 5)),
        y_recv=dma((4, 4, 5)),
        z_send=dma((4, 4, 5)),
        z_recv=dma((4, 4, 7)),
        cast_send=dma((4, 4, 6)),
        cast_recv=dma((4, 4, 8)),
        out_sem=dma((4, 4, 2)),
        tile_send=dma((4, 3)),
        tile_recv=dma((4, 4)),
        tile_own=dma((4,)),
    )
    names = (*inputs_of, *outputs_of, *scratch_of)
    cell_count = float(frames * nb * HGT * HGT)
    results = pl.pallas_call(
        functools.partial(block_kernel, (nb, chan, mid, cell_count), names),
        out_shape=[jax.ShapeDtypeStruct(shape, dtype) for shape, dtype, _ in outputs_of.values()],
        in_specs=[pl.BlockSpec(memory_space=space) for _, space in inputs_of.values()],
        out_specs=[pl.BlockSpec(memory_space=space) for _, _, space in outputs_of.values()],
        scratch_shapes=list(scratch_of.values()),
        compiler_params=pltpu.CompilerParams(
            collective_id=0, has_side_effects=True, vmem_limit_bytes=VMEM_LIMIT
        ),
    )(*(array for array, _ in inputs_of.values()))
    got = SimpleNamespace(**dict(zip(outputs_of, results)))

    def temporal(pair):
        return jnp.concatenate([pair[0], pair[1]], axis=1).astype(F32)

    def norm(row, like):
        size = like.shape[0]
        return lax.dynamic_slice_in_dim(got.norm_grads[row], b * size, size)

    return (
        untiled(got.block_out),
        untiled(got.grad_input),
        got.out1s.astype(F32),
        norm(0, first_mid_gain),
        norm(1, first_mid_bias),
        temporal(got.out1t),
        norm(2, first_out_gain),
        norm(3, first_out_bias),
        got.out2s.astype(F32),
        norm(4, second_mid_gain),
        norm(5, second_mid_bias),
        temporal(got.out2t),
        norm(6, second_out_gain),
        norm(7, second_out_bias),
    )


def extended(shard, sides, width):
    for axis, dim in sides:
        count, length = (lax.axis_size(axis), shard.shape[dim])
        up = [(i, (i + 1) % count) for i in range(count - 1)]
        down = [(j, i) for i, j in up]
        last = lax.slice_in_dim(shard, length - width, length, axis=dim)
        leading = lax.slice_in_dim(shard, 0, width, axis=dim)
        before = lax.ppermute(last, axis, up)
        after = lax.ppermute(leading, axis, down)
        shard = jnp.concatenate([before, shard, after], axis=dim)
    return shard


def passed_along(shard, axis, by):
    count = lax.axis_size(axis)
    pairs = [(i, i + by) for i in range(count) if 0 <= i + by < count]
    return lax.ppermute(shard, axis, pairs)


def for_sending(shard):

    def short(part):
        return part.astype(jnp.bfloat16) if part.dtype == jnp.float32 else part

    return jax.tree.map(short, shard)


def silu_slope(values):
    sigma = jax.nn.sigmoid(values)
    return sigma * (1.0 + values * (1.0 - sigma))


def spatial_forward(field_in, kernel):
    frames, tile_side = (field_in.shape[0], field_in.shape[1])
    padded = extended(field_in, (("ha", 1), ("wa", 2)), 1)
    pieces = [
        padded[:, offset // 3 : offset // 3 + tile_side, offset % 3 : offset % 3 + tile_side, :]
        for offset in range(9)
    ]
    patches = jnp.concatenate(pieces, axis=-1).reshape(frames * tile_side * tile_side, -1)
    return (patches, jnp.dot(patches, kernel, preferred_element_type=jnp.float32))


def spatial_backward(grad_out, patches, kernel):
    frames, tile_side, channels = (grad_out.shape[0], grad_out.shape[1], grad_out.shape[3])
    row_count = frames * tile_side * tile_side
    padded = extended(grad_out, (("ha", 1), ("wa", 2)), 1)
    pieces = [
        padded[
            :,
            2 - offset // 3 : 2 - offset // 3 + tile_side,
            2 - offset % 3 : 2 - offset % 3 + tile_side,
            :,
        ]
        for offset in range(9)
    ]
    stacked = jnp.concatenate(pieces, axis=-1).reshape(row_count, 9, channels)
    grad_in = jnp.einsum(
        "rkm,kcm->rc", stacked, kernel.reshape(9, -1, channels), preferred_element_type=jnp.float32
    )
    grad_kernel = jnp.einsum(
        "rk,rm->km",
        patches,
        grad_out.reshape(row_count, channels),
        preferred_element_type=jnp.float32,
    )
    return (grad_in, grad_kernel)


def temporal_forward(field_in, clip_gate, kernel):
    frames, tile_side = (field_in.shape[0], field_in.shape[1])
    gated_in = field_in * clip_gate
    earlier = passed_along(field_in[-1:], "batch", 1)
    later_frame = passed_along(gated_in[:1], "batch", -1)
    before = jnp.concatenate([earlier, field_in[:-1]], axis=0) * clip_gate
    after_tap = jnp.concatenate([gated_in[1:], later_frame], axis=0)
    joined = jnp.concatenate([before, field_in, after_tap], axis=-1).reshape(
        frames * tile_side * tile_side, -1
    )
    return (joined, jnp.dot(joined, kernel, preferred_element_type=jnp.float32))


def temporal_backward(grad_out, joined, clip_gate, kernel):
    frames, tile_side, channels = (grad_out.shape[0], grad_out.shape[1], grad_out.shape[3])
    row_count = frames * tile_side * tile_side
    gated_grad = grad_out * clip_gate
    later_frame = passed_along(gated_grad[:1], "batch", -1)
    earlier = passed_along(grad_out[-1:], "batch", 1)
    from_later = jnp.concatenate([gated_grad[1:], later_frame], axis=0)
    from_earlier = jnp.concatenate([earlier, grad_out[:-1]], axis=0) * clip_gate
    stacked = jnp.concatenate([from_later, grad_out, from_earlier], axis=-1).reshape(
        row_count, 3, channels
    )
    grad_in = jnp.einsum(
        "rkc,kmc->rm", stacked, kernel.reshape(3, -1, channels), preferred_element_type=jnp.float32
    )
    grad_kernel = jnp.einsum(
        "rk,rc->kc",
        joined,
        grad_out.reshape(row_count, channels),
        preferred_element_type=jnp.float32,
    )
    return (grad_in, grad_kernel)


def norm_forward(pre_norm, norm_gain, norm_bias, valid_rows, cell_count):
    first_sum = jnp.sum(pre_norm * valid_rows, axis=0)
    square_sum = jnp.sum(pre_norm * pre_norm * valid_rows, axis=0)
    first_sum, square_sum = lax.psum((first_sum, square_sum), ("ha", "wa", "batch"))
    mean_val = first_sum / cell_count
    inv_std = lax.rsqrt(square_sum / cell_count - mean_val * mean_val + epsilon)
    normed = (pre_norm - mean_val) * inv_std
    return (normed, inv_std, normed * norm_gain.astype(jnp.float32) + norm_bias.astype(jnp.float32))


def norm_backward(grad_norm, normed, inv_std, norm_gain, valid_rows, cell_count):
    bias_grad = jnp.sum(grad_norm, axis=0)
    gain_grad = jnp.sum(grad_norm * normed, axis=0)
    bias_grad, gain_grad = lax.psum((bias_grad, gain_grad), ("ha", "wa", "batch"))
    grad_in = (
        valid_rows
        * norm_gain.astype(jnp.float32)
        * inv_std
        * (grad_norm - bias_grad / cell_count - normed * gain_grad / cell_count)
    )
    return (grad_in, gain_grad, bias_grad)


def forward_pair(field_in, weights, clip_gate, valid_rows, cell_count):
    frames, tile_side = (field_in.shape[0], field_in.shape[1])
    patches, spatial_out = spatial_forward(field_in, weights[0])
    mid_hat, mid_scale, mid_norm = norm_forward(
        spatial_out, weights[1], weights[2], valid_rows, cell_count
    )
    hidden = (
        (jax.nn.silu(mid_norm) * valid_rows)
        .astype(jnp.bfloat16)
        .reshape(frames, tile_side, tile_side, -1)
    )
    joined, temporal_out = temporal_forward(hidden, clip_gate, weights[3])
    out_hat, out_scale, out_norm = norm_forward(
        temporal_out, weights[4], weights[5], valid_rows, cell_count
    )
    return ((patches, mid_hat, mid_scale, mid_norm, joined, out_hat, out_scale), out_norm)


def backward_pair(grad_norm, kept, weights, clip_gate, valid_rows, cell_count, tile_side):
    patches, mid_hat, mid_scale, mid_norm, joined, out_hat, out_scale = kept
    frames = clip_gate.shape[0]
    grad_time, out_gain_grad, out_bias_grad = norm_backward(
        grad_norm, out_hat, out_scale, weights[4], valid_rows, cell_count
    )
    grad_time = grad_time.astype(jnp.bfloat16).reshape(frames, tile_side, tile_side, -1)
    grad_hidden, temporal_grad = temporal_backward(grad_time, joined, clip_gate, weights[3])
    grad_mid = grad_hidden * valid_rows * silu_slope(mid_norm)
    grad_spatial, mid_gain_grad, mid_bias_grad = norm_backward(
        grad_mid, mid_hat, mid_scale, weights[1], valid_rows, cell_count
    )
    grad_spatial = grad_spatial.astype(jnp.bfloat16).reshape(frames, tile_side, tile_side, -1)
    grad_in, spatial_grad = spatial_backward(grad_spatial, patches, weights[0])
    return (
        grad_in,
        (spatial_grad, mid_gain_grad, mid_bias_grad, temporal_grad, out_gain_grad, out_bias_grad),
    )


def per_device(
    inputs,
    starts,
    first_spatial,
    first_mid_gain,
    first_mid_bias,
    first_temporal,
    first_out_gain,
    first_out_bias,
    second_spatial,
    second_mid_gain,
    second_mid_bias,
    second_temporal,
    second_out_gain,
    second_out_bias,
    cotangent,
):
    shards = (
        first_spatial,
        first_mid_gain,
        first_mid_bias,
        first_temporal,
        first_out_gain,
        first_out_bias,
        second_spatial,
        second_mid_gain,
        second_mid_bias,
        second_temporal,
        second_out_gain,
        second_out_bias,
    )
    micro_total, frames, tile_side, channels = (
        inputs.shape[0],
        inputs.shape[1],
        inputs.shape[2],
        inputs.shape[4],
    )
    row_count = frames * tile_side * tile_side
    cell_count = frames * lax.axis_size("batch") * HGT * HGT
    offsets = jnp.arange(tile_side)
    inside_h = lax.axis_index("ha") * tile_side + offsets < HGT
    inside_w = lax.axis_index("wa") * tile_side + offsets < HGT
    valid_grid = inside_h[:, None] & inside_w[None, :]
    valid_tile = valid_grid.astype(jnp.bfloat16)[None, :, :, None]
    valid_rows = jnp.broadcast_to(
        valid_grid.astype(jnp.float32)[None], (frames, tile_side, tile_side)
    ).reshape(row_count, 1)
    results = []
    input_grads = []
    kernel_total = None
    norm_total = None
    for micro_step in range(micro_total):
        gathered = (
            lax.all_gather(shards[0], "batch", axis=0, tiled=True),
            lax.all_gather(shards[1], "batch", axis=0, tiled=True),
            lax.all_gather(shards[2], "batch", axis=0, tiled=True),
            lax.all_gather(shards[3], "batch", axis=0, tiled=True),
            lax.all_gather(shards[4], "batch", axis=0, tiled=True),
            lax.all_gather(shards[5], "batch", axis=0, tiled=True),
            lax.all_gather(shards[6], "batch", axis=0, tiled=True),
            lax.all_gather(shards[7], "batch", axis=0, tiled=True),
            lax.all_gather(shards[8], "batch", axis=0, tiled=True),
            lax.all_gather(shards[9], "batch", axis=0, tiled=True),
            lax.all_gather(shards[10], "batch", axis=0, tiled=True),
            lax.all_gather(shards[11], "batch", axis=0, tiled=True),
        )
        clip_gate = (1 - starts[micro_step]).astype(jnp.bfloat16).reshape(frames, 1, 1, 1)
        x_in = inputs[micro_step] * valid_tile
        first_kept, first_norm = forward_pair(
            x_in, gathered[0:6], clip_gate, valid_rows, cell_count
        )
        first_act = (
            (jax.nn.silu(first_norm) * valid_rows)
            .astype(jnp.bfloat16)
            .reshape(frames, tile_side, tile_side, channels)
        )
        second_kept, second_norm = forward_pair(
            first_act, gathered[6:12], clip_gate, valid_rows, cell_count
        )
        pre_out = second_norm + x_in.reshape(row_count, channels).astype(jnp.float32)
        results.append(
            (jax.nn.silu(pre_out) * valid_rows).reshape(frames, tile_side, tile_side, channels)
        )
        grad_pre = (
            cotangent[micro_step].reshape(row_count, channels).astype(jnp.float32)
            * valid_rows
            * silu_slope(pre_out)
        )
        grad_act, second_grads = backward_pair(
            grad_pre, second_kept, gathered[6:12], clip_gate, valid_rows, cell_count, tile_side
        )
        grad_first = grad_act * valid_rows * silu_slope(first_norm)
        grad_conv, first_grads = backward_pair(
            grad_first, first_kept, gathered[0:6], clip_gate, valid_rows, cell_count, tile_side
        )
        input_grads.append(
            ((grad_conv + grad_pre) * valid_rows).reshape(frames, tile_side, tile_side, channels)
        )
        step_grads = first_grads + second_grads
        kernel_now = (step_grads[0], step_grads[3], step_grads[6], step_grads[9])
        norm_now = (
            step_grads[1],
            step_grads[2],
            step_grads[4],
            step_grads[5],
            step_grads[7],
            step_grads[8],
            step_grads[10],
            step_grads[11],
        )
        if micro_step == 0:
            kernel_total = kernel_now
            norm_total = norm_now
        else:
            kernel_total = jax.tree.map(jnp.add, kernel_total, kernel_now)
            norm_total = jax.tree.map(jnp.add, norm_total, norm_now)
    kernel_total = lax.psum_scatter(kernel_total, "batch", scatter_dimension=0, tiled=True)
    kernel_total = jax.tree.map(
        lambda part: part.astype(jnp.float32), lax.psum(for_sending(kernel_total), ("ha", "wa"))
    )
    shard_index = lax.axis_index("batch")
    batch_count = lax.axis_size("batch")
    norm_shards = tuple(
        (
            lax.dynamic_slice_in_dim(
                full_sum,
                shard_index * (full_sum.shape[0] // batch_count),
                full_sum.shape[0] // batch_count,
            )
            for full_sum in norm_total
        )
    )
    return (
        jnp.stack(results),
        jnp.stack(input_grads),
        kernel_total[0],
        norm_shards[0],
        norm_shards[1],
        kernel_total[1],
        norm_shards[2],
        norm_shards[3],
        kernel_total[2],
        norm_shards[4],
        norm_shards[5],
        kernel_total[3],
        norm_shards[6],
        norm_shards[7],
    )


def solution(mesh):
    in_specs = (
        P(None, "batch", "ha", "wa", None),
        P(None, "batch"),
        P("batch", None),
        P("batch"),
        P("batch"),
        P("batch", None),
        P("batch"),
        P("batch"),
        P("batch", None),
        P("batch"),
        P("batch"),
        P("batch", None),
        P("batch"),
        P("batch"),
        P(None, "batch", "ha", "wa", None),
    )
    out_specs = (
        P(None, "batch", "ha", "wa", None),
        P(None, "batch", "ha", "wa", None),
        P("batch", None),
        P("batch"),
        P("batch"),
        P("batch", None),
        P("batch"),
        P("batch"),
        P("batch", None),
        P("batch"),
        P("batch"),
        P("batch", None),
        P("batch"),
        P("batch"),
    )
    batch = mesh.shape["batch"]

    def program(*args):
        spat, temp = args[2].shape[0], args[5].shape[0]
        fits = args[0].shape == (2, 16, 4, 4, 512) and args[2].shape[1] == 1152
        if fits and batch == 8 and spat * batch == 9 * 512 and temp * batch == 3 * 1152:
            return per_device_fast(batch, *args)
        return per_device(*args)

    return jax.shard_map(
        program, mesh=mesh, in_specs=in_specs, out_specs=out_specs, check_vma=False
    )
```

```python
import functools
from types import SimpleNamespace

import jax
import jax.numpy as jnp
from jax import lax
from jax.experimental import pallas as pl
from jax.experimental.pallas import tpu as pltpu
from jax.sharding import PartitionSpec as P

HGT = 7
epsilon = 1e-05
MESH = pl.DeviceIdType.MESH
F32 = jnp.float32
BF16 = jnp.bfloat16

BASE = 10
CELL = 8
ROWS = HGT * 8 * CELL
PADDED = (BASE + HGT * 8 + BASE) * CELL
MAIN = BASE * CELL
CHUNK = 2 * CELL
CHUNKS = ROWS // CHUNK
VMEM_LIMIT = 64 * 1024 * 1024 - 1024 * 1024


def when(cond, work):
    if cond is True:
        work()
    elif cond is not False:
        pl.when(cond)(work)


def loop(count, body, init):
    def twice(i, carry):
        return body(2 * i + 1, body(2 * i, carry))

    return lax.fori_loop(0, count // 2, twice, init)


def sigmoid(x):
    return 0.5 * jnp.tanh(0.5 * x) + 0.5


def nn(a, b):
    return jnp.dot(a, b, preferred_element_type=F32)


def nt(a, b):
    return lax.dot_general(a, b, (((1,), (1,)), ((), ())), preferred_element_type=F32)


def tn(a, b):
    return lax.dot_general(a, b, (((0,), (0,)), ((), ())), preferred_element_type=F32)


def rows_of(start, size, step=16):
    if not isinstance(start, int):
        start = pl.multiple_of(start, step)
    return pl.ds(start, size)


def block_kernel(dims, names, *all_refs):
    r = SimpleNamespace(**dict(zip(names, all_refs, strict=True)))
    nb, chan, mid, cell_count = dims
    spat = 9 * chan // nb
    temp = 3 * mid // nb
    unit = spat // 6
    quarter = chan // 4
    half = chan // 2
    h = lax.axis_index("ha")
    w = lax.axis_index("wa")
    b = lax.axis_index("batch")
    par = lax.rem(b, 2)
    bh = lax.div(b, 2)
    pos = par * (nb - 1 - bh) + (1 - par) * bh

    def at(p):
        p = lax.rem(p + 4 * nb, nb)
        upper = lax.div(p, nb // 2)
        return (1 - upper) * (2 * p) + upper * (2 * (nb - 1 - p) + 1)

    def at_group(j):
        return (lax.rem(j, 2), lax.div(j, 2))

    mine = 2 * w + h
    sibling = (1 - h, w, b)
    beside = (h, 1 - w, b)
    later_dev = (1 - h, w, lax.rem(b + h, nb))
    earlier_dev = (1 - h, w, lax.rem(b + nb - 1 + h, nb))
    tile_group = [(lax.rem(mine + d, 4), (*at_group(lax.rem(mine + d, 4)), b)) for d in (1, 2, 3)]
    across = (h, w, b + 1 - 2 * par)
    pos_b = h * 2 + par
    plane = []
    for d in (1, 2, 3):
        q = lax.rem(pos_b + d, 4)
        plane.append((q, (lax.div(q, 2), w, b - par + lax.rem(q, 2))))
    depth = nb // 2
    line = []
    for d in range(1, depth):
        q = lax.rem(bh + d, depth)
        line.append((q, (h, w, 2 * q + par)))

    def named(dev):
        return dict(ha=dev[0], wa=dev[1], batch=dev[2])

    def rc(src, dst, send, recv, dev):
        return pltpu.make_async_remote_copy(
            src_ref=src, dst_ref=dst, send_sem=send, recv_sem=recv, device_id=named(dev), device_id_type=MESH
        )

    def lc(src, dst, sem):
        return pltpu.make_async_copy(src, dst, sem)

    partners = [sibling, beside, (h, w, at(pos + 1)), (h, w, at(pos - 1)), later_dev, earlier_dev]
    partners += [dev for _, dev in tile_group + plane + line]
    barrier = pltpu.get_barrier_semaphore()
    for dev in partners:
        pl.semaphore_signal(barrier, inc=1, device_id=named(dev), device_id_type=MESH)
    pl.semaphore_wait(barrier, len(partners))

    shards = (r.first_spatial, r.first_temporal, r.second_spatial, r.second_temporal)
    whole = (r.w1s, r.w1t, r.w2s, r.w2t)
    shared = 2 * w + h
    shared_beside = 2 * (1 - w) + h
    way = 1 - 2 * h
    onward = (h, w, at(pos + way))
    third = temp // 3

    def taken(i, core, side):
        if i % 2 == 0:
            return 3 * unit * core + unit * side, 2 * unit
        return (1 - core) * 2 * third * side + core * third, third

    def crosses(i, core, side):
        if i % 2 == 0:
            return 3 * unit * core + 2 * unit * side, unit
        return 2 * third * side, third

    def rows_in(i, ref, owner, part):
        size = spat if i % 2 == 0 else temp
        return ref.at[rows_of(owner * size + part[0], part[1]), :]

    def pieces(i):
        start, size = taken(i, h, w)
        if i:
            return ((start, size),)
        return ((start, size // 2), (start + size // 2, size // 2))

    def crossing(i, work):
        if i % 2 == 0:
            work()
        else:
            pl.when(h == 0)(work)

    def own_copy(i):
        rows = spat if i % 2 == 0 else temp
        return lc(shards[i], whole[i].at[rows_of(b * rows, rows), :], r.own_sem.at[i])

    def ring(i, k, s, owner, from_shard=False):
        part = pieces(i)[k]
        dst = rows_in(i, whole[i], owner, part)
        src = rows_in(i, shards[i], 0, part) if from_shard else dst
        return rc(src, dst, r.ring_send.at[i], r.ring_recv.at[i, k, s], onward)

    def cross(i, owner, part):
        ref = rows_in(i, whole[i], owner, part)
        return rc(ref, ref, r.sib_send.at[i], r.sib_recv.at[i], sibling)

    def over(i, s, owner, part):
        ref = rows_in(i, whole[i], owner, part)
        return rc(ref, ref, r.over_send.at[i], r.over_recv.at[i, s], beside)

    def gather_start(i):
        for k in range(len(pieces(i))):
            ring(i, k, 1, b, True).start()
        own_copy(i).start()

    def gather_relay(i, s):
        owner = at(pos - way * s)

        def work():
            part = crosses(i, h, 1 - w)
            over(i, s, owner, part).wait_recv()
            cross(i, owner, part).start()

        crossing(i, work)

    def gather_pump(i, s):
        owner = at(pos - way * s)
        for k in range(len(pieces(i))):
            ring(i, k, s, owner).wait_recv()
            if isinstance(s, int):
                if s < nb - 1:
                    ring(i, k, s + 1, owner).start()
            else:
                pl.when(s < nb - 1)(lambda k=k: ring(i, k, s + 1, owner).start())
        crossing(i, lambda: over(i, s, owner, crosses(i, h, w)).start())
        cross(i, owner, taken(i, h, w)).start()
        if isinstance(s, int):
            if s > 1:
                gather_relay(i, s - 1)
        else:
            pl.when(s > 1)(lambda: gather_relay(i, s - 1))

    def span(i, size):
        return whole[i].at[0 : (nb - 1) * size, :]

    def gather_finish(i):
        gather_relay(i, nb - 1)

        def arrived(size):
            ref = span(i, size)
            rc(ref, ref, r.sib_send.at[i], r.sib_recv.at[i], sibling).wait_recv()

        if i % 2 == 0:
            arrived(3 * unit)
        else:
            pl.when(h == 0)(lambda: arrived(third))
            pl.when(h == 1)(lambda: arrived(2 * third))
        own_copy(i).wait()

    def gather_sent(i):
        def sent(size, sem):
            ref = span(i, size)
            rc(ref, ref, sem.at[i], r.own_sem.at[i], sibling).wait_send()

        sent(taken(i, h, w)[1], r.ring_send)
        crossing(i, lambda: sent(crosses(i, h, w)[1], r.over_send))
        if i % 2 == 0:
            sent(3 * unit, r.sib_send)
        else:
            pl.when(h == 0)(lambda: sent(2 * third, r.sib_send))
            pl.when(h == 1)(lambda: sent(third, r.sib_send))

    def total(k, width, value, works=()):
        slot = k % 2
        wide = value.shape[1]
        cols = pl.ds(0, wide)
        works = list(works) + [None] * 2
        four, far = r.sum_b, r.sum_c
        four[slot, pos_b, :, cols] = value

        def phase(ref, me, group, send, recv, work):
            for _, dev in group:
                part = ref.at[slot, me, :, cols]
                rc(part, part, send.at[k], recv.at[k], dev).start()
            if work:
                work()
            ref = ref.at[slot, 0 : len(group), :, cols]
            every = rc(ref, ref, send.at[k], recv.at[k], sibling)
            every.wait_recv()
            return every

        first = phase(four, pos_b, plane, r.sb_send, r.sb_recv, works[0])
        far[slot, bh, :, cols] = (four[slot, 0, :, cols] + four[slot, 1, :, cols]) + (
            four[slot, 2, :, cols] + four[slot, 3, :, cols]
        )
        second = phase(far, bh, line, r.sc_send, r.sc_recv, works[1])
        result = far[slot, 0, :, cols]
        for q in range(1, depth):
            result = result + far[slot, q, :, cols]
        first.wait_send()
        second.wait_send()
        if wide == width:
            return result
        return jnp.concatenate([result[2 * n : 2 * n + 2] for n in range(width // wide)], axis=1)

    def chunk(ref, i, base=0, width=None):
        cols = slice(None) if width is None else pl.ds(0, width)
        value = ref[rows_of(base + i * CHUNK, CHUNK), cols]
        return value.astype(F32).reshape(2, CELL, value.shape[-1])

    def put(ref, i, value, base=0, width=None):
        cols = slice(None) if width is None else pl.ds(0, width)
        ref[rows_of(base + i * CHUNK, CHUNK), cols] = value.reshape(CHUNK, value.shape[-1]).astype(ref.dtype)

    def keep(i):
        inside = jnp.where(lax.rem(i, 4) == 3, 0.0, 1.0).astype(F32)
        first = lax.broadcasted_iota(jnp.int32, (2, 1, 1), 0) == 0
        return jnp.where(first, 1.0, inside)

    def packed(one, two, width):
        rows = jnp.concatenate([jnp.sum(v, axis=0, keepdims=True) for v in (one, two)], axis=0)
        wide = 384 if width == mid else 128
        parts = [rows[:, n * wide : (n + 1) * wide] for n in range(width // wide)]
        return jnp.concatenate((parts + parts[-1:])[0:4], axis=0)

    def moments(ref, width):
        def body(i, carry):
            v = chunk(ref, i)
            m = v * keep(i)
            return (carry[0] + m[0] + m[1], carry[1] + m[0] * v[0] + m[1] * v[1])

        zero = jnp.zeros((CELL, width), F32)
        return loop(CHUNKS, body, (zero, zero))

    def prepare(n, sums, width):
        tile = r.tile_mid if width == mid else r.tile_out
        n2 = n // 2
        gain = r.param[2 * n : 2 * n + 1, 0:width]
        bias = r.param[2 * n + 1 : 2 * n + 2, 0:width]
        mean = sums[0:1] / cell_count
        inv = lax.rsqrt(sums[1:2] / cell_count - mean * mean + epsilon)
        scale = inv * gain
        shift = bias - mean * scale
        for k, v in enumerate((scale, shift, inv, mean * inv)):
            tile[n2, k] = jnp.broadcast_to(v, (CELL, width))

    def tiles(n, width):
        tile = r.tile_mid if width == mid else r.tile_out
        return [tile[n // 2, k][None] for k in range(4)]

    def fill(ref_a, ref_b, value_of, width):
        pads(ref_a, ref_b, width)

        def body(i, before):
            v = value_of(i)
            put(ref_a, i, v, MAIN)
            pair = jnp.concatenate([before[None], v[0:1]], axis=0)
            put(ref_b, i, pair, MAIN - CHUNK)
            return v[1]

        loop(CHUNKS, body, jnp.zeros((CELL, width), F32))

    def activated(src, n, width):
        def value(i):
            scale, shift, _, _ = tiles(n, width)
            y = chunk(src, i) * scale + shift
            return y * sigmoid(y) * keep(i)

        return value

    def taps(ref_a, ref_b, k, size=ROWS):
        r0 = MAIN - 8 * CELL + 8 * CELL * k
        return (
            ref_b[rows_of(r0 - CHUNK, size), :],
            ref_a[rows_of(r0, size), :],
            ref_b[rows_of(r0, size), :],
        )

    def conv(ref_a, ref_b, weight, out, pump=None):
        for n, (c0, cw) in enumerate(((0, 512), (512, mid - 512))):

            def body(a, _, c0=c0, cw=cw, n=n):
                x = taps(ref_a, ref_b, a)
                acc = nn(jnp.concatenate(x, axis=1), weight[rows_of(a * 3 * chan, 3 * chan), c0 : c0 + cw])

                @pl.when(a == 0)
                def _():
                    out[:, c0 : c0 + cw] = acc

                @pl.when(a > 0)
                def _():
                    out[:, c0 : c0 + cw] += acc

                if pump is not None:
                    pump(n * 3 + a)
                return 0

            lax.fori_loop(0, 3, body, 0)

    def conv_back(ref_a, ref_b, weight, out, pump=None):
        def body(k, _):
            e = taps(ref_a, ref_b, k)
            acc = None
            for j in range(3):
                tap = 8 - 3 * k - j
                term = nt(e[j], weight[rows_of(tap * chan, chan), :])
                acc = term if acc is None else acc + term

            @pl.when(k == 0)
            def _():
                out[:, 0:chan] = acc

            @pl.when(k > 0)
            def _():
                out[:, 0:chan] += acc

            if pump is not None:
                pump(k)
            return 0

        lax.fori_loop(0, 3, body, 0)

    def send_frames(k):
        down, up = r.down, r.up
        count = ROWS // CELL
        for c in range(chan // 128):
            lanes = pl.ds(128 * c, 128)
            r.halo_out[0, :, lanes] = down[c, pl.ds(2 * CELL - 1, count, stride=CELL), :]
            r.halo_out[1, :, lanes] = up[c, pl.ds(0, count, stride=CELL), :]
        copies = []
        for n, dev in ((0, later_dev), (1, earlier_dev)):
            copies.append(
                rc(r.halo_out.at[n], r.halo_in.at[k, n], r.halo_send.at[k, n], r.halo_recv.at[k, n], dev)
            )
            copies[-1].start()
        return copies

    def take_frames(k, copies):
        down, up = r.down, r.up
        count = ROWS // CELL
        for copy in copies:
            copy.wait()
        at_start = jnp.logical_and(h == 0, b == 0)
        at_end = jnp.logical_and(h == 1, b == nb - 1)
        for c in range(chan // 128):
            lanes = pl.ds(128 * c, 128)
            before = r.halo_in[k, 0, :, lanes]
            after = r.halo_in[k, 1, :, lanes]
            down[c, pl.ds(CELL - 1, count, stride=CELL), :] = jnp.where(at_start, 0.0, before)
            up[c, pl.ds(CELL, count, stride=CELL), :] = jnp.where(at_end, 0.0, after)

    def by_lanes(ref, rows):
        return jnp.concatenate([ref[c, rows, :] for c in range(chan // 128)], axis=1)

    def put_lanes(ref, rows, value):
        for c in range(chan // 128):
            ref[c, rows, :] = value[:, 128 * c : 128 * c + 128]

    def shifted(i):
        before = by_lanes(r.down, rows_of(i * CHUNK, CHUNK + CELL))[CELL - 1 : CELL - 1 + CHUNK]
        after = by_lanes(r.up, rows_of(i * CHUNK, CHUNK + CELL))[1 : 1 + CHUNK]
        gate = r.gate[...][None]
        return (before.reshape(2, CELL, chan) * gate, after.reshape(2, CELL, chan))

    def temporal(k, v, weight, out, works=()):
        works = list(works) + [None] * 2
        put_lanes(r.down, pl.ds(CELL, ROWS), nn(v[...], weight[0:mid, :]))
        y2 = nn(v[...], weight[2 * mid : 3 * mid, :])
        y2 = (y2.reshape(ROWS // CELL, CELL, chan) * r.gate[...][None]).reshape(ROWS, chan)
        put_lanes(r.up, pl.ds(0, ROWS), y2)
        copies = send_frames(k)
        out[...] = nn(v[...], weight[mid : 2 * mid, :])
        if works[0]:
            works[0]()
        take_frames(k, copies)

        def body(i, carry):
            before, after = shifted(i)
            value = chunk(out, i) + before + after
            put(out, i, value)
            m = value * keep(i)
            return (carry[0] + m[0] + m[1], carry[1] + m[0] * value[0] + m[1] * value[1])

        zero = jnp.zeros((CELL, chan), F32)
        return loop(CHUNKS, body, (zero, zero))

    def temporal_back(k, weight, works=()):
        works = list(works) + [None] * 2
        copies = send_frames(k)
        e3 = r.e3
        for c0, cw in ((0, 512), (512, mid - 512)):
            r.grad_mid[:, c0 : c0 + cw] = nt(e3[1], weight[mid + c0 : mid + c0 + cw, :])
        if works[0]:
            works[0]()
        take_frames(k, copies)

        def body(i, _):
            before, after = shifted(i)
            e3[0, rows_of(i * CHUNK, CHUNK), :] = after.reshape(CHUNK, chan).astype(BF16)
            e3[2, rows_of(i * CHUNK, CHUNK), :] = before.reshape(CHUNK, chan).astype(BF16)
            return 0

        loop(CHUNKS, body, 0)
        share = share_e3(k)
        for c0, cw in ((0, 512), (512, mid - 512)):
            r.grad_mid[:, c0 : c0 + cw] += nt(e3[0], weight[c0 : c0 + cw, :]) + nt(
                e3[2], weight[2 * mid + c0 : 2 * mid + c0 + cw, :]
            )
        return share

    def share(k, src, dst):
        copy = rc(src, dst, r.share_send.at[k], r.share_recv.at[k], sibling)
        copy.start()
        return copy

    outs = (r.out1s, r.out1t, r.out2s, r.out2t)

    halves = ((0, 512), (512, mid - 512))

    def e_part(n, slot):
        c0, cw = halves[n]
        return r.e_all.at[slot * ROWS : (slot + 1) * ROWS, c0 : c0 + cw]

    def e_copies(k, n):
        send, near, over = r.e_send.at[k, n], r.e_recv.at[k, n, 0], r.e_recv.at[k, n, 1]
        return [
            rc(e_part(n, 0), e_part(n, 1), send, near, sibling),
            rc(e_part(n, 0), e_part(n, 2), send, over, beside),
            rc(e_part(n, 2), e_part(n, 3), send, near, sibling),
        ]

    def share_e(k):
        for n in (0, 1):
            near, over, _ = e_copies(k, n)
            over.start()
            near.start()

    def share_e_on(k, n):
        _, over, far = e_copies(k, n)
        over.wait_recv()
        far.start()

    def share_e_wait(k, n):
        c0, cw = halves[n]
        both = r.e_all.at[0 : 2 * ROWS, c0 : c0 + cw]
        rc(both, both, r.e_send.at[k, n], r.e_recv.at[k, n, 0], sibling).wait_recv()
        three = r.e_all.at[0 : 3 * ROWS, c0 : c0 + cw]
        rc(three, three, r.e_send.at[k, n], r.e_recv.at[k, n, 0], sibling).wait_send()

    def share_x(k, xa, xq):
        main = pl.ds(MAIN, ROWS)
        for n, dev in enumerate((sibling, beside, (1 - h, 1 - w, b))):
            lanes = rows_of((2 * dev[1] + dev[0]) * quarter, quarter, 128)
            rc(xa.at[main, lanes], xq.at[n, 0, main, :], r.xq_send.at[k], r.xq_recv.at[k], dev).start()
        all_three = xq.at[:, 0, main, :]
        return rc(all_three, all_three, r.xq_send.at[k], r.xq_recv.at[k], sibling)

    def pads(ref_a, ref_b, width):
        ref_a[0:MAIN, :] = jnp.zeros((MAIN, width), BF16)
        ref_a[MAIN + ROWS : PADDED, :] = jnp.zeros((PADDED - MAIN - ROWS, width), BF16)
        ref_b[0 : MAIN - CHUNK, :] = jnp.zeros((MAIN - CHUNK, width), BF16)
        ref_b[MAIN - CHUNK + ROWS : PADDED, :] = jnp.zeros((PADDED - MAIN + CHUNK - ROWS, width), BF16)

    def spread_x(xq):
        for n in range(3):
            pads(xq.at[n, 0], xq.at[n, 1], quarter)

        def body(i, before):
            after = []
            for n in range(3):
                v = chunk(xq.at[n, 0], i, MAIN)
                put(xq.at[n, 1], i, jnp.concatenate([before[n][None], v[0:1]], axis=0), MAIN - CHUNK)
                after.append(v[1])
            return tuple(after)

        loop(CHUNKS, body, (jnp.zeros((CELL, quarter), F32),) * 3)

    def share_e3(k):
        return share(
            k - 2, r.e3.at[:, :, rows_of((1 - h) * half, half, 128)], r.sib_e3
        )

    def line_row(place):
        return quarter * place + 64 * jnp.where(place > shared, 1, 0)

    def grad_row(tap, side):
        split = 2 * shared + 1
        owner = jnp.where(tap == split, 2 * shared + side, tap - jnp.where(tap > split, 1, 0))
        row = line_row(lax.div(owner, 2)) + jnp.where(tap == split, quarter, 64 * side)
        return 576 * lax.rem(owner, 2) + row

    spare = r.w2s

    def gq(i, row, size):
        return rows_of((mid if i == 0 else 0) + row, size, 64)

    def inbox(i, row, size):
        return rows_of(2 * mid + (mid if i == 0 else 0) + row, size, 64)

    def transpose_x(a, xa, xb, xq, near, far, row):
        lanes = rows_of(shared * quarter, quarter, 128)
        r0 = MAIN - 8 * CELL + 8 * CELL * a
        for j, (c, start) in enumerate(((1, r0 - CHUNK), (0, r0), (1, r0))):
            rows = rows_of(start, ROWS)
            own = (xb if c else xa)[rows, lanes]
            both = jnp.concatenate([own, xq[0, c, rows, :]], axis=0)
            near[rows_of(row + j * quarter, quarter), 0 : 2 * ROWS] = both.T
            both = jnp.concatenate([xq[1, c, rows, :], xq[2, c, rows, :]], axis=0)
            far[rows_of(row + j * quarter, quarter), 0 : 2 * ROWS] = both.T

    def spatial_part(i, near, far, row, tap, n):
        c0, cw = halves[n]
        rows = rows_of(row, 3 * quarter)
        acc = nn(near[rows, 0 : 2 * ROWS], r.e_all[0 : 2 * ROWS, c0 : c0 + cw])
        acc += nn(far[rows, 0 : 2 * ROWS], r.e_all[2 * ROWS : 4 * ROWS, c0 : c0 + cw])
        acc = acc.astype(BF16)
        for j in range(6):
            spare[gq(i, grad_row(tap + j // 2, j % 2), 64), c0 : c0 + cw] = acc[64 * j : 64 * j + 64]

    def transposes(xa, xb, xq, near, far):
        def body(a, _):
            transpose_x(a, xa, xb, xq, near, far, a * 3 * quarter)
            return 0

        lax.fori_loop(0, 3, body, 0)

    def spatial_half(i, near, far, n):
        def body(a, _):
            spatial_part(i, near, far, a * 3 * quarter, 3 * a, n)
            return 0

        lax.fori_loop(0, 3, body, 0)

    def transpose_v(v, sv):
        for c in range(mid // 128):
            lanes = pl.ds(128 * c, 128)
            r.xt[128 * c : 128 * c + 128, :] = jnp.concatenate([v[:, lanes], sv[:, lanes]], axis=0).T

    def temporal_grad(i, k):
        e = jnp.concatenate([r.e3[k, :, rows_of(h * half, half, 128)], r.sib_e3[k]], axis=0)
        acc = nn(r.xt[...], e).astype(BF16)
        for n in range(mid // third):
            owner, part = divmod(k * (mid // third) + n, 3)
            row = (owner % 2) * (depth * temp) + owner // 2 * temp + part * third
            whole[i][row : row + third, 0:half] = acc[n * third : n * third + third]

    def cols_of(n):
        c0, cw = halves[n]
        return pl.ds(c0, cw)

    def parts_of(i):
        return (0, 1) if i % 2 == 0 else (0,)

    line_size = 576

    def to_y(i, n, side):
        if i % 2 == 0:
            return spare.at[gq(i, line_size * side, line_size), cols_of(n)]
        return whole[i].at[rows_of(depth * temp * side, depth * temp), 0:half]

    def y_box(i, n):
        if i % 2 == 0:
            return spare.at[inbox(i, 0, line_size), cols_of(n)]
        return whole[i].at[0 : depth * temp, half:chan]

    def block_of(i, n, place, size):
        if i % 2 == 0:
            return spare.at[gq(i, line_size * par + line_row(place), size), cols_of(n)]
        return whole[i].at[rows_of(depth * temp * par + place * temp, temp), 0:half]

    def z_box(i, n, slot, size):
        if i % 2 == 0:
            return spare.at[inbox(i, line_size + slot * (line_size // 3), size), cols_of(n)]
        return whole[i].at[(depth + slot) * temp : (depth + slot + 1) * temp, half:chan]

    def sized(i, place, work):
        if i % 2:
            work(temp)
        else:
            pl.when(place != shared)(lambda: work(quarter))
            pl.when(place == shared)(lambda: work(quarter + 64))

    def t_inbox(i, n):
        return whole[i].at[n * temp : (n + 1) * temp, half:chan]

    def add_into(dst, parts, step):
        rows, cols = dst.shape

        def body(n, _):
            at_rows = rows_of(n * step, step)
            value = dst[at_rows, :].astype(F32)
            for part in parts:
                value = value + part[at_rows, :].astype(F32)
            dst[at_rows, :] = value.astype(BF16)
            return 0

        lax.fori_loop(0, rows // step, body, 0)

    def y_copy(i, n):
        return rc(to_y(i, n, 1 - par), y_box(i, n), r.y_send.at[i, n], r.y_recv.at[i, n], across)

    def z_copy(i, n, d, size):
        place = lax.rem(bh + d, depth)
        dev = (h, w, 2 * place + par)
        src, dst = block_of(i, n, place, size), z_box(i, n, 3 - d, size)
        return rc(src, dst, r.z_send.at[i, n], r.z_recv.at[i, n], dev)

    def step_of(i):
        return 32 if i % 2 == 0 else 48

    def reduce_start(i, n):
        y_copy(i, n).start()

    def reduce_middle(i, n):
        y_copy(i, n).wait()
        add_into(to_y(i, n, par), [y_box(i, n)], step_of(i))
        for d in (1, 2, 3):
            sized(i, lax.rem(bh + d, depth), lambda size, d=d: z_copy(i, n, d, size).start())

    def final_part(i, n, side, core):
        place = 2 * side + core
        start = quarter * place - 64 * b + 512 * jnp.where(b > 2 * place, 1, 0)
        return outs[i].at[rows_of(start, quarter, 64), cols_of(n)]

    def extra_part(i, n):
        return outs[i].at[rows_of(512 * (1 - par), 64, 64), cols_of(n)]

    def final_copies(i, n):
        if i % 2:
            src = block_of(i, n, bh, temp)
            part = outs[i].at[h]
            return lc(src, part, r.out_sem.at[i, 0, 0]), [
                (src, part, sibling, r.cast_send.at[i, 0, 0], r.cast_recv.at[i, 0, 0])
            ]
        src = block_of(i, n, bh, quarter)
        part = final_part(i, n, w, h)
        sends = [
            (src, part, dev, r.cast_send.at[i, n, d], r.cast_recv.at[i, n, d]) for d, dev in enumerate((beside, sibling))
        ]
        return lc(src, part, r.out_sem.at[i, n, 0]), sends

    def extra_copies(i, n):
        src = spare.at[gq(i, line_size * par + line_row(bh) + quarter, 64), cols_of(n)]
        part = extra_part(i, n)
        sends = [
            (src, part, dev, r.cast_send.at[i, n, 3 + d], r.cast_recv.at[i, n, 3 + d])
            for d, dev in enumerate((beside, sibling))
        ]
        return lc(src, part, r.out_sem.at[i, n, 1]), sends

    def begin(copies):
        local, sends = copies
        for src, part, dev, one, two in sends:
            rc(src, part, one, two, dev).start()
        local.start()

    def credit(n):
        pl.semaphore_signal(r.credit.at[n], inc=1, device_id=named(beside), device_id_type=MESH)

    def credited(n):
        pl.semaphore_wait(r.credit.at[n], 1)

    def beside_copy(i):
        return rc(block_of(i, 0, bh, temp), t_inbox(i, 7), r.fin_send.at[i], r.fin_recv.at[i], beside)

    def z_span(i, n, rows):
        return to_y(i, n, 0).at[0:rows, :]

    def reduce_last(i, n):
        def add(size):
            ref = z_span(i, n, 3 * size)
            rc(ref, ref, r.z_send.at[i, n], r.z_recv.at[i, n], across).wait_recv()
            add_into(block_of(i, n, bh, size), [z_box(i, n, slot, size) for slot in range(3)], step_of(i))

        sized(i, bh, add)
        if i % 2:
            credited(i // 2)
            beside_copy(i).start()
            return
        begin(final_copies(i, n))
        pl.when(bh == shared)(lambda: begin(extra_copies(i, n)))

    def reduce_out(i):
        beside_copy(i).wait()
        add_into(block_of(i, 0, bh, temp), [t_inbox(i, 7)], 48)
        begin(final_copies(i, 0))

    def final_on(i, n):
        def move(part, d):
            rc(part, part, r.cast_send.at[i, n, d], r.cast_recv.at[i, n, d], beside).wait_recv()
            rc(part, part, r.cast_send.at[i, n, d + 2], r.cast_recv.at[i, n, d + 2], sibling).start()

        move(final_part(i, n, 1 - w, h), 0)
        pl.when(bh == shared_beside)(lambda: move(extra_part(i, n), 3))

    def reduce_wait(i, n):
        local, sends = final_copies(i, n)
        local.wait()

        def sent(rows):
            ref = z_span(i, n, rows)
            rc(ref, ref, r.z_send.at[i, n], r.z_recv.at[i, n], across).wait_send()

        if i % 2:
            sent(3 * temp)
        else:
            pl.when(bh == shared)(lambda: sent(3 * quarter))
            pl.when(bh != shared)(lambda: sent(3 * quarter + 64))
        if i % 2:
            src, part, dev, one, two = sends[0]
            rc(src, outs[i].at[1 - h], one, two, dev).wait()
            return
        for src, part, dev, one, two in sends:
            rc(src, part, one, two, dev).wait_send()

        def far(part, d):
            return rc(part, part, r.cast_send.at[i, n, d], r.cast_recv.at[i, n, d], sibling)

        far(final_part(i, n, w, 1 - h), 1).wait_recv()
        far(final_part(i, n, 1 - w, h), 2).wait_send()
        far(final_part(i, n, 1 - w, 1 - h), 2).wait_recv()
        local, sends = extra_copies(i, n)

        @pl.when(bh == shared)
        def _():
            local.wait()
            for src, part, dev, one, two in sends:
                rc(src, part, one, two, dev).wait_send()

        pl.when(bh == shared_beside)(lambda: far(extra_part(i, n), 5).wait_send())
        pl.when(bh == 2 * w + 1 - h)(lambda: far(extra_part(i, n), 4).wait_recv())
        pl.when(bh == 2 * (1 - w) + 1 - h)(lambda: far(extra_part(i, n), 5).wait_recv())

    def tile_of(ref, jh, jw):
        return ref.at[rows_of(jh * 4, 4, 4), rows_of(jw * 32, 32), :]

    def tile_own(src, dst, n):
        return lc(src.at[mine], tile_of(dst, h, w), r.tile_own.at[n])

    def tiles_start(src, dst, n):
        for j, dev in tile_group:
            rc(src.at[j], tile_of(dst, h, w), r.tile_send.at[n], r.tile_recv.at[n], dev).start()
        tile_own(src, dst, n).start()

    def tiles_wait(src, dst, n):
        three = src.at[0:3]
        rc(three, three, r.tile_send.at[n], r.tile_recv.at[n], sibling).wait()
        tile_own(src, dst, n).wait()

    xg, cg = r.x_grid, r.cot_grid
    tiles_start(r.x_tiles, xg, 0)
    gather_start(0)
    r.param[...] = total(0, mid, r.param_in[...])
    tiles_wait(r.x_tiles, xg, 0)

    def grid_chunk(ref, i):
        v = ref[lax.div(i, 4), rows_of(lax.rem(i, 4) * CHUNK, CHUNK), :]
        return v.astype(F32).reshape(2, CELL, chan)

    fill(r.xa, r.xb, lambda i: grid_chunk(xg, i), chan)

    def pump_loop(i, lo, hi):
        def body(s, _):
            gather_pump(i, s)
            return 0

        lax.fori_loop(lo, hi, body, 0)

    pump_loop(0, 1, nb - 3)
    gather_start(1)
    pump_loop(0, nb - 3, nb - 1)
    gather_start(2)
    gather_pump(0, nb - 1)
    gather_pump(1, 1)
    gather_pump(2, 1)
    gather_pump(1, 2)
    gather_finish(0)

    def first_pump(n):
        pl.when(lax.rem(n, 2) == 0)(lambda: gather_pump(1, 3 + lax.div(n, 2)))
        pl.when(n == 3)(lambda: gather_pump(2, 2))

    conv(r.xa, r.xb, r.w1s, r.mid1, first_pump)
    def first_last():
        gather_pump(2, 3)
        gather_pump(1, nb - 1)

    sums = total(
        1,
        mid,
        packed(*moments(r.mid1, mid), mid),
        [lambda: gather_pump(1, nb - 2), first_last],
    )
    prepare(0, sums, mid)

    def hidden(src, n, dst):
        value = activated(src, n, mid)

        def body(i, _):
            put(dst, i, value(i))
            return 0

        loop(CHUNKS, body, 0)

    hidden(r.mid1, 0, r.v1)
    gather_pump(2, 4)
    gather_finish(1)
    stats = temporal(0, r.v1, r.w1t, r.time1, [lambda: gather_pump(2, 5)])

    def sixth():
        gather_pump(2, 6)

    sums = total(2, chan, packed(*stats, chan), [lambda: gather_start(3), sixth])
    prepare(1, sums, chan)
    fill(r.aa, r.ab, activated(r.time1, 1, chan), chan)
    gather_pump(3, 1)
    gather_pump(2, nb - 1)
    gather_pump(3, 2)
    gather_finish(2)
    tiles_start(r.cot_tiles, cg, 1)

    def second_pump(n):
        pl.when(n < nb - 3)(lambda: gather_pump(3, 3 + n))

    conv(r.aa, r.ab, r.w2s, r.mid2, second_pump)
    sums = total(3, mid, packed(*moments(r.mid2, mid), mid), [lambda: gather_finish(3)])
    prepare(2, sums, mid)
    hidden(r.mid2, 2, r.v2)
    stats = temporal(1, r.v2, r.w2t, r.time2)
    shared_xq2 = share_x(0, r.aa, r.xq2)
    shared_xq1 = share_x(1, r.xa, r.xq1)
    for i in range(4):
        gather_sent(i)
    share_v2 = share(4, r.v2, r.sib_v)
    sums = total(4, chan, packed(*stats, chan))
    tiles_wait(r.cot_tiles, cg, 1)
    prepare(3, sums, chan)

    out_grid = r.out_grid

    def grid_put(ref, i, v):
        ref[lax.div(i, 4), rows_of(lax.rem(i, 4) * CHUNK, CHUNK), :] = v.reshape(CHUNK, chan).astype(ref.dtype)

    def slope(y, s):
        return s * (1.0 + y * (1.0 - s))

    def pre_body(i, carry):
        scale, shift, inv, offset = tiles(3, chan)
        v = chunk(r.time2, i)
        y = v * scale + shift + chunk(r.xa, i, MAIN)
        s = sigmoid(y)
        m = keep(i)
        grid_put(out_grid, i, y * s * m)
        d = grid_chunk(cg, i) * m * slope(y, s)
        put(r.grad_pre, i, d)
        t = d * (v * inv - offset)
        return (carry[0] + d[0] + d[1], carry[1] + t[0] + t[1])

    zero_out = jnp.zeros((CELL, chan), F32)
    zero_mid = jnp.zeros((CELL, mid), F32)
    out_grid[HGT] = jnp.zeros((8 * CELL, chan), BF16)
    gg = loop(CHUNKS, pre_body, (zero_out, zero_out))

    def send_tiles(src, dst, n):
        for j, dev in tile_group:
            jh, jw = at_group(j)
            rc(tile_of(src, jh, jw), dst.at[mine], r.tile_send.at[n], r.tile_recv.at[n], dev).start()
        lc(tile_of(src, h, w), dst.at[mine], r.tile_own.at[n]).start()

    def sent_tiles(src, dst, n):
        three = dst.at[0:3]
        rc(three, three, r.tile_send.at[n], r.tile_recv.at[n], sibling).wait()
        lc(tile_of(src, h, w), dst.at[mine], r.tile_own.at[n]).wait()

    send_tiles(out_grid, r.block_out, 2)

    def norm_back(n, sums, width):
        r.norm_part[0, 2 * n : 2 * n + 1, 0:width] = sums[1:2]
        r.norm_part[0, 2 * n + 1 : 2 * n + 2, 0:width] = sums[0:1]
        back = r.back
        back[0, :, 0:width] = jnp.broadcast_to(sums[0:1] / cell_count, (CELL, width))
        back[1, :, 0:width] = jnp.broadcast_to(sums[1:2] / cell_count, (CELL, width))

    def through_norm(n, src, grad, i, width):
        scale, _, inv, offset = tiles(n, width)
        xhat = chunk(src, i) * inv - offset
        bias_part = r.back[0, :, 0:width][None]
        gain_part = r.back[1, :, 0:width][None]
        return scale * (chunk(grad, i, 0, width) - bias_part - xhat * gain_part) * keep(i)

    def through_act(n, src, grad, width):
        def body(i, carry):
            scale, shift, inv, offset = tiles(n, width)
            v = chunk(src, i)
            y = v * scale + shift
            s = sigmoid(y)
            d = chunk(grad, i, 0, width) * keep(i) * slope(y, s)
            put(grad, i, d, 0, width)
            t = d * (v * inv - offset)
            return (carry[0] + d[0] + d[1], carry[1] + t[0] + t[1])

        zero = jnp.zeros((CELL, width), F32)
        return loop(CHUNKS, body, (zero, zero))

    def to_frames(n, src, grad):
        def body(i, _):
            e = through_norm(n, src, grad, i, chan).astype(BF16)
            ef = e.astype(F32)
            r.e3[1, rows_of(i * CHUNK, CHUNK), :] = e.reshape(CHUNK, chan)
            put_lanes(r.down, rows_of(i * CHUNK + CELL, CHUNK, CELL), ef.reshape(CHUNK, chan))
            put_lanes(r.up, rows_of(i * CHUNK, CHUNK), (ef * r.gate[...][None]).reshape(CHUNK, chan))
            return 0

        loop(CHUNKS, body, 0)

    sums = total(5, chan, packed(*gg, chan))
    norm_back(3, sums, chan)
    to_frames(3, r.time2, r.grad_pre)
    shared_e3 = temporal_back(2, r.w2t)
    credit(1)
    gg = through_act(2, r.mid2, r.grad_mid, mid)
    shared_e3.wait()
    share_v2.wait()
    def temporal_grads(i, v):
        def first():
            transpose_v(v, r.sib_v)
            temporal_grad(i, 0)

        def others():
            temporal_grad(i, 1)
            temporal_grad(i, 2)

        return [first, others]

    sums = total(6, mid, packed(*gg, mid), temporal_grads(3, r.v2))
    reduce_start(3, 0)
    norm_back(2, sums, mid)

    def fill_e(n, src):
        def value(i):
            v = through_norm(n, src, r.grad_mid, i, mid)
            put(r.e_all, i, v)
            return v

        fill(r.ea, r.eb, value, mid)

    fill_e(2, r.mid2)
    share_e(0)
    conv_back(r.ea, r.eb, r.w2s, r.grad_mid)
    share_e_on(0, 0)
    gg = through_act(1, r.time1, r.grad_mid, chan)
    shared_xq2.wait()
    near, far = spare.at[mid : 2 * mid, :], spare.at[3 * mid : 4 * mid, :]

    def spread_and_turn():
        spread_x(r.xq2)
        transposes(r.aa, r.ab, r.xq2, near, far)

    def first_half():
        share_e_wait(0, 0)
        spatial_half(2, near, far, 0)

    sums = total(7, chan, packed(*gg, chan), [spread_and_turn, first_half])
    share_e_on(0, 1)
    reduce_start(2, 0)
    reduce_middle(3, 0)
    share_v1 = share(5, r.v1, r.sib_v)
    norm_back(1, sums, chan)
    to_frames(1, r.time1, r.grad_mid)

    def second_half():
        share_e_wait(0, 1)
        spatial_half(2, near, far, 1)
        credit(2)
        reduce_start(2, 1)

    shared_e3 = temporal_back(3, r.w1t, [second_half])
    credit(0)
    reduce_last(3, 0)
    gg = through_act(0, r.mid1, r.grad_mid, mid)
    shared_e3.wait()
    share_v1.wait()
    sums = total(8, mid, packed(*gg, mid), temporal_grads(1, r.v1))
    reduce_start(1, 0)
    norm_back(0, sums, mid)
    fill_e(0, r.mid1)
    credited(2)
    share_e(1)
    reduce_out(3)
    for n in (0, 1):
        reduce_middle(2, n)
    shared_xq1.wait()
    spread_x(r.xq1)
    sent_tiles(out_grid, r.block_out, 2)
    conv_back(r.ea, r.eb, r.w1s, r.grad_mid)
    share_e_on(1, 0)
    near, far = r.w1s.at[0:mid, :], r.w1s.at[mid : 2 * mid, :]
    transposes(r.xa, r.xb, r.xq1, near, far)
    share_e_wait(1, 0)
    spatial_half(0, near, far, 0)
    reduce_start(0, 0)
    share_e_on(1, 1)
    share_e_wait(1, 1)
    spatial_half(0, near, far, 1)
    reduce_start(0, 1)

    norm_copy = rc(r.norm_part.at[0], r.norm_part.at[1], r.norm_sem.at[0], r.norm_sem.at[1], beside)
    norm_copy.start()

    def last_body(i, _):
        grid_put(out_grid, i, (chunk(r.grad_mid, i, 0, chan) + chunk(r.grad_pre, i)) * keep(i))
        return 0

    loop(CHUNKS, last_body, 0)
    send_tiles(out_grid, r.grad_input, 3)
    for n in (0, 1):
        reduce_last(2, n)
    reduce_middle(1, 0)
    for n in (0, 1):
        final_on(2, n)
    reduce_middle(0, 0)
    reduce_last(1, 0)
    reduce_out(1)
    reduce_last(0, 0)
    reduce_middle(0, 1)
    final_on(0, 0)
    reduce_last(0, 1)
    norm_copy.wait()
    r.norm_grads[...] = r.norm_part[0] + r.norm_part[1]
    sent_tiles(out_grid, r.grad_input, 3)
    for n in (0, 1):
        reduce_wait(2, n)
    reduce_wait(3, 0)
    final_on(0, 1)
    reduce_wait(1, 0)
    for n in (0, 1):
        reduce_wait(0, n)


def per_device_fast(nb, *args):
    (
        inputs,
        starts,
        first_spatial,
        first_mid_gain,
        first_mid_bias,
        first_temporal,
        first_out_gain,
        first_out_bias,
        second_spatial,
        second_mid_gain,
        second_mid_bias,
        second_temporal,
        second_out_gain,
        second_out_bias,
        cotangent,
    ) = args
    micro, frames, side, _, chan = inputs.shape
    mid = first_spatial.shape[1]
    spat, temp = first_spatial.shape[0], first_temporal.shape[0]
    h, w, b = (lax.axis_index(name) for name in ("ha", "wa", "batch"))
    few = frames // 2
    offsets = jnp.arange(side)
    valid = (h * side + offsets < HGT)[:, None] & (w * side + offsets < HGT)[None, :]

    def tiles(array):
        array = array * valid.astype(BF16)[None, None, :, :, None]
        array = array.reshape(micro, 2, few, side, side, chan).transpose(0, 1, 3, 4, 2, 5)
        return array.reshape(4, side, side * few, chan)

    def untiled(array):
        array = array.reshape(micro, 2, side, side, few, chan).transpose(0, 1, 4, 2, 3, 5)
        return array.reshape(micro, frames, side, side, chan).astype(F32)

    gate = (1 - lax.dynamic_slice(starts, (w, h * few), (1, few))).astype(F32)
    gate = jnp.broadcast_to(gate.reshape(few, 1), (few, chan))
    here = jnp.where(h == 0, 1.0, 0.0)

    def placed(shard):
        row = jnp.zeros((mid,), F32)
        return lax.dynamic_update_slice(row, shard.astype(F32) * here, (b * shard.shape[0],))

    param = jnp.stack(
        [
            placed(v)
            for v in (
                first_mid_gain,
                first_mid_bias,
                first_out_gain,
                first_out_bias,
                second_mid_gain,
                second_mid_bias,
                second_out_gain,
                second_out_bias,
            )
        ]
    )
    half = chan // 2
    few_rows = ROWS // CELL

    inputs_of = dict(
        x_tiles=(tiles(inputs), pl.ANY),
        cot_tiles=(tiles(cotangent), pl.ANY),
        gate=(gate, pltpu.VMEM),
        param_in=(param, pltpu.VMEM),
        first_spatial=(first_spatial, pl.ANY),
        first_temporal=(first_temporal, pl.ANY),
        second_spatial=(second_spatial, pl.ANY),
        second_temporal=(second_temporal, pl.ANY),
    )
    outputs_of = dict(
        block_out=((4, side, side * CELL, chan), BF16, pl.ANY),
        grad_input=((4, side, side * CELL, chan), BF16, pl.ANY),
        norm_grads=((8, mid), F32, pltpu.VMEM),
        out1s=((spat, mid), BF16, pl.ANY),
        out1t=((2, temp, half), BF16, pl.ANY),
        out2s=((spat, mid), BF16, pl.ANY),
        out2t=((2, temp, half), BF16, pl.ANY),
    )
    dma = pltpu.SemaphoreType.DMA
    scratch_of = dict(
        w1s=pltpu.VMEM((9 * chan, mid), BF16),
        w1t=pltpu.VMEM((3 * mid, chan), BF16),
        w2s=pltpu.VMEM((9 * chan, mid), BF16),
        w2t=pltpu.VMEM((3 * mid, chan), BF16),
        x_grid=pltpu.VMEM((8, 8 * CELL, chan), BF16),
        cot_grid=pltpu.VMEM((8, 8 * CELL, chan), BF16),
        out_grid=pltpu.VMEM((8, 8 * CELL, chan), BF16),
        xa=pltpu.VMEM((PADDED, chan), BF16),
        xb=pltpu.VMEM((PADDED, chan), BF16),
        aa=pltpu.VMEM((PADDED, chan), BF16),
        ab=pltpu.VMEM((PADDED, chan), BF16),
        ea=pltpu.VMEM((PADDED, mid), BF16),
        eb=pltpu.VMEM((PADDED, mid), BF16),
        mid1=pltpu.VMEM((ROWS, mid), F32),
        mid2=pltpu.VMEM((ROWS, mid), F32),
        grad_mid=pltpu.VMEM((ROWS, mid), F32),
        v1=pltpu.VMEM((ROWS, mid), BF16),
        v2=pltpu.VMEM((ROWS, mid), BF16),
        time1=pltpu.VMEM((ROWS, chan), F32),
        time2=pltpu.VMEM((ROWS, chan), F32),
        grad_pre=pltpu.VMEM((ROWS, chan), F32),
        down=pltpu.VMEM((chan // 128, ROWS + CHUNK, 128), F32),
        up=pltpu.VMEM((chan // 128, ROWS + CHUNK, 128), F32),
        e3=pltpu.VMEM((3, ROWS, chan), BF16),
        sib_e3=pltpu.VMEM((3, ROWS, half), BF16),
        halo_out=pltpu.VMEM((2, few_rows, chan), F32),
        halo_in=pltpu.VMEM((4, 2, few_rows, chan), F32),
        param=pltpu.VMEM((8, mid), F32),
        tile_mid=pltpu.VMEM((2, 4, CELL, mid), F32),
        tile_out=pltpu.VMEM((2, 4, CELL, chan), F32),
        back=pltpu.VMEM((2, CELL, mid), F32),
        norm_part=pltpu.VMEM((2, 8, mid), F32),
        sum_b=pltpu.VMEM((2, 4, 8, mid), F32),
        sum_c=pltpu.VMEM((2, nb // 2, 8, mid), F32),
        own_sem=dma((4,)),
        ring_send=dma((4,)),
        ring_recv=dma((4, 2, nb)),
        sib_send=dma((4,)),
        sib_recv=dma((4,)),
        over_send=dma((4,)),
        over_recv=dma((4, nb)),
        norm_sem=dma((2,)),
        credit=pltpu.SemaphoreType.REGULAR((3,)),
        sb_send=dma((9,)),
        sb_recv=dma((9,)),
        sc_send=dma((9,)),
        sc_recv=dma((9,)),
        halo_send=dma((4, 2)),
        halo_recv=dma((4, 2)),
        share_send=dma((6,)),
        share_recv=dma((6,)),
        e_all=pltpu.VMEM((4 * ROWS, mid), BF16),
        xq1=pltpu.VMEM((3, 2, PADDED, chan // 4), BF16),
        xq2=pltpu.VMEM((3, 2, PADDED, chan // 4), BF16),
        xt=pltpu.VMEM((mid, 2 * ROWS), BF16),
        sib_v=pltpu.VMEM((ROWS, mid), BF16),
        e_send=dma((2, 2)),
        e_recv=dma((2, 2, 2)),
        xq_send=dma((2,)),
        xq_recv=dma((2,)),
        y_send=dma((4, 2)),
        y_recv=dma((4, 2)),
        z_send=dma((4, 2)),
        z_recv=dma((4, 2)),
        cast_send=dma((4, 2, 6)),
        cast_recv=dma((4, 2, 8)),
        out_sem=dma((4, 2, 2)),
        fin_send=dma((4,)),
        fin_recv=dma((4,)),
        tile_send=dma((4,)),
        tile_recv=dma((4,)),
        tile_own=dma((4,)),
    )
    names = (*inputs_of, *outputs_of, *scratch_of)
    cell_count = float(frames * nb * HGT * HGT)
    results = pl.pallas_call(
        functools.partial(block_kernel, (nb, chan, mid, cell_count), names),
        out_shape=[jax.ShapeDtypeStruct(shape, dtype) for shape, dtype, _ in outputs_of.values()],
        in_specs=[pl.BlockSpec(memory_space=space) for _, space in inputs_of.values()],
        out_specs=[pl.BlockSpec(memory_space=space) for _, _, space in outputs_of.values()],
        scratch_shapes=list(scratch_of.values()),
        compiler_params=pltpu.CompilerParams(
            collective_id=0, has_side_effects=True, vmem_limit_bytes=VMEM_LIMIT
        ),
    )(*(array for array, _ in inputs_of.values()))
    got = SimpleNamespace(**dict(zip(outputs_of, results)))

    def temporal(pair):
        return jnp.concatenate([pair[0], pair[1]], axis=1).astype(F32)

    def norm(row, like):
        size = like.shape[0]
        return lax.dynamic_slice_in_dim(got.norm_grads[row], b * size, size)

    return (
        untiled(got.block_out),
        untiled(got.grad_input),
        got.out1s.astype(F32),
        norm(0, first_mid_gain),
        norm(1, first_mid_bias),
        temporal(got.out1t),
        norm(2, first_out_gain),
        norm(3, first_out_bias),
        got.out2s.astype(F32),
        norm(4, second_mid_gain),
        norm(5, second_mid_bias),
        temporal(got.out2t),
        norm(6, second_out_gain),
        norm(7, second_out_bias),
    )


def extended(shard, sides, width):
    for axis, dim in sides:
        count, length = (lax.axis_size(axis), shard.shape[dim])
        up = [(i, (i + 1) % count) for i in range(count - 1)]
        down = [(j, i) for i, j in up]
        last = lax.slice_in_dim(shard, length - width, length, axis=dim)
        leading = lax.slice_in_dim(shard, 0, width, axis=dim)
        before = lax.ppermute(last, axis, up)
        after = lax.ppermute(leading, axis, down)
        shard = jnp.concatenate([before, shard, after], axis=dim)
    return shard


def passed_along(shard, axis, by):
    count = lax.axis_size(axis)
    pairs = [(i, i + by) for i in range(count) if 0 <= i + by < count]
    return lax.ppermute(shard, axis, pairs)


def for_sending(shard):

    def short(part):
        return part.astype(jnp.bfloat16) if part.dtype == jnp.float32 else part

    return jax.tree.map(short, shard)


def silu_slope(values):
    sigma = jax.nn.sigmoid(values)
    return sigma * (1.0 + values * (1.0 - sigma))


def spatial_forward(field_in, kernel):
    frames, tile_side = (field_in.shape[0], field_in.shape[1])
    padded = extended(field_in, (("ha", 1), ("wa", 2)), 1)
    pieces = [
        padded[:, offset // 3 : offset // 3 + tile_side, offset % 3 : offset % 3 + tile_side, :]
        for offset in range(9)
    ]
    patches = jnp.concatenate(pieces, axis=-1).reshape(frames * tile_side * tile_side, -1)
    return (patches, jnp.dot(patches, kernel, preferred_element_type=jnp.float32))


def spatial_backward(grad_out, patches, kernel):
    frames, tile_side, channels = (grad_out.shape[0], grad_out.shape[1], grad_out.shape[3])
    row_count = frames * tile_side * tile_side
    padded = extended(grad_out, (("ha", 1), ("wa", 2)), 1)
    pieces = [
        padded[
            :,
            2 - offset // 3 : 2 - offset // 3 + tile_side,
            2 - offset % 3 : 2 - offset % 3 + tile_side,
            :,
        ]
        for offset in range(9)
    ]
    stacked = jnp.concatenate(pieces, axis=-1).reshape(row_count, 9, channels)
    grad_in = jnp.einsum(
        "rkm,kcm->rc", stacked, kernel.reshape(9, -1, channels), preferred_element_type=jnp.float32
    )
    grad_kernel = jnp.einsum(
        "rk,rm->km",
        patches,
        grad_out.reshape(row_count, channels),
        preferred_element_type=jnp.float32,
    )
    return (grad_in, grad_kernel)


def temporal_forward(field_in, clip_gate, kernel):
    frames, tile_side = (field_in.shape[0], field_in.shape[1])
    gated_in = field_in * clip_gate
    earlier = passed_along(field_in[-1:], "batch", 1)
    later_frame = passed_along(gated_in[:1], "batch", -1)
    before = jnp.concatenate([earlier, field_in[:-1]], axis=0) * clip_gate
    after_tap = jnp.concatenate([gated_in[1:], later_frame], axis=0)
    joined = jnp.concatenate([before, field_in, after_tap], axis=-1).reshape(
        frames * tile_side * tile_side, -1
    )
    return (joined, jnp.dot(joined, kernel, preferred_element_type=jnp.float32))


def temporal_backward(grad_out, joined, clip_gate, kernel):
    frames, tile_side, channels = (grad_out.shape[0], grad_out.shape[1], grad_out.shape[3])
    row_count = frames * tile_side * tile_side
    gated_grad = grad_out * clip_gate
    later_frame = passed_along(gated_grad[:1], "batch", -1)
    earlier = passed_along(grad_out[-1:], "batch", 1)
    from_later = jnp.concatenate([gated_grad[1:], later_frame], axis=0)
    from_earlier = jnp.concatenate([earlier, grad_out[:-1]], axis=0) * clip_gate
    stacked = jnp.concatenate([from_later, grad_out, from_earlier], axis=-1).reshape(
        row_count, 3, channels
    )
    grad_in = jnp.einsum(
        "rkc,kmc->rm", stacked, kernel.reshape(3, -1, channels), preferred_element_type=jnp.float32
    )
    grad_kernel = jnp.einsum(
        "rk,rc->kc",
        joined,
        grad_out.reshape(row_count, channels),
        preferred_element_type=jnp.float32,
    )
    return (grad_in, grad_kernel)


def norm_forward(pre_norm, norm_gain, norm_bias, valid_rows, cell_count):
    first_sum = jnp.sum(pre_norm * valid_rows, axis=0)
    square_sum = jnp.sum(pre_norm * pre_norm * valid_rows, axis=0)
    first_sum, square_sum = lax.psum((first_sum, square_sum), ("ha", "wa", "batch"))
    mean_val = first_sum / cell_count
    inv_std = lax.rsqrt(square_sum / cell_count - mean_val * mean_val + epsilon)
    normed = (pre_norm - mean_val) * inv_std
    return (normed, inv_std, normed * norm_gain.astype(jnp.float32) + norm_bias.astype(jnp.float32))


def norm_backward(grad_norm, normed, inv_std, norm_gain, valid_rows, cell_count):
    bias_grad = jnp.sum(grad_norm, axis=0)
    gain_grad = jnp.sum(grad_norm * normed, axis=0)
    bias_grad, gain_grad = lax.psum((bias_grad, gain_grad), ("ha", "wa", "batch"))
    grad_in = (
        valid_rows
        * norm_gain.astype(jnp.float32)
        * inv_std
        * (grad_norm - bias_grad / cell_count - normed * gain_grad / cell_count)
    )
    return (grad_in, gain_grad, bias_grad)


def forward_pair(field_in, weights, clip_gate, valid_rows, cell_count):
    frames, tile_side = (field_in.shape[0], field_in.shape[1])
    patches, spatial_out = spatial_forward(field_in, weights[0])
    mid_hat, mid_scale, mid_norm = norm_forward(
        spatial_out, weights[1], weights[2], valid_rows, cell_count
    )
    hidden = (
        (jax.nn.silu(mid_norm) * valid_rows)
        .astype(jnp.bfloat16)
        .reshape(frames, tile_side, tile_side, -1)
    )
    joined, temporal_out = temporal_forward(hidden, clip_gate, weights[3])
    out_hat, out_scale, out_norm = norm_forward(
        temporal_out, weights[4], weights[5], valid_rows, cell_count
    )
    return ((patches, mid_hat, mid_scale, mid_norm, joined, out_hat, out_scale), out_norm)


def backward_pair(grad_norm, kept, weights, clip_gate, valid_rows, cell_count, tile_side):
    patches, mid_hat, mid_scale, mid_norm, joined, out_hat, out_scale = kept
    frames = clip_gate.shape[0]
    grad_time, out_gain_grad, out_bias_grad = norm_backward(
        grad_norm, out_hat, out_scale, weights[4], valid_rows, cell_count
    )
    grad_time = grad_time.astype(jnp.bfloat16).reshape(frames, tile_side, tile_side, -1)
    grad_hidden, temporal_grad = temporal_backward(grad_time, joined, clip_gate, weights[3])
    grad_mid = grad_hidden * valid_rows * silu_slope(mid_norm)
    grad_spatial, mid_gain_grad, mid_bias_grad = norm_backward(
        grad_mid, mid_hat, mid_scale, weights[1], valid_rows, cell_count
    )
    grad_spatial = grad_spatial.astype(jnp.bfloat16).reshape(frames, tile_side, tile_side, -1)
    grad_in, spatial_grad = spatial_backward(grad_spatial, patches, weights[0])
    return (
        grad_in,
        (spatial_grad, mid_gain_grad, mid_bias_grad, temporal_grad, out_gain_grad, out_bias_grad),
    )


def per_device(
    inputs,
    starts,
    first_spatial,
    first_mid_gain,
    first_mid_bias,
    first_temporal,
    first_out_gain,
    first_out_bias,
    second_spatial,
    second_mid_gain,
    second_mid_bias,
    second_temporal,
    second_out_gain,
    second_out_bias,
    cotangent,
):
    shards = (
        first_spatial,
        first_mid_gain,
        first_mid_bias,
        first_temporal,
        first_out_gain,
        first_out_bias,
        second_spatial,
        second_mid_gain,
        second_mid_bias,
        second_temporal,
        second_out_gain,
        second_out_bias,
    )
    micro_total, frames, tile_side, channels = (
        inputs.shape[0],
        inputs.shape[1],
        inputs.shape[2],
        inputs.shape[4],
    )
    row_count = frames * tile_side * tile_side
    cell_count = frames * lax.axis_size("batch") * HGT * HGT
    offsets = jnp.arange(tile_side)
    inside_h = lax.axis_index("ha") * tile_side + offsets < HGT
    inside_w = lax.axis_index("wa") * tile_side + offsets < HGT
    valid_grid = inside_h[:, None] & inside_w[None, :]
    valid_tile = valid_grid.astype(jnp.bfloat16)[None, :, :, None]
    valid_rows = jnp.broadcast_to(
        valid_grid.astype(jnp.float32)[None], (frames, tile_side, tile_side)
    ).reshape(row_count, 1)
    results = []
    input_grads = []
    kernel_total = None
    norm_total = None
    for micro_step in range(micro_total):
        gathered = (
            lax.all_gather(shards[0], "batch", axis=0, tiled=True),
            lax.all_gather(shards[1], "batch", axis=0, tiled=True),
            lax.all_gather(shards[2], "batch", axis=0, tiled=True),
            lax.all_gather(shards[3], "batch", axis=0, tiled=True),
            lax.all_gather(shards[4], "batch", axis=0, tiled=True),
            lax.all_gather(shards[5], "batch", axis=0, tiled=True),
            lax.all_gather(shards[6], "batch", axis=0, tiled=True),
            lax.all_gather(shards[7], "batch", axis=0, tiled=True),
            lax.all_gather(shards[8], "batch", axis=0, tiled=True),
            lax.all_gather(shards[9], "batch", axis=0, tiled=True),
            lax.all_gather(shards[10], "batch", axis=0, tiled=True),
            lax.all_gather(shards[11], "batch", axis=0, tiled=True),
        )
        clip_gate = (1 - starts[micro_step]).astype(jnp.bfloat16).reshape(frames, 1, 1, 1)
        x_in = inputs[micro_step] * valid_tile
        first_kept, first_norm = forward_pair(
            x_in, gathered[0:6], clip_gate, valid_rows, cell_count
        )
        first_act = (
            (jax.nn.silu(first_norm) * valid_rows)
            .astype(jnp.bfloat16)
            .reshape(frames, tile_side, tile_side, channels)
        )
        second_kept, second_norm = forward_pair(
            first_act, gathered[6:12], clip_gate, valid_rows, cell_count
        )
        pre_out = second_norm + x_in.reshape(row_count, channels).astype(jnp.float32)
        results.append(
            (jax.nn.silu(pre_out) * valid_rows).reshape(frames, tile_side, tile_side, channels)
        )
        grad_pre = (
            cotangent[micro_step].reshape(row_count, channels).astype(jnp.float32)
            * valid_rows
            * silu_slope(pre_out)
        )
        grad_act, second_grads = backward_pair(
            grad_pre, second_kept, gathered[6:12], clip_gate, valid_rows, cell_count, tile_side
        )
        grad_first = grad_act * valid_rows * silu_slope(first_norm)
        grad_conv, first_grads = backward_pair(
            grad_first, first_kept, gathered[0:6], clip_gate, valid_rows, cell_count, tile_side
        )
        input_grads.append(
            ((grad_conv + grad_pre) * valid_rows).reshape(frames, tile_side, tile_side, channels)
        )
        step_grads = first_grads + second_grads
        kernel_now = (step_grads[0], step_grads[3], step_grads[6], step_grads[9])
        norm_now = (
            step_grads[1],
            step_grads[2],
            step_grads[4],
            step_grads[5],
            step_grads[7],
            step_grads[8],
            step_grads[10],
            step_grads[11],
        )
        if micro_step == 0:
            kernel_total = kernel_now
            norm_total = norm_now
        else:
            kernel_total = jax.tree.map(jnp.add, kernel_total, kernel_now)
            norm_total = jax.tree.map(jnp.add, norm_total, norm_now)
    kernel_total = lax.psum_scatter(kernel_total, "batch", scatter_dimension=0, tiled=True)
    kernel_total = jax.tree.map(
        lambda part: part.astype(jnp.float32), lax.psum(for_sending(kernel_total), ("ha", "wa"))
    )
    shard_index = lax.axis_index("batch")
    batch_count = lax.axis_size("batch")
    norm_shards = tuple(
        (
            lax.dynamic_slice_in_dim(
                full_sum,
                shard_index * (full_sum.shape[0] // batch_count),
                full_sum.shape[0] // batch_count,
            )
            for full_sum in norm_total
        )
    )
    return (
        jnp.stack(results),
        jnp.stack(input_grads),
        kernel_total[0],
        norm_shards[0],
        norm_shards[1],
        kernel_total[1],
        norm_shards[2],
        norm_shards[3],
        kernel_total[2],
        norm_shards[4],
        norm_shards[5],
        kernel_total[3],
        norm_shards[6],
        norm_shards[7],
    )


def solution(mesh):
    in_specs = (
        P(None, "batch", "ha", "wa", None),
        P(None, "batch"),
        P("batch", None),
        P("batch"),
        P("batch"),
        P("batch", None),
        P("batch"),
        P("batch"),
        P("batch", None),
        P("batch"),
        P("batch"),
        P("batch", None),
        P("batch"),
        P("batch"),
        P(None, "batch", "ha", "wa", None),
    )
    out_specs = (
        P(None, "batch", "ha", "wa", None),
        P(None, "batch", "ha", "wa", None),
        P("batch", None),
        P("batch"),
        P("batch"),
        P("batch", None),
        P("batch"),
        P("batch"),
        P("batch", None),
        P("batch"),
        P("batch"),
        P("batch", None),
        P("batch"),
        P("batch"),
    )
    batch = mesh.shape["batch"]

    def program(*args):
        spat, temp = args[2].shape[0], args[5].shape[0]
        fits = args[0].shape == (2, 16, 4, 4, 512) and args[2].shape[1] == 1152
        if fits and batch == 8 and spat * batch == 9 * 512 and temp * batch == 3 * 1152:
            return per_device_fast(batch, *args)
        return per_device(*args)

    return jax.shard_map(
        program, mesh=mesh, in_specs=in_specs, out_specs=out_specs, check_vma=False
    )
```

```python
import functools
from types import SimpleNamespace

import jax
import jax.numpy as jnp
from jax import lax
from jax.experimental import pallas as pl
from jax.experimental.pallas import tpu as pltpu
from jax.sharding import PartitionSpec as P

HGT = 7
epsilon = 1e-05
MESH = pl.DeviceIdType.MESH
F32 = jnp.float32
BF16 = jnp.bfloat16

BASE = 10
CELL = 8
ROWS = HGT * 8 * CELL
PADDED = (BASE + HGT * 8 + BASE) * CELL
MAIN = BASE * CELL
CHUNK = 2 * CELL
CHUNKS = ROWS // CHUNK
VMEM_LIMIT = 64 * 1024 * 1024 - 1024 * 1024


def when(cond, work):
    if cond is True:
        work()
    elif cond is not False:
        pl.when(cond)(work)


def loop(count, body, init):
    def twice(i, carry):
        return body(2 * i + 1, body(2 * i, carry))

    return lax.fori_loop(0, count // 2, twice, init)


def sigmoid(x):
    return 0.5 * jnp.tanh(0.5 * x) + 0.5


def nn(a, b):
    return jnp.dot(a, b, preferred_element_type=F32)


def nt(a, b):
    return lax.dot_general(a, b, (((1,), (1,)), ((), ())), preferred_element_type=F32)


def tn(a, b):
    return lax.dot_general(a, b, (((0,), (0,)), ((), ())), preferred_element_type=F32)


def rows_of(start, size, step=16):
    if not isinstance(start, int):
        start = pl.multiple_of(start, step)
    return pl.ds(start, size)


def block_kernel(dims, names, *all_refs):
    r = SimpleNamespace(**dict(zip(names, all_refs, strict=True)))
    nb, chan, mid, cell_count = dims
    spat = 9 * chan // nb
    temp = 3 * mid // nb
    unit = spat // 6
    quarter = chan // 4
    half = chan // 2
    h = lax.axis_index("ha")
    w = lax.axis_index("wa")
    b = lax.axis_index("batch")
    par = lax.rem(b, 2)
    bh = lax.div(b, 2)
    pos = par * (nb - 1 - bh) + (1 - par) * bh

    def at(p):
        p = lax.rem(p + 4 * nb, nb)
        upper = lax.div(p, nb // 2)
        return (1 - upper) * (2 * p) + upper * (2 * (nb - 1 - p) + 1)

    def at_group(j):
        return (lax.rem(j, 2), lax.div(j, 2))

    mine = 2 * w + h
    sibling = (1 - h, w, b)
    beside = (h, 1 - w, b)
    later_dev = (1 - h, w, lax.rem(b + h, nb))
    earlier_dev = (1 - h, w, lax.rem(b + nb - 1 + h, nb))
    tile_group = [(lax.rem(mine + d, 4), (*at_group(lax.rem(mine + d, 4)), b)) for d in (1, 2, 3)]
    across = (h, w, b + 1 - 2 * par)
    pos_b = h * 2 + par
    plane = []
    for d in (1, 2, 3):
        q = lax.rem(pos_b + d, 4)
        plane.append((q, (lax.div(q, 2), w, b - par + lax.rem(q, 2))))
    depth = nb // 2
    line = []
    for d in range(1, depth):
        q = lax.rem(bh + d, depth)
        line.append((q, (h, w, 2 * q + par)))

    def named(dev):
        return dict(ha=dev[0], wa=dev[1], batch=dev[2])

    def rc(src, dst, send, recv, dev):
        return pltpu.make_async_remote_copy(
            src_ref=src, dst_ref=dst, send_sem=send, recv_sem=recv, device_id=named(dev), device_id_type=MESH
        )

    def lc(src, dst, sem):
        return pltpu.make_async_copy(src, dst, sem)

    partners = [sibling, beside, (h, w, at(pos + 1)), (h, w, at(pos - 1)), later_dev, earlier_dev]
    partners += [dev for _, dev in tile_group + plane + line]
    barrier = pltpu.get_barrier_semaphore()
    for dev in partners:
        pl.semaphore_signal(barrier, inc=1, device_id=named(dev), device_id_type=MESH)
    pl.semaphore_wait(barrier, len(partners))

    shards = (r.first_spatial, r.first_temporal, r.second_spatial, r.second_temporal)
    whole = ((r.w1s0, r.w1s1), (r.w1t0, r.w1t1), (r.w2s0, r.w2s1), (r.w2t0, r.w2t1))
    halves = ((0, 512), (512, mid - 512))
    shared = 2 * w + h
    shared_beside = 2 * (1 - w) + h
    way = 1 - 2 * h
    onward = (h, w, at(pos + way))
    third = temp // 3

    def taken(i, core, side):
        if i % 2 == 0:
            return 3 * unit * core + unit * side, 2 * unit
        return (1 - core) * 2 * third * side + core * third, third

    def crosses(i, core, side):
        if i % 2 == 0:
            return 3 * unit * core + 2 * unit * side, unit
        return 2 * third * side, third

    def rows_in(i, c, owner, part):
        size = spat if i % 2 == 0 else temp
        return whole[i][c].at[rows_of(owner * size + part[0], part[1]), :]

    def rows_from(i, c, part):
        c0, cw = halves[c] if i % 2 == 0 else (c * half, half)
        return shards[i].at[rows_of(part[0], part[1]), c0 : c0 + cw]

    def pieces(i):
        start, size = taken(i, h, w)
        if i:
            return ((start, size),)
        return ((start, size // 2), (start + size // 2, size // 2))

    def crossing(i, work):
        if i % 2 == 0:
            work()
        else:
            pl.when(h == 0)(work)

    def own_copy(i, c):
        rows = spat if i % 2 == 0 else temp
        return lc(rows_from(i, c, (0, rows)), rows_in(i, c, b, (0, rows)), r.own_sem.at[i, c])

    def ring(i, c, k, s, owner, from_shard=False):
        part = pieces(i)[k]
        dst = rows_in(i, c, owner, part)
        src = rows_from(i, c, part) if from_shard else dst
        return rc(src, dst, r.ring_send.at[i, c], r.ring_recv.at[i, c, k, s], onward)

    def cross(i, c, owner, part):
        ref = rows_in(i, c, owner, part)
        return rc(ref, ref, r.sib_send.at[i, c], r.sib_recv.at[i, c], sibling)

    def over(i, c, s, owner, part):
        ref = rows_in(i, c, owner, part)
        return rc(ref, ref, r.over_send.at[i, c], r.over_recv.at[i, c, s], beside)

    def gather_start(i):
        for k in range(len(pieces(i))):
            for c in (0, 1):
                ring(i, c, k, 1, b, True).start()
        for c in (0, 1):
            own_copy(i, c).start()

    def gather_relay(i, s):
        owner = at(pos - way * s)

        def work():
            part = crosses(i, h, 1 - w)
            for c in (0, 1):
                over(i, c, s, owner, part).wait_recv()
                cross(i, c, owner, part).start()

        crossing(i, work)

    def gather_pump(i, s):
        owner = at(pos - way * s)
        for k in range(len(pieces(i))):
            for c in (0, 1):
                ring(i, c, k, s, owner).wait_recv()
                if isinstance(s, int):
                    if s < nb - 1:
                        ring(i, c, k, s + 1, owner).start()
                else:
                    pl.when(s < nb - 1)(lambda k=k, c=c: ring(i, c, k, s + 1, owner).start())
        for c in (0, 1):
            crossing(i, lambda c=c: over(i, c, s, owner, crosses(i, h, w)).start())
            cross(i, c, owner, taken(i, h, w)).start()
        if isinstance(s, int):
            if s > 1:
                gather_relay(i, s - 1)
        else:
            pl.when(s > 1)(lambda: gather_relay(i, s - 1))

    def span(i, c, size):
        return whole[i][c].at[0 : (nb - 1) * size, :]

    def gather_finish(i):
        gather_relay(i, nb - 1)

        def arrived(size):
            for c in (0, 1):
                ref = span(i, c, size)
                rc(ref, ref, r.sib_send.at[i, c], r.sib_recv.at[i, c], sibling).wait_recv()

        if i % 2 == 0:
            arrived(3 * unit)
        else:
            pl.when(h == 0)(lambda: arrived(third))
            pl.when(h == 1)(lambda: arrived(2 * third))
        for c in (0, 1):
            own_copy(i, c).wait()

    def gather_sent(i):
        def sent(size, sem):
            for c in (0, 1):
                ref = span(i, c, size)
                rc(ref, ref, sem.at[i, c], r.own_sem.at[i, c], sibling).wait_send()

        sent(taken(i, h, w)[1], r.ring_send)
        crossing(i, lambda: sent(crosses(i, h, w)[1], r.over_send))
        if i % 2 == 0:
            sent(3 * unit, r.sib_send)
        else:
            pl.when(h == 0)(lambda: sent(2 * third, r.sib_send))
            pl.when(h == 1)(lambda: sent(third, r.sib_send))

    def total(k, width, value, works=()):
        slot = k % 2
        wide = value.shape[1]
        cols = pl.ds(0, wide)
        works = list(works) + [None] * 2
        four, far = r.sum_b, r.sum_c
        four[slot, pos_b, :, cols] = value

        def phase(ref, me, group, send, recv, work):
            for _, dev in group:
                part = ref.at[slot, me, :, cols]
                rc(part, part, send.at[k], recv.at[k], dev).start()
            if work:
                work()
            ref = ref.at[slot, 0 : len(group), :, cols]
            every = rc(ref, ref, send.at[k], recv.at[k], sibling)
            every.wait_recv()
            return every

        first = phase(four, pos_b, plane, r.sb_send, r.sb_recv, works[0])
        far[slot, bh, :, cols] = (four[slot, 0, :, cols] + four[slot, 1, :, cols]) + (
            four[slot, 2, :, cols] + four[slot, 3, :, cols]
        )
        second = phase(far, bh, line, r.sc_send, r.sc_recv, works[1])
        result = far[slot, 0, :, cols]
        for q in range(1, depth):
            result = result + far[slot, q, :, cols]
        first.wait_send()
        second.wait_send()
        if wide == width:
            return result
        return jnp.concatenate([result[2 * n : 2 * n + 2] for n in range(width // wide)], axis=1)

    def chunk(ref, i, base=0, width=None):
        cols = slice(None) if width is None else pl.ds(0, width)
        value = ref[rows_of(base + i * CHUNK, CHUNK), cols]
        return value.astype(F32).reshape(2, CELL, value.shape[-1])

    def put(ref, i, value, base=0, width=None):
        cols = slice(None) if width is None else pl.ds(0, width)
        ref[rows_of(base + i * CHUNK, CHUNK), cols] = value.reshape(CHUNK, value.shape[-1]).astype(ref.dtype)

    def keep(i):
        inside = jnp.where(lax.rem(i, 4) == 3, 0.0, 1.0).astype(F32)
        first = lax.broadcasted_iota(jnp.int32, (2, 1, 1), 0) == 0
        return jnp.where(first, 1.0, inside)

    def packed(one, two, width):
        rows = jnp.concatenate([jnp.sum(v, axis=0, keepdims=True) for v in (one, two)], axis=0)
        wide = 384 if width == mid else 128
        parts = [rows[:, n * wide : (n + 1) * wide] for n in range(width // wide)]
        return jnp.concatenate((parts + parts[-1:])[0:4], axis=0)

    def moments(ref, width):
        def body(i, carry):
            v = chunk(ref, i)
            m = v * keep(i)
            return (carry[0] + m[0] + m[1], carry[1] + m[0] * v[0] + m[1] * v[1])

        zero = jnp.zeros((CELL, width), F32)
        return loop(CHUNKS, body, (zero, zero))

    def prepare(n, sums, width):
        tile = r.tile_mid if width == mid else r.tile_out
        n2 = n // 2
        gain = r.param[2 * n : 2 * n + 1, 0:width]
        bias = r.param[2 * n + 1 : 2 * n + 2, 0:width]
        mean = sums[0:1] / cell_count
        inv = lax.rsqrt(sums[1:2] / cell_count - mean * mean + epsilon)
        scale = inv * gain
        shift = bias - mean * scale
        for k, v in enumerate((scale, shift, inv, mean * inv)):
            tile[n2, k] = jnp.broadcast_to(v, (CELL, width))

    def tiles(n, width):
        tile = r.tile_mid if width == mid else r.tile_out
        return [tile[n // 2, k][None] for k in range(4)]

    def fill(ref_a, ref_b, value_of, width):
        pads(ref_a, ref_b, width)

        def body(i, before):
            v = value_of(i)
            put(ref_a, i, v, MAIN)
            pair = jnp.concatenate([before[None], v[0:1]], axis=0)
            put(ref_b, i, pair, MAIN - CHUNK)
            return v[1]

        loop(CHUNKS, body, jnp.zeros((CELL, width), F32))

    def activated(src, n, width):
        def value(i):
            scale, shift, _, _ = tiles(n, width)
            y = chunk(src, i) * scale + shift
            return y * sigmoid(y) * keep(i)

        return value

    def taps(ref_a, ref_b, k, size=ROWS):
        r0 = MAIN - 8 * CELL + 8 * CELL * k
        return (
            ref_b[rows_of(r0 - CHUNK, size), :],
            ref_a[rows_of(r0, size), :],
            ref_b[rows_of(r0, size), :],
        )

    def conv(ref_a, ref_b, weight, out, pump=None):
        for n, (c0, cw) in enumerate(halves):

            def body(a, _, c0=c0, cw=cw, n=n):
                x = taps(ref_a, ref_b, a)
                acc = nn(jnp.concatenate(x, axis=1), weight[n][rows_of(a * 3 * chan, 3 * chan), :])

                @pl.when(a == 0)
                def _():
                    out[:, c0 : c0 + cw] = acc

                @pl.when(a > 0)
                def _():
                    out[:, c0 : c0 + cw] += acc

                if pump is not None:
                    pump(n * 3 + a)
                return 0

            lax.fori_loop(0, 3, body, 0)

    def conv_back(ref_a, ref_b, weight, out, pump=None):
        def body(k, _):
            e = taps(ref_a, ref_b, k)
            acc = None
            for j in range(3):
                tap = 8 - 3 * k - j
                for n, (c0, cw) in enumerate(halves):
                    term = nt(e[j][:, c0 : c0 + cw], weight[n][rows_of(tap * chan, chan), :])
                    acc = term if acc is None else acc + term

            @pl.when(k == 0)
            def _():
                out[:, 0:chan] = acc

            @pl.when(k > 0)
            def _():
                out[:, 0:chan] += acc

            if pump is not None:
                pump(k)
            return 0

        lax.fori_loop(0, 3, body, 0)

    def send_frames(k):
        down, up = r.down, r.up
        count = ROWS // CELL
        for c in range(chan // 128):
            lanes = pl.ds(128 * c, 128)
            r.halo_out[0, :, lanes] = down[c, pl.ds(2 * CELL - 1, count, stride=CELL), :]
            r.halo_out[1, :, lanes] = up[c, pl.ds(0, count, stride=CELL), :]
        copies = []
        for n, dev in ((0, later_dev), (1, earlier_dev)):
            copies.append(
                rc(r.halo_out.at[n], r.halo_in.at[k, n], r.halo_send.at[k, n], r.halo_recv.at[k, n], dev)
            )
            copies[-1].start()
        return copies

    def take_frames(k, copies):
        down, up = r.down, r.up
        count = ROWS // CELL
        for copy in copies:
            copy.wait()
        at_start = jnp.logical_and(h == 0, b == 0)
        at_end = jnp.logical_and(h == 1, b == nb - 1)
        for c in range(chan // 128):
            lanes = pl.ds(128 * c, 128)
            before = r.halo_in[k, 0, :, lanes]
            after = r.halo_in[k, 1, :, lanes]
            down[c, pl.ds(CELL - 1, count, stride=CELL), :] = jnp.where(at_start, 0.0, before)
            up[c, pl.ds(CELL, count, stride=CELL), :] = jnp.where(at_end, 0.0, after)

    def by_lanes(ref, rows):
        return jnp.concatenate([ref[c, rows, :] for c in range(chan // 128)], axis=1)

    def put_lanes(ref, rows, value):
        for c in range(chan // 128):
            ref[c, rows, :] = value[:, 128 * c : 128 * c + 128]

    def shifted(i):
        before = by_lanes(r.down, rows_of(i * CHUNK, CHUNK + CELL))[CELL - 1 : CELL - 1 + CHUNK]
        after = by_lanes(r.up, rows_of(i * CHUNK, CHUNK + CELL))[1 : 1 + CHUNK]
        gate = r.gate[...][None]
        return (before.reshape(2, CELL, chan) * gate, after.reshape(2, CELL, chan))

    def both_halves(weight, start, size):
        return jnp.concatenate([part[start : start + size, :] for part in weight], axis=1)

    def temporal(k, v, weight, out, works=()):
        works = list(works) + [None] * 2
        put_lanes(r.down, pl.ds(CELL, ROWS), nn(v[...], both_halves(weight, 0, mid)))
        y2 = nn(v[...], both_halves(weight, 2 * mid, mid))
        y2 = (y2.reshape(ROWS // CELL, CELL, chan) * r.gate[...][None]).reshape(ROWS, chan)
        put_lanes(r.up, pl.ds(0, ROWS), y2)
        copies = send_frames(k)
        out[...] = nn(v[...], both_halves(weight, mid, mid))
        if works[0]:
            works[0]()
        take_frames(k, copies)

        def body(i, carry):
            before, after = shifted(i)
            value = chunk(out, i) + before + after
            put(out, i, value)
            m = value * keep(i)
            return (carry[0] + m[0] + m[1], carry[1] + m[0] * value[0] + m[1] * value[1])

        zero = jnp.zeros((CELL, chan), F32)
        return loop(CHUNKS, body, (zero, zero))

    def put_e(tap, i, e):
        for c in (0, 1):
            r.e3[c, tap, rows_of(i * CHUNK, CHUNK), :] = e[:, c * half : (c + 1) * half]

    def temporal_back(k, weight, works=()):
        works = list(works) + [None] * 2
        copies = send_frames(k)
        e3 = r.e3

        def e_tap(n):
            return jnp.concatenate([e3[0, n], e3[1, n]], axis=1)

        for c0, cw in ((0, 512), (512, mid - 512)):
            r.grad_mid[:, c0 : c0 + cw] = nt(e_tap(1), both_halves(weight, mid + c0, cw))
        if works[0]:
            works[0]()
        take_frames(k, copies)

        def body(i, _):
            before, after = shifted(i)
            put_e(0, i, after.reshape(CHUNK, chan).astype(BF16))
            put_e(2, i, before.reshape(CHUNK, chan).astype(BF16))
            return 0

        loop(CHUNKS, body, 0)
        share = share_e3(k)
        for c0, cw in ((0, 512), (512, mid - 512)):
            r.grad_mid[:, c0 : c0 + cw] += nt(e_tap(0), both_halves(weight, c0, cw)) + nt(
                e_tap(2), both_halves(weight, 2 * mid + c0, cw)
            )
        return share

    def share(k, src, dst):
        copy = rc(src, dst, r.share_send.at[k], r.share_recv.at[k], sibling)
        copy.start()
        return copy

    outs = ((r.out1s0, r.out1s1), r.out1t, (r.out2s0, r.out2s1), r.out2t)

    e_all = (r.e_all0, r.e_all1)

    def e_part(n, slot):
        return e_all[n].at[slot * ROWS : (slot + 1) * ROWS, :]

    def e_copies(k, n):
        send, near, over = r.e_send.at[k, n], r.e_recv.at[k, n, 0], r.e_recv.at[k, n, 1]
        return [
            rc(e_part(n, 0), e_part(n, 1), send, near, sibling),
            rc(e_part(n, 0), e_part(n, 2), send, over, beside),
            rc(e_part(n, 2), e_part(n, 3), send, near, sibling),
        ]

    def share_e(k):
        for n in (0, 1):
            near, over, _ = e_copies(k, n)
            over.start()
            near.start()

    def share_e_on(k, n):
        _, over, far = e_copies(k, n)
        over.wait_recv()
        far.start()

    def share_e_wait(k, n):
        both = e_all[n].at[0 : 2 * ROWS, :]
        rc(both, both, r.e_send.at[k, n], r.e_recv.at[k, n, 0], sibling).wait_recv()
        three = e_all[n].at[0 : 3 * ROWS, :]
        rc(three, three, r.e_send.at[k, n], r.e_recv.at[k, n, 0], sibling).wait_send()

    def share_x(k, xa, xq):
        main = pl.ds(MAIN, ROWS)
        for n, dev in enumerate((sibling, beside, (1 - h, 1 - w, b))):
            lanes = rows_of((2 * dev[1] + dev[0]) * quarter, quarter, 128)
            rc(xa.at[main, lanes], xq.at[n, 0, main, :], r.xq_send.at[k], r.xq_recv.at[k], dev).start()
        all_three = xq.at[:, 0, main, :]
        return rc(all_three, all_three, r.xq_send.at[k], r.xq_recv.at[k], sibling)

    def pads(ref_a, ref_b, width):
        ref_a[0:MAIN, :] = jnp.zeros((MAIN, width), BF16)
        ref_a[MAIN + ROWS : PADDED, :] = jnp.zeros((PADDED - MAIN - ROWS, width), BF16)
        ref_b[0 : MAIN - CHUNK, :] = jnp.zeros((MAIN - CHUNK, width), BF16)
        ref_b[MAIN - CHUNK + ROWS : PADDED, :] = jnp.zeros((PADDED - MAIN + CHUNK - ROWS, width), BF16)

    def spread_x(xq):
        for n in range(3):
            pads(xq.at[n, 0], xq.at[n, 1], quarter)

        def body(i, before):
            after = []
            for n in range(3):
                v = chunk(xq.at[n, 0], i, MAIN)
                put(xq.at[n, 1], i, jnp.concatenate([before[n][None], v[0:1]], axis=0), MAIN - CHUNK)
                after.append(v[1])
            return tuple(after)

        loop(CHUNKS, body, (jnp.zeros((CELL, quarter), F32),) * 3)

    def share_e3(k):
        return share(
            k - 2, r.e3.at[1 - h], r.sib_e3
        )

    def line_row(place):
        return quarter * place + 64 * jnp.where(place > shared, 1, 0)

    def grad_row(tap, side):
        split = 2 * shared + 1
        owner = jnp.where(tap == split, 2 * shared + side, tap - jnp.where(tap > split, 1, 0))
        row = line_row(lax.div(owner, 2)) + jnp.where(tap == split, quarter, 64 * side)
        return 576 * lax.rem(owner, 2) + row

    spare = whole[2]

    def gq(i, row, size):
        return rows_of((mid if i == 0 else 0) + row, size, 64)

    def inbox(i, row, size):
        return rows_of(2 * mid + (mid if i == 0 else 0) + row, size, 64)

    def transpose_x(a, xa, xb, xq, near, far, row):
        lanes = rows_of(shared * quarter, quarter, 128)
        r0 = MAIN - 8 * CELL + 8 * CELL * a
        for j, (c, start) in enumerate(((1, r0 - CHUNK), (0, r0), (1, r0))):
            rows = rows_of(start, ROWS)
            own = (xb if c else xa)[rows, lanes]
            both = jnp.concatenate([own, xq[0, c, rows, :]], axis=0)
            near[rows_of(row + j * quarter, quarter), 0 : 2 * ROWS] = both.T
            both = jnp.concatenate([xq[1, c, rows, :], xq[2, c, rows, :]], axis=0)
            far[rows_of(row + j * quarter, quarter), 0 : 2 * ROWS] = both.T

    def spatial_part(i, near, far, row, tap, n):
        rows = rows_of(row, 3 * quarter)
        acc = nn(near[rows, :], e_all[n][0 : 2 * ROWS, :])
        acc += nn(far[rows, :], e_all[n][2 * ROWS : 4 * ROWS, :])
        acc = acc.astype(BF16)
        for j in range(6):
            spare[n][gq(i, grad_row(tap + j // 2, j % 2), 64), :] = acc[64 * j : 64 * j + 64]

    def transposes(xa, xb, xq, near, far):
        def body(a, _):
            transpose_x(a, xa, xb, xq, near, far, a * 3 * quarter)
            return 0

        lax.fori_loop(0, 3, body, 0)

    def spatial_half(i, near, far, n):
        def body(a, _):
            spatial_part(i, near, far, a * 3 * quarter, 3 * a, n)
            return 0

        lax.fori_loop(0, 3, body, 0)

    def transpose_v(v, sv):
        for c in range(mid // 128):
            lanes = pl.ds(128 * c, 128)
            r.xt[128 * c : 128 * c + 128, :] = jnp.concatenate([v[:, lanes], sv[:, lanes]], axis=0).T

    def temporal_grad(i, first, count):
        taps_of = [jnp.concatenate([r.e3[h, k], r.sib_e3[k]], axis=0) for k in range(first, first + count)]
        e = jnp.concatenate(taps_of, axis=1)
        whole_tap = mid // third
        for top in range(0, whole_tap, whole_tap // 2):
            acc = nn(r.xt[top * third : (top + whole_tap // 2) * third, :], e).astype(BF16)
            for k in range(count):
                for n in range(whole_tap // 2):
                    owner, part = divmod((first + k) * whole_tap + top + n, 3)
                    row = (owner % 2) * (depth * temp) + owner // 2 * temp + part * third
                    whole[i][0][row : row + third, :] = acc[n * third : n * third + third, k * half : (k + 1) * half]

    def parts_of(i):
        return (0, 1) if i % 2 == 0 else (0,)

    line_size = 576

    def to_y(i, n, side):
        if i % 2 == 0:
            return spare[n].at[gq(i, line_size * side, line_size), :]
        return whole[i][0].at[rows_of(depth * temp * side, depth * temp), :]

    def y_box(i, n):
        if i % 2 == 0:
            return spare[n].at[inbox(i, 0, line_size), :]
        return whole[i][1].at[0 : depth * temp, :]

    def block_of(i, n, place, size):
        if i % 2 == 0:
            return spare[n].at[gq(i, line_size * par + line_row(place), size), :]
        return whole[i][0].at[rows_of(depth * temp * par + place * temp, temp), :]

    def z_box(i, n, slot, size):
        if i % 2 == 0:
            return spare[n].at[inbox(i, line_size + slot * (line_size // 3), size), :]
        return whole[i][1].at[(depth + slot) * temp : (depth + slot + 1) * temp, :]

    def sized(i, place, work):
        if i % 2:
            work(temp)
        else:
            pl.when(place != shared)(lambda: work(quarter))
            pl.when(place == shared)(lambda: work(quarter + 64))

    def t_inbox(i, n):
        return whole[i][1].at[n * temp : (n + 1) * temp, :]

    def add_into(dst, parts, step):
        rows, cols = dst.shape

        def body(n, _):
            at_rows = rows_of(n * step, step)
            value = dst[at_rows, :].astype(F32)
            for part in parts:
                value = value + part[at_rows, :].astype(F32)
            dst[at_rows, :] = value.astype(BF16)
            return 0

        lax.fori_loop(0, rows // step, body, 0)

    def y_copy(i, n):
        return rc(to_y(i, n, 1 - par), y_box(i, n), r.y_send.at[i, n], r.y_recv.at[i, n], across)

    def z_copy(i, n, d, size):
        place = lax.rem(bh + d, depth)
        dev = (h, w, 2 * place + par)
        src, dst = block_of(i, n, place, size), z_box(i, n, 3 - d, size)
        return rc(src, dst, r.z_send.at[i, n], r.z_recv.at[i, n], dev)

    def step_of(i):
        return 32 if i % 2 == 0 else 48

    def reduce_start(i, n):
        y_copy(i, n).start()

    def reduce_middle(i, n):
        y_copy(i, n).wait()
        add_into(to_y(i, n, par), [y_box(i, n)], step_of(i))
        for d in (1, 2, 3):
            sized(i, lax.rem(bh + d, depth), lambda size, d=d: z_copy(i, n, d, size).start())

    def final_part(i, n, side, core):
        place = 2 * side + core
        start = quarter * place - 64 * b + 512 * jnp.where(b > 2 * place, 1, 0)
        return outs[i][n].at[rows_of(start, quarter, 64), :]

    def extra_part(i, n):
        return outs[i][n].at[rows_of(512 * (1 - par), 64, 64), :]

    def final_copies(i, n):
        if i % 2:
            src = block_of(i, n, bh, temp)
            part = outs[i].at[h]
            return lc(src, part, r.out_sem.at[i, 0, 0]), [
                (src, part, sibling, r.cast_send.at[i, 0, 0], r.cast_recv.at[i, 0, 0])
            ]
        src = block_of(i, n, bh, quarter)
        part = final_part(i, n, w, h)
        sends = [
            (src, part, dev, r.cast_send.at[i, n, d], r.cast_recv.at[i, n, d]) for d, dev in enumerate((beside, sibling))
        ]
        return lc(src, part, r.out_sem.at[i, n, 0]), sends

    def extra_copies(i, n):
        src = spare[n].at[gq(i, line_size * par + line_row(bh) + quarter, 64), :]
        part = extra_part(i, n)
        sends = [
            (src, part, dev, r.cast_send.at[i, n, 3 + d], r.cast_recv.at[i, n, 3 + d])
            for d, dev in enumerate((beside, sibling))
        ]
        return lc(src, part, r.out_sem.at[i, n, 1]), sends

    def begin(copies):
        local, sends = copies
        for src, part, dev, one, two in sends:
            rc(src, part, one, two, dev).start()
        local.start()

    def credit(n):
        pl.semaphore_signal(r.credit.at[n], inc=1, device_id=named(beside), device_id_type=MESH)

    def credited(n):
        pl.semaphore_wait(r.credit.at[n], 1)

    def beside_copy(i):
        return rc(block_of(i, 0, bh, temp), t_inbox(i, 7), r.fin_send.at[i], r.fin_recv.at[i], beside)

    def z_span(i, n, rows):
        return to_y(i, n, 0).at[0:rows, :]

    def reduce_last(i, n):
        def add(size):
            ref = z_span(i, n, 3 * size)
            rc(ref, ref, r.z_send.at[i, n], r.z_recv.at[i, n], across).wait_recv()
            add_into(block_of(i, n, bh, size), [z_box(i, n, slot, size) for slot in range(3)], step_of(i))

        sized(i, bh, add)
        if i % 2:
            credited(i // 2)
            beside_copy(i).start()
            return
        begin(final_copies(i, n))
        pl.when(bh == shared)(lambda: begin(extra_copies(i, n)))

    def reduce_out(i):
        beside_copy(i).wait()
        add_into(block_of(i, 0, bh, temp), [t_inbox(i, 7)], 48)
        begin(final_copies(i, 0))

    def final_on(i, n):
        def move(part, d):
            rc(part, part, r.cast_send.at[i, n, d], r.cast_recv.at[i, n, d], beside).wait_recv()
            rc(part, part, r.cast_send.at[i, n, d + 2], r.cast_recv.at[i, n, d + 2], sibling).start()

        move(final_part(i, n, 1 - w, h), 0)
        pl.when(bh == shared_beside)(lambda: move(extra_part(i, n), 3))

    def reduce_wait(i, n):
        local, sends = final_copies(i, n)
        local.wait()

        def sent(rows):
            ref = z_span(i, n, rows)
            rc(ref, ref, r.z_send.at[i, n], r.z_recv.at[i, n], across).wait_send()

        if i % 2:
            sent(3 * temp)
        else:
            pl.when(bh == shared)(lambda: sent(3 * quarter))
            pl.when(bh != shared)(lambda: sent(3 * quarter + 64))
        if i % 2:
            src, part, dev, one, two = sends[0]
            rc(src, outs[i].at[1 - h], one, two, dev).wait()
            return
        for src, part, dev, one, two in sends:
            rc(src, part, one, two, dev).wait_send()

        def far(part, d):
            return rc(part, part, r.cast_send.at[i, n, d], r.cast_recv.at[i, n, d], sibling)

        far(final_part(i, n, w, 1 - h), 1).wait_recv()
        far(final_part(i, n, 1 - w, h), 2).wait_send()
        far(final_part(i, n, 1 - w, 1 - h), 2).wait_recv()
        local, sends = extra_copies(i, n)

        @pl.when(bh == shared)
        def _():
            local.wait()
            for src, part, dev, one, two in sends:
                rc(src, part, one, two, dev).wait_send()

        pl.when(bh == shared_beside)(lambda: far(extra_part(i, n), 5).wait_send())
        pl.when(bh == 2 * w + 1 - h)(lambda: far(extra_part(i, n), 4).wait_recv())
        pl.when(bh == 2 * (1 - w) + 1 - h)(lambda: far(extra_part(i, n), 5).wait_recv())

    def tile_of(ref, jh, jw):
        return ref.at[rows_of(jh * 4, 4, 4), rows_of(jw * 32, 32), :]

    def tile_own(src, dst, n):
        return lc(src.at[mine], tile_of(dst, h, w), r.tile_own.at[n])

    def tiles_start(src, dst, n):
        for j, dev in tile_group:
            rc(src.at[j], tile_of(dst, h, w), r.tile_send.at[n], r.tile_recv.at[n], dev).start()
        tile_own(src, dst, n).start()

    def tiles_wait(src, dst, n):
        three = src.at[0:3]
        rc(three, three, r.tile_send.at[n], r.tile_recv.at[n], sibling).wait()
        tile_own(src, dst, n).wait()

    xg, cg = r.x_grid, r.cot_grid
    tiles_start(r.x_tiles, xg, 0)
    gather_start(0)
    r.param[...] = total(0, mid, r.param_in[...])
    tiles_wait(r.x_tiles, xg, 0)

    def grid_chunk(ref, i):
        v = ref[lax.div(i, 4), rows_of(lax.rem(i, 4) * CHUNK, CHUNK), :]
        return v.astype(F32).reshape(2, CELL, chan)

    fill(r.xa, r.xb, lambda i: grid_chunk(xg, i), chan)

    def pump_loop(i, lo, hi):
        def body(s, _):
            gather_pump(i, s)
            return 0

        lax.fori_loop(lo, hi, body, 0)

    pump_loop(0, 1, nb - 3)
    gather_start(1)
    pump_loop(0, nb - 3, nb - 1)
    gather_start(2)
    gather_pump(0, nb - 1)
    gather_pump(1, 1)
    gather_pump(2, 1)
    gather_pump(1, 2)
    gather_finish(0)

    def first_pump(n):
        pl.when(lax.rem(n, 2) == 0)(lambda: gather_pump(1, 3 + lax.div(n, 2)))
        pl.when(n == 3)(lambda: gather_pump(2, 2))

    conv(r.xa, r.xb, whole[0], r.mid1, first_pump)
    def first_last():
        gather_pump(2, 3)
        gather_pump(1, nb - 1)

    sums = total(
        1,
        mid,
        packed(*moments(r.mid1, mid), mid),
        [lambda: gather_pump(1, nb - 2), first_last],
    )
    prepare(0, sums, mid)

    def hidden(src, n, dst):
        value = activated(src, n, mid)

        def body(i, _):
            put(dst, i, value(i))
            return 0

        loop(CHUNKS, body, 0)

    hidden(r.mid1, 0, r.v1)
    gather_pump(2, 4)
    gather_finish(1)
    stats = temporal(0, r.v1, whole[1], r.time1, [lambda: gather_pump(2, 5)])

    def sixth():
        gather_pump(2, 6)

    sums = total(2, chan, packed(*stats, chan), [lambda: gather_start(3), sixth])
    prepare(1, sums, chan)
    fill(r.aa, r.ab, activated(r.time1, 1, chan), chan)
    gather_pump(3, 1)
    gather_pump(2, nb - 1)
    gather_pump(3, 2)
    gather_finish(2)
    tiles_start(r.cot_tiles, cg, 1)

    def second_pump(n):
        pl.when(n < nb - 3)(lambda: gather_pump(3, 3 + n))

    conv(r.aa, r.ab, whole[2], r.mid2, second_pump)
    sums = total(3, mid, packed(*moments(r.mid2, mid), mid), [lambda: gather_finish(3)])
    prepare(2, sums, mid)
    hidden(r.mid2, 2, r.v2)
    stats = temporal(1, r.v2, whole[3], r.time2)
    shared_xq2 = share_x(0, r.aa, r.xq2)
    shared_xq1 = share_x(1, r.xa, r.xq1)
    for i in range(4):
        gather_sent(i)
    share_v2 = share(4, r.v2, r.sib_v)
    sums = total(4, chan, packed(*stats, chan))
    tiles_wait(r.cot_tiles, cg, 1)
    prepare(3, sums, chan)

    out_grid = r.out_grid

    def grid_put(ref, i, v):
        ref[lax.div(i, 4), rows_of(lax.rem(i, 4) * CHUNK, CHUNK), :] = v.reshape(CHUNK, chan).astype(ref.dtype)

    def slope(y, s):
        return s * (1.0 + y * (1.0 - s))

    def pre_body(i, carry):
        scale, shift, inv, offset = tiles(3, chan)
        v = chunk(r.time2, i)
        y = v * scale + shift + chunk(r.xa, i, MAIN)
        s = sigmoid(y)
        m = keep(i)
        grid_put(out_grid, i, y * s * m)
        d = grid_chunk(cg, i) * m * slope(y, s)
        put(r.grad_pre, i, d)
        t = d * (v * inv - offset)
        return (carry[0] + d[0] + d[1], carry[1] + t[0] + t[1])

    zero_out = jnp.zeros((CELL, chan), F32)
    zero_mid = jnp.zeros((CELL, mid), F32)
    out_grid[HGT] = jnp.zeros((8 * CELL, chan), BF16)
    gg = loop(CHUNKS, pre_body, (zero_out, zero_out))

    def send_tiles(src, dst, n):
        for j, dev in tile_group:
            jh, jw = at_group(j)
            rc(tile_of(src, jh, jw), dst.at[mine], r.tile_send.at[n], r.tile_recv.at[n], dev).start()
        lc(tile_of(src, h, w), dst.at[mine], r.tile_own.at[n]).start()

    def sent_tiles(src, dst, n):
        three = dst.at[0:3]
        rc(three, three, r.tile_send.at[n], r.tile_recv.at[n], sibling).wait()
        lc(tile_of(src, h, w), dst.at[mine], r.tile_own.at[n]).wait()

    send_tiles(out_grid, r.block_out, 2)

    def norm_back(n, sums, width):
        r.norm_part[0, 2 * n : 2 * n + 1, 0:width] = sums[1:2]
        r.norm_part[0, 2 * n + 1 : 2 * n + 2, 0:width] = sums[0:1]
        back = r.back
        back[0, :, 0:width] = jnp.broadcast_to(sums[0:1] / cell_count, (CELL, width))
        back[1, :, 0:width] = jnp.broadcast_to(sums[1:2] / cell_count, (CELL, width))

    def through_norm(n, src, grad, i, width):
        scale, _, inv, offset = tiles(n, width)
        xhat = chunk(src, i) * inv - offset
        bias_part = r.back[0, :, 0:width][None]
        gain_part = r.back[1, :, 0:width][None]
        return scale * (chunk(grad, i, 0, width) - bias_part - xhat * gain_part) * keep(i)

    def through_act(n, src, grad, width):
        def body(i, carry):
            scale, shift, inv, offset = tiles(n, width)
            v = chunk(src, i)
            y = v * scale + shift
            s = sigmoid(y)
            d = chunk(grad, i, 0, width) * keep(i) * slope(y, s)
            put(grad, i, d, 0, width)
            t = d * (v * inv - offset)
            return (carry[0] + d[0] + d[1], carry[1] + t[0] + t[1])

        zero = jnp.zeros((CELL, width), F32)
        return loop(CHUNKS, body, (zero, zero))

    def to_frames(n, src, grad):
        def body(i, _):
            e = through_norm(n, src, grad, i, chan).astype(BF16)
            ef = e.astype(F32)
            put_e(1, i, e.reshape(CHUNK, chan))
            put_lanes(r.down, rows_of(i * CHUNK + CELL, CHUNK, CELL), ef.reshape(CHUNK, chan))
            put_lanes(r.up, rows_of(i * CHUNK, CHUNK), (ef * r.gate[...][None]).reshape(CHUNK, chan))
            return 0

        loop(CHUNKS, body, 0)

    sums = total(5, chan, packed(*gg, chan))
    norm_back(3, sums, chan)
    to_frames(3, r.time2, r.grad_pre)
    shared_e3 = temporal_back(2, whole[3])
    credit(1)
    gg = through_act(2, r.mid2, r.grad_mid, mid)
    shared_e3.wait()
    share_v2.wait()
    def temporal_grads(i, v):
        def first():
            transpose_v(v, r.sib_v)
            temporal_grad(i, 0, 2)

        return [first, lambda: temporal_grad(i, 2, 1)]

    sums = total(6, mid, packed(*gg, mid), temporal_grads(3, r.v2))
    reduce_start(3, 0)
    norm_back(2, sums, mid)

    def fill_e(n, src):
        def value(i):
            v = through_norm(n, src, r.grad_mid, i, mid)
            for part, (c0, cw) in zip(e_all, halves):
                put(part, i, v[:, :, c0 : c0 + cw])
            return v

        fill(r.ea, r.eb, value, mid)

    fill_e(2, r.mid2)
    share_e(0)
    conv_back(r.ea, r.eb, whole[2], r.grad_mid)
    share_e_on(0, 0)
    gg = through_act(1, r.time1, r.grad_mid, chan)
    shared_xq2.wait()
    near, far = r.xt, r.xt2

    def spread_and_turn():
        spread_x(r.xq2)
        transposes(r.aa, r.ab, r.xq2, near, far)

    def first_half():
        share_e_wait(0, 0)
        spatial_half(2, near, far, 0)

    sums = total(7, chan, packed(*gg, chan), [spread_and_turn, first_half])
    share_e_on(0, 1)
    reduce_start(2, 0)
    reduce_middle(3, 0)
    share_v1 = share(5, r.v1, r.sib_v)
    norm_back(1, sums, chan)
    to_frames(1, r.time1, r.grad_mid)

    def second_half():
        share_e_wait(0, 1)
        spatial_half(2, near, far, 1)
        credit(2)
        reduce_start(2, 1)

    shared_e3 = temporal_back(3, whole[1], [second_half])
    credit(0)
    reduce_last(3, 0)
    gg = through_act(0, r.mid1, r.grad_mid, mid)
    shared_e3.wait()
    share_v1.wait()
    sums = total(8, mid, packed(*gg, mid), temporal_grads(1, r.v1))
    reduce_start(1, 0)
    norm_back(0, sums, mid)
    fill_e(0, r.mid1)
    credited(2)
    share_e(1)
    reduce_out(3)
    for n in (0, 1):
        reduce_middle(2, n)
    shared_xq1.wait()
    spread_x(r.xq1)
    sent_tiles(out_grid, r.block_out, 2)
    transposes(r.xa, r.xb, r.xq1, near, far)
    share_e_on(1, 0)
    share_e_wait(1, 0)
    spatial_half(0, near, far, 0)
    reduce_start(0, 0)
    conv_back(r.ea, r.eb, whole[0], r.grad_mid)
    share_e_on(1, 1)
    share_e_wait(1, 1)
    spatial_half(0, near, far, 1)
    reduce_start(0, 1)

    norm_copy = rc(r.norm_part.at[0], r.norm_part.at[1], r.norm_sem.at[0], r.norm_sem.at[1], beside)
    norm_copy.start()

    def last_body(i, _):
        grid_put(out_grid, i, (chunk(r.grad_mid, i, 0, chan) + chunk(r.grad_pre, i)) * keep(i))
        return 0

    loop(CHUNKS, last_body, 0)
    send_tiles(out_grid, r.grad_input, 3)
    for n in (0, 1):
        reduce_last(2, n)
    reduce_middle(1, 0)
    for n in (0, 1):
        final_on(2, n)
    reduce_middle(0, 0)
    reduce_last(1, 0)
    reduce_out(1)
    reduce_last(0, 0)
    reduce_middle(0, 1)
    final_on(0, 0)
    reduce_last(0, 1)
    norm_copy.wait()
    r.norm_grads[...] = r.norm_part[0] + r.norm_part[1]
    sent_tiles(out_grid, r.grad_input, 3)
    for n in (0, 1):
        reduce_wait(2, n)
    reduce_wait(3, 0)
    final_on(0, 1)
    reduce_wait(1, 0)
    for n in (0, 1):
        reduce_wait(0, n)


def per_device_fast(nb, *args):
    (
        inputs,
        starts,
        first_spatial,
        first_mid_gain,
        first_mid_bias,
        first_temporal,
        first_out_gain,
        first_out_bias,
        second_spatial,
        second_mid_gain,
        second_mid_bias,
        second_temporal,
        second_out_gain,
        second_out_bias,
        cotangent,
    ) = args
    micro, frames, side, _, chan = inputs.shape
    mid = first_spatial.shape[1]
    spat, temp = first_spatial.shape[0], first_temporal.shape[0]
    h, w, b = (lax.axis_index(name) for name in ("ha", "wa", "batch"))
    few = frames // 2
    offsets = jnp.arange(side)
    valid = (h * side + offsets < HGT)[:, None] & (w * side + offsets < HGT)[None, :]

    def tiles(array):
        array = array * valid.astype(BF16)[None, None, :, :, None]
        array = array.reshape(micro, 2, few, side, side, chan).transpose(0, 1, 3, 4, 2, 5)
        return array.reshape(4, side, side * few, chan)

    def untiled(array):
        array = array.reshape(micro, 2, side, side, few, chan).transpose(0, 1, 4, 2, 3, 5)
        return array.reshape(micro, frames, side, side, chan).astype(F32)

    gate = (1 - lax.dynamic_slice(starts, (w, h * few), (1, few))).astype(F32)
    gate = jnp.broadcast_to(gate.reshape(few, 1), (few, chan))
    here = jnp.where(h == 0, 1.0, 0.0)

    def placed(shard):
        row = jnp.zeros((mid,), F32)
        return lax.dynamic_update_slice(row, shard.astype(F32) * here, (b * shard.shape[0],))

    param = jnp.stack(
        [
            placed(v)
            for v in (
                first_mid_gain,
                first_mid_bias,
                first_out_gain,
                first_out_bias,
                second_mid_gain,
                second_mid_bias,
                second_out_gain,
                second_out_bias,
            )
        ]
    )
    half = chan // 2
    few_rows = ROWS // CELL

    inputs_of = dict(
        x_tiles=(tiles(inputs), pl.ANY),
        cot_tiles=(tiles(cotangent), pl.ANY),
        gate=(gate, pltpu.VMEM),
        param_in=(param, pltpu.VMEM),
        first_spatial=(first_spatial, pl.ANY),
        first_temporal=(first_temporal, pl.ANY),
        second_spatial=(second_spatial, pl.ANY),
        second_temporal=(second_temporal, pl.ANY),
    )
    outputs_of = dict(
        block_out=((4, side, side * CELL, chan), BF16, pl.ANY),
        grad_input=((4, side, side * CELL, chan), BF16, pl.ANY),
        norm_grads=((8, mid), F32, pltpu.VMEM),
        out1s0=((spat, 512), BF16, pl.ANY),
        out1s1=((spat, mid - 512), BF16, pl.ANY),
        out1t=((2, temp, half), BF16, pl.ANY),
        out2s0=((spat, 512), BF16, pl.ANY),
        out2s1=((spat, mid - 512), BF16, pl.ANY),
        out2t=((2, temp, half), BF16, pl.ANY),
    )
    dma = pltpu.SemaphoreType.DMA
    scratch_of = dict(
        w1s0=pltpu.VMEM((9 * chan, 512), BF16),
        w1s1=pltpu.VMEM((9 * chan, mid - 512), BF16),
        w1t0=pltpu.VMEM((3 * mid, half), BF16),
        w1t1=pltpu.VMEM((3 * mid, half), BF16),
        w2s0=pltpu.VMEM((9 * chan, 512), BF16),
        w2s1=pltpu.VMEM((9 * chan, mid - 512), BF16),
        w2t0=pltpu.VMEM((3 * mid, half), BF16),
        w2t1=pltpu.VMEM((3 * mid, half), BF16),
        x_grid=pltpu.VMEM((8, 8 * CELL, chan), BF16),
        cot_grid=pltpu.VMEM((8, 8 * CELL, chan), BF16),
        out_grid=pltpu.VMEM((8, 8 * CELL, chan), BF16),
        xa=pltpu.VMEM((PADDED, chan), BF16),
        xb=pltpu.VMEM((PADDED, chan), BF16),
        aa=pltpu.VMEM((PADDED, chan), BF16),
        ab=pltpu.VMEM((PADDED, chan), BF16),
        ea=pltpu.VMEM((PADDED, mid), BF16),
        eb=pltpu.VMEM((PADDED, mid), BF16),
        mid1=pltpu.VMEM((ROWS, mid), F32),
        mid2=pltpu.VMEM((ROWS, mid), F32),
        grad_mid=pltpu.VMEM((ROWS, mid), F32),
        v1=pltpu.VMEM((ROWS, mid), BF16),
        v2=pltpu.VMEM((ROWS, mid), BF16),
        time1=pltpu.VMEM((ROWS, chan), F32),
        time2=pltpu.VMEM((ROWS, chan), F32),
        grad_pre=pltpu.VMEM((ROWS, chan), F32),
        down=pltpu.VMEM((chan // 128, ROWS + CHUNK, 128), F32),
        up=pltpu.VMEM((chan // 128, ROWS + CHUNK, 128), F32),
        e3=pltpu.VMEM((2, 3, ROWS, half), BF16),
        sib_e3=pltpu.VMEM((3, ROWS, half), BF16),
        halo_out=pltpu.VMEM((2, few_rows, chan), F32),
        halo_in=pltpu.VMEM((4, 2, few_rows, chan), F32),
        param=pltpu.VMEM((8, mid), F32),
        tile_mid=pltpu.VMEM((2, 4, CELL, mid), F32),
        tile_out=pltpu.VMEM((2, 4, CELL, chan), F32),
        back=pltpu.VMEM((2, CELL, mid), F32),
        norm_part=pltpu.VMEM((2, 8, mid), F32),
        sum_b=pltpu.VMEM((2, 4, 8, mid), F32),
        sum_c=pltpu.VMEM((2, nb // 2, 8, mid), F32),
        own_sem=dma((4, 2)),
        ring_send=dma((4, 2)),
        ring_recv=dma((4, 2, 2, nb)),
        sib_send=dma((4, 2)),
        sib_recv=dma((4, 2)),
        over_send=dma((4, 2)),
        over_recv=dma((4, 2, nb)),
        norm_sem=dma((2,)),
        credit=pltpu.SemaphoreType.REGULAR((3,)),
        sb_send=dma((9,)),
        sb_recv=dma((9,)),
        sc_send=dma((9,)),
        sc_recv=dma((9,)),
        halo_send=dma((4, 2)),
        halo_recv=dma((4, 2)),
        share_send=dma((6,)),
        share_recv=dma((6,)),
        e_all0=pltpu.VMEM((4 * ROWS, 512), BF16),
        e_all1=pltpu.VMEM((4 * ROWS, mid - 512), BF16),
        xq1=pltpu.VMEM((3, 2, PADDED, chan // 4), BF16),
        xq2=pltpu.VMEM((3, 2, PADDED, chan // 4), BF16),
        xt=pltpu.VMEM((mid, 2 * ROWS), BF16),
        xt2=pltpu.VMEM((mid, 2 * ROWS), BF16),
        sib_v=pltpu.VMEM((ROWS, mid), BF16),
        e_send=dma((2, 2)),
        e_recv=dma((2, 2, 2)),
        xq_send=dma((2,)),
        xq_recv=dma((2,)),
        y_send=dma((4, 2)),
        y_recv=dma((4, 2)),
        z_send=dma((4, 2)),
        z_recv=dma((4, 2)),
        cast_send=dma((4, 2, 6)),
        cast_recv=dma((4, 2, 8)),
        out_sem=dma((4, 2, 2)),
        fin_send=dma((4,)),
        fin_recv=dma((4,)),
        tile_send=dma((4,)),
        tile_recv=dma((4,)),
        tile_own=dma((4,)),
    )
    names = (*inputs_of, *outputs_of, *scratch_of)
    cell_count = float(frames * nb * HGT * HGT)
    results = pl.pallas_call(
        functools.partial(block_kernel, (nb, chan, mid, cell_count), names),
        out_shape=[jax.ShapeDtypeStruct(shape, dtype) for shape, dtype, _ in outputs_of.values()],
        in_specs=[pl.BlockSpec(memory_space=space) for _, space in inputs_of.values()],
        out_specs=[pl.BlockSpec(memory_space=space) for _, _, space in outputs_of.values()],
        scratch_shapes=list(scratch_of.values()),
        compiler_params=pltpu.CompilerParams(
            collective_id=0, has_side_effects=True, vmem_limit_bytes=VMEM_LIMIT
        ),
    )(*(array for array, _ in inputs_of.values()))
    got = SimpleNamespace(**dict(zip(outputs_of, results)))

    def spatial(left, right):
        return jnp.concatenate([left, right], axis=1).astype(F32)

    def temporal(pair):
        return jnp.concatenate([pair[0], pair[1]], axis=1).astype(F32)

    def norm(row, like):
        size = like.shape[0]
        return lax.dynamic_slice_in_dim(got.norm_grads[row], b * size, size)

    return (
        untiled(got.block_out),
        untiled(got.grad_input),
        spatial(got.out1s0, got.out1s1),
        norm(0, first_mid_gain),
        norm(1, first_mid_bias),
        temporal(got.out1t),
        norm(2, first_out_gain),
        norm(3, first_out_bias),
        spatial(got.out2s0, got.out2s1),
        norm(4, second_mid_gain),
        norm(5, second_mid_bias),
        temporal(got.out2t),
        norm(6, second_out_gain),
        norm(7, second_out_bias),
    )


def extended(shard, sides, width):
    for axis, dim in sides:
        count, length = (lax.axis_size(axis), shard.shape[dim])
        up = [(i, (i + 1) % count) for i in range(count - 1)]
        down = [(j, i) for i, j in up]
        last = lax.slice_in_dim(shard, length - width, length, axis=dim)
        leading = lax.slice_in_dim(shard, 0, width, axis=dim)
        before = lax.ppermute(last, axis, up)
        after = lax.ppermute(leading, axis, down)
        shard = jnp.concatenate([before, shard, after], axis=dim)
    return shard


def passed_along(shard, axis, by):
    count = lax.axis_size(axis)
    pairs = [(i, i + by) for i in range(count) if 0 <= i + by < count]
    return lax.ppermute(shard, axis, pairs)


def for_sending(shard):

    def short(part):
        return part.astype(jnp.bfloat16) if part.dtype == jnp.float32 else part

    return jax.tree.map(short, shard)


def silu_slope(values):
    sigma = jax.nn.sigmoid(values)
    return sigma * (1.0 + values * (1.0 - sigma))


def spatial_forward(field_in, kernel):
    frames, tile_side = (field_in.shape[0], field_in.shape[1])
    padded = extended(field_in, (("ha", 1), ("wa", 2)), 1)
    pieces = [
        padded[:, offset // 3 : offset // 3 + tile_side, offset % 3 : offset % 3 + tile_side, :]
        for offset in range(9)
    ]
    patches = jnp.concatenate(pieces, axis=-1).reshape(frames * tile_side * tile_side, -1)
    return (patches, jnp.dot(patches, kernel, preferred_element_type=jnp.float32))


def spatial_backward(grad_out, patches, kernel):
    frames, tile_side, channels = (grad_out.shape[0], grad_out.shape[1], grad_out.shape[3])
    row_count = frames * tile_side * tile_side
    padded = extended(grad_out, (("ha", 1), ("wa", 2)), 1)
    pieces = [
        padded[
            :,
            2 - offset // 3 : 2 - offset // 3 + tile_side,
            2 - offset % 3 : 2 - offset % 3 + tile_side,
            :,
        ]
        for offset in range(9)
    ]
    stacked = jnp.concatenate(pieces, axis=-1).reshape(row_count, 9, channels)
    grad_in = jnp.einsum(
        "rkm,kcm->rc", stacked, kernel.reshape(9, -1, channels), preferred_element_type=jnp.float32
    )
    grad_kernel = jnp.einsum(
        "rk,rm->km",
        patches,
        grad_out.reshape(row_count, channels),
        preferred_element_type=jnp.float32,
    )
    return (grad_in, grad_kernel)


def temporal_forward(field_in, clip_gate, kernel):
    frames, tile_side = (field_in.shape[0], field_in.shape[1])
    gated_in = field_in * clip_gate
    earlier = passed_along(field_in[-1:], "batch", 1)
    later_frame = passed_along(gated_in[:1], "batch", -1)
    before = jnp.concatenate([earlier, field_in[:-1]], axis=0) * clip_gate
    after_tap = jnp.concatenate([gated_in[1:], later_frame], axis=0)
    joined = jnp.concatenate([before, field_in, after_tap], axis=-1).reshape(
        frames * tile_side * tile_side, -1
    )
    return (joined, jnp.dot(joined, kernel, preferred_element_type=jnp.float32))


def temporal_backward(grad_out, joined, clip_gate, kernel):
    frames, tile_side, channels = (grad_out.shape[0], grad_out.shape[1], grad_out.shape[3])
    row_count = frames * tile_side * tile_side
    gated_grad = grad_out * clip_gate
    later_frame = passed_along(gated_grad[:1], "batch", -1)
    earlier = passed_along(grad_out[-1:], "batch", 1)
    from_later = jnp.concatenate([gated_grad[1:], later_frame], axis=0)
    from_earlier = jnp.concatenate([earlier, grad_out[:-1]], axis=0) * clip_gate
    stacked = jnp.concatenate([from_later, grad_out, from_earlier], axis=-1).reshape(
        row_count, 3, channels
    )
    grad_in = jnp.einsum(
        "rkc,kmc->rm", stacked, kernel.reshape(3, -1, channels), preferred_element_type=jnp.float32
    )
    grad_kernel = jnp.einsum(
        "rk,rc->kc",
        joined,
        grad_out.reshape(row_count, channels),
        preferred_element_type=jnp.float32,
    )
    return (grad_in, grad_kernel)


def norm_forward(pre_norm, norm_gain, norm_bias, valid_rows, cell_count):
    first_sum = jnp.sum(pre_norm * valid_rows, axis=0)
    square_sum = jnp.sum(pre_norm * pre_norm * valid_rows, axis=0)
    first_sum, square_sum = lax.psum((first_sum, square_sum), ("ha", "wa", "batch"))
    mean_val = first_sum / cell_count
    inv_std = lax.rsqrt(square_sum / cell_count - mean_val * mean_val + epsilon)
    normed = (pre_norm - mean_val) * inv_std
    return (normed, inv_std, normed * norm_gain.astype(jnp.float32) + norm_bias.astype(jnp.float32))


def norm_backward(grad_norm, normed, inv_std, norm_gain, valid_rows, cell_count):
    bias_grad = jnp.sum(grad_norm, axis=0)
    gain_grad = jnp.sum(grad_norm * normed, axis=0)
    bias_grad, gain_grad = lax.psum((bias_grad, gain_grad), ("ha", "wa", "batch"))
    grad_in = (
        valid_rows
        * norm_gain.astype(jnp.float32)
        * inv_std
        * (grad_norm - bias_grad / cell_count - normed * gain_grad / cell_count)
    )
    return (grad_in, gain_grad, bias_grad)


def forward_pair(field_in, weights, clip_gate, valid_rows, cell_count):
    frames, tile_side = (field_in.shape[0], field_in.shape[1])
    patches, spatial_out = spatial_forward(field_in, weights[0])
    mid_hat, mid_scale, mid_norm = norm_forward(
        spatial_out, weights[1], weights[2], valid_rows, cell_count
    )
    hidden = (
        (jax.nn.silu(mid_norm) * valid_rows)
        .astype(jnp.bfloat16)
        .reshape(frames, tile_side, tile_side, -1)
    )
    joined, temporal_out = temporal_forward(hidden, clip_gate, weights[3])
    out_hat, out_scale, out_norm = norm_forward(
        temporal_out, weights[4], weights[5], valid_rows, cell_count
    )
    return ((patches, mid_hat, mid_scale, mid_norm, joined, out_hat, out_scale), out_norm)


def backward_pair(grad_norm, kept, weights, clip_gate, valid_rows, cell_count, tile_side):
    patches, mid_hat, mid_scale, mid_norm, joined, out_hat, out_scale = kept
    frames = clip_gate.shape[0]
    grad_time, out_gain_grad, out_bias_grad = norm_backward(
        grad_norm, out_hat, out_scale, weights[4], valid_rows, cell_count
    )
    grad_time = grad_time.astype(jnp.bfloat16).reshape(frames, tile_side, tile_side, -1)
    grad_hidden, temporal_grad = temporal_backward(grad_time, joined, clip_gate, weights[3])
    grad_mid = grad_hidden * valid_rows * silu_slope(mid_norm)
    grad_spatial, mid_gain_grad, mid_bias_grad = norm_backward(
        grad_mid, mid_hat, mid_scale, weights[1], valid_rows, cell_count
    )
    grad_spatial = grad_spatial.astype(jnp.bfloat16).reshape(frames, tile_side, tile_side, -1)
    grad_in, spatial_grad = spatial_backward(grad_spatial, patches, weights[0])
    return (
        grad_in,
        (spatial_grad, mid_gain_grad, mid_bias_grad, temporal_grad, out_gain_grad, out_bias_grad),
    )


def per_device(
    inputs,
    starts,
    first_spatial,
    first_mid_gain,
    first_mid_bias,
    first_temporal,
    first_out_gain,
    first_out_bias,
    second_spatial,
    second_mid_gain,
    second_mid_bias,
    second_temporal,
    second_out_gain,
    second_out_bias,
    cotangent,
):
    shards = (
        first_spatial,
        first_mid_gain,
        first_mid_bias,
        first_temporal,
        first_out_gain,
        first_out_bias,
        second_spatial,
        second_mid_gain,
        second_mid_bias,
        second_temporal,
        second_out_gain,
        second_out_bias,
    )
    micro_total, frames, tile_side, channels = (
        inputs.shape[0],
        inputs.shape[1],
        inputs.shape[2],
        inputs.shape[4],
    )
    row_count = frames * tile_side * tile_side
    cell_count = frames * lax.axis_size("batch") * HGT * HGT
    offsets = jnp.arange(tile_side)
    inside_h = lax.axis_index("ha") * tile_side + offsets < HGT
    inside_w = lax.axis_index("wa") * tile_side + offsets < HGT
    valid_grid = inside_h[:, None] & inside_w[None, :]
    valid_tile = valid_grid.astype(jnp.bfloat16)[None, :, :, None]
    valid_rows = jnp.broadcast_to(
        valid_grid.astype(jnp.float32)[None], (frames, tile_side, tile_side)
    ).reshape(row_count, 1)
    results = []
    input_grads = []
    kernel_total = None
    norm_total = None
    for micro_step in range(micro_total):
        gathered = (
            lax.all_gather(shards[0], "batch", axis=0, tiled=True),
            lax.all_gather(shards[1], "batch", axis=0, tiled=True),
            lax.all_gather(shards[2], "batch", axis=0, tiled=True),
            lax.all_gather(shards[3], "batch", axis=0, tiled=True),
            lax.all_gather(shards[4], "batch", axis=0, tiled=True),
            lax.all_gather(shards[5], "batch", axis=0, tiled=True),
            lax.all_gather(shards[6], "batch", axis=0, tiled=True),
            lax.all_gather(shards[7], "batch", axis=0, tiled=True),
            lax.all_gather(shards[8], "batch", axis=0, tiled=True),
            lax.all_gather(shards[9], "batch", axis=0, tiled=True),
            lax.all_gather(shards[10], "batch", axis=0, tiled=True),
            lax.all_gather(shards[11], "batch", axis=0, tiled=True),
        )
        clip_gate = (1 - starts[micro_step]).astype(jnp.bfloat16).reshape(frames, 1, 1, 1)
        x_in = inputs[micro_step] * valid_tile
        first_kept, first_norm = forward_pair(
            x_in, gathered[0:6], clip_gate, valid_rows, cell_count
        )
        first_act = (
            (jax.nn.silu(first_norm) * valid_rows)
            .astype(jnp.bfloat16)
            .reshape(frames, tile_side, tile_side, channels)
        )
        second_kept, second_norm = forward_pair(
            first_act, gathered[6:12], clip_gate, valid_rows, cell_count
        )
        pre_out = second_norm + x_in.reshape(row_count, channels).astype(jnp.float32)
        results.append(
            (jax.nn.silu(pre_out) * valid_rows).reshape(frames, tile_side, tile_side, channels)
        )
        grad_pre = (
            cotangent[micro_step].reshape(row_count, channels).astype(jnp.float32)
            * valid_rows
            * silu_slope(pre_out)
        )
        grad_act, second_grads = backward_pair(
            grad_pre, second_kept, gathered[6:12], clip_gate, valid_rows, cell_count, tile_side
        )
        grad_first = grad_act * valid_rows * silu_slope(first_norm)
        grad_conv, first_grads = backward_pair(
            grad_first, first_kept, gathered[0:6], clip_gate, valid_rows, cell_count, tile_side
        )
        input_grads.append(
            ((grad_conv + grad_pre) * valid_rows).reshape(frames, tile_side, tile_side, channels)
        )
        step_grads = first_grads + second_grads
        kernel_now = (step_grads[0], step_grads[3], step_grads[6], step_grads[9])
        norm_now = (
            step_grads[1],
            step_grads[2],
            step_grads[4],
            step_grads[5],
            step_grads[7],
            step_grads[8],
            step_grads[10],
            step_grads[11],
        )
        if micro_step == 0:
            kernel_total = kernel_now
            norm_total = norm_now
        else:
            kernel_total = jax.tree.map(jnp.add, kernel_total, kernel_now)
            norm_total = jax.tree.map(jnp.add, norm_total, norm_now)
    kernel_total = lax.psum_scatter(kernel_total, "batch", scatter_dimension=0, tiled=True)
    kernel_total = jax.tree.map(
        lambda part: part.astype(jnp.float32), lax.psum(for_sending(kernel_total), ("ha", "wa"))
    )
    shard_index = lax.axis_index("batch")
    batch_count = lax.axis_size("batch")
    norm_shards = tuple(
        (
            lax.dynamic_slice_in_dim(
                full_sum,
                shard_index * (full_sum.shape[0] // batch_count),
                full_sum.shape[0] // batch_count,
            )
            for full_sum in norm_total
        )
    )
    return (
        jnp.stack(results),
        jnp.stack(input_grads),
        kernel_total[0],
        norm_shards[0],
        norm_shards[1],
        kernel_total[1],
        norm_shards[2],
        norm_shards[3],
        kernel_total[2],
        norm_shards[4],
        norm_shards[5],
        kernel_total[3],
        norm_shards[6],
        norm_shards[7],
    )


def solution(mesh):
    in_specs = (
        P(None, "batch", "ha", "wa", None),
        P(None, "batch"),
        P("batch", None),
        P("batch"),
        P("batch"),
        P("batch", None),
        P("batch"),
        P("batch"),
        P("batch", None),
        P("batch"),
        P("batch"),
        P("batch", None),
        P("batch"),
        P("batch"),
        P(None, "batch", "ha", "wa", None),
    )
    out_specs = (
        P(None, "batch", "ha", "wa", None),
        P(None, "batch", "ha", "wa", None),
        P("batch", None),
        P("batch"),
        P("batch"),
        P("batch", None),
        P("batch"),
        P("batch"),
        P("batch", None),
        P("batch"),
        P("batch"),
        P("batch", None),
        P("batch"),
        P("batch"),
    )
    batch = mesh.shape["batch"]

    def program(*args):
        spat, temp = args[2].shape[0], args[5].shape[0]
        fits = args[0].shape == (2, 16, 4, 4, 512) and args[2].shape[1] == 1152
        if fits and batch == 8 and spat * batch == 9 * 512 and temp * batch == 3 * 1152:
            return per_device_fast(batch, *args)
        return per_device(*args)

    return jax.shard_map(
        program, mesh=mesh, in_specs=in_specs, out_specs=out_specs, check_vma=False
    )
```

```python
import functools
from types import SimpleNamespace

import jax
import jax.numpy as jnp
from jax import lax
from jax.experimental import pallas as pl
from jax.experimental.pallas import tpu as pltpu
from jax.sharding import PartitionSpec as P

HGT = 7
epsilon = 1e-05
MESH = pl.DeviceIdType.MESH
F32 = jnp.float32
BF16 = jnp.bfloat16

BASE = 10
CELL = 8
ROWS = HGT * 8 * CELL
PADDED = (BASE + HGT * 8 + BASE) * CELL
MAIN = BASE * CELL
CHUNK = 2 * CELL
CHUNKS = ROWS // CHUNK
VMEM_LIMIT = 64 * 1024 * 1024 - 1024 * 1024


def when(cond, work):
    if cond is True:
        work()
    elif cond is not False:
        pl.when(cond)(work)


def loop(count, body, init):
    def twice(i, carry):
        return body(2 * i + 1, body(2 * i, carry))

    return lax.fori_loop(0, count // 2, twice, init)


def sigmoid(x):
    return 0.5 * jnp.tanh(0.5 * x) + 0.5


def nn(a, b):
    return jnp.dot(a, b, preferred_element_type=F32)


def nt(a, b):
    return lax.dot_general(a, b, (((1,), (1,)), ((), ())), preferred_element_type=F32)


def tn(a, b):
    return lax.dot_general(a, b, (((0,), (0,)), ((), ())), preferred_element_type=F32)


def rows_of(start, size, step=16):
    if not isinstance(start, int):
        start = pl.multiple_of(start, step)
    return pl.ds(start, size)


def block_kernel(dims, names, *all_refs):
    r = SimpleNamespace(**dict(zip(names, all_refs, strict=True)))
    nb, chan, mid, cell_count = dims
    spat = 9 * chan // nb
    temp = 3 * mid // nb
    unit = spat // 6
    quarter = chan // 4
    half = chan // 2
    h = lax.axis_index("ha")
    w = lax.axis_index("wa")
    b = lax.axis_index("batch")
    par = lax.rem(b, 2)
    bh = lax.div(b, 2)
    pos = par * (nb - 1 - bh) + (1 - par) * bh

    def at(p):
        p = lax.rem(p + 4 * nb, nb)
        upper = lax.div(p, nb // 2)
        return (1 - upper) * (2 * p) + upper * (2 * (nb - 1 - p) + 1)

    def at_group(j):
        return (lax.rem(j, 2), lax.div(j, 2))

    mine = 2 * w + h
    sibling = (1 - h, w, b)
    beside = (h, 1 - w, b)
    later_dev = (1 - h, w, lax.rem(b + h, nb))
    earlier_dev = (1 - h, w, lax.rem(b + nb - 1 + h, nb))
    tile_group = [(lax.rem(mine + d, 4), (*at_group(lax.rem(mine + d, 4)), b)) for d in (1, 2, 3)]
    across = (h, w, b + 1 - 2 * par)
    pos_b = h * 2 + par
    plane = []
    for d in (1, 2, 3):
        q = lax.rem(pos_b + d, 4)
        plane.append((q, (lax.div(q, 2), w, b - par + lax.rem(q, 2))))
    depth = nb // 2
    line = []
    for d in range(1, depth):
        q = lax.rem(bh + d, depth)
        line.append((q, (h, w, 2 * q + par)))

    def named(dev):
        return dict(ha=dev[0], wa=dev[1], batch=dev[2])

    def rc(src, dst, send, recv, dev):
        return pltpu.make_async_remote_copy(
            src_ref=src, dst_ref=dst, send_sem=send, recv_sem=recv, device_id=named(dev), device_id_type=MESH
        )

    def lc(src, dst, sem):
        return pltpu.make_async_copy(src, dst, sem)

    partners = [sibling, beside, (h, w, at(pos + 1)), (h, w, at(pos - 1)), later_dev, earlier_dev]
    partners += [dev for _, dev in tile_group + plane + line]
    barrier = pltpu.get_barrier_semaphore()
    for dev in partners:
        pl.semaphore_signal(barrier, inc=1, device_id=named(dev), device_id_type=MESH)
    pl.semaphore_wait(barrier, len(partners))

    shards = (r.first_spatial, r.first_temporal, r.second_spatial, r.second_temporal)
    whole = ((r.w1s0, r.w1s1), (r.w1t0, r.w1t1), (r.w2s0, r.w2s1), (r.w2t0, r.w2t1))
    halves = ((0, 512), (512, mid - 512))
    shared = 2 * w + h
    shared_beside = 2 * (1 - w) + h
    way = 1 - 2 * h
    onward = (h, w, at(pos + way))
    third = temp // 3

    def taken(i, core, side):
        if i % 2 == 0:
            return 3 * unit * core + unit * side, 2 * unit
        return (1 - core) * 2 * third * side + core * third, third

    def crosses(i, core, side):
        if i % 2 == 0:
            return 3 * unit * core + 2 * unit * side, unit
        return 2 * third * side, third

    def rows_in(i, c, owner, part):
        size = spat if i % 2 == 0 else temp
        return whole[i][c].at[rows_of(owner * size + part[0], part[1]), :]

    def rows_from(i, c, part):
        c0, cw = halves[c] if i % 2 == 0 else (c * half, half)
        return shards[i].at[rows_of(part[0], part[1]), c0 : c0 + cw]

    def pieces(i):
        start, size = taken(i, h, w)
        return ((start, size),)

    def crossing(i, work):
        if i % 2 == 0:
            work()
        else:
            pl.when(h == 0)(work)

    def own_copy(i, c):
        rows = spat if i % 2 == 0 else temp
        return lc(rows_from(i, c, (0, rows)), rows_in(i, c, b, (0, rows)), r.own_sem.at[i, c])

    def ring(i, c, k, s, owner, from_shard=False):
        part = pieces(i)[k]
        dst = rows_in(i, c, owner, part)
        src = rows_from(i, c, part) if from_shard else dst
        return rc(src, dst, r.ring_send.at[i, c], r.ring_recv.at[i, c, k, s], onward)

    def cross(i, c, owner, part):
        ref = rows_in(i, c, owner, part)
        return rc(ref, ref, r.sib_send.at[i, c], r.sib_recv.at[i, c], sibling)

    def over(i, c, s, owner, part):
        ref = rows_in(i, c, owner, part)
        return rc(ref, ref, r.over_send.at[i, c], r.over_recv.at[i, c, s], beside)

    def gather_start(i, cols=(0, 1)):
        for k in range(len(pieces(i))):
            for c in cols:
                ring(i, c, k, 1, b, True).start()
        for c in cols:
            own_copy(i, c).start()

    def gather_relay(i, s, cols):
        owner = at(pos - way * s)

        def work():
            part = crosses(i, h, 1 - w)
            for c in cols:
                over(i, c, s, owner, part).wait_recv()
                cross(i, c, owner, part).start()

        crossing(i, work)

    def gather_pump(i, s, cols=(0, 1)):
        owner = at(pos - way * s)
        for k in range(len(pieces(i))):
            for c in cols:
                ring(i, c, k, s, owner).wait_recv()
                if isinstance(s, int):
                    if s < nb - 1:
                        ring(i, c, k, s + 1, owner).start()
                else:
                    pl.when(s < nb - 1)(lambda k=k, c=c: ring(i, c, k, s + 1, owner).start())
        for c in cols:
            crossing(i, lambda c=c: over(i, c, s, owner, crosses(i, h, w)).start())
            cross(i, c, owner, taken(i, h, w)).start()
        if isinstance(s, int):
            if s > 1:
                gather_relay(i, s - 1, cols)
        else:
            pl.when(s > 1)(lambda: gather_relay(i, s - 1, cols))

    def span(i, c, size):
        return whole[i][c].at[0 : (nb - 1) * size, :]

    def gather_finish(i, cols=(0, 1)):
        gather_relay(i, nb - 1, cols)

        def arrived(size):
            for c in cols:
                ref = span(i, c, size)
                rc(ref, ref, r.sib_send.at[i, c], r.sib_recv.at[i, c], sibling).wait_recv()

        if i % 2 == 0:
            arrived(3 * unit)
        else:
            pl.when(h == 0)(lambda: arrived(third))
            pl.when(h == 1)(lambda: arrived(2 * third))
        for c in cols:
            own_copy(i, c).wait()

    def gather_sent(i):
        def sent(size, sem):
            for c in (0, 1):
                ref = span(i, c, size)
                rc(ref, ref, sem.at[i, c], r.own_sem.at[i, c], sibling).wait_send()

        sent(taken(i, h, w)[1], r.ring_send)
        crossing(i, lambda: sent(crosses(i, h, w)[1], r.over_send))
        if i % 2 == 0:
            sent(3 * unit, r.sib_send)
        else:
            pl.when(h == 0)(lambda: sent(2 * third, r.sib_send))
            pl.when(h == 1)(lambda: sent(third, r.sib_send))

    def total(k, width, value, works=()):
        slot = k % 2
        wide = value.shape[1]
        cols = pl.ds(0, wide)
        works = list(works) + [None] * 2
        four, far = r.sum_b, r.sum_c
        four[slot, pos_b, :, cols] = value

        def phase(ref, me, group, send, recv, work):
            for _, dev in group:
                part = ref.at[slot, me, :, cols]
                rc(part, part, send.at[k], recv.at[k], dev).start()
            if work:
                work()
            ref = ref.at[slot, 0 : len(group), :, cols]
            every = rc(ref, ref, send.at[k], recv.at[k], sibling)
            every.wait_recv()
            return every

        first = phase(four, pos_b, plane, r.sb_send, r.sb_recv, works[0])
        far[slot, bh, :, cols] = (four[slot, 0, :, cols] + four[slot, 1, :, cols]) + (
            four[slot, 2, :, cols] + four[slot, 3, :, cols]
        )
        second = phase(far, bh, line, r.sc_send, r.sc_recv, works[1])
        result = far[slot, 0, :, cols]
        for q in range(1, depth):
            result = result + far[slot, q, :, cols]
        first.wait_send()
        second.wait_send()
        if wide == width:
            return result
        return jnp.concatenate([result[2 * n : 2 * n + 2] for n in range(width // wide)], axis=1)

    def chunk(ref, i, base=0, width=None):
        cols = slice(None) if width is None else pl.ds(0, width)
        value = ref[rows_of(base + i * CHUNK, CHUNK), cols]
        return value.astype(F32).reshape(2, CELL, value.shape[-1])

    def put(ref, i, value, base=0, width=None):
        cols = slice(None) if width is None else pl.ds(0, width)
        ref[rows_of(base + i * CHUNK, CHUNK), cols] = value.reshape(CHUNK, value.shape[-1]).astype(ref.dtype)

    def keep(i):
        inside = jnp.where(lax.rem(i, 4) == 3, 0.0, 1.0).astype(F32)
        first = lax.broadcasted_iota(jnp.int32, (2, 1, 1), 0) == 0
        return jnp.where(first, 1.0, inside)

    def packed(one, two, width):
        rows = jnp.concatenate([jnp.sum(v, axis=0, keepdims=True) for v in (one, two)], axis=0)
        wide = 384 if width == mid else 128
        parts = [rows[:, n * wide : (n + 1) * wide] for n in range(width // wide)]
        return jnp.concatenate((parts + parts[-1:])[0:4], axis=0)

    def moments(ref, width):
        def body(i, carry):
            v = chunk(ref, i)
            m = v * keep(i)
            return (carry[0] + m[0] + m[1], carry[1] + m[0] * v[0] + m[1] * v[1])

        zero = jnp.zeros((CELL, width), F32)
        return loop(CHUNKS, body, (zero, zero))

    def prepare(n, sums, width):
        tile = r.tile_mid if width == mid else r.tile_out
        n2 = n // 2
        gain = r.param[2 * n : 2 * n + 1, 0:width]
        bias = r.param[2 * n + 1 : 2 * n + 2, 0:width]
        mean = sums[0:1] / cell_count
        inv = lax.rsqrt(sums[1:2] / cell_count - mean * mean + epsilon)
        scale = inv * gain
        shift = bias - mean * scale
        for k, v in enumerate((scale, shift, inv, mean * inv)):
            tile[n2, k] = jnp.broadcast_to(v, (CELL, width))

    def tiles(n, width):
        tile = r.tile_mid if width == mid else r.tile_out
        return [tile[n // 2, k][None] for k in range(4)]

    def fill(ref_a, ref_b, value_of, width):
        pads(ref_a, ref_b, width)

        def body(i, before):
            v = value_of(i)
            put(ref_a, i, v, MAIN)
            pair = jnp.concatenate([before[None], v[0:1]], axis=0)
            put(ref_b, i, pair, MAIN - CHUNK)
            return v[1]

        loop(CHUNKS, body, jnp.zeros((CELL, width), F32))

    def activated(src, n, width):
        def value(i):
            scale, shift, _, _ = tiles(n, width)
            y = chunk(src, i) * scale + shift
            return y * sigmoid(y) * keep(i)

        return value

    def taps(ref_a, ref_b, k, size=ROWS):
        r0 = MAIN - 8 * CELL + 8 * CELL * k
        return (
            ref_b[rows_of(r0 - CHUNK, size), :],
            ref_a[rows_of(r0, size), :],
            ref_b[rows_of(r0, size), :],
        )

    def conv(ref_a, ref_b, weight, out, pump, between):
        for n, (c0, cw) in enumerate(halves):
            if n:
                between()

            def body(a, _, c0=c0, cw=cw, n=n):
                x = taps(ref_a, ref_b, a)
                acc = nn(jnp.concatenate(x, axis=1), weight[n][rows_of(a * 3 * chan, 3 * chan), :])

                @pl.when(a == 0)
                def _():
                    out[:, c0 : c0 + cw] = acc

                @pl.when(a > 0)
                def _():
                    out[:, c0 : c0 + cw] += acc

                if pump is not None:
                    pump(n * 3 + a)
                return 0

            lax.fori_loop(0, 3, body, 0)

    def conv_back(ref_a, ref_b, weight, out, pump=None):
        def body(k, _):
            e = taps(ref_a, ref_b, k)
            acc = None
            for j in range(3):
                tap = 8 - 3 * k - j
                for n, (c0, cw) in enumerate(halves):
                    term = nt(e[j][:, c0 : c0 + cw], weight[n][rows_of(tap * chan, chan), :])
                    acc = term if acc is None else acc + term

            @pl.when(k == 0)
            def _():
                out[:, 0:chan] = acc

            @pl.when(k > 0)
            def _():
                out[:, 0:chan] += acc

            if pump is not None:
                pump(k)
            return 0

        lax.fori_loop(0, 3, body, 0)

    def send_frames(k):
        down, up = r.down, r.up
        count = ROWS // CELL
        for c in range(chan // 128):
            lanes = pl.ds(128 * c, 128)
            r.halo_out[0, :, lanes] = down[c, pl.ds(2 * CELL - 1, count, stride=CELL), :]
            r.halo_out[1, :, lanes] = up[c, pl.ds(0, count, stride=CELL), :]
        copies = []
        for n, dev in ((0, later_dev), (1, earlier_dev)):
            copies.append(
                rc(r.halo_out.at[n], r.halo_in.at[k, n], r.halo_send.at[k, n], r.halo_recv.at[k, n], dev)
            )
            copies[-1].start()
        return copies

    def take_frames(k, copies):
        down, up = r.down, r.up
        count = ROWS // CELL
        for copy in copies:
            copy.wait()
        at_start = jnp.logical_and(h == 0, b == 0)
        at_end = jnp.logical_and(h == 1, b == nb - 1)
        for c in range(chan // 128):
            lanes = pl.ds(128 * c, 128)
            before = r.halo_in[k, 0, :, lanes]
            after = r.halo_in[k, 1, :, lanes]
            down[c, pl.ds(CELL - 1, count, stride=CELL), :] = jnp.where(at_start, 0.0, before)
            up[c, pl.ds(CELL, count, stride=CELL), :] = jnp.where(at_end, 0.0, after)

    def by_lanes(ref, rows):
        return jnp.concatenate([ref[c, rows, :] for c in range(chan // 128)], axis=1)

    def put_lanes(ref, rows, value):
        for c in range(chan // 128):
            ref[c, rows, :] = value[:, 128 * c : 128 * c + 128]

    def shifted(i):
        before = by_lanes(r.down, rows_of(i * CHUNK, CHUNK + CELL))[CELL - 1 : CELL - 1 + CHUNK]
        after = by_lanes(r.up, rows_of(i * CHUNK, CHUNK + CELL))[1 : 1 + CHUNK]
        gate = r.gate[...][None]
        return (before.reshape(2, CELL, chan) * gate, after.reshape(2, CELL, chan))

    def both_halves(weight, start, size):
        return jnp.concatenate([part[start : start + size, :] for part in weight], axis=1)

    def temporal(k, v, weight, out, works=()):
        works = list(works) + [None] * 2
        put_lanes(r.down, pl.ds(CELL, ROWS), nn(v[...], both_halves(weight, 0, mid)))
        y2 = nn(v[...], both_halves(weight, 2 * mid, mid))
        y2 = (y2.reshape(ROWS // CELL, CELL, chan) * r.gate[...][None]).reshape(ROWS, chan)
        put_lanes(r.up, pl.ds(0, ROWS), y2)
        copies = send_frames(k)
        out[...] = nn(v[...], both_halves(weight, mid, mid))
        if works[0]:
            works[0]()
        take_frames(k, copies)

        def body(i, carry):
            before, after = shifted(i)
            value = chunk(out, i) + before + after
            put(out, i, value)
            m = value * keep(i)
            return (carry[0] + m[0] + m[1], carry[1] + m[0] * value[0] + m[1] * value[1])

        zero = jnp.zeros((CELL, chan), F32)
        return loop(CHUNKS, body, (zero, zero))

    def put_e(tap, i, e):
        for c in (0, 1):
            r.e3[c, tap, rows_of(i * CHUNK, CHUNK), :] = e[:, c * half : (c + 1) * half]

    def temporal_back(k, weight, works=()):
        works = list(works) + [None] * 2
        copies = send_frames(k)
        e3 = r.e3

        def e_tap(n):
            return jnp.concatenate([e3[0, n], e3[1, n]], axis=1)

        for c0, cw in ((0, 512), (512, mid - 512)):
            r.grad_mid[:, c0 : c0 + cw] = nt(e_tap(1), both_halves(weight, mid + c0, cw))
        if works[0]:
            works[0]()
        take_frames(k, copies)

        def body(i, _):
            before, after = shifted(i)
            put_e(0, i, after.reshape(CHUNK, chan).astype(BF16))
            put_e(2, i, before.reshape(CHUNK, chan).astype(BF16))
            return 0

        loop(CHUNKS, body, 0)
        share = share_e3(k)
        for c0, cw in ((0, 512), (512, mid - 512)):
            r.grad_mid[:, c0 : c0 + cw] += nt(e_tap(0), both_halves(weight, c0, cw)) + nt(
                e_tap(2), both_halves(weight, 2 * mid + c0, cw)
            )
        return share

    def share(k, src, dst):
        copy = rc(src, dst, r.share_send.at[k], r.share_recv.at[k], sibling)
        copy.start()
        return copy

    outs = ((r.out1s0, r.out1s1), r.out1t, (r.out2s0, r.out2s1), r.out2t)

    e_all = (r.e_all0, r.e_all1)

    def e_part(n, slot):
        return e_all[n].at[slot * ROWS : (slot + 1) * ROWS, :]

    def e_copies(k, n):
        send, near, over = r.e_send.at[k, n], r.e_recv.at[k, n, 0], r.e_recv.at[k, n, 1]
        return [
            rc(e_part(n, 0), e_part(n, 1), send, near, sibling),
            rc(e_part(n, 0), e_part(n, 2), send, over, beside),
            rc(e_part(n, 2), e_part(n, 3), send, near, sibling),
        ]

    def share_e(k):
        for n in (0, 1):
            near, over, _ = e_copies(k, n)
            over.start()
            near.start()

    def share_e_on(k, n):
        _, over, far = e_copies(k, n)
        over.wait_recv()
        far.start()

    def share_e_wait(k, n):
        both = e_all[n].at[0 : 2 * ROWS, :]
        rc(both, both, r.e_send.at[k, n], r.e_recv.at[k, n, 0], sibling).wait_recv()
        three = e_all[n].at[0 : 3 * ROWS, :]
        rc(three, three, r.e_send.at[k, n], r.e_recv.at[k, n, 0], sibling).wait_send()

    def share_x(k, xa, xq):
        main = pl.ds(MAIN, ROWS)
        for n, dev in enumerate((sibling, beside, (1 - h, 1 - w, b))):
            lanes = rows_of((2 * dev[1] + dev[0]) * quarter, quarter, 128)
            rc(xa.at[main, lanes], xq.at[n, 0, main, :], r.xq_send.at[k], r.xq_recv.at[k], dev).start()
        all_three = xq.at[:, 0, main, :]
        return rc(all_three, all_three, r.xq_send.at[k], r.xq_recv.at[k], sibling)

    def pads(ref_a, ref_b, width):
        ref_a[0:MAIN, :] = jnp.zeros((MAIN, width), BF16)
        ref_a[MAIN + ROWS : PADDED, :] = jnp.zeros((PADDED - MAIN - ROWS, width), BF16)
        ref_b[0 : MAIN - CHUNK, :] = jnp.zeros((MAIN - CHUNK, width), BF16)
        ref_b[MAIN - CHUNK + ROWS : PADDED, :] = jnp.zeros((PADDED - MAIN + CHUNK - ROWS, width), BF16)

    def spread_x(xq):
        for n in range(3):
            pads(xq.at[n, 0], xq.at[n, 1], quarter)

        def body(i, before):
            after = []
            for n in range(3):
                v = chunk(xq.at[n, 0], i, MAIN)
                put(xq.at[n, 1], i, jnp.concatenate([before[n][None], v[0:1]], axis=0), MAIN - CHUNK)
                after.append(v[1])
            return tuple(after)

        loop(CHUNKS, body, (jnp.zeros((CELL, quarter), F32),) * 3)

    def share_e3(k):
        return share(
            k - 2, r.e3.at[1 - h], r.sib_e3
        )

    def line_row(place):
        return quarter * place + 64 * jnp.where(place > shared, 1, 0)

    def grad_row(tap, side):
        split = 2 * shared + 1
        owner = jnp.where(tap == split, 2 * shared + side, tap - jnp.where(tap > split, 1, 0))
        row = line_row(lax.div(owner, 2)) + jnp.where(tap == split, quarter, 64 * side)
        return 576 * lax.rem(owner, 2) + row

    spare = whole[2]

    def gq(i, row, size):
        return rows_of((mid if i == 0 else 0) + row, size, 64)

    def inbox(i, row, size):
        return rows_of(2 * mid + (mid if i == 0 else 0) + row, size, 64)

    def transpose_x(a, xa, xb, xq, near, far, row):
        lanes = rows_of(shared * quarter, quarter, 128)
        r0 = MAIN - 8 * CELL + 8 * CELL * a
        for j, (c, start) in enumerate(((1, r0 - CHUNK), (0, r0), (1, r0))):
            rows = rows_of(start, ROWS)
            own = (xb if c else xa)[rows, lanes]
            both = jnp.concatenate([own, xq[0, c, rows, :]], axis=0)
            near[rows_of(row + j * quarter, quarter), 0 : 2 * ROWS] = both.T
            both = jnp.concatenate([xq[1, c, rows, :], xq[2, c, rows, :]], axis=0)
            far[rows_of(row + j * quarter, quarter), 0 : 2 * ROWS] = both.T

    def spatial_part(i, near, far, row, tap, n):
        rows = rows_of(row, 3 * quarter)
        acc = nn(near[rows, :], e_all[n][0 : 2 * ROWS, :])
        acc += nn(far[rows, :], e_all[n][2 * ROWS : 4 * ROWS, :])
        acc = acc.astype(BF16)
        for j in range(6):
            spare[n][gq(i, grad_row(tap + j // 2, j % 2), 64), :] = acc[64 * j : 64 * j + 64]

    def transposes(xa, xb, xq, near, far):
        def body(a, _):
            transpose_x(a, xa, xb, xq, near, far, a * 3 * quarter)
            return 0

        lax.fori_loop(0, 3, body, 0)

    def spatial_half(i, near, far, n):
        def body(a, _):
            spatial_part(i, near, far, a * 3 * quarter, 3 * a, n)
            return 0

        lax.fori_loop(0, 3, body, 0)

    def transpose_v(v, sv):
        for c in range(mid // 128):
            lanes = pl.ds(128 * c, 128)
            turned = jnp.concatenate([v[:, lanes], sv[:, lanes]], axis=0).T
            for row in (0, 64):
                ref = r.ea if 128 * c + row < mid // 2 else r.eb
                at_row = (128 * c + row) % (mid // 2)
                ref[at_row : at_row + 64, 0 : 2 * ROWS] = turned[row : row + 64]

    def temporal_grad(i, first, count):
        taps_of = [jnp.concatenate([r.e3[h, k], r.sib_e3[k]], axis=0) for k in range(first, first + count)]
        e = jnp.concatenate(taps_of, axis=1)
        whole_tap = mid // third
        for top in range(0, whole_tap, whole_tap // 2):
            acc = nn((r.eb if top else r.ea)[0 : mid // 2, 0 : 2 * ROWS], e).astype(BF16)
            for k in range(count):
                for n in range(whole_tap // 2):
                    owner, part = divmod((first + k) * whole_tap + top + n, 3)
                    row = (owner % 2) * (depth * temp) + owner // 2 * temp + part * third
                    whole[i][0][row : row + third, :] = acc[n * third : n * third + third, k * half : (k + 1) * half]

    def parts_of(i):
        return (0, 1) if i % 2 == 0 else (0,)

    line_size = 576

    def to_y(i, n, side):
        if i % 2 == 0:
            return spare[n].at[gq(i, line_size * side, line_size), :]
        return whole[i][0].at[rows_of(depth * temp * side, depth * temp), :]

    def y_box(i, n):
        if i % 2 == 0:
            return spare[n].at[inbox(i, 0, line_size), :]
        return whole[i][1].at[0 : depth * temp, :]

    def block_of(i, n, place, size):
        if i % 2 == 0:
            return spare[n].at[gq(i, line_size * par + line_row(place), size), :]
        return whole[i][0].at[rows_of(depth * temp * par + place * temp, temp), :]

    def z_box(i, n, slot, size):
        if i % 2 == 0:
            return spare[n].at[inbox(i, line_size + slot * (line_size // 3), size), :]
        return whole[i][1].at[(depth + slot) * temp : (depth + slot + 1) * temp, :]

    def sized(i, place, work):
        if i % 2:
            work(temp)
        else:
            pl.when(place != shared)(lambda: work(quarter))
            pl.when(place == shared)(lambda: work(quarter + 64))

    def t_inbox(i, n):
        return whole[i][1].at[n * temp : (n + 1) * temp, :]

    def add_into(dst, parts, step):
        rows, cols = dst.shape

        def body(n, _):
            at_rows = rows_of(n * step, step)
            value = dst[at_rows, :].astype(F32)
            for part in parts:
                value = value + part[at_rows, :].astype(F32)
            dst[at_rows, :] = value.astype(BF16)
            return 0

        lax.fori_loop(0, rows // step, body, 0)

    def y_copy(i, n):
        return rc(to_y(i, n, 1 - par), y_box(i, n), r.y_send.at[i, n], r.y_recv.at[i, n], across)

    def z_copy(i, n, d, size):
        place = lax.rem(bh + d, depth)
        dev = (h, w, 2 * place + par)
        src, dst = block_of(i, n, place, size), z_box(i, n, 3 - d, size)
        return rc(src, dst, r.z_send.at[i, n], r.z_recv.at[i, n], dev)

    def step_of(i):
        return 32 if i % 2 == 0 else 48

    def reduce_start(i, n):
        y_copy(i, n).start()

    def reduce_middle(i, n):
        y_copy(i, n).wait()
        add_into(to_y(i, n, par), [y_box(i, n)], step_of(i))
        for d in (1, 2, 3):
            sized(i, lax.rem(bh + d, depth), lambda size, d=d: z_copy(i, n, d, size).start())

    def final_part(i, n, side, core):
        place = 2 * side + core
        start = quarter * place - 64 * b + 512 * jnp.where(b > 2 * place, 1, 0)
        return outs[i][n].at[rows_of(start, quarter, 64), :]

    def extra_part(i, n):
        return outs[i][n].at[rows_of(512 * (1 - par), 64, 64), :]

    def final_copies(i, n):
        if i % 2:
            src = block_of(i, n, bh, temp)
            part = outs[i].at[h]
            return lc(src, part, r.out_sem.at[i, 0, 0]), [
                (src, part, sibling, r.cast_send.at[i, 0, 0], r.cast_recv.at[i, 0, 0])
            ]
        src = block_of(i, n, bh, quarter)
        part = final_part(i, n, w, h)
        sends = [
            (src, part, dev, r.cast_send.at[i, n, d], r.cast_recv.at[i, n, d]) for d, dev in enumerate((beside, sibling))
        ]
        return lc(src, part, r.out_sem.at[i, n, 0]), sends

    def extra_copies(i, n):
        src = spare[n].at[gq(i, line_size * par + line_row(bh) + quarter, 64), :]
        part = extra_part(i, n)
        sends = [
            (src, part, dev, r.cast_send.at[i, n, 3 + d], r.cast_recv.at[i, n, 3 + d])
            for d, dev in enumerate((beside, sibling))
        ]
        return lc(src, part, r.out_sem.at[i, n, 1]), sends

    def begin(copies):
        local, sends = copies
        for src, part, dev, one, two in sends:
            rc(src, part, one, two, dev).start()
        local.start()

    def credit(n):
        pl.semaphore_signal(r.credit.at[n], inc=1, device_id=named(beside), device_id_type=MESH)

    def credited(n):
        pl.semaphore_wait(r.credit.at[n], 1)

    def beside_copy(i):
        return rc(block_of(i, 0, bh, temp), t_inbox(i, 7), r.fin_send.at[i], r.fin_recv.at[i], beside)

    def z_span(i, n, rows):
        return to_y(i, n, 0).at[0:rows, :]

    def reduce_last(i, n):
        def add(size):
            ref = z_span(i, n, 3 * size)
            rc(ref, ref, r.z_send.at[i, n], r.z_recv.at[i, n], across).wait_recv()
            add_into(block_of(i, n, bh, size), [z_box(i, n, slot, size) for slot in range(3)], step_of(i))

        sized(i, bh, add)
        if i % 2:
            credited(i // 2)
            beside_copy(i).start()
            return
        begin(final_copies(i, n))
        pl.when(bh == shared)(lambda: begin(extra_copies(i, n)))

    def reduce_out(i):
        beside_copy(i).wait()
        add_into(block_of(i, 0, bh, temp), [t_inbox(i, 7)], 48)
        begin(final_copies(i, 0))

    def final_on(i, n):
        def move(part, d):
            rc(part, part, r.cast_send.at[i, n, d], r.cast_recv.at[i, n, d], beside).wait_recv()
            rc(part, part, r.cast_send.at[i, n, d + 2], r.cast_recv.at[i, n, d + 2], sibling).start()

        move(final_part(i, n, 1 - w, h), 0)
        pl.when(bh == shared_beside)(lambda: move(extra_part(i, n), 3))

    def reduce_wait(i, n):
        local, sends = final_copies(i, n)
        local.wait()

        def sent(rows):
            ref = z_span(i, n, rows)
            rc(ref, ref, r.z_send.at[i, n], r.z_recv.at[i, n], across).wait_send()

        if i % 2:
            sent(3 * temp)
        else:
            pl.when(bh == shared)(lambda: sent(3 * quarter))
            pl.when(bh != shared)(lambda: sent(3 * quarter + 64))
        if i % 2:
            src, part, dev, one, two = sends[0]
            rc(src, outs[i].at[1 - h], one, two, dev).wait()
            return
        for src, part, dev, one, two in sends:
            rc(src, part, one, two, dev).wait_send()

        def far(part, d):
            return rc(part, part, r.cast_send.at[i, n, d], r.cast_recv.at[i, n, d], sibling)

        far(final_part(i, n, w, 1 - h), 1).wait_recv()
        far(final_part(i, n, 1 - w, h), 2).wait_send()
        far(final_part(i, n, 1 - w, 1 - h), 2).wait_recv()
        local, sends = extra_copies(i, n)

        @pl.when(bh == shared)
        def _():
            local.wait()
            for src, part, dev, one, two in sends:
                rc(src, part, one, two, dev).wait_send()

        pl.when(bh == shared_beside)(lambda: far(extra_part(i, n), 5).wait_send())
        pl.when(bh == 2 * w + 1 - h)(lambda: far(extra_part(i, n), 4).wait_recv())
        pl.when(bh == 2 * (1 - w) + 1 - h)(lambda: far(extra_part(i, n), 5).wait_recv())

    def tile_of(ref, jh, jw):
        return ref.at[rows_of(jh * 4, 4, 4), rows_of(jw * 32, 32), :]

    def tile_own(src, dst, n):
        return lc(src.at[mine], tile_of(dst, h, w), r.tile_own.at[n])

    def tiles_start(src, dst, n):
        for j, dev in tile_group:
            rc(src.at[j], tile_of(dst, h, w), r.tile_send.at[n], r.tile_recv.at[n], dev).start()
        tile_own(src, dst, n).start()

    def tiles_wait(src, dst, n):
        three = src.at[0:3]
        rc(three, three, r.tile_send.at[n], r.tile_recv.at[n], sibling).wait()
        tile_own(src, dst, n).wait()

    xg, cg = r.x_grid, r.cot_grid
    tiles_start(r.x_tiles, xg, 0)
    gather_start(0, (0,))
    r.param[...] = total(0, mid, r.param_in[...])
    tiles_wait(r.x_tiles, xg, 0)

    def grid_chunk(ref, i):
        v = ref[lax.div(i, 4), rows_of(lax.rem(i, 4) * CHUNK, CHUNK), :]
        return v.astype(F32).reshape(2, CELL, chan)

    fill(r.xa, r.xb, lambda i: grid_chunk(xg, i), chan)

    left, right = (0,), (1,)
    gather_pump(0, 1, left)
    gather_start(0, right)
    gather_pump(0, 2, left)

    def two(s, _):
        gather_pump(0, s, left)
        gather_pump(0, s - 2, right)
        return 0

    lax.fori_loop(3, nb - 2, two, 0)
    gather_start(1)
    two(nb - 2, 0)
    gather_start(2)
    two(nb - 1, 0)
    gather_pump(0, nb - 2, right)
    gather_finish(0, left)

    def first_pump(n):
        pl.when(n == 0)(lambda: gather_pump(0, nb - 1, right))
        pl.when(n > 0)(lambda: gather_pump(1, n))
        pl.when(lax.rem(n, 3) == 2)(lambda: gather_pump(2, 1 + lax.div(n, 3)))

    conv(r.xa, r.xb, whole[0], r.mid1, first_pump, lambda: gather_finish(0, right))

    def first_last():
        gather_pump(2, 3)
        gather_pump(1, nb - 1)

    sums = total(
        1,
        mid,
        packed(*moments(r.mid1, mid), mid),
        [lambda: gather_pump(1, nb - 2), first_last],
    )
    prepare(0, sums, mid)

    def hidden(src, n, dst):
        value = activated(src, n, mid)

        def body(i, _):
            put(dst, i, value(i))
            return 0

        loop(CHUNKS, body, 0)

    hidden(r.mid1, 0, r.v1)
    gather_pump(2, 4)
    gather_finish(1)
    stats = temporal(0, r.v1, whole[1], r.time1, [lambda: gather_pump(2, 5)])

    def sixth():
        gather_pump(2, 6)

    sums = total(2, chan, packed(*stats, chan), [lambda: gather_start(3), sixth])
    prepare(1, sums, chan)
    fill(r.aa, r.ab, activated(r.time1, 1, chan), chan)
    gather_pump(3, 1)
    gather_pump(2, nb - 1, left)
    gather_finish(2, left)
    tiles_start(r.cot_tiles, cg, 1)

    def second_pump(n):
        pl.when(n == 0)(lambda: gather_pump(2, nb - 1, right))
        pl.when(n > 0)(lambda: gather_pump(3, 1 + n))

    conv(r.aa, r.ab, whole[2], r.mid2, second_pump, lambda: gather_finish(2, right))

    def last_piece():
        gather_pump(3, nb - 1)
        gather_finish(3)

    sums = total(3, mid, packed(*moments(r.mid2, mid), mid), [last_piece])
    prepare(2, sums, mid)
    hidden(r.mid2, 2, r.v2)
    stats = temporal(1, r.v2, whole[3], r.time2)
    shared_xq2 = share_x(0, r.aa, r.xq2)
    shared_xq1 = share_x(1, r.xa, r.xq1)
    for i in range(4):
        gather_sent(i)
    share_v2 = share(4, r.v2, r.sib_v)
    sums = total(4, chan, packed(*stats, chan), [lambda: tiles_wait(r.cot_tiles, cg, 1)])
    prepare(3, sums, chan)

    out_grid = r.out_grid

    def grid_put(ref, i, v):
        ref[lax.div(i, 4), rows_of(lax.rem(i, 4) * CHUNK, CHUNK), :] = v.reshape(CHUNK, chan).astype(ref.dtype)

    def slope(y, s):
        return s * (1.0 + y * (1.0 - s))

    def pre_body(i, carry):
        scale, shift, inv, offset = tiles(3, chan)
        v = chunk(r.time2, i)
        y = v * scale + shift + chunk(r.xa, i, MAIN)
        s = sigmoid(y)
        m = keep(i)
        grid_put(out_grid, i, y * s * m)
        d = grid_chunk(cg, i) * m * slope(y, s)
        put(r.grad_pre, i, d)
        t = d * (v * inv - offset)
        return (carry[0] + d[0] + d[1], carry[1] + t[0] + t[1])

    zero_out = jnp.zeros((CELL, chan), F32)
    zero_mid = jnp.zeros((CELL, mid), F32)
    out_grid[HGT] = jnp.zeros((8 * CELL, chan), BF16)
    gg = loop(CHUNKS, pre_body, (zero_out, zero_out))

    def send_tiles(src, dst, n):
        for j, dev in tile_group:
            jh, jw = at_group(j)
            rc(tile_of(src, jh, jw), dst.at[mine], r.tile_send.at[n], r.tile_recv.at[n], dev).start()
        lc(tile_of(src, h, w), dst.at[mine], r.tile_own.at[n]).start()

    def sent_tiles(src, dst, n):
        three = dst.at[0:3]
        rc(three, three, r.tile_send.at[n], r.tile_recv.at[n], sibling).wait()
        lc(tile_of(src, h, w), dst.at[mine], r.tile_own.at[n]).wait()

    send_tiles(out_grid, r.block_out, 2)

    def norm_back(n, sums, width):
        r.norm_part[0, 2 * n : 2 * n + 1, 0:width] = sums[1:2]
        r.norm_part[0, 2 * n + 1 : 2 * n + 2, 0:width] = sums[0:1]
        back = r.back
        back[0, :, 0:width] = jnp.broadcast_to(sums[0:1] / cell_count, (CELL, width))
        back[1, :, 0:width] = jnp.broadcast_to(sums[1:2] / cell_count, (CELL, width))

    def through_norm(n, src, grad, i, width):
        scale, _, inv, offset = tiles(n, width)
        xhat = chunk(src, i) * inv - offset
        bias_part = r.back[0, :, 0:width][None]
        gain_part = r.back[1, :, 0:width][None]
        return scale * (chunk(grad, i, 0, width) - bias_part - xhat * gain_part) * keep(i)

    def through_act(n, src, grad, width):
        def body(i, carry):
            scale, shift, inv, offset = tiles(n, width)
            v = chunk(src, i)
            y = v * scale + shift
            s = sigmoid(y)
            d = chunk(grad, i, 0, width) * keep(i) * slope(y, s)
            put(grad, i, d, 0, width)
            t = d * (v * inv - offset)
            return (carry[0] + d[0] + d[1], carry[1] + t[0] + t[1])

        zero = jnp.zeros((CELL, width), F32)
        return loop(CHUNKS, body, (zero, zero))

    def to_frames(n, src, grad):
        def body(i, _):
            e = through_norm(n, src, grad, i, chan).astype(BF16)
            ef = e.astype(F32)
            put_e(1, i, e.reshape(CHUNK, chan))
            put_lanes(r.down, rows_of(i * CHUNK + CELL, CHUNK, CELL), ef.reshape(CHUNK, chan))
            put_lanes(r.up, rows_of(i * CHUNK, CHUNK), (ef * r.gate[...][None]).reshape(CHUNK, chan))
            return 0

        loop(CHUNKS, body, 0)

    near, far = r.xt, r.xt2

    def spread():
        shared_xq2.wait()
        spread_x(r.xq2)

    sums = total(5, chan, packed(*gg, chan), [spread, lambda: transposes(r.aa, r.ab, r.xq2, near, far)])
    norm_back(3, sums, chan)
    to_frames(3, r.time2, r.grad_pre)
    shared_e3 = temporal_back(2, whole[3])
    credit(1)
    gg = through_act(2, r.mid2, r.grad_mid, mid)
    shared_e3.wait()
    share_v2.wait()
    def temporal_grads(i, v):
        def first():
            transpose_v(v, r.sib_v)
            temporal_grad(i, 0, 2)

        return [first, lambda: temporal_grad(i, 2, 1)]

    sums = total(6, mid, packed(*gg, mid), temporal_grads(3, r.v2))
    reduce_start(3, 0)
    norm_back(2, sums, mid)

    def fill_e(n, src):
        def value(i):
            v = through_norm(n, src, r.grad_mid, i, mid)
            for part, (c0, cw) in zip(e_all, halves):
                put(part, i, v[:, :, c0 : c0 + cw])
            return v

        fill(r.ea, r.eb, value, mid)

    fill_e(2, r.mid2)
    share_e(0)
    conv_back(r.ea, r.eb, whole[2], r.grad_mid)
    gg = through_act(1, r.time1, r.grad_mid, chan)

    def first_half():
        share_e_wait(0, 0)
        spatial_half(2, near, far, 0)

    sums = total(7, chan, packed(*gg, chan), [lambda: share_e_on(0, 0), first_half])
    share_e_on(0, 1)
    reduce_start(2, 0)
    share_v1 = share(5, r.v1, r.sib_v)
    norm_back(1, sums, chan)
    to_frames(1, r.time1, r.grad_mid)

    def second_half():
        share_e_wait(0, 1)
        spatial_half(2, near, far, 1)
        credit(2)
        reduce_start(2, 1)

    shared_e3 = temporal_back(3, whole[1], [second_half])
    credit(0)
    gg = through_act(0, r.mid1, r.grad_mid, mid)
    shared_e3.wait()
    share_v1.wait()
    sums = total(8, mid, packed(*gg, mid), temporal_grads(1, r.v1))
    reduce_start(1, 0)
    norm_back(0, sums, mid)
    fill_e(0, r.mid1)
    credited(2)
    share_e(1)
    shared_xq1.wait()
    spread_x(r.xq1)
    transposes(r.xa, r.xb, r.xq1, near, far)
    reduce_middle(3, 0)
    share_e_on(1, 0)
    reduce_middle(2, 0)
    share_e_wait(1, 0)
    spatial_half(0, near, far, 0)
    reduce_start(0, 0)
    sent_tiles(out_grid, r.block_out, 2)
    conv_back(r.ea, r.eb, whole[0], r.grad_mid)
    share_e_on(1, 1)
    reduce_middle(2, 1)
    reduce_last(3, 0)
    share_e_wait(1, 1)
    spatial_half(0, near, far, 1)
    reduce_start(0, 1)

    norm_copy = rc(r.norm_part.at[0], r.norm_part.at[1], r.norm_sem.at[0], r.norm_sem.at[1], beside)
    norm_copy.start()

    def last_body(i, _):
        grid_put(out_grid, i, (chunk(r.grad_mid, i, 0, chan) + chunk(r.grad_pre, i)) * keep(i))
        return 0

    loop(CHUNKS, last_body, 0)
    send_tiles(out_grid, r.grad_input, 3)
    reduce_out(3)
    reduce_middle(1, 0)
    reduce_middle(0, 0)
    for n in (0, 1):
        reduce_last(2, n)
    reduce_last(1, 0)
    for n in (0, 1):
        final_on(2, n)
    reduce_last(0, 0)
    reduce_out(1)
    norm_copy.wait()
    r.norm_grads[...] = r.norm_part[0] + r.norm_part[1]
    reduce_middle(0, 1)
    final_on(0, 0)
    sent_tiles(out_grid, r.grad_input, 3)
    for n in (0, 1):
        reduce_wait(2, n)
    reduce_wait(3, 0)
    reduce_last(0, 1)
    reduce_wait(1, 0)
    final_on(0, 1)
    for n in (0, 1):
        reduce_wait(0, n)


def per_device_fast(nb, *args):
    (
        inputs,
        starts,
        first_spatial,
        first_mid_gain,
        first_mid_bias,
        first_temporal,
        first_out_gain,
        first_out_bias,
        second_spatial,
        second_mid_gain,
        second_mid_bias,
        second_temporal,
        second_out_gain,
        second_out_bias,
        cotangent,
    ) = args
    micro, frames, side, _, chan = inputs.shape
    mid = first_spatial.shape[1]
    spat, temp = first_spatial.shape[0], first_temporal.shape[0]
    h, w, b = (lax.axis_index(name) for name in ("ha", "wa", "batch"))
    few = frames // 2
    offsets = jnp.arange(side)
    valid = (h * side + offsets < HGT)[:, None] & (w * side + offsets < HGT)[None, :]

    def tiles(array):
        array = array * valid.astype(BF16)[None, None, :, :, None]
        array = array.reshape(micro, 2, few, side, side, chan).transpose(0, 1, 3, 4, 2, 5)
        return array.reshape(4, side, side * few, chan)

    def untiled(array):
        array = array.reshape(micro, 2, side, side, few, chan).transpose(0, 1, 4, 2, 3, 5)
        return array.reshape(micro, frames, side, side, chan).astype(F32)

    gate = (1 - lax.dynamic_slice(starts, (w, h * few), (1, few))).astype(F32)
    gate = jnp.broadcast_to(gate.reshape(few, 1), (few, chan))
    here = jnp.where(h == 0, 1.0, 0.0)

    def placed(shard):
        row = jnp.zeros((mid,), F32)
        return lax.dynamic_update_slice(row, shard.astype(F32) * here, (b * shard.shape[0],))

    param = jnp.stack(
        [
            placed(v)
            for v in (
                first_mid_gain,
                first_mid_bias,
                first_out_gain,
                first_out_bias,
                second_mid_gain,
                second_mid_bias,
                second_out_gain,
                second_out_bias,
            )
        ]
    )
    half = chan // 2
    few_rows = ROWS // CELL

    inputs_of = dict(
        x_tiles=(tiles(inputs), pl.ANY),
        cot_tiles=(tiles(cotangent), pl.ANY),
        gate=(gate, pltpu.VMEM),
        param_in=(param, pltpu.VMEM),
        first_spatial=(first_spatial, pl.ANY),
        first_temporal=(first_temporal, pl.ANY),
        second_spatial=(second_spatial, pl.ANY),
        second_temporal=(second_temporal, pl.ANY),
    )
    outputs_of = dict(
        block_out=((4, side, side * CELL, chan), BF16, pl.ANY),
        grad_input=((4, side, side * CELL, chan), BF16, pl.ANY),
        norm_grads=((8, mid), F32, pltpu.VMEM),
        out1s0=((spat, 512), BF16, pl.ANY),
        out1s1=((spat, mid - 512), BF16, pl.ANY),
        out1t=((2, temp, half), BF16, pl.ANY),
        out2s0=((spat, 512), BF16, pl.ANY),
        out2s1=((spat, mid - 512), BF16, pl.ANY),
        out2t=((2, temp, half), BF16, pl.ANY),
    )
    dma = pltpu.SemaphoreType.DMA
    scratch_of = dict(
        w1s0=pltpu.VMEM((9 * chan, 512), BF16),
        w1s1=pltpu.VMEM((9 * chan, mid - 512), BF16),
        w1t0=pltpu.VMEM((3 * mid, half), BF16),
        w1t1=pltpu.VMEM((3 * mid, half), BF16),
        w2s0=pltpu.VMEM((9 * chan, 512), BF16),
        w2s1=pltpu.VMEM((9 * chan, mid - 512), BF16),
        w2t0=pltpu.VMEM((3 * mid, half), BF16),
        w2t1=pltpu.VMEM((3 * mid, half), BF16),
        x_grid=pltpu.VMEM((8, 8 * CELL, chan), BF16),
        cot_grid=pltpu.VMEM((8, 8 * CELL, chan), BF16),
        out_grid=pltpu.VMEM((8, 8 * CELL, chan), BF16),
        xa=pltpu.VMEM((PADDED, chan), BF16),
        xb=pltpu.VMEM((PADDED, chan), BF16),
        aa=pltpu.VMEM((PADDED, chan), BF16),
        ab=pltpu.VMEM((PADDED, chan), BF16),
        ea=pltpu.VMEM((PADDED, mid), BF16),
        eb=pltpu.VMEM((PADDED, mid), BF16),
        mid1=pltpu.VMEM((ROWS, mid), F32),
        mid2=pltpu.VMEM((ROWS, mid), F32),
        grad_mid=pltpu.VMEM((ROWS, mid), F32),
        v1=pltpu.VMEM((ROWS, mid), BF16),
        v2=pltpu.VMEM((ROWS, mid), BF16),
        time1=pltpu.VMEM((ROWS, chan), F32),
        time2=pltpu.VMEM((ROWS, chan), F32),
        grad_pre=pltpu.VMEM((ROWS, chan), F32),
        down=pltpu.VMEM((chan // 128, ROWS + CHUNK, 128), F32),
        up=pltpu.VMEM((chan // 128, ROWS + CHUNK, 128), F32),
        e3=pltpu.VMEM((2, 3, ROWS, half), BF16),
        sib_e3=pltpu.VMEM((3, ROWS, half), BF16),
        halo_out=pltpu.VMEM((2, few_rows, chan), F32),
        halo_in=pltpu.VMEM((4, 2, few_rows, chan), F32),
        param=pltpu.VMEM((8, mid), F32),
        tile_mid=pltpu.VMEM((2, 4, CELL, mid), F32),
        tile_out=pltpu.VMEM((2, 4, CELL, chan), F32),
        back=pltpu.VMEM((2, CELL, mid), F32),
        norm_part=pltpu.VMEM((2, 8, mid), F32),
        sum_b=pltpu.VMEM((2, 4, 8, mid), F32),
        sum_c=pltpu.VMEM((2, nb // 2, 8, mid), F32),
        own_sem=dma((4, 2)),
        ring_send=dma((4, 2)),
        ring_recv=dma((4, 2, 2, nb)),
        sib_send=dma((4, 2)),
        sib_recv=dma((4, 2)),
        over_send=dma((4, 2)),
        over_recv=dma((4, 2, nb)),
        norm_sem=dma((2,)),
        credit=pltpu.SemaphoreType.REGULAR((3,)),
        sb_send=dma((9,)),
        sb_recv=dma((9,)),
        sc_send=dma((9,)),
        sc_recv=dma((9,)),
        halo_send=dma((4, 2)),
        halo_recv=dma((4, 2)),
        share_send=dma((6,)),
        share_recv=dma((6,)),
        e_all0=pltpu.VMEM((4 * ROWS, 512), BF16),
        e_all1=pltpu.VMEM((4 * ROWS, mid - 512), BF16),
        xq1=pltpu.VMEM((3, 2, PADDED, chan // 4), BF16),
        xq2=pltpu.VMEM((3, 2, PADDED, chan // 4), BF16),
        xt=pltpu.VMEM((mid, 2 * ROWS), BF16),
        xt2=pltpu.VMEM((mid, 2 * ROWS), BF16),
        sib_v=pltpu.VMEM((ROWS, mid), BF16),
        e_send=dma((2, 2)),
        e_recv=dma((2, 2, 2)),
        xq_send=dma((2,)),
        xq_recv=dma((2,)),
        y_send=dma((4, 2)),
        y_recv=dma((4, 2)),
        z_send=dma((4, 2)),
        z_recv=dma((4, 2)),
        cast_send=dma((4, 2, 6)),
        cast_recv=dma((4, 2, 8)),
        out_sem=dma((4, 2, 2)),
        fin_send=dma((4,)),
        fin_recv=dma((4,)),
        tile_send=dma((4,)),
        tile_recv=dma((4,)),
        tile_own=dma((4,)),
    )
    names = (*inputs_of, *outputs_of, *scratch_of)
    cell_count = float(frames * nb * HGT * HGT)
    results = pl.pallas_call(
        functools.partial(block_kernel, (nb, chan, mid, cell_count), names),
        out_shape=[jax.ShapeDtypeStruct(shape, dtype) for shape, dtype, _ in outputs_of.values()],
        in_specs=[pl.BlockSpec(memory_space=space) for _, space in inputs_of.values()],
        out_specs=[pl.BlockSpec(memory_space=space) for _, _, space in outputs_of.values()],
        scratch_shapes=list(scratch_of.values()),
        compiler_params=pltpu.CompilerParams(
            collective_id=0, has_side_effects=True, vmem_limit_bytes=VMEM_LIMIT
        ),
    )(*(array for array, _ in inputs_of.values()))
    got = SimpleNamespace(**dict(zip(outputs_of, results)))

    def spatial(left, right):
        return jnp.concatenate([left, right], axis=1).astype(F32)

    def temporal(pair):
        return jnp.concatenate([pair[0], pair[1]], axis=1).astype(F32)

    def norm(row, like):
        size = like.shape[0]
        return lax.dynamic_slice_in_dim(got.norm_grads[row], b * size, size)

    return (
        untiled(got.block_out),
        untiled(got.grad_input),
        spatial(got.out1s0, got.out1s1),
        norm(0, first_mid_gain),
        norm(1, first_mid_bias),
        temporal(got.out1t),
        norm(2, first_out_gain),
        norm(3, first_out_bias),
        spatial(got.out2s0, got.out2s1),
        norm(4, second_mid_gain),
        norm(5, second_mid_bias),
        temporal(got.out2t),
        norm(6, second_out_gain),
        norm(7, second_out_bias),
    )


def extended(shard, sides, width):
    for axis, dim in sides:
        count, length = (lax.axis_size(axis), shard.shape[dim])
        up = [(i, (i + 1) % count) for i in range(count - 1)]
        down = [(j, i) for i, j in up]
        last = lax.slice_in_dim(shard, length - width, length, axis=dim)
        leading = lax.slice_in_dim(shard, 0, width, axis=dim)
        before = lax.ppermute(last, axis, up)
        after = lax.ppermute(leading, axis, down)
        shard = jnp.concatenate([before, shard, after], axis=dim)
    return shard


def passed_along(shard, axis, by):
    count = lax.axis_size(axis)
    pairs = [(i, i + by) for i in range(count) if 0 <= i + by < count]
    return lax.ppermute(shard, axis, pairs)


def for_sending(shard):

    def short(part):
        return part.astype(jnp.bfloat16) if part.dtype == jnp.float32 else part

    return jax.tree.map(short, shard)


def silu_slope(values):
    sigma = jax.nn.sigmoid(values)
    return sigma * (1.0 + values * (1.0 - sigma))


def spatial_forward(field_in, kernel):
    frames, tile_side = (field_in.shape[0], field_in.shape[1])
    padded = extended(field_in, (("ha", 1), ("wa", 2)), 1)
    pieces = [
        padded[:, offset // 3 : offset // 3 + tile_side, offset % 3 : offset % 3 + tile_side, :]
        for offset in range(9)
    ]
    patches = jnp.concatenate(pieces, axis=-1).reshape(frames * tile_side * tile_side, -1)
    return (patches, jnp.dot(patches, kernel, preferred_element_type=jnp.float32))


def spatial_backward(grad_out, patches, kernel):
    frames, tile_side, channels = (grad_out.shape[0], grad_out.shape[1], grad_out.shape[3])
    row_count = frames * tile_side * tile_side
    padded = extended(grad_out, (("ha", 1), ("wa", 2)), 1)
    pieces = [
        padded[
            :,
            2 - offset // 3 : 2 - offset // 3 + tile_side,
            2 - offset % 3 : 2 - offset % 3 + tile_side,
            :,
        ]
        for offset in range(9)
    ]
    stacked = jnp.concatenate(pieces, axis=-1).reshape(row_count, 9, channels)
    grad_in = jnp.einsum(
        "rkm,kcm->rc", stacked, kernel.reshape(9, -1, channels), preferred_element_type=jnp.float32
    )
    grad_kernel = jnp.einsum(
        "rk,rm->km",
        patches,
        grad_out.reshape(row_count, channels),
        preferred_element_type=jnp.float32,
    )
    return (grad_in, grad_kernel)


def temporal_forward(field_in, clip_gate, kernel):
    frames, tile_side = (field_in.shape[0], field_in.shape[1])
    gated_in = field_in * clip_gate
    earlier = passed_along(field_in[-1:], "batch", 1)
    later_frame = passed_along(gated_in[:1], "batch", -1)
    before = jnp.concatenate([earlier, field_in[:-1]], axis=0) * clip_gate
    after_tap = jnp.concatenate([gated_in[1:], later_frame], axis=0)
    joined = jnp.concatenate([before, field_in, after_tap], axis=-1).reshape(
        frames * tile_side * tile_side, -1
    )
    return (joined, jnp.dot(joined, kernel, preferred_element_type=jnp.float32))


def temporal_backward(grad_out, joined, clip_gate, kernel):
    frames, tile_side, channels = (grad_out.shape[0], grad_out.shape[1], grad_out.shape[3])
    row_count = frames * tile_side * tile_side
    gated_grad = grad_out * clip_gate
    later_frame = passed_along(gated_grad[:1], "batch", -1)
    earlier = passed_along(grad_out[-1:], "batch", 1)
    from_later = jnp.concatenate([gated_grad[1:], later_frame], axis=0)
    from_earlier = jnp.concatenate([earlier, grad_out[:-1]], axis=0) * clip_gate
    stacked = jnp.concatenate([from_later, grad_out, from_earlier], axis=-1).reshape(
        row_count, 3, channels
    )
    grad_in = jnp.einsum(
        "rkc,kmc->rm", stacked, kernel.reshape(3, -1, channels), preferred_element_type=jnp.float32
    )
    grad_kernel = jnp.einsum(
        "rk,rc->kc",
        joined,
        grad_out.reshape(row_count, channels),
        preferred_element_type=jnp.float32,
    )
    return (grad_in, grad_kernel)


def norm_forward(pre_norm, norm_gain, norm_bias, valid_rows, cell_count):
    first_sum = jnp.sum(pre_norm * valid_rows, axis=0)
    square_sum = jnp.sum(pre_norm * pre_norm * valid_rows, axis=0)
    first_sum, square_sum = lax.psum((first_sum, square_sum), ("ha", "wa", "batch"))
    mean_val = first_sum / cell_count
    inv_std = lax.rsqrt(square_sum / cell_count - mean_val * mean_val + epsilon)
    normed = (pre_norm - mean_val) * inv_std
    return (normed, inv_std, normed * norm_gain.astype(jnp.float32) + norm_bias.astype(jnp.float32))


def norm_backward(grad_norm, normed, inv_std, norm_gain, valid_rows, cell_count):
    bias_grad = jnp.sum(grad_norm, axis=0)
    gain_grad = jnp.sum(grad_norm * normed, axis=0)
    bias_grad, gain_grad = lax.psum((bias_grad, gain_grad), ("ha", "wa", "batch"))
    grad_in = (
        valid_rows
        * norm_gain.astype(jnp.float32)
        * inv_std
        * (grad_norm - bias_grad / cell_count - normed * gain_grad / cell_count)
    )
    return (grad_in, gain_grad, bias_grad)


def forward_pair(field_in, weights, clip_gate, valid_rows, cell_count):
    frames, tile_side = (field_in.shape[0], field_in.shape[1])
    patches, spatial_out = spatial_forward(field_in, weights[0])
    mid_hat, mid_scale, mid_norm = norm_forward(
        spatial_out, weights[1], weights[2], valid_rows, cell_count
    )
    hidden = (
        (jax.nn.silu(mid_norm) * valid_rows)
        .astype(jnp.bfloat16)
        .reshape(frames, tile_side, tile_side, -1)
    )
    joined, temporal_out = temporal_forward(hidden, clip_gate, weights[3])
    out_hat, out_scale, out_norm = norm_forward(
        temporal_out, weights[4], weights[5], valid_rows, cell_count
    )
    return ((patches, mid_hat, mid_scale, mid_norm, joined, out_hat, out_scale), out_norm)


def backward_pair(grad_norm, kept, weights, clip_gate, valid_rows, cell_count, tile_side):
    patches, mid_hat, mid_scale, mid_norm, joined, out_hat, out_scale = kept
    frames = clip_gate.shape[0]
    grad_time, out_gain_grad, out_bias_grad = norm_backward(
        grad_norm, out_hat, out_scale, weights[4], valid_rows, cell_count
    )
    grad_time = grad_time.astype(jnp.bfloat16).reshape(frames, tile_side, tile_side, -1)
    grad_hidden, temporal_grad = temporal_backward(grad_time, joined, clip_gate, weights[3])
    grad_mid = grad_hidden * valid_rows * silu_slope(mid_norm)
    grad_spatial, mid_gain_grad, mid_bias_grad = norm_backward(
        grad_mid, mid_hat, mid_scale, weights[1], valid_rows, cell_count
    )
    grad_spatial = grad_spatial.astype(jnp.bfloat16).reshape(frames, tile_side, tile_side, -1)
    grad_in, spatial_grad = spatial_backward(grad_spatial, patches, weights[0])
    return (
        grad_in,
        (spatial_grad, mid_gain_grad, mid_bias_grad, temporal_grad, out_gain_grad, out_bias_grad),
    )


def per_device(
    inputs,
    starts,
    first_spatial,
    first_mid_gain,
    first_mid_bias,
    first_temporal,
    first_out_gain,
    first_out_bias,
    second_spatial,
    second_mid_gain,
    second_mid_bias,
    second_temporal,
    second_out_gain,
    second_out_bias,
    cotangent,
):
    shards = (
        first_spatial,
        first_mid_gain,
        first_mid_bias,
        first_temporal,
        first_out_gain,
        first_out_bias,
        second_spatial,
        second_mid_gain,
        second_mid_bias,
        second_temporal,
        second_out_gain,
        second_out_bias,
    )
    micro_total, frames, tile_side, channels = (
        inputs.shape[0],
        inputs.shape[1],
        inputs.shape[2],
        inputs.shape[4],
    )
    row_count = frames * tile_side * tile_side
    cell_count = frames * lax.axis_size("batch") * HGT * HGT
    offsets = jnp.arange(tile_side)
    inside_h = lax.axis_index("ha") * tile_side + offsets < HGT
    inside_w = lax.axis_index("wa") * tile_side + offsets < HGT
    valid_grid = inside_h[:, None] & inside_w[None, :]
    valid_tile = valid_grid.astype(jnp.bfloat16)[None, :, :, None]
    valid_rows = jnp.broadcast_to(
        valid_grid.astype(jnp.float32)[None], (frames, tile_side, tile_side)
    ).reshape(row_count, 1)
    results = []
    input_grads = []
    kernel_total = None
    norm_total = None
    for micro_step in range(micro_total):
        gathered = (
            lax.all_gather(shards[0], "batch", axis=0, tiled=True),
            lax.all_gather(shards[1], "batch", axis=0, tiled=True),
            lax.all_gather(shards[2], "batch", axis=0, tiled=True),
            lax.all_gather(shards[3], "batch", axis=0, tiled=True),
            lax.all_gather(shards[4], "batch", axis=0, tiled=True),
            lax.all_gather(shards[5], "batch", axis=0, tiled=True),
            lax.all_gather(shards[6], "batch", axis=0, tiled=True),
            lax.all_gather(shards[7], "batch", axis=0, tiled=True),
            lax.all_gather(shards[8], "batch", axis=0, tiled=True),
            lax.all_gather(shards[9], "batch", axis=0, tiled=True),
            lax.all_gather(shards[10], "batch", axis=0, tiled=True),
            lax.all_gather(shards[11], "batch", axis=0, tiled=True),
        )
        clip_gate = (1 - starts[micro_step]).astype(jnp.bfloat16).reshape(frames, 1, 1, 1)
        x_in = inputs[micro_step] * valid_tile
        first_kept, first_norm = forward_pair(
            x_in, gathered[0:6], clip_gate, valid_rows, cell_count
        )
        first_act = (
            (jax.nn.silu(first_norm) * valid_rows)
            .astype(jnp.bfloat16)
            .reshape(frames, tile_side, tile_side, channels)
        )
        second_kept, second_norm = forward_pair(
            first_act, gathered[6:12], clip_gate, valid_rows, cell_count
        )
        pre_out = second_norm + x_in.reshape(row_count, channels).astype(jnp.float32)
        results.append(
            (jax.nn.silu(pre_out) * valid_rows).reshape(frames, tile_side, tile_side, channels)
        )
        grad_pre = (
            cotangent[micro_step].reshape(row_count, channels).astype(jnp.float32)
            * valid_rows
            * silu_slope(pre_out)
        )
        grad_act, second_grads = backward_pair(
            grad_pre, second_kept, gathered[6:12], clip_gate, valid_rows, cell_count, tile_side
        )
        grad_first = grad_act * valid_rows * silu_slope(first_norm)
        grad_conv, first_grads = backward_pair(
            grad_first, first_kept, gathered[0:6], clip_gate, valid_rows, cell_count, tile_side
        )
        input_grads.append(
            ((grad_conv + grad_pre) * valid_rows).reshape(frames, tile_side, tile_side, channels)
        )
        step_grads = first_grads + second_grads
        kernel_now = (step_grads[0], step_grads[3], step_grads[6], step_grads[9])
        norm_now = (
            step_grads[1],
            step_grads[2],
            step_grads[4],
            step_grads[5],
            step_grads[7],
            step_grads[8],
            step_grads[10],
            step_grads[11],
        )
        if micro_step == 0:
            kernel_total = kernel_now
            norm_total = norm_now
        else:
            kernel_total = jax.tree.map(jnp.add, kernel_total, kernel_now)
            norm_total = jax.tree.map(jnp.add, norm_total, norm_now)
    kernel_total = lax.psum_scatter(kernel_total, "batch", scatter_dimension=0, tiled=True)
    kernel_total = jax.tree.map(
        lambda part: part.astype(jnp.float32), lax.psum(for_sending(kernel_total), ("ha", "wa"))
    )
    shard_index = lax.axis_index("batch")
    batch_count = lax.axis_size("batch")
    norm_shards = tuple(
        (
            lax.dynamic_slice_in_dim(
                full_sum,
                shard_index * (full_sum.shape[0] // batch_count),
                full_sum.shape[0] // batch_count,
            )
            for full_sum in norm_total
        )
    )
    return (
        jnp.stack(results),
        jnp.stack(input_grads),
        kernel_total[0],
        norm_shards[0],
        norm_shards[1],
        kernel_total[1],
        norm_shards[2],
        norm_shards[3],
        kernel_total[2],
        norm_shards[4],
        norm_shards[5],
        kernel_total[3],
        norm_shards[6],
        norm_shards[7],
    )


def solution(mesh):
    in_specs = (
        P(None, "batch", "ha", "wa", None),
        P(None, "batch"),
        P("batch", None),
        P("batch"),
        P("batch"),
        P("batch", None),
        P("batch"),
        P("batch"),
        P("batch", None),
        P("batch"),
        P("batch"),
        P("batch", None),
        P("batch"),
        P("batch"),
        P(None, "batch", "ha", "wa", None),
    )
    out_specs = (
        P(None, "batch", "ha", "wa", None),
        P(None, "batch", "ha", "wa", None),
        P("batch", None),
        P("batch"),
        P("batch"),
        P("batch", None),
        P("batch"),
        P("batch"),
        P("batch", None),
        P("batch"),
        P("batch"),
        P("batch", None),
        P("batch"),
        P("batch"),
    )
    batch = mesh.shape["batch"]

    def program(*args):
        spat, temp = args[2].shape[0], args[5].shape[0]
        fits = args[0].shape == (2, 16, 4, 4, 512) and args[2].shape[1] == 1152
        if fits and batch == 8 and spat * batch == 9 * 512 and temp * batch == 3 * 1152:
            return per_device_fast(batch, *args)
        return per_device(*args)

    return jax.shard_map(
        program, mesh=mesh, in_specs=in_specs, out_specs=out_specs, check_vma=False
    )
```

```python
import functools
from types import SimpleNamespace

import jax
import jax.numpy as jnp
from jax import lax
from jax.experimental import pallas as pl
from jax.experimental.pallas import tpu as pltpu
from jax.sharding import PartitionSpec as P

HGT = 7
epsilon = 1e-05
MESH = pl.DeviceIdType.MESH
F32 = jnp.float32
BF16 = jnp.bfloat16

BASE = 10
CELL = 8
ROWS = HGT * 8 * CELL
PADDED = (BASE + HGT * 8 + BASE) * CELL
MAIN = BASE * CELL
CHUNK = 2 * CELL
CHUNKS = ROWS // CHUNK
VMEM_LIMIT = 64 * 1024 * 1024 - 1024 * 1024


def when(cond, work):
    if cond is True:
        work()
    elif cond is not False:
        pl.when(cond)(work)


def loop(count, body, init):
    def twice(i, carry):
        return body(2 * i + 1, body(2 * i, carry))

    return lax.fori_loop(0, count // 2, twice, init)


def sigmoid(x):
    return 0.5 * jnp.tanh(0.5 * x) + 0.5


def nn(a, b):
    return jnp.dot(a, b, preferred_element_type=F32)


def nt(a, b):
    return lax.dot_general(a, b, (((1,), (1,)), ((), ())), preferred_element_type=F32)


def tn(a, b):
    return lax.dot_general(a, b, (((0,), (0,)), ((), ())), preferred_element_type=F32)


def rows_of(start, size, step=16):
    if not isinstance(start, int):
        start = pl.multiple_of(start, step)
    return pl.ds(start, size)


def block_kernel(dims, names, *all_refs):
    r = SimpleNamespace(**dict(zip(names, all_refs, strict=True)))
    nb, chan, mid, cell_count = dims
    spat = 9 * chan // nb
    temp = 3 * mid // nb
    unit = spat // 6
    quarter = chan // 4
    half = chan // 2
    h = lax.axis_index("ha")
    w = lax.axis_index("wa")
    b = lax.axis_index("batch")
    par = lax.rem(b, 2)
    bh = lax.div(b, 2)
    pos = par * (nb - 1 - bh) + (1 - par) * bh

    def at(p):
        p = lax.rem(p + 4 * nb, nb)
        upper = lax.div(p, nb // 2)
        return (1 - upper) * (2 * p) + upper * (2 * (nb - 1 - p) + 1)

    def at_group(j):
        return (lax.rem(j, 2), lax.div(j, 2))

    mine = 2 * w + h
    sibling = (1 - h, w, b)
    beside = (h, 1 - w, b)
    later_dev = (1 - h, w, lax.rem(b + h, nb))
    earlier_dev = (1 - h, w, lax.rem(b + nb - 1 + h, nb))
    tile_group = [(lax.rem(mine + d, 4), (*at_group(lax.rem(mine + d, 4)), b)) for d in (1, 2, 3)]
    across = (h, w, b + 1 - 2 * par)
    pos_b = h * 2 + par
    plane = []
    for d in (1, 2, 3):
        q = lax.rem(pos_b + d, 4)
        plane.append((q, (lax.div(q, 2), w, b - par + lax.rem(q, 2))))
    depth = nb // 2
    line = []
    for d in range(1, depth):
        q = lax.rem(bh + d, depth)
        line.append((q, (h, w, 2 * q + par)))

    def named(dev):
        return dict(ha=dev[0], wa=dev[1], batch=dev[2])

    def rc(src, dst, send, recv, dev):
        return pltpu.make_async_remote_copy(
            src_ref=src, dst_ref=dst, send_sem=send, recv_sem=recv, device_id=named(dev), device_id_type=MESH
        )

    def lc(src, dst, sem):
        return pltpu.make_async_copy(src, dst, sem)

    partners = [sibling, beside, (h, w, at(pos + 1)), (h, w, at(pos - 1)), later_dev, earlier_dev]
    partners += [dev for _, dev in tile_group + plane + line]
    barrier = pltpu.get_barrier_semaphore()
    for dev in partners:
        pl.semaphore_signal(barrier, inc=1, device_id=named(dev), device_id_type=MESH)
    pl.semaphore_wait(barrier, len(partners))

    shards = (r.first_spatial, r.first_temporal, r.second_spatial, r.second_temporal)
    whole = ((r.w1s0, r.w1s1), (r.w1t0, r.w1t1), (r.w2s0, r.w2s1), (r.w2t0, r.w2t1))
    halves = ((0, 512), (512, mid - 512))
    shared = 2 * w + h
    shared_beside = 2 * (1 - w) + h
    way = 1 - 2 * h
    onward = (h, w, at(pos + way))
    third = temp // 3

    def taken(i, core, side):
        if i % 2 == 0:
            return 3 * unit * core + unit * side, 2 * unit
        return (1 - core) * 2 * third * side + core * third, third

    def crosses(i, core, side):
        if i % 2 == 0:
            return 3 * unit * core + 2 * unit * side, unit
        return 2 * third * side, third

    def rows_in(i, c, owner, part):
        size = spat if i % 2 == 0 else temp
        return whole[i][c].at[rows_of(owner * size + part[0], part[1]), :]

    def rows_from(i, c, part):
        c0, cw = halves[c] if i % 2 == 0 else (c * half, half)
        return shards[i].at[rows_of(part[0], part[1]), c0 : c0 + cw]

    def pieces(i):
        start, size = taken(i, h, w)
        if i:
            return ((start, size),)
        return ((start, size // 2), (start + size // 2, size // 2))

    def crossing(i, work):
        if i % 2 == 0:
            work()
        else:
            pl.when(h == 0)(work)

    def own_copy(i, c):
        rows = spat if i % 2 == 0 else temp
        return lc(rows_from(i, c, (0, rows)), rows_in(i, c, b, (0, rows)), r.own_sem.at[i, c])

    def ring(i, c, k, s, owner, from_shard=False):
        part = pieces(i)[k]
        dst = rows_in(i, c, owner, part)
        src = rows_from(i, c, part) if from_shard else dst
        return rc(src, dst, r.ring_send.at[i, c], r.ring_recv.at[i, c, k, s], onward)

    def cross(i, c, owner, part):
        ref = rows_in(i, c, owner, part)
        return rc(ref, ref, r.sib_send.at[i, c], r.sib_recv.at[i, c], sibling)

    def over(i, c, s, owner, part):
        ref = rows_in(i, c, owner, part)
        return rc(ref, ref, r.over_send.at[i, c], r.over_recv.at[i, c, s], beside)

    def gather_start(i):
        for k in range(len(pieces(i))):
            for c in (0, 1):
                ring(i, c, k, 1, b, True).start()
        for c in (0, 1):
            own_copy(i, c).start()

    def gather_relay(i, s):
        owner = at(pos - way * s)

        def work():
            part = crosses(i, h, 1 - w)
            for c in (0, 1):
                over(i, c, s, owner, part).wait_recv()
                cross(i, c, owner, part).start()

        crossing(i, work)

    def gather_pump(i, s):
        owner = at(pos - way * s)
        for k in range(len(pieces(i))):
            for c in (0, 1):
                ring(i, c, k, s, owner).wait_recv()
                if isinstance(s, int):
                    if s < nb - 1:
                        ring(i, c, k, s + 1, owner).start()
                else:
                    pl.when(s < nb - 1)(lambda k=k, c=c: ring(i, c, k, s + 1, owner).start())
        for c in (0, 1):
            crossing(i, lambda c=c: over(i, c, s, owner, crosses(i, h, w)).start())
            cross(i, c, owner, taken(i, h, w)).start()
        if isinstance(s, int):
            if s > 1:
                gather_relay(i, s - 1)
        else:
            pl.when(s > 1)(lambda: gather_relay(i, s - 1))

    def span(i, c, size):
        return whole[i][c].at[0 : (nb - 1) * size, :]

    def gather_finish(i):
        gather_relay(i, nb - 1)

        def arrived(size):
            for c in (0, 1):
                ref = span(i, c, size)
                rc(ref, ref, r.sib_send.at[i, c], r.sib_recv.at[i, c], sibling).wait_recv()

        if i % 2 == 0:
            arrived(3 * unit)
        else:
            pl.when(h == 0)(lambda: arrived(third))
            pl.when(h == 1)(lambda: arrived(2 * third))
        for c in (0, 1):
            own_copy(i, c).wait()

    def gather_sent(i):
        def sent(size, sem):
            for c in (0, 1):
                ref = span(i, c, size)
                rc(ref, ref, sem.at[i, c], r.own_sem.at[i, c], sibling).wait_send()

        sent(taken(i, h, w)[1], r.ring_send)
        crossing(i, lambda: sent(crosses(i, h, w)[1], r.over_send))
        if i % 2 == 0:
            sent(3 * unit, r.sib_send)
        else:
            pl.when(h == 0)(lambda: sent(2 * third, r.sib_send))
            pl.when(h == 1)(lambda: sent(third, r.sib_send))

    def total(k, width, value, works=()):
        slot = k % 2
        wide = value.shape[1]
        cols = pl.ds(0, wide)
        works = list(works) + [None] * 2
        four, far = r.sum_b, r.sum_c
        four[slot, pos_b, :, cols] = value

        def phase(ref, me, group, send, recv, work):
            for _, dev in group:
                part = ref.at[slot, me, :, cols]
                rc(part, part, send.at[k], recv.at[k], dev).start()
            if work:
                work()
            ref = ref.at[slot, 0 : len(group), :, cols]
            every = rc(ref, ref, send.at[k], recv.at[k], sibling)
            every.wait_recv()
            return every

        first = phase(four, pos_b, plane, r.sb_send, r.sb_recv, works[0])
        far[slot, bh, :, cols] = (four[slot, 0, :, cols] + four[slot, 1, :, cols]) + (
            four[slot, 2, :, cols] + four[slot, 3, :, cols]
        )
        second = phase(far, bh, line, r.sc_send, r.sc_recv, works[1])
        result = far[slot, 0, :, cols]
        for q in range(1, depth):
            result = result + far[slot, q, :, cols]
        first.wait_send()
        second.wait_send()
        if wide == width:
            return result
        return jnp.concatenate([result[2 * n : 2 * n + 2] for n in range(width // wide)], axis=1)

    def chunk(ref, i, base=0, width=None):
        cols = slice(None) if width is None else pl.ds(0, width)
        value = ref[rows_of(base + i * CHUNK, CHUNK), cols]
        return value.astype(F32).reshape(2, CELL, value.shape[-1])

    def put(ref, i, value, base=0, width=None):
        cols = slice(None) if width is None else pl.ds(0, width)
        ref[rows_of(base + i * CHUNK, CHUNK), cols] = value.reshape(CHUNK, value.shape[-1]).astype(ref.dtype)

    def keep(i):
        inside = jnp.where(lax.rem(i, 4) == 3, 0.0, 1.0).astype(F32)
        first = lax.broadcasted_iota(jnp.int32, (2, 1, 1), 0) == 0
        return jnp.where(first, 1.0, inside)

    def packed(one, two, width):
        rows = jnp.concatenate([jnp.sum(v, axis=0, keepdims=True) for v in (one, two)], axis=0)
        wide = 384 if width == mid else 128
        parts = [rows[:, n * wide : (n + 1) * wide] for n in range(width // wide)]
        return jnp.concatenate((parts + parts[-1:])[0:4], axis=0)

    def moments(ref, width):
        def body(i, carry):
            v = chunk(ref, i)
            m = v * keep(i)
            return (carry[0] + m[0] + m[1], carry[1] + m[0] * v[0] + m[1] * v[1])

        zero = jnp.zeros((CELL, width), F32)
        return loop(CHUNKS, body, (zero, zero))

    def prepare(n, sums, width):
        tile = r.tile_mid if width == mid else r.tile_out
        n2 = n // 2
        gain = r.param[2 * n : 2 * n + 1, 0:width]
        bias = r.param[2 * n + 1 : 2 * n + 2, 0:width]
        mean = sums[0:1] / cell_count
        inv = lax.rsqrt(sums[1:2] / cell_count - mean * mean + epsilon)
        scale = inv * gain
        shift = bias - mean * scale
        for k, v in enumerate((scale, shift, inv, mean * inv)):
            tile[n2, k] = jnp.broadcast_to(v, (CELL, width))

    def tiles(n, width):
        tile = r.tile_mid if width == mid else r.tile_out
        return [tile[n // 2, k][None] for k in range(4)]

    def fill(ref_a, ref_b, value_of, width):
        pads(ref_a, ref_b, width)

        def body(i, before):
            v = value_of(i)
            put(ref_a, i, v, MAIN)
            pair = jnp.concatenate([before[None], v[0:1]], axis=0)
            put(ref_b, i, pair, MAIN - CHUNK)
            return v[1]

        loop(CHUNKS, body, jnp.zeros((CELL, width), F32))

    def activated(src, n, width):
        def value(i):
            scale, shift, _, _ = tiles(n, width)
            y = chunk(src, i) * scale + shift
            return y * sigmoid(y) * keep(i)

        return value

    def taps(ref_a, ref_b, k, size=ROWS):
        r0 = MAIN - 8 * CELL + 8 * CELL * k
        return (
            ref_b[rows_of(r0 - CHUNK, size), :],
            ref_a[rows_of(r0, size), :],
            ref_b[rows_of(r0, size), :],
        )

    def conv(ref_a, ref_b, weight, out, pump=None):
        for n, (c0, cw) in enumerate(halves):

            def body(a, _, c0=c0, cw=cw, n=n):
                x = taps(ref_a, ref_b, a)
                acc = nn(jnp.concatenate(x, axis=1), weight[n][rows_of(a * 3 * chan, 3 * chan), :])

                @pl.when(a == 0)
                def _():
                    out[:, c0 : c0 + cw] = acc

                @pl.when(a > 0)
                def _():
                    out[:, c0 : c0 + cw] += acc

                if pump is not None:
                    pump(n * 3 + a)
                return 0

            lax.fori_loop(0, 3, body, 0)

    def conv_back(ref_a, ref_b, weight, out, pump=None):
        def body(k, _):
            e = taps(ref_a, ref_b, k)
            acc = None
            for j in range(3):
                tap = 8 - 3 * k - j
                for n, (c0, cw) in enumerate(halves):
                    term = nt(e[j][:, c0 : c0 + cw], weight[n][rows_of(tap * chan, chan), :])
                    acc = term if acc is None else acc + term

            @pl.when(k == 0)
            def _():
                out[:, 0:chan] = acc

            @pl.when(k > 0)
            def _():
                out[:, 0:chan] += acc

            if pump is not None:
                pump(k)
            return 0

        lax.fori_loop(0, 3, body, 0)

    def send_frames(k):
        down, up = r.down, r.up
        count = ROWS // CELL
        for c in range(chan // 128):
            lanes = pl.ds(128 * c, 128)
            r.halo_out[0, :, lanes] = down[c, pl.ds(2 * CELL - 1, count, stride=CELL), :]
            r.halo_out[1, :, lanes] = up[c, pl.ds(0, count, stride=CELL), :]
        copies = []
        for n, dev in ((0, later_dev), (1, earlier_dev)):
            copies.append(
                rc(r.halo_out.at[n], r.halo_in.at[k, n], r.halo_send.at[k, n], r.halo_recv.at[k, n], dev)
            )
            copies[-1].start()
        return copies

    def take_frames(k, copies):
        down, up = r.down, r.up
        count = ROWS // CELL
        for copy in copies:
            copy.wait()
        at_start = jnp.logical_and(h == 0, b == 0)
        at_end = jnp.logical_and(h == 1, b == nb - 1)
        for c in range(chan // 128):
            lanes = pl.ds(128 * c, 128)
            before = r.halo_in[k, 0, :, lanes]
            after = r.halo_in[k, 1, :, lanes]
            down[c, pl.ds(CELL - 1, count, stride=CELL), :] = jnp.where(at_start, 0.0, before)
            up[c, pl.ds(CELL, count, stride=CELL), :] = jnp.where(at_end, 0.0, after)

    def by_lanes(ref, rows):
        return jnp.concatenate([ref[c, rows, :] for c in range(chan // 128)], axis=1)

    def put_lanes(ref, rows, value):
        for c in range(chan // 128):
            ref[c, rows, :] = value[:, 128 * c : 128 * c + 128]

    def shifted(i):
        before = by_lanes(r.down, rows_of(i * CHUNK, CHUNK + CELL))[CELL - 1 : CELL - 1 + CHUNK]
        after = by_lanes(r.up, rows_of(i * CHUNK, CHUNK + CELL))[1 : 1 + CHUNK]
        gate = r.gate[...][None]
        return (before.reshape(2, CELL, chan) * gate, after.reshape(2, CELL, chan))

    def both_halves(weight, start, size):
        return jnp.concatenate([part[start : start + size, :] for part in weight], axis=1)

    def temporal(k, v, weight, out, works=()):
        works = list(works) + [None] * 2
        put_lanes(r.down, pl.ds(CELL, ROWS), nn(v[...], both_halves(weight, 0, mid)))
        y2 = nn(v[...], both_halves(weight, 2 * mid, mid))
        y2 = (y2.reshape(ROWS // CELL, CELL, chan) * r.gate[...][None]).reshape(ROWS, chan)
        put_lanes(r.up, pl.ds(0, ROWS), y2)
        copies = send_frames(k)
        out[...] = nn(v[...], both_halves(weight, mid, mid))
        if works[0]:
            works[0]()
        take_frames(k, copies)

        def body(i, carry):
            before, after = shifted(i)
            value = chunk(out, i) + before + after
            put(out, i, value)
            m = value * keep(i)
            return (carry[0] + m[0] + m[1], carry[1] + m[0] * value[0] + m[1] * value[1])

        zero = jnp.zeros((CELL, chan), F32)
        return loop(CHUNKS, body, (zero, zero))

    def put_e(tap, i, e):
        for c in (0, 1):
            r.e3[c, tap, rows_of(i * CHUNK, CHUNK), :] = e[:, c * half : (c + 1) * half]

    def temporal_back(k, weight, works=()):
        works = list(works) + [None] * 2
        copies = send_frames(k)
        e3 = r.e3

        def e_tap(n):
            return jnp.concatenate([e3[0, n], e3[1, n]], axis=1)

        for c0, cw in ((0, 512), (512, mid - 512)):
            r.grad_mid[:, c0 : c0 + cw] = nt(e_tap(1), both_halves(weight, mid + c0, cw))
        if works[0]:
            works[0]()
        take_frames(k, copies)

        def body(i, _):
            before, after = shifted(i)
            put_e(0, i, after.reshape(CHUNK, chan).astype(BF16))
            put_e(2, i, before.reshape(CHUNK, chan).astype(BF16))
            return 0

        loop(CHUNKS, body, 0)
        share = share_e3(k)
        for c0, cw in ((0, 512), (512, mid - 512)):
            r.grad_mid[:, c0 : c0 + cw] += nt(e_tap(0), both_halves(weight, c0, cw)) + nt(
                e_tap(2), both_halves(weight, 2 * mid + c0, cw)
            )
        return share

    def share(k, src, dst):
        copy = rc(src, dst, r.share_send.at[k], r.share_recv.at[k], sibling)
        copy.start()
        return copy

    outs = ((r.out1s0, r.out1s1), r.out1t, (r.out2s0, r.out2s1), r.out2t)

    e_all = (r.e_all0, r.e_all1)

    def e_part(n, slot):
        return e_all[n].at[slot * ROWS : (slot + 1) * ROWS, :]

    def e_copies(k, n):
        send, near, over = r.e_send.at[k, n], r.e_recv.at[k, n, 0], r.e_recv.at[k, n, 1]
        return [
            rc(e_part(n, 0), e_part(n, 1), send, near, sibling),
            rc(e_part(n, 0), e_part(n, 2), send, over, beside),
            rc(e_part(n, 2), e_part(n, 3), send, near, sibling),
        ]

    def share_e(k):
        for n in (0, 1):
            near, over, _ = e_copies(k, n)
            over.start()
            near.start()

    def share_e_on(k, n):
        _, over, far = e_copies(k, n)
        over.wait_recv()
        far.start()

    def share_e_wait(k, n):
        both = e_all[n].at[0 : 2 * ROWS, :]
        rc(both, both, r.e_send.at[k, n], r.e_recv.at[k, n, 0], sibling).wait_recv()
        three = e_all[n].at[0 : 3 * ROWS, :]
        rc(three, three, r.e_send.at[k, n], r.e_recv.at[k, n, 0], sibling).wait_send()

    def share_x(k, xa, xq):
        main = pl.ds(MAIN, ROWS)
        for n, dev in enumerate((sibling, beside, (1 - h, 1 - w, b))):
            lanes = rows_of((2 * dev[1] + dev[0]) * quarter, quarter, 128)
            rc(xa.at[main, lanes], xq.at[n, 0, main, :], r.xq_send.at[k], r.xq_recv.at[k], dev).start()
        all_three = xq.at[:, 0, main, :]
        return rc(all_three, all_three, r.xq_send.at[k], r.xq_recv.at[k], sibling)

    def pads(ref_a, ref_b, width):
        ref_a[0:MAIN, :] = jnp.zeros((MAIN, width), BF16)
        ref_a[MAIN + ROWS : PADDED, :] = jnp.zeros((PADDED - MAIN - ROWS, width), BF16)
        ref_b[0 : MAIN - CHUNK, :] = jnp.zeros((MAIN - CHUNK, width), BF16)
        ref_b[MAIN - CHUNK + ROWS : PADDED, :] = jnp.zeros((PADDED - MAIN + CHUNK - ROWS, width), BF16)

    def spread_x(xq):
        for n in range(3):
            pads(xq.at[n, 0], xq.at[n, 1], quarter)

        def body(i, before):
            after = []
            for n in range(3):
                v = chunk(xq.at[n, 0], i, MAIN)
                put(xq.at[n, 1], i, jnp.concatenate([before[n][None], v[0:1]], axis=0), MAIN - CHUNK)
                after.append(v[1])
            return tuple(after)

        loop(CHUNKS, body, (jnp.zeros((CELL, quarter), F32),) * 3)

    def share_e3(k):
        return share(
            k - 2, r.e3.at[1 - h], r.sib_e3
        )

    def line_row(place):
        return quarter * place + 64 * jnp.where(place > shared, 1, 0)

    def grad_row(tap, side):
        split = 2 * shared + 1
        owner = jnp.where(tap == split, 2 * shared + side, tap - jnp.where(tap > split, 1, 0))
        row = line_row(lax.div(owner, 2)) + jnp.where(tap == split, quarter, 64 * side)
        return 576 * lax.rem(owner, 2) + row

    spare = whole[2]

    def gq(i, row, size):
        return rows_of((mid if i == 0 else 0) + row, size, 64)

    def inbox(i, row, size):
        return rows_of(2 * mid + (mid if i == 0 else 0) + row, size, 64)

    def transpose_x(a, xa, xb, xq, near, far, row):
        lanes = rows_of(shared * quarter, quarter, 128)
        r0 = MAIN - 8 * CELL + 8 * CELL * a
        for j, (c, start) in enumerate(((1, r0 - CHUNK), (0, r0), (1, r0))):
            rows = rows_of(start, ROWS)
            own = (xb if c else xa)[rows, lanes]
            both = jnp.concatenate([own, xq[0, c, rows, :]], axis=0)
            near[rows_of(row + j * quarter, quarter), 0 : 2 * ROWS] = both.T
            both = jnp.concatenate([xq[1, c, rows, :], xq[2, c, rows, :]], axis=0)
            far[rows_of(row + j * quarter, quarter), 0 : 2 * ROWS] = both.T

    def spatial_part(i, near, far, row, tap, n):
        rows = rows_of(row, 3 * quarter)
        acc = nn(near[rows, :], e_all[n][0 : 2 * ROWS, :])
        acc += nn(far[rows, :], e_all[n][2 * ROWS : 4 * ROWS, :])
        acc = acc.astype(BF16)
        for j in range(6):
            spare[n][gq(i, grad_row(tap + j // 2, j % 2), 64), :] = acc[64 * j : 64 * j + 64]

    def transposes(xa, xb, xq, near, far):
        def body(a, _):
            transpose_x(a, xa, xb, xq, near, far, a * 3 * quarter)
            return 0

        lax.fori_loop(0, 3, body, 0)

    def spatial_half(i, near, far, n):
        def body(a, _):
            spatial_part(i, near, far, a * 3 * quarter, 3 * a, n)
            return 0

        lax.fori_loop(0, 3, body, 0)

    def transpose_v(v, sv):
        for c in range(mid // 128):
            lanes = pl.ds(128 * c, 128)
            turned = jnp.concatenate([v[:, lanes], sv[:, lanes]], axis=0).T
            for row in (0, 64):
                ref = r.ea if 128 * c + row < mid // 2 else r.eb
                at_row = (128 * c + row) % (mid // 2)
                ref[at_row : at_row + 64, 0 : 2 * ROWS] = turned[row : row + 64]

    def temporal_grad(i, first, count):
        taps_of = [jnp.concatenate([r.e3[h, k], r.sib_e3[k]], axis=0) for k in range(first, first + count)]
        e = jnp.concatenate(taps_of, axis=1)
        whole_tap = mid // third
        for top in range(0, whole_tap, whole_tap // 2):
            acc = nn((r.eb if top else r.ea)[0 : mid // 2, 0 : 2 * ROWS], e).astype(BF16)
            for k in range(count):
                for n in range(whole_tap // 2):
                    owner, part = divmod((first + k) * whole_tap + top + n, 3)
                    row = (owner % 2) * (depth * temp) + owner // 2 * temp + part * third
                    whole[i][0][row : row + third, :] = acc[n * third : n * third + third, k * half : (k + 1) * half]

    def parts_of(i):
        return (0, 1) if i % 2 == 0 else (0,)

    line_size = 576

    def to_y(i, n, side):
        if i % 2 == 0:
            return spare[n].at[gq(i, line_size * side, line_size), :]
        return whole[i][0].at[rows_of(depth * temp * side, depth * temp), :]

    def y_box(i, n):
        if i % 2 == 0:
            return spare[n].at[inbox(i, 0, line_size), :]
        return whole[i][1].at[0 : depth * temp, :]

    def block_of(i, n, place, size):
        if i % 2 == 0:
            return spare[n].at[gq(i, line_size * par + line_row(place), size), :]
        return whole[i][0].at[rows_of(depth * temp * par + place * temp, temp), :]

    def z_box(i, n, slot, size):
        if i % 2 == 0:
            return spare[n].at[inbox(i, line_size + slot * (line_size // 3), size), :]
        return whole[i][1].at[(depth + slot) * temp : (depth + slot + 1) * temp, :]

    def sized(i, place, work):
        if i % 2:
            work(temp)
        else:
            pl.when(place != shared)(lambda: work(quarter))
            pl.when(place == shared)(lambda: work(quarter + 64))

    def t_inbox(i, n):
        return whole[i][1].at[n * temp : (n + 1) * temp, :]

    def add_into(dst, parts, step):
        rows, cols = dst.shape

        def body(n, _):
            at_rows = rows_of(n * step, step)
            value = dst[at_rows, :].astype(F32)
            for part in parts:
                value = value + part[at_rows, :].astype(F32)
            dst[at_rows, :] = value.astype(BF16)
            return 0

        lax.fori_loop(0, rows // step, body, 0)

    def y_copy(i, n):
        return rc(to_y(i, n, 1 - par), y_box(i, n), r.y_send.at[i, n], r.y_recv.at[i, n], across)

    def z_copy(i, n, d, size):
        place = lax.rem(bh + d, depth)
        dev = (h, w, 2 * place + par)
        src, dst = block_of(i, n, place, size), z_box(i, n, 3 - d, size)
        return rc(src, dst, r.z_send.at[i, n], r.z_recv.at[i, n], dev)

    def step_of(i):
        return 32 if i % 2 == 0 else 48

    def reduce_start(i, n):
        y_copy(i, n).start()

    def reduce_middle(i, n):
        y_copy(i, n).wait()
        add_into(to_y(i, n, par), [y_box(i, n)], step_of(i))
        for d in (1, 2, 3):
            sized(i, lax.rem(bh + d, depth), lambda size, d=d: z_copy(i, n, d, size).start())

    def final_part(i, n, side, core):
        place = 2 * side + core
        start = quarter * place - 64 * b + 512 * jnp.where(b > 2 * place, 1, 0)
        return outs[i][n].at[rows_of(start, quarter, 64), :]

    def extra_part(i, n):
        return outs[i][n].at[rows_of(512 * (1 - par), 64, 64), :]

    def final_copies(i, n):
        if i % 2:
            src = block_of(i, n, bh, temp)
            part = outs[i].at[h]
            return lc(src, part, r.out_sem.at[i, 0, 0]), [
                (src, part, sibling, r.cast_send.at[i, 0, 0], r.cast_recv.at[i, 0, 0])
            ]
        src = block_of(i, n, bh, quarter)
        part = final_part(i, n, w, h)
        sends = [
            (src, part, dev, r.cast_send.at[i, n, d], r.cast_recv.at[i, n, d]) for d, dev in enumerate((beside, sibling))
        ]
        return lc(src, part, r.out_sem.at[i, n, 0]), sends

    def extra_copies(i, n):
        src = spare[n].at[gq(i, line_size * par + line_row(bh) + quarter, 64), :]
        part = extra_part(i, n)
        sends = [
            (src, part, dev, r.cast_send.at[i, n, 3 + d], r.cast_recv.at[i, n, 3 + d])
            for d, dev in enumerate((beside, sibling))
        ]
        return lc(src, part, r.out_sem.at[i, n, 1]), sends

    def begin(copies):
        local, sends = copies
        for src, part, dev, one, two in sends:
            rc(src, part, one, two, dev).start()
        local.start()

    def credit(n):
        pl.semaphore_signal(r.credit.at[n], inc=1, device_id=named(beside), device_id_type=MESH)

    def credited(n):
        pl.semaphore_wait(r.credit.at[n], 1)

    def beside_copy(i):
        return rc(block_of(i, 0, bh, temp), t_inbox(i, 7), r.fin_send.at[i], r.fin_recv.at[i], beside)

    def z_span(i, n, rows):
        return to_y(i, n, 0).at[0:rows, :]

    def reduce_last(i, n):
        def add(size):
            ref = z_span(i, n, 3 * size)
            rc(ref, ref, r.z_send.at[i, n], r.z_recv.at[i, n], across).wait_recv()
            add_into(block_of(i, n, bh, size), [z_box(i, n, slot, size) for slot in range(3)], step_of(i))

        sized(i, bh, add)
        if i % 2:
            credited(i // 2)
            beside_copy(i).start()
            return
        begin(final_copies(i, n))
        pl.when(bh == shared)(lambda: begin(extra_copies(i, n)))

    def reduce_out(i):
        beside_copy(i).wait()
        add_into(block_of(i, 0, bh, temp), [t_inbox(i, 7)], 48)
        begin(final_copies(i, 0))

    def final_on(i, n):
        def move(part, d):
            rc(part, part, r.cast_send.at[i, n, d], r.cast_recv.at[i, n, d], beside).wait_recv()
            rc(part, part, r.cast_send.at[i, n, d + 2], r.cast_recv.at[i, n, d + 2], sibling).start()

        move(final_part(i, n, 1 - w, h), 0)
        pl.when(bh == shared_beside)(lambda: move(extra_part(i, n), 3))

    def reduce_wait(i, n):
        local, sends = final_copies(i, n)
        local.wait()

        def sent(rows):
            ref = z_span(i, n, rows)
            rc(ref, ref, r.z_send.at[i, n], r.z_recv.at[i, n], across).wait_send()

        if i % 2:
            sent(3 * temp)
        else:
            pl.when(bh == shared)(lambda: sent(3 * quarter))
            pl.when(bh != shared)(lambda: sent(3 * quarter + 64))
        if i % 2:
            src, part, dev, one, two = sends[0]
            rc(src, outs[i].at[1 - h], one, two, dev).wait()
            return
        for src, part, dev, one, two in sends:
            rc(src, part, one, two, dev).wait_send()

        def far(part, d):
            return rc(part, part, r.cast_send.at[i, n, d], r.cast_recv.at[i, n, d], sibling)

        far(final_part(i, n, w, 1 - h), 1).wait_recv()
        far(final_part(i, n, 1 - w, h), 2).wait_send()
        far(final_part(i, n, 1 - w, 1 - h), 2).wait_recv()
        local, sends = extra_copies(i, n)

        @pl.when(bh == shared)
        def _():
            local.wait()
            for src, part, dev, one, two in sends:
                rc(src, part, one, two, dev).wait_send()

        pl.when(bh == shared_beside)(lambda: far(extra_part(i, n), 5).wait_send())
        pl.when(bh == 2 * w + 1 - h)(lambda: far(extra_part(i, n), 4).wait_recv())
        pl.when(bh == 2 * (1 - w) + 1 - h)(lambda: far(extra_part(i, n), 5).wait_recv())

    def tile_of(ref, jh, jw):
        return ref.at[rows_of(jh * 4, 4, 4), rows_of(jw * 32, 32), :]

    def tile_own(src, dst, n):
        return lc(src.at[mine], tile_of(dst, h, w), r.tile_own.at[n])

    def tiles_start(src, dst, n):
        for j, dev in tile_group:
            rc(src.at[j], tile_of(dst, h, w), r.tile_send.at[n], r.tile_recv.at[n], dev).start()
        tile_own(src, dst, n).start()

    def tiles_wait(src, dst, n):
        three = src.at[0:3]
        rc(three, three, r.tile_send.at[n], r.tile_recv.at[n], sibling).wait()
        tile_own(src, dst, n).wait()

    xg, cg = r.x_grid, r.cot_grid
    tiles_start(r.x_tiles, xg, 0)
    gather_start(0)
    r.param[...] = total(0, mid, r.param_in[...])
    tiles_wait(r.x_tiles, xg, 0)

    def grid_chunk(ref, i):
        v = ref[lax.div(i, 4), rows_of(lax.rem(i, 4) * CHUNK, CHUNK), :]
        return v.astype(F32).reshape(2, CELL, chan)

    fill(r.xa, r.xb, lambda i: grid_chunk(xg, i), chan)

    def pump_loop(i, lo, hi):
        def body(s, _):
            gather_pump(i, s)
            return 0

        lax.fori_loop(lo, hi, body, 0)

    pump_loop(0, 1, nb - 3)
    gather_start(1)
    pump_loop(0, nb - 3, nb - 1)
    gather_start(2)
    gather_pump(0, nb - 1)
    gather_pump(1, 1)
    gather_pump(2, 1)
    gather_pump(1, 2)
    gather_finish(0)

    def first_pump(n):
        pl.when(lax.rem(n, 2) == 0)(lambda: gather_pump(1, 3 + lax.div(n, 2)))
        pl.when(n == 3)(lambda: gather_pump(2, 2))

    conv(r.xa, r.xb, whole[0], r.mid1, first_pump)
    def first_last():
        gather_pump(2, 3)
        gather_pump(1, nb - 1)

    sums = total(
        1,
        mid,
        packed(*moments(r.mid1, mid), mid),
        [lambda: gather_pump(1, nb - 2), first_last],
    )
    prepare(0, sums, mid)

    def hidden(src, n, dst):
        value = activated(src, n, mid)

        def body(i, _):
            put(dst, i, value(i))
            return 0

        loop(CHUNKS, body, 0)

    hidden(r.mid1, 0, r.v1)
    gather_pump(2, 4)
    gather_finish(1)
    stats = temporal(0, r.v1, whole[1], r.time1, [lambda: gather_pump(2, 5)])

    def sixth():
        gather_pump(2, 6)

    sums = total(2, chan, packed(*stats, chan), [lambda: gather_start(3), sixth])
    prepare(1, sums, chan)
    fill(r.aa, r.ab, activated(r.time1, 1, chan), chan)
    gather_pump(3, 1)
    gather_pump(2, nb - 1)
    gather_pump(3, 2)
    gather_finish(2)
    tiles_start(r.cot_tiles, cg, 1)

    def second_pump(n):
        pl.when(n < nb - 3)(lambda: gather_pump(3, 3 + n))

    conv(r.aa, r.ab, whole[2], r.mid2, second_pump)
    sums = total(3, mid, packed(*moments(r.mid2, mid), mid), [lambda: gather_finish(3)])
    prepare(2, sums, mid)
    hidden(r.mid2, 2, r.v2)
    stats = temporal(1, r.v2, whole[3], r.time2)
    shared_xq2 = share_x(0, r.aa, r.xq2)
    shared_xq1 = share_x(1, r.xa, r.xq1)
    for i in range(4):
        gather_sent(i)
    share_v2 = share(4, r.v2, r.sib_v)
    sums = total(4, chan, packed(*stats, chan), [lambda: tiles_wait(r.cot_tiles, cg, 1)])
    prepare(3, sums, chan)

    out_grid = r.out_grid

    def grid_put(ref, i, v):
        ref[lax.div(i, 4), rows_of(lax.rem(i, 4) * CHUNK, CHUNK), :] = v.reshape(CHUNK, chan).astype(ref.dtype)

    def slope(y, s):
        return s * (1.0 + y * (1.0 - s))

    def pre_body(i, carry):
        scale, shift, inv, offset = tiles(3, chan)
        v = chunk(r.time2, i)
        y = v * scale + shift + chunk(r.xa, i, MAIN)
        s = sigmoid(y)
        m = keep(i)
        grid_put(out_grid, i, y * s * m)
        d = grid_chunk(cg, i) * m * slope(y, s)
        put(r.grad_pre, i, d)
        t = d * (v * inv - offset)
        return (carry[0] + d[0] + d[1], carry[1] + t[0] + t[1])

    zero_out = jnp.zeros((CELL, chan), F32)
    zero_mid = jnp.zeros((CELL, mid), F32)
    out_grid[HGT] = jnp.zeros((8 * CELL, chan), BF16)
    gg = loop(CHUNKS, pre_body, (zero_out, zero_out))

    def send_tiles(src, dst, n):
        for j, dev in tile_group:
            jh, jw = at_group(j)
            rc(tile_of(src, jh, jw), dst.at[mine], r.tile_send.at[n], r.tile_recv.at[n], dev).start()
        lc(tile_of(src, h, w), dst.at[mine], r.tile_own.at[n]).start()

    def sent_tiles(src, dst, n):
        three = dst.at[0:3]
        rc(three, three, r.tile_send.at[n], r.tile_recv.at[n], sibling).wait()
        lc(tile_of(src, h, w), dst.at[mine], r.tile_own.at[n]).wait()

    send_tiles(out_grid, r.block_out, 2)

    def norm_back(n, sums, width):
        r.norm_part[0, 2 * n : 2 * n + 1, 0:width] = sums[1:2]
        r.norm_part[0, 2 * n + 1 : 2 * n + 2, 0:width] = sums[0:1]
        back = r.back
        back[0, :, 0:width] = jnp.broadcast_to(sums[0:1] / cell_count, (CELL, width))
        back[1, :, 0:width] = jnp.broadcast_to(sums[1:2] / cell_count, (CELL, width))

    def through_norm(n, src, grad, i, width):
        scale, _, inv, offset = tiles(n, width)
        xhat = chunk(src, i) * inv - offset
        bias_part = r.back[0, :, 0:width][None]
        gain_part = r.back[1, :, 0:width][None]
        return scale * (chunk(grad, i, 0, width) - bias_part - xhat * gain_part) * keep(i)

    def through_act(n, src, grad, width):
        def body(i, carry):
            scale, shift, inv, offset = tiles(n, width)
            v = chunk(src, i)
            y = v * scale + shift
            s = sigmoid(y)
            d = chunk(grad, i, 0, width) * keep(i) * slope(y, s)
            put(grad, i, d, 0, width)
            t = d * (v * inv - offset)
            return (carry[0] + d[0] + d[1], carry[1] + t[0] + t[1])

        zero = jnp.zeros((CELL, width), F32)
        return loop(CHUNKS, body, (zero, zero))

    def to_frames(n, src, grad):
        def body(i, _):
            e = through_norm(n, src, grad, i, chan).astype(BF16)
            ef = e.astype(F32)
            put_e(1, i, e.reshape(CHUNK, chan))
            put_lanes(r.down, rows_of(i * CHUNK + CELL, CHUNK, CELL), ef.reshape(CHUNK, chan))
            put_lanes(r.up, rows_of(i * CHUNK, CHUNK), (ef * r.gate[...][None]).reshape(CHUNK, chan))
            return 0

        loop(CHUNKS, body, 0)

    near, far = r.xt, r.xt2

    def spread():
        shared_xq2.wait()
        spread_x(r.xq2)
        shared_xq1.wait()
        spread_x(r.xq1)

    sums = total(5, chan, packed(*gg, chan), [spread, lambda: transposes(r.aa, r.ab, r.xq2, near, far)])
    norm_back(3, sums, chan)
    to_frames(3, r.time2, r.grad_pre)
    shared_e3 = temporal_back(2, whole[3])
    credit(1)
    gg = through_act(2, r.mid2, r.grad_mid, mid)
    shared_e3.wait()
    share_v2.wait()
    def temporal_grads(i, v):
        def first():
            transpose_v(v, r.sib_v)
            temporal_grad(i, 0, 2)

        return [first, lambda: temporal_grad(i, 2, 1)]

    sums = total(6, mid, packed(*gg, mid), temporal_grads(3, r.v2))
    reduce_start(3, 0)
    norm_back(2, sums, mid)

    def fill_e(n, src):
        def value(i):
            v = through_norm(n, src, r.grad_mid, i, mid)
            for part, (c0, cw) in zip(e_all, halves):
                put(part, i, v[:, :, c0 : c0 + cw])
            return v

        fill(r.ea, r.eb, value, mid)

    fill_e(2, r.mid2)
    share_e(0)
    conv_back(r.ea, r.eb, whole[2], r.grad_mid)
    gg = through_act(1, r.time1, r.grad_mid, chan)

    def first_half():
        share_e_wait(0, 0)
        spatial_half(2, near, far, 0)

    sums = total(7, chan, packed(*gg, chan), [lambda: share_e_on(0, 0), first_half])
    reduce_start(2, 0)
    share_v1 = share(5, r.v1, r.sib_v)
    norm_back(1, sums, chan)
    to_frames(1, r.time1, r.grad_mid)
    reduce_middle(3, 0)
    share_e_on(0, 1)

    def second_half():
        share_e_wait(0, 1)
        spatial_half(2, near, far, 1)
        credit(2)
        reduce_start(2, 1)

    shared_e3 = temporal_back(3, whole[1], [second_half])
    credit(0)
    reduce_middle(2, 0)
    gg = through_act(0, r.mid1, r.grad_mid, mid)
    shared_e3.wait()
    share_v1.wait()
    sums = total(8, mid, packed(*gg, mid), temporal_grads(1, r.v1))
    reduce_start(1, 0)
    reduce_middle(2, 1)
    norm_back(0, sums, mid)
    fill_e(0, r.mid1)
    credited(2)
    share_e(1)
    reduce_last(3, 0)
    transposes(r.xa, r.xb, r.xq1, near, far)
    share_e_on(1, 0)
    reduce_out(3)
    sent_tiles(out_grid, r.block_out, 2)
    share_e_wait(1, 0)
    spatial_half(0, near, far, 0)
    reduce_start(0, 0)
    reduce_middle(1, 0)

    def pass_on(k):
        pl.when(k == 2)(lambda: share_e_on(1, 1))

    conv_back(r.ea, r.eb, whole[0], r.grad_mid, pass_on)
    share_e_wait(1, 1)
    spatial_half(0, near, far, 1)
    reduce_start(0, 1)
    reduce_middle(0, 0)

    norm_copy = rc(r.norm_part.at[0], r.norm_part.at[1], r.norm_sem.at[0], r.norm_sem.at[1], beside)
    norm_copy.start()

    def last_body(i, _):
        grid_put(out_grid, i, (chunk(r.grad_mid, i, 0, chan) + chunk(r.grad_pre, i)) * keep(i))
        return 0

    loop(CHUNKS, last_body, 0)
    send_tiles(out_grid, r.grad_input, 3)
    for n in (0, 1):
        reduce_last(2, n)
    reduce_last(1, 0)
    for n in (0, 1):
        final_on(2, n)
    reduce_out(1)
    reduce_last(0, 0)
    norm_copy.wait()
    r.norm_grads[...] = r.norm_part[0] + r.norm_part[1]
    reduce_middle(0, 1)
    final_on(0, 0)
    sent_tiles(out_grid, r.grad_input, 3)
    for n in (0, 1):
        reduce_wait(2, n)
    reduce_wait(3, 0)
    reduce_wait(1, 0)
    reduce_last(0, 1)
    final_on(0, 1)
    for n in (0, 1):
        reduce_wait(0, n)


def per_device_fast(nb, *args):
    (
        inputs,
        starts,
        first_spatial,
        first_mid_gain,
        first_mid_bias,
        first_temporal,
        first_out_gain,
        first_out_bias,
        second_spatial,
        second_mid_gain,
        second_mid_bias,
        second_temporal,
        second_out_gain,
        second_out_bias,
        cotangent,
    ) = args
    micro, frames, side, _, chan = inputs.shape
    mid = first_spatial.shape[1]
    spat, temp = first_spatial.shape[0], first_temporal.shape[0]
    h, w, b = (lax.axis_index(name) for name in ("ha", "wa", "batch"))
    few = frames // 2
    offsets = jnp.arange(side)
    valid = (h * side + offsets < HGT)[:, None] & (w * side + offsets < HGT)[None, :]

    def tiles(array):
        array = array * valid.astype(BF16)[None, None, :, :, None]
        array = array.reshape(micro, 2, few, side, side, chan).transpose(0, 1, 3, 4, 2, 5)
        return array.reshape(4, side, side * few, chan)

    def untiled(array):
        array = array.reshape(micro, 2, side, side, few, chan).transpose(0, 1, 4, 2, 3, 5)
        return array.reshape(micro, frames, side, side, chan).astype(F32)

    gate = (1 - lax.dynamic_slice(starts, (w, h * few), (1, few))).astype(F32)
    gate = jnp.broadcast_to(gate.reshape(few, 1), (few, chan))
    here = jnp.where(h == 0, 1.0, 0.0)

    def placed(shard):
        row = jnp.zeros((mid,), F32)
        return lax.dynamic_update_slice(row, shard.astype(F32) * here, (b * shard.shape[0],))

    param = jnp.stack(
        [
            placed(v)
            for v in (
                first_mid_gain,
                first_mid_bias,
                first_out_gain,
                first_out_bias,
                second_mid_gain,
                second_mid_bias,
                second_out_gain,
                second_out_bias,
            )
        ]
    )
    half = chan // 2
    few_rows = ROWS // CELL

    inputs_of = dict(
        x_tiles=(tiles(inputs), pl.ANY),
        cot_tiles=(tiles(cotangent), pl.ANY),
        gate=(gate, pltpu.VMEM),
        param_in=(param, pltpu.VMEM),
        first_spatial=(first_spatial, pl.ANY),
        first_temporal=(first_temporal, pl.ANY),
        second_spatial=(second_spatial, pl.ANY),
        second_temporal=(second_temporal, pl.ANY),
    )
    outputs_of = dict(
        block_out=((4, side, side * CELL, chan), BF16, pl.ANY),
        grad_input=((4, side, side * CELL, chan), BF16, pl.ANY),
        norm_grads=((8, mid), F32, pltpu.VMEM),
        out1s0=((spat, 512), BF16, pl.ANY),
        out1s1=((spat, mid - 512), BF16, pl.ANY),
        out1t=((2, temp, half), BF16, pl.ANY),
        out2s0=((spat, 512), BF16, pl.ANY),
        out2s1=((spat, mid - 512), BF16, pl.ANY),
        out2t=((2, temp, half), BF16, pl.ANY),
    )
    dma = pltpu.SemaphoreType.DMA
    scratch_of = dict(
        w1s0=pltpu.VMEM((9 * chan, 512), BF16),
        w1s1=pltpu.VMEM((9 * chan, mid - 512), BF16),
        w1t0=pltpu.VMEM((3 * mid, half), BF16),
        w1t1=pltpu.VMEM((3 * mid, half), BF16),
        w2s0=pltpu.VMEM((9 * chan, 512), BF16),
        w2s1=pltpu.VMEM((9 * chan, mid - 512), BF16),
        w2t0=pltpu.VMEM((3 * mid, half), BF16),
        w2t1=pltpu.VMEM((3 * mid, half), BF16),
        x_grid=pltpu.VMEM((8, 8 * CELL, chan), BF16),
        cot_grid=pltpu.VMEM((8, 8 * CELL, chan), BF16),
        out_grid=pltpu.VMEM((8, 8 * CELL, chan), BF16),
        xa=pltpu.VMEM((PADDED, chan), BF16),
        xb=pltpu.VMEM((PADDED, chan), BF16),
        aa=pltpu.VMEM((PADDED, chan), BF16),
        ab=pltpu.VMEM((PADDED, chan), BF16),
        ea=pltpu.VMEM((PADDED, mid), BF16),
        eb=pltpu.VMEM((PADDED, mid), BF16),
        mid1=pltpu.VMEM((ROWS, mid), F32),
        mid2=pltpu.VMEM((ROWS, mid), F32),
        grad_mid=pltpu.VMEM((ROWS, mid), F32),
        v1=pltpu.VMEM((ROWS, mid), BF16),
        v2=pltpu.VMEM((ROWS, mid), BF16),
        time1=pltpu.VMEM((ROWS, chan), F32),
        time2=pltpu.VMEM((ROWS, chan), F32),
        grad_pre=pltpu.VMEM((ROWS, chan), F32),
        down=pltpu.VMEM((chan // 128, ROWS + CHUNK, 128), F32),
        up=pltpu.VMEM((chan // 128, ROWS + CHUNK, 128), F32),
        e3=pltpu.VMEM((2, 3, ROWS, half), BF16),
        sib_e3=pltpu.VMEM((3, ROWS, half), BF16),
        halo_out=pltpu.VMEM((2, few_rows, chan), F32),
        halo_in=pltpu.VMEM((4, 2, few_rows, chan), F32),
        param=pltpu.VMEM((8, mid), F32),
        tile_mid=pltpu.VMEM((2, 4, CELL, mid), F32),
        tile_out=pltpu.VMEM((2, 4, CELL, chan), F32),
        back=pltpu.VMEM((2, CELL, mid), F32),
        norm_part=pltpu.VMEM((2, 8, mid), F32),
        sum_b=pltpu.VMEM((2, 4, 8, mid), F32),
        sum_c=pltpu.VMEM((2, nb // 2, 8, mid), F32),
        own_sem=dma((4, 2)),
        ring_send=dma((4, 2)),
        ring_recv=dma((4, 2, 2, nb)),
        sib_send=dma((4, 2)),
        sib_recv=dma((4, 2)),
        over_send=dma((4, 2)),
        over_recv=dma((4, 2, nb)),
        norm_sem=dma((2,)),
        credit=pltpu.SemaphoreType.REGULAR((3,)),
        sb_send=dma((9,)),
        sb_recv=dma((9,)),
        sc_send=dma((9,)),
        sc_recv=dma((9,)),
        halo_send=dma((4, 2)),
        halo_recv=dma((4, 2)),
        share_send=dma((6,)),
        share_recv=dma((6,)),
        e_all0=pltpu.VMEM((4 * ROWS, 512), BF16),
        e_all1=pltpu.VMEM((4 * ROWS, mid - 512), BF16),
        xq1=pltpu.VMEM((3, 2, PADDED, chan // 4), BF16),
        xq2=pltpu.VMEM((3, 2, PADDED, chan // 4), BF16),
        xt=pltpu.VMEM((mid, 2 * ROWS), BF16),
        xt2=pltpu.VMEM((mid, 2 * ROWS), BF16),
        sib_v=pltpu.VMEM((ROWS, mid), BF16),
        e_send=dma((2, 2)),
        e_recv=dma((2, 2, 2)),
        xq_send=dma((2,)),
        xq_recv=dma((2,)),
        y_send=dma((4, 2)),
        y_recv=dma((4, 2)),
        z_send=dma((4, 2)),
        z_recv=dma((4, 2)),
        cast_send=dma((4, 2, 6)),
        cast_recv=dma((4, 2, 8)),
        out_sem=dma((4, 2, 2)),
        fin_send=dma((4,)),
        fin_recv=dma((4,)),
        tile_send=dma((4,)),
        tile_recv=dma((4,)),
        tile_own=dma((4,)),
    )
    names = (*inputs_of, *outputs_of, *scratch_of)
    cell_count = float(frames * nb * HGT * HGT)
    results = pl.pallas_call(
        functools.partial(block_kernel, (nb, chan, mid, cell_count), names),
        out_shape=[jax.ShapeDtypeStruct(shape, dtype) for shape, dtype, _ in outputs_of.values()],
        in_specs=[pl.BlockSpec(memory_space=space) for _, space in inputs_of.values()],
        out_specs=[pl.BlockSpec(memory_space=space) for _, _, space in outputs_of.values()],
        scratch_shapes=list(scratch_of.values()),
        compiler_params=pltpu.CompilerParams(
            collective_id=0, has_side_effects=True, vmem_limit_bytes=VMEM_LIMIT
        ),
    )(*(array for array, _ in inputs_of.values()))
    got = SimpleNamespace(**dict(zip(outputs_of, results)))

    def spatial(left, right):
        return jnp.concatenate([left, right], axis=1).astype(F32)

    def temporal(pair):
        return jnp.concatenate([pair[0], pair[1]], axis=1).astype(F32)

    def norm(row, like):
        size = like.shape[0]
        return lax.dynamic_slice_in_dim(got.norm_grads[row], b * size, size)

    return (
        untiled(got.block_out),
        untiled(got.grad_input),
        spatial(got.out1s0, got.out1s1),
        norm(0, first_mid_gain),
        norm(1, first_mid_bias),
        temporal(got.out1t),
        norm(2, first_out_gain),
        norm(3, first_out_bias),
        spatial(got.out2s0, got.out2s1),
        norm(4, second_mid_gain),
        norm(5, second_mid_bias),
        temporal(got.out2t),
        norm(6, second_out_gain),
        norm(7, second_out_bias),
    )


def extended(shard, sides, width):
    for axis, dim in sides:
        count, length = (lax.axis_size(axis), shard.shape[dim])
        up = [(i, (i + 1) % count) for i in range(count - 1)]
        down = [(j, i) for i, j in up]
        last = lax.slice_in_dim(shard, length - width, length, axis=dim)
        leading = lax.slice_in_dim(shard, 0, width, axis=dim)
        before = lax.ppermute(last, axis, up)
        after = lax.ppermute(leading, axis, down)
        shard = jnp.concatenate([before, shard, after], axis=dim)
    return shard


def passed_along(shard, axis, by):
    count = lax.axis_size(axis)
    pairs = [(i, i + by) for i in range(count) if 0 <= i + by < count]
    return lax.ppermute(shard, axis, pairs)


def for_sending(shard):

    def short(part):
        return part.astype(jnp.bfloat16) if part.dtype == jnp.float32 else part

    return jax.tree.map(short, shard)


def silu_slope(values):
    sigma = jax.nn.sigmoid(values)
    return sigma * (1.0 + values * (1.0 - sigma))


def spatial_forward(field_in, kernel):
    frames, tile_side = (field_in.shape[0], field_in.shape[1])
    padded = extended(field_in, (("ha", 1), ("wa", 2)), 1)
    pieces = [
        padded[:, offset // 3 : offset // 3 + tile_side, offset % 3 : offset % 3 + tile_side, :]
        for offset in range(9)
    ]
    patches = jnp.concatenate(pieces, axis=-1).reshape(frames * tile_side * tile_side, -1)
    return (patches, jnp.dot(patches, kernel, preferred_element_type=jnp.float32))


def spatial_backward(grad_out, patches, kernel):
    frames, tile_side, channels = (grad_out.shape[0], grad_out.shape[1], grad_out.shape[3])
    row_count = frames * tile_side * tile_side
    padded = extended(grad_out, (("ha", 1), ("wa", 2)), 1)
    pieces = [
        padded[
            :,
            2 - offset // 3 : 2 - offset // 3 + tile_side,
            2 - offset % 3 : 2 - offset % 3 + tile_side,
            :,
        ]
        for offset in range(9)
    ]
    stacked = jnp.concatenate(pieces, axis=-1).reshape(row_count, 9, channels)
    grad_in = jnp.einsum(
        "rkm,kcm->rc", stacked, kernel.reshape(9, -1, channels), preferred_element_type=jnp.float32
    )
    grad_kernel = jnp.einsum(
        "rk,rm->km",
        patches,
        grad_out.reshape(row_count, channels),
        preferred_element_type=jnp.float32,
    )
    return (grad_in, grad_kernel)


def temporal_forward(field_in, clip_gate, kernel):
    frames, tile_side = (field_in.shape[0], field_in.shape[1])
    gated_in = field_in * clip_gate
    earlier = passed_along(field_in[-1:], "batch", 1)
    later_frame = passed_along(gated_in[:1], "batch", -1)
    before = jnp.concatenate([earlier, field_in[:-1]], axis=0) * clip_gate
    after_tap = jnp.concatenate([gated_in[1:], later_frame], axis=0)
    joined = jnp.concatenate([before, field_in, after_tap], axis=-1).reshape(
        frames * tile_side * tile_side, -1
    )
    return (joined, jnp.dot(joined, kernel, preferred_element_type=jnp.float32))


def temporal_backward(grad_out, joined, clip_gate, kernel):
    frames, tile_side, channels = (grad_out.shape[0], grad_out.shape[1], grad_out.shape[3])
    row_count = frames * tile_side * tile_side
    gated_grad = grad_out * clip_gate
    later_frame = passed_along(gated_grad[:1], "batch", -1)
    earlier = passed_along(grad_out[-1:], "batch", 1)
    from_later = jnp.concatenate([gated_grad[1:], later_frame], axis=0)
    from_earlier = jnp.concatenate([earlier, grad_out[:-1]], axis=0) * clip_gate
    stacked = jnp.concatenate([from_later, grad_out, from_earlier], axis=-1).reshape(
        row_count, 3, channels
    )
    grad_in = jnp.einsum(
        "rkc,kmc->rm", stacked, kernel.reshape(3, -1, channels), preferred_element_type=jnp.float32
    )
    grad_kernel = jnp.einsum(
        "rk,rc->kc",
        joined,
        grad_out.reshape(row_count, channels),
        preferred_element_type=jnp.float32,
    )
    return (grad_in, grad_kernel)


def norm_forward(pre_norm, norm_gain, norm_bias, valid_rows, cell_count):
    first_sum = jnp.sum(pre_norm * valid_rows, axis=0)
    square_sum = jnp.sum(pre_norm * pre_norm * valid_rows, axis=0)
    first_sum, square_sum = lax.psum((first_sum, square_sum), ("ha", "wa", "batch"))
    mean_val = first_sum / cell_count
    inv_std = lax.rsqrt(square_sum / cell_count - mean_val * mean_val + epsilon)
    normed = (pre_norm - mean_val) * inv_std
    return (normed, inv_std, normed * norm_gain.astype(jnp.float32) + norm_bias.astype(jnp.float32))


def norm_backward(grad_norm, normed, inv_std, norm_gain, valid_rows, cell_count):
    bias_grad = jnp.sum(grad_norm, axis=0)
    gain_grad = jnp.sum(grad_norm * normed, axis=0)
    bias_grad, gain_grad = lax.psum((bias_grad, gain_grad), ("ha", "wa", "batch"))
    grad_in = (
        valid_rows
        * norm_gain.astype(jnp.float32)
        * inv_std
        * (grad_norm - bias_grad / cell_count - normed * gain_grad / cell_count)
    )
    return (grad_in, gain_grad, bias_grad)


def forward_pair(field_in, weights, clip_gate, valid_rows, cell_count):
    frames, tile_side = (field_in.shape[0], field_in.shape[1])
    patches, spatial_out = spatial_forward(field_in, weights[0])
    mid_hat, mid_scale, mid_norm = norm_forward(
        spatial_out, weights[1], weights[2], valid_rows, cell_count
    )
    hidden = (
        (jax.nn.silu(mid_norm) * valid_rows)
        .astype(jnp.bfloat16)
        .reshape(frames, tile_side, tile_side, -1)
    )
    joined, temporal_out = temporal_forward(hidden, clip_gate, weights[3])
    out_hat, out_scale, out_norm = norm_forward(
        temporal_out, weights[4], weights[5], valid_rows, cell_count
    )
    return ((patches, mid_hat, mid_scale, mid_norm, joined, out_hat, out_scale), out_norm)


def backward_pair(grad_norm, kept, weights, clip_gate, valid_rows, cell_count, tile_side):
    patches, mid_hat, mid_scale, mid_norm, joined, out_hat, out_scale = kept
    frames = clip_gate.shape[0]
    grad_time, out_gain_grad, out_bias_grad = norm_backward(
        grad_norm, out_hat, out_scale, weights[4], valid_rows, cell_count
    )
    grad_time = grad_time.astype(jnp.bfloat16).reshape(frames, tile_side, tile_side, -1)
    grad_hidden, temporal_grad = temporal_backward(grad_time, joined, clip_gate, weights[3])
    grad_mid = grad_hidden * valid_rows * silu_slope(mid_norm)
    grad_spatial, mid_gain_grad, mid_bias_grad = norm_backward(
        grad_mid, mid_hat, mid_scale, weights[1], valid_rows, cell_count
    )
    grad_spatial = grad_spatial.astype(jnp.bfloat16).reshape(frames, tile_side, tile_side, -1)
    grad_in, spatial_grad = spatial_backward(grad_spatial, patches, weights[0])
    return (
        grad_in,
        (spatial_grad, mid_gain_grad, mid_bias_grad, temporal_grad, out_gain_grad, out_bias_grad),
    )


def per_device(
    inputs,
    starts,
    first_spatial,
    first_mid_gain,
    first_mid_bias,
    first_temporal,
    first_out_gain,
    first_out_bias,
    second_spatial,
    second_mid_gain,
    second_mid_bias,
    second_temporal,
    second_out_gain,
    second_out_bias,
    cotangent,
):
    shards = (
        first_spatial,
        first_mid_gain,
        first_mid_bias,
        first_temporal,
        first_out_gain,
        first_out_bias,
        second_spatial,
        second_mid_gain,
        second_mid_bias,
        second_temporal,
        second_out_gain,
        second_out_bias,
    )
    micro_total, frames, tile_side, channels = (
        inputs.shape[0],
        inputs.shape[1],
        inputs.shape[2],
        inputs.shape[4],
    )
    row_count = frames * tile_side * tile_side
    cell_count = frames * lax.axis_size("batch") * HGT * HGT
    offsets = jnp.arange(tile_side)
    inside_h = lax.axis_index("ha") * tile_side + offsets < HGT
    inside_w = lax.axis_index("wa") * tile_side + offsets < HGT
    valid_grid = inside_h[:, None] & inside_w[None, :]
    valid_tile = valid_grid.astype(jnp.bfloat16)[None, :, :, None]
    valid_rows = jnp.broadcast_to(
        valid_grid.astype(jnp.float32)[None], (frames, tile_side, tile_side)
    ).reshape(row_count, 1)
    results = []
    input_grads = []
    kernel_total = None
    norm_total = None
    for micro_step in range(micro_total):
        gathered = (
            lax.all_gather(shards[0], "batch", axis=0, tiled=True),
            lax.all_gather(shards[1], "batch", axis=0, tiled=True),
            lax.all_gather(shards[2], "batch", axis=0, tiled=True),
            lax.all_gather(shards[3], "batch", axis=0, tiled=True),
            lax.all_gather(shards[4], "batch", axis=0, tiled=True),
            lax.all_gather(shards[5], "batch", axis=0, tiled=True),
            lax.all_gather(shards[6], "batch", axis=0, tiled=True),
            lax.all_gather(shards[7], "batch", axis=0, tiled=True),
            lax.all_gather(shards[8], "batch", axis=0, tiled=True),
            lax.all_gather(shards[9], "batch", axis=0, tiled=True),
            lax.all_gather(shards[10], "batch", axis=0, tiled=True),
            lax.all_gather(shards[11], "batch", axis=0, tiled=True),
        )
        clip_gate = (1 - starts[micro_step]).astype(jnp.bfloat16).reshape(frames, 1, 1, 1)
        x_in = inputs[micro_step] * valid_tile
        first_kept, first_norm = forward_pair(
            x_in, gathered[0:6], clip_gate, valid_rows, cell_count
        )
        first_act = (
            (jax.nn.silu(first_norm) * valid_rows)
            .astype(jnp.bfloat16)
            .reshape(frames, tile_side, tile_side, channels)
        )
        second_kept, second_norm = forward_pair(
            first_act, gathered[6:12], clip_gate, valid_rows, cell_count
        )
        pre_out = second_norm + x_in.reshape(row_count, channels).astype(jnp.float32)
        results.append(
            (jax.nn.silu(pre_out) * valid_rows).reshape(frames, tile_side, tile_side, channels)
        )
        grad_pre = (
            cotangent[micro_step].reshape(row_count, channels).astype(jnp.float32)
            * valid_rows
            * silu_slope(pre_out)
        )
        grad_act, second_grads = backward_pair(
            grad_pre, second_kept, gathered[6:12], clip_gate, valid_rows, cell_count, tile_side
        )
        grad_first = grad_act * valid_rows * silu_slope(first_norm)
        grad_conv, first_grads = backward_pair(
            grad_first, first_kept, gathered[0:6], clip_gate, valid_rows, cell_count, tile_side
        )
        input_grads.append(
            ((grad_conv + grad_pre) * valid_rows).reshape(frames, tile_side, tile_side, channels)
        )
        step_grads = first_grads + second_grads
        kernel_now = (step_grads[0], step_grads[3], step_grads[6], step_grads[9])
        norm_now = (
            step_grads[1],
            step_grads[2],
            step_grads[4],
            step_grads[5],
            step_grads[7],
            step_grads[8],
            step_grads[10],
            step_grads[11],
        )
        if micro_step == 0:
            kernel_total = kernel_now
            norm_total = norm_now
        else:
            kernel_total = jax.tree.map(jnp.add, kernel_total, kernel_now)
            norm_total = jax.tree.map(jnp.add, norm_total, norm_now)
    kernel_total = lax.psum_scatter(kernel_total, "batch", scatter_dimension=0, tiled=True)
    kernel_total = jax.tree.map(
        lambda part: part.astype(jnp.float32), lax.psum(for_sending(kernel_total), ("ha", "wa"))
    )
    shard_index = lax.axis_index("batch")
    batch_count = lax.axis_size("batch")
    norm_shards = tuple(
        (
            lax.dynamic_slice_in_dim(
                full_sum,
                shard_index * (full_sum.shape[0] // batch_count),
                full_sum.shape[0] // batch_count,
            )
            for full_sum in norm_total
        )
    )
    return (
        jnp.stack(results),
        jnp.stack(input_grads),
        kernel_total[0],
        norm_shards[0],
        norm_shards[1],
        kernel_total[1],
        norm_shards[2],
        norm_shards[3],
        kernel_total[2],
        norm_shards[4],
        norm_shards[5],
        kernel_total[3],
        norm_shards[6],
        norm_shards[7],
    )


def solution(mesh):
    in_specs = (
        P(None, "batch", "ha", "wa", None),
        P(None, "batch"),
        P("batch", None),
        P("batch"),
        P("batch"),
        P("batch", None),
        P("batch"),
        P("batch"),
        P("batch", None),
        P("batch"),
        P("batch"),
        P("batch", None),
        P("batch"),
        P("batch"),
        P(None, "batch", "ha", "wa", None),
    )
    out_specs = (
        P(None, "batch", "ha", "wa", None),
        P(None, "batch", "ha", "wa", None),
        P("batch", None),
        P("batch"),
        P("batch"),
        P("batch", None),
        P("batch"),
        P("batch"),
        P("batch", None),
        P("batch"),
        P("batch"),
        P("batch", None),
        P("batch"),
        P("batch"),
    )
    batch = mesh.shape["batch"]

    def program(*args):
        spat, temp = args[2].shape[0], args[5].shape[0]
        fits = args[0].shape == (2, 16, 4, 4, 512) and args[2].shape[1] == 1152
        if fits and batch == 8 and spat * batch == 9 * 512 and temp * batch == 3 * 1152:
            return per_device_fast(batch, *args)
        return per_device(*args)

    return jax.shard_map(
        program, mesh=mesh, in_specs=in_specs, out_specs=out_specs, check_vma=False
    )
```

```python
import functools
from types import SimpleNamespace

import jax
import jax.numpy as jnp
from jax import lax
from jax.experimental import pallas as pl
from jax.experimental.pallas import tpu as pltpu
from jax.sharding import PartitionSpec as P

HGT = 7
epsilon = 1e-05
MESH = pl.DeviceIdType.MESH
F32 = jnp.float32
BF16 = jnp.bfloat16

BASE = 10
CELL = 8
ROWS = HGT * 8 * CELL
PADDED = (BASE + HGT * 8 + BASE) * CELL
MAIN = BASE * CELL
CHUNK = 2 * CELL
CHUNKS = ROWS // CHUNK
VMEM_LIMIT = 64 * 1024 * 1024 - 1024 * 1024


def when(cond, work):
    if cond is True:
        work()
    elif cond is not False:
        pl.when(cond)(work)


def loop(count, body, init):
    def twice(i, carry):
        return body(2 * i + 1, body(2 * i, carry))

    return lax.fori_loop(0, count // 2, twice, init)


def sigmoid(x):
    return 0.5 * jnp.tanh(0.5 * x) + 0.5


def nn(a, b):
    return jnp.dot(a, b, preferred_element_type=F32)


def nt(a, b):
    return lax.dot_general(a, b, (((1,), (1,)), ((), ())), preferred_element_type=F32)


def tn(a, b):
    return lax.dot_general(a, b, (((0,), (0,)), ((), ())), preferred_element_type=F32)


def rows_of(start, size, step=16):
    if not isinstance(start, int):
        start = pl.multiple_of(start, step)
    return pl.ds(start, size)


def block_kernel(dims, names, *all_refs):
    r = SimpleNamespace(**dict(zip(names, all_refs, strict=True)))
    nb, chan, mid, cell_count = dims
    spat = 9 * chan // nb
    temp = 3 * mid // nb
    unit = spat // 6
    quarter = chan // 4
    half = chan // 2
    h = lax.axis_index("ha")
    w = lax.axis_index("wa")
    b = lax.axis_index("batch")
    par = lax.rem(b, 2)
    bh = lax.div(b, 2)
    pos = par * (nb - 1 - bh) + (1 - par) * bh

    def at(p):
        p = lax.rem(p + 4 * nb, nb)
        upper = lax.div(p, nb // 2)
        return (1 - upper) * (2 * p) + upper * (2 * (nb - 1 - p) + 1)

    def at_group(j):
        return (lax.rem(j, 2), lax.div(j, 2))

    mine = 2 * w + h
    sibling = (1 - h, w, b)
    beside = (h, 1 - w, b)
    later_dev = (1 - h, w, lax.rem(b + h, nb))
    earlier_dev = (1 - h, w, lax.rem(b + nb - 1 + h, nb))
    tile_group = [(lax.rem(mine + d, 4), (*at_group(lax.rem(mine + d, 4)), b)) for d in (1, 2, 3)]
    across = (h, w, b + 1 - 2 * par)
    pos_b = h * 2 + par
    plane = []
    for d in (1, 2, 3):
        q = lax.rem(pos_b + d, 4)
        plane.append((q, (lax.div(q, 2), w, b - par + lax.rem(q, 2))))
    depth = nb // 2
    line = []
    for d in range(1, depth):
        q = lax.rem(bh + d, depth)
        line.append((q, (h, w, 2 * q + par)))

    def named(dev):
        return dict(ha=dev[0], wa=dev[1], batch=dev[2])

    def rc(src, dst, send, recv, dev):
        return pltpu.make_async_remote_copy(
            src_ref=src, dst_ref=dst, send_sem=send, recv_sem=recv, device_id=named(dev), device_id_type=MESH
        )

    def lc(src, dst, sem):
        return pltpu.make_async_copy(src, dst, sem)

    partners = [sibling, beside, (h, w, at(pos + 1)), (h, w, at(pos - 1)), later_dev, earlier_dev]
    partners += [dev for _, dev in tile_group + plane + line]
    barrier = pltpu.get_barrier_semaphore()
    for dev in partners:
        pl.semaphore_signal(barrier, inc=1, device_id=named(dev), device_id_type=MESH)
    pl.semaphore_wait(barrier, len(partners))

    shards = (r.first_spatial, r.first_temporal, r.second_spatial, r.second_temporal)
    whole = ((r.w1s0, r.w1s1), (r.w1t0, r.w1t1), (r.w2s0, r.w2s1), (r.w2t0, r.w2t1))
    halves = ((0, 512), (512, mid - 512))
    shared = 2 * w + h
    shared_beside = 2 * (1 - w) + h
    way = 1 - 2 * h
    ways = (way, -way)
    onward = [(h, w, at(pos + d)) for d in ways]
    steps = (nb // 2, nb // 2 - 1)
    third = temp // 3

    def taken(i, core, side):
        if i % 2 == 0:
            return 3 * unit * core + unit * side, 2 * unit
        return (1 - core) * 2 * third * side + core * third, third

    def crosses(i, core, side):
        if i % 2 == 0:
            return 3 * unit * core + 2 * unit * side, unit
        return 2 * third * side, third

    def rows_in(i, c, owner, part):
        size = spat if i % 2 == 0 else temp
        return whole[i][c].at[rows_of(owner * size + part[0], part[1]), :]

    def rows_from(i, c, part):
        c0, cw = halves[c] if i % 2 == 0 else (c * half, half)
        return shards[i].at[rows_of(part[0], part[1]), c0 : c0 + cw]

    def pieces(i):
        start, size = taken(i, h, w)
        if i % 2:
            return ((start, size),)
        return ((start, size // 2), (start + size // 2, size // 2))

    def crossing(i, work):
        if i % 2 == 0:
            work()
        else:
            pl.when(h == 0)(work)

    def own_copy(i, c):
        rows = spat if i % 2 == 0 else temp
        return lc(rows_from(i, c, (0, rows)), rows_in(i, c, b, (0, rows)), r.own_sem.at[i, c])

    def ring(i, c, k, d, s, owner, from_shard=False):
        part = pieces(i)[k]
        dst = rows_in(i, c, owner, part)
        src = rows_from(i, c, part) if from_shard else dst
        return rc(src, dst, r.ring_send.at[i, c], r.ring_recv.at[i, c, k, d, s], onward[d])

    def cross(i, c, owner, part):
        ref = rows_in(i, c, owner, part)
        return rc(ref, ref, r.sib_send.at[i, c], r.sib_recv.at[i, c], sibling)

    def over(i, c, d, s, owner, part):
        ref = rows_in(i, c, owner, part)
        return rc(ref, ref, r.over_send.at[i, c], r.over_recv.at[i, c, d, s], beside)

    def gather_start(i):
        for k in range(len(pieces(i))):
            for d in (0, 1):
                for c in (0, 1):
                    ring(i, c, k, d, 1, b, True).start()
        for c in (0, 1):
            own_copy(i, c).start()

    def owners(s):
        return [(d, at(pos - ways[d] * s)) for d in (0, 1) if s <= steps[d]]

    def gather_relay(i, s):
        def work():
            part = crosses(i, h, 1 - w)
            for d, owner in owners(s):
                for c in (0, 1):
                    over(i, c, d, s, owner, part).wait_recv()
                    cross(i, c, owner, part).start()

        crossing(i, work)

    def gather_pump(i, s):
        for k in range(len(pieces(i))):
            for d, owner in owners(s):
                for c in (0, 1):
                    ring(i, c, k, d, s, owner).wait_recv()
                    if s < steps[d]:
                        ring(i, c, k, d, s + 1, owner).start()
        for d, owner in owners(s):
            for c in (0, 1):
                crossing(i, lambda c=c, d=d, owner=owner: over(i, c, d, s, owner, crosses(i, h, w)).start())
                cross(i, c, owner, taken(i, h, w)).start()
        if s > 1:
            gather_relay(i, s - 1)

    def span(i, c, size):
        return whole[i][c].at[0 : (nb - 1) * size, :]

    def gather_finish(i):
        gather_relay(i, steps[0])

        def arrived(size):
            for c in (0, 1):
                ref = span(i, c, size)
                rc(ref, ref, r.sib_send.at[i, c], r.sib_recv.at[i, c], sibling).wait_recv()

        if i % 2 == 0:
            arrived(3 * unit)
        else:
            pl.when(h == 0)(lambda: arrived(third))
            pl.when(h == 1)(lambda: arrived(2 * third))
        for c in (0, 1):
            own_copy(i, c).wait()

    def gather_sent(i):
        def sent(size, sem):
            for c in (0, 1):
                ref = span(i, c, size)
                rc(ref, ref, sem.at[i, c], r.own_sem.at[i, c], sibling).wait_send()

        sent(taken(i, h, w)[1], r.ring_send)
        crossing(i, lambda: sent(crosses(i, h, w)[1], r.over_send))
        if i % 2 == 0:
            sent(3 * unit, r.sib_send)
        else:
            pl.when(h == 0)(lambda: sent(2 * third, r.sib_send))
            pl.when(h == 1)(lambda: sent(third, r.sib_send))

    def total(k, width, value, works=()):
        slot = k % 2
        wide = value.shape[1]
        cols = pl.ds(0, wide)
        works = list(works) + [None] * 2
        four, far = r.sum_b, r.sum_c
        four[slot, pos_b, :, cols] = value

        def phase(ref, me, group, send, recv, work):
            for _, dev in group:
                part = ref.at[slot, me, :, cols]
                rc(part, part, send.at[k], recv.at[k], dev).start()
            if work:
                work()
            ref = ref.at[slot, 0 : len(group), :, cols]
            every = rc(ref, ref, send.at[k], recv.at[k], sibling)
            every.wait_recv()
            return every

        first = phase(four, pos_b, plane, r.sb_send, r.sb_recv, works[0])
        far[slot, bh, :, cols] = (four[slot, 0, :, cols] + four[slot, 1, :, cols]) + (
            four[slot, 2, :, cols] + four[slot, 3, :, cols]
        )
        second = phase(far, bh, line, r.sc_send, r.sc_recv, works[1])
        result = far[slot, 0, :, cols]
        for q in range(1, depth):
            result = result + far[slot, q, :, cols]
        first.wait_send()
        second.wait_send()
        if wide == width:
            return result
        return jnp.concatenate([result[2 * n : 2 * n + 2] for n in range(width // wide)], axis=1)

    def chunk(ref, i, base=0, width=None):
        cols = slice(None) if width is None else pl.ds(0, width)
        value = ref[rows_of(base + i * CHUNK, CHUNK), cols]
        return value.astype(F32).reshape(2, CELL, value.shape[-1])

    def put(ref, i, value, base=0, width=None):
        cols = slice(None) if width is None else pl.ds(0, width)
        ref[rows_of(base + i * CHUNK, CHUNK), cols] = value.reshape(CHUNK, value.shape[-1]).astype(ref.dtype)

    def keep(i):
        inside = jnp.where(lax.rem(i, 4) == 3, 0.0, 1.0).astype(F32)
        first = lax.broadcasted_iota(jnp.int32, (2, 1, 1), 0) == 0
        return jnp.where(first, 1.0, inside)

    def packed(one, two, width):
        rows = jnp.concatenate([jnp.sum(v, axis=0, keepdims=True) for v in (one, two)], axis=0)
        wide = 384 if width == mid else 128
        parts = [rows[:, n * wide : (n + 1) * wide] for n in range(width // wide)]
        return jnp.concatenate((parts + parts[-1:])[0:4], axis=0)

    def moments(ref, width):
        def body(i, carry):
            v = chunk(ref, i)
            m = v * keep(i)
            return (carry[0] + m[0] + m[1], carry[1] + m[0] * v[0] + m[1] * v[1])

        zero = jnp.zeros((CELL, width), F32)
        return loop(CHUNKS, body, (zero, zero))

    def prepare(n, sums, width):
        tile = r.tile_mid if width == mid else r.tile_out
        n2 = n // 2
        gain = r.param[2 * n : 2 * n + 1, 0:width]
        bias = r.param[2 * n + 1 : 2 * n + 2, 0:width]
        mean = sums[0:1] / cell_count
        inv = lax.rsqrt(sums[1:2] / cell_count - mean * mean + epsilon)
        scale = inv * gain
        shift = bias - mean * scale
        for k, v in enumerate((scale, shift, inv, mean * inv)):
            tile[n2, k] = jnp.broadcast_to(v, (CELL, width))

    def tiles(n, width):
        tile = r.tile_mid if width == mid else r.tile_out
        return [tile[n // 2, k][None] for k in range(4)]

    def fill(ref_a, ref_b, value_of, width):
        pads(ref_a, ref_b, width)

        def body(i, before):
            v = value_of(i)
            put(ref_a, i, v, MAIN)
            pair = jnp.concatenate([before[None], v[0:1]], axis=0)
            put(ref_b, i, pair, MAIN - CHUNK)
            return v[1]

        loop(CHUNKS, body, jnp.zeros((CELL, width), F32))

    def activated(src, n, width):
        def value(i):
            scale, shift, _, _ = tiles(n, width)
            y = chunk(src, i) * scale + shift
            return y * sigmoid(y) * keep(i)

        return value

    def taps(ref_a, ref_b, k, size=ROWS):
        r0 = MAIN - 8 * CELL + 8 * CELL * k
        return (
            ref_b[rows_of(r0 - CHUNK, size), :],
            ref_a[rows_of(r0, size), :],
            ref_b[rows_of(r0, size), :],
        )

    def conv(ref_a, ref_b, weight, out, pump=None):
        for n, (c0, cw) in enumerate(halves):

            def body(a, _, c0=c0, cw=cw, n=n):
                x = taps(ref_a, ref_b, a)
                acc = nn(jnp.concatenate(x, axis=1), weight[n][rows_of(a * 3 * chan, 3 * chan), :])

                @pl.when(a == 0)
                def _():
                    out[:, c0 : c0 + cw] = acc

                @pl.when(a > 0)
                def _():
                    out[:, c0 : c0 + cw] += acc

                if pump is not None:
                    pump(n * 3 + a)
                return 0

            lax.fori_loop(0, 3, body, 0)

    def conv_back(ref_a, ref_b, weight, out, pump=None):
        def body(k, _):
            e = taps(ref_a, ref_b, k)
            acc = None
            for j in range(3):
                tap = 8 - 3 * k - j
                for n, (c0, cw) in enumerate(halves):
                    term = nt(e[j][:, c0 : c0 + cw], weight[n][rows_of(tap * chan, chan), :])
                    acc = term if acc is None else acc + term

            @pl.when(k == 0)
            def _():
                out[:, 0:chan] = acc

            @pl.when(k > 0)
            def _():
                out[:, 0:chan] += acc

            if pump is not None:
                pump(k)
            return 0

        lax.fori_loop(0, 3, body, 0)

    def send_frames(k):
        down, up = r.down, r.up
        count = ROWS // CELL
        for c in range(chan // 128):
            lanes = pl.ds(128 * c, 128)
            r.halo_out[0, :, lanes] = down[c, pl.ds(2 * CELL - 1, count, stride=CELL), :]
            r.halo_out[1, :, lanes] = up[c, pl.ds(0, count, stride=CELL), :]
        copies = []
        for n, dev in ((0, later_dev), (1, earlier_dev)):
            copies.append(
                rc(r.halo_out.at[n], r.halo_in.at[k, n], r.halo_send.at[k, n], r.halo_recv.at[k, n], dev)
            )
            copies[-1].start()
        return copies

    def take_frames(k, copies):
        down, up = r.down, r.up
        count = ROWS // CELL
        for copy in copies:
            copy.wait()
        at_start = jnp.logical_and(h == 0, b == 0)
        at_end = jnp.logical_and(h == 1, b == nb - 1)
        for c in range(chan // 128):
            lanes = pl.ds(128 * c, 128)
            before = r.halo_in[k, 0, :, lanes]
            after = r.halo_in[k, 1, :, lanes]
            down[c, pl.ds(CELL - 1, count, stride=CELL), :] = jnp.where(at_start, 0.0, before)
            up[c, pl.ds(CELL, count, stride=CELL), :] = jnp.where(at_end, 0.0, after)

    def by_lanes(ref, rows):
        return jnp.concatenate([ref[c, rows, :] for c in range(chan // 128)], axis=1)

    def put_lanes(ref, rows, value):
        for c in range(chan // 128):
            ref[c, rows, :] = value[:, 128 * c : 128 * c + 128]

    def shifted(i):
        before = by_lanes(r.down, rows_of(i * CHUNK, CHUNK + CELL))[CELL - 1 : CELL - 1 + CHUNK]
        after = by_lanes(r.up, rows_of(i * CHUNK, CHUNK + CELL))[1 : 1 + CHUNK]
        gate = r.gate[...][None]
        return (before.reshape(2, CELL, chan) * gate, after.reshape(2, CELL, chan))

    def both_halves(weight, start, size):
        return jnp.concatenate([part[start : start + size, :] for part in weight], axis=1)

    def temporal(k, v, weight, out, works=()):
        works = list(works) + [None] * 2
        put_lanes(r.down, pl.ds(CELL, ROWS), nn(v[...], both_halves(weight, 0, mid)))
        y2 = nn(v[...], both_halves(weight, 2 * mid, mid))
        y2 = (y2.reshape(ROWS // CELL, CELL, chan) * r.gate[...][None]).reshape(ROWS, chan)
        put_lanes(r.up, pl.ds(0, ROWS), y2)
        copies = send_frames(k)
        out[...] = nn(v[...], both_halves(weight, mid, mid))
        if works[0]:
            works[0]()
        take_frames(k, copies)

        def body(i, carry):
            before, after = shifted(i)
            value = chunk(out, i) + before + after
            put(out, i, value)
            m = value * keep(i)
            return (carry[0] + m[0] + m[1], carry[1] + m[0] * value[0] + m[1] * value[1])

        zero = jnp.zeros((CELL, chan), F32)
        return loop(CHUNKS, body, (zero, zero))

    def put_e(tap, i, e):
        for c in (0, 1):
            r.e3[c, tap, rows_of(i * CHUNK, CHUNK), :] = e[:, c * half : (c + 1) * half]

    def temporal_back(k, weight, works=()):
        works = list(works) + [None] * 2
        copies = send_frames(k)
        e3 = r.e3

        def e_tap(n):
            return jnp.concatenate([e3[0, n], e3[1, n]], axis=1)

        for c0, cw in ((0, 512), (512, mid - 512)):
            r.grad_mid[:, c0 : c0 + cw] = nt(e_tap(1), both_halves(weight, mid + c0, cw))
        if works[0]:
            works[0]()
        take_frames(k, copies)

        def body(i, _):
            before, after = shifted(i)
            put_e(0, i, after.reshape(CHUNK, chan).astype(BF16))
            put_e(2, i, before.reshape(CHUNK, chan).astype(BF16))
            return 0

        loop(CHUNKS, body, 0)
        share = share_e3(k)
        for c0, cw in ((0, 512), (512, mid - 512)):
            r.grad_mid[:, c0 : c0 + cw] += nt(e_tap(0), both_halves(weight, c0, cw)) + nt(
                e_tap(2), both_halves(weight, 2 * mid + c0, cw)
            )
        return share

    def share(k, src, dst):
        copy = rc(src, dst, r.share_send.at[k], r.share_recv.at[k], sibling)
        copy.start()
        return copy

    outs = ((r.out1s0, r.out1s1), r.out1t, (r.out2s0, r.out2s1), r.out2t)

    e_all = (r.e_all0, r.e_all1)

    def e_part(n, slot):
        return e_all[n].at[slot * ROWS : (slot + 1) * ROWS, :]

    def e_copies(k, n):
        send, near, over = r.e_send.at[k, n], r.e_recv.at[k, n, 0], r.e_recv.at[k, n, 1]
        return [
            rc(e_part(n, 0), e_part(n, 1), send, near, sibling),
            rc(e_part(n, 0), e_part(n, 2), send, over, beside),
            rc(e_part(n, 2), e_part(n, 3), send, near, sibling),
        ]

    def share_e(k):
        for n in (0, 1):
            near, over, _ = e_copies(k, n)
            over.start()
            near.start()

    def share_e_on(k, n):
        _, over, far = e_copies(k, n)
        over.wait_recv()
        far.start()

    def share_e_wait(k, n):
        both = e_all[n].at[0 : 2 * ROWS, :]
        rc(both, both, r.e_send.at[k, n], r.e_recv.at[k, n, 0], sibling).wait_recv()
        three = e_all[n].at[0 : 3 * ROWS, :]
        rc(three, three, r.e_send.at[k, n], r.e_recv.at[k, n, 0], sibling).wait_send()

    def share_x(k, xa, xq):
        main = pl.ds(MAIN, ROWS)
        for n, dev in enumerate((sibling, beside, (1 - h, 1 - w, b))):
            lanes = rows_of((2 * dev[1] + dev[0]) * quarter, quarter, 128)
            rc(xa.at[main, lanes], xq.at[n, 0, main, :], r.xq_send.at[k], r.xq_recv.at[k], dev).start()
        all_three = xq.at[:, 0, main, :]
        return rc(all_three, all_three, r.xq_send.at[k], r.xq_recv.at[k], sibling)

    def pads(ref_a, ref_b, width):
        ref_a[0:MAIN, :] = jnp.zeros((MAIN, width), BF16)
        ref_a[MAIN + ROWS : PADDED, :] = jnp.zeros((PADDED - MAIN - ROWS, width), BF16)
        ref_b[0 : MAIN - CHUNK, :] = jnp.zeros((MAIN - CHUNK, width), BF16)
        ref_b[MAIN - CHUNK + ROWS : PADDED, :] = jnp.zeros((PADDED - MAIN + CHUNK - ROWS, width), BF16)

    def spread_x(xq):
        for n in range(3):
            pads(xq.at[n, 0], xq.at[n, 1], quarter)

        def body(i, before):
            after = []
            for n in range(3):
                v = chunk(xq.at[n, 0], i, MAIN)
                put(xq.at[n, 1], i, jnp.concatenate([before[n][None], v[0:1]], axis=0), MAIN - CHUNK)
                after.append(v[1])
            return tuple(after)

        loop(CHUNKS, body, (jnp.zeros((CELL, quarter), F32),) * 3)

    def share_e3(k):
        return share(
            k - 2, r.e3.at[1 - h], r.sib_e3
        )

    def line_row(place):
        return quarter * place + 64 * jnp.where(place > shared, 1, 0)

    def grad_row(tap, side):
        split = 2 * shared + 1
        owner = jnp.where(tap == split, 2 * shared + side, tap - jnp.where(tap > split, 1, 0))
        row = line_row(lax.div(owner, 2)) + jnp.where(tap == split, quarter, 64 * side)
        return 576 * lax.rem(owner, 2) + row

    spare = whole[2]

    def gq(i, row, size):
        return rows_of((mid if i == 0 else 0) + row, size, 64)

    def inbox(i, row, size):
        return rows_of(2 * mid + (mid if i == 0 else 0) + row, size, 64)

    def transpose_x(a, xa, xb, xq, near, far, row):
        lanes = rows_of(shared * quarter, quarter, 128)
        r0 = MAIN - 8 * CELL + 8 * CELL * a
        for j, (c, start) in enumerate(((1, r0 - CHUNK), (0, r0), (1, r0))):
            rows = rows_of(start, ROWS)
            own = (xb if c else xa)[rows, lanes]
            both = jnp.concatenate([own, xq[0, c, rows, :]], axis=0)
            near[rows_of(row + j * quarter, quarter), 0 : 2 * ROWS] = both.T
            both = jnp.concatenate([xq[1, c, rows, :], xq[2, c, rows, :]], axis=0)
            far[rows_of(row + j * quarter, quarter), 0 : 2 * ROWS] = both.T

    def spatial_part(i, near, far, row, tap, n):
        rows = rows_of(row, 3 * quarter)
        acc = nn(near[rows, :], e_all[n][0 : 2 * ROWS, :])
        acc += nn(far[rows, :], e_all[n][2 * ROWS : 4 * ROWS, :])
        acc = acc.astype(BF16)
        for j in range(6):
            spare[n][gq(i, grad_row(tap + j // 2, j % 2), 64), :] = acc[64 * j : 64 * j + 64]

    def transposes(xa, xb, xq, near, far):
        def body(a, _):
            transpose_x(a, xa, xb, xq, near, far, a * 3 * quarter)
            return 0

        lax.fori_loop(0, 3, body, 0)

    def spatial_half(i, near, far, n):
        def body(a, _):
            spatial_part(i, near, far, a * 3 * quarter, 3 * a, n)
            return 0

        lax.fori_loop(0, 3, body, 0)

    def transpose_v(v, sv):
        for c in range(mid // 128):
            lanes = pl.ds(128 * c, 128)
            turned = jnp.concatenate([v[:, lanes], sv[:, lanes]], axis=0).T
            for row in (0, 64):
                ref = r.ea if 128 * c + row < mid // 2 else r.eb
                at_row = (128 * c + row) % (mid // 2)
                ref[at_row : at_row + 64, 0 : 2 * ROWS] = turned[row : row + 64]

    def temporal_grad(i, first, count):
        taps_of = [jnp.concatenate([r.e3[h, k], r.sib_e3[k]], axis=0) for k in range(first, first + count)]
        e = jnp.concatenate(taps_of, axis=1)
        whole_tap = mid // third
        for top in range(0, whole_tap, whole_tap // 2):
            acc = nn((r.eb if top else r.ea)[0 : mid // 2, 0 : 2 * ROWS], e).astype(BF16)
            for k in range(count):
                for n in range(whole_tap // 2):
                    owner, part = divmod((first + k) * whole_tap + top + n, 3)
                    row = (owner % 2) * (depth * temp) + owner // 2 * temp + part * third
                    whole[i][0][row : row + third, :] = acc[n * third : n * third + third, k * half : (k + 1) * half]

    def parts_of(i):
        return (0, 1) if i % 2 == 0 else (0,)

    line_size = 576

    def to_y(i, n, side):
        if i % 2 == 0:
            return spare[n].at[gq(i, line_size * side, line_size), :]
        return whole[i][0].at[rows_of(depth * temp * side, depth * temp), :]

    def y_box(i, n):
        if i % 2 == 0:
            return spare[n].at[inbox(i, 0, line_size), :]
        return whole[i][1].at[0 : depth * temp, :]

    def block_of(i, n, place, size):
        if i % 2 == 0:
            return spare[n].at[gq(i, line_size * par + line_row(place), size), :]
        return whole[i][0].at[rows_of(depth * temp * par + place * temp, temp), :]

    def z_box(i, n, slot, size):
        if i % 2 == 0:
            return spare[n].at[inbox(i, line_size + slot * (line_size // 3), size), :]
        return whole[i][1].at[(depth + slot) * temp : (depth + slot + 1) * temp, :]

    def sized(i, place, work):
        if i % 2:
            work(temp)
        else:
            pl.when(place != shared)(lambda: work(quarter))
            pl.when(place == shared)(lambda: work(quarter + 64))

    def t_inbox(i, n):
        return whole[i][1].at[n * temp : (n + 1) * temp, :]

    def add_into(dst, parts, step):
        rows, cols = dst.shape

        def body(n, _):
            at_rows = rows_of(n * step, step)
            value = dst[at_rows, :].astype(F32)
            for part in parts:
                value = value + part[at_rows, :].astype(F32)
            dst[at_rows, :] = value.astype(BF16)
            return 0

        lax.fori_loop(0, rows // step, body, 0)

    def y_copy(i, n):
        return rc(to_y(i, n, 1 - par), y_box(i, n), r.y_send.at[i, n], r.y_recv.at[i, n], across)

    def z_copy(i, n, d, size):
        place = lax.rem(bh + d, depth)
        dev = (h, w, 2 * place + par)
        src, dst = block_of(i, n, place, size), z_box(i, n, 3 - d, size)
        return rc(src, dst, r.z_send.at[i, n], r.z_recv.at[i, n], dev)

    def step_of(i):
        return 32 if i % 2 == 0 else 48

    def reduce_start(i, n):
        y_copy(i, n).start()

    def reduce_middle(i, n):
        y_copy(i, n).wait()
        add_into(to_y(i, n, par), [y_box(i, n)], step_of(i))
        for d in (1, 2, 3):
            sized(i, lax.rem(bh + d, depth), lambda size, d=d: z_copy(i, n, d, size).start())

    def final_part(i, n, side, core):
        place = 2 * side + core
        start = quarter * place - 64 * b + 512 * jnp.where(b > 2 * place, 1, 0)
        return outs[i][n].at[rows_of(start, quarter, 64), :]

    def extra_part(i, n):
        return outs[i][n].at[rows_of(512 * (1 - par), 64, 64), :]

    def final_copies(i, n):
        if i % 2:
            src = block_of(i, n, bh, temp)
            part = outs[i].at[h]
            return lc(src, part, r.out_sem.at[i, 0, 0]), [
                (src, part, sibling, r.cast_send.at[i, 0, 0], r.cast_recv.at[i, 0, 0])
            ]
        src = block_of(i, n, bh, quarter)
        part = final_part(i, n, w, h)
        sends = [
            (src, part, dev, r.cast_send.at[i, n, d], r.cast_recv.at[i, n, d]) for d, dev in enumerate((beside, sibling))
        ]
        return lc(src, part, r.out_sem.at[i, n, 0]), sends

    def extra_copies(i, n):
        src = spare[n].at[gq(i, line_size * par + line_row(bh) + quarter, 64), :]
        part = extra_part(i, n)
        sends = [
            (src, part, dev, r.cast_send.at[i, n, 3 + d], r.cast_recv.at[i, n, 3 + d])
            for d, dev in enumerate((beside, sibling))
        ]
        return lc(src, part, r.out_sem.at[i, n, 1]), sends

    def begin(copies):
        local, sends = copies
        for src, part, dev, one, two in sends:
            rc(src, part, one, two, dev).start()
        local.start()

    def credit(n):
        pl.semaphore_signal(r.credit.at[n], inc=1, device_id=named(beside), device_id_type=MESH)

    def credited(n):
        pl.semaphore_wait(r.credit.at[n], 1)

    def beside_copy(i):
        return rc(block_of(i, 0, bh, temp), t_inbox(i, 7), r.fin_send.at[i], r.fin_recv.at[i], beside)

    def z_span(i, n, rows):
        return to_y(i, n, 0).at[0:rows, :]

    def reduce_last(i, n):
        def add(size):
            ref = z_span(i, n, 3 * size)
            rc(ref, ref, r.z_send.at[i, n], r.z_recv.at[i, n], across).wait_recv()
            add_into(block_of(i, n, bh, size), [z_box(i, n, slot, size) for slot in range(3)], step_of(i))

        sized(i, bh, add)
        if i % 2:
            credited(i // 2)
            beside_copy(i).start()
            return
        begin(final_copies(i, n))
        pl.when(bh == shared)(lambda: begin(extra_copies(i, n)))

    def reduce_out(i):
        beside_copy(i).wait()
        add_into(block_of(i, 0, bh, temp), [t_inbox(i, 7)], 48)
        begin(final_copies(i, 0))

    def final_on(i, n):
        def move(part, d):
            rc(part, part, r.cast_send.at[i, n, d], r.cast_recv.at[i, n, d], beside).wait_recv()
            rc(part, part, r.cast_send.at[i, n, d + 2], r.cast_recv.at[i, n, d + 2], sibling).start()

        move(final_part(i, n, 1 - w, h), 0)
        pl.when(bh == shared_beside)(lambda: move(extra_part(i, n), 3))

    def reduce_wait(i, n):
        local, sends = final_copies(i, n)
        local.wait()

        def sent(rows):
            ref = z_span(i, n, rows)
            rc(ref, ref, r.z_send.at[i, n], r.z_recv.at[i, n], across).wait_send()

        if i % 2:
            sent(3 * temp)
        else:
            pl.when(bh == shared)(lambda: sent(3 * quarter))
            pl.when(bh != shared)(lambda: sent(3 * quarter + 64))
        if i % 2:
            src, part, dev, one, two = sends[0]
            rc(src, outs[i].at[1 - h], one, two, dev).wait()
            return
        for src, part, dev, one, two in sends:
            rc(src, part, one, two, dev).wait_send()

        def far(part, d):
            return rc(part, part, r.cast_send.at[i, n, d], r.cast_recv.at[i, n, d], sibling)

        far(final_part(i, n, w, 1 - h), 1).wait_recv()
        far(final_part(i, n, 1 - w, h), 2).wait_send()
        far(final_part(i, n, 1 - w, 1 - h), 2).wait_recv()
        local, sends = extra_copies(i, n)

        @pl.when(bh == shared)
        def _():
            local.wait()
            for src, part, dev, one, two in sends:
                rc(src, part, one, two, dev).wait_send()

        pl.when(bh == shared_beside)(lambda: far(extra_part(i, n), 5).wait_send())
        pl.when(bh == 2 * w + 1 - h)(lambda: far(extra_part(i, n), 4).wait_recv())
        pl.when(bh == 2 * (1 - w) + 1 - h)(lambda: far(extra_part(i, n), 5).wait_recv())

    def tile_of(ref, jh, jw):
        return ref.at[rows_of(jh * 4, 4, 4), rows_of(jw * 32, 32), :]

    def tile_own(src, dst, n):
        return lc(src.at[mine], tile_of(dst, h, w), r.tile_own.at[n])

    def tiles_start(src, dst, n):
        for j, dev in tile_group:
            rc(src.at[j], tile_of(dst, h, w), r.tile_send.at[n], r.tile_recv.at[n], dev).start()
        tile_own(src, dst, n).start()

    def tiles_wait(src, dst, n):
        three = src.at[0:3]
        rc(three, three, r.tile_send.at[n], r.tile_recv.at[n], sibling).wait()
        tile_own(src, dst, n).wait()

    xg, cg = r.x_grid, r.cot_grid
    tiles_start(r.x_tiles, xg, 0)
    gather_start(0)
    r.param[...] = total(0, mid, r.param_in[...])
    tiles_wait(r.x_tiles, xg, 0)

    def grid_chunk(ref, i):
        v = ref[lax.div(i, 4), rows_of(lax.rem(i, 4) * CHUNK, CHUNK), :]
        return v.astype(F32).reshape(2, CELL, chan)

    fill(r.xa, r.xb, lambda i: grid_chunk(xg, i), chan)

    last = steps[0]
    for step in range(1, last):
        gather_pump(0, step)
    gather_start(1)
    gather_start(2)
    gather_pump(0, last)
    gather_finish(0)

    def first_pump(n):
        pl.when(n == 0)(lambda: gather_pump(1, 1))
        pl.when(n == 2)(lambda: gather_pump(1, 2))
        pl.when(n == 3)(lambda: gather_pump(2, 1))
        pl.when(n == 5)(lambda: gather_pump(1, 3))

    conv(r.xa, r.xb, whole[0], r.mid1, first_pump)
    sums = total(
        1, mid, packed(*moments(r.mid1, mid), mid), [lambda: gather_pump(1, last), lambda: gather_pump(2, 2)]
    )
    prepare(0, sums, mid)

    def hidden(src, n, dst):
        value = activated(src, n, mid)

        def body(i, _):
            put(dst, i, value(i))
            return 0

        loop(CHUNKS, body, 0)

    hidden(r.mid1, 0, r.v1)
    gather_finish(1)
    stats = temporal(0, r.v1, whole[1], r.time1, [lambda: gather_pump(2, 3)])
    sums = total(
        2, chan, packed(*stats, chan), [lambda: gather_start(3), lambda: gather_pump(2, last)]
    )
    prepare(1, sums, chan)
    fill(r.aa, r.ab, activated(r.time1, 1, chan), chan)
    gather_finish(2)
    tiles_start(r.cot_tiles, cg, 1)

    def second_pump(n):
        for step in range(1, last):
            pl.when(n == 2 * step - 1)(lambda step=step: gather_pump(3, step))

    conv(r.aa, r.ab, whole[2], r.mid2, second_pump)

    def last_piece():
        gather_pump(3, last)
        gather_finish(3)

    sums = total(3, mid, packed(*moments(r.mid2, mid), mid), [last_piece])
    prepare(2, sums, mid)
    hidden(r.mid2, 2, r.v2)
    stats = temporal(1, r.v2, whole[3], r.time2)
    shared_xq2 = share_x(0, r.aa, r.xq2)
    shared_xq1 = share_x(1, r.xa, r.xq1)
    for i in range(4):
        gather_sent(i)
    share_v2 = share(4, r.v2, r.sib_v)
    sums = total(4, chan, packed(*stats, chan), [lambda: tiles_wait(r.cot_tiles, cg, 1)])
    prepare(3, sums, chan)

    out_grid = r.out_grid

    def grid_put(ref, i, v):
        ref[lax.div(i, 4), rows_of(lax.rem(i, 4) * CHUNK, CHUNK), :] = v.reshape(CHUNK, chan).astype(ref.dtype)

    def slope(y, s):
        return s * (1.0 + y * (1.0 - s))

    def pre_body(i, carry):
        scale, shift, inv, offset = tiles(3, chan)
        v = chunk(r.time2, i)
        y = v * scale + shift + chunk(r.xa, i, MAIN)
        s = sigmoid(y)
        m = keep(i)
        grid_put(out_grid, i, y * s * m)
        d = grid_chunk(cg, i) * m * slope(y, s)
        put(r.grad_pre, i, d)
        t = d * (v * inv - offset)
        return (carry[0] + d[0] + d[1], carry[1] + t[0] + t[1])

    zero_out = jnp.zeros((CELL, chan), F32)
    zero_mid = jnp.zeros((CELL, mid), F32)
    out_grid[HGT] = jnp.zeros((8 * CELL, chan), BF16)
    gg = loop(CHUNKS, pre_body, (zero_out, zero_out))

    def send_tiles(src, dst, n):
        for j, dev in tile_group:
            jh, jw = at_group(j)
            rc(tile_of(src, jh, jw), dst.at[mine], r.tile_send.at[n], r.tile_recv.at[n], dev).start()
        lc(tile_of(src, h, w), dst.at[mine], r.tile_own.at[n]).start()

    def sent_tiles(src, dst, n):
        three = dst.at[0:3]
        rc(three, three, r.tile_send.at[n], r.tile_recv.at[n], sibling).wait()
        lc(tile_of(src, h, w), dst.at[mine], r.tile_own.at[n]).wait()

    send_tiles(out_grid, r.block_out, 2)

    def norm_back(n, sums, width):
        r.norm_part[0, 2 * n : 2 * n + 1, 0:width] = sums[1:2]
        r.norm_part[0, 2 * n + 1 : 2 * n + 2, 0:width] = sums[0:1]
        back = r.back
        back[0, :, 0:width] = jnp.broadcast_to(sums[0:1] / cell_count, (CELL, width))
        back[1, :, 0:width] = jnp.broadcast_to(sums[1:2] / cell_count, (CELL, width))

    def through_norm(n, src, grad, i, width):
        scale, _, inv, offset = tiles(n, width)
        xhat = chunk(src, i) * inv - offset
        bias_part = r.back[0, :, 0:width][None]
        gain_part = r.back[1, :, 0:width][None]
        return scale * (chunk(grad, i, 0, width) - bias_part - xhat * gain_part) * keep(i)

    def through_act(n, src, grad, width):
        def body(i, carry):
            scale, shift, inv, offset = tiles(n, width)
            v = chunk(src, i)
            y = v * scale + shift
            s = sigmoid(y)
            d = chunk(grad, i, 0, width) * keep(i) * slope(y, s)
            put(grad, i, d, 0, width)
            t = d * (v * inv - offset)
            return (carry[0] + d[0] + d[1], carry[1] + t[0] + t[1])

        zero = jnp.zeros((CELL, width), F32)
        return loop(CHUNKS, body, (zero, zero))

    def to_frames(n, src, grad):
        def body(i, _):
            e = through_norm(n, src, grad, i, chan).astype(BF16)
            ef = e.astype(F32)
            put_e(1, i, e.reshape(CHUNK, chan))
            put_lanes(r.down, rows_of(i * CHUNK + CELL, CHUNK, CELL), ef.reshape(CHUNK, chan))
            put_lanes(r.up, rows_of(i * CHUNK, CHUNK), (ef * r.gate[...][None]).reshape(CHUNK, chan))
            return 0

        loop(CHUNKS, body, 0)

    near, far = r.xt, r.xt2

    def spread():
        shared_xq2.wait()
        spread_x(r.xq2)
        shared_xq1.wait()
        spread_x(r.xq1)

    sums = total(5, chan, packed(*gg, chan), [spread, lambda: transposes(r.aa, r.ab, r.xq2, near, far)])
    norm_back(3, sums, chan)
    to_frames(3, r.time2, r.grad_pre)
    shared_e3 = temporal_back(2, whole[3])
    credit(1)
    gg = through_act(2, r.mid2, r.grad_mid, mid)
    shared_e3.wait()
    share_v2.wait()
    def temporal_grads(i, v):
        def first():
            transpose_v(v, r.sib_v)
            temporal_grad(i, 0, 2)

        return [first, lambda: temporal_grad(i, 2, 1)]

    sums = total(6, mid, packed(*gg, mid), temporal_grads(3, r.v2))
    reduce_start(3, 0)
    norm_back(2, sums, mid)

    def fill_e(n, src):
        def value(i):
            v = through_norm(n, src, r.grad_mid, i, mid)
            for part, (c0, cw) in zip(e_all, halves):
                put(part, i, v[:, :, c0 : c0 + cw])
            return v

        fill(r.ea, r.eb, value, mid)

    fill_e(2, r.mid2)
    share_e(0)
    conv_back(r.ea, r.eb, whole[2], r.grad_mid)
    gg = through_act(1, r.time1, r.grad_mid, chan)

    def first_half():
        share_e_wait(0, 0)
        spatial_half(2, near, far, 0)

    sums = total(7, chan, packed(*gg, chan), [lambda: share_e_on(0, 0), first_half])
    reduce_start(2, 0)
    share_v1 = share(5, r.v1, r.sib_v)
    norm_back(1, sums, chan)
    to_frames(1, r.time1, r.grad_mid)
    reduce_middle(3, 0)
    share_e_on(0, 1)

    def second_half():
        share_e_wait(0, 1)
        spatial_half(2, near, far, 1)
        credit(2)
        reduce_start(2, 1)

    shared_e3 = temporal_back(3, whole[1], [second_half])
    credit(0)
    reduce_middle(2, 0)
    gg = through_act(0, r.mid1, r.grad_mid, mid)
    shared_e3.wait()
    share_v1.wait()
    sums = total(8, mid, packed(*gg, mid), temporal_grads(1, r.v1))
    reduce_start(1, 0)
    reduce_middle(2, 1)
    norm_back(0, sums, mid)
    fill_e(0, r.mid1)
    credited(2)
    share_e(1)
    reduce_last(3, 0)
    transposes(r.xa, r.xb, r.xq1, near, far)
    share_e_on(1, 0)
    reduce_out(3)
    sent_tiles(out_grid, r.block_out, 2)
    share_e_wait(1, 0)
    spatial_half(0, near, far, 0)
    reduce_start(0, 0)
    reduce_middle(1, 0)

    def pass_on(k):
        pl.when(k == 2)(lambda: share_e_on(1, 1))

    conv_back(r.ea, r.eb, whole[0], r.grad_mid, pass_on)
    share_e_wait(1, 1)
    spatial_half(0, near, far, 1)
    reduce_start(0, 1)
    reduce_middle(0, 0)

    norm_copy = rc(r.norm_part.at[0], r.norm_part.at[1], r.norm_sem.at[0], r.norm_sem.at[1], beside)
    norm_copy.start()

    def last_body(i, _):
        grid_put(out_grid, i, (chunk(r.grad_mid, i, 0, chan) + chunk(r.grad_pre, i)) * keep(i))
        return 0

    loop(CHUNKS, last_body, 0)
    send_tiles(out_grid, r.grad_input, 3)
    for n in (0, 1):
        reduce_last(2, n)
    reduce_last(1, 0)
    for n in (0, 1):
        final_on(2, n)
    reduce_out(1)
    reduce_last(0, 0)
    norm_copy.wait()
    r.norm_grads[...] = r.norm_part[0] + r.norm_part[1]
    reduce_middle(0, 1)
    final_on(0, 0)
    sent_tiles(out_grid, r.grad_input, 3)
    for n in (0, 1):
        reduce_wait(2, n)
    reduce_wait(3, 0)
    reduce_wait(1, 0)
    reduce_last(0, 1)
    final_on(0, 1)
    for n in (0, 1):
        reduce_wait(0, n)


def per_device_fast(nb, *args):
    (
        inputs,
        starts,
        first_spatial,
        first_mid_gain,
        first_mid_bias,
        first_temporal,
        first_out_gain,
        first_out_bias,
        second_spatial,
        second_mid_gain,
        second_mid_bias,
        second_temporal,
        second_out_gain,
        second_out_bias,
        cotangent,
    ) = args
    micro, frames, side, _, chan = inputs.shape
    mid = first_spatial.shape[1]
    spat, temp = first_spatial.shape[0], first_temporal.shape[0]
    h, w, b = (lax.axis_index(name) for name in ("ha", "wa", "batch"))
    few = frames // 2
    offsets = jnp.arange(side)
    valid = (h * side + offsets < HGT)[:, None] & (w * side + offsets < HGT)[None, :]

    def tiles(array):
        array = array * valid.astype(BF16)[None, None, :, :, None]
        array = array.reshape(micro, 2, few, side, side, chan).transpose(0, 1, 3, 4, 2, 5)
        return array.reshape(4, side, side * few, chan)

    def untiled(array):
        array = array.reshape(micro, 2, side, side, few, chan).transpose(0, 1, 4, 2, 3, 5)
        return array.reshape(micro, frames, side, side, chan).astype(F32)

    gate = (1 - lax.dynamic_slice(starts, (w, h * few), (1, few))).astype(F32)
    gate = jnp.broadcast_to(gate.reshape(few, 1), (few, chan))
    here = jnp.where(h == 0, 1.0, 0.0)

    def placed(shard):
        row = jnp.zeros((mid,), F32)
        return lax.dynamic_update_slice(row, shard.astype(F32) * here, (b * shard.shape[0],))

    param = jnp.stack(
        [
            placed(v)
            for v in (
                first_mid_gain,
                first_mid_bias,
                first_out_gain,
                first_out_bias,
                second_mid_gain,
                second_mid_bias,
                second_out_gain,
                second_out_bias,
            )
        ]
    )
    half = chan // 2
    few_rows = ROWS // CELL

    inputs_of = dict(
        x_tiles=(tiles(inputs), pl.ANY),
        cot_tiles=(tiles(cotangent), pl.ANY),
        gate=(gate, pltpu.VMEM),
        param_in=(param, pltpu.VMEM),
        first_spatial=(first_spatial, pl.ANY),
        first_temporal=(first_temporal, pl.ANY),
        second_spatial=(second_spatial, pl.ANY),
        second_temporal=(second_temporal, pl.ANY),
    )
    outputs_of = dict(
        block_out=((4, side, side * CELL, chan), BF16, pl.ANY),
        grad_input=((4, side, side * CELL, chan), BF16, pl.ANY),
        norm_grads=((8, mid), F32, pltpu.VMEM),
        out1s0=((spat, 512), BF16, pl.ANY),
        out1s1=((spat, mid - 512), BF16, pl.ANY),
        out1t=((2, temp, half), BF16, pl.ANY),
        out2s0=((spat, 512), BF16, pl.ANY),
        out2s1=((spat, mid - 512), BF16, pl.ANY),
        out2t=((2, temp, half), BF16, pl.ANY),
    )
    dma = pltpu.SemaphoreType.DMA
    scratch_of = dict(
        w1s0=pltpu.VMEM((9 * chan, 512), BF16),
        w1s1=pltpu.VMEM((9 * chan, mid - 512), BF16),
        w1t0=pltpu.VMEM((3 * mid, half), BF16),
        w1t1=pltpu.VMEM((3 * mid, half), BF16),
        w2s0=pltpu.VMEM((9 * chan, 512), BF16),
        w2s1=pltpu.VMEM((9 * chan, mid - 512), BF16),
        w2t0=pltpu.VMEM((3 * mid, half), BF16),
        w2t1=pltpu.VMEM((3 * mid, half), BF16),
        x_grid=pltpu.VMEM((8, 8 * CELL, chan), BF16),
        cot_grid=pltpu.VMEM((8, 8 * CELL, chan), BF16),
        out_grid=pltpu.VMEM((8, 8 * CELL, chan), BF16),
        xa=pltpu.VMEM((PADDED, chan), BF16),
        xb=pltpu.VMEM((PADDED, chan), BF16),
        aa=pltpu.VMEM((PADDED, chan), BF16),
        ab=pltpu.VMEM((PADDED, chan), BF16),
        ea=pltpu.VMEM((PADDED, mid), BF16),
        eb=pltpu.VMEM((PADDED, mid), BF16),
        mid1=pltpu.VMEM((ROWS, mid), F32),
        mid2=pltpu.VMEM((ROWS, mid), F32),
        grad_mid=pltpu.VMEM((ROWS, mid), F32),
        v1=pltpu.VMEM((ROWS, mid), BF16),
        v2=pltpu.VMEM((ROWS, mid), BF16),
        time1=pltpu.VMEM((ROWS, chan), F32),
        time2=pltpu.VMEM((ROWS, chan), F32),
        grad_pre=pltpu.VMEM((ROWS, chan), F32),
        down=pltpu.VMEM((chan // 128, ROWS + CHUNK, 128), F32),
        up=pltpu.VMEM((chan // 128, ROWS + CHUNK, 128), F32),
        e3=pltpu.VMEM((2, 3, ROWS, half), BF16),
        sib_e3=pltpu.VMEM((3, ROWS, half), BF16),
        halo_out=pltpu.VMEM((2, few_rows, chan), F32),
        halo_in=pltpu.VMEM((4, 2, few_rows, chan), F32),
        param=pltpu.VMEM((8, mid), F32),
        tile_mid=pltpu.VMEM((2, 4, CELL, mid), F32),
        tile_out=pltpu.VMEM((2, 4, CELL, chan), F32),
        back=pltpu.VMEM((2, CELL, mid), F32),
        norm_part=pltpu.VMEM((2, 8, mid), F32),
        sum_b=pltpu.VMEM((2, 4, 8, mid), F32),
        sum_c=pltpu.VMEM((2, nb // 2, 8, mid), F32),
        own_sem=dma((4, 2)),
        ring_send=dma((4, 2)),
        ring_recv=dma((4, 2, 2, 2, nb // 2 + 1)),
        sib_send=dma((4, 2)),
        sib_recv=dma((4, 2)),
        over_send=dma((4, 2)),
        over_recv=dma((4, 2, 2, nb // 2 + 1)),
        norm_sem=dma((2,)),
        credit=pltpu.SemaphoreType.REGULAR((3,)),
        sb_send=dma((9,)),
        sb_recv=dma((9,)),
        sc_send=dma((9,)),
        sc_recv=dma((9,)),
        halo_send=dma((4, 2)),
        halo_recv=dma((4, 2)),
        share_send=dma((6,)),
        share_recv=dma((6,)),
        e_all0=pltpu.VMEM((4 * ROWS, 512), BF16),
        e_all1=pltpu.VMEM((4 * ROWS, mid - 512), BF16),
        xq1=pltpu.VMEM((3, 2, PADDED, chan // 4), BF16),
        xq2=pltpu.VMEM((3, 2, PADDED, chan // 4), BF16),
        xt=pltpu.VMEM((mid, 2 * ROWS), BF16),
        xt2=pltpu.VMEM((mid, 2 * ROWS), BF16),
        sib_v=pltpu.VMEM((ROWS, mid), BF16),
        e_send=dma((2, 2)),
        e_recv=dma((2, 2, 2)),
        xq_send=dma((2,)),
        xq_recv=dma((2,)),
        y_send=dma((4, 2)),
        y_recv=dma((4, 2)),
        z_send=dma((4, 2)),
        z_recv=dma((4, 2)),
        cast_send=dma((4, 2, 6)),
        cast_recv=dma((4, 2, 8)),
        out_sem=dma((4, 2, 2)),
        fin_send=dma((4,)),
        fin_recv=dma((4,)),
        tile_send=dma((4,)),
        tile_recv=dma((4,)),
        tile_own=dma((4,)),
    )
    names = (*inputs_of, *outputs_of, *scratch_of)
    cell_count = float(frames * nb * HGT * HGT)
    results = pl.pallas_call(
        functools.partial(block_kernel, (nb, chan, mid, cell_count), names),
        out_shape=[jax.ShapeDtypeStruct(shape, dtype) for shape, dtype, _ in outputs_of.values()],
        in_specs=[pl.BlockSpec(memory_space=space) for _, space in inputs_of.values()],
        out_specs=[pl.BlockSpec(memory_space=space) for _, _, space in outputs_of.values()],
        scratch_shapes=list(scratch_of.values()),
        compiler_params=pltpu.CompilerParams(
            collective_id=0, has_side_effects=True, vmem_limit_bytes=VMEM_LIMIT
        ),
    )(*(array for array, _ in inputs_of.values()))
    got = SimpleNamespace(**dict(zip(outputs_of, results)))

    def spatial(left, right):
        return jnp.concatenate([left, right], axis=1).astype(F32)

    def temporal(pair):
        return jnp.concatenate([pair[0], pair[1]], axis=1).astype(F32)

    def norm(row, like):
        size = like.shape[0]
        return lax.dynamic_slice_in_dim(got.norm_grads[row], b * size, size)

    return (
        untiled(got.block_out),
        untiled(got.grad_input),
        spatial(got.out1s0, got.out1s1),
        norm(0, first_mid_gain),
        norm(1, first_mid_bias),
        temporal(got.out1t),
        norm(2, first_out_gain),
        norm(3, first_out_bias),
        spatial(got.out2s0, got.out2s1),
        norm(4, second_mid_gain),
        norm(5, second_mid_bias),
        temporal(got.out2t),
        norm(6, second_out_gain),
        norm(7, second_out_bias),
    )


def extended(shard, sides, width):
    for axis, dim in sides:
        count, length = (lax.axis_size(axis), shard.shape[dim])
        up = [(i, (i + 1) % count) for i in range(count - 1)]
        down = [(j, i) for i, j in up]
        last = lax.slice_in_dim(shard, length - width, length, axis=dim)
        leading = lax.slice_in_dim(shard, 0, width, axis=dim)
        before = lax.ppermute(last, axis, up)
        after = lax.ppermute(leading, axis, down)
        shard = jnp.concatenate([before, shard, after], axis=dim)
    return shard


def passed_along(shard, axis, by):
    count = lax.axis_size(axis)
    pairs = [(i, i + by) for i in range(count) if 0 <= i + by < count]
    return lax.ppermute(shard, axis, pairs)


def for_sending(shard):

    def short(part):
        return part.astype(jnp.bfloat16) if part.dtype == jnp.float32 else part

    return jax.tree.map(short, shard)


def silu_slope(values):
    sigma = jax.nn.sigmoid(values)
    return sigma * (1.0 + values * (1.0 - sigma))


def spatial_forward(field_in, kernel):
    frames, tile_side = (field_in.shape[0], field_in.shape[1])
    padded = extended(field_in, (("ha", 1), ("wa", 2)), 1)
    pieces = [
        padded[:, offset // 3 : offset // 3 + tile_side, offset % 3 : offset % 3 + tile_side, :]
        for offset in range(9)
    ]
    patches = jnp.concatenate(pieces, axis=-1).reshape(frames * tile_side * tile_side, -1)
    return (patches, jnp.dot(patches, kernel, preferred_element_type=jnp.float32))


def spatial_backward(grad_out, patches, kernel):
    frames, tile_side, channels = (grad_out.shape[0], grad_out.shape[1], grad_out.shape[3])
    row_count = frames * tile_side * tile_side
    padded = extended(grad_out, (("ha", 1), ("wa", 2)), 1)
    pieces = [
        padded[
            :,
            2 - offset // 3 : 2 - offset // 3 + tile_side,
            2 - offset % 3 : 2 - offset % 3 + tile_side,
            :,
        ]
        for offset in range(9)
    ]
    stacked = jnp.concatenate(pieces, axis=-1).reshape(row_count, 9, channels)
    grad_in = jnp.einsum(
        "rkm,kcm->rc", stacked, kernel.reshape(9, -1, channels), preferred_element_type=jnp.float32
    )
    grad_kernel = jnp.einsum(
        "rk,rm->km",
        patches,
        grad_out.reshape(row_count, channels),
        preferred_element_type=jnp.float32,
    )
    return (grad_in, grad_kernel)


def temporal_forward(field_in, clip_gate, kernel):
    frames, tile_side = (field_in.shape[0], field_in.shape[1])
    gated_in = field_in * clip_gate
    earlier = passed_along(field_in[-1:], "batch", 1)
    later_frame = passed_along(gated_in[:1], "batch", -1)
    before = jnp.concatenate([earlier, field_in[:-1]], axis=0) * clip_gate
    after_tap = jnp.concatenate([gated_in[1:], later_frame], axis=0)
    joined = jnp.concatenate([before, field_in, after_tap], axis=-1).reshape(
        frames * tile_side * tile_side, -1
    )
    return (joined, jnp.dot(joined, kernel, preferred_element_type=jnp.float32))


def temporal_backward(grad_out, joined, clip_gate, kernel):
    frames, tile_side, channels = (grad_out.shape[0], grad_out.shape[1], grad_out.shape[3])
    row_count = frames * tile_side * tile_side
    gated_grad = grad_out * clip_gate
    later_frame = passed_along(gated_grad[:1], "batch", -1)
    earlier = passed_along(grad_out[-1:], "batch", 1)
    from_later = jnp.concatenate([gated_grad[1:], later_frame], axis=0)
    from_earlier = jnp.concatenate([earlier, grad_out[:-1]], axis=0) * clip_gate
    stacked = jnp.concatenate([from_later, grad_out, from_earlier], axis=-1).reshape(
        row_count, 3, channels
    )
    grad_in = jnp.einsum(
        "rkc,kmc->rm", stacked, kernel.reshape(3, -1, channels), preferred_element_type=jnp.float32
    )
    grad_kernel = jnp.einsum(
        "rk,rc->kc",
        joined,
        grad_out.reshape(row_count, channels),
        preferred_element_type=jnp.float32,
    )
    return (grad_in, grad_kernel)


def norm_forward(pre_norm, norm_gain, norm_bias, valid_rows, cell_count):
    first_sum = jnp.sum(pre_norm * valid_rows, axis=0)
    square_sum = jnp.sum(pre_norm * pre_norm * valid_rows, axis=0)
    first_sum, square_sum = lax.psum((first_sum, square_sum), ("ha", "wa", "batch"))
    mean_val = first_sum / cell_count
    inv_std = lax.rsqrt(square_sum / cell_count - mean_val * mean_val + epsilon)
    normed = (pre_norm - mean_val) * inv_std
    return (normed, inv_std, normed * norm_gain.astype(jnp.float32) + norm_bias.astype(jnp.float32))


def norm_backward(grad_norm, normed, inv_std, norm_gain, valid_rows, cell_count):
    bias_grad = jnp.sum(grad_norm, axis=0)
    gain_grad = jnp.sum(grad_norm * normed, axis=0)
    bias_grad, gain_grad = lax.psum((bias_grad, gain_grad), ("ha", "wa", "batch"))
    grad_in = (
        valid_rows
        * norm_gain.astype(jnp.float32)
        * inv_std
        * (grad_norm - bias_grad / cell_count - normed * gain_grad / cell_count)
    )
    return (grad_in, gain_grad, bias_grad)


def forward_pair(field_in, weights, clip_gate, valid_rows, cell_count):
    frames, tile_side = (field_in.shape[0], field_in.shape[1])
    patches, spatial_out = spatial_forward(field_in, weights[0])
    mid_hat, mid_scale, mid_norm = norm_forward(
        spatial_out, weights[1], weights[2], valid_rows, cell_count
    )
    hidden = (
        (jax.nn.silu(mid_norm) * valid_rows)
        .astype(jnp.bfloat16)
        .reshape(frames, tile_side, tile_side, -1)
    )
    joined, temporal_out = temporal_forward(hidden, clip_gate, weights[3])
    out_hat, out_scale, out_norm = norm_forward(
        temporal_out, weights[4], weights[5], valid_rows, cell_count
    )
    return ((patches, mid_hat, mid_scale, mid_norm, joined, out_hat, out_scale), out_norm)


def backward_pair(grad_norm, kept, weights, clip_gate, valid_rows, cell_count, tile_side):
    patches, mid_hat, mid_scale, mid_norm, joined, out_hat, out_scale = kept
    frames = clip_gate.shape[0]
    grad_time, out_gain_grad, out_bias_grad = norm_backward(
        grad_norm, out_hat, out_scale, weights[4], valid_rows, cell_count
    )
    grad_time = grad_time.astype(jnp.bfloat16).reshape(frames, tile_side, tile_side, -1)
    grad_hidden, temporal_grad = temporal_backward(grad_time, joined, clip_gate, weights[3])
    grad_mid = grad_hidden * valid_rows * silu_slope(mid_norm)
    grad_spatial, mid_gain_grad, mid_bias_grad = norm_backward(
        grad_mid, mid_hat, mid_scale, weights[1], valid_rows, cell_count
    )
    grad_spatial = grad_spatial.astype(jnp.bfloat16).reshape(frames, tile_side, tile_side, -1)
    grad_in, spatial_grad = spatial_backward(grad_spatial, patches, weights[0])
    return (
        grad_in,
        (spatial_grad, mid_gain_grad, mid_bias_grad, temporal_grad, out_gain_grad, out_bias_grad),
    )


def per_device(
    inputs,
    starts,
    first_spatial,
    first_mid_gain,
    first_mid_bias,
    first_temporal,
    first_out_gain,
    first_out_bias,
    second_spatial,
    second_mid_gain,
    second_mid_bias,
    second_temporal,
    second_out_gain,
    second_out_bias,
    cotangent,
):
    shards = (
        first_spatial,
        first_mid_gain,
        first_mid_bias,
        first_temporal,
        first_out_gain,
        first_out_bias,
        second_spatial,
        second_mid_gain,
        second_mid_bias,
        second_temporal,
        second_out_gain,
        second_out_bias,
    )
    micro_total, frames, tile_side, channels = (
        inputs.shape[0],
        inputs.shape[1],
        inputs.shape[2],
        inputs.shape[4],
    )
    row_count = frames * tile_side * tile_side
    cell_count = frames * lax.axis_size("batch") * HGT * HGT
    offsets = jnp.arange(tile_side)
    inside_h = lax.axis_index("ha") * tile_side + offsets < HGT
    inside_w = lax.axis_index("wa") * tile_side + offsets < HGT
    valid_grid = inside_h[:, None] & inside_w[None, :]
    valid_tile = valid_grid.astype(jnp.bfloat16)[None, :, :, None]
    valid_rows = jnp.broadcast_to(
        valid_grid.astype(jnp.float32)[None], (frames, tile_side, tile_side)
    ).reshape(row_count, 1)
    results = []
    input_grads = []
    kernel_total = None
    norm_total = None
    for micro_step in range(micro_total):
        gathered = (
            lax.all_gather(shards[0], "batch", axis=0, tiled=True),
            lax.all_gather(shards[1], "batch", axis=0, tiled=True),
            lax.all_gather(shards[2], "batch", axis=0, tiled=True),
            lax.all_gather(shards[3], "batch", axis=0, tiled=True),
            lax.all_gather(shards[4], "batch", axis=0, tiled=True),
            lax.all_gather(shards[5], "batch", axis=0, tiled=True),
            lax.all_gather(shards[6], "batch", axis=0, tiled=True),
            lax.all_gather(shards[7], "batch", axis=0, tiled=True),
            lax.all_gather(shards[8], "batch", axis=0, tiled=True),
            lax.all_gather(shards[9], "batch", axis=0, tiled=True),
            lax.all_gather(shards[10], "batch", axis=0, tiled=True),
            lax.all_gather(shards[11], "batch", axis=0, tiled=True),
        )
        clip_gate = (1 - starts[micro_step]).astype(jnp.bfloat16).reshape(frames, 1, 1, 1)
        x_in = inputs[micro_step] * valid_tile
        first_kept, first_norm = forward_pair(
            x_in, gathered[0:6], clip_gate, valid_rows, cell_count
        )
        first_act = (
            (jax.nn.silu(first_norm) * valid_rows)
            .astype(jnp.bfloat16)
            .reshape(frames, tile_side, tile_side, channels)
        )
        second_kept, second_norm = forward_pair(
            first_act, gathered[6:12], clip_gate, valid_rows, cell_count
        )
        pre_out = second_norm + x_in.reshape(row_count, channels).astype(jnp.float32)
        results.append(
            (jax.nn.silu(pre_out) * valid_rows).reshape(frames, tile_side, tile_side, channels)
        )
        grad_pre = (
            cotangent[micro_step].reshape(row_count, channels).astype(jnp.float32)
            * valid_rows
            * silu_slope(pre_out)
        )
        grad_act, second_grads = backward_pair(
            grad_pre, second_kept, gathered[6:12], clip_gate, valid_rows, cell_count, tile_side
        )
        grad_first = grad_act * valid_rows * silu_slope(first_norm)
        grad_conv, first_grads = backward_pair(
            grad_first, first_kept, gathered[0:6], clip_gate, valid_rows, cell_count, tile_side
        )
        input_grads.append(
            ((grad_conv + grad_pre) * valid_rows).reshape(frames, tile_side, tile_side, channels)
        )
        step_grads = first_grads + second_grads
        kernel_now = (step_grads[0], step_grads[3], step_grads[6], step_grads[9])
        norm_now = (
            step_grads[1],
            step_grads[2],
            step_grads[4],
            step_grads[5],
            step_grads[7],
            step_grads[8],
            step_grads[10],
            step_grads[11],
        )
        if micro_step == 0:
            kernel_total = kernel_now
            norm_total = norm_now
        else:
            kernel_total = jax.tree.map(jnp.add, kernel_total, kernel_now)
            norm_total = jax.tree.map(jnp.add, norm_total, norm_now)
    kernel_total = lax.psum_scatter(kernel_total, "batch", scatter_dimension=0, tiled=True)
    kernel_total = jax.tree.map(
        lambda part: part.astype(jnp.float32), lax.psum(for_sending(kernel_total), ("ha", "wa"))
    )
    shard_index = lax.axis_index("batch")
    batch_count = lax.axis_size("batch")
    norm_shards = tuple(
        (
            lax.dynamic_slice_in_dim(
                full_sum,
                shard_index * (full_sum.shape[0] // batch_count),
                full_sum.shape[0] // batch_count,
            )
            for full_sum in norm_total
        )
    )
    return (
        jnp.stack(results),
        jnp.stack(input_grads),
        kernel_total[0],
        norm_shards[0],
        norm_shards[1],
        kernel_total[1],
        norm_shards[2],
        norm_shards[3],
        kernel_total[2],
        norm_shards[4],
        norm_shards[5],
        kernel_total[3],
        norm_shards[6],
        norm_shards[7],
    )


def solution(mesh):
    in_specs = (
        P(None, "batch", "ha", "wa", None),
        P(None, "batch"),
        P("batch", None),
        P("batch"),
        P("batch"),
        P("batch", None),
        P("batch"),
        P("batch"),
        P("batch", None),
        P("batch"),
        P("batch"),
        P("batch", None),
        P("batch"),
        P("batch"),
        P(None, "batch", "ha", "wa", None),
    )
    out_specs = (
        P(None, "batch", "ha", "wa", None),
        P(None, "batch", "ha", "wa", None),
        P("batch", None),
        P("batch"),
        P("batch"),
        P("batch", None),
        P("batch"),
        P("batch"),
        P("batch", None),
        P("batch"),
        P("batch"),
        P("batch", None),
        P("batch"),
        P("batch"),
    )
    batch = mesh.shape["batch"]

    def program(*args):
        spat, temp = args[2].shape[0], args[5].shape[0]
        fits = args[0].shape == (2, 16, 4, 4, 512) and args[2].shape[1] == 1152
        if fits and batch == 8 and spat * batch == 9 * 512 and temp * batch == 3 * 1152:
            return per_device_fast(batch, *args)
        return per_device(*args)

    return jax.shard_map(
        program, mesh=mesh, in_specs=in_specs, out_specs=out_specs, check_vma=False
    )
```

```python
import functools
from types import SimpleNamespace

import jax
import jax.numpy as jnp
from jax import lax
from jax.experimental import pallas as pl
from jax.experimental.pallas import tpu as pltpu
from jax.sharding import PartitionSpec as P

HGT = 7
epsilon = 1e-05
MESH = pl.DeviceIdType.MESH
F32 = jnp.float32
BF16 = jnp.bfloat16

BASE = 10
CELL = 8
ROWS = HGT * 8 * CELL
PADDED = (BASE + HGT * 8 + BASE) * CELL
MAIN = BASE * CELL
CHUNK = 2 * CELL
CHUNKS = ROWS // CHUNK
VMEM_LIMIT = 64 * 1024 * 1024 - 1024 * 1024


def when(cond, work):
    if cond is True:
        work()
    elif cond is not False:
        pl.when(cond)(work)


def loop(count, body, init):
    def twice(i, carry):
        return body(2 * i + 1, body(2 * i, carry))

    return lax.fori_loop(0, count // 2, twice, init)


def sigmoid(x):
    return 0.5 * jnp.tanh(0.5 * x) + 0.5


def nn(a, b):
    return jnp.dot(a, b, preferred_element_type=F32)


def nt(a, b):
    return lax.dot_general(a, b, (((1,), (1,)), ((), ())), preferred_element_type=F32)


def tn(a, b):
    return lax.dot_general(a, b, (((0,), (0,)), ((), ())), preferred_element_type=F32)


def rows_of(start, size, step=16):
    if not isinstance(start, int):
        start = pl.multiple_of(start, step)
    return pl.ds(start, size)


def block_kernel(dims, names, *all_refs):
    r = SimpleNamespace(**dict(zip(names, all_refs, strict=True)))
    nb, chan, mid, cell_count = dims
    spat = 9 * chan // nb
    temp = 3 * mid // nb
    unit = spat // 6
    quarter = chan // 4
    half = chan // 2
    h = lax.axis_index("ha")
    w = lax.axis_index("wa")
    b = lax.axis_index("batch")
    par = lax.rem(b, 2)
    bh = lax.div(b, 2)
    pos = par * (nb - 1 - bh) + (1 - par) * bh

    def at(p):
        p = lax.rem(p + 4 * nb, nb)
        upper = lax.div(p, nb // 2)
        return (1 - upper) * (2 * p) + upper * (2 * (nb - 1 - p) + 1)

    def at_group(j):
        return (lax.rem(j, 2), lax.div(j, 2))

    mine = 2 * w + h
    sibling = (1 - h, w, b)
    beside = (h, 1 - w, b)
    later_dev = (1 - h, w, lax.rem(b + h, nb))
    earlier_dev = (1 - h, w, lax.rem(b + nb - 1 + h, nb))
    tile_group = [(lax.rem(mine + d, 4), (*at_group(lax.rem(mine + d, 4)), b)) for d in (1, 2, 3)]
    across = (h, w, b + 1 - 2 * par)
    pos_b = h * 2 + par
    plane = []
    for d in (1, 2, 3):
        q = lax.rem(pos_b + d, 4)
        plane.append((q, (lax.div(q, 2), w, b - par + lax.rem(q, 2))))
    depth = nb // 2
    place = (h * 2 + par) * depth + bh
    crowd = []
    for d in range(1, 2 * nb):
        q = lax.rem(place + d, 2 * nb)
        side, far = lax.div(q, depth), lax.rem(q, depth)
        crowd.append((lax.div(side, 2), w, 2 * far + lax.rem(side, 2)))
    line = []
    for d in range(1, depth):
        q = lax.rem(bh + d, depth)
        line.append((q, (h, w, 2 * q + par)))

    def named(dev):
        return dict(ha=dev[0], wa=dev[1], batch=dev[2])

    def rc(src, dst, send, recv, dev):
        return pltpu.make_async_remote_copy(
            src_ref=src, dst_ref=dst, send_sem=send, recv_sem=recv, device_id=named(dev), device_id_type=MESH
        )

    def lc(src, dst, sem):
        return pltpu.make_async_copy(src, dst, sem)

    partners = []
    partners += [dev for _, dev in tile_group] + crowd
    barrier = pltpu.get_barrier_semaphore()
    for dev in partners:
        pl.semaphore_signal(barrier, inc=1, device_id=named(dev), device_id_type=MESH)
    pl.semaphore_wait(barrier, len(partners))

    shards = (r.first_spatial, r.first_temporal, r.second_spatial, r.second_temporal)
    whole = ((r.w1s0, r.w1s1), (r.w1t0, r.w1t1), (r.w2s0, r.w2s1), (r.w2t0, r.w2t1))
    halves = ((0, 512), (512, mid - 512))
    shared = 2 * w + h
    shared_beside = 2 * (1 - w) + h
    way = 1 - 2 * h
    ways = (way, -way)
    onward = [(h, w, at(pos + d)) for d in ways]
    steps = (nb // 2, nb // 2 - 1)
    third = temp // 3

    def taken(i, core, side):
        if i % 2 == 0:
            return 3 * unit * core + unit * side, 2 * unit
        return (1 - core) * 2 * third * side + core * third, third

    def crosses(i, core, side):
        if i % 2 == 0:
            return 3 * unit * core + 2 * unit * side, unit
        return 2 * third * side, third

    def rows_in(i, c, owner, part):
        size = spat if i % 2 == 0 else temp
        return whole[i][c].at[rows_of(owner * size + part[0], part[1]), :]

    def rows_from(i, c, part):
        c0, cw = halves[c] if i % 2 == 0 else (c * half, half)
        return shards[i].at[rows_of(part[0], part[1]), c0 : c0 + cw]

    def pieces(i):
        start, size = taken(i, h, w)
        if i % 2:
            return ((start, size),)
        return ((start, size // 2), (start + size // 2, size // 2))

    def crossing(i, work):
        if i % 2 == 0:
            work()
        else:
            pl.when(h == 0)(work)

    def own_copy(i, c):
        rows = spat if i % 2 == 0 else temp
        return lc(rows_from(i, c, (0, rows)), rows_in(i, c, b, (0, rows)), r.own_sem.at[i, c])

    def ring(i, c, k, d, s, owner, from_shard=False):
        part = pieces(i)[k]
        dst = rows_in(i, c, owner, part)
        src = rows_from(i, c, part) if from_shard else dst
        return rc(src, dst, r.ring_send.at[i, c], r.ring_recv.at[i, c, k, d, s], onward[d])

    def cross(i, c, owner, part):
        ref = rows_in(i, c, owner, part)
        return rc(ref, ref, r.sib_send.at[i, c], r.sib_recv.at[i, c], sibling)

    def over(i, c, d, s, owner, part):
        ref = rows_in(i, c, owner, part)
        return rc(ref, ref, r.over_send.at[i, c], r.over_recv.at[i, c, d, s], beside)

    def gather_start(i):
        for k in range(len(pieces(i))):
            for d in (0, 1):
                for c in (0, 1):
                    ring(i, c, k, d, 1, b, True).start()
        for c in (0, 1):
            own_copy(i, c).start()

    def owners(s):
        return [(d, at(pos - ways[d] * s)) for d in (0, 1) if s <= steps[d]]

    def gather_relay(i, s):
        def work():
            part = crosses(i, h, 1 - w)
            for d, owner in owners(s):
                for c in (0, 1):
                    over(i, c, d, s, owner, part).wait_recv()
                    cross(i, c, owner, part).start()

        crossing(i, work)

    def gather_pump(i, s):
        for k in range(len(pieces(i))):
            for d, owner in owners(s):
                for c in (0, 1):
                    ring(i, c, k, d, s, owner).wait_recv()
                    if s < steps[d]:
                        ring(i, c, k, d, s + 1, owner).start()
        for d, owner in owners(s):
            for c in (0, 1):
                crossing(i, lambda c=c, d=d, owner=owner: over(i, c, d, s, owner, crosses(i, h, w)).start())
                cross(i, c, owner, taken(i, h, w)).start()
        if s > 1:
            gather_relay(i, s - 1)

    def span(i, c, size):
        return whole[i][c].at[0 : (nb - 1) * size, :]

    def gather_finish(i):
        gather_relay(i, steps[0])

        def arrived(size):
            for c in (0, 1):
                ref = span(i, c, size)
                rc(ref, ref, r.sib_send.at[i, c], r.sib_recv.at[i, c], sibling).wait_recv()

        if i % 2 == 0:
            arrived(3 * unit)
        else:
            pl.when(h == 0)(lambda: arrived(third))
            pl.when(h == 1)(lambda: arrived(2 * third))
        for c in (0, 1):
            own_copy(i, c).wait()

    def gather_sent(i):
        def sent(size, sem):
            for c in (0, 1):
                ref = span(i, c, size)
                rc(ref, ref, sem.at[i, c], r.own_sem.at[i, c], sibling).wait_send()

        sent(taken(i, h, w)[1], r.ring_send)
        crossing(i, lambda: sent(crosses(i, h, w)[1], r.over_send))
        if i % 2 == 0:
            sent(3 * unit, r.sib_send)
        else:
            pl.when(h == 0)(lambda: sent(2 * third, r.sib_send))
            pl.when(h == 1)(lambda: sent(third, r.sib_send))

    def total(k, width, value, works=()):
        slot = k % 2
        if width == chan:
            flat, me = r.sum_flat, pos_b * depth + bh
            flat[slot, me] = value
            for dev in crowd:
                part = flat.at[slot, me]
                rc(part, part, r.sb_send.at[k], r.sb_recv.at[k], dev).start()
            for work in works:
                if work:
                    work()
            ref = flat.at[slot, 0 : len(crowd)]
            every = rc(ref, ref, r.sb_send.at[k], r.sb_recv.at[k], sibling)
            every.wait_recv()
            result = jnp.sum(flat[slot], axis=0)
            every.wait_send()
            return jnp.concatenate([result[2 * n : 2 * n + 2] for n in range(4)], axis=1)
        wide = value.shape[1]
        cols = pl.ds(0, wide)
        works = list(works) + [None] * 2
        four, far = r.sum_b, r.sum_c
        four[slot, pos_b, :, cols] = value

        def phase(ref, me, group, send, recv, work):
            for _, dev in group:
                part = ref.at[slot, me, :, cols]
                rc(part, part, send.at[k], recv.at[k], dev).start()
            if work:
                work()
            ref = ref.at[slot, 0 : len(group), :, cols]
            every = rc(ref, ref, send.at[k], recv.at[k], sibling)
            every.wait_recv()
            return every

        first = phase(four, pos_b, plane, r.sb_send, r.sb_recv, works[0])
        far[slot, bh, :, cols] = (four[slot, 0, :, cols] + four[slot, 1, :, cols]) + (
            four[slot, 2, :, cols] + four[slot, 3, :, cols]
        )
        second = phase(far, bh, line, r.sc_send, r.sc_recv, works[1])
        result = far[slot, 0, :, cols]
        for q in range(1, depth):
            result = result + far[slot, q, :, cols]
        first.wait_send()
        second.wait_send()
        if wide == width:
            return result
        return jnp.concatenate([result[2 * n : 2 * n + 2] for n in range(width // wide)], axis=1)

    def chunk(ref, i, base=0, width=None):
        cols = slice(None) if width is None else pl.ds(0, width)
        value = ref[rows_of(base + i * CHUNK, CHUNK), cols]
        return value.astype(F32).reshape(2, CELL, value.shape[-1])

    def put(ref, i, value, base=0, width=None):
        cols = slice(None) if width is None else pl.ds(0, width)
        ref[rows_of(base + i * CHUNK, CHUNK), cols] = value.reshape(CHUNK, value.shape[-1]).astype(ref.dtype)

    def keep(i):
        inside = jnp.where(lax.rem(i, 4) == 3, 0.0, 1.0).astype(F32)
        first = lax.broadcasted_iota(jnp.int32, (2, 1, 1), 0) == 0
        return jnp.where(first, 1.0, inside)

    def packed(one, two, width):
        rows = jnp.concatenate([jnp.sum(v, axis=0, keepdims=True) for v in (one, two)], axis=0)
        wide = 384 if width == mid else 128
        parts = [rows[:, n * wide : (n + 1) * wide] for n in range(width // wide)]
        return jnp.concatenate((parts + parts[-1:])[0:4], axis=0)

    def moments(ref, width):
        def body(i, carry):
            v = chunk(ref, i)
            m = v * keep(i)
            return (carry[0] + m[0] + m[1], carry[1] + m[0] * v[0] + m[1] * v[1])

        zero = jnp.zeros((CELL, width), F32)
        return loop(CHUNKS, body, (zero, zero))

    def prepare(n, sums, width):
        tile = r.tile_mid if width == mid else r.tile_out
        n2 = n // 2
        gain = r.param[2 * n : 2 * n + 1, 0:width]
        bias = r.param[2 * n + 1 : 2 * n + 2, 0:width]
        mean = sums[0:1] / cell_count
        inv = lax.rsqrt(sums[1:2] / cell_count - mean * mean + epsilon)
        scale = inv * gain
        shift = bias - mean * scale
        for k, v in enumerate((scale, shift, inv, mean * inv)):
            tile[n2, k] = jnp.broadcast_to(v, (CELL, width))

    def tiles(n, width):
        tile = r.tile_mid if width == mid else r.tile_out
        return [tile[n // 2, k][None] for k in range(4)]

    def fill(ref_a, ref_b, value_of, width):
        pads(ref_a, ref_b, width)

        def body(i, before):
            v = value_of(i)
            put(ref_a, i, v, MAIN)
            pair = jnp.concatenate([before[None], v[0:1]], axis=0)
            put(ref_b, i, pair, MAIN - CHUNK)
            return v[1]

        loop(CHUNKS, body, jnp.zeros((CELL, width), F32))

    def activated(src, n, width):
        def value(i):
            scale, shift, _, _ = tiles(n, width)
            y = chunk(src, i) * scale + shift
            return y * sigmoid(y) * keep(i)

        return value

    def taps(ref_a, ref_b, k, size=ROWS):
        r0 = MAIN - 8 * CELL + 8 * CELL * k
        return (
            ref_b[rows_of(r0 - CHUNK, size), :],
            ref_a[rows_of(r0, size), :],
            ref_b[rows_of(r0, size), :],
        )

    def conv(ref_a, ref_b, weight, out, pump=None):
        for n, (c0, cw) in enumerate(halves):

            def body(a, _, c0=c0, cw=cw, n=n):
                x = taps(ref_a, ref_b, a)
                acc = nn(jnp.concatenate(x, axis=1), weight[n][rows_of(a * 3 * chan, 3 * chan), :])

                @pl.when(a == 0)
                def _():
                    out[:, c0 : c0 + cw] = acc

                @pl.when(a > 0)
                def _():
                    out[:, c0 : c0 + cw] += acc

                if pump is not None:
                    pump(n * 3 + a)
                return 0

            lax.fori_loop(0, 3, body, 0)

    def conv_back(ref_a, ref_b, weight, out, pump=None):
        def body(k, _):
            e = taps(ref_a, ref_b, k)
            acc = None
            for j in range(3):
                tap = 8 - 3 * k - j
                for n, (c0, cw) in enumerate(halves):
                    term = nt(e[j][:, c0 : c0 + cw], weight[n][rows_of(tap * chan, chan), :])
                    acc = term if acc is None else acc + term

            @pl.when(k == 0)
            def _():
                out[:, 0:chan] = acc

            @pl.when(k > 0)
            def _():
                out[:, 0:chan] += acc

            if pump is not None:
                pump(k)
            return 0

        lax.fori_loop(0, 3, body, 0)

    def send_frames(k, which=(0, 1)):
        down, up = r.down, r.up
        count = ROWS // CELL
        copies = []
        for n in which:
            for c in range(chan // 128):
                lanes = pl.ds(128 * c, 128)
                if n == 0:
                    r.halo_out[0, :, lanes] = down[c, pl.ds(2 * CELL - 1, count, stride=CELL), :]
                else:
                    r.halo_out[1, :, lanes] = up[c, pl.ds(0, count, stride=CELL), :]
            dev = (later_dev, earlier_dev)[n]
            copies.append(
                rc(r.halo_out.at[n], r.halo_in.at[k, n], r.halo_send.at[k, n], r.halo_recv.at[k, n], dev)
            )
            copies[-1].start()
        return copies

    def take_frames(k, copies):
        down, up = r.down, r.up
        count = ROWS // CELL
        for copy in copies:
            copy.wait()
        at_start = jnp.logical_and(h == 0, b == 0)
        at_end = jnp.logical_and(h == 1, b == nb - 1)
        for c in range(chan // 128):
            lanes = pl.ds(128 * c, 128)
            before = r.halo_in[k, 0, :, lanes]
            after = r.halo_in[k, 1, :, lanes]
            down[c, pl.ds(CELL - 1, count, stride=CELL), :] = jnp.where(at_start, 0.0, before)
            up[c, pl.ds(CELL, count, stride=CELL), :] = jnp.where(at_end, 0.0, after)

    def by_lanes(ref, rows):
        return jnp.concatenate([ref[c, rows, :] for c in range(chan // 128)], axis=1)

    def put_lanes(ref, rows, value):
        for c in range(chan // 128):
            ref[c, rows, :] = value[:, 128 * c : 128 * c + 128]

    def shifted(i):
        before = by_lanes(r.down, rows_of(i * CHUNK, CHUNK + CELL))[CELL - 1 : CELL - 1 + CHUNK]
        after = by_lanes(r.up, rows_of(i * CHUNK, CHUNK + CELL))[1 : 1 + CHUNK]
        gate = r.gate[...][None]
        return (before.reshape(2, CELL, chan) * gate, after.reshape(2, CELL, chan))

    def both_halves(weight, start, size):
        return jnp.concatenate([part[start : start + size, :] for part in weight], axis=1)

    def temporal(k, v, weight, out, works=()):
        works = list(works) + [None] * 2
        put_lanes(r.down, pl.ds(CELL, ROWS), nn(v[...], both_halves(weight, 0, mid)))
        copies = send_frames(k, (0,))
        y2 = nn(v[...], both_halves(weight, 2 * mid, mid))
        y2 = (y2.reshape(ROWS // CELL, CELL, chan) * r.gate[...][None]).reshape(ROWS, chan)
        put_lanes(r.up, pl.ds(0, ROWS), y2)
        copies += send_frames(k, (1,))
        out[...] = nn(v[...], both_halves(weight, mid, mid))
        if works[0]:
            works[0]()
        take_frames(k, copies)

        def body(i, carry):
            before, after = shifted(i)
            value = chunk(out, i) + before + after
            put(out, i, value)
            m = value * keep(i)
            return (carry[0] + m[0] + m[1], carry[1] + m[0] * value[0] + m[1] * value[1])

        zero = jnp.zeros((CELL, chan), F32)
        return loop(CHUNKS, body, (zero, zero))

    def put_e(tap, i, e):
        for c in (0, 1):
            r.e3[c, tap, rows_of(i * CHUNK, CHUNK), :] = e[:, c * half : (c + 1) * half]

    def temporal_back(k, weight, works=()):
        works = list(works) + [None] * 2
        copies = send_frames(k)
        e3 = r.e3

        def e_tap(n):
            return jnp.concatenate([e3[0, n], e3[1, n]], axis=1)

        for c0, cw in ((0, 512), (512, mid - 512)):
            r.grad_mid[:, c0 : c0 + cw] = nt(e_tap(1), both_halves(weight, mid + c0, cw))
        if works[0]:
            works[0]()
        take_frames(k, copies)

        def body(i, _):
            before, after = shifted(i)
            put_e(0, i, after.reshape(CHUNK, chan).astype(BF16))
            put_e(2, i, before.reshape(CHUNK, chan).astype(BF16))
            return 0

        loop(CHUNKS, body, 0)
        share = share_e3(k)
        for c0, cw in ((0, 512), (512, mid - 512)):
            r.grad_mid[:, c0 : c0 + cw] += nt(e_tap(0), both_halves(weight, c0, cw)) + nt(
                e_tap(2), both_halves(weight, 2 * mid + c0, cw)
            )
        return share

    def share(k, src, dst):
        copy = rc(src, dst, r.share_send.at[k], r.share_recv.at[k], sibling)
        copy.start()
        return copy

    outs = ((r.out1s0, r.out1s1), r.out1t, (r.out2s0, r.out2s1), r.out2t)

    e_all = (r.e_all0, r.e_all1)

    def e_part(n, slot):
        return e_all[n].at[slot * ROWS : (slot + 1) * ROWS, :]

    def e_copies(k, n):
        send, near, over = r.e_send.at[k, n], r.e_recv.at[k, n, 0], r.e_recv.at[k, n, 1]
        return [
            rc(e_part(n, 0), e_part(n, 1), send, near, sibling),
            rc(e_part(n, 0), e_part(n, 2), send, over, beside),
            rc(e_part(n, 2), e_part(n, 3), send, near, sibling),
        ]

    def share_e(k):
        for n in (0, 1):
            near, over, _ = e_copies(k, n)
            over.start()
            near.start()

    def share_e_on(k, n):
        _, over, far = e_copies(k, n)
        over.wait_recv()
        far.start()

    def share_e_wait(k, n):
        both = e_all[n].at[0 : 2 * ROWS, :]
        rc(both, both, r.e_send.at[k, n], r.e_recv.at[k, n, 0], sibling).wait_recv()
        three = e_all[n].at[0 : 3 * ROWS, :]
        rc(three, three, r.e_send.at[k, n], r.e_recv.at[k, n, 0], sibling).wait_send()

    def share_x(k, xa, xq):
        main = pl.ds(MAIN, ROWS)
        for n, dev in enumerate((sibling, beside, (1 - h, 1 - w, b))):
            lanes = rows_of((2 * dev[1] + dev[0]) * quarter, quarter, 128)
            rc(xa.at[main, lanes], xq.at[n, 0, main, :], r.xq_send.at[k], r.xq_recv.at[k], dev).start()
        all_three = xq.at[:, 0, main, :]
        return rc(all_three, all_three, r.xq_send.at[k], r.xq_recv.at[k], sibling)

    def pads(ref_a, ref_b, width):
        ref_a[0:MAIN, :] = jnp.zeros((MAIN, width), BF16)
        ref_a[MAIN + ROWS : PADDED, :] = jnp.zeros((PADDED - MAIN - ROWS, width), BF16)
        ref_b[0 : MAIN - CHUNK, :] = jnp.zeros((MAIN - CHUNK, width), BF16)
        ref_b[MAIN - CHUNK + ROWS : PADDED, :] = jnp.zeros((PADDED - MAIN + CHUNK - ROWS, width), BF16)

    def spread_x(xq):
        for n in range(3):
            pads(xq.at[n, 0], xq.at[n, 1], quarter)

        def body(i, before):
            after = []
            for n in range(3):
                v = chunk(xq.at[n, 0], i, MAIN)
                put(xq.at[n, 1], i, jnp.concatenate([before[n][None], v[0:1]], axis=0), MAIN - CHUNK)
                after.append(v[1])
            return tuple(after)

        loop(CHUNKS, body, (jnp.zeros((CELL, quarter), F32),) * 3)

    def share_e3(k):
        return share(
            k - 2, r.e3.at[1 - h], r.sib_e3
        )

    def line_row(place):
        return quarter * place + 64 * jnp.where(place > shared, 1, 0)

    def grad_row(tap, side):
        split = 2 * shared + 1
        owner = jnp.where(tap == split, 2 * shared + side, tap - jnp.where(tap > split, 1, 0))
        row = line_row(lax.div(owner, 2)) + jnp.where(tap == split, quarter, 64 * side)
        return 576 * lax.rem(owner, 2) + row

    spare = whole[2]

    def gq(i, row, size):
        return rows_of((mid if i == 0 else 0) + row, size, 64)

    def inbox(i, row, size):
        return rows_of(2 * mid + (mid if i == 0 else 0) + row, size, 64)

    def transpose_x(a, xa, xb, xq, near, far, row):
        lanes = rows_of(shared * quarter, quarter, 128)
        r0 = MAIN - 8 * CELL + 8 * CELL * a
        for j, (c, start) in enumerate(((1, r0 - CHUNK), (0, r0), (1, r0))):
            rows = rows_of(start, ROWS)
            own = (xb if c else xa)[rows, lanes]
            both = jnp.concatenate([own, xq[0, c, rows, :]], axis=0)
            near[rows_of(row + j * quarter, quarter), 0 : 2 * ROWS] = both.T
            both = jnp.concatenate([xq[1, c, rows, :], xq[2, c, rows, :]], axis=0)
            far[rows_of(row + j * quarter, quarter), 0 : 2 * ROWS] = both.T

    def spatial_part(i, near, far, row, tap, n):
        rows = rows_of(row, 3 * quarter)
        acc = nn(near[rows, :], e_all[n][0 : 2 * ROWS, :])
        acc += nn(far[rows, :], e_all[n][2 * ROWS : 4 * ROWS, :])
        acc = acc.astype(BF16)
        for j in range(6):
            spare[n][gq(i, grad_row(tap + j // 2, j % 2), 64), :] = acc[64 * j : 64 * j + 64]

    def transposes(xa, xb, xq, near, far):
        def body(a, _):
            transpose_x(a, xa, xb, xq, near, far, a * 3 * quarter)
            return 0

        lax.fori_loop(0, 3, body, 0)

    def spatial_half(i, near, far, n):
        def body(a, _):
            spatial_part(i, near, far, a * 3 * quarter, 3 * a, n)
            return 0

        lax.fori_loop(0, 3, body, 0)

    def transpose_v(v, sv):
        for c in range(mid // 128):
            lanes = pl.ds(128 * c, 128)
            turned = jnp.concatenate([v[:, lanes], sv[:, lanes]], axis=0).T
            for row in (0, 64):
                ref = r.ea if 128 * c + row < mid // 2 else r.eb
                at_row = (128 * c + row) % (mid // 2)
                ref[at_row : at_row + 64, 0 : 2 * ROWS] = turned[row : row + 64]

    def temporal_grad(i, first, count):
        taps_of = [jnp.concatenate([r.e3[h, k], r.sib_e3[k]], axis=0) for k in range(first, first + count)]
        e = jnp.concatenate(taps_of, axis=1)
        whole_tap = mid // third
        for top in range(0, whole_tap, whole_tap // 2):
            acc = nn((r.eb if top else r.ea)[0 : mid // 2, 0 : 2 * ROWS], e).astype(BF16)
            for k in range(count):
                for n in range(whole_tap // 2):
                    owner, part = divmod((first + k) * whole_tap + top + n, 3)
                    row = (owner % 2) * (depth * temp) + owner // 2 * temp + part * third
                    whole[i][0][row : row + third, :] = acc[n * third : n * third + third, k * half : (k + 1) * half]

    def parts_of(i):
        return (0, 1) if i % 2 == 0 else (0,)

    line_size = 576

    def to_y(i, n, side):
        if i % 2 == 0:
            return spare[n].at[gq(i, line_size * side, line_size), :]
        return whole[i][0].at[rows_of(depth * temp * side, depth * temp), :]

    def y_box(i, n):
        if i % 2 == 0:
            return spare[n].at[inbox(i, 0, line_size), :]
        return whole[i][1].at[0 : depth * temp, :]

    def block_of(i, n, place, size):
        if i % 2 == 0:
            return spare[n].at[gq(i, line_size * par + line_row(place), size), :]
        return whole[i][0].at[rows_of(depth * temp * par + place * temp, temp), :]

    def z_box(i, n, slot, size):
        if i % 2 == 0:
            return spare[n].at[inbox(i, line_size + slot * (line_size // 3), size), :]
        return whole[i][1].at[(depth + slot) * temp : (depth + slot + 1) * temp, :]

    def sized(i, place, work):
        if i % 2:
            work(temp)
        else:
            pl.when(place != shared)(lambda: work(quarter))
            pl.when(place == shared)(lambda: work(quarter + 64))

    def t_inbox(i, n):
        return whole[i][1].at[n * temp : (n + 1) * temp, :]

    def add_into(dst, parts, step):
        rows, cols = dst.shape

        def body(n, _):
            at_rows = rows_of(n * step, step)
            value = dst[at_rows, :].astype(F32)
            for part in parts:
                value = value + part[at_rows, :].astype(F32)
            dst[at_rows, :] = value.astype(BF16)
            return 0

        lax.fori_loop(0, rows // step, body, 0)

    def y_copy(i, n):
        return rc(to_y(i, n, 1 - par), y_box(i, n), r.y_send.at[i, n], r.y_recv.at[i, n], across)

    def z_copy(i, n, d, size):
        place = lax.rem(bh + d, depth)
        dev = (h, w, 2 * place + par)
        src, dst = block_of(i, n, place, size), z_box(i, n, 3 - d, size)
        return rc(src, dst, r.z_send.at[i, n], r.z_recv.at[i, n], dev)

    def step_of(i):
        return 32 if i % 2 == 0 else 48

    def reduce_start(i, n):
        y_copy(i, n).start()

    def reduce_middle(i, n):
        y_copy(i, n).wait()
        add_into(to_y(i, n, par), [y_box(i, n)], step_of(i))
        for d in (1, 2, 3):
            sized(i, lax.rem(bh + d, depth), lambda size, d=d: z_copy(i, n, d, size).start())

    def final_part(i, n, side, core):
        place = 2 * side + core
        start = quarter * place - 64 * b + 512 * jnp.where(b > 2 * place, 1, 0)
        return outs[i][n].at[rows_of(start, quarter, 64), :]

    def extra_part(i, n):
        return outs[i][n].at[rows_of(512 * (1 - par), 64, 64), :]

    def final_copies(i, n):
        if i % 2:
            src = block_of(i, n, bh, temp)
            part = outs[i].at[h]
            return lc(src, part, r.out_sem.at[i, 0, 0]), [
                (src, part, sibling, r.cast_send.at[i, 0, 0], r.cast_recv.at[i, 0, 0])
            ]
        src = block_of(i, n, bh, quarter)
        part = final_part(i, n, w, h)
        sends = [
            (src, part, dev, r.cast_send.at[i, n, d], r.cast_recv.at[i, n, d]) for d, dev in enumerate((beside, sibling))
        ]
        return lc(src, part, r.out_sem.at[i, n, 0]), sends

    def extra_copies(i, n):
        src = spare[n].at[gq(i, line_size * par + line_row(bh) + quarter, 64), :]
        part = extra_part(i, n)
        sends = [
            (src, part, dev, r.cast_send.at[i, n, 3 + d], r.cast_recv.at[i, n, 3 + d])
            for d, dev in enumerate((beside, sibling))
        ]
        return lc(src, part, r.out_sem.at[i, n, 1]), sends

    def begin(copies):
        local, sends = copies
        for src, part, dev, one, two in sends:
            rc(src, part, one, two, dev).start()
        local.start()

    def credit(n):
        pl.semaphore_signal(r.credit.at[n], inc=1, device_id=named(beside), device_id_type=MESH)

    def credited(n):
        pl.semaphore_wait(r.credit.at[n], 1)

    def beside_copy(i):
        return rc(block_of(i, 0, bh, temp), t_inbox(i, 7), r.fin_send.at[i], r.fin_recv.at[i], beside)

    def z_span(i, n, rows):
        return to_y(i, n, 0).at[0:rows, :]

    def reduce_last(i, n):
        def add(size):
            ref = z_span(i, n, 3 * size)
            rc(ref, ref, r.z_send.at[i, n], r.z_recv.at[i, n], across).wait_recv()
            add_into(block_of(i, n, bh, size), [z_box(i, n, slot, size) for slot in range(3)], step_of(i))

        sized(i, bh, add)
        if i % 2:
            credited(i // 2)
            beside_copy(i).start()
            return
        begin(final_copies(i, n))
        pl.when(bh == shared)(lambda: begin(extra_copies(i, n)))

    def reduce_out(i):
        beside_copy(i).wait()
        add_into(block_of(i, 0, bh, temp), [t_inbox(i, 7)], 48)
        begin(final_copies(i, 0))

    def final_on(i, n):
        def move(part, d):
            rc(part, part, r.cast_send.at[i, n, d], r.cast_recv.at[i, n, d], beside).wait_recv()
            rc(part, part, r.cast_send.at[i, n, d + 2], r.cast_recv.at[i, n, d + 2], sibling).start()

        move(final_part(i, n, 1 - w, h), 0)
        pl.when(bh == shared_beside)(lambda: move(extra_part(i, n), 3))

    def reduce_wait(i, n):
        local, sends = final_copies(i, n)
        local.wait()

        def sent(rows):
            ref = z_span(i, n, rows)
            rc(ref, ref, r.z_send.at[i, n], r.z_recv.at[i, n], across).wait_send()

        if i % 2:
            sent(3 * temp)
        else:
            pl.when(bh == shared)(lambda: sent(3 * quarter))
            pl.when(bh != shared)(lambda: sent(3 * quarter + 64))
        if i % 2:
            src, part, dev, one, two = sends[0]
            rc(src, outs[i].at[1 - h], one, two, dev).wait()
            return
        for src, part, dev, one, two in sends:
            rc(src, part, one, two, dev).wait_send()

        def far(part, d):
            return rc(part, part, r.cast_send.at[i, n, d], r.cast_recv.at[i, n, d], sibling)

        far(final_part(i, n, w, 1 - h), 1).wait_recv()
        far(final_part(i, n, 1 - w, h), 2).wait_send()
        far(final_part(i, n, 1 - w, 1 - h), 2).wait_recv()
        local, sends = extra_copies(i, n)

        @pl.when(bh == shared)
        def _():
            local.wait()
            for src, part, dev, one, two in sends:
                rc(src, part, one, two, dev).wait_send()

        pl.when(bh == shared_beside)(lambda: far(extra_part(i, n), 5).wait_send())
        pl.when(bh == 2 * w + 1 - h)(lambda: far(extra_part(i, n), 4).wait_recv())
        pl.when(bh == 2 * (1 - w) + 1 - h)(lambda: far(extra_part(i, n), 5).wait_recv())

    def tile_of(ref, jh, jw):
        return ref.at[rows_of(jh * 4, 4, 4), rows_of(jw * 32, 32), :]

    def tile_own(src, dst, n):
        return lc(src.at[mine], tile_of(dst, h, w), r.tile_own.at[n])

    def tiles_start(src, dst, n):
        for j, dev in tile_group:
            rc(src.at[j], tile_of(dst, h, w), r.tile_send.at[n], r.tile_recv.at[n], dev).start()
        tile_own(src, dst, n).start()

    def tiles_wait(src, dst, n):
        three = src.at[0:3]
        rc(three, three, r.tile_send.at[n], r.tile_recv.at[n], sibling).wait()
        tile_own(src, dst, n).wait()

    xg, cg = r.x_grid, r.cot_grid
    tiles_start(r.x_tiles, xg, 0)
    gather_start(0)
    r.param[...] = total(0, mid, r.param_in[...])
    tiles_wait(r.x_tiles, xg, 0)

    def grid_chunk(ref, i):
        v = ref[lax.div(i, 4), rows_of(lax.rem(i, 4) * CHUNK, CHUNK), :]
        return v.astype(F32).reshape(2, CELL, chan)

    fill(r.xa, r.xb, lambda i: grid_chunk(xg, i), chan)

    last = steps[0]
    gather_start(1)
    for step in range(1, last):
        gather_pump(0, step)
        gather_pump(1, step)
    gather_start(2)
    gather_pump(0, last)
    gather_pump(1, last)
    gather_finish(0)

    def first_pump(n):
        pl.when(n == 1)(lambda: gather_pump(2, 1))

    conv(r.xa, r.xb, whole[0], r.mid1, first_pump)
    sums = total(1, mid, packed(*moments(r.mid1, mid), mid), [lambda: gather_pump(2, 2), lambda: gather_finish(1)])
    prepare(0, sums, mid)

    def hidden(src, n, dst):
        value = activated(src, n, mid)

        def body(i, _):
            put(dst, i, value(i))
            return 0

        loop(CHUNKS, body, 0)

    hidden(r.mid1, 0, r.v1)
    stats = temporal(0, r.v1, whole[1], r.time1, [lambda: gather_pump(2, 3)])
    sums = total(
        2, chan, packed(*stats, chan), [lambda: gather_start(3), lambda: gather_pump(2, last)]
    )
    prepare(1, sums, chan)
    fill(r.aa, r.ab, activated(r.time1, 1, chan), chan)
    gather_finish(2)
    tiles_start(r.cot_tiles, cg, 1)

    def second_pump(n):
        for step in range(1, last):
            pl.when(n == 2 * step - 1)(lambda step=step: gather_pump(3, step))

    conv(r.aa, r.ab, whole[2], r.mid2, second_pump)

    def last_piece():
        gather_pump(3, last)
        gather_finish(3)

    sums = total(3, mid, packed(*moments(r.mid2, mid), mid), [last_piece])
    prepare(2, sums, mid)
    hidden(r.mid2, 2, r.v2)
    stats = temporal(1, r.v2, whole[3], r.time2)
    shared_xq2 = share_x(0, r.aa, r.xq2)
    shared_xq1 = share_x(1, r.xa, r.xq1)
    for i in range(4):
        gather_sent(i)
    share_v2 = share(4, r.v2, r.sib_v)
    sums = total(4, chan, packed(*stats, chan), [lambda: tiles_wait(r.cot_tiles, cg, 1)])
    prepare(3, sums, chan)

    out_grid = r.out_grid

    def grid_put(ref, i, v):
        ref[lax.div(i, 4), rows_of(lax.rem(i, 4) * CHUNK, CHUNK), :] = v.reshape(CHUNK, chan).astype(ref.dtype)

    def slope(y, s):
        return s * (1.0 + y * (1.0 - s))

    def pre_body(i, carry):
        scale, shift, inv, offset = tiles(3, chan)
        v = chunk(r.time2, i)
        y = v * scale + shift + chunk(r.xa, i, MAIN)
        s = sigmoid(y)
        m = keep(i)
        grid_put(out_grid, i, y * s * m)
        d = grid_chunk(cg, i) * m * slope(y, s)
        put(r.grad_pre, i, d)
        t = d * (v * inv - offset)
        return (carry[0] + d[0] + d[1], carry[1] + t[0] + t[1])

    zero_out = jnp.zeros((CELL, chan), F32)
    zero_mid = jnp.zeros((CELL, mid), F32)
    out_grid[HGT] = jnp.zeros((8 * CELL, chan), BF16)
    gg = loop(CHUNKS, pre_body, (zero_out, zero_out))

    def send_tiles(src, dst, n):
        for j, dev in tile_group:
            jh, jw = at_group(j)
            rc(tile_of(src, jh, jw), dst.at[mine], r.tile_send.at[n], r.tile_recv.at[n], dev).start()
        lc(tile_of(src, h, w), dst.at[mine], r.tile_own.at[n]).start()

    def sent_tiles(src, dst, n):
        three = dst.at[0:3]
        rc(three, three, r.tile_send.at[n], r.tile_recv.at[n], sibling).wait()
        lc(tile_of(src, h, w), dst.at[mine], r.tile_own.at[n]).wait()

    send_tiles(out_grid, r.block_out, 2)

    def norm_back(n, sums, width):
        r.norm_part[0, 2 * n : 2 * n + 1, 0:width] = sums[1:2]
        r.norm_part[0, 2 * n + 1 : 2 * n + 2, 0:width] = sums[0:1]
        back = r.back
        back[0, :, 0:width] = jnp.broadcast_to(sums[0:1] / cell_count, (CELL, width))
        back[1, :, 0:width] = jnp.broadcast_to(sums[1:2] / cell_count, (CELL, width))

    def through_norm(n, src, grad, i, width):
        scale, _, inv, offset = tiles(n, width)
        xhat = chunk(src, i) * inv - offset
        bias_part = r.back[0, :, 0:width][None]
        gain_part = r.back[1, :, 0:width][None]
        return scale * (chunk(grad, i, 0, width) - bias_part - xhat * gain_part) * keep(i)

    def through_act(n, src, grad, width):
        def body(i, carry):
            scale, shift, inv, offset = tiles(n, width)
            v = chunk(src, i)
            y = v * scale + shift
            s = sigmoid(y)
            d = chunk(grad, i, 0, width) * keep(i) * slope(y, s)
            put(grad, i, d, 0, width)
            t = d * (v * inv - offset)
            return (carry[0] + d[0] + d[1], carry[1] + t[0] + t[1])

        zero = jnp.zeros((CELL, width), F32)
        return loop(CHUNKS, body, (zero, zero))

    def to_frames(n, src, grad):
        def body(i, _):
            e = through_norm(n, src, grad, i, chan).astype(BF16)
            ef = e.astype(F32)
            put_e(1, i, e.reshape(CHUNK, chan))
            put_lanes(r.down, rows_of(i * CHUNK + CELL, CHUNK, CELL), ef.reshape(CHUNK, chan))
            put_lanes(r.up, rows_of(i * CHUNK, CHUNK), (ef * r.gate[...][None]).reshape(CHUNK, chan))
            return 0

        loop(CHUNKS, body, 0)

    near, far = r.xt, r.xt2

    def spread():
        shared_xq2.wait()
        spread_x(r.xq2)
        shared_xq1.wait()
        spread_x(r.xq1)

    sums = total(5, chan, packed(*gg, chan), [spread])
    norm_back(3, sums, chan)
    to_frames(3, r.time2, r.grad_pre)
    shared_e3 = temporal_back(2, whole[3], [lambda: transposes(r.aa, r.ab, r.xq2, near, far)])
    credit(1)
    gg = through_act(2, r.mid2, r.grad_mid, mid)
    shared_e3.wait()
    share_v2.wait()
    def temporal_grads(i, v):
        def first():
            transpose_v(v, r.sib_v)
            temporal_grad(i, 0, 2)

        return [first, lambda: temporal_grad(i, 2, 1)]

    sums = total(6, mid, packed(*gg, mid), temporal_grads(3, r.v2))
    reduce_start(3, 0)
    norm_back(2, sums, mid)

    def fill_e(n, src):
        def value(i):
            v = through_norm(n, src, r.grad_mid, i, mid)
            for part, (c0, cw) in zip(e_all, halves):
                put(part, i, v[:, :, c0 : c0 + cw])
            return v

        fill(r.ea, r.eb, value, mid)

    fill_e(2, r.mid2)
    share_e(0)
    conv_back(r.ea, r.eb, whole[2], r.grad_mid)
    gg = through_act(1, r.time1, r.grad_mid, chan)

    def first_half():
        share_e_wait(0, 0)
        spatial_half(2, near, far, 0)

    sums = total(7, chan, packed(*gg, chan), [lambda: share_e_on(0, 0), first_half])
    reduce_start(2, 0)
    share_v1 = share(5, r.v1, r.sib_v)
    norm_back(1, sums, chan)
    to_frames(1, r.time1, r.grad_mid)
    reduce_middle(3, 0)
    share_e_on(0, 1)

    def second_half():
        share_e_wait(0, 1)
        spatial_half(2, near, far, 1)
        credit(2)
        reduce_start(2, 1)

    shared_e3 = temporal_back(3, whole[1], [second_half])
    credit(0)
    reduce_middle(2, 0)
    gg = through_act(0, r.mid1, r.grad_mid, mid)
    shared_e3.wait()
    share_v1.wait()
    sums = total(8, mid, packed(*gg, mid), temporal_grads(1, r.v1))
    reduce_start(1, 0)
    reduce_middle(2, 1)
    norm_back(0, sums, mid)
    fill_e(0, r.mid1)
    credited(2)
    share_e(1)
    reduce_last(3, 0)
    transposes(r.xa, r.xb, r.xq1, near, far)
    share_e_on(1, 0)
    reduce_out(3)
    sent_tiles(out_grid, r.block_out, 2)
    share_e_wait(1, 0)
    spatial_half(0, near, far, 0)
    reduce_start(0, 0)
    reduce_middle(1, 0)

    def pass_on(k):
        pl.when(k == 2)(lambda: share_e_on(1, 1))

    conv_back(r.ea, r.eb, whole[0], r.grad_mid, pass_on)
    share_e_wait(1, 1)
    spatial_half(0, near, far, 1)
    reduce_start(0, 1)
    reduce_middle(0, 0)

    norm_copy = rc(r.norm_part.at[0], r.norm_part.at[1], r.norm_sem.at[0], r.norm_sem.at[1], beside)
    norm_copy.start()

    def last_body(i, _):
        grid_put(out_grid, i, (chunk(r.grad_mid, i, 0, chan) + chunk(r.grad_pre, i)) * keep(i))
        return 0

    loop(CHUNKS, last_body, 0)
    send_tiles(out_grid, r.grad_input, 3)
    for n in (0, 1):
        reduce_last(2, n)
    reduce_last(1, 0)
    for n in (0, 1):
        final_on(2, n)
    reduce_out(1)
    reduce_last(0, 0)
    norm_copy.wait()
    r.norm_grads[...] = r.norm_part[0] + r.norm_part[1]
    reduce_middle(0, 1)
    final_on(0, 0)
    sent_tiles(out_grid, r.grad_input, 3)
    for n in (0, 1):
        reduce_wait(2, n)
    reduce_wait(3, 0)
    reduce_wait(1, 0)
    reduce_last(0, 1)
    final_on(0, 1)
    for n in (0, 1):
        reduce_wait(0, n)


def per_device_fast(nb, *args):
    (
        inputs,
        starts,
        first_spatial,
        first_mid_gain,
        first_mid_bias,
        first_temporal,
        first_out_gain,
        first_out_bias,
        second_spatial,
        second_mid_gain,
        second_mid_bias,
        second_temporal,
        second_out_gain,
        second_out_bias,
        cotangent,
    ) = args
    micro, frames, side, _, chan = inputs.shape
    mid = first_spatial.shape[1]
    spat, temp = first_spatial.shape[0], first_temporal.shape[0]
    h, w, b = (lax.axis_index(name) for name in ("ha", "wa", "batch"))
    few = frames // 2
    offsets = jnp.arange(side)
    valid = (h * side + offsets < HGT)[:, None] & (w * side + offsets < HGT)[None, :]

    def tiles(array):
        array = array * valid.astype(BF16)[None, None, :, :, None]
        array = array.reshape(micro, 2, few, side, side, chan).transpose(0, 1, 3, 4, 2, 5)
        return array.reshape(4, side, side * few, chan)

    def untiled(array):
        array = array.reshape(micro, 2, side, side, few, chan).transpose(0, 1, 4, 2, 3, 5)
        return array.reshape(micro, frames, side, side, chan).astype(F32)

    gate = (1 - lax.dynamic_slice(starts, (w, h * few), (1, few))).astype(F32)
    gate = jnp.broadcast_to(gate.reshape(few, 1), (few, chan))
    here = jnp.where(h == 0, 1.0, 0.0)

    def placed(shard):
        row = jnp.zeros((mid,), F32)
        return lax.dynamic_update_slice(row, shard.astype(F32) * here, (b * shard.shape[0],))

    param = jnp.stack(
        [
            placed(v)
            for v in (
                first_mid_gain,
                first_mid_bias,
                first_out_gain,
                first_out_bias,
                second_mid_gain,
                second_mid_bias,
                second_out_gain,
                second_out_bias,
            )
        ]
    )
    half = chan // 2
    few_rows = ROWS // CELL

    inputs_of = dict(
        x_tiles=(tiles(inputs), pl.ANY),
        cot_tiles=(tiles(cotangent), pl.ANY),
        gate=(gate, pltpu.VMEM),
        param_in=(param, pltpu.VMEM),
        first_spatial=(first_spatial, pl.ANY),
        first_temporal=(first_temporal, pl.ANY),
        second_spatial=(second_spatial, pl.ANY),
        second_temporal=(second_temporal, pl.ANY),
    )
    outputs_of = dict(
        block_out=((4, side, side * CELL, chan), BF16, pl.ANY),
        grad_input=((4, side, side * CELL, chan), BF16, pl.ANY),
        norm_grads=((8, mid), F32, pltpu.VMEM),
        out1s0=((spat, 512), BF16, pl.ANY),
        out1s1=((spat, mid - 512), BF16, pl.ANY),
        out1t=((2, temp, half), BF16, pl.ANY),
        out2s0=((spat, 512), BF16, pl.ANY),
        out2s1=((spat, mid - 512), BF16, pl.ANY),
        out2t=((2, temp, half), BF16, pl.ANY),
    )
    dma = pltpu.SemaphoreType.DMA
    scratch_of = dict(
        w1s0=pltpu.VMEM((9 * chan, 512), BF16),
        w1s1=pltpu.VMEM((9 * chan, mid - 512), BF16),
        w1t0=pltpu.VMEM((3 * mid, half), BF16),
        w1t1=pltpu.VMEM((3 * mid, half), BF16),
        w2s0=pltpu.VMEM((9 * chan, 512), BF16),
        w2s1=pltpu.VMEM((9 * chan, mid - 512), BF16),
        w2t0=pltpu.VMEM((3 * mid, half), BF16),
        w2t1=pltpu.VMEM((3 * mid, half), BF16),
        x_grid=pltpu.VMEM((8, 8 * CELL, chan), BF16),
        cot_grid=pltpu.VMEM((8, 8 * CELL, chan), BF16),
        out_grid=pltpu.VMEM((8, 8 * CELL, chan), BF16),
        xa=pltpu.VMEM((PADDED, chan), BF16),
        xb=pltpu.VMEM((PADDED, chan), BF16),
        aa=pltpu.VMEM((PADDED, chan), BF16),
        ab=pltpu.VMEM((PADDED, chan), BF16),
        ea=pltpu.VMEM((PADDED, mid), BF16),
        eb=pltpu.VMEM((PADDED, mid), BF16),
        mid1=pltpu.VMEM((ROWS, mid), F32),
        mid2=pltpu.VMEM((ROWS, mid), F32),
        grad_mid=pltpu.VMEM((ROWS, mid), F32),
        v1=pltpu.VMEM((ROWS, mid), BF16),
        v2=pltpu.VMEM((ROWS, mid), BF16),
        time1=pltpu.VMEM((ROWS, chan), F32),
        time2=pltpu.VMEM((ROWS, chan), F32),
        grad_pre=pltpu.VMEM((ROWS, chan), F32),
        down=pltpu.VMEM((chan // 128, ROWS + CHUNK, 128), F32),
        up=pltpu.VMEM((chan // 128, ROWS + CHUNK, 128), F32),
        e3=pltpu.VMEM((2, 3, ROWS, half), BF16),
        sib_e3=pltpu.VMEM((3, ROWS, half), BF16),
        halo_out=pltpu.VMEM((2, few_rows, chan), F32),
        halo_in=pltpu.VMEM((4, 2, few_rows, chan), F32),
        param=pltpu.VMEM((8, mid), F32),
        tile_mid=pltpu.VMEM((2, 4, CELL, mid), F32),
        tile_out=pltpu.VMEM((2, 4, CELL, chan), F32),
        back=pltpu.VMEM((2, CELL, mid), F32),
        sum_flat=pltpu.VMEM((2, 2 * nb, 8, chan // 4), F32),
        norm_part=pltpu.VMEM((2, 8, mid), F32),
        sum_b=pltpu.VMEM((2, 4, 8, mid), F32),
        sum_c=pltpu.VMEM((2, nb // 2, 8, mid), F32),
        own_sem=dma((4, 2)),
        ring_send=dma((4, 2)),
        ring_recv=dma((4, 2, 2, 2, nb // 2 + 1)),
        sib_send=dma((4, 2)),
        sib_recv=dma((4, 2)),
        over_send=dma((4, 2)),
        over_recv=dma((4, 2, 2, nb // 2 + 1)),
        norm_sem=dma((2,)),
        credit=pltpu.SemaphoreType.REGULAR((3,)),
        sb_send=dma((9,)),
        sb_recv=dma((9,)),
        sc_send=dma((9,)),
        sc_recv=dma((9,)),
        halo_send=dma((4, 2)),
        halo_recv=dma((4, 2)),
        share_send=dma((6,)),
        share_recv=dma((6,)),
        e_all0=pltpu.VMEM((4 * ROWS, 512), BF16),
        e_all1=pltpu.VMEM((4 * ROWS, mid - 512), BF16),
        xq1=pltpu.VMEM((3, 2, PADDED, chan // 4), BF16),
        xq2=pltpu.VMEM((3, 2, PADDED, chan // 4), BF16),
        xt=pltpu.VMEM((mid, 2 * ROWS), BF16),
        xt2=pltpu.VMEM((mid, 2 * ROWS), BF16),
        sib_v=pltpu.VMEM((ROWS, mid), BF16),
        e_send=dma((2, 2)),
        e_recv=dma((2, 2, 2)),
        xq_send=dma((2,)),
        xq_recv=dma((2,)),
        y_send=dma((4, 2)),
        y_recv=dma((4, 2)),
        z_send=dma((4, 2)),
        z_recv=dma((4, 2)),
        cast_send=dma((4, 2, 6)),
        cast_recv=dma((4, 2, 8)),
        out_sem=dma((4, 2, 2)),
        fin_send=dma((4,)),
        fin_recv=dma((4,)),
        tile_send=dma((4,)),
        tile_recv=dma((4,)),
        tile_own=dma((4,)),
    )
    names = (*inputs_of, *outputs_of, *scratch_of)
    cell_count = float(frames * nb * HGT * HGT)
    results = pl.pallas_call(
        functools.partial(block_kernel, (nb, chan, mid, cell_count), names),
        out_shape=[jax.ShapeDtypeStruct(shape, dtype) for shape, dtype, _ in outputs_of.values()],
        in_specs=[pl.BlockSpec(memory_space=space) for _, space in inputs_of.values()],
        out_specs=[pl.BlockSpec(memory_space=space) for _, _, space in outputs_of.values()],
        scratch_shapes=list(scratch_of.values()),
        compiler_params=pltpu.CompilerParams(
            collective_id=0, has_side_effects=True, vmem_limit_bytes=VMEM_LIMIT
        ),
    )(*(array for array, _ in inputs_of.values()))
    got = SimpleNamespace(**dict(zip(outputs_of, results)))

    def spatial(left, right):
        return jnp.concatenate([left, right], axis=1).astype(F32)

    def temporal(pair):
        return jnp.concatenate([pair[0], pair[1]], axis=1).astype(F32)

    def norm(row, like):
        size = like.shape[0]
        return lax.dynamic_slice_in_dim(got.norm_grads[row], b * size, size)

    return (
        untiled(got.block_out),
        untiled(got.grad_input),
        spatial(got.out1s0, got.out1s1),
        norm(0, first_mid_gain),
        norm(1, first_mid_bias),
        temporal(got.out1t),
        norm(2, first_out_gain),
        norm(3, first_out_bias),
        spatial(got.out2s0, got.out2s1),
        norm(4, second_mid_gain),
        norm(5, second_mid_bias),
        temporal(got.out2t),
        norm(6, second_out_gain),
        norm(7, second_out_bias),
    )


def extended(shard, sides, width):
    for axis, dim in sides:
        count, length = (lax.axis_size(axis), shard.shape[dim])
        up = [(i, (i + 1) % count) for i in range(count - 1)]
        down = [(j, i) for i, j in up]
        last = lax.slice_in_dim(shard, length - width, length, axis=dim)
        leading = lax.slice_in_dim(shard, 0, width, axis=dim)
        before = lax.ppermute(last, axis, up)
        after = lax.ppermute(leading, axis, down)
        shard = jnp.concatenate([before, shard, after], axis=dim)
    return shard


def passed_along(shard, axis, by):
    count = lax.axis_size(axis)
    pairs = [(i, i + by) for i in range(count) if 0 <= i + by < count]
    return lax.ppermute(shard, axis, pairs)


def for_sending(shard):

    def short(part):
        return part.astype(jnp.bfloat16) if part.dtype == jnp.float32 else part

    return jax.tree.map(short, shard)


def silu_slope(values):
    sigma = jax.nn.sigmoid(values)
    return sigma * (1.0 + values * (1.0 - sigma))


def spatial_forward(field_in, kernel):
    frames, tile_side = (field_in.shape[0], field_in.shape[1])
    padded = extended(field_in, (("ha", 1), ("wa", 2)), 1)
    pieces = [
        padded[:, offset // 3 : offset // 3 + tile_side, offset % 3 : offset % 3 + tile_side, :]
        for offset in range(9)
    ]
    patches = jnp.concatenate(pieces, axis=-1).reshape(frames * tile_side * tile_side, -1)
    return (patches, jnp.dot(patches, kernel, preferred_element_type=jnp.float32))


def spatial_backward(grad_out, patches, kernel):
    frames, tile_side, channels = (grad_out.shape[0], grad_out.shape[1], grad_out.shape[3])
    row_count = frames * tile_side * tile_side
    padded = extended(grad_out, (("ha", 1), ("wa", 2)), 1)
    pieces = [
        padded[
            :,
            2 - offset // 3 : 2 - offset // 3 + tile_side,
            2 - offset % 3 : 2 - offset % 3 + tile_side,
            :,
        ]
        for offset in range(9)
    ]
    stacked = jnp.concatenate(pieces, axis=-1).reshape(row_count, 9, channels)
    grad_in = jnp.einsum(
        "rkm,kcm->rc", stacked, kernel.reshape(9, -1, channels), preferred_element_type=jnp.float32
    )
    grad_kernel = jnp.einsum(
        "rk,rm->km",
        patches,
        grad_out.reshape(row_count, channels),
        preferred_element_type=jnp.float32,
    )
    return (grad_in, grad_kernel)


def temporal_forward(field_in, clip_gate, kernel):
    frames, tile_side = (field_in.shape[0], field_in.shape[1])
    gated_in = field_in * clip_gate
    earlier = passed_along(field_in[-1:], "batch", 1)
    later_frame = passed_along(gated_in[:1], "batch", -1)
    before = jnp.concatenate([earlier, field_in[:-1]], axis=0) * clip_gate
    after_tap = jnp.concatenate([gated_in[1:], later_frame], axis=0)
    joined = jnp.concatenate([before, field_in, after_tap], axis=-1).reshape(
        frames * tile_side * tile_side, -1
    )
    return (joined, jnp.dot(joined, kernel, preferred_element_type=jnp.float32))


def temporal_backward(grad_out, joined, clip_gate, kernel):
    frames, tile_side, channels = (grad_out.shape[0], grad_out.shape[1], grad_out.shape[3])
    row_count = frames * tile_side * tile_side
    gated_grad = grad_out * clip_gate
    later_frame = passed_along(gated_grad[:1], "batch", -1)
    earlier = passed_along(grad_out[-1:], "batch", 1)
    from_later = jnp.concatenate([gated_grad[1:], later_frame], axis=0)
    from_earlier = jnp.concatenate([earlier, grad_out[:-1]], axis=0) * clip_gate
    stacked = jnp.concatenate([from_later, grad_out, from_earlier], axis=-1).reshape(
        row_count, 3, channels
    )
    grad_in = jnp.einsum(
        "rkc,kmc->rm", stacked, kernel.reshape(3, -1, channels), preferred_element_type=jnp.float32
    )
    grad_kernel = jnp.einsum(
        "rk,rc->kc",
        joined,
        grad_out.reshape(row_count, channels),
        preferred_element_type=jnp.float32,
    )
    return (grad_in, grad_kernel)


def norm_forward(pre_norm, norm_gain, norm_bias, valid_rows, cell_count):
    first_sum = jnp.sum(pre_norm * valid_rows, axis=0)
    square_sum = jnp.sum(pre_norm * pre_norm * valid_rows, axis=0)
    first_sum, square_sum = lax.psum((first_sum, square_sum), ("ha", "wa", "batch"))
    mean_val = first_sum / cell_count
    inv_std = lax.rsqrt(square_sum / cell_count - mean_val * mean_val + epsilon)
    normed = (pre_norm - mean_val) * inv_std
    return (normed, inv_std, normed * norm_gain.astype(jnp.float32) + norm_bias.astype(jnp.float32))


def norm_backward(grad_norm, normed, inv_std, norm_gain, valid_rows, cell_count):
    bias_grad = jnp.sum(grad_norm, axis=0)
    gain_grad = jnp.sum(grad_norm * normed, axis=0)
    bias_grad, gain_grad = lax.psum((bias_grad, gain_grad), ("ha", "wa", "batch"))
    grad_in = (
        valid_rows
        * norm_gain.astype(jnp.float32)
        * inv_std
        * (grad_norm - bias_grad / cell_count - normed * gain_grad / cell_count)
    )
    return (grad_in, gain_grad, bias_grad)


def forward_pair(field_in, weights, clip_gate, valid_rows, cell_count):
    frames, tile_side = (field_in.shape[0], field_in.shape[1])
    patches, spatial_out = spatial_forward(field_in, weights[0])
    mid_hat, mid_scale, mid_norm = norm_forward(
        spatial_out, weights[1], weights[2], valid_rows, cell_count
    )
    hidden = (
        (jax.nn.silu(mid_norm) * valid_rows)
        .astype(jnp.bfloat16)
        .reshape(frames, tile_side, tile_side, -1)
    )
    joined, temporal_out = temporal_forward(hidden, clip_gate, weights[3])
    out_hat, out_scale, out_norm = norm_forward(
        temporal_out, weights[4], weights[5], valid_rows, cell_count
    )
    return ((patches, mid_hat, mid_scale, mid_norm, joined, out_hat, out_scale), out_norm)


def backward_pair(grad_norm, kept, weights, clip_gate, valid_rows, cell_count, tile_side):
    patches, mid_hat, mid_scale, mid_norm, joined, out_hat, out_scale = kept
    frames = clip_gate.shape[0]
    grad_time, out_gain_grad, out_bias_grad = norm_backward(
        grad_norm, out_hat, out_scale, weights[4], valid_rows, cell_count
    )
    grad_time = grad_time.astype(jnp.bfloat16).reshape(frames, tile_side, tile_side, -1)
    grad_hidden, temporal_grad = temporal_backward(grad_time, joined, clip_gate, weights[3])
    grad_mid = grad_hidden * valid_rows * silu_slope(mid_norm)
    grad_spatial, mid_gain_grad, mid_bias_grad = norm_backward(
        grad_mid, mid_hat, mid_scale, weights[1], valid_rows, cell_count
    )
    grad_spatial = grad_spatial.astype(jnp.bfloat16).reshape(frames, tile_side, tile_side, -1)
    grad_in, spatial_grad = spatial_backward(grad_spatial, patches, weights[0])
    return (
        grad_in,
        (spatial_grad, mid_gain_grad, mid_bias_grad, temporal_grad, out_gain_grad, out_bias_grad),
    )


def per_device(
    inputs,
    starts,
    first_spatial,
    first_mid_gain,
    first_mid_bias,
    first_temporal,
    first_out_gain,
    first_out_bias,
    second_spatial,
    second_mid_gain,
    second_mid_bias,
    second_temporal,
    second_out_gain,
    second_out_bias,
    cotangent,
):
    shards = (
        first_spatial,
        first_mid_gain,
        first_mid_bias,
        first_temporal,
        first_out_gain,
        first_out_bias,
        second_spatial,
        second_mid_gain,
        second_mid_bias,
        second_temporal,
        second_out_gain,
        second_out_bias,
    )
    micro_total, frames, tile_side, channels = (
        inputs.shape[0],
        inputs.shape[1],
        inputs.shape[2],
        inputs.shape[4],
    )
    row_count = frames * tile_side * tile_side
    cell_count = frames * lax.axis_size("batch") * HGT * HGT
    offsets = jnp.arange(tile_side)
    inside_h = lax.axis_index("ha") * tile_side + offsets < HGT
    inside_w = lax.axis_index("wa") * tile_side + offsets < HGT
    valid_grid = inside_h[:, None] & inside_w[None, :]
    valid_tile = valid_grid.astype(jnp.bfloat16)[None, :, :, None]
    valid_rows = jnp.broadcast_to(
        valid_grid.astype(jnp.float32)[None], (frames, tile_side, tile_side)
    ).reshape(row_count, 1)
    results = []
    input_grads = []
    kernel_total = None
    norm_total = None
    for micro_step in range(micro_total):
        gathered = (
            lax.all_gather(shards[0], "batch", axis=0, tiled=True),
            lax.all_gather(shards[1], "batch", axis=0, tiled=True),
            lax.all_gather(shards[2], "batch", axis=0, tiled=True),
            lax.all_gather(shards[3], "batch", axis=0, tiled=True),
            lax.all_gather(shards[4], "batch", axis=0, tiled=True),
            lax.all_gather(shards[5], "batch", axis=0, tiled=True),
            lax.all_gather(shards[6], "batch", axis=0, tiled=True),
            lax.all_gather(shards[7], "batch", axis=0, tiled=True),
            lax.all_gather(shards[8], "batch", axis=0, tiled=True),
            lax.all_gather(shards[9], "batch", axis=0, tiled=True),
            lax.all_gather(shards[10], "batch", axis=0, tiled=True),
            lax.all_gather(shards[11], "batch", axis=0, tiled=True),
        )
        clip_gate = (1 - starts[micro_step]).astype(jnp.bfloat16).reshape(frames, 1, 1, 1)
        x_in = inputs[micro_step] * valid_tile
        first_kept, first_norm = forward_pair(
            x_in, gathered[0:6], clip_gate, valid_rows, cell_count
        )
        first_act = (
            (jax.nn.silu(first_norm) * valid_rows)
            .astype(jnp.bfloat16)
            .reshape(frames, tile_side, tile_side, channels)
        )
        second_kept, second_norm = forward_pair(
            first_act, gathered[6:12], clip_gate, valid_rows, cell_count
        )
        pre_out = second_norm + x_in.reshape(row_count, channels).astype(jnp.float32)
        results.append(
            (jax.nn.silu(pre_out) * valid_rows).reshape(frames, tile_side, tile_side, channels)
        )
        grad_pre = (
            cotangent[micro_step].reshape(row_count, channels).astype(jnp.float32)
            * valid_rows
            * silu_slope(pre_out)
        )
        grad_act, second_grads = backward_pair(
            grad_pre, second_kept, gathered[6:12], clip_gate, valid_rows, cell_count, tile_side
        )
        grad_first = grad_act * valid_rows * silu_slope(first_norm)
        grad_conv, first_grads = backward_pair(
            grad_first, first_kept, gathered[0:6], clip_gate, valid_rows, cell_count, tile_side
        )
        input_grads.append(
            ((grad_conv + grad_pre) * valid_rows).reshape(frames, tile_side, tile_side, channels)
        )
        step_grads = first_grads + second_grads
        kernel_now = (step_grads[0], step_grads[3], step_grads[6], step_grads[9])
        norm_now = (
            step_grads[1],
            step_grads[2],
            step_grads[4],
            step_grads[5],
            step_grads[7],
            step_grads[8],
            step_grads[10],
            step_grads[11],
        )
        if micro_step == 0:
            kernel_total = kernel_now
            norm_total = norm_now
        else:
            kernel_total = jax.tree.map(jnp.add, kernel_total, kernel_now)
            norm_total = jax.tree.map(jnp.add, norm_total, norm_now)
    kernel_total = lax.psum_scatter(kernel_total, "batch", scatter_dimension=0, tiled=True)
    kernel_total = jax.tree.map(
        lambda part: part.astype(jnp.float32), lax.psum(for_sending(kernel_total), ("ha", "wa"))
    )
    shard_index = lax.axis_index("batch")
    batch_count = lax.axis_size("batch")
    norm_shards = tuple(
        (
            lax.dynamic_slice_in_dim(
                full_sum,
                shard_index * (full_sum.shape[0] // batch_count),
                full_sum.shape[0] // batch_count,
            )
            for full_sum in norm_total
        )
    )
    return (
        jnp.stack(results),
        jnp.stack(input_grads),
        kernel_total[0],
        norm_shards[0],
        norm_shards[1],
        kernel_total[1],
        norm_shards[2],
        norm_shards[3],
        kernel_total[2],
        norm_shards[4],
        norm_shards[5],
        kernel_total[3],
        norm_shards[6],
        norm_shards[7],
    )


def solution(mesh):
    in_specs = (
        P(None, "batch", "ha", "wa", None),
        P(None, "batch"),
        P("batch", None),
        P("batch"),
        P("batch"),
        P("batch", None),
        P("batch"),
        P("batch"),
        P("batch", None),
        P("batch"),
        P("batch"),
        P("batch", None),
        P("batch"),
        P("batch"),
        P(None, "batch", "ha", "wa", None),
    )
    out_specs = (
        P(None, "batch", "ha", "wa", None),
        P(None, "batch", "ha", "wa", None),
        P("batch", None),
        P("batch"),
        P("batch"),
        P("batch", None),
        P("batch"),
        P("batch"),
        P("batch", None),
        P("batch"),
        P("batch"),
        P("batch", None),
        P("batch"),
        P("batch"),
    )
    batch = mesh.shape["batch"]

    def program(*args):
        spat, temp = args[2].shape[0], args[5].shape[0]
        fits = args[0].shape == (2, 16, 4, 4, 512) and args[2].shape[1] == 1152
        if fits and batch == 8 and spat * batch == 9 * 512 and temp * batch == 3 * 1152:
            return per_device_fast(batch, *args)
        return per_device(*args)

    return jax.shard_map(
        program, mesh=mesh, in_specs=in_specs, out_specs=out_specs, check_vma=False
    )
```

```python
import functools
from types import SimpleNamespace

import jax
import jax.numpy as jnp
from jax import lax
from jax.experimental import pallas as pl
from jax.experimental.pallas import tpu as pltpu
from jax.sharding import PartitionSpec as P

HGT = 7
epsilon = 1e-05
MESH = pl.DeviceIdType.MESH
F32 = jnp.float32
BF16 = jnp.bfloat16

BASE = 10
CELL = 8
ROWS = HGT * 8 * CELL
PADDED = (BASE + HGT * 8 + BASE) * CELL
MAIN = BASE * CELL
CHUNK = 2 * CELL
CHUNKS = ROWS // CHUNK
VMEM_LIMIT = 64 * 1024 * 1024 - 1024 * 1024


def when(cond, work):
    if cond is True:
        work()
    elif cond is not False:
        pl.when(cond)(work)


def loop(count, body, init):
    def twice(i, carry):
        return body(2 * i + 1, body(2 * i, carry))

    return lax.fori_loop(0, count // 2, twice, init)


def sigmoid(x):
    return 0.5 * jnp.tanh(0.5 * x) + 0.5


def nn(a, b):
    return jnp.dot(a, b, preferred_element_type=F32)


def nt(a, b):
    return lax.dot_general(a, b, (((1,), (1,)), ((), ())), preferred_element_type=F32)


def tn(a, b):
    return lax.dot_general(a, b, (((0,), (0,)), ((), ())), preferred_element_type=F32)


def rows_of(start, size, step=16):
    if not isinstance(start, int):
        start = pl.multiple_of(start, step)
    return pl.ds(start, size)


def block_kernel(dims, names, *all_refs):
    r = SimpleNamespace(**dict(zip(names, all_refs, strict=True)))
    nb, chan, mid, cell_count = dims
    spat = 9 * chan // nb
    temp = 3 * mid // nb
    unit = spat // 6
    quarter = chan // 4
    half = chan // 2
    h = lax.axis_index("ha")
    w = lax.axis_index("wa")
    b = lax.axis_index("batch")
    par = lax.rem(b, 2)
    bh = lax.div(b, 2)
    pos = par * (nb - 1 - bh) + (1 - par) * bh

    def at(p):
        p = lax.rem(p + 4 * nb, nb)
        upper = lax.div(p, nb // 2)
        return (1 - upper) * (2 * p) + upper * (2 * (nb - 1 - p) + 1)

    def at_group(j):
        return (lax.rem(j, 2), lax.div(j, 2))

    mine = 2 * w + h
    sibling = (1 - h, w, b)
    beside = (h, 1 - w, b)
    later_dev = (1 - h, w, lax.rem(b + h, nb))
    earlier_dev = (1 - h, w, lax.rem(b + nb - 1 + h, nb))
    tile_group = [(lax.rem(mine + d, 4), (*at_group(lax.rem(mine + d, 4)), b)) for d in (1, 2, 3)]
    across = (h, w, b + 1 - 2 * par)
    pos_b = h * 2 + par
    plane = []
    for d in (1, 2, 3):
        q = lax.rem(pos_b + d, 4)
        plane.append((q, (lax.div(q, 2), w, b - par + lax.rem(q, 2))))
    depth = nb // 2
    place = (h * 2 + par) * depth + bh
    crowd = []
    for d in range(1, 2 * nb):
        q = lax.rem(place + d, 2 * nb)
        side, far = lax.div(q, depth), lax.rem(q, depth)
        crowd.append((lax.div(side, 2), w, 2 * far + lax.rem(side, 2)))
    line = []
    for d in range(1, depth):
        q = lax.rem(bh + d, depth)
        line.append((q, (h, w, 2 * q + par)))

    def named(dev):
        return dict(ha=dev[0], wa=dev[1], batch=dev[2])

    def rc(src, dst, send, recv, dev):
        return pltpu.make_async_remote_copy(
            src_ref=src, dst_ref=dst, send_sem=send, recv_sem=recv, device_id=named(dev), device_id_type=MESH
        )

    def lc(src, dst, sem):
        return pltpu.make_async_copy(src, dst, sem)

    partners = []
    partners += [dev for _, dev in tile_group] + crowd
    barrier = pltpu.get_barrier_semaphore()
    for dev in partners:
        pl.semaphore_signal(barrier, inc=1, device_id=named(dev), device_id_type=MESH)
    pl.semaphore_wait(barrier, len(partners))

    shards = (r.first_spatial, r.first_temporal, r.second_spatial, r.second_temporal)
    whole = ((r.w1s0, r.w1s1), (r.w1t0, r.w1t1), (r.w2s0, r.w2s1), (r.w2t0, r.w2t1))
    halves = ((0, 512), (512, mid - 512))
    shared = 2 * w + h
    shared_beside = 2 * (1 - w) + h
    way = 1 - 2 * h
    ways = (way, -way)
    onward = [(h, w, at(pos + d)) for d in ways]
    steps = (nb // 2, nb // 2 - 1)
    third = temp // 3

    def taken(i, core, side):
        if i % 2 == 0:
            return 3 * unit * core + unit * side, 2 * unit
        return (1 - core) * 2 * third * side + core * third, third

    def crosses(i, core, side):
        if i % 2 == 0:
            return 3 * unit * core + 2 * unit * side, unit
        return 2 * third * side, third

    def rows_in(i, c, owner, part):
        size = spat if i % 2 == 0 else temp
        return whole[i][c].at[rows_of(owner * size + part[0], part[1]), :]

    def rows_from(i, c, part):
        c0, cw = halves[c] if i % 2 == 0 else (c * half, half)
        return shards[i].at[rows_of(part[0], part[1]), c0 : c0 + cw]

    def pieces(i):
        start, size = taken(i, h, w)
        if i % 2:
            return ((start, size),)
        return ((start, size // 2), (start + size // 2, size // 2))

    def crossing(i, work):
        if i % 2 == 0:
            work()
        else:
            pl.when(h == 0)(work)

    def own_copy(i, c):
        rows = spat if i % 2 == 0 else temp
        return lc(rows_from(i, c, (0, rows)), rows_in(i, c, b, (0, rows)), r.own_sem.at[i, c])

    def ring(i, c, k, d, s, owner, from_shard=False):
        part = pieces(i)[k]
        dst = rows_in(i, c, owner, part)
        src = rows_from(i, c, part) if from_shard else dst
        return rc(src, dst, r.ring_send.at[i, c], r.ring_recv.at[i, c, k, d, s], onward[d])

    def cross(i, c, owner, part):
        ref = rows_in(i, c, owner, part)
        return rc(ref, ref, r.sib_send.at[i, c], r.sib_recv.at[i, c], sibling)

    def over(i, c, d, s, owner, part):
        ref = rows_in(i, c, owner, part)
        return rc(ref, ref, r.over_send.at[i, c], r.over_recv.at[i, c, d, s], beside)

    def gather_start(i):
        for k in range(len(pieces(i))):
            for d in (0, 1):
                for c in (0, 1):
                    ring(i, c, k, d, 1, b, True).start()
        for c in (0, 1):
            own_copy(i, c).start()

    def owners(s):
        return [(d, at(pos - ways[d] * s)) for d in (0, 1) if s <= steps[d]]

    def gather_relay(i, s):
        def work():
            part = crosses(i, h, 1 - w)
            for d, owner in owners(s):
                for c in (0, 1):
                    over(i, c, d, s, owner, part).wait_recv()
                    cross(i, c, owner, part).start()

        crossing(i, work)

    def gather_pump(i, s):
        for k in range(len(pieces(i))):
            for d, owner in owners(s):
                for c in (0, 1):
                    ring(i, c, k, d, s, owner).wait_recv()
                    if s < steps[d]:
                        ring(i, c, k, d, s + 1, owner).start()
        for d, owner in owners(s):
            for c in (0, 1):
                crossing(i, lambda c=c, d=d, owner=owner: over(i, c, d, s, owner, crosses(i, h, w)).start())
                cross(i, c, owner, taken(i, h, w)).start()
        if s > 1:
            gather_relay(i, s - 1)

    def span(i, c, size):
        return whole[i][c].at[0 : (nb - 1) * size, :]

    def gather_finish(i):
        gather_relay(i, steps[0])

        def arrived(size):
            for c in (0, 1):
                ref = span(i, c, size)
                rc(ref, ref, r.sib_send.at[i, c], r.sib_recv.at[i, c], sibling).wait_recv()

        if i % 2 == 0:
            arrived(3 * unit)
        else:
            pl.when(h == 0)(lambda: arrived(third))
            pl.when(h == 1)(lambda: arrived(2 * third))
        for c in (0, 1):
            own_copy(i, c).wait()

    def gather_sent(i):
        def sent(size, sem):
            for c in (0, 1):
                ref = span(i, c, size)
                rc(ref, ref, sem.at[i, c], r.own_sem.at[i, c], sibling).wait_send()

        sent(taken(i, h, w)[1], r.ring_send)
        crossing(i, lambda: sent(crosses(i, h, w)[1], r.over_send))
        if i % 2 == 0:
            sent(3 * unit, r.sib_send)
        else:
            pl.when(h == 0)(lambda: sent(2 * third, r.sib_send))
            pl.when(h == 1)(lambda: sent(third, r.sib_send))

    def total(k, width, value, works=()):
        slot = k % 2
        if width == chan:
            flat, me = r.sum_flat, pos_b * depth + bh
            flat[slot, me] = value
            for dev in crowd:
                part = flat.at[slot, me]
                rc(part, part, r.sb_send.at[k], r.sb_recv.at[k], dev).start()
            for work in works:
                if work:
                    work()
            ref = flat.at[slot, 0 : len(crowd)]
            every = rc(ref, ref, r.sb_send.at[k], r.sb_recv.at[k], sibling)
            every.wait_recv()
            result = jnp.sum(flat[slot], axis=0)
            every.wait_send()
            return jnp.concatenate([result[2 * n : 2 * n + 2] for n in range(4)], axis=1)
        wide = value.shape[1]
        cols = pl.ds(0, wide)
        works = list(works) + [None] * 2
        four, far = r.sum_b, r.sum_c
        four[slot, pos_b, :, cols] = value

        def phase(ref, me, group, send, recv, work):
            for _, dev in group:
                part = ref.at[slot, me, :, cols]
                rc(part, part, send.at[k], recv.at[k], dev).start()
            if work:
                work()
            ref = ref.at[slot, 0 : len(group), :, cols]
            every = rc(ref, ref, send.at[k], recv.at[k], sibling)
            every.wait_recv()
            return every

        first = phase(four, pos_b, plane, r.sb_send, r.sb_recv, works[0])
        far[slot, bh, :, cols] = (four[slot, 0, :, cols] + four[slot, 1, :, cols]) + (
            four[slot, 2, :, cols] + four[slot, 3, :, cols]
        )
        second = phase(far, bh, line, r.sc_send, r.sc_recv, works[1])
        result = far[slot, 0, :, cols]
        for q in range(1, depth):
            result = result + far[slot, q, :, cols]
        first.wait_send()
        second.wait_send()
        if wide == width:
            return result
        return jnp.concatenate([result[2 * n : 2 * n + 2] for n in range(width // wide)], axis=1)

    def chunk(ref, i, base=0, width=None):
        cols = slice(None) if width is None else pl.ds(0, width)
        value = ref[rows_of(base + i * CHUNK, CHUNK), cols]
        return value.astype(F32).reshape(2, CELL, value.shape[-1])

    def put(ref, i, value, base=0, width=None):
        cols = slice(None) if width is None else pl.ds(0, width)
        ref[rows_of(base + i * CHUNK, CHUNK), cols] = value.reshape(CHUNK, value.shape[-1]).astype(ref.dtype)

    def keep(i):
        inside = jnp.where(lax.rem(i, 4) == 3, 0.0, 1.0).astype(F32)
        first = lax.broadcasted_iota(jnp.int32, (2, 1, 1), 0) == 0
        return jnp.where(first, 1.0, inside)

    def packed(one, two, width):
        rows = jnp.concatenate([jnp.sum(v, axis=0, keepdims=True) for v in (one, two)], axis=0)
        wide = 384 if width == mid else 128
        parts = [rows[:, n * wide : (n + 1) * wide] for n in range(width // wide)]
        return jnp.concatenate((parts + parts[-1:])[0:4], axis=0)

    def moments(ref, width):
        def body(i, carry):
            v = chunk(ref, i)
            m = v * keep(i)
            return (carry[0] + m[0] + m[1], carry[1] + m[0] * v[0] + m[1] * v[1])

        zero = jnp.zeros((CELL, width), F32)
        return loop(CHUNKS, body, (zero, zero))

    def prepare(n, sums, width):
        tile = r.tile_mid if width == mid else r.tile_out
        n2 = n // 2
        gain = r.param[2 * n : 2 * n + 1, 0:width]
        bias = r.param[2 * n + 1 : 2 * n + 2, 0:width]
        mean = sums[0:1] / cell_count
        inv = lax.rsqrt(sums[1:2] / cell_count - mean * mean + epsilon)
        scale = inv * gain
        shift = bias - mean * scale
        for k, v in enumerate((scale, shift, inv, mean * inv)):
            tile[n2, k] = jnp.broadcast_to(v, (CELL, width))

    def tiles(n, width):
        tile = r.tile_mid if width == mid else r.tile_out
        return [tile[n // 2, k][None] for k in range(4)]

    def fill(ref_a, ref_b, value_of, width):
        pads(ref_a, ref_b, width)

        def body(i, before):
            v = value_of(i)
            put(ref_a, i, v, MAIN)
            pair = jnp.concatenate([before[None], v[0:1]], axis=0)
            put(ref_b, i, pair, MAIN - CHUNK)
            return v[1]

        loop(CHUNKS, body, jnp.zeros((CELL, width), F32))

    def activated(src, n, width):
        def value(i):
            scale, shift, _, _ = tiles(n, width)
            y = chunk(src, i) * scale + shift
            return y * sigmoid(y) * keep(i)

        return value

    def taps(ref_a, ref_b, k, size=ROWS):
        r0 = MAIN - 8 * CELL + 8 * CELL * k
        return (
            ref_b[rows_of(r0 - CHUNK, size), :],
            ref_a[rows_of(r0, size), :],
            ref_b[rows_of(r0, size), :],
        )

    def conv(ref_a, ref_b, weight, out, pump=None):
        for n, (c0, cw) in enumerate(halves):

            def body(a, _, c0=c0, cw=cw, n=n):
                x = taps(ref_a, ref_b, a)
                acc = nn(jnp.concatenate(x, axis=1), weight[n][rows_of(a * 3 * chan, 3 * chan), :])

                @pl.when(a == 0)
                def _():
                    out[:, c0 : c0 + cw] = acc

                @pl.when(a > 0)
                def _():
                    out[:, c0 : c0 + cw] += acc

                if pump is not None:
                    pump(n * 3 + a)
                return 0

            lax.fori_loop(0, 3, body, 0)

    def conv_back(ref_a, ref_b, weight, out, pump=None):
        def body(k, _):
            e = taps(ref_a, ref_b, k)
            acc = None
            for j in range(3):
                tap = 8 - 3 * k - j
                for n, (c0, cw) in enumerate(halves):
                    term = nt(e[j][:, c0 : c0 + cw], weight[n][rows_of(tap * chan, chan), :])
                    acc = term if acc is None else acc + term

            @pl.when(k == 0)
            def _():
                out[:, 0:chan] = acc

            @pl.when(k > 0)
            def _():
                out[:, 0:chan] += acc

            if pump is not None:
                pump(k)
            return 0

        lax.fori_loop(0, 3, body, 0)

    def send_frames(k, which=(0, 1)):
        down, up = r.down, r.up
        count = ROWS // CELL
        copies = []
        for n in which:
            for c in range(chan // 128):
                lanes = pl.ds(128 * c, 128)
                if n == 0:
                    r.halo_out[0, :, lanes] = down[c, pl.ds(2 * CELL - 1, count, stride=CELL), :]
                else:
                    r.halo_out[1, :, lanes] = up[c, pl.ds(0, count, stride=CELL), :]
            dev = (later_dev, earlier_dev)[n]
            copies.append(
                rc(r.halo_out.at[n], r.halo_in.at[k, n], r.halo_send.at[k, n], r.halo_recv.at[k, n], dev)
            )
            copies[-1].start()
        return copies

    def take_frames(k, copies):
        down, up = r.down, r.up
        count = ROWS // CELL
        for copy in copies:
            copy.wait()
        at_start = jnp.logical_and(h == 0, b == 0)
        at_end = jnp.logical_and(h == 1, b == nb - 1)
        for c in range(chan // 128):
            lanes = pl.ds(128 * c, 128)
            before = r.halo_in[k, 0, :, lanes]
            after = r.halo_in[k, 1, :, lanes]
            down[c, pl.ds(CELL - 1, count, stride=CELL), :] = jnp.where(at_start, 0.0, before)
            up[c, pl.ds(CELL, count, stride=CELL), :] = jnp.where(at_end, 0.0, after)

    def by_lanes(ref, rows):
        return jnp.concatenate([ref[c, rows, :] for c in range(chan // 128)], axis=1)

    def put_lanes(ref, rows, value):
        for c in range(chan // 128):
            ref[c, rows, :] = value[:, 128 * c : 128 * c + 128]

    def shifted(i):
        before = by_lanes(r.down, rows_of(i * CHUNK, CHUNK + CELL))[CELL - 1 : CELL - 1 + CHUNK]
        after = by_lanes(r.up, rows_of(i * CHUNK, CHUNK + CELL))[1 : 1 + CHUNK]
        gate = r.param_in[CELL : 2 * CELL, 0:chan][None]
        return (before.reshape(2, CELL, chan) * gate, after.reshape(2, CELL, chan))

    def both_halves(weight, start, size):
        return jnp.concatenate([part[start : start + size, :] for part in weight], axis=1)

    def temporal(k, v, weight, out, works=()):
        works = list(works) + [None] * 2
        put_lanes(r.down, pl.ds(CELL, ROWS), nn(v[...], both_halves(weight, 0, mid)))
        copies = send_frames(k, (0,))
        y2 = nn(v[...], both_halves(weight, 2 * mid, mid))
        y2 = (y2.reshape(ROWS // CELL, CELL, chan) * r.param_in[CELL : 2 * CELL, 0:chan][None]).reshape(ROWS, chan)
        put_lanes(r.up, pl.ds(0, ROWS), y2)
        copies += send_frames(k, (1,))
        out[...] = nn(v[...], both_halves(weight, mid, mid))
        if works[0]:
            works[0]()
        take_frames(k, copies)

        def body(i, carry):
            before, after = shifted(i)
            value = chunk(out, i) + before + after
            put(out, i, value)
            m = value * keep(i)
            return (carry[0] + m[0] + m[1], carry[1] + m[0] * value[0] + m[1] * value[1])

        zero = jnp.zeros((CELL, chan), F32)
        return loop(CHUNKS, body, (zero, zero))

    def put_e(tap, i, e):
        for c in (0, 1):
            r.e3[c, tap, rows_of(i * CHUNK, CHUNK), :] = e[:, c * half : (c + 1) * half]

    def temporal_back(k, weight, works=()):
        works = list(works) + [None] * 2
        copies = send_frames(k)
        e3 = r.e3

        def e_tap(n):
            return jnp.concatenate([e3[0, n], e3[1, n]], axis=1)

        for c0, cw in ((0, 512), (512, mid - 512)):
            r.grad_mid[:, c0 : c0 + cw] = nt(e_tap(1), both_halves(weight, mid + c0, cw))
        if works[0]:
            works[0]()
        take_frames(k, copies)

        def body(i, _):
            before, after = shifted(i)
            put_e(0, i, after.reshape(CHUNK, chan).astype(BF16))
            put_e(2, i, before.reshape(CHUNK, chan).astype(BF16))
            return 0

        loop(CHUNKS, body, 0)
        share = share_e3(k)
        for c0, cw in ((0, 512), (512, mid - 512)):
            r.grad_mid[:, c0 : c0 + cw] += nt(e_tap(0), both_halves(weight, c0, cw)) + nt(
                e_tap(2), both_halves(weight, 2 * mid + c0, cw)
            )
        return share

    def share(k, src, dst):
        copy = rc(src, dst, r.share_send.at[k], r.share_recv.at[k], sibling)
        copy.start()
        return copy

    outs = ((r.out1s0, r.out1s1), r.out1t, (r.out2s0, r.out2s1), r.out2t)

    e_all = (r.e_all0, r.e_all1)

    def e_part(n, slot):
        return e_all[n].at[slot * ROWS : (slot + 1) * ROWS, :]

    def e_copies(k, n):
        send, near, over = r.e_send.at[k, n], r.e_recv.at[k, n, 0], r.e_recv.at[k, n, 1]
        return [
            rc(e_part(n, 0), e_part(n, 1), send, near, sibling),
            rc(e_part(n, 0), e_part(n, 2), send, over, beside),
            rc(e_part(n, 2), e_part(n, 3), send, near, sibling),
        ]

    def share_e(k):
        for n in (0, 1):
            near, over, _ = e_copies(k, n)
            over.start()
            near.start()

    def share_e_on(k, n):
        _, over, far = e_copies(k, n)
        over.wait_recv()
        far.start()

    def share_e_wait(k, n):
        both = e_all[n].at[0 : 2 * ROWS, :]
        rc(both, both, r.e_send.at[k, n], r.e_recv.at[k, n, 0], sibling).wait_recv()
        three = e_all[n].at[0 : 3 * ROWS, :]
        rc(three, three, r.e_send.at[k, n], r.e_recv.at[k, n, 0], sibling).wait_send()

    def share_x(k, xa, xq):
        main = pl.ds(MAIN, ROWS)
        for n, dev in enumerate((sibling, beside, (1 - h, 1 - w, b))):
            lanes = rows_of((2 * dev[1] + dev[0]) * quarter, quarter, 128)
            rc(xa.at[main, lanes], xq.at[n, 0, main, :], r.xq_send.at[k], r.xq_recv.at[k], dev).start()
        all_three = xq.at[:, 0, main, :]
        return rc(all_three, all_three, r.xq_send.at[k], r.xq_recv.at[k], sibling)

    def pads(ref_a, ref_b, width):
        ref_a[0:MAIN, :] = jnp.zeros((MAIN, width), BF16)
        ref_a[MAIN + ROWS : PADDED, :] = jnp.zeros((PADDED - MAIN - ROWS, width), BF16)
        ref_b[0 : MAIN - CHUNK, :] = jnp.zeros((MAIN - CHUNK, width), BF16)
        ref_b[MAIN - CHUNK + ROWS : PADDED, :] = jnp.zeros((PADDED - MAIN + CHUNK - ROWS, width), BF16)

    def spread_x(xq):
        for n in range(3):
            pads(xq.at[n, 0], xq.at[n, 1], quarter)

        def body(i, before):
            after = []
            for n in range(3):
                v = chunk(xq.at[n, 0], i, MAIN)
                put(xq.at[n, 1], i, jnp.concatenate([before[n][None], v[0:1]], axis=0), MAIN - CHUNK)
                after.append(v[1])
            return tuple(after)

        loop(CHUNKS, body, (jnp.zeros((CELL, quarter), F32),) * 3)

    def share_e3(k):
        return share(
            k - 2, r.e3.at[1 - h], r.sib_e3
        )

    def line_row(place):
        return quarter * place + 64 * jnp.where(place > shared, 1, 0)

    def grad_row(tap, side):
        split = 2 * shared + 1
        owner = jnp.where(tap == split, 2 * shared + side, tap - jnp.where(tap > split, 1, 0))
        row = line_row(lax.div(owner, 2)) + jnp.where(tap == split, quarter, 64 * side)
        return 576 * lax.rem(owner, 2) + row

    spare = whole[2]

    def gq(i, row, size):
        return rows_of((mid if i == 0 else 0) + row, size, 64)

    def inbox(i, row, size):
        return rows_of(2 * mid + (mid if i == 0 else 0) + row, size, 64)

    def transpose_x(a, xa, xb, xq, near, far, row):
        lanes = rows_of(shared * quarter, quarter, 128)
        r0 = MAIN - 8 * CELL + 8 * CELL * a
        for j, (c, start) in enumerate(((1, r0 - CHUNK), (0, r0), (1, r0))):
            rows = rows_of(start, ROWS)
            own = (xb if c else xa)[rows, lanes]
            both = jnp.concatenate([own, xq[0, c, rows, :]], axis=0)
            near[rows_of(row + j * quarter, quarter), 0 : 2 * ROWS] = both.T
            both = jnp.concatenate([xq[1, c, rows, :], xq[2, c, rows, :]], axis=0)
            far[rows_of(row + j * quarter, quarter), 0 : 2 * ROWS] = both.T

    def spatial_part(i, near, far, a, n):
        size = mid // 2
        rows = rows_of(a * size, size)
        acc = nn(near[rows, :], e_all[n][0 : 2 * ROWS, :])
        acc += nn(far[rows, :], e_all[n][2 * ROWS : 4 * ROWS, :])
        acc = acc.astype(BF16)
        for j in range(size // 64):
            part = a * (size // 64) + j
            row = grad_row(lax.div(part, 2), lax.rem(part, 2))
            spare[n][gq(i, row, 64), :] = acc[64 * j : 64 * j + 64]

    def transposes(xa, xb, xq, near, far):
        def body(a, _):
            transpose_x(a, xa, xb, xq, near, far, a * 3 * quarter)
            return 0

        lax.fori_loop(0, 3, body, 0)

    def spatial_half(i, near, far, n):
        def body(a, _):
            spatial_part(i, near, far, a, n)
            return 0

        lax.fori_loop(0, 2, body, 0)

    def transpose_v(v, sv):
        for c in range(mid // 128):
            lanes = pl.ds(128 * c, 128)
            turned = jnp.concatenate([v[:, lanes], sv[:, lanes]], axis=0).T
            for row in (0, 64):
                ref = r.ea if 128 * c + row < mid // 2 else r.eb
                at_row = (128 * c + row) % (mid // 2)
                ref[at_row : at_row + 64, 0 : 2 * ROWS] = turned[row : row + 64]

    def temporal_grad(i, first, count):
        taps_of = [jnp.concatenate([r.e3[h, k], r.sib_e3[k]], axis=0) for k in range(first, first + count)]
        e = jnp.concatenate(taps_of, axis=1)
        whole_tap = mid // third
        for top in range(0, whole_tap, whole_tap // 2):
            acc = nn((r.eb if top else r.ea)[0 : mid // 2, 0 : 2 * ROWS], e).astype(BF16)
            for k in range(count):
                for n in range(whole_tap // 2):
                    owner, part = divmod((first + k) * whole_tap + top + n, 3)
                    row = (owner % 2) * (depth * temp) + owner // 2 * temp + part * third
                    whole[i][0][row : row + third, :] = acc[n * third : n * third + third, k * half : (k + 1) * half]

    def parts_of(i):
        return (0, 1) if i % 2 == 0 else (0,)

    line_size = 576

    def to_y(i, n, side):
        if i % 2 == 0:
            return spare[n].at[gq(i, line_size * side, line_size), :]
        return whole[i][0].at[rows_of(depth * temp * side, depth * temp), :]

    def y_box(i, n):
        if i % 2 == 0:
            return spare[n].at[inbox(i, 0, line_size), :]
        return whole[i][1].at[0 : depth * temp, :]

    def block_of(i, n, place, size):
        if i % 2 == 0:
            return spare[n].at[gq(i, line_size * par + line_row(place), size), :]
        return whole[i][0].at[rows_of(depth * temp * par + place * temp, temp), :]

    def z_box(i, n, slot, size):
        if i % 2 == 0:
            return spare[n].at[inbox(i, line_size + slot * (line_size // 3), size), :]
        return whole[i][1].at[(depth + slot) * temp : (depth + slot + 1) * temp, :]

    def sized(i, place, work):
        if i % 2:
            work(temp)
        else:
            pl.when(place != shared)(lambda: work(quarter))
            pl.when(place == shared)(lambda: work(quarter + 64))

    def t_inbox(i, n):
        return whole[i][1].at[n * temp : (n + 1) * temp, :]

    def add_into(dst, parts, step):
        rows, cols = dst.shape

        def body(n, _):
            at_rows = rows_of(n * step, step)
            value = dst[at_rows, :].astype(F32)
            for part in parts:
                value = value + part[at_rows, :].astype(F32)
            dst[at_rows, :] = value.astype(BF16)
            return 0

        lax.fori_loop(0, rows // step, body, 0)

    def y_copy(i, n):
        return rc(to_y(i, n, 1 - par), y_box(i, n), r.y_send.at[i, n], r.y_recv.at[i, n], across)

    def z_copy(i, n, d, size):
        place = lax.rem(bh + d, depth)
        dev = (h, w, 2 * place + par)
        src, dst = block_of(i, n, place, size), z_box(i, n, 3 - d, size)
        return rc(src, dst, r.z_send.at[i, n], r.z_recv.at[i, n], dev)

    def step_of(i):
        return 32 if i % 2 == 0 else 48

    def reduce_start(i, n):
        y_copy(i, n).start()

    def reduce_middle(i, n):
        y_copy(i, n).wait()
        add_into(to_y(i, n, par), [y_box(i, n)], step_of(i))
        for d in (1, 2, 3):
            sized(i, lax.rem(bh + d, depth), lambda size, d=d: z_copy(i, n, d, size).start())

    def final_part(i, n, side, core):
        place = 2 * side + core
        start = quarter * place - 64 * b + 512 * jnp.where(b > 2 * place, 1, 0)
        return outs[i][n].at[rows_of(start, quarter, 64), :]

    def extra_part(i, n):
        return outs[i][n].at[rows_of(512 * (1 - par), 64, 64), :]

    def final_copies(i, n):
        if i % 2:
            src = block_of(i, n, bh, temp)
            part = outs[i].at[h]
            return lc(src, part, r.out_sem.at[i, 0, 0]), [
                (src, part, sibling, r.cast_send.at[i, 0, 0], r.cast_recv.at[i, 0, 0])
            ]
        src = block_of(i, n, bh, quarter)
        part = final_part(i, n, w, h)
        sends = [
            (src, part, dev, r.cast_send.at[i, n, d], r.cast_recv.at[i, n, d]) for d, dev in enumerate((beside, sibling))
        ]
        return lc(src, part, r.out_sem.at[i, n, 0]), sends

    def extra_copies(i, n):
        src = spare[n].at[gq(i, line_size * par + line_row(bh) + quarter, 64), :]
        part = extra_part(i, n)
        sends = [
            (src, part, dev, r.cast_send.at[i, n, 3 + d], r.cast_recv.at[i, n, 3 + d])
            for d, dev in enumerate((beside, sibling))
        ]
        return lc(src, part, r.out_sem.at[i, n, 1]), sends

    def begin(copies):
        local, sends = copies
        for src, part, dev, one, two in sends:
            rc(src, part, one, two, dev).start()
        local.start()

    def credit(n):
        pl.semaphore_signal(r.credit.at[n], inc=1, device_id=named(beside), device_id_type=MESH)

    def credited(n):
        pl.semaphore_wait(r.credit.at[n], 1)

    def beside_copy(i):
        return rc(block_of(i, 0, bh, temp), t_inbox(i, 7), r.fin_send.at[i], r.fin_recv.at[i], beside)

    def z_span(i, n, rows):
        return to_y(i, n, 0).at[0:rows, :]

    def reduce_last(i, n):
        def add(size):
            ref = z_span(i, n, 3 * size)
            rc(ref, ref, r.z_send.at[i, n], r.z_recv.at[i, n], across).wait_recv()
            add_into(block_of(i, n, bh, size), [z_box(i, n, slot, size) for slot in range(3)], step_of(i))

        sized(i, bh, add)
        if i % 2:
            credited(i // 2)
            beside_copy(i).start()
            return
        begin(final_copies(i, n))
        pl.when(bh == shared)(lambda: begin(extra_copies(i, n)))

    def reduce_out(i):
        beside_copy(i).wait()
        add_into(block_of(i, 0, bh, temp), [t_inbox(i, 7)], 48)
        begin(final_copies(i, 0))

    def final_on(i, n):
        def move(part, d):
            rc(part, part, r.cast_send.at[i, n, d], r.cast_recv.at[i, n, d], beside).wait_recv()
            rc(part, part, r.cast_send.at[i, n, d + 2], r.cast_recv.at[i, n, d + 2], sibling).start()

        move(final_part(i, n, 1 - w, h), 0)
        pl.when(bh == shared_beside)(lambda: move(extra_part(i, n), 3))

    def reduce_wait(i, n):
        local, sends = final_copies(i, n)
        local.wait()

        def sent(rows):
            ref = z_span(i, n, rows)
            rc(ref, ref, r.z_send.at[i, n], r.z_recv.at[i, n], across).wait_send()

        if i % 2:
            sent(3 * temp)
        else:
            pl.when(bh == shared)(lambda: sent(3 * quarter))
            pl.when(bh != shared)(lambda: sent(3 * quarter + 64))
        if i % 2:
            src, part, dev, one, two = sends[0]
            rc(src, outs[i].at[1 - h], one, two, dev).wait()
            return
        for src, part, dev, one, two in sends:
            rc(src, part, one, two, dev).wait_send()

        def far(part, d):
            return rc(part, part, r.cast_send.at[i, n, d], r.cast_recv.at[i, n, d], sibling)

        far(final_part(i, n, w, 1 - h), 1).wait_recv()
        far(final_part(i, n, 1 - w, h), 2).wait_send()
        far(final_part(i, n, 1 - w, 1 - h), 2).wait_recv()
        local, sends = extra_copies(i, n)

        @pl.when(bh == shared)
        def _():
            local.wait()
            for src, part, dev, one, two in sends:
                rc(src, part, one, two, dev).wait_send()

        pl.when(bh == shared_beside)(lambda: far(extra_part(i, n), 5).wait_send())
        pl.when(bh == 2 * w + 1 - h)(lambda: far(extra_part(i, n), 4).wait_recv())
        pl.when(bh == 2 * (1 - w) + 1 - h)(lambda: far(extra_part(i, n), 5).wait_recv())

    def tile_of(ref, jh, jw):
        return ref.at[rows_of(jh * 4, 4, 4), rows_of(jw * 32, 32), :]

    def tile_own(src, dst, n):
        return lc(src.at[mine], tile_of(dst, h, w), r.tile_own.at[n])

    def tiles_start(src, dst, n):
        for j, dev in tile_group:
            rc(src.at[j], tile_of(dst, h, w), r.tile_send.at[n], r.tile_recv.at[n], dev).start()
        tile_own(src, dst, n).start()

    def tiles_wait(src, dst, n):
        three = src.at[0:3]
        rc(three, three, r.tile_send.at[n], r.tile_recv.at[n], sibling).wait()
        tile_own(src, dst, n).wait()

    xg, cg = r.x_grid, r.cot_grid
    tiles_start(r.x_tiles, xg, 0)
    gather_start(0)
    r.param[...] = total(0, mid, r.param_in[0:CELL, :])
    tiles_wait(r.x_tiles, xg, 0)

    def grid_chunk(ref, i):
        v = ref[lax.div(i, 4), rows_of(lax.rem(i, 4) * CHUNK, CHUNK), :]
        return v.astype(F32).reshape(2, CELL, chan)

    fill(r.xa, r.xb, lambda i: grid_chunk(xg, i), chan)

    last = steps[0]
    gather_start(1)
    for step in range(1, last):
        gather_pump(0, step)
        gather_pump(1, step)
    gather_start(2)
    gather_pump(0, last)
    gather_pump(1, last)
    gather_finish(0)

    def first_pump(n):
        pl.when(n == 1)(lambda: gather_pump(2, 1))

    conv(r.xa, r.xb, whole[0], r.mid1, first_pump)
    sums = total(1, mid, packed(*moments(r.mid1, mid), mid), [lambda: gather_pump(2, 2), lambda: gather_finish(1)])
    prepare(0, sums, mid)

    def hidden(src, n, dst):
        value = activated(src, n, mid)

        def body(i, _):
            put(dst, i, value(i))
            return 0

        loop(CHUNKS, body, 0)

    hidden(r.mid1, 0, r.v1)
    stats = temporal(0, r.v1, whole[1], r.time1, [lambda: gather_pump(2, 3)])
    sums = total(
        2, chan, packed(*stats, chan), [lambda: gather_start(3), lambda: gather_pump(2, last)]
    )
    prepare(1, sums, chan)
    fill(r.aa, r.ab, activated(r.time1, 1, chan), chan)
    gather_finish(2)
    tiles_start(r.cot_tiles, cg, 1)

    def second_pump(n):
        for step in range(1, last):
            pl.when(n == 2 * step - 1)(lambda step=step: gather_pump(3, step))

    conv(r.aa, r.ab, whole[2], r.mid2, second_pump)

    def last_piece():
        gather_pump(3, last)
        gather_finish(3)

    sums = total(3, mid, packed(*moments(r.mid2, mid), mid), [last_piece])
    prepare(2, sums, mid)
    hidden(r.mid2, 2, r.v2)
    stats = temporal(1, r.v2, whole[3], r.time2)
    shared_xq2 = share_x(0, r.aa, r.xq2)
    shared_xq1 = share_x(1, r.xa, r.xq1)
    for i in range(4):
        gather_sent(i)
    share_v2 = share(4, r.v2, r.sib_v)
    sums = total(4, chan, packed(*stats, chan), [lambda: tiles_wait(r.cot_tiles, cg, 1)])
    prepare(3, sums, chan)

    out_grid = r.out_grid

    def grid_put(ref, i, v):
        ref[lax.div(i, 4), rows_of(lax.rem(i, 4) * CHUNK, CHUNK), :] = v.reshape(CHUNK, chan).astype(ref.dtype)

    def slope(y, s):
        return s * (1.0 + y * (1.0 - s))

    def pre_body(i, carry):
        scale, shift, inv, offset = tiles(3, chan)
        v = chunk(r.time2, i)
        y = v * scale + shift + chunk(r.xa, i, MAIN)
        s = sigmoid(y)
        m = keep(i)
        grid_put(out_grid, i, y * s * m)
        d = grid_chunk(cg, i) * m * slope(y, s)
        put(r.grad_pre, i, d)
        t = d * (v * inv - offset)
        return (carry[0] + d[0] + d[1], carry[1] + t[0] + t[1])

    zero_out = jnp.zeros((CELL, chan), F32)
    zero_mid = jnp.zeros((CELL, mid), F32)
    out_grid[HGT] = jnp.zeros((8 * CELL, chan), BF16)
    gg = loop(CHUNKS, pre_body, (zero_out, zero_out))

    def send_tiles(src, dst, n):
        for j, dev in tile_group:
            jh, jw = at_group(j)
            rc(tile_of(src, jh, jw), dst.at[mine], r.tile_send.at[n], r.tile_recv.at[n], dev).start()
        lc(tile_of(src, h, w), dst.at[mine], r.tile_own.at[n]).start()

    def sent_tiles(src, dst, n):
        three = dst.at[0:3]
        rc(three, three, r.tile_send.at[n], r.tile_recv.at[n], sibling).wait()
        lc(tile_of(src, h, w), dst.at[mine], r.tile_own.at[n]).wait()

    send_tiles(out_grid, r.block_out, 2)

    def norm_back(n, sums, width):
        r.norm_part[0, 2 * n : 2 * n + 1, 0:width] = sums[1:2]
        r.norm_part[0, 2 * n + 1 : 2 * n + 2, 0:width] = sums[0:1]
        back = r.back
        back[0, :, 0:width] = jnp.broadcast_to(sums[0:1] / cell_count, (CELL, width))
        back[1, :, 0:width] = jnp.broadcast_to(sums[1:2] / cell_count, (CELL, width))

    def through_norm(n, src, grad, i, width):
        scale, _, inv, offset = tiles(n, width)
        xhat = chunk(src, i) * inv - offset
        bias_part = r.back[0, :, 0:width][None]
        gain_part = r.back[1, :, 0:width][None]
        return scale * (chunk(grad, i, 0, width) - bias_part - xhat * gain_part) * keep(i)

    def through_act(n, src, grad, width):
        def body(i, carry):
            scale, shift, inv, offset = tiles(n, width)
            v = chunk(src, i)
            y = v * scale + shift
            s = sigmoid(y)
            d = chunk(grad, i, 0, width) * keep(i) * slope(y, s)
            put(grad, i, d, 0, width)
            t = d * (v * inv - offset)
            return (carry[0] + d[0] + d[1], carry[1] + t[0] + t[1])

        zero = jnp.zeros((CELL, width), F32)
        return loop(CHUNKS, body, (zero, zero))

    def to_frames(n, src, grad):
        def body(i, _):
            e = through_norm(n, src, grad, i, chan).astype(BF16)
            ef = e.astype(F32)
            put_e(1, i, e.reshape(CHUNK, chan))
            put_lanes(r.down, rows_of(i * CHUNK + CELL, CHUNK, CELL), ef.reshape(CHUNK, chan))
            put_lanes(r.up, rows_of(i * CHUNK, CHUNK), (ef * r.param_in[CELL : 2 * CELL, 0:chan][None]).reshape(CHUNK, chan))
            return 0

        loop(CHUNKS, body, 0)

    near, far = r.xt, r.xt2

    def spread():
        shared_xq2.wait()
        spread_x(r.xq2)
        shared_xq1.wait()
        spread_x(r.xq1)

    sums = total(5, chan, packed(*gg, chan), [spread])
    norm_back(3, sums, chan)
    to_frames(3, r.time2, r.grad_pre)
    shared_e3 = temporal_back(2, whole[3], [lambda: transposes(r.aa, r.ab, r.xq2, near, far)])
    credit(1)
    gg = through_act(2, r.mid2, r.grad_mid, mid)
    shared_e3.wait()
    share_v2.wait()
    def temporal_grads(i, v):
        def first():
            transpose_v(v, r.sib_v)
            temporal_grad(i, 0, 2)

        return [first, lambda: temporal_grad(i, 2, 1)]

    sums = total(6, mid, packed(*gg, mid), temporal_grads(3, r.v2))
    reduce_start(3, 0)
    norm_back(2, sums, mid)

    def fill_e(n, src):
        def value(i):
            v = through_norm(n, src, r.grad_mid, i, mid)
            for part, (c0, cw) in zip(e_all, halves):
                put(part, i, v[:, :, c0 : c0 + cw])
            return v

        fill(r.ea, r.eb, value, mid)

    fill_e(2, r.mid2)
    share_e(0)
    conv_back(r.ea, r.eb, whole[2], r.grad_mid)
    gg = through_act(1, r.time1, r.grad_mid, chan)

    def first_half():
        share_e_wait(0, 0)
        spatial_half(2, near, far, 0)

    sums = total(7, chan, packed(*gg, chan), [lambda: share_e_on(0, 0), first_half])
    reduce_start(2, 0)
    share_v1 = share(5, r.v1, r.sib_v)
    norm_back(1, sums, chan)
    to_frames(1, r.time1, r.grad_mid)
    reduce_middle(3, 0)
    share_e_on(0, 1)

    def second_half():
        share_e_wait(0, 1)
        spatial_half(2, near, far, 1)
        credit(2)
        reduce_start(2, 1)

    shared_e3 = temporal_back(3, whole[1], [second_half])
    credit(0)
    reduce_middle(2, 0)
    gg = through_act(0, r.mid1, r.grad_mid, mid)
    shared_e3.wait()
    share_v1.wait()
    sums = total(8, mid, packed(*gg, mid), temporal_grads(1, r.v1))
    reduce_start(1, 0)
    reduce_middle(2, 1)
    norm_back(0, sums, mid)
    fill_e(0, r.mid1)
    credited(2)
    share_e(1)
    reduce_last(3, 0)
    transposes(r.xa, r.xb, r.xq1, near, far)
    share_e_on(1, 0)
    reduce_out(3)
    sent_tiles(out_grid, r.block_out, 2)
    share_e_wait(1, 0)
    spatial_half(0, near, far, 0)
    reduce_start(0, 0)
    reduce_middle(1, 0)
    share_e_on(1, 1)
    for n in (0, 1):
        reduce_last(2, n)
    share_e_wait(1, 1)
    spatial_half(0, near, far, 1)
    reduce_start(0, 1)
    reduce_middle(0, 0)
    conv_back(r.ea, r.eb, whole[0], r.grad_mid)

    norm_copy = rc(r.norm_part.at[0], r.norm_part.at[1], r.norm_sem.at[0], r.norm_sem.at[1], beside)
    norm_copy.start()

    def last_body(i, _):
        grid_put(out_grid, i, (chunk(r.grad_mid, i, 0, chan) + chunk(r.grad_pre, i)) * keep(i))
        return 0

    loop(CHUNKS, last_body, 0)
    send_tiles(out_grid, r.grad_input, 3)
    reduce_last(1, 0)
    for n in (0, 1):
        final_on(2, n)
    reduce_out(1)
    reduce_last(0, 0)
    norm_copy.wait()
    r.norm_grads[...] = r.norm_part[0] + r.norm_part[1]
    reduce_middle(0, 1)
    final_on(0, 0)
    sent_tiles(out_grid, r.grad_input, 3)
    for n in (0, 1):
        reduce_wait(2, n)
    reduce_wait(3, 0)
    reduce_wait(1, 0)
    reduce_last(0, 1)
    final_on(0, 1)
    for n in (0, 1):
        reduce_wait(0, n)


def per_device_fast(nb, *args):
    (
        inputs,
        starts,
        first_spatial,
        first_mid_gain,
        first_mid_bias,
        first_temporal,
        first_out_gain,
        first_out_bias,
        second_spatial,
        second_mid_gain,
        second_mid_bias,
        second_temporal,
        second_out_gain,
        second_out_bias,
        cotangent,
    ) = args
    micro, frames, side, _, chan = inputs.shape
    mid = first_spatial.shape[1]
    spat, temp = first_spatial.shape[0], first_temporal.shape[0]
    h, w, b = (lax.axis_index(name) for name in ("ha", "wa", "batch"))
    few = frames // 2
    offsets = jnp.arange(side)
    valid = (h * side + offsets < HGT)[:, None] & (w * side + offsets < HGT)[None, :]

    def tiles(array):
        array = array * valid.astype(BF16)[None, None, :, :, None]
        array = array.reshape(micro, 2, few, side, side, chan).transpose(0, 1, 3, 4, 2, 5)
        return array.reshape(4, side, side * few, chan)

    def untiled(array):
        array = array.reshape(micro, 2, side, side, few, chan).transpose(0, 1, 4, 2, 3, 5)
        return array.reshape(micro, frames, side, side, chan).astype(F32)

    gate = (1 - lax.dynamic_slice(starts, (w, h * few), (1, few))).astype(F32)
    gate = jnp.broadcast_to(gate.reshape(few, 1), (few, mid))
    here = jnp.where(h == 0, 1.0, 0.0)

    def placed(shard):
        row = jnp.zeros((mid,), F32)
        return lax.dynamic_update_slice(row, shard.astype(F32) * here, (b * shard.shape[0],))

    param = jnp.stack(
        [
            placed(v)
            for v in (
                first_mid_gain,
                first_mid_bias,
                first_out_gain,
                first_out_bias,
                second_mid_gain,
                second_mid_bias,
                second_out_gain,
                second_out_bias,
            )
        ]
    )
    half = chan // 2
    few_rows = ROWS // CELL

    inputs_of = dict(
        x_tiles=(tiles(inputs), pl.ANY),
        cot_tiles=(tiles(cotangent), pl.ANY),
        param_in=(jnp.concatenate([param, gate], axis=0), pltpu.VMEM),
        first_spatial=(first_spatial, pl.ANY),
        first_temporal=(first_temporal, pl.ANY),
        second_spatial=(second_spatial, pl.ANY),
        second_temporal=(second_temporal, pl.ANY),
    )
    outputs_of = dict(
        block_out=((4, side, side * CELL, chan), BF16, pl.ANY),
        grad_input=((4, side, side * CELL, chan), BF16, pl.ANY),
        norm_grads=((8, mid), F32, pltpu.VMEM),
        out1s0=((spat, 512), BF16, pl.ANY),
        out1s1=((spat, mid - 512), BF16, pl.ANY),
        out1t=((2, temp, half), BF16, pl.ANY),
        out2s0=((spat, 512), BF16, pl.ANY),
        out2s1=((spat, mid - 512), BF16, pl.ANY),
        out2t=((2, temp, half), BF16, pl.ANY),
    )
    dma = pltpu.SemaphoreType.DMA
    scratch_of = dict(
        w1s0=pltpu.VMEM((9 * chan, 512), BF16),
        w1s1=pltpu.VMEM((9 * chan, mid - 512), BF16),
        w1t0=pltpu.VMEM((3 * mid, half), BF16),
        w1t1=pltpu.VMEM((3 * mid, half), BF16),
        w2s0=pltpu.VMEM((9 * chan, 512), BF16),
        w2s1=pltpu.VMEM((9 * chan, mid - 512), BF16),
        w2t0=pltpu.VMEM((3 * mid, half), BF16),
        w2t1=pltpu.VMEM((3 * mid, half), BF16),
        x_grid=pltpu.VMEM((8, 8 * CELL, chan), BF16),
        cot_grid=pltpu.VMEM((8, 8 * CELL, chan), BF16),
        out_grid=pltpu.VMEM((8, 8 * CELL, chan), BF16),
        xa=pltpu.VMEM((PADDED, chan), BF16),
        xb=pltpu.VMEM((PADDED, chan), BF16),
        aa=pltpu.VMEM((PADDED, chan), BF16),
        ab=pltpu.VMEM((PADDED, chan), BF16),
        ea=pltpu.VMEM((PADDED, mid), BF16),
        eb=pltpu.VMEM((PADDED, mid), BF16),
        mid1=pltpu.VMEM((ROWS, mid), F32),
        mid2=pltpu.VMEM((ROWS, mid), F32),
        grad_mid=pltpu.VMEM((ROWS, mid), F32),
        v1=pltpu.VMEM((ROWS, mid), BF16),
        v2=pltpu.VMEM((ROWS, mid), BF16),
        time1=pltpu.VMEM((ROWS, chan), F32),
        time2=pltpu.VMEM((ROWS, chan), F32),
        grad_pre=pltpu.VMEM((ROWS, chan), F32),
        down=pltpu.VMEM((chan // 128, ROWS + CHUNK, 128), F32),
        up=pltpu.VMEM((chan // 128, ROWS + CHUNK, 128), F32),
        e3=pltpu.VMEM((2, 3, ROWS, half), BF16),
        sib_e3=pltpu.VMEM((3, ROWS, half), BF16),
        halo_out=pltpu.VMEM((2, few_rows, chan), F32),
        halo_in=pltpu.VMEM((4, 2, few_rows, chan), F32),
        param=pltpu.VMEM((8, mid), F32),
        tile_mid=pltpu.VMEM((2, 4, CELL, mid), F32),
        tile_out=pltpu.VMEM((2, 4, CELL, chan), F32),
        back=pltpu.VMEM((2, CELL, mid), F32),
        sum_flat=pltpu.VMEM((2, 2 * nb, 8, chan // 4), F32),
        norm_part=pltpu.VMEM((2, 8, mid), F32),
        sum_b=pltpu.VMEM((2, 4, 8, mid), F32),
        sum_c=pltpu.VMEM((2, nb // 2, 8, mid), F32),
        own_sem=dma((4, 2)),
        ring_send=dma((4, 2)),
        ring_recv=dma((4, 2, 2, 2, nb // 2 + 1)),
        sib_send=dma((4, 2)),
        sib_recv=dma((4, 2)),
        over_send=dma((4, 2)),
        over_recv=dma((4, 2, 2, nb // 2 + 1)),
        norm_sem=dma((2,)),
        credit=pltpu.SemaphoreType.REGULAR((3,)),
        sb_send=dma((9,)),
        sb_recv=dma((9,)),
        sc_send=dma((9,)),
        sc_recv=dma((9,)),
        halo_send=dma((4, 2)),
        halo_recv=dma((4, 2)),
        share_send=dma((6,)),
        share_recv=dma((6,)),
        e_all0=pltpu.VMEM((4 * ROWS, 512), BF16),
        e_all1=pltpu.VMEM((4 * ROWS, mid - 512), BF16),
        xq1=pltpu.VMEM((3, 2, PADDED, chan // 4), BF16),
        xq2=pltpu.VMEM((3, 2, PADDED, chan // 4), BF16),
        xt=pltpu.VMEM((mid, 2 * ROWS), BF16),
        xt2=pltpu.VMEM((mid, 2 * ROWS), BF16),
        sib_v=pltpu.VMEM((ROWS, mid), BF16),
        e_send=dma((2, 2)),
        e_recv=dma((2, 2, 2)),
        xq_send=dma((2,)),
        xq_recv=dma((2,)),
        y_send=dma((4, 2)),
        y_recv=dma((4, 2)),
        z_send=dma((4, 2)),
        z_recv=dma((4, 2)),
        cast_send=dma((4, 2, 6)),
        cast_recv=dma((4, 2, 8)),
        out_sem=dma((4, 2, 2)),
        fin_send=dma((4,)),
        fin_recv=dma((4,)),
        tile_send=dma((4,)),
        tile_recv=dma((4,)),
        tile_own=dma((4,)),
    )
    names = (*inputs_of, *outputs_of, *scratch_of)
    cell_count = float(frames * nb * HGT * HGT)
    results = pl.pallas_call(
        functools.partial(block_kernel, (nb, chan, mid, cell_count), names),
        out_shape=[jax.ShapeDtypeStruct(shape, dtype) for shape, dtype, _ in outputs_of.values()],
        in_specs=[pl.BlockSpec(memory_space=space) for _, space in inputs_of.values()],
        out_specs=[pl.BlockSpec(memory_space=space) for _, _, space in outputs_of.values()],
        scratch_shapes=list(scratch_of.values()),
        compiler_params=pltpu.CompilerParams(
            collective_id=0, has_side_effects=True, vmem_limit_bytes=VMEM_LIMIT
        ),
    )(*(array for array, _ in inputs_of.values()))
    got = SimpleNamespace(**dict(zip(outputs_of, results)))

    def spatial(left, right):
        return jnp.concatenate([left, right], axis=1).astype(F32)

    def temporal(pair):
        return jnp.concatenate([pair[0], pair[1]], axis=1).astype(F32)

    def norm(row, like):
        size = like.shape[0]
        return lax.dynamic_slice_in_dim(got.norm_grads[row], b * size, size)

    return (
        untiled(got.block_out),
        untiled(got.grad_input),
        spatial(got.out1s0, got.out1s1),
        norm(0, first_mid_gain),
        norm(1, first_mid_bias),
        temporal(got.out1t),
        norm(2, first_out_gain),
        norm(3, first_out_bias),
        spatial(got.out2s0, got.out2s1),
        norm(4, second_mid_gain),
        norm(5, second_mid_bias),
        temporal(got.out2t),
        norm(6, second_out_gain),
        norm(7, second_out_bias),
    )


def extended(shard, sides, width):
    for axis, dim in sides:
        count, length = (lax.axis_size(axis), shard.shape[dim])
        up = [(i, (i + 1) % count) for i in range(count - 1)]
        down = [(j, i) for i, j in up]
        last = lax.slice_in_dim(shard, length - width, length, axis=dim)
        leading = lax.slice_in_dim(shard, 0, width, axis=dim)
        before = lax.ppermute(last, axis, up)
        after = lax.ppermute(leading, axis, down)
        shard = jnp.concatenate([before, shard, after], axis=dim)
    return shard


def passed_along(shard, axis, by):
    count = lax.axis_size(axis)
    pairs = [(i, i + by) for i in range(count) if 0 <= i + by < count]
    return lax.ppermute(shard, axis, pairs)


def for_sending(shard):

    def short(part):
        return part.astype(jnp.bfloat16) if part.dtype == jnp.float32 else part

    return jax.tree.map(short, shard)


def silu_slope(values):
    sigma = jax.nn.sigmoid(values)
    return sigma * (1.0 + values * (1.0 - sigma))


def spatial_forward(field_in, kernel):
    frames, tile_side = (field_in.shape[0], field_in.shape[1])
    padded = extended(field_in, (("ha", 1), ("wa", 2)), 1)
    pieces = [
        padded[:, offset // 3 : offset // 3 + tile_side, offset % 3 : offset % 3 + tile_side, :]
        for offset in range(9)
    ]
    patches = jnp.concatenate(pieces, axis=-1).reshape(frames * tile_side * tile_side, -1)
    return (patches, jnp.dot(patches, kernel, preferred_element_type=jnp.float32))


def spatial_backward(grad_out, patches, kernel):
    frames, tile_side, channels = (grad_out.shape[0], grad_out.shape[1], grad_out.shape[3])
    row_count = frames * tile_side * tile_side
    padded = extended(grad_out, (("ha", 1), ("wa", 2)), 1)
    pieces = [
        padded[
            :,
            2 - offset // 3 : 2 - offset // 3 + tile_side,
            2 - offset % 3 : 2 - offset % 3 + tile_side,
            :,
        ]
        for offset in range(9)
    ]
    stacked = jnp.concatenate(pieces, axis=-1).reshape(row_count, 9, channels)
    grad_in = jnp.einsum(
        "rkm,kcm->rc", stacked, kernel.reshape(9, -1, channels), preferred_element_type=jnp.float32
    )
    grad_kernel = jnp.einsum(
        "rk,rm->km",
        patches,
        grad_out.reshape(row_count, channels),
        preferred_element_type=jnp.float32,
    )
    return (grad_in, grad_kernel)


def temporal_forward(field_in, clip_gate, kernel):
    frames, tile_side = (field_in.shape[0], field_in.shape[1])
    gated_in = field_in * clip_gate
    earlier = passed_along(field_in[-1:], "batch", 1)
    later_frame = passed_along(gated_in[:1], "batch", -1)
    before = jnp.concatenate([earlier, field_in[:-1]], axis=0) * clip_gate
    after_tap = jnp.concatenate([gated_in[1:], later_frame], axis=0)
    joined = jnp.concatenate([before, field_in, after_tap], axis=-1).reshape(
        frames * tile_side * tile_side, -1
    )
    return (joined, jnp.dot(joined, kernel, preferred_element_type=jnp.float32))


def temporal_backward(grad_out, joined, clip_gate, kernel):
    frames, tile_side, channels = (grad_out.shape[0], grad_out.shape[1], grad_out.shape[3])
    row_count = frames * tile_side * tile_side
    gated_grad = grad_out * clip_gate
    later_frame = passed_along(gated_grad[:1], "batch", -1)
    earlier = passed_along(grad_out[-1:], "batch", 1)
    from_later = jnp.concatenate([gated_grad[1:], later_frame], axis=0)
    from_earlier = jnp.concatenate([earlier, grad_out[:-1]], axis=0) * clip_gate
    stacked = jnp.concatenate([from_later, grad_out, from_earlier], axis=-1).reshape(
        row_count, 3, channels
    )
    grad_in = jnp.einsum(
        "rkc,kmc->rm", stacked, kernel.reshape(3, -1, channels), preferred_element_type=jnp.float32
    )
    grad_kernel = jnp.einsum(
        "rk,rc->kc",
        joined,
        grad_out.reshape(row_count, channels),
        preferred_element_type=jnp.float32,
    )
    return (grad_in, grad_kernel)


def norm_forward(pre_norm, norm_gain, norm_bias, valid_rows, cell_count):
    first_sum = jnp.sum(pre_norm * valid_rows, axis=0)
    square_sum = jnp.sum(pre_norm * pre_norm * valid_rows, axis=0)
    first_sum, square_sum = lax.psum((first_sum, square_sum), ("ha", "wa", "batch"))
    mean_val = first_sum / cell_count
    inv_std = lax.rsqrt(square_sum / cell_count - mean_val * mean_val + epsilon)
    normed = (pre_norm - mean_val) * inv_std
    return (normed, inv_std, normed * norm_gain.astype(jnp.float32) + norm_bias.astype(jnp.float32))


def norm_backward(grad_norm, normed, inv_std, norm_gain, valid_rows, cell_count):
    bias_grad = jnp.sum(grad_norm, axis=0)
    gain_grad = jnp.sum(grad_norm * normed, axis=0)
    bias_grad, gain_grad = lax.psum((bias_grad, gain_grad), ("ha", "wa", "batch"))
    grad_in = (
        valid_rows
        * norm_gain.astype(jnp.float32)
        * inv_std
        * (grad_norm - bias_grad / cell_count - normed * gain_grad / cell_count)
    )
    return (grad_in, gain_grad, bias_grad)


def forward_pair(field_in, weights, clip_gate, valid_rows, cell_count):
    frames, tile_side = (field_in.shape[0], field_in.shape[1])
    patches, spatial_out = spatial_forward(field_in, weights[0])
    mid_hat, mid_scale, mid_norm = norm_forward(
        spatial_out, weights[1], weights[2], valid_rows, cell_count
    )
    hidden = (
        (jax.nn.silu(mid_norm) * valid_rows)
        .astype(jnp.bfloat16)
        .reshape(frames, tile_side, tile_side, -1)
    )
    joined, temporal_out = temporal_forward(hidden, clip_gate, weights[3])
    out_hat, out_scale, out_norm = norm_forward(
        temporal_out, weights[4], weights[5], valid_rows, cell_count
    )
    return ((patches, mid_hat, mid_scale, mid_norm, joined, out_hat, out_scale), out_norm)


def backward_pair(grad_norm, kept, weights, clip_gate, valid_rows, cell_count, tile_side):
    patches, mid_hat, mid_scale, mid_norm, joined, out_hat, out_scale = kept
    frames = clip_gate.shape[0]
    grad_time, out_gain_grad, out_bias_grad = norm_backward(
        grad_norm, out_hat, out_scale, weights[4], valid_rows, cell_count
    )
    grad_time = grad_time.astype(jnp.bfloat16).reshape(frames, tile_side, tile_side, -1)
    grad_hidden, temporal_grad = temporal_backward(grad_time, joined, clip_gate, weights[3])
    grad_mid = grad_hidden * valid_rows * silu_slope(mid_norm)
    grad_spatial, mid_gain_grad, mid_bias_grad = norm_backward(
        grad_mid, mid_hat, mid_scale, weights[1], valid_rows, cell_count
    )
    grad_spatial = grad_spatial.astype(jnp.bfloat16).reshape(frames, tile_side, tile_side, -1)
    grad_in, spatial_grad = spatial_backward(grad_spatial, patches, weights[0])
    return (
        grad_in,
        (spatial_grad, mid_gain_grad, mid_bias_grad, temporal_grad, out_gain_grad, out_bias_grad),
    )


def per_device(
    inputs,
    starts,
    first_spatial,
    first_mid_gain,
    first_mid_bias,
    first_temporal,
    first_out_gain,
    first_out_bias,
    second_spatial,
    second_mid_gain,
    second_mid_bias,
    second_temporal,
    second_out_gain,
    second_out_bias,
    cotangent,
):
    shards = (
        first_spatial,
        first_mid_gain,
        first_mid_bias,
        first_temporal,
        first_out_gain,
        first_out_bias,
        second_spatial,
        second_mid_gain,
        second_mid_bias,
        second_temporal,
        second_out_gain,
        second_out_bias,
    )
    micro_total, frames, tile_side, channels = (
        inputs.shape[0],
        inputs.shape[1],
        inputs.shape[2],
        inputs.shape[4],
    )
    row_count = frames * tile_side * tile_side
    cell_count = frames * lax.axis_size("batch") * HGT * HGT
    offsets = jnp.arange(tile_side)
    inside_h = lax.axis_index("ha") * tile_side + offsets < HGT
    inside_w = lax.axis_index("wa") * tile_side + offsets < HGT
    valid_grid = inside_h[:, None] & inside_w[None, :]
    valid_tile = valid_grid.astype(jnp.bfloat16)[None, :, :, None]
    valid_rows = jnp.broadcast_to(
        valid_grid.astype(jnp.float32)[None], (frames, tile_side, tile_side)
    ).reshape(row_count, 1)
    results = []
    input_grads = []
    kernel_total = None
    norm_total = None
    for micro_step in range(micro_total):
        gathered = (
            lax.all_gather(shards[0], "batch", axis=0, tiled=True),
            lax.all_gather(shards[1], "batch", axis=0, tiled=True),
            lax.all_gather(shards[2], "batch", axis=0, tiled=True),
            lax.all_gather(shards[3], "batch", axis=0, tiled=True),
            lax.all_gather(shards[4], "batch", axis=0, tiled=True),
            lax.all_gather(shards[5], "batch", axis=0, tiled=True),
            lax.all_gather(shards[6], "batch", axis=0, tiled=True),
            lax.all_gather(shards[7], "batch", axis=0, tiled=True),
            lax.all_gather(shards[8], "batch", axis=0, tiled=True),
            lax.all_gather(shards[9], "batch", axis=0, tiled=True),
            lax.all_gather(shards[10], "batch", axis=0, tiled=True),
            lax.all_gather(shards[11], "batch", axis=0, tiled=True),
        )
        clip_gate = (1 - starts[micro_step]).astype(jnp.bfloat16).reshape(frames, 1, 1, 1)
        x_in = inputs[micro_step] * valid_tile
        first_kept, first_norm = forward_pair(
            x_in, gathered[0:6], clip_gate, valid_rows, cell_count
        )
        first_act = (
            (jax.nn.silu(first_norm) * valid_rows)
            .astype(jnp.bfloat16)
            .reshape(frames, tile_side, tile_side, channels)
        )
        second_kept, second_norm = forward_pair(
            first_act, gathered[6:12], clip_gate, valid_rows, cell_count
        )
        pre_out = second_norm + x_in.reshape(row_count, channels).astype(jnp.float32)
        results.append(
            (jax.nn.silu(pre_out) * valid_rows).reshape(frames, tile_side, tile_side, channels)
        )
        grad_pre = (
            cotangent[micro_step].reshape(row_count, channels).astype(jnp.float32)
            * valid_rows
            * silu_slope(pre_out)
        )
        grad_act, second_grads = backward_pair(
            grad_pre, second_kept, gathered[6:12], clip_gate, valid_rows, cell_count, tile_side
        )
        grad_first = grad_act * valid_rows * silu_slope(first_norm)
        grad_conv, first_grads = backward_pair(
            grad_first, first_kept, gathered[0:6], clip_gate, valid_rows, cell_count, tile_side
        )
        input_grads.append(
            ((grad_conv + grad_pre) * valid_rows).reshape(frames, tile_side, tile_side, channels)
        )
        step_grads = first_grads + second_grads
        kernel_now = (step_grads[0], step_grads[3], step_grads[6], step_grads[9])
        norm_now = (
            step_grads[1],
            step_grads[2],
            step_grads[4],
            step_grads[5],
            step_grads[7],
            step_grads[8],
            step_grads[10],
            step_grads[11],
        )
        if micro_step == 0:
            kernel_total = kernel_now
            norm_total = norm_now
        else:
            kernel_total = jax.tree.map(jnp.add, kernel_total, kernel_now)
            norm_total = jax.tree.map(jnp.add, norm_total, norm_now)
    kernel_total = lax.psum_scatter(kernel_total, "batch", scatter_dimension=0, tiled=True)
    kernel_total = jax.tree.map(
        lambda part: part.astype(jnp.float32), lax.psum(for_sending(kernel_total), ("ha", "wa"))
    )
    shard_index = lax.axis_index("batch")
    batch_count = lax.axis_size("batch")
    norm_shards = tuple(
        (
            lax.dynamic_slice_in_dim(
                full_sum,
                shard_index * (full_sum.shape[0] // batch_count),
                full_sum.shape[0] // batch_count,
            )
            for full_sum in norm_total
        )
    )
    return (
        jnp.stack(results),
        jnp.stack(input_grads),
        kernel_total[0],
        norm_shards[0],
        norm_shards[1],
        kernel_total[1],
        norm_shards[2],
        norm_shards[3],
        kernel_total[2],
        norm_shards[4],
        norm_shards[5],
        kernel_total[3],
        norm_shards[6],
        norm_shards[7],
    )


def solution(mesh):
    in_specs = (
        P(None, "batch", "ha", "wa", None),
        P(None, "batch"),
        P("batch", None),
        P("batch"),
        P("batch"),
        P("batch", None),
        P("batch"),
        P("batch"),
        P("batch", None),
        P("batch"),
        P("batch"),
        P("batch", None),
        P("batch"),
        P("batch"),
        P(None, "batch", "ha", "wa", None),
    )
    out_specs = (
        P(None, "batch", "ha", "wa", None),
        P(None, "batch", "ha", "wa", None),
        P("batch", None),
        P("batch"),
        P("batch"),
        P("batch", None),
        P("batch"),
        P("batch"),
        P("batch", None),
        P("batch"),
        P("batch"),
        P("batch", None),
        P("batch"),
        P("batch"),
    )
    batch = mesh.shape["batch"]

    def program(*args):
        spat, temp = args[2].shape[0], args[5].shape[0]
        fits = args[0].shape == (2, 16, 4, 4, 512) and args[2].shape[1] == 1152
        if fits and batch == 8 and spat * batch == 9 * 512 and temp * batch == 3 * 1152:
            return per_device_fast(batch, *args)
        return per_device(*args)

    return jax.shard_map(
        program, mesh=mesh, in_specs=in_specs, out_specs=out_specs, check_vma=False
    )
```
